32 devices in a mesh: fsdp: 8 (over z, x), tp: 4 (over y, core).
Axes of the slice: x: 2, y: 2, z: 4, core: 2. Of those that a mesh axis runs over, the one named last changes fastest.
Arguments:
- tokens: bfloat16 [4096, 2048], P('fsdp', 'tp'), may hold values from -6 to 6
- cotangent: bfloat16 [4096, 2048], P('fsdp', 'tp'), may hold values from -6 to 6
- routes: int32 [4096, 8], P('fsdp'), may hold values from 0 to 31, all different within a row; in each aligned block of 256 rows (0 to 255, 256 to 511, ...) at most 128 rows name the same one
- doc_ids: int32 [2, 2048], P(None, 'fsdp'), may hold values from 0 to 3, as said below
- gain_attn: float32 [2048], replicated, may hold values from 0.1 to 1.9
- w_query: bfloat16 [2048, 4096], P('fsdp', 'tp'), may hold values from -0.125 to 0.125
- key_weight: bfloat16 [2048, 512], P('fsdp', 'tp'), may hold values from -0.125 to 0.125
- value_weight: bfloat16 [2048, 512], P('fsdp', 'tp'), may hold values from -0.125 to 0.125
- w_out: bfloat16 [2048, 4096], P('fsdp', 'tp'), may hold values from -1 to 1
- gain_query: float32 [128], replicated, may hold values from 0.1 to 1.9
- key_norm_gain: float32 [128], replicated, may hold values from 0.1 to 1.9
- gain_moe: float32 [2048], replicated, may hold values from 0.1 to 1.9
- router: bfloat16 [2048, 32], replicated, may hold values from -0.0625 to 0.0625
- w_gate: bfloat16 [32, 2048, 768], P(('fsdp', 'tp')), may hold values from -0.125 to 0.125
- w_up: bfloat16 [32, 2048, 768], P(('fsdp', 'tp')), may hold values from -0.125 to 0.125
- w_down: bfloat16 [32, 768, 2048], P(('fsdp', 'tp')), may hold values from -0.875 to 0.875
Outputs:
- block_out: bfloat16 [4096, 2048], P('fsdp', 'tp')
- token_grad: bfloat16 [4096, 2048], P('fsdp', 'tp')
- gain_attn_grad: float32 [2048], replicated
- w_query_grad: float32 [2048, 4096], P('fsdp', 'tp')
- w_key_grad: float32 [2048, 512], P('fsdp', 'tp')
- w_value_grad: float32 [2048, 512], P('fsdp', 'tp')
- w_out_grad: float32 [2048, 4096], P('fsdp', 'tp')
- gain_query_grad: float32 [128], replicated
- gain_key_grad: float32 [128], replicated
- gain_moe_grad: float32 [2048], replicated
- router_grad: float32 [2048, 32], replicated
- w_gate_grad: float32 [32, 2048, 768], P(('fsdp', 'tp'))
- w_up_grad: float32 [32, 2048, 768], P(('fsdp', 'tp'))
- w_down_grad: float32 [32, 768, 2048], P(('fsdp', 'tp'))
The draws below stay inside these ranges and needn't reach their ends.
Inputs may be any that keep to these rules, and one draw needn't show every extreme that they name: `doc_ids`: row m holds the document numbers of micro-batch m's 2048 positions; they never fall, all 4 numbers occur, and one document begins within the first 256 positions and ends within the last 256. `routes`: A row names 8 different experts. In each aligned block of 256 rows (one fsdp index's tokens of one micro-batch) no expert is named by more than 128 rows, and in some block one expert is named by exactly 128.
All inputs are finite; a program needn't handle non-finite values.
Results may differ from the reference program's by a relative error of at most 0.025.
Values may be sent and summed in bfloat16 or wider, within the bound.
A program may use at most 256 MiB of HBM per device.

```python
import math
import jax
import jax.numpy as jnp
import numpy as np
from jax import lax

MODEL_DIM = 2048
QUERY_HEAD_NUM = 32
KV_HEAD_TOTAL = 4
HEAD_DIM = 128
F = 768
TOPK = 8
MICRO = 2
DOCS = 4
MB_ROWS = 256
EXPERTS = 32
STREAM = 2048
TOKENS = 4096
CAP = 128
N_FSDP = 8


def draw_doc_ids(key, part):
    key = jax.random.fold_in(key, 7)
    sequence_length = N_FSDP * MB_ROWS
    first_key, second_key, third_key = jax.random.split(key, 3)
    opening = jax.random.randint(first_key, (MICRO, 1), 1, MB_ROWS)
    closing = jax.random.randint(second_key, (MICRO, 1), sequence_length - MB_ROWS + 1, sequence_length - 1)
    final_cut = jax.random.randint(third_key, (MICRO, 1), closing + 1, sequence_length)
    position = jnp.arange(sequence_length, dtype=jnp.int32)[None, :]
    return (position >= opening).astype(jnp.int32) + (position >= closing).astype(jnp.int32) + (position >= final_cut).astype(jnp.int32)


def level_of(own_key, extent, cuts, smallest, high):
    loudness = 1.0
    for axis_at, shards_of in cuts:
        steps = jax.random.uniform(jax.random.fold_in(jax.random.fold_in(own_key, 6), axis_at), (shards_of,), jnp.float32, smallest / len(cuts), high / len(cuts))
        loudness = loudness * jnp.repeat(jnp.exp(steps), extent[axis_at] // shards_of).reshape((-1,) + (1,) * (len(extent) - 1 - axis_at))
    return loudness


def shared_out(own_key, own, number, rows, amount, top, bound, lean):
    sequence = jax.random.permutation(own_key, amount)
    heavy_load, ordinary = shares(amount, rows * top, bound, lean, True), shares(amount, rows * top, bound, lean, False)
    places = jnp.arange(amount)

    def named(lengths, rotation):
        used = int((lengths > 0).sum())
        fixed = max(1, used // 4)
        moved = fixed + (places - fixed + rotation * (used - fixed)) % max(1, amount - fixed)
        return jnp.zeros((amount,), jnp.int32).at[sequence[jnp.where(places < fixed, places, moved)]].set(jnp.asarray(lengths, jnp.int32))

    lengths = jnp.where(number % 4 == 0, named(heavy_load, number // 4), named(ordinary, number - number // 4 - 1))
    mixed = jax.random.permutation(jax.random.fold_in(own, 3), amount)
    giver, sink = mixed[0:amount // 2 * 2:2], mixed[1:amount // 2 * 2:2]
    margin = jnp.minimum(lengths[giver] - 1, bound - lengths[sink]) // 2
    margin = jnp.where((giver == sequence[0]) | (sink == sequence[0]) | (lengths[sink] == 0), 0, jnp.maximum(margin, 0))
    moved = jax.random.randint(jax.random.fold_in(own, 4), (amount // 2,), 0, 1 << 20) % (margin + 1)
    lengths = lengths.at[giver].add(-moved).at[sink].add(moved)
    members = jnp.searchsorted(jnp.cumsum(lengths), jnp.arange(rows * top), side="right").astype(jnp.int32)
    grid = members.reshape(top, rows).T
    grid = grid[jax.random.permutation(jax.random.fold_in(own, 1), rows)]
    rotation = jax.random.randint(jax.random.fold_in(own, 2), (rows, 1), 0, top)
    return jnp.take_along_axis(grid, (jnp.arange(top)[None, :] + rotation) % top, axis=1)


def shares(count, total, most, lean, full):
    loads = [(1 << 20) // math.isqrt(rank ** lean) + 1 for rank in range(1, count + 1)]
    largest = most if full else min(most, max(-(-total // count), total * loads[0] // sum(loads)))
    least = 1 if total - largest >= count - 1 else 0
    holding, rest = [largest] + [least] * (count - 1), total - largest - least * (count - 1)
    while rest > 0:
        candidates = [i for i in range(1, count) if holding[i] < largest] or [i for i in range(1, count) if holding[i] < most]
        whole, left = sum([loads[i] for i in candidates]), rest
        for i in candidates:
            extra = min(most - holding[i], max(1, left * loads[i] // whole), rest)
            holding[i] = holding[i] + extra
            rest = rest - extra
    return np.array(holding)


def bell_draw(stream_key, shape, scale, reach, shards=(), kind=jnp.bfloat16):
    entries = scale * jax.random.normal(stream_key, shape, jnp.float32)
    if shards:
        entries = entries * level_of(stream_key, shape, shards, -0.22, 0.18)
    return jnp.clip(entries, -reach, reach).astype(kind)


def setup_inputs(seed: int = 0) -> dict:
    keys = jax.random.split(jax.random.key(seed), 17)
    tokens = bell_draw(keys[0], (TOKENS, MODEL_DIM), 1.0, 6.0, ((0, 8), (1, 4)))
    cotangent = bell_draw(keys[1], (TOKENS, MODEL_DIM), 1.0, 6.0, ((0, 8), (1, 4)))
    routes_keys = jax.random.split(jax.random.fold_in(keys[2], 1), TOKENS // MB_ROWS)
    routes_turns = jax.random.permutation(jax.random.fold_in(keys[2], 3), TOKENS // MB_ROWS)
    routes = jax.vmap(lambda own, number: shared_out(jax.random.fold_in(keys[2], 2), own, number, MB_ROWS, EXPERTS, TOPK, CAP, 2))(routes_keys, routes_turns).reshape((TOKENS, TOPK))
    doc_ids = draw_doc_ids(jax.random.fold_in(keys[16], 71), 0)
    gain_attn = jnp.clip(1.0 + 0.18 * jax.random.normal(keys[4], (MODEL_DIM,), jnp.float32), 0.1, 1.9)
    w_query = bell_draw(keys[5], (MODEL_DIM, QUERY_HEAD_NUM * HEAD_DIM), MODEL_DIM ** -0.5, 0.125, ((0, 8), (1, 4)))
    key_weight = bell_draw(keys[6], (MODEL_DIM, KV_HEAD_TOTAL * HEAD_DIM), MODEL_DIM ** -0.5, 0.125, ((0, 8), (1, 4)))
    value_weight = bell_draw(keys[7], (MODEL_DIM, KV_HEAD_TOTAL * HEAD_DIM), MODEL_DIM ** -0.5, 0.125, ((0, 8), (1, 4)))
    w_out = bell_draw(keys[8], (MODEL_DIM, QUERY_HEAD_NUM * HEAD_DIM), (max(1, QUERY_HEAD_NUM * HEAD_DIM * 16 // STREAM)) ** -0.5, 1.0, ((0, 8), (1, 4)))
    gain_query = jnp.clip(1.0 + 0.18 * jax.random.normal(keys[9], (HEAD_DIM,), jnp.float32), 0.1, 1.9)
    key_norm_gain = jnp.clip(1.0 + 0.18 * jax.random.normal(keys[10], (HEAD_DIM,), jnp.float32), 0.1, 1.9)
    gain_moe = jnp.clip(1.0 + 0.18 * jax.random.normal(keys[11], (MODEL_DIM,), jnp.float32), 0.1, 1.9)
    router = bell_draw(keys[12], (MODEL_DIM, EXPERTS), (4 * MODEL_DIM) ** -0.5, 0.0625)
    w_gate = bell_draw(keys[13], (EXPERTS, MODEL_DIM, F), MODEL_DIM ** -0.5, 0.125, ((0, 32),))
    w_up = bell_draw(keys[14], (EXPERTS, MODEL_DIM, F), MODEL_DIM ** -0.5, 0.125, ((0, 32),))
    w_down = bell_draw(keys[15], (EXPERTS, F, MODEL_DIM), (F // 16) ** -0.5, 0.875, ((0, 32),))
    return dict(tokens=tokens, cotangent=cotangent, routes=routes, doc_ids=doc_ids, gain_attn=gain_attn, w_query=w_query, key_weight=key_weight, value_weight=value_weight, w_out=w_out, gain_query=gain_query, key_norm_gain=key_norm_gain, gain_moe=gain_moe, router=router, w_gate=w_gate, w_up=w_up, w_down=w_down)


@jax.custom_vjp
def reduced_precision(v):
    return lax.optimization_barrier(v.astype(jnp.bfloat16)).astype(jnp.float32)

@jax.custom_vjp
def reduced_backward(v):
    return v

def low_keep(v):
    return (reduced_precision(v), None)

def low_pass(kept, grad):
    return (grad,)

def back_keep(v):
    return (v, None)

def back_low(kept, grad):
    return (reduced_precision(grad),)
reduced_precision.defvjp(low_keep, low_pass)
reduced_backward.defvjp(back_keep, back_low)
highest_precision = lax.Precision.HIGHEST
theta_base = 1000000.0
norm_eps = 1e-06
masked_score = -1e+30

def root_mean_norm(row_block, gain_row):
    return row_block * lax.rsqrt(lax.optimization_barrier(jnp.mean(row_block * row_block, axis=-1, keepdims=True)) + norm_eps) * gain_row

def rotary_apply(row_block, cosine_lookup, sine_lookup):
    half_width = row_block.shape[-1] // 2
    turned = jnp.concatenate([-row_block[..., half_width:], row_block[..., :half_width]], axis=-1)
    return row_block * cosine_lookup + turned * sine_lookup

def rope_tables(positions, head_width):
    half_width = head_width // 2
    frequency = theta_base ** (-2.0 * jnp.arange(half_width, dtype=jnp.int32).astype(jnp.float32) / head_width)
    angles = positions.astype(jnp.float32)[:, None] * frequency[None, :]
    cosine_lookup = jnp.cos(angles)
    sine_lookup = jnp.sin(angles)
    return (jnp.concatenate([cosine_lookup, cosine_lookup], axis=-1), jnp.concatenate([sine_lookup, sine_lookup], axis=-1))

def doc_starts(ids_row):
    doc_range = jnp.arange(DOCS, dtype=jnp.int32)
    member = ids_row[:, None] == doc_range[None, :]
    totals = lax.optimization_barrier(jnp.sum(member.astype(jnp.int32), axis=0)).astype(jnp.int32)
    starts = (jnp.cumsum(totals) - totals).astype(jnp.int32)
    return lax.optimization_barrier(jnp.sum(jnp.where(member, starts[None, :], 0), axis=1)).astype(jnp.int32)

def expert_slots(route_ids):
    grouped_heads = route_ids.reshape(N_FSDP, MB_ROWS * TOPK)
    one_hot = (grouped_heads[:, :, None] == jnp.arange(EXPERTS, dtype=jnp.int32)[None, None, :]).astype(jnp.int32)
    ranks = lax.optimization_barrier(jnp.sum((jnp.cumsum(one_hot, axis=1).astype(jnp.int32) - one_hot) * one_hot, axis=2)).astype(jnp.int32)
    slot_index = jnp.arange(N_FSDP, dtype=jnp.int32)[:, None] * CAP + ranks
    return (grouped_heads * (N_FSDP * CAP) + slot_index).reshape(-1).astype(jnp.int32)

def stream_forward(stream_tokens, route_ids, ids_row, gain_attn, w_query, key_weight, value_weight, w_out, gain_query, key_norm_gain, gain_moe, router, w_gate, w_up, w_down):
    sequence_length = stream_tokens.shape[0]
    group_width = QUERY_HEAD_NUM // KV_HEAD_TOTAL
    index_row = jnp.arange(sequence_length, dtype=jnp.int32)
    start_row = doc_starts(ids_row)
    cosine_lookup, sine_lookup = rope_tables(index_row - start_row, HEAD_DIM)
    normed_reduced = reduced_precision(root_mean_norm(stream_tokens, gain_attn))
    query_pre = reduced_backward(jnp.dot(normed_reduced, w_query, precision=highest_precision))
    key_before_norm = reduced_backward(jnp.dot(normed_reduced, key_weight, precision=highest_precision))
    value_reduced = reduced_precision(reduced_backward(jnp.dot(normed_reduced, value_weight, precision=highest_precision))).reshape(sequence_length, KV_HEAD_TOTAL, HEAD_DIM)
    query_low = reduced_precision(rotary_apply(root_mean_norm(query_pre.reshape(sequence_length, QUERY_HEAD_NUM, HEAD_DIM), gain_query), cosine_lookup[:, None, :], sine_lookup[:, None, :]))
    key_reduced = reduced_precision(rotary_apply(root_mean_norm(key_before_norm.reshape(sequence_length, KV_HEAD_TOTAL, HEAD_DIM), key_norm_gain), cosine_lookup[:, None, :], sine_lookup[:, None, :]))
    query_tile_rows = math.gcd(sequence_length, 512)
    block_count = sequence_length // query_tile_rows

    def attend_block(pieces):
        query_portion, index_part, start_part = pieces
        grouped_heads = query_portion.reshape(query_tile_rows, KV_HEAD_TOTAL, group_width, HEAD_DIM)
        scores = reduced_backward(jnp.einsum('qhgd,khd->hgqk', grouped_heads, key_reduced, precision=highest_precision) * HEAD_DIM ** (-0.5))
        allowed = (index_row[None, :] >= start_part[:, None]) & (index_row[None, :] <= index_part[:, None])
        scores = jnp.where(allowed, scores, masked_score)
        row_peak = lax.optimization_barrier(jnp.max(scores, axis=-1, keepdims=True))
        weights = jnp.where(allowed, jnp.exp(scores - row_peak), 0.0)
        prob_low = reduced_precision(weights / lax.optimization_barrier(jnp.sum(weights, axis=-1, keepdims=True)))
        mixed_heads = jnp.einsum('hgqk,khd->qhgd', prob_low, value_reduced, precision=highest_precision)
        return mixed_heads.reshape(query_tile_rows, QUERY_HEAD_NUM * HEAD_DIM)
    heads_out = lax.map(jax.checkpoint(attend_block), (query_low.reshape(block_count, query_tile_rows, QUERY_HEAD_NUM, HEAD_DIM), index_row.reshape(block_count, query_tile_rows), start_row.reshape(block_count, query_tile_rows)))
    heads_low = reduced_backward(reduced_precision(heads_out.reshape(sequence_length, QUERY_HEAD_NUM * HEAD_DIM)))
    attn_out = reduced_backward(jnp.dot(heads_low, w_out.T, precision=highest_precision))
    middle = stream_tokens + attn_out
    moe_low = reduced_precision(root_mean_norm(middle, gain_moe))
    logits = jnp.dot(moe_low, router, precision=highest_precision)
    chosen = jnp.take_along_axis(logits, route_ids, axis=1)
    gate_weights = jax.nn.softmax(chosen, axis=-1)
    slots_total = N_FSDP * CAP
    flat_slot = expert_slots(route_ids)
    pair_count = sequence_length * TOPK
    pair_of = jnp.full((EXPERTS * slots_total,), pair_count, jnp.int32).at[flat_slot].set(jnp.arange(pair_count, dtype=jnp.int32))
    token_of = (jnp.minimum(pair_of, pair_count - 1) // TOPK).astype(jnp.int32)
    slot_valid = (pair_of < pair_count).astype(jnp.float32)

    def run_expert(pieces):
        gate_one, up_one, down_one, token_one, valid_one = pieces
        rows_in = reduced_backward(moe_low[token_one]) * valid_one[:, None]
        gate_pre = reduced_backward(jnp.dot(rows_in, gate_one, precision=highest_precision))
        up_pre = reduced_backward(jnp.dot(rows_in, up_one, precision=highest_precision))
        hidden_low = reduced_precision(jax.nn.silu(gate_pre) * up_pre)
        return reduced_backward(reduced_precision(jnp.dot(hidden_low, down_one, precision=highest_precision)))
    expert_out = lax.map(jax.checkpoint(run_expert), (w_gate, w_up, w_down, token_of.reshape(EXPERTS, slots_total), slot_valid.reshape(EXPERTS, slots_total)))
    pair_out = expert_out.reshape(EXPERTS * slots_total, MODEL_DIM)[flat_slot].reshape(sequence_length, TOPK, MODEL_DIM)
    return middle + jnp.einsum('sk,skd->sd', gate_weights, pair_out, precision=highest_precision)

def reorder(array):
    return array.reshape(N_FSDP, MICRO, MB_ROWS, array.shape[-1]).transpose(1, 0, 2, 3).reshape(MICRO, STREAM, array.shape[-1])

def forward_all(tokens, gain_attn, w_query, key_weight, value_weight, w_out, gain_query, key_norm_gain, gain_moe, router, w_gate, w_up, w_down, routes, doc_ids):

    def one_stream(unused, pieces):
        stream_tokens, route_ids, ids_row = pieces
        return (unused, stream_forward(stream_tokens, route_ids, ids_row, gain_attn, w_query, key_weight, value_weight, w_out, gain_query, key_norm_gain, gain_moe, router, w_gate, w_up, w_down))
    unused, outputs = lax.scan(one_stream, jnp.zeros((), jnp.float32), (reorder(tokens), reorder(routes), doc_ids))
    return outputs.reshape(MICRO, N_FSDP, MB_ROWS, MODEL_DIM).transpose(1, 0, 2, 3).reshape(TOKENS, MODEL_DIM)

def reference(tokens, cotangent, routes, doc_ids, gain_attn, w_query, key_weight, value_weight, w_out, gain_query, key_norm_gain, gain_moe, router, w_gate, w_up, w_down):
    floats = tuple((array.astype(jnp.float32) for array in (tokens, gain_attn, w_query, key_weight, value_weight, w_out, gain_query, key_norm_gain, gain_moe, router, w_gate, w_up, w_down)))

    def closed(*values):
        return forward_all(*values, routes, doc_ids)
    block_out, pull = jax.vjp(closed, *floats)
    grads = pull(cotangent.astype(jnp.float32))
    return (block_out.astype(jnp.bfloat16), grads[0].astype(jnp.bfloat16), grads[1], grads[2], grads[3], grads[4], grads[5], grads[6], grads[7], grads[8], grads[9], grads[10], grads[11], grads[12])
```

```python
import functools
import math

import jax
import jax.numpy as jnp
from jax import lax
from jax.experimental import pallas as pl
from jax.experimental.pallas import tpu as pltpu
from jax.sharding import PartitionSpec as P

TOPK = 8
DOCS = 4


theta_base = 1000000.0
norm_eps = 1e-06
masked_score = -1e30
highest_precision = lax.Precision.HIGHEST


def root_mean_norm(row_block, gain_row):
    return (
        row_block
        * lax.rsqrt(jnp.mean(row_block * row_block, axis=-1, keepdims=True) + norm_eps)
        * gain_row
    )


def rotary_apply(row_block, cosine_lookup, sine_lookup):
    half_width = row_block.shape[-1] // 2
    turned = jnp.concatenate([-row_block[..., half_width:], row_block[..., :half_width]], axis=-1)
    return row_block * cosine_lookup + turned * sine_lookup


def rope_tables(positions, head_width):
    half_width = head_width // 2
    frequency = theta_base ** (
        -2.0 * jnp.arange(half_width, dtype=jnp.int32).astype(jnp.float32) / head_width
    )
    angles = positions.astype(jnp.float32)[:, None] * frequency[None, :]
    cosine_lookup = jnp.cos(angles)
    sine_lookup = jnp.sin(angles)
    return (
        jnp.concatenate([cosine_lookup, cosine_lookup], axis=-1),
        jnp.concatenate([sine_lookup, sine_lookup], axis=-1),
    )


def swiglu(gate_pre, up_pre):
    return jax.nn.silu(gate_pre) * up_pre


def dot_first(left_side, right_side):
    return lax.dot_general(
        left_side, right_side, (((0,), (0,)), ((), ())), preferred_element_type=jnp.float32
    )


def dot_last(left_side, right_side):
    return lax.dot_general(
        left_side, right_side, (((1,), (1,)), ((), ())), preferred_element_type=jnp.float32
    )


def gather_weights(w_query, key_weight, value_weight, w_out):
    return (
        lax.all_gather(w_query, "fsdp", axis=0, tiled=True),
        lax.all_gather(key_weight, "fsdp", axis=0, tiled=True),
        lax.all_gather(value_weight, "fsdp", axis=0, tiled=True),
        lax.all_gather(w_out, "fsdp", axis=0, tiled=True),
    )


def gather_keys(keys_low, values_low):
    return (
        lax.all_gather(keys_low, "fsdp", axis=0, tiled=True),
        lax.all_gather(values_low, "fsdp", axis=0, tiled=True),
    )


def send_rows(buffer):
    return lax.all_to_all(buffer, "fsdp", split_axis=0, concat_axis=0, tiled=True)


def return_rows(buffer):
    return lax.all_to_all(buffer, "fsdp", split_axis=0, concat_axis=0, tiled=True)


def to_heads(per_token, kv_local, group_width):
    token_count, head_total, head_width = per_token.shape
    grouped_heads = per_token.reshape(token_count, kv_local, group_width, head_width)
    return grouped_heads.transpose(1, 2, 0, 3).reshape(
        kv_local, group_width * token_count, head_width
    )


def to_tokens(per_head, group_width):
    kv_local, row_count, head_width = per_head.shape
    token_count = row_count // group_width
    grouped_heads = per_head.reshape(kv_local, group_width, token_count, head_width)
    return grouped_heads.transpose(2, 0, 1, 3).reshape(
        token_count, kv_local * group_width * head_width
    )


def key_block(keys_all, key_start, block_keys, kv_local, head_width):
    return lax.dynamic_slice_in_dim(keys_all, key_start, block_keys, 0).reshape(
        block_keys, kv_local, head_width
    )


def block_scores(queries, keys_part, key_start, query_index, query_start):
    head_width = queries.shape[-1]
    scores = jnp.einsum(
        "hrd,khd->hrk", queries, keys_part, preferred_element_type=jnp.float32
    ) * head_width ** (-0.5)
    key_index = key_start + jnp.arange(keys_part.shape[0])
    allowed = (key_index[None, :] >= query_start[:, None]) & (
        key_index[None, :] <= query_index[:, None]
    )
    return (jnp.where(allowed[None], scores, masked_score), allowed)


def attend_forward(queries, keys_all, values_all, query_index, query_start, block_keys):
    kv_local, row_count, head_width = queries.shape
    lowest_block = jnp.min(query_start) // block_keys
    highest_block = jnp.max(query_index) // block_keys + 1

    def visit_block(block_index, running):
        run_peak, run_total, run_acc = running
        key_start = block_index * block_keys
        keys_part = key_block(keys_all, key_start, block_keys, kv_local, head_width)
        values_part = key_block(values_all, key_start, block_keys, kv_local, head_width)
        scores, allowed = block_scores(queries, keys_part, key_start, query_index, query_start)
        new_peak = jnp.maximum(run_peak, jnp.max(scores, axis=-1))
        weights = jnp.where(allowed[None], jnp.exp(scores - new_peak[..., None]), 0.0)
        factor = jnp.exp(run_peak - new_peak)
        run_total = run_total * factor + jnp.sum(weights, axis=-1)
        run_acc = run_acc * factor[..., None] + jnp.einsum(
            "hrk,khd->hrd",
            weights.astype(jnp.bfloat16),
            values_part,
            preferred_element_type=jnp.float32,
        )
        return (new_peak, run_total, run_acc)

    start_state = (
        jnp.full((kv_local, row_count), masked_score, jnp.float32),
        jnp.zeros((kv_local, row_count), jnp.float32),
        jnp.zeros((kv_local, row_count, head_width), jnp.float32),
    )
    run_peak, run_total, run_acc = lax.fori_loop(
        lowest_block, highest_block, visit_block, start_state
    )
    return (run_acc / run_total[..., None], run_peak + jnp.log(run_total))


def attend_backward(
    queries,
    keys_all,
    values_all,
    query_index,
    query_start,
    block_keys,
    outputs,
    log_total,
    grad_low,
):
    kv_local, row_count, head_width = queries.shape
    key_count = keys_all.shape[0]
    score_scale = head_width ** (-0.5)
    row_delta = jnp.sum(grad_low.astype(jnp.float32) * outputs, axis=-1)
    lowest_block = jnp.min(query_start) // block_keys
    highest_block = jnp.max(query_index) // block_keys + 1

    def visit_block(block_index, running):
        query_acc, key_acc, value_acc = running
        key_start = block_index * block_keys
        keys_part = key_block(keys_all, key_start, block_keys, kv_local, head_width)
        values_part = key_block(values_all, key_start, block_keys, kv_local, head_width)
        scores, allowed = block_scores(queries, keys_part, key_start, query_index, query_start)
        prob_block = jnp.where(allowed[None], jnp.exp(scores - log_total[..., None]), 0.0)
        prob_grad = jnp.einsum(
            "hrd,khd->hrk", grad_low, values_part, preferred_element_type=jnp.float32
        )
        score_grad = (prob_block * (prob_grad - row_delta[..., None])).astype(jnp.bfloat16)
        query_acc = (
            query_acc
            + jnp.einsum("hrk,khd->hrd", score_grad, keys_part, preferred_element_type=jnp.float32)
            * score_scale
        )
        key_part = (
            jnp.einsum("hrk,hrd->khd", score_grad, queries, preferred_element_type=jnp.float32)
            * score_scale
        )
        value_part = jnp.einsum(
            "hrk,hrd->khd",
            prob_block.astype(jnp.bfloat16),
            grad_low,
            preferred_element_type=jnp.float32,
        )
        key_acc = lax.dynamic_update_slice_in_dim(
            key_acc, key_part.reshape(block_keys, kv_local * head_width), key_start, 0
        )
        value_acc = lax.dynamic_update_slice_in_dim(
            value_acc, value_part.reshape(block_keys, kv_local * head_width), key_start, 0
        )
        return (query_acc, key_acc, value_acc)

    start_state = (
        jnp.zeros((kv_local, row_count, head_width), jnp.float32),
        jnp.zeros((key_count, kv_local * head_width), jnp.float32),
        jnp.zeros((key_count, kv_local * head_width), jnp.float32),
    )
    return lax.fori_loop(lowest_block, highest_block, visit_block, start_state)


def body(
    tokens,
    cotangent,
    routes,
    doc_ids,
    gain_attn,
    w_query,
    key_weight,
    value_weight,
    w_out,
    gain_query,
    key_norm_gain,
    gain_moe,
    router,
    w_gate,
    w_up,
    w_down,
):
    shard_count = lax.axis_size("fsdp")
    group_count = lax.axis_size("tp")
    shard_index = lax.axis_index("fsdp")
    group_index = lax.axis_index("tp")
    full_tokens, full_grads = (
        lax.all_gather(tokens, "tp", axis=1, tiled=True),
        lax.all_gather(cotangent, "tp", axis=1, tiled=True),
    )
    slice_width = tokens.shape[1]
    model_width = full_tokens.shape[1]
    micro_count, micro_rows = doc_ids.shape
    head_width = gain_query.shape[0]
    query_local = w_query.shape[1] // head_width
    kv_local = key_weight.shape[1] // head_width
    group_width = query_local // kv_local
    expert_total = router.shape[1]
    capacity = max(2, 2 * micro_rows * TOPK // expert_total)
    slot_total = shard_count * capacity
    pair_total = micro_rows * TOPK
    block_keys = micro_rows * math.gcd(shard_count, max(1, 512 // micro_rows))
    doc_range = jnp.arange(DOCS)
    expert_range = jnp.arange(expert_total)
    local_counts = jnp.sum((doc_ids[:, :, None] == doc_range).astype(jnp.float32), axis=1)
    doc_totals = lax.psum(local_counts, "fsdp")
    doc_begin = (jnp.cumsum(doc_totals, axis=1) - doc_totals).astype(jnp.int32)
    gate_expert = w_gate[0]
    up_expert = w_up[0]
    down_expert = w_down[0]
    router_wide = router.astype(jnp.float32)
    query_acc = jnp.zeros((model_width, query_local * head_width), jnp.float32)
    key_acc = jnp.zeros((model_width, kv_local * head_width), jnp.float32)
    value_acc = jnp.zeros((model_width, kv_local * head_width), jnp.float32)
    out_acc = jnp.zeros((model_width, query_local * head_width), jnp.float32)
    gate_acc = jnp.zeros(gate_expert.shape, jnp.float32)
    up_acc = jnp.zeros(up_expert.shape, jnp.float32)
    down_acc = jnp.zeros(down_expert.shape, jnp.float32)
    router_acc = jnp.zeros(router.shape, jnp.float32)
    gain_attn_acc = jnp.zeros(gain_attn.shape, jnp.float32)
    gain_moe_acc = jnp.zeros(gain_moe.shape, jnp.float32)
    gain_query_acc = jnp.zeros(gain_query.shape, jnp.float32)
    gain_key_acc = jnp.zeros(key_norm_gain.shape, jnp.float32)
    out_parts = []
    grad_parts = []
    for micro_index in range(micro_count):
        row_begin = micro_index * micro_rows
        token_block = full_tokens[row_begin : row_begin + micro_rows].astype(jnp.float32)
        ids_now = doc_ids[micro_index]
        query_index = shard_index * micro_rows + jnp.arange(micro_rows)
        query_start = jnp.sum(
            jnp.where(ids_now[:, None] == doc_range, doc_begin[micro_index][None, :], 0), axis=1
        )
        cosine_lookup, sine_lookup = rope_tables(query_index - query_start, head_width)
        gathered = gather_weights(w_query, key_weight, value_weight, w_out)
        normed, norm_pull = jax.vjp(root_mean_norm, token_block, gain_attn)
        normed_reduced = normed.astype(jnp.bfloat16)
        query_pre = jnp.dot(normed_reduced, gathered[0], preferred_element_type=jnp.float32)
        key_before_norm = jnp.dot(normed_reduced, gathered[1], preferred_element_type=jnp.float32)
        value_reduced = jnp.dot(
            normed_reduced, gathered[2], preferred_element_type=jnp.float32
        ).astype(jnp.bfloat16)

        def shape_heads(query_raw, key_raw, query_gain, key_gain):
            query_heads = rotary_apply(
                root_mean_norm(query_raw.reshape(micro_rows, query_local, head_width), query_gain),
                cosine_lookup[:, None, :],
                sine_lookup[:, None, :],
            )
            key_heads = rotary_apply(
                root_mean_norm(key_raw.reshape(micro_rows, kv_local, head_width), key_gain),
                cosine_lookup[:, None, :],
                sine_lookup[:, None, :],
            )
            return (query_heads, key_heads)

        (query_heads, key_heads), heads_pull = jax.vjp(
            shape_heads, query_pre, key_before_norm, gain_query, key_norm_gain
        )
        queries = to_heads(query_heads.astype(jnp.bfloat16), kv_local, group_width)
        keys_low = key_heads.reshape(micro_rows, kv_local * head_width).astype(jnp.bfloat16)
        keys_all, values_all = gather_keys(keys_low, value_reduced)
        row_index = jnp.tile(query_index, group_width)
        row_start = jnp.tile(query_start, group_width)
        head_out, log_total = attend_forward(
            queries, keys_all, values_all, row_index, row_start, block_keys
        )
        heads_low = to_tokens(head_out, group_width).astype(jnp.bfloat16)
        attn_part = dot_last(heads_low, gathered[3])
        middle = token_block + lax.psum(attn_part.astype(jnp.bfloat16), "tp").astype(jnp.float32)
        moe_normed, moe_pull = jax.vjp(root_mean_norm, middle, gain_moe)
        moe_low = moe_normed.astype(jnp.bfloat16)
        logits = jnp.dot(moe_low, router, preferred_element_type=jnp.float32)
        routes_now = routes[row_begin : row_begin + micro_rows]
        route_match = routes_now[:, :, None] == expert_range
        chosen = jnp.sum(jnp.where(route_match, logits[:, None, :], 0.0), axis=-1)
        gate_weights, softmax_pull = jax.vjp(jax.nn.softmax, chosen)
        mine = routes_now % group_count == group_index
        pair_target = jnp.where(mine, routes_now // group_count, shard_count).reshape(pair_total)
        target_hot = (pair_target[:, None] == jnp.arange(shard_count)).astype(jnp.int32)
        pair_rank = jnp.sum((jnp.cumsum(target_hot, axis=0) - target_hot) * target_hot, axis=1)
        pair_slot = jnp.where(
            pair_target < shard_count, pair_target * capacity + pair_rank, slot_total
        )
        slot_pair = (
            jnp.full((slot_total + 1,), pair_total, jnp.int32)
            .at[pair_slot]
            .set(jnp.arange(pair_total, dtype=jnp.int32))[:slot_total]
        )
        slot_token = slot_pair // TOPK
        slot_grid = pair_slot.reshape(micro_rows, TOPK)
        padded_low = jnp.concatenate([moe_low, jnp.zeros((1, model_width), jnp.bfloat16)], axis=0)
        received = send_rows(
            padded_low[slot_token].reshape(shard_count, capacity, model_width)
        ).reshape(slot_total, model_width)
        gate_pre = jnp.dot(received, gate_expert, preferred_element_type=jnp.float32)
        up_pre = jnp.dot(received, up_expert, preferred_element_type=jnp.float32)
        hidden, swiglu_pull = jax.vjp(swiglu, gate_pre, up_pre)
        hidden_low = hidden.astype(jnp.bfloat16)
        expert_out = jnp.dot(hidden_low, down_expert, preferred_element_type=jnp.float32).astype(
            jnp.bfloat16
        )
        returned = return_rows(expert_out.reshape(shard_count, capacity, model_width)).reshape(
            slot_total, model_width
        )
        padded_out = jnp.concatenate([returned, jnp.zeros((1, model_width), jnp.bfloat16)], axis=0)
        moe_part = jnp.zeros((micro_rows, model_width), jnp.float32)
        for pick_index in range(TOPK):
            moe_part = moe_part + gate_weights[:, pick_index : pick_index + 1] * padded_out[
                slot_grid[:, pick_index]
            ].astype(jnp.float32)
        moe_share = lax.psum_scatter(
            moe_part.astype(jnp.bfloat16), "tp", scatter_dimension=1, tiled=True
        ).astype(jnp.float32)
        middle_slice = lax.dynamic_slice_in_dim(middle, group_index * slice_width, slice_width, 1)
        out_parts.append((middle_slice + moe_share).astype(jnp.bfloat16))
        grad_block = full_grads[row_begin : row_begin + micro_rows].astype(jnp.float32)
        gate_columns = []
        for pick_index in range(TOPK):
            gate_columns.append(
                jnp.sum(
                    grad_block * padded_out[slot_grid[:, pick_index]].astype(jnp.float32), axis=1
                )
            )
        gates_grad = jnp.stack(gate_columns, axis=1)
        flat_gates = jnp.concatenate(
            [gate_weights.reshape(pair_total), jnp.zeros((1,), jnp.float32)]
        )
        padded_grad = jnp.concatenate(
            [grad_block, jnp.zeros((1, model_width), jnp.float32)], axis=0
        )
        send_grad = (padded_grad[slot_token] * flat_gates[slot_pair][:, None]).astype(jnp.bfloat16)
        received_grad = send_rows(send_grad.reshape(shard_count, capacity, model_width)).reshape(
            slot_total, model_width
        )
        hidden_grad = dot_last(received_grad, down_expert)
        down_acc = down_acc + dot_first(hidden_low, received_grad)
        gate_pre_grad, up_pre_grad = swiglu_pull(hidden_grad)
        gate_pre_low = gate_pre_grad.astype(jnp.bfloat16)
        up_pre_low = up_pre_grad.astype(jnp.bfloat16)
        gate_acc = gate_acc + dot_first(received, gate_pre_low)
        up_acc = up_acc + dot_first(received, up_pre_low)
        rows_back = (dot_last(gate_pre_low, gate_expert) + dot_last(up_pre_low, up_expert)).astype(
            jnp.bfloat16
        )
        back_rows = return_rows(rows_back.reshape(shard_count, capacity, model_width)).reshape(
            slot_total, model_width
        )
        padded_back = jnp.concatenate(
            [back_rows, jnp.zeros((1, model_width), jnp.bfloat16)], axis=0
        )
        moe_grad = jnp.zeros((micro_rows, model_width), jnp.float32)
        for pick_index in range(TOPK):
            moe_grad = moe_grad + padded_back[slot_grid[:, pick_index]].astype(jnp.float32)
        (chosen_grad,) = softmax_pull(gates_grad)
        logit_grad = jnp.sum(jnp.where(route_match, chosen_grad[:, :, None], 0.0), axis=1)
        router_acc = router_acc + lax.dot_general(
            moe_low.astype(jnp.float32),
            logit_grad,
            (((0,), (0,)), ((), ())),
            precision=highest_precision,
        )
        moe_grad = moe_grad + lax.dot_general(
            logit_grad, router_wide, (((1,), (1,)), ((), ())), precision=highest_precision
        )
        middle_part, gain_moe_part = moe_pull(moe_grad)
        gain_moe_acc = gain_moe_acc + gain_moe_part
        middle_grad = grad_block + lax.psum(middle_part.astype(jnp.bfloat16), "tp").astype(
            jnp.float32
        )
        middle_low = middle_grad.astype(jnp.bfloat16)
        gathered_back = gather_weights(w_query, key_weight, value_weight, w_out)
        out_acc = out_acc + dot_first(middle_low, heads_low)
        heads_grad = jnp.dot(middle_low, gathered_back[3], preferred_element_type=jnp.float32)
        grad_low = to_heads(
            heads_grad.reshape(micro_rows, query_local, head_width).astype(jnp.bfloat16),
            kv_local,
            group_width,
        )
        query_side, key_side_all, value_side_all = attend_backward(
            queries,
            keys_all,
            values_all,
            row_index,
            row_start,
            block_keys,
            head_out,
            log_total,
            grad_low,
        )
        key_side, value_side = (
            lax.psum_scatter(
                key_side_all.astype(jnp.bfloat16), "fsdp", scatter_dimension=0, tiled=True
            ).astype(jnp.float32),
            lax.psum_scatter(
                value_side_all.astype(jnp.bfloat16), "fsdp", scatter_dimension=0, tiled=True
            ).astype(jnp.float32),
        )
        query_pre_grad, key_pre_grad, gain_query_part, gain_key_part = heads_pull(
            (
                to_tokens(query_side, group_width).reshape(micro_rows, query_local, head_width),
                key_side.reshape(micro_rows, kv_local, head_width),
            )
        )
        gain_query_acc = gain_query_acc + gain_query_part
        gain_key_acc = gain_key_acc + gain_key_part
        query_pre_low = query_pre_grad.astype(jnp.bfloat16)
        key_pre_low = key_pre_grad.astype(jnp.bfloat16)
        value_pre_low = value_side.astype(jnp.bfloat16)
        query_acc = query_acc + dot_first(normed_reduced, query_pre_low)
        key_acc = key_acc + dot_first(normed_reduced, key_pre_low)
        value_acc = value_acc + dot_first(normed_reduced, value_pre_low)
        normed_grad = (
            dot_last(query_pre_low, gathered_back[0])
            + dot_last(key_pre_low, gathered_back[1])
            + dot_last(value_pre_low, gathered_back[2])
        )
        token_part, gain_attn_part = norm_pull(normed_grad)
        gain_attn_acc = gain_attn_acc + gain_attn_part
        token_share = lax.psum_scatter(
            token_part.astype(jnp.bfloat16), "tp", scatter_dimension=1, tiled=True
        ).astype(jnp.float32)
        grad_slice = lax.dynamic_slice_in_dim(
            middle_grad, group_index * slice_width, slice_width, 1
        )
        grad_parts.append((grad_slice + token_share).astype(jnp.bfloat16))
    weight_sums = (
        lax.psum_scatter(
            query_acc.astype(jnp.bfloat16), "fsdp", scatter_dimension=0, tiled=True
        ).astype(jnp.float32),
        lax.psum_scatter(
            key_acc.astype(jnp.bfloat16), "fsdp", scatter_dimension=0, tiled=True
        ).astype(jnp.float32),
        lax.psum_scatter(
            value_acc.astype(jnp.bfloat16), "fsdp", scatter_dimension=0, tiled=True
        ).astype(jnp.float32),
        lax.psum_scatter(
            out_acc.astype(jnp.bfloat16), "fsdp", scatter_dimension=0, tiled=True
        ).astype(jnp.float32),
    )
    small_sums = lax.psum(
        (gain_attn_acc, gain_query_acc, gain_key_acc, gain_moe_acc, router_acc), ("fsdp", "tp")
    )
    return (
        jnp.concatenate(out_parts, axis=0),
        jnp.concatenate(grad_parts, axis=0),
        small_sums[0],
        weight_sums[0],
        weight_sums[1],
        weight_sums[2],
        weight_sums[3],
        small_sums[1],
        small_sums[2],
        small_sums[3],
        small_sums[4],
        gate_acc[None],
        up_acc[None],
        down_acc[None],
    )


MESH = pl.DeviceIdType.MESH


def place():
    f = lax.axis_index("fsdp")
    t = lax.axis_index("tp")
    return f // 2, f % 2, t // 2, t % 2


def device(z, x, y, c):
    return (z * 2 + x, y * 2 + c)


def greet(devices):
    barrier = pltpu.get_barrier_semaphore()
    total = 0
    for valid, where in devices:
        if valid is None:
            pl.semaphore_signal(barrier, inc=1, device_id=where, device_id_type=MESH)
            total = total + 1
        else:
            @pl.when(valid)
            def _():
                pl.semaphore_signal(barrier, inc=1, device_id=where, device_id_type=MESH)
            total = total + valid.astype(jnp.int32)
    pl.semaphore_wait(barrier, total)


def remote(src, dst, send, recv, where):
    return pltpu.make_async_remote_copy(
        src_ref=src, dst_ref=dst, send_sem=send, recv_sem=recv, device_id=where, device_id_type=MESH
    )


def gather_all_kernel(nz, x_ref, o_ref, lsem, s_p, s_u, s_d, s_x, s_y, s_dx, s_dy,
                      r_z, r_x, r_y, r_dx, r_dy, r_p):
    z, x, y, c = place()
    rows, cols = x_ref.shape
    half = rows // 2
    partner = device(z, x, y, 1 - c)
    xn = device(z, 1 - x, y, c)
    yn = device(z, x, 1 - y, c)
    up = device(z + 1, x, y, c)
    down = device(z - 1, x, y, c)
    greet([(None, partner), (None, xn), (None, yn), (z < nz - 1, up), (z > 0, down)])

    def block(zz, xx, yy, cc, part=None):
        start = (zz * 2 + xx) * rows
        size = rows
        if part is not None:
            start = start + part * half
            size = half
        return o_ref.at[pl.ds(pl.multiple_of(start, half), size),
                        pl.ds(pl.multiple_of((yy * 2 + cc) * cols, cols), cols)]

    own = pltpu.make_async_copy(x_ref, block(z, x, y, c), lsem)
    own.start()

    items = [(0, 0)]
    for dist in range(1, nz):
        items += [(dist, -1), (dist, 1)]

    def guard(item, fn):
        dist, side = item
        zz = z + side * dist
        if dist == 0:
            fn(zz)
        else:
            pl.when((zz >= 0) & (zz < nz))(lambda: fn(zz))

    def c_z(zz, src):
        dst = block(zz, x, y, c)
        return (remote(src, dst, s_u.at[zz], r_z.at[zz], up),
                remote(src, dst, s_d.at[zz], r_z.at[zz], down))

    def c_xy(zz, src):
        dst = block(zz, x, y, c)
        return (remote(src, dst, s_x.at[zz], r_x.at[zz], xn),
                remote(src, dst, s_y.at[zz], r_y.at[zz], yn))

    def c_p(zz, rel, src=None):
        xx = 1 - x if rel in (1, 3, 4) else x
        yy = 1 - y if rel in (2, 3, 4) else y
        part = {3: 0, 4: 1}.get(rel)
        dst = block(zz, xx, yy, c, part)
        k = zz * 5 + rel
        return remote(dst if src is None else src, dst, s_p.at[k], r_p.at[k], partner)

    def w_p(zz, rel):
        xx = 1 - x if rel in (1, 3, 4) else x
        yy = 1 - y if rel in (2, 3, 4) else y
        part = {3: 0, 4: 1}.get(rel)
        dst = block(zz, xx, yy, 1 - c, part)
        k = zz * 5 + rel
        return remote(dst, dst, s_p.at[k], r_p.at[k], partner)

    def c_diag(zz):
        a = block(zz, 1 - x, y, c, 0)
        b = block(zz, x, 1 - y, c, 1)
        return (remote(a, a, s_dy.at[zz], r_dy.at[zz], yn),
                remote(b, b, s_dx.at[zz], r_dx.at[zz], xn))

    def stage_a(item):
        dist, side = item

        def run(zz):
            src = x_ref if dist == 0 else block(zz, x, y, c)
            cu, cd = c_z(zz, src)
            if dist:
                cu.wait_recv()
            if side <= 0:
                pl.when(z < nz - 1)(cu.start)
            if dist == 0 or side > 0:
                pl.when(z > 0)(cd.start)
            for cc in c_xy(zz, src):
                cc.start()
            c_p(zz, 0, src).start()

        guard(item, run)

    def stage_b(item):
        def run(zz):
            cx, cy = c_xy(zz, block(zz, x, y, c))
            dy, dx = c_diag(zz)
            cx.wait_recv()
            dy.start()
            c_p(zz, 1).start()
            cy.wait_recv()
            dx.start()
            c_p(zz, 2).start()

        guard(item, run)

    def stage_c(item):
        def run(zz):
            dy, dx = c_diag(zz)
            dy.wait_recv()
            c_p(zz, 3).start()
            dx.wait_recv()
            c_p(zz, 4).start()

        guard(item, run)

    count = len(items)
    for k in range(count + 2):
        if k < count:
            stage_a(items[k])
        if 0 <= k - 1 < count:
            stage_b(items[k - 1])
        if 0 <= k - 2 < count:
            stage_c(items[k - 2])

    def finish(zz, carry):
        for rel in range(5):
            w_p(zz, rel).wait_recv()
            c_p(zz, rel).wait_send()
        cu, cd = c_z(zz, block(zz, x, y, c))
        pl.when((zz <= z) & (z < nz - 1))(cu.wait_send)
        pl.when((zz >= z) & (z > 0))(cd.wait_send)
        for cc in c_xy(zz, block(zz, x, y, c)) + c_diag(zz):
            cc.wait_send()
        return carry

    lax.fori_loop(0, nz, finish, 0)
    own.wait()


def gather_all(block, nz, collective_id):
    rows, cols = block.shape
    dma = pltpu.SemaphoreType.DMA
    return pl.pallas_call(
        functools.partial(gather_all_kernel, nz),
        out_shape=jax.ShapeDtypeStruct((rows * nz * 2, cols * 4), block.dtype),
        in_specs=[pl.BlockSpec(memory_space=pl.ANY)],
        out_specs=pl.BlockSpec(memory_space=pl.ANY),
        scratch_shapes=[dma] + [dma((5 * nz,))] + [dma((nz,))] * 6 + [dma((nz,))] * 5 + [dma((5 * nz,))],
        compiler_params=pltpu.CompilerParams(collective_id=collective_id, has_side_effects=True),
        name="gather_all",
    )(block)


def scatter_all_kernel(nz, p_ref, o_ref, w, lp, rx, rxd, ry, ryd, rz,
                       s_l, s_p, r_p, s_x, s_y, s_dx, s_dy, s_z, r_x, r_y, r_dx, r_dy, r_z):
    z, x, y, c = place()
    rows, cols = o_ref.shape
    half = rows // 2
    partner = device(z, x, y, 1 - c)
    xn = device(z, 1 - x, y, c)
    yn = device(z, x, 1 - y, c)
    up = device(z + 1, x, y, c)
    down = device(z - 1, x, y, c)
    greet([(None, partner), (None, xn), (None, yn), (z < nz - 1, up), (z > 0, down)])
    chunk = 64

    def block(zz, rel, cc):
        xx = 1 - x if rel in (1, 3) else x
        yy = 1 - y if rel in (2, 3) else y
        return p_ref.at[pl.ds(pl.multiple_of((zz * 2 + xx) * rows, rows), rows),
                        pl.ds(pl.multiple_of((yy * 2 + cc) * cols, cols), cols)]

    items = []
    for dist in range(nz - 1, 0, -1):
        items += [(dist, -1), (dist, 1)]
    items += [(0, 0)]

    def guard(item, fn):
        dist, side = item
        zz = z + side * dist
        if dist == 0:
            fn(zz)
        else:
            pl.when((zz >= 0) & (zz < nz))(lambda: fn(zz))

    def c_p(zz, rel):
        k = zz * 4 + rel
        return remote(block(zz, rel, 1 - c), lp.at[zz, rel], s_p.at[k], r_p.at[k], partner)

    def c_l(zz, rel):
        return pltpu.make_async_copy(block(zz, rel, c), w.at[zz, rel], s_l.at[zz * 4 + rel])

    def c_diag(zz):
        return (remote(w.at[zz, 3, pl.ds(0, half)], rxd.at[zz], s_dx.at[zz], r_dx.at[zz], xn),
                remote(w.at[zz, 3, pl.ds(half, half)], ryd.at[zz], s_dy.at[zz], r_dy.at[zz], yn))

    def c_xy(zz):
        return (remote(w.at[zz, 1], rx.at[zz], s_x.at[zz], r_x.at[zz], xn),
                remote(w.at[zz, 2], ry.at[zz], s_y.at[zz], r_y.at[zz], yn))

    def c_z(zz, slot, where):
        return remote(w.at[zz, 0], rz.at[slot], s_z.at[zz], r_z.at[slot], where)

    def add(dst, srcs, start, count):
        def step(i, carry):
            off = pl.multiple_of(i * chunk, chunk)
            here = pl.ds(pl.multiple_of(start + off, chunk), chunk)
            total = dst[here, :].astype(jnp.float32)
            for src in srcs:
                total = total + src[pl.ds(off, chunk), :].astype(jnp.float32)
            dst[here, :] = total.astype(dst.dtype)
            return carry
        lax.fori_loop(0, count // chunk, step, 0)

    def stage_0(item):
        def run(zz):
            for rel in (3, 1, 2, 0):
                c_p(zz, rel).start()
                c_l(zz, rel).start()
        guard(item, run)

    def stage_d(item):
        def run(zz):
            for rel in (3, 1, 2, 0):
                c_p(zz, rel).wait_recv()
                c_l(zz, rel).wait()
                add(w.at[zz, rel], [lp.at[zz, rel]], 0, rows)
                if rel == 3:
                    for cc in c_diag(zz):
                        cc.start()
        guard(item, run)

    def stage_e(item):
        def run(zz):
            dx, dy = c_diag(zz)
            cx, cy = c_xy(zz)
            dy.wait_recv()
            add(w.at[zz, 1], [ryd.at[zz]], half, half)
            cx.start()
            dx.wait_recv()
            add(w.at[zz, 2], [rxd.at[zz]], 0, half)
            cy.start()
        guard(item, run)

    def stage_f(item):
        dist, side = item

        def run(zz):
            cx, cy = c_xy(zz)
            cx.wait_recv()
            cy.wait_recv()
            if dist:
                add(w.at[zz, 0], [rx.at[zz], ry.at[zz]], 0, rows)
                has = z > 0 if side > 0 else z < nz - 1
                cz = c_z(zz, zz, up if side > 0 else down)

                @pl.when(has)
                def _():
                    cz.wait_recv()
                    add(w.at[zz, 0], [rz.at[zz]], 0, rows)
                if side > 0:
                    cz.start()
                else:
                    if dist == 1:
                        c_z(zz, nz, down).start()
                    else:
                        cz.start()
            else:
                below, above = c_z(zz, zz, up), c_z(zz, nz, down)

                def total(refs):
                    def step(i, carry):
                        here = pl.ds(pl.multiple_of(i * chunk, chunk), chunk)
                        acc = w[zz, 0, here, :].astype(jnp.float32)
                        for ref in refs:
                            acc = acc + ref[here, :].astype(jnp.float32)
                        o_ref[here, :] = acc
                        return carry
                    lax.fori_loop(0, rows // chunk, step, 0)

                pl.when(z > 0)(below.wait_recv)
                pl.when(z < nz - 1)(above.wait_recv)
                pl.when(z == 0)(lambda: total([rx.at[zz], ry.at[zz], rz.at[nz]]))
                pl.when(z == nz - 1)(lambda: total([rx.at[zz], ry.at[zz], rz.at[zz]]))
                pl.when((z > 0) & (z < nz - 1))(
                    lambda: total([rx.at[zz], ry.at[zz], rz.at[zz], rz.at[nz]]))
        guard(item, run)

    for item in items:
        stage_0(item)
    count = len(items)
    for k in range(count + 2):
        if k < count:
            stage_d(items[k])
        if 0 <= k - 1 < count:
            stage_e(items[k - 1])
        if 0 <= k - 2 < count:
            stage_f(items[k - 2])

    def finish(zz, carry):
        for rel in range(4):
            c_p(zz, rel).wait_send()
        for cc in c_diag(zz) + c_xy(zz):
            cc.wait_send()
        pl.when(zz != z)(c_z(zz, zz, up).wait_send)
        return carry

    lax.fori_loop(0, nz, finish, 0)


def scatter_all(partial, nz, collective_id):
    rows, cols = partial.shape[0] // (2 * nz), partial.shape[1] // 4
    half = rows // 2
    dma = pltpu.SemaphoreType.DMA
    kind = partial.dtype
    vm = pltpu.VMEM
    return pl.pallas_call(
        functools.partial(scatter_all_kernel, nz),
        out_shape=jax.ShapeDtypeStruct((rows, cols), jnp.float32),
        in_specs=[pl.BlockSpec(memory_space=pl.ANY)],
        out_specs=pl.BlockSpec(memory_space=pltpu.VMEM),
        scratch_shapes=[vm((nz, 4, rows, cols), kind), vm((nz, 4, rows, cols), kind),
                        vm((nz, rows, cols), kind), vm((nz, half, cols), kind),
                        vm((nz, rows, cols), kind), vm((nz, half, cols), kind),
                        vm((nz + 1, rows, cols), kind)]
        + [dma((4 * nz,))] * 3 + [dma((nz,))] * 5 + [dma((nz,))] * 4 + [dma((nz + 1,))],
        compiler_params=pltpu.CompilerParams(collective_id=collective_id, has_side_effects=True,
                                             vmem_limit_bytes=48 << 20),
        name="scatter_all",
    )(partial)


def z_items(nz, near_first):
    items = [(0, 0)] if near_first else []
    order = range(1, nz) if near_first else range(nz - 1, 0, -1)
    for dist in order:
        items += [(dist, -1), (dist, 1)]
    return items if near_first else items + [(0, 0)]


def z_guard(item, z, nz, fn):
    dist, side = item
    zz = z + side * dist
    if dist == 0:
        fn(zz)
    else:
        pl.when((zz >= 0) & (zz < nz))(lambda: fn(zz))


def gather_rows_kernel(nz, count, *refs):
    srcs, outs = refs[:count], refs[count : 2 * count]
    lsem, s_u, s_d, s_x, r_z, r_x = refs[2 * count :]
    z, x, y, c = place()
    xn, up, down = device(z, 1 - x, y, c), device(z + 1, x, y, c), device(z - 1, x, y, c)
    greet([(None, xn), (z < nz - 1, up), (z > 0, down)])

    def block(n, zz, xx):
        rows = srcs[n].shape[0]
        return outs[n].at[pl.ds(pl.multiple_of((zz * 2 + xx) * rows, rows), rows)]

    own = [pltpu.make_async_copy(srcs[n], block(n, z, x), lsem.at[n]) for n in range(count)]
    for copy in own:
        copy.start()
    items = z_items(nz, True)

    def copies(n, zz, src):
        dst = block(n, zz, x)
        k = n * nz + zz
        return (remote(src, dst, s_u.at[k], r_z.at[k], up),
                remote(src, dst, s_d.at[k], r_z.at[k], down),
                remote(src, dst, s_x.at[k], r_x.at[k], xn))

    for item in items:
        dist, side = item

        def run(zz):
            for n in range(count):
                src = srcs[n] if dist == 0 else block(n, zz, x)
                cu, cd, cx = copies(n, zz, src)
                if dist:
                    cu.wait_recv()
                if side <= 0:
                    pl.when(z < nz - 1)(cu.start)
                if side > 0 or dist == 0:
                    pl.when(z > 0)(cd.start)
                cx.start()

        z_guard(item, z, nz, run)

    def finish(zz, carry):
        for n in range(count):
            cu, cd, cx = copies(n, zz, block(n, zz, x))
            cx.wait_recv()
            cx.wait_send()
            pl.when((zz <= z) & (z < nz - 1))(cu.wait_send)
            pl.when((zz >= z) & (z > 0))(cd.wait_send)
        return carry

    lax.fori_loop(0, nz, finish, 0)
    for copy in own:
        copy.wait()


def gather_rows(blocks, nz, collective_id):
    count = len(blocks)
    dma = pltpu.SemaphoreType.DMA
    any_space = pl.BlockSpec(memory_space=pl.ANY)
    return pl.pallas_call(
        functools.partial(gather_rows_kernel, nz, count),
        out_shape=[
            jax.ShapeDtypeStruct((b.shape[0] * nz * 2,) + b.shape[1:], b.dtype) for b in blocks
        ],
        in_specs=[any_space] * count,
        out_specs=[any_space] * count,
        scratch_shapes=[dma((count,))] + [dma((count * nz,))] * 5,
        compiler_params=pltpu.CompilerParams(collective_id=collective_id, has_side_effects=True),
        name="gather_rows",
    )(*blocks)


def add_blocks(dst, srcs, start, count, out=None, chunk=64):
    target = dst if out is None else out

    def step(i, carry):
        off = pl.multiple_of(i * chunk, chunk)
        here = pl.ds(pl.multiple_of(start + off, chunk), chunk)
        total = dst[here, :].astype(jnp.float32)
        for src in srcs:
            total = total + src[pl.ds(off, chunk), :].astype(jnp.float32)
        target[here, :] = total.astype(target.dtype)
        return carry

    lax.fori_loop(0, count // chunk, step, 0)


def reduce_rows_kernel(nz, p_ref, o_ref, w, rx, rz, s_l, s_x, s_z, r_x, r_z):
    z, x, y, c = place()
    rows = o_ref.shape[0]
    xn, up, down = device(z, 1 - x, y, c), device(z + 1, x, y, c), device(z - 1, x, y, c)
    greet([(None, xn), (z < nz - 1, up), (z > 0, down)])

    def block(zz, xx):
        return p_ref.at[pl.ds(pl.multiple_of((zz * 2 + xx) * rows, rows), rows)]

    def c_x(zz):
        return remote(block(zz, 1 - x), rx.at[zz], s_x.at[zz], r_x.at[zz], xn)

    def c_l(zz):
        return pltpu.make_async_copy(block(zz, x), w.at[zz], s_l.at[zz])

    def c_z(zz, slot, where):
        return remote(w.at[zz], rz.at[slot], s_z.at[zz], r_z.at[slot], where)

    items = z_items(nz, False)

    def start(zz):
        c_x(zz).start()
        c_l(zz).start()

    for item in items:
        z_guard(item, z, nz, start)
    for item in items:
        dist, side = item

        def run(zz):
            c_l(zz).wait()
            c_x(zz).wait_recv()
            if dist:
                add_blocks(w.at[zz], [rx.at[zz]], 0, rows)
                cz = c_z(zz, zz, up if side > 0 else down)

                @pl.when(z > 0 if side > 0 else z < nz - 1)
                def _():
                    cz.wait_recv()
                    add_blocks(w.at[zz], [rz.at[zz]], 0, rows)

                (c_z(zz, nz, down) if side < 0 and dist == 1 else cz).start()
            else:
                pl.when(z > 0)(c_z(zz, zz, up).wait_recv)
                pl.when(z < nz - 1)(c_z(zz, nz, down).wait_recv)
                low, high = rz.at[zz], rz.at[nz]
                pl.when(z == 0)(lambda: add_blocks(w.at[zz], [rx.at[zz], high], 0, rows, o_ref))
                pl.when(z == nz - 1)(lambda: add_blocks(w.at[zz], [rx.at[zz], low], 0, rows, o_ref))
                pl.when((z > 0) & (z < nz - 1))(
                    lambda: add_blocks(w.at[zz], [rx.at[zz], low, high], 0, rows, o_ref)
                )

        z_guard(item, z, nz, run)

    def finish(zz, carry):
        c_x(zz).wait_send()
        pl.when(zz != z)(c_z(zz, zz, up).wait_send)
        return carry

    lax.fori_loop(0, nz, finish, 0)


def reduce_rows(partial, nz, collective_id):
    rows, cols = partial.shape[0] // (2 * nz), partial.shape[1]
    dma, vm, kind = pltpu.SemaphoreType.DMA, pltpu.VMEM, partial.dtype
    return pl.pallas_call(
        functools.partial(reduce_rows_kernel, nz),
        out_shape=jax.ShapeDtypeStruct((rows, cols), jnp.float32),
        in_specs=[pl.BlockSpec(memory_space=pl.ANY)],
        out_specs=pl.BlockSpec(memory_space=pltpu.VMEM),
        scratch_shapes=[vm((nz, rows, cols), kind), vm((nz, rows, cols), kind),
                        vm((nz + 1, rows, cols), kind)]
        + [dma((nz,))] * 4 + [dma((nz + 1,))],
        compiler_params=pltpu.CompilerParams(
            collective_id=collective_id, has_side_effects=True, vmem_limit_bytes=48 << 20
        ),
        name="reduce_rows",
    )(partial)


def gather_cols_kernel(x_ref, o_ref, lsem, s_p, s_y, r_p, r_y):
    z, x, y, c = place()
    cols = x_ref.shape[1]
    partner, yn = device(z, x, y, 1 - c), device(z, x, 1 - y, c)
    greet([(None, partner), (None, yn)])

    def block(yy, cc):
        return o_ref.at[:, pl.ds(pl.multiple_of((yy * 2 + cc) * cols, cols), cols)]

    own = pltpu.make_async_copy(x_ref, block(y, c), lsem)
    cy = remote(x_ref, block(y, c), s_y, r_y, yn)
    cp = remote(x_ref, block(y, c), s_p.at[0], r_p.at[0], partner)
    cf = remote(block(1 - y, c), block(1 - y, c), s_p.at[1], r_p.at[1], partner)
    cy.start()
    cp.start()
    own.start()
    cy.wait_recv()
    cf.start()
    cp.wait()
    cf.wait()
    cy.wait_send()
    own.wait()


def gather_cols(block, collective_id):
    dma = pltpu.SemaphoreType.DMA
    any_space = pl.BlockSpec(memory_space=pl.ANY)
    return pl.pallas_call(
        gather_cols_kernel,
        out_shape=jax.ShapeDtypeStruct((block.shape[0], block.shape[1] * 4), block.dtype),
        in_specs=[any_space],
        out_specs=any_space,
        scratch_shapes=[dma, dma((2,)), dma, dma((2,)), dma],
        compiler_params=pltpu.CompilerParams(collective_id=collective_id, has_side_effects=True),
        name="gather_cols",
    )(block)


def reduce_cols_kernel(p_ref, o_ref, w, rp, ry, s_l, s_p, s_y, r_p, r_y):
    z, x, y, c = place()
    rows, cols = o_ref.shape
    partner, yn = device(z, x, y, 1 - c), device(z, x, 1 - y, c)
    greet([(None, partner), (None, yn)])

    def block(yy, cc):
        return p_ref.at[:, pl.ds(pl.multiple_of((yy * 2 + cc) * cols, cols), cols)]

    sends = [remote(block(yy, 1 - c), rp.at[k], s_p.at[k], r_p.at[k], partner)
             for k, yy in enumerate((1 - y, y))]
    loads = [pltpu.make_async_copy(block(yy, c), w.at[k], s_l.at[k])
             for k, yy in enumerate((1 - y, y))]
    cy = remote(w.at[0], ry, s_y, r_y, yn)
    for k in range(2):
        sends[k].start()
        loads[k].start()
    loads[0].wait()
    sends[0].wait_recv()
    add_blocks(w.at[0], [rp.at[0]], 0, rows)
    cy.start()
    loads[1].wait()
    sends[1].wait_recv()
    cy.wait_recv()
    add_blocks(w.at[1], [rp.at[1], ry], 0, rows, o_ref)
    for k in range(2):
        sends[k].wait_send()
    cy.wait_send()


def reduce_cols(partial, collective_id):
    rows, cols = partial.shape[0], partial.shape[1] // 4
    dma, vm, kind = pltpu.SemaphoreType.DMA, pltpu.VMEM, partial.dtype
    return pl.pallas_call(
        reduce_cols_kernel,
        out_shape=jax.ShapeDtypeStruct((rows, cols), jnp.float32),
        in_specs=[pl.BlockSpec(memory_space=pl.ANY)],
        out_specs=pl.BlockSpec(memory_space=pltpu.VMEM),
        scratch_shapes=[vm((2, rows, cols), kind), vm((2, rows, cols), kind), vm((rows, cols), kind),
                        dma((2,)), dma((2,)), dma, dma((2,)), dma],
        compiler_params=pltpu.CompilerParams(
            collective_id=collective_id, has_side_effects=True, vmem_limit_bytes=24 << 20
        ),
        name="reduce_cols",
    )(partial)


def sum_cols_kernel(v_ref, o_ref, got, s, r):
    group = lax.axis_index("tp")
    shard = lax.axis_index("fsdp")
    peers = [(shard, (group + k) % 4) for k in range(1, 4)]
    greet([(None, peer) for peer in peers])
    copies = [remote(v_ref, got.at[k], s.at[k], r.at[k], peer) for k, peer in enumerate(peers)]
    for copy in copies:
        copy.start()
    for copy in copies:
        copy.wait()
    o_ref[...] = v_ref[...] + got[0] + got[1] + got[2]


def sum_cols(vector, collective_id):
    dma = pltpu.SemaphoreType.DMA
    shape = vector.shape
    return pl.pallas_call(
        sum_cols_kernel,
        out_shape=jax.ShapeDtypeStruct(shape, jnp.float32),
        in_specs=[pl.BlockSpec(memory_space=pltpu.VMEM)],
        out_specs=pl.BlockSpec(memory_space=pltpu.VMEM),
        scratch_shapes=[pltpu.VMEM((3,) + shape, jnp.float32), dma((3,)), dma((3,))],
        compiler_params=pltpu.CompilerParams(collective_id=collective_id, has_side_effects=True),
        name="sum_cols",
    )(vector)


def greet_all(shard, group, shards, groups):
    barrier = pltpu.get_barrier_semaphore()
    total = shards * groups

    def step(k, carry):
        other = (shard * groups + group + k) % total
        pl.semaphore_signal(
            barrier, inc=1, device_id=(other // groups, other % groups), device_id_type=MESH
        )
        return carry

    lax.fori_loop(1, total, step, 0)
    pl.semaphore_wait(barrier, total - 1)


def swap_rows_kernel(shards, groups, v_ref, o_ref, s, r):
    shard, group = lax.axis_index("fsdp"), lax.axis_index("tp")
    total = shards * groups
    me = shard * groups + group
    greet_all(shard, group, shards, groups)

    def copy(k):
        other = (me + k) % total
        return remote(v_ref.at[other // groups], o_ref.at[me], s.at[k], r.at[k],
                      (other // groups, other % groups))

    def start(k, carry):
        copy(k).start()
        return carry

    def wait(k, carry):
        copy(k).wait()
        return carry

    lax.fori_loop(1, total, start, 0)
    o_ref[me] = v_ref[shard]
    lax.fori_loop(1, total, wait, 0)


def swap_rows(values, shards, groups, collective_id):
    dma, total = pltpu.SemaphoreType.DMA, shards * groups
    return pl.pallas_call(
        functools.partial(swap_rows_kernel, shards, groups),
        out_shape=jax.ShapeDtypeStruct((total,) + values.shape[1:], values.dtype),
        in_specs=[pl.BlockSpec(memory_space=pltpu.VMEM)],
        out_specs=pl.BlockSpec(memory_space=pltpu.VMEM),
        scratch_shapes=[dma((total,)), dma((total,))],
        compiler_params=pltpu.CompilerParams(collective_id=collective_id, has_side_effects=True),
        name="swap_rows",
    )(values)


def sum_small_kernel(shards, groups, v_ref, o_ref, got, s1, r1, s2, r2):
    shard, group = lax.axis_index("fsdp"), lax.axis_index("tp")
    total = shards * groups
    me = shard * groups + group
    greet_all(shard, group, shards, groups)

    def first(k):
        other = (shard + k) % shards
        return remote(v_ref.at[other], got.at[k], s1.at[k], r1.at[k], (other, group))

    def second(k):
        other = (me + k) % total
        return remote(o_ref.at[me], o_ref.at[me], s2.at[k], r2.at[k],
                      (other // groups, other % groups))

    for k in range(1, shards):
        first(k).start()
    acc = v_ref[shard]
    for k in range(1, shards):
        first(k).wait()
        acc = acc + got[k]
    o_ref[me] = acc

    def start(k, carry):
        second(k).start()
        return carry

    def wait(k, carry):
        second(k).wait()
        return carry

    lax.fori_loop(1, total, start, 0)
    lax.fori_loop(1, total, wait, 0)


def sum_small(values, shards, groups, collective_id):
    dma, total = pltpu.SemaphoreType.DMA, shards * groups
    part = values.shape[1:]
    return pl.pallas_call(
        functools.partial(sum_small_kernel, shards, groups),
        out_shape=jax.ShapeDtypeStruct((total,) + part, values.dtype),
        in_specs=[pl.BlockSpec(memory_space=pltpu.VMEM)],
        out_specs=pl.BlockSpec(memory_space=pltpu.VMEM),
        scratch_shapes=[pltpu.VMEM((shards,) + part, values.dtype), dma((shards,)), dma((shards,)),
                        dma((total,)), dma((total,))],
        compiler_params=pltpu.CompilerParams(collective_id=collective_id, has_side_effects=True),
        name="sum_small",
    )(values)


def dot_plain(left, right):
    return jnp.dot(left, right, preferred_element_type=jnp.float32)


def expert_kernel(slots, block_rows, e_ref, x_ref, g_ref, routes_ref, router_ref, wg, wu, wd,
                  out_ref, back_ref, gg_ref, gates_ref, dwg, dwu, dwd,
                  xr, gs, acc_g, acc_u, acc_d, sems):
    step = pl.program_id(0)
    rows, width = x_ref.shape
    blocks = rows // block_rows
    experts = router_ref.shape[1]
    chunk = 512
    f32, low = jnp.float32, jnp.bfloat16

    @pl.when(step == 0)
    def _():
        acc_g[...] = jnp.zeros_like(acc_g)
        acc_u[...] = jnp.zeros_like(acc_u)
        acc_d[...] = jnp.zeros_like(acc_d)

    lanes = lax.broadcasted_iota(jnp.int32, (rows, experts), 1)
    routes = routes_ref[...]
    chosen = routes[:, 0:1] == lanes
    for j in range(1, TOPK):
        chosen = chosen | (routes[:, j : j + 1] == lanes)
    logits = jnp.where(chosen, dot_plain(x_ref[...], router_ref[...]), masked_score)
    peak = jnp.max(logits, axis=1, keepdims=True)
    weights = jnp.where(chosen, jnp.exp(logits - peak), 0.0)
    gates = weights / jnp.sum(weights, axis=1, keepdims=True)
    gates_ref[...] = gates
    mine = lanes == e_ref[0]
    gate_col = jnp.sum(jnp.where(mine, gates, 0.0), axis=1, keepdims=True)
    match_col = jnp.sum(jnp.where(mine & chosen, 1.0, 0.0), axis=1, keepdims=True)
    sub = lax.broadcasted_iota(jnp.int32, (block_rows, block_rows), 0)
    lane = lax.broadcasted_iota(jnp.int32, (block_rows, block_rows), 1)
    eye = sub == lane
    before = (sub > lane).astype(low)
    chosen_low = chosen.astype(f32).astype(low)
    pick, put, slot_gate = [], [], []
    slot_lane = lax.broadcasted_iota(jnp.int32, (block_rows, slots), 1).astype(f32)
    slot_sub = lax.broadcasted_iota(jnp.int32, (slots, block_rows), 0).astype(f32)
    for b in range(blocks):
        part = slice(b * block_rows, (b + 1) * block_rows)
        ranks = dot_plain(before, chosen_low[part])
        rank = jnp.sum(jnp.where(mine[part], ranks, 0.0), axis=1, keepdims=True)
        rank = jnp.where(match_col[part] > 0.0, rank, -1.0)
        rank_row = jnp.sum(jnp.where(eye, rank, 0.0), axis=0, keepdims=True)
        gate_row = jnp.sum(jnp.where(eye, gate_col[part], 0.0), axis=0, keepdims=True)
        hot = rank_row == slot_sub
        pick.append(hot.astype(f32).astype(low))
        put.append((rank == slot_lane).astype(f32).astype(low))
        slot_gate.append(jnp.sum(jnp.where(hot, gate_row, 0.0), axis=1, keepdims=True))
    slot_gate = jnp.concatenate(slot_gate, axis=0)

    def columns(i):
        return pl.ds(pl.multiple_of(i * chunk, chunk), chunk)

    def gather(ref, cols):
        return jnp.concatenate(
            [dot_plain(pick[b], ref[pl.ds(b * block_rows, block_rows), cols]) for b in range(blocks)],
            axis=0,
        )

    def scatter(ref, cols, values):
        for b in range(blocks):
            ref[pl.ds(b * block_rows, block_rows), cols] = dot_plain(
                put[b], values[b * slots : (b + 1) * slots]
            ).astype(low)

    def take(i, carry):
        cols = columns(i)
        xr[:, cols] = gather(x_ref, cols).astype(low)
        return carry

    lax.fori_loop(0, width // chunk, take, 0)
    gate_pre = dot_plain(xr[...], wg[...])
    up_pre = dot_plain(xr[...], wu[...])
    sig = jax.nn.sigmoid(gate_pre)
    silu = gate_pre * sig
    hidden_low = (silu * up_pre).astype(low)

    def middle_part(i, carry):
        total, hidden_grad = carry
        cols = columns(i)
        grad = gather(g_ref, cols)
        expert_out = dot_plain(hidden_low, wd[:, cols]).astype(low).astype(f32)
        total = total + jnp.sum(grad * expert_out, axis=1, keepdims=True)
        pair_grad = (grad * slot_gate).astype(low)
        scatter(out_ref, cols, (expert_out * slot_gate).astype(low))
        acc_d[:, cols] += dot_first(hidden_low, pair_grad)
        return total, hidden_grad + dot_last(pair_grad, wd[:, cols])

    gates_grad, hidden_grad = lax.fori_loop(
        0,
        width // chunk,
        middle_part,
        (jnp.zeros(slot_gate.shape, f32), jnp.zeros(gate_pre.shape, f32)),
    )
    for b in range(blocks):
        part = slice(b * slots, (b + 1) * slots)
        gg_ref[0, :, pl.ds(b * block_rows, block_rows)] = jnp.sum(
            pick[b].astype(f32) * gates_grad[part], axis=0, keepdims=True
        )
    gate_grad = (hidden_grad * up_pre * (sig * (1.0 + gate_pre * (1.0 - sig)))).astype(low)
    up_grad = (hidden_grad * silu).astype(low)

    def last_part(i, carry):
        cols = columns(i)
        acc_g[cols, :] += dot_first(xr[:, cols], gate_grad)
        acc_u[cols, :] += dot_first(xr[:, cols], up_grad)
        row_grad = dot_last(gate_grad, wg[cols, :]) + dot_last(up_grad, wu[cols, :])
        scatter(back_ref, cols, row_grad.astype(low))
        return carry

    lax.fori_loop(0, width // chunk, last_part, 0)

    @pl.when(step == pl.num_programs(0) - 1)
    def _():
        copies = [
            pltpu.make_async_copy(src, dst, sems.at[i])
            for i, (src, dst) in enumerate(((acc_g, dwg), (acc_u, dwu), (acc_d, dwd)))
        ]
        for copy in copies:
            copy.start()
        for copy in copies:
            copy.wait()


def run_experts(expert, x_all, g_all, routes_all, router, gate_w, up_w, down_w, block_rows, slots):
    total, width = x_all.shape
    hidden = gate_w.shape[1]
    experts = router.shape[1]
    rows = 2 * block_rows
    steps = total // rows
    f32, low = jnp.float32, jnp.bfloat16
    once = pl.Buffered(1)
    whole = lambda shape: pl.BlockSpec(shape, lambda i, e: (0, 0), pipeline_mode=once)
    tile = lambda cols: pl.BlockSpec((rows, cols), lambda i, e: (i, 0))
    any_space = pl.BlockSpec(memory_space=pl.ANY)
    return pl.pallas_call(
        functools.partial(expert_kernel, slots, block_rows),
        grid_spec=pltpu.PrefetchScalarGridSpec(
            num_scalar_prefetch=1,
            grid=(steps,),
            in_specs=[
                tile(width), tile(width), tile(routes_all.shape[1]), whole((width, experts)),
                whole((width, hidden)), whole((width, hidden)), whole((hidden, width)),
            ],
            out_specs=[
                tile(width), tile(width),
                pl.BlockSpec((1, 1, rows), lambda i, e: (i, 0, 0)),
                tile(experts), any_space, any_space, any_space,
            ],
            scratch_shapes=[
                pltpu.VMEM((2 * slots, width), low), pltpu.VMEM((2 * slots, width), low),
                pltpu.VMEM((width, hidden), f32), pltpu.VMEM((width, hidden), f32),
                pltpu.VMEM((hidden, width), f32), pltpu.SemaphoreType.DMA((3,)),
            ],
        ),
        out_shape=[
            jax.ShapeDtypeStruct((total, width), low),
            jax.ShapeDtypeStruct((total, width), low),
            jax.ShapeDtypeStruct((steps, 1, rows), f32),
            jax.ShapeDtypeStruct((total, experts), f32),
            jax.ShapeDtypeStruct((width, hidden), f32),
            jax.ShapeDtypeStruct((width, hidden), f32),
            jax.ShapeDtypeStruct((hidden, width), f32),
        ],
        compiler_params=pltpu.CompilerParams(
            dimension_semantics=("arbitrary",), vmem_limit_bytes=60 << 20
        ),
        name="experts",
    )(expert, x_all, g_all, routes_all, router, gate_w, up_w, down_w)


def gathered_body(
    tokens,
    cotangent,
    routes,
    doc_ids,
    gain_attn,
    w_query,
    key_weight,
    value_weight,
    w_out,
    gain_query,
    key_norm_gain,
    gain_moe,
    router,
    w_gate,
    w_up,
    w_down,
):
    shard_count = lax.axis_size("fsdp")
    group_count = lax.axis_size("tp")
    shard_index = lax.axis_index("fsdp")
    group_index = lax.axis_index("tp")
    nz = shard_count // 2
    f32, low = jnp.float32, jnp.bfloat16
    row_count, slice_width = tokens.shape
    model_width = slice_width * group_count
    micro_count, micro_rows = doc_ids.shape
    head_width = gain_query.shape[0]
    query_width, kv_width = w_query.shape[1], key_weight.shape[1]
    query_local = query_width // head_width
    kv_local = kv_width // head_width
    group_width = query_local // kv_local
    expert_total = router.shape[1]
    capacity = max(2, 2 * micro_rows * TOPK // expert_total)
    block_keys = micro_rows * math.gcd(shard_count, max(1, 512 // micro_rows))
    my_columns = group_index * slice_width

    small = jnp.concatenate([routes, doc_ids.reshape(row_count, 1)], axis=1)
    small_all = lax.all_gather(small, "fsdp", axis=0, tiled=True)
    routes_all = small_all[:, :TOPK]
    ids_all = small_all[:, TOPK].reshape(shard_count, micro_count, micro_rows)
    doc_range = jnp.arange(DOCS)
    doc_totals = jnp.sum((ids_all[..., None] == doc_range).astype(jnp.int32), axis=(0, 2))
    doc_begin = jnp.cumsum(doc_totals, axis=1) - doc_totals
    query_index = shard_index * micro_rows + jnp.arange(micro_rows)
    query_start = jnp.sum(
        jnp.where(doc_ids[:, :, None] == doc_range, doc_begin[:, None, :], 0), axis=2
    )
    positions = (query_index[None, :] - query_start).reshape(row_count)
    cosine_lookup, sine_lookup = rope_tables(positions, head_width)

    full_tokens = gather_cols(tokens, 1).astype(f32)
    wq_all, wk_all, wv_all, wo_all = gather_rows(
        [w_query, key_weight, value_weight, w_out], nz, 2
    )
    grads_all = gather_all(cotangent, nz, 3)
    token_mean = jnp.mean(full_tokens * full_tokens, axis=-1, keepdims=True)
    token_scale = lax.rsqrt(token_mean + norm_eps)
    normed_low = (full_tokens * token_scale * gain_attn).astype(low)
    query_pre = jnp.dot(normed_low, wq_all, preferred_element_type=f32)
    key_pre = jnp.dot(normed_low, wk_all, preferred_element_type=f32)
    value_low = jnp.dot(normed_low, wv_all, preferred_element_type=f32).astype(low)

    def shape_heads(query_raw, key_raw, query_gain, key_gain):
        query_heads = rotary_apply(
            root_mean_norm(query_raw.reshape(row_count, query_local, head_width), query_gain),
            cosine_lookup[:, None, :],
            sine_lookup[:, None, :],
        )
        key_heads = rotary_apply(
            root_mean_norm(key_raw.reshape(row_count, kv_local, head_width), key_gain),
            cosine_lookup[:, None, :],
            sine_lookup[:, None, :],
        )
        return (query_heads, key_heads)

    (query_heads, key_heads), heads_pull = jax.vjp(
        shape_heads, query_pre, key_pre, gain_query, key_norm_gain
    )
    query_low = query_heads.astype(low)
    key_low = key_heads.reshape(row_count, kv_width).astype(low)
    keys_got, values_got = gather_rows([key_low, value_low], nz, 4)

    def by_stream(array):
        return array.reshape(shard_count, micro_count, micro_rows, kv_width).transpose(
            1, 0, 2, 3
        ).reshape(micro_count, shard_count * micro_rows, kv_width)

    keys_all, values_all = by_stream(keys_got), by_stream(values_got)
    row_index = jnp.tile(query_index, group_width)
    saved, head_parts = [], []
    for micro_index in range(micro_count):
        here = slice(micro_index * micro_rows, (micro_index + 1) * micro_rows)
        queries = to_heads(query_low[here], kv_local, group_width)
        row_start = jnp.tile(query_start[micro_index], group_width)
        head_out, log_total = attend_forward(
            queries, keys_all[micro_index], values_all[micro_index], row_index, row_start, block_keys
        )
        saved.append((queries, row_start, head_out, log_total))
        head_parts.append(to_tokens(head_out, group_width).astype(low))
    heads_low = jnp.concatenate(head_parts, axis=0)
    attn_part = dot_last(heads_low, wo_all).astype(low)
    middle = tokens.astype(f32) + reduce_cols(attn_part, 5)

    def row_mean(values, collective_id):
        total = jnp.sum(values, axis=1).reshape(row_count // 128, 128)
        return sum_cols(total, collective_id).reshape(row_count, 1) / model_width

    scale = lax.rsqrt(row_mean(middle * middle, 6) + norm_eps)
    gain_slice = lax.dynamic_slice_in_dim(gain_moe, my_columns, slice_width)
    moe_low = (middle * scale * gain_slice).astype(low)
    moe_all = gather_all(moe_low, nz, 7)
    expert = (shard_index * group_count + group_index).astype(jnp.int32).reshape(1)
    out_part, back_part, gates_grad, gates_all, gate_acc, up_acc, down_acc = run_experts(
        expert, moe_all, grads_all, routes_all, router, w_gate[0], w_up[0], w_down[0],
        micro_rows, capacity,
    )
    back = scatter_all(back_part, nz, 8)
    gates_grad = swap_rows(
        gates_grad.reshape(shard_count, row_count // 128, 128), shard_count, group_count, 9
    ).reshape(expert_total, row_count).T
    gates = lax.dynamic_slice_in_dim(gates_all, shard_index * row_count, row_count)
    logit_grad = gates * (gates_grad - jnp.sum(gates * gates_grad, axis=1, keepdims=True))
    router_slice = lax.dynamic_slice_in_dim(router, my_columns, slice_width).astype(f32)
    moe_grad = back + lax.dot_general(
        logit_grad, router_slice, (((1,), (1,)), ((), ())), precision=highest_precision
    )
    router_part = lax.dot_general(
        moe_low.astype(f32), logit_grad, (((0,), (0,)), ((), ())), precision=highest_precision
    )
    gain_moe_part = jnp.sum(moe_grad * middle * scale, axis=0)
    grad_slice = cotangent.astype(f32)
    inner = gain_slice * moe_grad
    middle_grad = (
        grad_slice + scale * inner - middle * scale**3 * row_mean(middle * inner, 10)
    )
    middle_low = gather_cols(middle_grad.astype(low), 11)
    out_grad_part = dot_first(middle_low, heads_low).astype(low)
    heads_grad = jnp.dot(middle_low, wo_all, preferred_element_type=f32).astype(low)
    block_out = (middle + scatter_all(out_part, nz, 12)).astype(low)
    w_out_grad = reduce_rows(out_grad_part, nz, 13)
    query_sides, key_sides = [], []
    for micro_index in range(micro_count):
        here = slice(micro_index * micro_rows, (micro_index + 1) * micro_rows)
        queries, row_start, head_out, log_total = saved[micro_index]
        grad_low = to_heads(
            heads_grad[here].reshape(micro_rows, query_local, head_width), kv_local, group_width
        )
        query_side, key_side, value_side = attend_backward(
            queries,
            keys_all[micro_index],
            values_all[micro_index],
            row_index,
            row_start,
            block_keys,
            head_out,
            log_total,
            grad_low,
        )
        query_sides.append(to_tokens(query_side, group_width))
        key_sides.append(jnp.concatenate([key_side, value_side], axis=1).astype(low))
    sides = jnp.stack(key_sides).reshape(micro_count, shard_count, micro_rows, 2 * kv_width)
    sides = reduce_rows(
        sides.transpose(1, 0, 2, 3).reshape(shard_count * row_count, 2 * kv_width), nz, 14
    )
    query_pre_grad, key_pre_grad, gain_query_part, gain_key_part = heads_pull(
        (
            jnp.concatenate(query_sides, axis=0).reshape(row_count, query_local, head_width),
            sides[:, :kv_width].reshape(row_count, kv_local, head_width),
        )
    )
    query_pre_low = query_pre_grad.astype(low)
    key_pre_low = key_pre_grad.astype(low)
    value_pre_low = sides[:, kv_width:].astype(low)
    normed_part = (
        dot_last(query_pre_low, wq_all)
        + dot_last(key_pre_low, wk_all)
        + dot_last(value_pre_low, wv_all)
    ).astype(low)
    normed_grad = reduce_cols(normed_part, 15)
    pre_low = jnp.concatenate([query_pre_low, key_pre_low, value_pre_low], axis=1)
    weight_grad = reduce_rows(dot_first(normed_low, pre_low).astype(low), nz, 16)
    token_slice = tokens.astype(f32)
    attn_gain = lax.dynamic_slice_in_dim(gain_attn, my_columns, slice_width)
    gain_attn_part = jnp.sum(normed_grad * token_slice * token_scale, axis=0)
    inner = attn_gain * normed_grad
    token_grad = (
        middle_grad
        + token_scale * inner
        - token_slice * token_scale**3 * row_mean(token_slice * inner, 17)
    ).astype(low)

    pieces = [router_part.reshape(-1), gain_attn_part, gain_moe_part, gain_query_part, gain_key_part]
    length = sum(piece.shape[0] for piece in pieces)
    part_rows = -(-length // (shard_count * 1024)) * 8
    flat = jnp.concatenate(
        pieces + [jnp.zeros((shard_count * part_rows * 128 - length,), f32)]
    ).reshape(shard_count, part_rows, 128)
    summed = sum_small(flat, shard_count, group_count, 18).reshape(
        shard_count, group_count, part_rows * 128
    ).transpose(1, 0, 2).reshape(group_count, shard_count * part_rows * 128)
    at = 0
    sums = []
    for piece in pieces:
        sums.append(summed[:, at : at + piece.shape[0]])
        at += piece.shape[0]
    return (
        block_out,
        token_grad,
        sums[1].reshape(-1),
        weight_grad[:, :query_width],
        weight_grad[:, query_width : query_width + kv_width],
        weight_grad[:, query_width + kv_width :],
        w_out_grad,
        jnp.sum(sums[3], axis=0),
        jnp.sum(sums[4], axis=0),
        sums[2].reshape(-1),
        sums[0].reshape(router.shape),
        gate_acc[None],
        up_acc[None],
        down_acc[None],
    )


def solution(mesh):
    small = mesh.shape["fsdp"] * mesh.shape["tp"] <= 32 and mesh.shape["tp"] == 4
    return jax.shard_map(
        gathered_body if small else body,
        mesh=mesh,
        in_specs=(
            P("fsdp", "tp"),
            P("fsdp", "tp"),
            P("fsdp", None),
            P(None, "fsdp"),
            P(),
            P("fsdp", "tp"),
            P("fsdp", "tp"),
            P("fsdp", "tp"),
            P("fsdp", "tp"),
            P(),
            P(),
            P(),
            P(),
            P(("fsdp", "tp"), None, None),
            P(("fsdp", "tp"), None, None),
            P(("fsdp", "tp"), None, None),
        ),
        out_specs=(
            P("fsdp", "tp"),
            P("fsdp", "tp"),
            P(),
            P("fsdp", "tp"),
            P("fsdp", "tp"),
            P("fsdp", "tp"),
            P("fsdp", "tp"),
            P(),
            P(),
            P(),
            P(),
            P(("fsdp", "tp"), None, None),
            P(("fsdp", "tp"), None, None),
            P(("fsdp", "tp"), None, None),
        ),
        check_vma=False,
    )
```

```python
import functools
import math

import jax
import jax.numpy as jnp
from jax import lax
from jax.experimental import pallas as pl
from jax.experimental.pallas import tpu as pltpu
from jax.sharding import PartitionSpec as P

TOPK = 8
DOCS = 4


theta_base = 1000000.0
norm_eps = 1e-06
masked_score = -1e30
highest_precision = lax.Precision.HIGHEST


def root_mean_norm(row_block, gain_row):
    return (
        row_block
        * lax.rsqrt(jnp.mean(row_block * row_block, axis=-1, keepdims=True) + norm_eps)
        * gain_row
    )


def rotary_apply(row_block, cosine_lookup, sine_lookup):
    half_width = row_block.shape[-1] // 2
    turned = jnp.concatenate([-row_block[..., half_width:], row_block[..., :half_width]], axis=-1)
    return row_block * cosine_lookup + turned * sine_lookup


def rope_tables(positions, head_width):
    half_width = head_width // 2
    frequency = theta_base ** (
        -2.0 * jnp.arange(half_width, dtype=jnp.int32).astype(jnp.float32) / head_width
    )
    angles = positions.astype(jnp.float32)[:, None] * frequency[None, :]
    cosine_lookup = jnp.cos(angles)
    sine_lookup = jnp.sin(angles)
    return (
        jnp.concatenate([cosine_lookup, cosine_lookup], axis=-1),
        jnp.concatenate([sine_lookup, sine_lookup], axis=-1),
    )


def swiglu(gate_pre, up_pre):
    return jax.nn.silu(gate_pre) * up_pre


def dot_first(left_side, right_side):
    return lax.dot_general(
        left_side, right_side, (((0,), (0,)), ((), ())), preferred_element_type=jnp.float32
    )


def dot_last(left_side, right_side):
    return lax.dot_general(
        left_side, right_side, (((1,), (1,)), ((), ())), preferred_element_type=jnp.float32
    )


def gather_weights(w_query, key_weight, value_weight, w_out):
    return (
        lax.all_gather(w_query, "fsdp", axis=0, tiled=True),
        lax.all_gather(key_weight, "fsdp", axis=0, tiled=True),
        lax.all_gather(value_weight, "fsdp", axis=0, tiled=True),
        lax.all_gather(w_out, "fsdp", axis=0, tiled=True),
    )


def gather_keys(keys_low, values_low):
    return (
        lax.all_gather(keys_low, "fsdp", axis=0, tiled=True),
        lax.all_gather(values_low, "fsdp", axis=0, tiled=True),
    )


def send_rows(buffer):
    return lax.all_to_all(buffer, "fsdp", split_axis=0, concat_axis=0, tiled=True)


def return_rows(buffer):
    return lax.all_to_all(buffer, "fsdp", split_axis=0, concat_axis=0, tiled=True)


def to_heads(per_token, kv_local, group_width):
    token_count, head_total, head_width = per_token.shape
    grouped_heads = per_token.reshape(token_count, kv_local, group_width, head_width)
    return grouped_heads.transpose(1, 2, 0, 3).reshape(
        kv_local, group_width * token_count, head_width
    )


def to_tokens(per_head, group_width):
    kv_local, row_count, head_width = per_head.shape
    token_count = row_count // group_width
    grouped_heads = per_head.reshape(kv_local, group_width, token_count, head_width)
    return grouped_heads.transpose(2, 0, 1, 3).reshape(
        token_count, kv_local * group_width * head_width
    )


def key_block(keys_all, key_start, block_keys, kv_local, head_width):
    return lax.dynamic_slice_in_dim(keys_all, key_start, block_keys, 0).reshape(
        block_keys, kv_local, head_width
    )


def block_scores(queries, keys_part, key_start, query_index, query_start):
    head_width = queries.shape[-1]
    scores = jnp.einsum(
        "hrd,khd->hrk", queries, keys_part, preferred_element_type=jnp.float32
    ) * head_width ** (-0.5)
    key_index = key_start + jnp.arange(keys_part.shape[0])
    allowed = (key_index[None, :] >= query_start[:, None]) & (
        key_index[None, :] <= query_index[:, None]
    )
    return (jnp.where(allowed[None], scores, masked_score), allowed)


def attend_forward(queries, keys_all, values_all, query_index, query_start, block_keys):
    kv_local, row_count, head_width = queries.shape
    lowest_block = jnp.min(query_start) // block_keys
    highest_block = jnp.max(query_index) // block_keys + 1

    def visit_block(block_index, running):
        run_peak, run_total, run_acc = running
        key_start = block_index * block_keys
        keys_part = key_block(keys_all, key_start, block_keys, kv_local, head_width)
        values_part = key_block(values_all, key_start, block_keys, kv_local, head_width)
        scores, allowed = block_scores(queries, keys_part, key_start, query_index, query_start)
        new_peak = jnp.maximum(run_peak, jnp.max(scores, axis=-1))
        weights = jnp.where(allowed[None], jnp.exp(scores - new_peak[..., None]), 0.0)
        factor = jnp.exp(run_peak - new_peak)
        run_total = run_total * factor + jnp.sum(weights, axis=-1)
        run_acc = run_acc * factor[..., None] + jnp.einsum(
            "hrk,khd->hrd",
            weights.astype(jnp.bfloat16),
            values_part,
            preferred_element_type=jnp.float32,
        )
        return (new_peak, run_total, run_acc)

    start_state = (
        jnp.full((kv_local, row_count), masked_score, jnp.float32),
        jnp.zeros((kv_local, row_count), jnp.float32),
        jnp.zeros((kv_local, row_count, head_width), jnp.float32),
    )
    run_peak, run_total, run_acc = lax.fori_loop(
        lowest_block, highest_block, visit_block, start_state
    )
    return (run_acc / run_total[..., None], run_peak + jnp.log(run_total))


def attend_backward(
    queries,
    keys_all,
    values_all,
    query_index,
    query_start,
    block_keys,
    outputs,
    log_total,
    grad_low,
):
    kv_local, row_count, head_width = queries.shape
    key_count = keys_all.shape[0]
    score_scale = head_width ** (-0.5)
    row_delta = jnp.sum(grad_low.astype(jnp.float32) * outputs, axis=-1)
    lowest_block = jnp.min(query_start) // block_keys
    highest_block = jnp.max(query_index) // block_keys + 1

    def visit_block(block_index, running):
        query_acc, key_acc, value_acc = running
        key_start = block_index * block_keys
        keys_part = key_block(keys_all, key_start, block_keys, kv_local, head_width)
        values_part = key_block(values_all, key_start, block_keys, kv_local, head_width)
        scores, allowed = block_scores(queries, keys_part, key_start, query_index, query_start)
        prob_block = jnp.where(allowed[None], jnp.exp(scores - log_total[..., None]), 0.0)
        prob_grad = jnp.einsum(
            "hrd,khd->hrk", grad_low, values_part, preferred_element_type=jnp.float32
        )
        score_grad = (prob_block * (prob_grad - row_delta[..., None])).astype(jnp.bfloat16)
        query_acc = (
            query_acc
            + jnp.einsum("hrk,khd->hrd", score_grad, keys_part, preferred_element_type=jnp.float32)
            * score_scale
        )
        key_part = (
            jnp.einsum("hrk,hrd->khd", score_grad, queries, preferred_element_type=jnp.float32)
            * score_scale
        )
        value_part = jnp.einsum(
            "hrk,hrd->khd",
            prob_block.astype(jnp.bfloat16),
            grad_low,
            preferred_element_type=jnp.float32,
        )
        key_acc = lax.dynamic_update_slice_in_dim(
            key_acc, key_part.reshape(block_keys, kv_local * head_width), key_start, 0
        )
        value_acc = lax.dynamic_update_slice_in_dim(
            value_acc, value_part.reshape(block_keys, kv_local * head_width), key_start, 0
        )
        return (query_acc, key_acc, value_acc)

    start_state = (
        jnp.zeros((kv_local, row_count, head_width), jnp.float32),
        jnp.zeros((key_count, kv_local * head_width), jnp.float32),
        jnp.zeros((key_count, kv_local * head_width), jnp.float32),
    )
    return lax.fori_loop(lowest_block, highest_block, visit_block, start_state)


def body(
    tokens,
    cotangent,
    routes,
    doc_ids,
    gain_attn,
    w_query,
    key_weight,
    value_weight,
    w_out,
    gain_query,
    key_norm_gain,
    gain_moe,
    router,
    w_gate,
    w_up,
    w_down,
):
    shard_count = lax.axis_size("fsdp")
    group_count = lax.axis_size("tp")
    shard_index = lax.axis_index("fsdp")
    group_index = lax.axis_index("tp")
    full_tokens, full_grads = (
        lax.all_gather(tokens, "tp", axis=1, tiled=True),
        lax.all_gather(cotangent, "tp", axis=1, tiled=True),
    )
    slice_width = tokens.shape[1]
    model_width = full_tokens.shape[1]
    micro_count, micro_rows = doc_ids.shape
    head_width = gain_query.shape[0]
    query_local = w_query.shape[1] // head_width
    kv_local = key_weight.shape[1] // head_width
    group_width = query_local // kv_local
    expert_total = router.shape[1]
    capacity = max(2, 2 * micro_rows * TOPK // expert_total)
    slot_total = shard_count * capacity
    pair_total = micro_rows * TOPK
    block_keys = micro_rows * math.gcd(shard_count, max(1, 512 // micro_rows))
    doc_range = jnp.arange(DOCS)
    expert_range = jnp.arange(expert_total)
    local_counts = jnp.sum((doc_ids[:, :, None] == doc_range).astype(jnp.float32), axis=1)
    doc_totals = lax.psum(local_counts, "fsdp")
    doc_begin = (jnp.cumsum(doc_totals, axis=1) - doc_totals).astype(jnp.int32)
    gate_expert = w_gate[0]
    up_expert = w_up[0]
    down_expert = w_down[0]
    router_wide = router.astype(jnp.float32)
    query_acc = jnp.zeros((model_width, query_local * head_width), jnp.float32)
    key_acc = jnp.zeros((model_width, kv_local * head_width), jnp.float32)
    value_acc = jnp.zeros((model_width, kv_local * head_width), jnp.float32)
    out_acc = jnp.zeros((model_width, query_local * head_width), jnp.float32)
    gate_acc = jnp.zeros(gate_expert.shape, jnp.float32)
    up_acc = jnp.zeros(up_expert.shape, jnp.float32)
    down_acc = jnp.zeros(down_expert.shape, jnp.float32)
    router_acc = jnp.zeros(router.shape, jnp.float32)
    gain_attn_acc = jnp.zeros(gain_attn.shape, jnp.float32)
    gain_moe_acc = jnp.zeros(gain_moe.shape, jnp.float32)
    gain_query_acc = jnp.zeros(gain_query.shape, jnp.float32)
    gain_key_acc = jnp.zeros(key_norm_gain.shape, jnp.float32)
    out_parts = []
    grad_parts = []
    for micro_index in range(micro_count):
        row_begin = micro_index * micro_rows
        token_block = full_tokens[row_begin : row_begin + micro_rows].astype(jnp.float32)
        ids_now = doc_ids[micro_index]
        query_index = shard_index * micro_rows + jnp.arange(micro_rows)
        query_start = jnp.sum(
            jnp.where(ids_now[:, None] == doc_range, doc_begin[micro_index][None, :], 0), axis=1
        )
        cosine_lookup, sine_lookup = rope_tables(query_index - query_start, head_width)
        gathered = gather_weights(w_query, key_weight, value_weight, w_out)
        normed, norm_pull = jax.vjp(root_mean_norm, token_block, gain_attn)
        normed_reduced = normed.astype(jnp.bfloat16)
        query_pre = jnp.dot(normed_reduced, gathered[0], preferred_element_type=jnp.float32)
        key_before_norm = jnp.dot(normed_reduced, gathered[1], preferred_element_type=jnp.float32)
        value_reduced = jnp.dot(
            normed_reduced, gathered[2], preferred_element_type=jnp.float32
        ).astype(jnp.bfloat16)

        def shape_heads(query_raw, key_raw, query_gain, key_gain):
            query_heads = rotary_apply(
                root_mean_norm(query_raw.reshape(micro_rows, query_local, head_width), query_gain),
                cosine_lookup[:, None, :],
                sine_lookup[:, None, :],
            )
            key_heads = rotary_apply(
                root_mean_norm(key_raw.reshape(micro_rows, kv_local, head_width), key_gain),
                cosine_lookup[:, None, :],
                sine_lookup[:, None, :],
            )
            return (query_heads, key_heads)

        (query_heads, key_heads), heads_pull = jax.vjp(
            shape_heads, query_pre, key_before_norm, gain_query, key_norm_gain
        )
        queries = to_heads(query_heads.astype(jnp.bfloat16), kv_local, group_width)
        keys_low = key_heads.reshape(micro_rows, kv_local * head_width).astype(jnp.bfloat16)
        keys_all, values_all = gather_keys(keys_low, value_reduced)
        row_index = jnp.tile(query_index, group_width)
        row_start = jnp.tile(query_start, group_width)
        head_out, log_total = attend_forward(
            queries, keys_all, values_all, row_index, row_start, block_keys
        )
        heads_low = to_tokens(head_out, group_width).astype(jnp.bfloat16)
        attn_part = dot_last(heads_low, gathered[3])
        middle = token_block + lax.psum(attn_part.astype(jnp.bfloat16), "tp").astype(jnp.float32)
        moe_normed, moe_pull = jax.vjp(root_mean_norm, middle, gain_moe)
        moe_low = moe_normed.astype(jnp.bfloat16)
        logits = jnp.dot(moe_low, router, preferred_element_type=jnp.float32)
        routes_now = routes[row_begin : row_begin + micro_rows]
        route_match = routes_now[:, :, None] == expert_range
        chosen = jnp.sum(jnp.where(route_match, logits[:, None, :], 0.0), axis=-1)
        gate_weights, softmax_pull = jax.vjp(jax.nn.softmax, chosen)
        mine = routes_now % group_count == group_index
        pair_target = jnp.where(mine, routes_now // group_count, shard_count).reshape(pair_total)
        target_hot = (pair_target[:, None] == jnp.arange(shard_count)).astype(jnp.int32)
        pair_rank = jnp.sum((jnp.cumsum(target_hot, axis=0) - target_hot) * target_hot, axis=1)
        pair_slot = jnp.where(
            pair_target < shard_count, pair_target * capacity + pair_rank, slot_total
        )
        slot_pair = (
            jnp.full((slot_total + 1,), pair_total, jnp.int32)
            .at[pair_slot]
            .set(jnp.arange(pair_total, dtype=jnp.int32))[:slot_total]
        )
        slot_token = slot_pair // TOPK
        slot_grid = pair_slot.reshape(micro_rows, TOPK)
        padded_low = jnp.concatenate([moe_low, jnp.zeros((1, model_width), jnp.bfloat16)], axis=0)
        received = send_rows(
            padded_low[slot_token].reshape(shard_count, capacity, model_width)
        ).reshape(slot_total, model_width)
        gate_pre = jnp.dot(received, gate_expert, preferred_element_type=jnp.float32)
        up_pre = jnp.dot(received, up_expert, preferred_element_type=jnp.float32)
        hidden, swiglu_pull = jax.vjp(swiglu, gate_pre, up_pre)
        hidden_low = hidden.astype(jnp.bfloat16)
        expert_out = jnp.dot(hidden_low, down_expert, preferred_element_type=jnp.float32).astype(
            jnp.bfloat16
        )
        returned = return_rows(expert_out.reshape(shard_count, capacity, model_width)).reshape(
            slot_total, model_width
        )
        padded_out = jnp.concatenate([returned, jnp.zeros((1, model_width), jnp.bfloat16)], axis=0)
        moe_part = jnp.zeros((micro_rows, model_width), jnp.float32)
        for pick_index in range(TOPK):
            moe_part = moe_part + gate_weights[:, pick_index : pick_index + 1] * padded_out[
                slot_grid[:, pick_index]
            ].astype(jnp.float32)
        moe_share = lax.psum_scatter(
            moe_part.astype(jnp.bfloat16), "tp", scatter_dimension=1, tiled=True
        ).astype(jnp.float32)
        middle_slice = lax.dynamic_slice_in_dim(middle, group_index * slice_width, slice_width, 1)
        out_parts.append((middle_slice + moe_share).astype(jnp.bfloat16))
        grad_block = full_grads[row_begin : row_begin + micro_rows].astype(jnp.float32)
        gate_columns = []
        for pick_index in range(TOPK):
            gate_columns.append(
                jnp.sum(
                    grad_block * padded_out[slot_grid[:, pick_index]].astype(jnp.float32), axis=1
                )
            )
        gates_grad = jnp.stack(gate_columns, axis=1)
        flat_gates = jnp.concatenate(
            [gate_weights.reshape(pair_total), jnp.zeros((1,), jnp.float32)]
        )
        padded_grad = jnp.concatenate(
            [grad_block, jnp.zeros((1, model_width), jnp.float32)], axis=0
        )
        send_grad = (padded_grad[slot_token] * flat_gates[slot_pair][:, None]).astype(jnp.bfloat16)
        received_grad = send_rows(send_grad.reshape(shard_count, capacity, model_width)).reshape(
            slot_total, model_width
        )
        hidden_grad = dot_last(received_grad, down_expert)
        down_acc = down_acc + dot_first(hidden_low, received_grad)
        gate_pre_grad, up_pre_grad = swiglu_pull(hidden_grad)
        gate_pre_low = gate_pre_grad.astype(jnp.bfloat16)
        up_pre_low = up_pre_grad.astype(jnp.bfloat16)
        gate_acc = gate_acc + dot_first(received, gate_pre_low)
        up_acc = up_acc + dot_first(received, up_pre_low)
        rows_back = (dot_last(gate_pre_low, gate_expert) + dot_last(up_pre_low, up_expert)).astype(
            jnp.bfloat16
        )
        back_rows = return_rows(rows_back.reshape(shard_count, capacity, model_width)).reshape(
            slot_total, model_width
        )
        padded_back = jnp.concatenate(
            [back_rows, jnp.zeros((1, model_width), jnp.bfloat16)], axis=0
        )
        moe_grad = jnp.zeros((micro_rows, model_width), jnp.float32)
        for pick_index in range(TOPK):
            moe_grad = moe_grad + padded_back[slot_grid[:, pick_index]].astype(jnp.float32)
        (chosen_grad,) = softmax_pull(gates_grad)
        logit_grad = jnp.sum(jnp.where(route_match, chosen_grad[:, :, None], 0.0), axis=1)
        router_acc = router_acc + lax.dot_general(
            moe_low.astype(jnp.float32),
            logit_grad,
            (((0,), (0,)), ((), ())),
            precision=highest_precision,
        )
        moe_grad = moe_grad + lax.dot_general(
            logit_grad, router_wide, (((1,), (1,)), ((), ())), precision=highest_precision
        )
        middle_part, gain_moe_part = moe_pull(moe_grad)
        gain_moe_acc = gain_moe_acc + gain_moe_part
        middle_grad = grad_block + lax.psum(middle_part.astype(jnp.bfloat16), "tp").astype(
            jnp.float32
        )
        middle_low = middle_grad.astype(jnp.bfloat16)
        gathered_back = gather_weights(w_query, key_weight, value_weight, w_out)
        out_acc = out_acc + dot_first(middle_low, heads_low)
        heads_grad = jnp.dot(middle_low, gathered_back[3], preferred_element_type=jnp.float32)
        grad_low = to_heads(
            heads_grad.reshape(micro_rows, query_local, head_width).astype(jnp.bfloat16),
            kv_local,
            group_width,
        )
        query_side, key_side_all, value_side_all = attend_backward(
            queries,
            keys_all,
            values_all,
            row_index,
            row_start,
            block_keys,
            head_out,
            log_total,
            grad_low,
        )
        key_side, value_side = (
            lax.psum_scatter(
                key_side_all.astype(jnp.bfloat16), "fsdp", scatter_dimension=0, tiled=True
            ).astype(jnp.float32),
            lax.psum_scatter(
                value_side_all.astype(jnp.bfloat16), "fsdp", scatter_dimension=0, tiled=True
            ).astype(jnp.float32),
        )
        query_pre_grad, key_pre_grad, gain_query_part, gain_key_part = heads_pull(
            (
                to_tokens(query_side, group_width).reshape(micro_rows, query_local, head_width),
                key_side.reshape(micro_rows, kv_local, head_width),
            )
        )
        gain_query_acc = gain_query_acc + gain_query_part
        gain_key_acc = gain_key_acc + gain_key_part
        query_pre_low = query_pre_grad.astype(jnp.bfloat16)
        key_pre_low = key_pre_grad.astype(jnp.bfloat16)
        value_pre_low = value_side.astype(jnp.bfloat16)
        query_acc = query_acc + dot_first(normed_reduced, query_pre_low)
        key_acc = key_acc + dot_first(normed_reduced, key_pre_low)
        value_acc = value_acc + dot_first(normed_reduced, value_pre_low)
        normed_grad = (
            dot_last(query_pre_low, gathered_back[0])
            + dot_last(key_pre_low, gathered_back[1])
            + dot_last(value_pre_low, gathered_back[2])
        )
        token_part, gain_attn_part = norm_pull(normed_grad)
        gain_attn_acc = gain_attn_acc + gain_attn_part
        token_share = lax.psum_scatter(
            token_part.astype(jnp.bfloat16), "tp", scatter_dimension=1, tiled=True
        ).astype(jnp.float32)
        grad_slice = lax.dynamic_slice_in_dim(
            middle_grad, group_index * slice_width, slice_width, 1
        )
        grad_parts.append((grad_slice + token_share).astype(jnp.bfloat16))
    weight_sums = (
        lax.psum_scatter(
            query_acc.astype(jnp.bfloat16), "fsdp", scatter_dimension=0, tiled=True
        ).astype(jnp.float32),
        lax.psum_scatter(
            key_acc.astype(jnp.bfloat16), "fsdp", scatter_dimension=0, tiled=True
        ).astype(jnp.float32),
        lax.psum_scatter(
            value_acc.astype(jnp.bfloat16), "fsdp", scatter_dimension=0, tiled=True
        ).astype(jnp.float32),
        lax.psum_scatter(
            out_acc.astype(jnp.bfloat16), "fsdp", scatter_dimension=0, tiled=True
        ).astype(jnp.float32),
    )
    small_sums = lax.psum(
        (gain_attn_acc, gain_query_acc, gain_key_acc, gain_moe_acc, router_acc), ("fsdp", "tp")
    )
    return (
        jnp.concatenate(out_parts, axis=0),
        jnp.concatenate(grad_parts, axis=0),
        small_sums[0],
        weight_sums[0],
        weight_sums[1],
        weight_sums[2],
        weight_sums[3],
        small_sums[1],
        small_sums[2],
        small_sums[3],
        small_sums[4],
        gate_acc[None],
        up_acc[None],
        down_acc[None],
    )


MESH = pl.DeviceIdType.MESH


def place():
    f = lax.axis_index("fsdp")
    t = lax.axis_index("tp")
    return f // 2, f % 2, t // 2, t % 2


def device(z, x, y, c):
    return (z * 2 + x, y * 2 + c)


def greet(devices):
    barrier = pltpu.get_barrier_semaphore()
    total = 0
    for valid, where in devices:
        if valid is None:
            pl.semaphore_signal(barrier, inc=1, device_id=where, device_id_type=MESH)
            total = total + 1
        else:
            @pl.when(valid)
            def _():
                pl.semaphore_signal(barrier, inc=1, device_id=where, device_id_type=MESH)
            total = total + valid.astype(jnp.int32)
    pl.semaphore_wait(barrier, total)


def remote(src, dst, send, recv, where):
    return pltpu.make_async_remote_copy(
        src_ref=src, dst_ref=dst, send_sem=send, recv_sem=recv, device_id=where, device_id_type=MESH
    )


def gather_all_kernel(nz, x_ref, o_ref, lsem, s_p, s_u, s_d, s_x, s_y, s_dx, s_dy,
                      r_z, r_x, r_y, r_dx, r_dy, r_p):
    z, x, y, c = place()
    rows, cols = x_ref.shape
    half = rows // 2
    partner = device(z, x, y, 1 - c)
    xn = device(z, 1 - x, y, c)
    yn = device(z, x, 1 - y, c)
    up = device(z + 1, x, y, c)
    down = device(z - 1, x, y, c)
    greet([(None, partner), (None, xn), (None, yn), (z < nz - 1, up), (z > 0, down)])

    def block(zz, xx, yy, cc, part=None):
        start = (zz * 2 + xx) * rows
        size = rows
        if part is not None:
            start = start + part * half
            size = half
        return o_ref.at[pl.ds(pl.multiple_of(start, half), size),
                        pl.ds(pl.multiple_of((yy * 2 + cc) * cols, cols), cols)]

    own = pltpu.make_async_copy(x_ref, block(z, x, y, c), lsem)
    own.start()

    items = [(0, 0)]
    for dist in range(1, nz):
        items += [(dist, -1), (dist, 1)]

    def guard(item, fn):
        dist, side = item
        zz = z + side * dist
        if dist == 0:
            fn(zz)
        else:
            pl.when((zz >= 0) & (zz < nz))(lambda: fn(zz))

    def c_z(zz, src):
        dst = block(zz, x, y, c)
        return (remote(src, dst, s_u.at[zz], r_z.at[zz], up),
                remote(src, dst, s_d.at[zz], r_z.at[zz], down))

    def c_xy(zz, src):
        dst = block(zz, x, y, c)
        return (remote(src, dst, s_x.at[zz], r_x.at[zz], xn),
                remote(src, dst, s_y.at[zz], r_y.at[zz], yn))

    def c_p(zz, rel, src=None):
        xx = 1 - x if rel in (1, 3, 4) else x
        yy = 1 - y if rel in (2, 3, 4) else y
        part = {3: 0, 4: 1}.get(rel)
        dst = block(zz, xx, yy, c, part)
        k = zz * 5 + rel
        return remote(dst if src is None else src, dst, s_p.at[k], r_p.at[k], partner)

    def w_p(zz, rel):
        xx = 1 - x if rel in (1, 3, 4) else x
        yy = 1 - y if rel in (2, 3, 4) else y
        part = {3: 0, 4: 1}.get(rel)
        dst = block(zz, xx, yy, 1 - c, part)
        k = zz * 5 + rel
        return remote(dst, dst, s_p.at[k], r_p.at[k], partner)

    def c_diag(zz):
        a = block(zz, 1 - x, y, c, 0)
        b = block(zz, x, 1 - y, c, 1)
        return (remote(a, a, s_dy.at[zz], r_dy.at[zz], yn),
                remote(b, b, s_dx.at[zz], r_dx.at[zz], xn))

    def stage_a(item):
        dist, side = item

        def run(zz):
            src = x_ref if dist == 0 else block(zz, x, y, c)
            cu, cd = c_z(zz, src)
            if dist:
                cu.wait_recv()
            if side <= 0:
                pl.when(z < nz - 1)(cu.start)
            if dist == 0 or side > 0:
                pl.when(z > 0)(cd.start)
            for cc in c_xy(zz, src):
                cc.start()
            c_p(zz, 0, src).start()

        guard(item, run)

    def stage_b(item):
        def run(zz):
            cx, cy = c_xy(zz, block(zz, x, y, c))
            dy, dx = c_diag(zz)
            cx.wait_recv()
            dy.start()
            c_p(zz, 1).start()
            cy.wait_recv()
            dx.start()
            c_p(zz, 2).start()

        guard(item, run)

    def stage_c(item):
        def run(zz):
            dy, dx = c_diag(zz)
            dy.wait_recv()
            c_p(zz, 3).start()
            dx.wait_recv()
            c_p(zz, 4).start()

        guard(item, run)

    count = len(items)
    for k in range(count + 2):
        if k < count:
            stage_a(items[k])
        if 0 <= k - 1 < count:
            stage_b(items[k - 1])
        if 0 <= k - 2 < count:
            stage_c(items[k - 2])

    def finish(zz, carry):
        for rel in range(5):
            w_p(zz, rel).wait_recv()
            c_p(zz, rel).wait_send()
        cu, cd = c_z(zz, block(zz, x, y, c))
        pl.when((zz <= z) & (z < nz - 1))(cu.wait_send)
        pl.when((zz >= z) & (z > 0))(cd.wait_send)
        for cc in c_xy(zz, block(zz, x, y, c)) + c_diag(zz):
            cc.wait_send()
        return carry

    lax.fori_loop(0, nz, finish, 0)
    own.wait()


def gather_all(block, nz, collective_id):
    rows, cols = block.shape
    dma = pltpu.SemaphoreType.DMA
    return pl.pallas_call(
        functools.partial(gather_all_kernel, nz),
        out_shape=jax.ShapeDtypeStruct((rows * nz * 2, cols * 4), block.dtype),
        in_specs=[pl.BlockSpec(memory_space=pl.ANY)],
        out_specs=pl.BlockSpec(memory_space=pl.ANY),
        scratch_shapes=[dma] + [dma((5 * nz,))] + [dma((nz,))] * 6 + [dma((nz,))] * 5 + [dma((5 * nz,))],
        compiler_params=pltpu.CompilerParams(collective_id=collective_id, has_side_effects=True),
        name="gather_all",
    )(block)


def scatter_all_kernel(nz, p_ref, o_ref, w, lp, rx, rxd, ry, ryd, rz,
                       s_l, s_p, r_p, s_x, s_y, s_dx, s_dy, s_z, r_x, r_y, r_dx, r_dy, r_z):
    z, x, y, c = place()
    rows, cols = o_ref.shape
    half = rows // 2
    partner = device(z, x, y, 1 - c)
    xn = device(z, 1 - x, y, c)
    yn = device(z, x, 1 - y, c)
    up = device(z + 1, x, y, c)
    down = device(z - 1, x, y, c)
    greet([(None, partner), (None, xn), (None, yn), (z < nz - 1, up), (z > 0, down)])
    chunk = 64

    def block(zz, rel, cc):
        xx = 1 - x if rel in (1, 3) else x
        yy = 1 - y if rel in (2, 3) else y
        return p_ref.at[pl.ds(pl.multiple_of((zz * 2 + xx) * rows, rows), rows),
                        pl.ds(pl.multiple_of((yy * 2 + cc) * cols, cols), cols)]

    items = []
    for dist in range(nz - 1, 0, -1):
        items += [(dist, -1), (dist, 1)]
    items += [(0, 0)]

    def guard(item, fn):
        dist, side = item
        zz = z + side * dist
        if dist == 0:
            fn(zz)
        else:
            pl.when((zz >= 0) & (zz < nz))(lambda: fn(zz))

    def c_p(zz, rel):
        k = zz * 4 + rel
        return remote(block(zz, rel, 1 - c), lp.at[zz, rel], s_p.at[k], r_p.at[k], partner)

    def c_l(zz, rel):
        return pltpu.make_async_copy(block(zz, rel, c), w.at[zz, rel], s_l.at[zz * 4 + rel])

    def c_diag(zz):
        return (remote(w.at[zz, 3, pl.ds(0, half)], rxd.at[zz], s_dx.at[zz], r_dx.at[zz], xn),
                remote(w.at[zz, 3, pl.ds(half, half)], ryd.at[zz], s_dy.at[zz], r_dy.at[zz], yn))

    def c_xy(zz):
        return (remote(w.at[zz, 1], rx.at[zz], s_x.at[zz], r_x.at[zz], xn),
                remote(w.at[zz, 2], ry.at[zz], s_y.at[zz], r_y.at[zz], yn))

    def c_z(zz, slot, where):
        return remote(w.at[zz, 0], rz.at[slot], s_z.at[zz], r_z.at[slot], where)

    def add(dst, srcs, start, count):
        def step(i, carry):
            off = pl.multiple_of(i * chunk, chunk)
            here = pl.ds(pl.multiple_of(start + off, chunk), chunk)
            total = dst[here, :].astype(jnp.float32)
            for src in srcs:
                total = total + src[pl.ds(off, chunk), :].astype(jnp.float32)
            dst[here, :] = total.astype(dst.dtype)
            return carry
        lax.fori_loop(0, count // chunk, step, 0)

    def stage_0(item):
        def run(zz):
            for rel in (3, 1, 2, 0):
                c_p(zz, rel).start()
                c_l(zz, rel).start()
        guard(item, run)

    def stage_d(item):
        def run(zz):
            for rel in (3, 1, 2, 0):
                c_p(zz, rel).wait_recv()
                c_l(zz, rel).wait()
                add(w.at[zz, rel], [lp.at[zz, rel]], 0, rows)
                if rel == 3:
                    for cc in c_diag(zz):
                        cc.start()
        guard(item, run)

    def stage_e(item):
        def run(zz):
            dx, dy = c_diag(zz)
            cx, cy = c_xy(zz)
            dy.wait_recv()
            add(w.at[zz, 1], [ryd.at[zz]], half, half)
            cx.start()
            dx.wait_recv()
            add(w.at[zz, 2], [rxd.at[zz]], 0, half)
            cy.start()
        guard(item, run)

    def stage_f(item):
        dist, side = item

        def run(zz):
            cx, cy = c_xy(zz)
            cx.wait_recv()
            cy.wait_recv()
            if dist:
                add(w.at[zz, 0], [rx.at[zz], ry.at[zz]], 0, rows)
                has = z > 0 if side > 0 else z < nz - 1
                cz = c_z(zz, zz, up if side > 0 else down)

                @pl.when(has)
                def _():
                    cz.wait_recv()
                    add(w.at[zz, 0], [rz.at[zz]], 0, rows)
                if side > 0:
                    cz.start()
                else:
                    if dist == 1:
                        c_z(zz, nz, down).start()
                    else:
                        cz.start()
            else:
                below, above = c_z(zz, zz, up), c_z(zz, nz, down)

                def total(refs):
                    def step(i, carry):
                        here = pl.ds(pl.multiple_of(i * chunk, chunk), chunk)
                        acc = w[zz, 0, here, :].astype(jnp.float32)
                        for ref in refs:
                            acc = acc + ref[here, :].astype(jnp.float32)
                        o_ref[here, :] = acc
                        return carry
                    lax.fori_loop(0, rows // chunk, step, 0)

                pl.when(z > 0)(below.wait_recv)
                pl.when(z < nz - 1)(above.wait_recv)
                pl.when(z == 0)(lambda: total([rx.at[zz], ry.at[zz], rz.at[nz]]))
                pl.when(z == nz - 1)(lambda: total([rx.at[zz], ry.at[zz], rz.at[zz]]))
                pl.when((z > 0) & (z < nz - 1))(
                    lambda: total([rx.at[zz], ry.at[zz], rz.at[zz], rz.at[nz]]))
        guard(item, run)

    for item in items:
        stage_0(item)
    count = len(items)
    for k in range(count + 2):
        if k < count:
            stage_d(items[k])
        if 0 <= k - 1 < count:
            stage_e(items[k - 1])
        if 0 <= k - 2 < count:
            stage_f(items[k - 2])

    def finish(zz, carry):
        for rel in range(4):
            c_p(zz, rel).wait_send()
        for cc in c_diag(zz) + c_xy(zz):
            cc.wait_send()
        pl.when(zz != z)(c_z(zz, zz, up).wait_send)
        return carry

    lax.fori_loop(0, nz, finish, 0)


def scatter_all(partial, nz, collective_id):
    rows, cols = partial.shape[0] // (2 * nz), partial.shape[1] // 4
    half = rows // 2
    dma = pltpu.SemaphoreType.DMA
    kind = partial.dtype
    vm = pltpu.VMEM
    return pl.pallas_call(
        functools.partial(scatter_all_kernel, nz),
        out_shape=jax.ShapeDtypeStruct((rows, cols), jnp.float32),
        in_specs=[pl.BlockSpec(memory_space=pl.ANY)],
        out_specs=pl.BlockSpec(memory_space=pltpu.VMEM),
        scratch_shapes=[vm((nz, 4, rows, cols), kind), vm((nz, 4, rows, cols), kind),
                        vm((nz, rows, cols), kind), vm((nz, half, cols), kind),
                        vm((nz, rows, cols), kind), vm((nz, half, cols), kind),
                        vm((nz + 1, rows, cols), kind)]
        + [dma((4 * nz,))] * 3 + [dma((nz,))] * 5 + [dma((nz,))] * 4 + [dma((nz + 1,))],
        compiler_params=pltpu.CompilerParams(collective_id=collective_id, has_side_effects=True,
                                             vmem_limit_bytes=48 << 20),
        name="scatter_all",
    )(partial)


def z_items(nz, near_first):
    items = [(0, 0)] if near_first else []
    order = range(1, nz) if near_first else range(nz - 1, 0, -1)
    for dist in order:
        items += [(dist, -1), (dist, 1)]
    return items if near_first else items + [(0, 0)]


def z_guard(item, z, nz, fn):
    dist, side = item
    zz = z + side * dist
    if dist == 0:
        fn(zz)
    else:
        pl.when((zz >= 0) & (zz < nz))(lambda: fn(zz))


def gather_rows_kernel(nz, count, columns, *refs):
    total = count + columns
    srcs, refs = refs[:total], refs[total:]
    outs, refs = refs[:total], refs[total:]
    wide, refs = refs[: min(columns, 1)], refs[min(columns, 1) :]
    lsem, s_u, s_d, s_x, r_z, r_x, s_c, r_c, s_w, r_w = refs
    z, x, y, c = place()
    xn, up, down = device(z, 1 - x, y, c), device(z + 1, x, y, c), device(z - 1, x, y, c)
    partner, yn = device(z, x, y, 1 - c), device(z, x, 1 - y, c)
    wanted = [(None, xn), (z < nz - 1, up), (z > 0, down)]
    greet(wanted + [(None, partner), (None, yn), (None, device(nz - 1 - z, 1 - x, y, c))] * min(columns, 1))

    def block(n, zz, xx):
        rows = srcs[n].shape[0]
        return outs[n].at[pl.ds(pl.multiple_of((zz * 2 + xx) * rows, rows), rows)]

    own = [(srcs[n], block(n, z, x)) for n in range(count)]
    column_copies, swaps = [], []
    if columns:
        mirror = device(nz - 1 - z, 1 - x, y, c)
        first, out = outs[count], wide[0]
        rows, cols = first.shape
        top, bottom = pl.ds(0, rows // 2), pl.ds(rows // 2, rows // 2)
        for n in range(columns):
            src, dst = srcs[count + n], outs[count + n]
            swaps.append(remote(src.at[bottom], dst.at[bottom], s_w.at[n], r_w.at[n], mirror))
            own.append((src.at[top], dst.at[top]))

        def column(yy):
            return out.at[:, pl.ds(pl.multiple_of((yy * 2 + c) * cols, cols), cols)]

        column_copies = [
            remote(first, column(y), s_c.at[0], r_c.at[0], yn),
            remote(first, column(y), s_c.at[1], r_c.at[1], partner),
            remote(column(1 - y), column(1 - y), s_c.at[2], r_c.at[2], partner),
        ]
        last = pltpu.make_async_copy(first, column(y), lsem.at[total])
    own = [pltpu.make_async_copy(src, dst, lsem.at[n]) for n, (src, dst) in enumerate(own)]
    for copy in swaps + own:
        copy.start()

    def copies(n, zz, src):
        dst = block(n, zz, x)
        k = n * nz + zz
        return (remote(src, dst, s_u.at[k], r_z.at[k], up),
                remote(src, dst, s_d.at[k], r_z.at[k], down),
                remote(src, dst, s_x.at[k], r_x.at[k], xn))

    for item in z_items(nz, True):
        dist, side = item

        def run(zz):
            for n in range(count):
                src = srcs[n] if dist == 0 else block(n, zz, x)
                cu, cd, cx = copies(n, zz, src)
                if dist:
                    cu.wait_recv()
                if side <= 0:
                    pl.when(z < nz - 1)(cu.start)
                if side > 0 or dist == 0:
                    pl.when(z > 0)(cd.start)
                cx.start()

        z_guard(item, z, nz, run)
        if columns and dist == 0:
            own[count].wait()
            swaps[0].wait_recv()
            column_copies[0].start()
            column_copies[1].start()
            last.start()
        if columns and item == (1, 1):
            column_copies[0].wait_recv()
            column_copies[2].start()

    def finish(zz, carry):
        for n in range(count):
            cu, cd, cx = copies(n, zz, block(n, zz, x))
            cx.wait_recv()
            cx.wait_send()
            pl.when((zz <= z) & (z < nz - 1))(cu.wait_send)
            pl.when((zz >= z) & (z > 0))(cd.wait_send)
        return carry

    lax.fori_loop(0, nz, finish, 0)
    for n, copy in enumerate(own):
        if n != count:
            copy.wait()
    if columns:
        column_copies[0].wait_send()
        column_copies[1].wait()
        column_copies[2].wait()
        last.wait()
        swaps[0].wait_send()
        for copy in swaps[1:]:
            copy.wait()


def gather_rows(blocks, nz, collective_id, swapped=()):
    count, columns = len(blocks), len(swapped)
    dma = pltpu.SemaphoreType.DMA
    any_space = pl.BlockSpec(memory_space=pl.ANY)
    shapes = [
        jax.ShapeDtypeStruct((b.shape[0] * nz * 2,) + b.shape[1:], b.dtype) for b in blocks
    ] + [jax.ShapeDtypeStruct(b.shape, b.dtype) for b in swapped]
    if columns:
        rows, cols = swapped[0].shape
        shapes.append(jax.ShapeDtypeStruct((rows, cols * 4), swapped[0].dtype))
    total = count + columns
    return pl.pallas_call(
        functools.partial(gather_rows_kernel, nz, count, columns),
        out_shape=shapes,
        in_specs=[any_space] * total,
        out_specs=[any_space] * len(shapes),
        scratch_shapes=[dma((total + 1,))] + [dma((count * nz,))] * 5 + [dma((3,))] * 2
        + [dma((max(columns, 1),))] * 2,
        compiler_params=pltpu.CompilerParams(collective_id=collective_id, has_side_effects=True),
        name="gather_rows",
    )(*blocks, *swapped)


def swap_back_kernel(nz, *refs):
    count = (len(refs) - 2) // 2
    srcs, outs = refs[:count], refs[count : 2 * count]
    s, r = refs[2 * count :]
    z, x, y, c = place()
    mirror = device(nz - 1 - z, 1 - x, y, c)
    greet([(None, mirror)])
    copies = [remote(src, out, s.at[n], r.at[n], mirror)
              for n, (src, out) in enumerate(zip(srcs, outs))]
    for copy in copies:
        copy.start()
    for copy in copies:
        copy.wait()


def swap_back(blocks, nz, collective_id):
    count = len(blocks)
    dma = pltpu.SemaphoreType.DMA
    any_space = pl.BlockSpec(memory_space=pl.ANY)
    return pl.pallas_call(
        functools.partial(swap_back_kernel, nz),
        out_shape=[jax.ShapeDtypeStruct(b.shape, b.dtype) for b in blocks],
        in_specs=[any_space] * count,
        out_specs=[any_space] * count,
        scratch_shapes=[dma((count,))] * 2,
        compiler_params=pltpu.CompilerParams(collective_id=collective_id, has_side_effects=True),
        name="swap_back",
    )(*blocks)


def add_blocks(dst, srcs, start, count, out=None, chunk=64):
    target = dst if out is None else out

    def step(i, carry):
        off = pl.multiple_of(i * chunk, chunk)
        here = pl.ds(pl.multiple_of(start + off, chunk), chunk)
        total = dst[here, :].astype(jnp.float32)
        for src in srcs:
            total = total + src[pl.ds(off, chunk), :].astype(jnp.float32)
        target[here, :] = total.astype(target.dtype)
        return carry

    lax.fori_loop(0, count // chunk, step, 0)


def reduce_rows_kernel(nz, p_ref, o_ref, w, rx, rz, s_l, s_x, s_z, r_x, r_z):
    z, x, y, c = place()
    rows = o_ref.shape[0]
    xn, up, down = device(z, 1 - x, y, c), device(z + 1, x, y, c), device(z - 1, x, y, c)
    greet([(None, xn), (z < nz - 1, up), (z > 0, down)])

    def block(zz, xx):
        return p_ref.at[pl.ds(pl.multiple_of((zz * 2 + xx) * rows, rows), rows)]

    def c_x(zz):
        return remote(block(zz, 1 - x), rx.at[zz], s_x.at[zz], r_x.at[zz], xn)

    def c_l(zz):
        return pltpu.make_async_copy(block(zz, x), w.at[zz], s_l.at[zz])

    def c_z(zz, slot, where):
        return remote(w.at[zz], rz.at[slot], s_z.at[zz], r_z.at[slot], where)

    items = z_items(nz, False)

    def start(zz):
        c_x(zz).start()
        c_l(zz).start()

    for item in items:
        z_guard(item, z, nz, start)
    for item in items:
        dist, side = item

        def run(zz):
            c_l(zz).wait()
            c_x(zz).wait_recv()
            if dist:
                add_blocks(w.at[zz], [rx.at[zz]], 0, rows)
                cz = c_z(zz, zz, up if side > 0 else down)

                @pl.when(z > 0 if side > 0 else z < nz - 1)
                def _():
                    cz.wait_recv()
                    add_blocks(w.at[zz], [rz.at[zz]], 0, rows)

                (c_z(zz, nz, down) if side < 0 and dist == 1 else cz).start()
            else:
                pl.when(z > 0)(c_z(zz, zz, up).wait_recv)
                pl.when(z < nz - 1)(c_z(zz, nz, down).wait_recv)
                low, high = rz.at[zz], rz.at[nz]
                pl.when(z == 0)(lambda: add_blocks(w.at[zz], [rx.at[zz], high], 0, rows, o_ref))
                pl.when(z == nz - 1)(lambda: add_blocks(w.at[zz], [rx.at[zz], low], 0, rows, o_ref))
                pl.when((z > 0) & (z < nz - 1))(
                    lambda: add_blocks(w.at[zz], [rx.at[zz], low, high], 0, rows, o_ref)
                )

        z_guard(item, z, nz, run)

    def finish(zz, carry):
        c_x(zz).wait_send()
        pl.when(zz != z)(c_z(zz, zz, up).wait_send)
        return carry

    lax.fori_loop(0, nz, finish, 0)


def reduce_rows(partial, nz, collective_id):
    rows, cols = partial.shape[0] // (2 * nz), partial.shape[1]
    dma, vm, kind = pltpu.SemaphoreType.DMA, pltpu.VMEM, partial.dtype
    return pl.pallas_call(
        functools.partial(reduce_rows_kernel, nz),
        out_shape=jax.ShapeDtypeStruct((rows, cols), jnp.float32),
        in_specs=[pl.BlockSpec(memory_space=pl.ANY)],
        out_specs=pl.BlockSpec(memory_space=pltpu.VMEM),
        scratch_shapes=[vm((nz, rows, cols), kind), vm((nz, rows, cols), kind),
                        vm((nz + 1, rows, cols), kind)]
        + [dma((nz,))] * 4 + [dma((nz + 1,))],
        compiler_params=pltpu.CompilerParams(
            collective_id=collective_id, has_side_effects=True, vmem_limit_bytes=48 << 20
        ),
        name="reduce_rows",
    )(partial)


def gather_cols_kernel(x_ref, o_ref, lsem, s_p, s_y, r_p, r_y):
    z, x, y, c = place()
    cols = x_ref.shape[1]
    partner, yn = device(z, x, y, 1 - c), device(z, x, 1 - y, c)
    greet([(None, partner), (None, yn)])

    def block(yy, cc):
        return o_ref.at[:, pl.ds(pl.multiple_of((yy * 2 + cc) * cols, cols), cols)]

    own = pltpu.make_async_copy(x_ref, block(y, c), lsem)
    cy = remote(x_ref, block(y, c), s_y, r_y, yn)
    cp = remote(x_ref, block(y, c), s_p.at[0], r_p.at[0], partner)
    cf = remote(block(1 - y, c), block(1 - y, c), s_p.at[1], r_p.at[1], partner)
    cy.start()
    cp.start()
    own.start()
    cy.wait_recv()
    cf.start()
    cp.wait()
    cf.wait()
    cy.wait_send()
    own.wait()


def gather_cols(block, collective_id):
    dma = pltpu.SemaphoreType.DMA
    any_space = pl.BlockSpec(memory_space=pl.ANY)
    return pl.pallas_call(
        gather_cols_kernel,
        out_shape=jax.ShapeDtypeStruct((block.shape[0], block.shape[1] * 4), block.dtype),
        in_specs=[any_space],
        out_specs=any_space,
        scratch_shapes=[dma, dma((2,)), dma, dma((2,)), dma],
        compiler_params=pltpu.CompilerParams(collective_id=collective_id, has_side_effects=True),
        name="gather_cols",
    )(block)


def reduce_cols_kernel(p_ref, o_ref, w, rp, ry, s_l, s_p, s_y, r_p, r_y):
    z, x, y, c = place()
    rows, cols = o_ref.shape
    partner, yn = device(z, x, y, 1 - c), device(z, x, 1 - y, c)
    greet([(None, partner), (None, yn)])

    def block(yy, cc):
        return p_ref.at[:, pl.ds(pl.multiple_of((yy * 2 + cc) * cols, cols), cols)]

    sends = [remote(block(yy, 1 - c), rp.at[k], s_p.at[k], r_p.at[k], partner)
             for k, yy in enumerate((1 - y, y))]
    loads = [pltpu.make_async_copy(block(yy, c), w.at[k], s_l.at[k])
             for k, yy in enumerate((1 - y, y))]
    cy = remote(w.at[0], ry, s_y, r_y, yn)
    for k in range(2):
        sends[k].start()
        loads[k].start()
    loads[0].wait()
    sends[0].wait_recv()
    add_blocks(w.at[0], [rp.at[0]], 0, rows)
    cy.start()
    loads[1].wait()
    sends[1].wait_recv()
    cy.wait_recv()
    add_blocks(w.at[1], [rp.at[1], ry], 0, rows, o_ref)
    for k in range(2):
        sends[k].wait_send()
    cy.wait_send()


def reduce_cols(partial, collective_id):
    rows, cols = partial.shape[0], partial.shape[1] // 4
    dma, vm, kind = pltpu.SemaphoreType.DMA, pltpu.VMEM, partial.dtype
    return pl.pallas_call(
        reduce_cols_kernel,
        out_shape=jax.ShapeDtypeStruct((rows, cols), jnp.float32),
        in_specs=[pl.BlockSpec(memory_space=pl.ANY)],
        out_specs=pl.BlockSpec(memory_space=pltpu.VMEM),
        scratch_shapes=[vm((2, rows, cols), kind), vm((2, rows, cols), kind), vm((rows, cols), kind),
                        dma((2,)), dma((2,)), dma, dma((2,)), dma],
        compiler_params=pltpu.CompilerParams(
            collective_id=collective_id, has_side_effects=True, vmem_limit_bytes=24 << 20
        ),
        name="reduce_cols",
    )(partial)


def sum_cols_kernel(v_ref, o_ref, got, s, r):
    group = lax.axis_index("tp")
    shard = lax.axis_index("fsdp")
    peers = [(shard, (group + k) % 4) for k in range(1, 4)]
    greet([(None, peer) for peer in peers])
    copies = [remote(v_ref, got.at[k], s.at[k], r.at[k], peer) for k, peer in enumerate(peers)]
    for copy in copies:
        copy.start()
    for copy in copies:
        copy.wait()
    o_ref[...] = v_ref[...] + got[0] + got[1] + got[2]


def sum_cols(vector, collective_id):
    dma = pltpu.SemaphoreType.DMA
    shape = vector.shape
    return pl.pallas_call(
        sum_cols_kernel,
        out_shape=jax.ShapeDtypeStruct(shape, jnp.float32),
        in_specs=[pl.BlockSpec(memory_space=pltpu.VMEM)],
        out_specs=pl.BlockSpec(memory_space=pltpu.VMEM),
        scratch_shapes=[pltpu.VMEM((3,) + shape, jnp.float32), dma((3,)), dma((3,))],
        compiler_params=pltpu.CompilerParams(collective_id=collective_id, has_side_effects=True),
        name="sum_cols",
    )(vector)


def greet_all(shard, group, shards, groups):
    barrier = pltpu.get_barrier_semaphore()
    total = shards * groups

    def step(k, carry):
        other = (shard * groups + group + k) % total
        pl.semaphore_signal(
            barrier, inc=1, device_id=(other // groups, other % groups), device_id_type=MESH
        )
        return carry

    lax.fori_loop(1, total, step, 0)
    pl.semaphore_wait(barrier, total - 1)


def swap_rows_kernel(shards, groups, v_ref, o_ref, s, r):
    shard, group = lax.axis_index("fsdp"), lax.axis_index("tp")
    total = shards * groups
    me = shard * groups + group
    greet_all(shard, group, shards, groups)

    def copy(k):
        other = (me + k) % total
        return remote(v_ref.at[other // groups], o_ref.at[me], s.at[k], r.at[k],
                      (other // groups, other % groups))

    def start(k, carry):
        copy(k).start()
        return carry

    def wait(k, carry):
        copy(k).wait()
        return carry

    lax.fori_loop(1, total, start, 0)
    o_ref[me] = v_ref[shard]
    lax.fori_loop(1, total, wait, 0)


def swap_rows(values, shards, groups, collective_id):
    dma, total = pltpu.SemaphoreType.DMA, shards * groups
    return pl.pallas_call(
        functools.partial(swap_rows_kernel, shards, groups),
        out_shape=jax.ShapeDtypeStruct((total,) + values.shape[1:], values.dtype),
        in_specs=[pl.BlockSpec(memory_space=pltpu.VMEM)],
        out_specs=pl.BlockSpec(memory_space=pltpu.VMEM),
        scratch_shapes=[dma((total,)), dma((total,))],
        compiler_params=pltpu.CompilerParams(collective_id=collective_id, has_side_effects=True),
        name="swap_rows",
    )(values)


def sum_small_kernel(shards, groups, v_ref, o_ref, got, s1, r1, s2, r2):
    shard, group = lax.axis_index("fsdp"), lax.axis_index("tp")
    total = shards * groups
    me = shard * groups + group
    greet_all(shard, group, shards, groups)

    def first(k):
        other = (shard + k) % shards
        return remote(v_ref.at[other], got.at[k], s1.at[k], r1.at[k], (other, group))

    def second(k):
        other = (me + k) % total
        return remote(o_ref.at[me], o_ref.at[me], s2.at[k], r2.at[k],
                      (other // groups, other % groups))

    for k in range(1, shards):
        first(k).start()
    acc = v_ref[shard]
    for k in range(1, shards):
        first(k).wait()
        acc = acc + got[k]
    o_ref[me] = acc

    def start(k, carry):
        second(k).start()
        return carry

    def wait(k, carry):
        second(k).wait()
        return carry

    lax.fori_loop(1, total, start, 0)
    lax.fori_loop(1, total, wait, 0)


def sum_small(values, shards, groups, collective_id):
    dma, total = pltpu.SemaphoreType.DMA, shards * groups
    part = values.shape[1:]
    return pl.pallas_call(
        functools.partial(sum_small_kernel, shards, groups),
        out_shape=jax.ShapeDtypeStruct((total,) + part, values.dtype),
        in_specs=[pl.BlockSpec(memory_space=pltpu.VMEM)],
        out_specs=pl.BlockSpec(memory_space=pltpu.VMEM),
        scratch_shapes=[pltpu.VMEM((shards,) + part, values.dtype), dma((shards,)), dma((shards,)),
                        dma((total,)), dma((total,))],
        compiler_params=pltpu.CompilerParams(collective_id=collective_id, has_side_effects=True),
        name="sum_small",
    )(values)


def dot_plain(left, right):
    return jnp.dot(left, right, preferred_element_type=jnp.float32)


def far_first(nz, z, k):
    at = 0
    for here in range(nz):
        order = sorted(range(nz), key=lambda other: (-abs(other - here), other))
        for step, other in enumerate(order):
            at = at + jnp.where((z == here) & (k == step), other, 0)
    return at


def expert_kernel(nz, slots, block_rows, x_all, g_all, routes_all, router_ref, wg, wu, wd,
                  out_all, back_ref, gg_ref, gates_ref, xr_all, gs_all, hid_all, gp_all, up_all,
                  x_ref, g_ref, t_ref, o_ref, xr, gs, hid, gp, up, st,
                  w, lp, rx, rxd, ry, ryd, rz,
                  s_in, s_out, s_save, s_p, r_p, s_x, s_y, s_dx, s_dy, s_z, r_x, r_y, r_dx, r_dy, r_z):
    z, x, y, c = place()
    expert = lax.axis_index("fsdp") * 4 + lax.axis_index("tp")
    rows, cols = back_ref.shape
    width = x_ref.shape[1]
    half = rows // 2
    blocks = rows // block_rows
    experts = router_ref.shape[1]
    f32, low = jnp.float32, jnp.bfloat16
    partner = device(z, x, y, 1 - c)
    xn, yn = device(z, 1 - x, y, c), device(z, x, 1 - y, c)
    up_dev, down_dev = device(z + 1, x, y, c), device(z - 1, x, y, c)
    greet([(None, partner), (None, xn), (None, yn), (z < nz - 1, up_dev), (z > 0, down_dev)])
    tiles = 2 * nz

    def tile_of(j):
        return far_first(nz, z, j // 2) * 2 + jnp.where(j % 2 == 0, 1 - x, x)

    def tile_rows(j):
        return pl.ds(pl.multiple_of(tile_of(j) * rows, rows), rows)

    def load(j, kind):
        src, dst = ((x_all, x_ref), (g_all, g_ref), (routes_all, t_ref))[kind]
        return pltpu.make_async_copy(src.at[tile_rows(j)], dst, s_in.at[kind])

    def save_out(j):
        return pltpu.make_async_copy(o_ref, out_all.at[tile_rows(j)], s_out)

    def saves(j):
        pairs = ((xr, xr_all), (gs, gs_all), (hid, hid_all), (gp, gp_all), (up, up_all))
        return [pltpu.make_async_copy(src, dst.at[j], s_save.at[n])
                for n, (src, dst) in enumerate(pairs)]

    def c_p(zz, rel, slot):
        k = zz * 4 + rel
        return remote(st.at[slot, rel // 2], lp.at[zz, rel], s_p.at[k], r_p.at[k], partner)

    def c_diag(zz):
        return (remote(w.at[zz, 3, pl.ds(0, half)], rxd.at[zz], s_dx.at[zz], r_dx.at[zz], xn),
                remote(w.at[zz, 3, pl.ds(half, half)], ryd.at[zz], s_dy.at[zz], r_dy.at[zz], yn))

    def c_xy(zz):
        return (remote(w.at[zz, 1], rx.at[zz], s_x.at[zz], r_x.at[zz], xn),
                remote(w.at[zz, 2], ry.at[zz], s_y.at[zz], r_y.at[zz], yn))

    def c_z(zz, slot, where):
        return remote(w.at[zz, 0], rz.at[slot], s_z.at[zz], r_z.at[slot], where)

    def send_z(zz):
        pl.when(zz > z)(lambda: c_z(zz, zz, up_dev).start())
        pl.when(zz == z - 1)(lambda: c_z(zz, nz, down_dev).start())
        pl.when(zz < z - 1)(lambda: c_z(zz, zz, down_dev).start())

    def stage_d(zz, rel, slot):
        c_p(zz, rel, slot).wait_recv()
        add_blocks(w.at[zz, rel], [lp.at[zz, rel]], 0, rows)
        if rel == 3:
            for copy in c_diag(zz):
                copy.start()

    def stage_e(zz):
        dx, dy = c_diag(zz)
        cx, cy = c_xy(zz)
        dy.wait_recv()
        add_blocks(w.at[zz, 1], [ryd.at[zz]], half, half)
        cx.start()
        dx.wait_recv()
        add_blocks(w.at[zz, 2], [rxd.at[zz]], 0, half)
        cy.start()

    def passes(zz):
        return ((zz > z) & (z > 0)) | ((zz < z) & (z < nz - 1))

    def stage_f1(zz):
        cx, cy = c_xy(zz)
        cx.wait_recv()
        cy.wait_recv()
        add_blocks(w.at[zz, 0], [rx.at[zz], ry.at[zz]], 0, rows)
        pl.when((zz != z) & jnp.logical_not(passes(zz)))(lambda: send_z(zz))

    def stage_f2(zz):
        @pl.when((zz != z) & passes(zz))
        def _():
            c_z(zz, zz, up_dev).wait_recv()
            add_blocks(w.at[zz, 0], [rz.at[zz]], 0, rows)
            send_z(zz)

        @pl.when(zz == z)
        def _():
            low_part, high_part = rz.at[zz], rz.at[nz]
            pl.when(z > 0)(lambda: c_z(zz, zz, up_dev).wait_recv())
            pl.when(z < nz - 1)(lambda: c_z(zz, nz, down_dev).wait_recv())
            own = w.at[zz, 0]
            pl.when(z == 0)(lambda: add_blocks(own, [high_part], 0, rows, back_ref))
            pl.when(z == nz - 1)(lambda: add_blocks(own, [low_part], 0, rows, back_ref))
            pl.when((z > 0) & (z < nz - 1))(
                lambda: add_blocks(own, [low_part, high_part], 0, rows, back_ref)
            )

    def compute(j):
        zz = far_first(nz, z, j // 2)
        slot = j % 2
        load(j, 2).wait()
        load(j, 0).wait()
        lanes = lax.broadcasted_iota(jnp.int32, (rows, experts), 1)
        routes = t_ref[...]
        chosen = routes[:, 0:1] == lanes
        for n in range(1, TOPK):
            chosen = chosen | (routes[:, n : n + 1] == lanes)
        logits = jnp.where(chosen, dot_plain(x_ref[...], router_ref[...]), masked_score)
        peak = jnp.max(logits, axis=1, keepdims=True)
        weights = jnp.where(chosen, jnp.exp(logits - peak), 0.0)
        gates = weights / jnp.sum(weights, axis=1, keepdims=True)
        gates_ref[...] = gates
        mine = lanes == expert
        gate_col = jnp.sum(jnp.where(mine, gates, 0.0), axis=1, keepdims=True)
        match_col = jnp.sum(jnp.where(mine & chosen, 1.0, 0.0), axis=1, keepdims=True)
        sub = lax.broadcasted_iota(jnp.int32, (block_rows, block_rows), 0)
        lane = lax.broadcasted_iota(jnp.int32, (block_rows, block_rows), 1)
        eye = sub == lane
        before = (sub > lane).astype(f32).astype(low)
        chosen_low = chosen.astype(f32).astype(low)
        pick, put, slot_gate = [], [], []
        slot_lane = lax.broadcasted_iota(jnp.int32, (block_rows, slots), 1).astype(f32)
        slot_sub = lax.broadcasted_iota(jnp.int32, (slots, block_rows), 0).astype(f32)
        for b in range(blocks):
            part = slice(b * block_rows, (b + 1) * block_rows)
            ranks = dot_plain(before, chosen_low[part])
            rank = jnp.sum(jnp.where(mine[part], ranks, 0.0), axis=1, keepdims=True)
            rank = jnp.where(match_col[part] > 0.0, rank, -1.0)
            rank_row = jnp.sum(jnp.where(eye, rank, 0.0), axis=0, keepdims=True)
            gate_row = jnp.sum(jnp.where(eye, gate_col[part], 0.0), axis=0, keepdims=True)
            hot = rank_row == slot_sub
            pick.append(hot.astype(f32).astype(low))
            put.append((rank == slot_lane).astype(f32).astype(low))
            slot_gate.append(jnp.sum(jnp.where(hot, gate_row, 0.0), axis=1, keepdims=True))
        slot_gate = jnp.concatenate(slot_gate, axis=0)

        def gather(ref, at):
            return jnp.concatenate(
                [dot_plain(pick[b], ref[pl.ds(b * block_rows, block_rows), at])
                 for b in range(blocks)],
                axis=0,
            )

        def scatter(ref, at, values):
            for b in range(blocks):
                ref[pl.ds(b * block_rows, block_rows), at] = dot_plain(
                    put[b], values[b * slots : (b + 1) * slots]
                ).astype(low)

        def columns(i):
            return pl.ds(pl.multiple_of(i * cols, cols), cols)

        @pl.when(j > 0)
        def _():
            for copy in saves(j):
                copy.wait()

        def take(i, carry):
            xr[:, columns(i)] = gather(x_ref, columns(i)).astype(low)
            return carry

        lax.fori_loop(0, width // cols, take, 0)

        @pl.when(j < tiles - 1)
        def _():
            load(j + 1, 2).start()
            load(j + 1, 0).start()

        gate_pre = dot_plain(xr[...], wg[...])
        up_pre = dot_plain(xr[...], wu[...])
        sig = jax.nn.sigmoid(gate_pre)
        silu = gate_pre * sig
        hidden_low = (silu * up_pre).astype(low)
        hid[...] = hidden_low
        load(j, 1).wait()
        pl.when(j > 0)(lambda: save_out(j).wait())

        def middle_part(i, carry):
            total, hidden_grad = carry
            at = columns(i)
            grad = gather(g_ref, at)
            expert_out = dot_plain(hidden_low, wd[:, at]).astype(low).astype(f32)
            total = total + jnp.sum(grad * expert_out, axis=1, keepdims=True)
            pair_grad = (grad * slot_gate).astype(low)
            gs[:, at] = pair_grad
            scatter(o_ref, at, (expert_out * slot_gate).astype(low))
            return total, hidden_grad + dot_last(pair_grad, wd[:, at])

        gates_grad, hidden_grad = lax.fori_loop(
            0,
            width // cols,
            middle_part,
            (jnp.zeros(slot_gate.shape, f32), jnp.zeros(gate_pre.shape, f32)),
        )
        save_out(j).start()
        pl.when(j < tiles - 1)(lambda: load(j + 1, 1).start())
        for b in range(blocks):
            gg_ref[tile_of(j), :, pl.ds(b * block_rows, block_rows)] = jnp.sum(
                pick[b].astype(f32) * gates_grad[b * slots : (b + 1) * slots],
                axis=0,
                keepdims=True,
            )
        gate_grad = (hidden_grad * up_pre * (sig * (1.0 + gate_pre * (1.0 - sig)))).astype(low)
        up_grad = (hidden_grad * silu).astype(low)
        gp[...] = gate_grad
        up[...] = up_grad
        for copy in saves(j):
            copy.start()

        def part_of(i, yy, cc):
            at = columns(yy * 2 + cc)
            row_grad = dot_last(gate_grad, wg[at, :]) + dot_last(up_grad, wu[at, :])
            return row_grad.astype(low)

        first = jnp.where(slot == 0, 1, 0)

        def to_partner(i, carry):
            yy = jnp.where(i == 1, 1 - y, y)
            rel = first + 2 * i

            @pl.when(j >= 2)
            def _():
                before_zz = far_first(nz, z, j // 2 - 1)
                k = before_zz * 4 + rel
                remote(st.at[slot, i], lp.at[before_zz, rel], s_p.at[k], r_p.at[k], partner).wait_send()

            scatter(st.at[slot, i], slice(None), part_of(i, yy, 1 - c))
            k = zz * 4 + rel
            remote(st.at[slot, i], lp.at[zz, rel], s_p.at[k], r_p.at[k], partner).start()
            return carry

        def to_own(i, carry):
            yy = jnp.where(i == 1, 1 - y, y)
            scatter(w.at[zz, first + 2 * i], slice(None), part_of(i, yy, c))
            return carry

        lax.fori_loop(0, 2, to_partner, 0)
        lax.fori_loop(0, 2, to_own, 0)

    for kind in (2, 0, 1):
        load(0, kind).start()

    def step(j, carry):
        k, odd = j // 2, j % 2 == 1
        pl.when(j < tiles)(lambda: compute(j))

        @pl.when(odd & (k < nz))
        def _():
            zz = far_first(nz, z, k)
            stage_d(zz, 3, 0)
            stage_d(zz, 1, 0)

        @pl.when(jnp.logical_not(odd) & (k >= 1) & (k <= nz))
        def _():
            zz = far_first(nz, z, k - 1)
            stage_d(zz, 2, 1)
            stage_d(zz, 0, 1)
            stage_e(zz)

        @pl.when((k >= 2) & jnp.logical_not(odd))
        def _():
            stage_f1(far_first(nz, z, k - 2))

        @pl.when((k >= 2) & odd)
        def _():
            stage_f2(far_first(nz, z, k - 2))

        return carry

    lax.fori_loop(0, 2 * (nz + 2), step, 0)
    save_out(tiles - 1).wait()
    for copy in saves(tiles - 1):
        copy.wait()
    for slot in range(2):
        for i in range(2):
            c_p(z, 1 - slot + 2 * i, slot).wait_send()

    def finish(zz, carry):
        for copy in c_diag(zz) + c_xy(zz):
            copy.wait_send()
        pl.when(zz != z)(c_z(zz, zz, up_dev).wait_send)
        return carry

    lax.fori_loop(0, nz, finish, 0)


def run_experts(x_all, g_all, routes_all, router, gate_w, up_w, down_w, block_rows, slots, nz,
                collective_id):
    total, width = x_all.shape
    hidden = gate_w.shape[1]
    experts = router.shape[1]
    tiles = 2 * nz
    rows, cols = total // tiles, width // 4
    pairs = rows // block_rows * slots
    half = rows // 2
    f32, low = jnp.float32, jnp.bfloat16
    any_space = pl.BlockSpec(memory_space=pl.ANY)
    vmem = pl.BlockSpec(memory_space=pltpu.VMEM)
    vm, dma, shape = pltpu.VMEM, pltpu.SemaphoreType.DMA, jax.ShapeDtypeStruct
    return pl.pallas_call(
        functools.partial(expert_kernel, nz, slots, block_rows),
        in_specs=[any_space] * 3 + [vmem] * 4,
        out_specs=[any_space, vmem, vmem, vmem] + [any_space] * 5,
        out_shape=[
            shape((total, width), low), shape((rows, cols), f32), shape((tiles, 1, rows), f32),
            shape((rows, experts), f32),
            shape((tiles, pairs, width), low), shape((tiles, pairs, width), low),
            shape((tiles, pairs, hidden), low), shape((tiles, pairs, hidden), low),
            shape((tiles, pairs, hidden), low),
        ],
        scratch_shapes=[
            vm((rows, width), low), vm((rows, width), low),
            vm((rows, routes_all.shape[1]), jnp.int32), vm((rows, width), low),
            vm((pairs, width), low), vm((pairs, width), low),
            vm((pairs, hidden), low), vm((pairs, hidden), low), vm((pairs, hidden), low),
            vm((2, 2, rows, cols), low),
            vm((nz, 4, rows, cols), low), vm((nz, 4, rows, cols), low),
            vm((nz, rows, cols), low), vm((nz, half, cols), low),
            vm((nz, rows, cols), low), vm((nz, half, cols), low),
            vm((nz + 1, rows, cols), low),
            dma((3,)), dma, dma((5,)), dma((4 * nz,)), dma((4 * nz,)),
        ] + [dma((nz,))] * 9 + [dma((nz + 1,))],
        compiler_params=pltpu.CompilerParams(
            collective_id=collective_id, has_side_effects=True, vmem_limit_bytes=62 << 20
        ),
        name="experts",
    )(x_all, g_all, routes_all, router, gate_w, up_w, down_w)


def gathered_body(
    tokens,
    cotangent,
    routes,
    doc_ids,
    gain_attn,
    w_query,
    key_weight,
    value_weight,
    w_out,
    gain_query,
    key_norm_gain,
    gain_moe,
    router,
    w_gate,
    w_up,
    w_down,
):
    shard_count = lax.axis_size("fsdp")
    group_count = lax.axis_size("tp")
    shard_index = lax.axis_index("fsdp")
    group_index = lax.axis_index("tp")
    nz = shard_count // 2
    f32, low = jnp.float32, jnp.bfloat16
    row_count, slice_width = tokens.shape
    model_width = slice_width * group_count
    micro_count, micro_rows = doc_ids.shape
    head_width = gain_query.shape[0]
    query_width, kv_width = w_query.shape[1], key_weight.shape[1]
    query_local = query_width // head_width
    kv_local = kv_width // head_width
    group_width = query_local // kv_local
    expert_total = router.shape[1]
    capacity = max(2, 2 * micro_rows * TOPK // expert_total)
    block_keys = micro_rows * math.gcd(shard_count, max(1, 512 // micro_rows))
    my_columns = group_index * slice_width

    mirror_index = shard_count - 1 - shard_index
    owners = jnp.stack([shard_index, mirror_index])

    def to_owners(array):
        return jnp.stack([array[:, 0], array[::-1, 1]], axis=1)

    small = jnp.concatenate([routes.reshape(-1), doc_ids.reshape(-1)])
    small_rows = -(-small.shape[0] // 1024) * 8
    small = jnp.pad(small, (0, small_rows * 128 - small.shape[0])).reshape(small_rows, 128)
    small_all, wq_all, wk_all, wv_all, wo_all, tokens, cotangent, full_tokens = gather_rows(
        [small, w_query, key_weight, value_weight, w_out], nz, 2, [tokens, cotangent]
    )
    small_all = small_all.reshape(shard_count, small_rows * 128)
    routes_all = to_owners(
        small_all[:, : row_count * TOPK].reshape(shard_count, micro_count, micro_rows, TOPK)
    ).reshape(shard_count * row_count, TOPK)
    ids_all = small_all[:, row_count * TOPK : row_count * (TOPK + 1)].reshape(
        shard_count, micro_count, micro_rows
    )
    doc_range = jnp.arange(DOCS)
    doc_totals = jnp.sum((ids_all[..., None] == doc_range).astype(jnp.int32), axis=(0, 2))
    doc_begin = jnp.cumsum(doc_totals, axis=1) - doc_totals
    query_index = owners[:, None] * micro_rows + jnp.arange(micro_rows)
    my_ids = jnp.stack(
        [lax.dynamic_index_in_dim(ids_all[:, m], owners[m], 0, False) for m in range(micro_count)]
    )
    query_start = jnp.sum(
        jnp.where(my_ids[:, :, None] == doc_range, doc_begin[:, None, :], 0), axis=2
    )
    positions = (query_index - query_start).reshape(row_count)
    cosine_lookup, sine_lookup = rope_tables(positions, head_width)

    full_tokens = full_tokens.astype(f32)
    grads_all = gather_all(cotangent, nz, 3)
    token_mean = jnp.mean(full_tokens * full_tokens, axis=-1, keepdims=True)
    token_scale = lax.rsqrt(token_mean + norm_eps)
    normed_low = (full_tokens * token_scale * gain_attn).astype(low)
    query_pre = jnp.dot(normed_low, wq_all, preferred_element_type=f32)
    key_pre = jnp.dot(normed_low, wk_all, preferred_element_type=f32)
    value_low = jnp.dot(normed_low, wv_all, preferred_element_type=f32).astype(low)

    def shape_heads(query_raw, key_raw, query_gain, key_gain):
        query_heads = rotary_apply(
            root_mean_norm(query_raw.reshape(row_count, query_local, head_width), query_gain),
            cosine_lookup[:, None, :],
            sine_lookup[:, None, :],
        )
        key_heads = rotary_apply(
            root_mean_norm(key_raw.reshape(row_count, kv_local, head_width), key_gain),
            cosine_lookup[:, None, :],
            sine_lookup[:, None, :],
        )
        return (query_heads, key_heads)

    (query_heads, key_heads), heads_pull = jax.vjp(
        shape_heads, query_pre, key_pre, gain_query, key_norm_gain
    )
    query_low = query_heads.astype(low)
    key_low = key_heads.reshape(row_count, kv_width).astype(low)
    keys_got, values_got = gather_rows([key_low, value_low], nz, 4)

    def by_stream(array):
        array = array.reshape(shard_count, micro_count, micro_rows, kv_width)
        return to_owners(array).transpose(1, 0, 2, 3).reshape(
            micro_count, shard_count * micro_rows, kv_width
        )

    keys_all, values_all = by_stream(keys_got), by_stream(values_got)
    row_index = jnp.tile(query_index, (1, group_width))
    saved, head_parts = [], []
    for micro_index in range(micro_count):
        here = slice(micro_index * micro_rows, (micro_index + 1) * micro_rows)
        queries = to_heads(query_low[here], kv_local, group_width)
        row_start = jnp.tile(query_start[micro_index], group_width)
        head_out, log_total = attend_forward(
            queries,
            keys_all[micro_index],
            values_all[micro_index],
            row_index[micro_index],
            row_start,
            block_keys,
        )
        saved.append((queries, row_start, head_out, log_total))
        head_parts.append(to_tokens(head_out, group_width).astype(low))
    heads_low = jnp.concatenate(head_parts, axis=0)
    attn_part = dot_last(heads_low, wo_all).astype(low)
    middle = tokens.astype(f32) + reduce_cols(attn_part, 5)

    def row_mean(values, collective_id):
        total = jnp.sum(values, axis=1).reshape(row_count // 128, 128)
        return sum_cols(total, collective_id).reshape(row_count, 1) / model_width

    scale = lax.rsqrt(row_mean(middle * middle, 6) + norm_eps)
    gain_slice = lax.dynamic_slice_in_dim(gain_moe, my_columns, slice_width)
    moe_low = (middle * scale * gain_slice).astype(low)
    moe_all = gather_all(moe_low, nz, 7)
    out_part, back, gates_grad, gates, *kept = run_experts(
        moe_all, grads_all, routes_all, router, w_gate[0], w_up[0], w_down[0],
        micro_rows, capacity, nz, 8,
    )
    rows_in, pair_grad, hidden_low, gate_pre_low, up_pre_low = (
        array.reshape(-1, array.shape[2]) for array in kept
    )
    gate_acc = dot_first(rows_in, gate_pre_low)
    up_acc = dot_first(rows_in, up_pre_low)
    down_acc = dot_first(hidden_low, pair_grad)
    gates_grad = swap_rows(
        gates_grad.reshape(shard_count, row_count // 128, 128), shard_count, group_count, 9
    ).reshape(expert_total, row_count).T
    logit_grad = gates * (gates_grad - jnp.sum(gates * gates_grad, axis=1, keepdims=True))
    router_slice = lax.dynamic_slice_in_dim(router, my_columns, slice_width).astype(f32)
    moe_grad = back + lax.dot_general(
        logit_grad, router_slice, (((1,), (1,)), ((), ())), precision=highest_precision
    )
    router_part = lax.dot_general(
        moe_low.astype(f32), logit_grad, (((0,), (0,)), ((), ())), precision=highest_precision
    )
    gain_moe_part = jnp.sum(moe_grad * middle * scale, axis=0)
    grad_slice = cotangent.astype(f32)
    inner = gain_slice * moe_grad
    middle_grad = (
        grad_slice + scale * inner - middle * scale**3 * row_mean(middle * inner, 10)
    )
    middle_low = gather_cols(middle_grad.astype(low), 11)
    out_grad_part = dot_first(middle_low, heads_low).astype(low)
    heads_grad = jnp.dot(middle_low, wo_all, preferred_element_type=f32).astype(low)
    block_out = (middle + scatter_all(out_part, nz, 12)).astype(low)
    w_out_grad = reduce_rows(out_grad_part, nz, 13)
    query_sides, key_sides = [], []
    for micro_index in range(micro_count):
        here = slice(micro_index * micro_rows, (micro_index + 1) * micro_rows)
        queries, row_start, head_out, log_total = saved[micro_index]
        grad_low = to_heads(
            heads_grad[here].reshape(micro_rows, query_local, head_width), kv_local, group_width
        )
        query_side, key_side, value_side = attend_backward(
            queries,
            keys_all[micro_index],
            values_all[micro_index],
            row_index[micro_index],
            row_start,
            block_keys,
            head_out,
            log_total,
            grad_low,
        )
        query_sides.append(to_tokens(query_side, group_width))
        key_sides.append(jnp.concatenate([key_side, value_side], axis=1).astype(low))
    sides = jnp.stack(key_sides).reshape(micro_count, shard_count, micro_rows, 2 * kv_width)
    sides = reduce_rows(
        to_owners(sides.transpose(1, 0, 2, 3)).reshape(shard_count * row_count, 2 * kv_width), nz, 14
    )
    query_pre_grad, key_pre_grad, gain_query_part, gain_key_part = heads_pull(
        (
            jnp.concatenate(query_sides, axis=0).reshape(row_count, query_local, head_width),
            sides[:, :kv_width].reshape(row_count, kv_local, head_width),
        )
    )
    query_pre_low = query_pre_grad.astype(low)
    key_pre_low = key_pre_grad.astype(low)
    value_pre_low = sides[:, kv_width:].astype(low)
    normed_part = (
        dot_last(query_pre_low, wq_all)
        + dot_last(key_pre_low, wk_all)
        + dot_last(value_pre_low, wv_all)
    ).astype(low)
    normed_grad = reduce_cols(normed_part, 15)
    pre_low = jnp.concatenate([query_pre_low, key_pre_low, value_pre_low], axis=1)
    weight_grad = reduce_rows(dot_first(normed_low, pre_low).astype(low), nz, 16)
    token_slice = tokens.astype(f32)
    attn_gain = lax.dynamic_slice_in_dim(gain_attn, my_columns, slice_width)
    gain_attn_part = jnp.sum(normed_grad * token_slice * token_scale, axis=0)
    inner = attn_gain * normed_grad
    token_grad = (
        middle_grad
        + token_scale * inner
        - token_slice * token_scale**3 * row_mean(token_slice * inner, 17)
    ).astype(low)

    there = swap_back([block_out[micro_rows:], token_grad[micro_rows:]], nz, 19)
    block_out = jnp.concatenate([block_out[:micro_rows], there[0]], axis=0)
    token_grad = jnp.concatenate([token_grad[:micro_rows], there[1]], axis=0)

    pieces = [router_part.reshape(-1), gain_attn_part, gain_moe_part, gain_query_part, gain_key_part]
    length = sum(piece.shape[0] for piece in pieces)
    part_rows = -(-length // (shard_count * 1024)) * 8
    flat = jnp.concatenate(
        pieces + [jnp.zeros((shard_count * part_rows * 128 - length,), f32)]
    ).reshape(shard_count, part_rows, 128)
    summed = sum_small(flat, shard_count, group_count, 18).reshape(
        shard_count, group_count, part_rows * 128
    ).transpose(1, 0, 2).reshape(group_count, shard_count * part_rows * 128)
    at = 0
    sums = []
    for piece in pieces:
        sums.append(summed[:, at : at + piece.shape[0]])
        at += piece.shape[0]
    return (
        block_out,
        token_grad,
        sums[1].reshape(-1),
        weight_grad[:, :query_width],
        weight_grad[:, query_width : query_width + kv_width],
        weight_grad[:, query_width + kv_width :],
        w_out_grad,
        jnp.sum(sums[3], axis=0),
        jnp.sum(sums[4], axis=0),
        sums[2].reshape(-1),
        sums[0].reshape(router.shape),
        gate_acc[None],
        up_acc[None],
        down_acc[None],
    )


def solution(mesh):
    small = mesh.shape["fsdp"] * mesh.shape["tp"] <= 32 and mesh.shape["tp"] == 4
    return jax.shard_map(
        gathered_body if small else body,
        mesh=mesh,
        in_specs=(
            P("fsdp", "tp"),
            P("fsdp", "tp"),
            P("fsdp", None),
            P(None, "fsdp"),
            P(),
            P("fsdp", "tp"),
            P("fsdp", "tp"),
            P("fsdp", "tp"),
            P("fsdp", "tp"),
            P(),
            P(),
            P(),
            P(),
            P(("fsdp", "tp"), None, None),
            P(("fsdp", "tp"), None, None),
            P(("fsdp", "tp"), None, None),
        ),
        out_specs=(
            P("fsdp", "tp"),
            P("fsdp", "tp"),
            P(),
            P("fsdp", "tp"),
            P("fsdp", "tp"),
            P("fsdp", "tp"),
            P("fsdp", "tp"),
            P(),
            P(),
            P(),
            P(),
            P(("fsdp", "tp"), None, None),
            P(("fsdp", "tp"), None, None),
            P(("fsdp", "tp"), None, None),
        ),
        check_vma=False,
    )
```

```python
import functools
import math

import jax
import jax.numpy as jnp
from jax import lax
from jax.experimental import pallas as pl
from jax.experimental.pallas import tpu as pltpu
from jax.sharding import PartitionSpec as P

TOPK = 8
DOCS = 4


theta_base = 1000000.0
norm_eps = 1e-06
masked_score = -1e30
highest_precision = lax.Precision.HIGHEST


def root_mean_norm(row_block, gain_row):
    return (
        row_block
        * lax.rsqrt(jnp.mean(row_block * row_block, axis=-1, keepdims=True) + norm_eps)
        * gain_row
    )


def rotary_apply(row_block, cosine_lookup, sine_lookup):
    half_width = row_block.shape[-1] // 2
    turned = jnp.concatenate([-row_block[..., half_width:], row_block[..., :half_width]], axis=-1)
    return row_block * cosine_lookup + turned * sine_lookup


def rope_tables(positions, head_width):
    half_width = head_width // 2
    frequency = theta_base ** (
        -2.0 * jnp.arange(half_width, dtype=jnp.int32).astype(jnp.float32) / head_width
    )
    angles = positions.astype(jnp.float32)[:, None] * frequency[None, :]
    cosine_lookup = jnp.cos(angles)
    sine_lookup = jnp.sin(angles)
    return (
        jnp.concatenate([cosine_lookup, cosine_lookup], axis=-1),
        jnp.concatenate([sine_lookup, sine_lookup], axis=-1),
    )


def swiglu(gate_pre, up_pre):
    return jax.nn.silu(gate_pre) * up_pre


def dot_first(left_side, right_side):
    return lax.dot_general(
        left_side, right_side, (((0,), (0,)), ((), ())), preferred_element_type=jnp.float32
    )


def dot_last(left_side, right_side):
    return lax.dot_general(
        left_side, right_side, (((1,), (1,)), ((), ())), preferred_element_type=jnp.float32
    )


def gather_weights(w_query, key_weight, value_weight, w_out):
    return (
        lax.all_gather(w_query, "fsdp", axis=0, tiled=True),
        lax.all_gather(key_weight, "fsdp", axis=0, tiled=True),
        lax.all_gather(value_weight, "fsdp", axis=0, tiled=True),
        lax.all_gather(w_out, "fsdp", axis=0, tiled=True),
    )


def gather_keys(keys_low, values_low):
    return (
        lax.all_gather(keys_low, "fsdp", axis=0, tiled=True),
        lax.all_gather(values_low, "fsdp", axis=0, tiled=True),
    )


def send_rows(buffer):
    return lax.all_to_all(buffer, "fsdp", split_axis=0, concat_axis=0, tiled=True)


def return_rows(buffer):
    return lax.all_to_all(buffer, "fsdp", split_axis=0, concat_axis=0, tiled=True)


def to_heads(per_token, kv_local, group_width):
    token_count, head_total, head_width = per_token.shape
    grouped_heads = per_token.reshape(token_count, kv_local, group_width, head_width)
    return grouped_heads.transpose(1, 2, 0, 3).reshape(
        kv_local, group_width * token_count, head_width
    )


def to_tokens(per_head, group_width):
    kv_local, row_count, head_width = per_head.shape
    token_count = row_count // group_width
    grouped_heads = per_head.reshape(kv_local, group_width, token_count, head_width)
    return grouped_heads.transpose(2, 0, 1, 3).reshape(
        token_count, kv_local * group_width * head_width
    )


def key_block(keys_all, key_start, block_keys, kv_local, head_width):
    return lax.dynamic_slice_in_dim(keys_all, key_start, block_keys, 0).reshape(
        block_keys, kv_local, head_width
    )


def block_scores(queries, keys_part, key_start, query_index, query_start):
    head_width = queries.shape[-1]
    scores = jnp.einsum(
        "hrd,khd->hrk", queries, keys_part, preferred_element_type=jnp.float32
    ) * head_width ** (-0.5)
    key_index = key_start + jnp.arange(keys_part.shape[0])
    allowed = (key_index[None, :] >= query_start[:, None]) & (
        key_index[None, :] <= query_index[:, None]
    )
    return (jnp.where(allowed[None], scores, masked_score), allowed)


def attend_forward(queries, keys_all, values_all, query_index, query_start, block_keys):
    kv_local, row_count, head_width = queries.shape
    lowest_block = jnp.min(query_start) // block_keys
    highest_block = jnp.max(query_index) // block_keys + 1

    def visit_block(block_index, running):
        run_peak, run_total, run_acc = running
        key_start = block_index * block_keys
        keys_part = key_block(keys_all, key_start, block_keys, kv_local, head_width)
        values_part = key_block(values_all, key_start, block_keys, kv_local, head_width)
        scores, allowed = block_scores(queries, keys_part, key_start, query_index, query_start)
        new_peak = jnp.maximum(run_peak, jnp.max(scores, axis=-1))
        weights = jnp.where(allowed[None], jnp.exp(scores - new_peak[..., None]), 0.0)
        factor = jnp.exp(run_peak - new_peak)
        run_total = run_total * factor + jnp.sum(weights, axis=-1)
        run_acc = run_acc * factor[..., None] + jnp.einsum(
            "hrk,khd->hrd",
            weights.astype(jnp.bfloat16),
            values_part,
            preferred_element_type=jnp.float32,
        )
        return (new_peak, run_total, run_acc)

    start_state = (
        jnp.full((kv_local, row_count), masked_score, jnp.float32),
        jnp.zeros((kv_local, row_count), jnp.float32),
        jnp.zeros((kv_local, row_count, head_width), jnp.float32),
    )
    run_peak, run_total, run_acc = lax.fori_loop(
        lowest_block, highest_block, visit_block, start_state
    )
    return (run_acc / run_total[..., None], run_peak + jnp.log(run_total))


def attend_backward(
    queries,
    keys_all,
    values_all,
    query_index,
    query_start,
    block_keys,
    outputs,
    log_total,
    grad_low,
):
    kv_local, row_count, head_width = queries.shape
    key_count = keys_all.shape[0]
    score_scale = head_width ** (-0.5)
    row_delta = jnp.sum(grad_low.astype(jnp.float32) * outputs, axis=-1)
    lowest_block = jnp.min(query_start) // block_keys
    highest_block = jnp.max(query_index) // block_keys + 1

    def visit_block(block_index, running):
        query_acc, key_acc, value_acc = running
        key_start = block_index * block_keys
        keys_part = key_block(keys_all, key_start, block_keys, kv_local, head_width)
        values_part = key_block(values_all, key_start, block_keys, kv_local, head_width)
        scores, allowed = block_scores(queries, keys_part, key_start, query_index, query_start)
        prob_block = jnp.where(allowed[None], jnp.exp(scores - log_total[..., None]), 0.0)
        prob_grad = jnp.einsum(
            "hrd,khd->hrk", grad_low, values_part, preferred_element_type=jnp.float32
        )
        score_grad = (prob_block * (prob_grad - row_delta[..., None])).astype(jnp.bfloat16)
        query_acc = (
            query_acc
            + jnp.einsum("hrk,khd->hrd", score_grad, keys_part, preferred_element_type=jnp.float32)
            * score_scale
        )
        key_part = (
            jnp.einsum("hrk,hrd->khd", score_grad, queries, preferred_element_type=jnp.float32)
            * score_scale
        )
        value_part = jnp.einsum(
            "hrk,hrd->khd",
            prob_block.astype(jnp.bfloat16),
            grad_low,
            preferred_element_type=jnp.float32,
        )
        key_acc = lax.dynamic_update_slice_in_dim(
            key_acc, key_part.reshape(block_keys, kv_local * head_width), key_start, 0
        )
        value_acc = lax.dynamic_update_slice_in_dim(
            value_acc, value_part.reshape(block_keys, kv_local * head_width), key_start, 0
        )
        return (query_acc, key_acc, value_acc)

    start_state = (
        jnp.zeros((kv_local, row_count, head_width), jnp.float32),
        jnp.zeros((key_count, kv_local * head_width), jnp.float32),
        jnp.zeros((key_count, kv_local * head_width), jnp.float32),
    )
    return lax.fori_loop(lowest_block, highest_block, visit_block, start_state)


def body(
    tokens,
    cotangent,
    routes,
    doc_ids,
    gain_attn,
    w_query,
    key_weight,
    value_weight,
    w_out,
    gain_query,
    key_norm_gain,
    gain_moe,
    router,
    w_gate,
    w_up,
    w_down,
):
    shard_count = lax.axis_size("fsdp")
    group_count = lax.axis_size("tp")
    shard_index = lax.axis_index("fsdp")
    group_index = lax.axis_index("tp")
    full_tokens, full_grads = (
        lax.all_gather(tokens, "tp", axis=1, tiled=True),
        lax.all_gather(cotangent, "tp", axis=1, tiled=True),
    )
    slice_width = tokens.shape[1]
    model_width = full_tokens.shape[1]
    micro_count, micro_rows = doc_ids.shape
    head_width = gain_query.shape[0]
    query_local = w_query.shape[1] // head_width
    kv_local = key_weight.shape[1] // head_width
    group_width = query_local // kv_local
    expert_total = router.shape[1]
    capacity = max(2, 2 * micro_rows * TOPK // expert_total)
    slot_total = shard_count * capacity
    pair_total = micro_rows * TOPK
    block_keys = micro_rows * math.gcd(shard_count, max(1, 512 // micro_rows))
    doc_range = jnp.arange(DOCS)
    expert_range = jnp.arange(expert_total)
    local_counts = jnp.sum((doc_ids[:, :, None] == doc_range).astype(jnp.float32), axis=1)
    doc_totals = lax.psum(local_counts, "fsdp")
    doc_begin = (jnp.cumsum(doc_totals, axis=1) - doc_totals).astype(jnp.int32)
    gate_expert = w_gate[0]
    up_expert = w_up[0]
    down_expert = w_down[0]
    router_wide = router.astype(jnp.float32)
    query_acc = jnp.zeros((model_width, query_local * head_width), jnp.float32)
    key_acc = jnp.zeros((model_width, kv_local * head_width), jnp.float32)
    value_acc = jnp.zeros((model_width, kv_local * head_width), jnp.float32)
    out_acc = jnp.zeros((model_width, query_local * head_width), jnp.float32)
    gate_acc = jnp.zeros(gate_expert.shape, jnp.float32)
    up_acc = jnp.zeros(up_expert.shape, jnp.float32)
    down_acc = jnp.zeros(down_expert.shape, jnp.float32)
    router_acc = jnp.zeros(router.shape, jnp.float32)
    gain_attn_acc = jnp.zeros(gain_attn.shape, jnp.float32)
    gain_moe_acc = jnp.zeros(gain_moe.shape, jnp.float32)
    gain_query_acc = jnp.zeros(gain_query.shape, jnp.float32)
    gain_key_acc = jnp.zeros(key_norm_gain.shape, jnp.float32)
    out_parts = []
    grad_parts = []
    for micro_index in range(micro_count):
        row_begin = micro_index * micro_rows
        token_block = full_tokens[row_begin : row_begin + micro_rows].astype(jnp.float32)
        ids_now = doc_ids[micro_index]
        query_index = shard_index * micro_rows + jnp.arange(micro_rows)
        query_start = jnp.sum(
            jnp.where(ids_now[:, None] == doc_range, doc_begin[micro_index][None, :], 0), axis=1
        )
        cosine_lookup, sine_lookup = rope_tables(query_index - query_start, head_width)
        gathered = gather_weights(w_query, key_weight, value_weight, w_out)
        normed, norm_pull = jax.vjp(root_mean_norm, token_block, gain_attn)
        normed_reduced = normed.astype(jnp.bfloat16)
        query_pre = jnp.dot(normed_reduced, gathered[0], preferred_element_type=jnp.float32)
        key_before_norm = jnp.dot(normed_reduced, gathered[1], preferred_element_type=jnp.float32)
        value_reduced = jnp.dot(
            normed_reduced, gathered[2], preferred_element_type=jnp.float32
        ).astype(jnp.bfloat16)

        def shape_heads(query_raw, key_raw, query_gain, key_gain):
            query_heads = rotary_apply(
                root_mean_norm(query_raw.reshape(micro_rows, query_local, head_width), query_gain),
                cosine_lookup[:, None, :],
                sine_lookup[:, None, :],
            )
            key_heads = rotary_apply(
                root_mean_norm(key_raw.reshape(micro_rows, kv_local, head_width), key_gain),
                cosine_lookup[:, None, :],
                sine_lookup[:, None, :],
            )
            return (query_heads, key_heads)

        (query_heads, key_heads), heads_pull = jax.vjp(
            shape_heads, query_pre, key_before_norm, gain_query, key_norm_gain
        )
        queries = to_heads(query_heads.astype(jnp.bfloat16), kv_local, group_width)
        keys_low = key_heads.reshape(micro_rows, kv_local * head_width).astype(jnp.bfloat16)
        keys_all, values_all = gather_keys(keys_low, value_reduced)
        row_index = jnp.tile(query_index, group_width)
        row_start = jnp.tile(query_start, group_width)
        head_out, log_total = attend_forward(
            queries, keys_all, values_all, row_index, row_start, block_keys
        )
        heads_low = to_tokens(head_out, group_width).astype(jnp.bfloat16)
        attn_part = dot_last(heads_low, gathered[3])
        middle = token_block + lax.psum(attn_part.astype(jnp.bfloat16), "tp").astype(jnp.float32)
        moe_normed, moe_pull = jax.vjp(root_mean_norm, middle, gain_moe)
        moe_low = moe_normed.astype(jnp.bfloat16)
        logits = jnp.dot(moe_low, router, preferred_element_type=jnp.float32)
        routes_now = routes[row_begin : row_begin + micro_rows]
        route_match = routes_now[:, :, None] == expert_range
        chosen = jnp.sum(jnp.where(route_match, logits[:, None, :], 0.0), axis=-1)
        gate_weights, softmax_pull = jax.vjp(jax.nn.softmax, chosen)
        mine = routes_now % group_count == group_index
        pair_target = jnp.where(mine, routes_now // group_count, shard_count).reshape(pair_total)
        target_hot = (pair_target[:, None] == jnp.arange(shard_count)).astype(jnp.int32)
        pair_rank = jnp.sum((jnp.cumsum(target_hot, axis=0) - target_hot) * target_hot, axis=1)
        pair_slot = jnp.where(
            pair_target < shard_count, pair_target * capacity + pair_rank, slot_total
        )
        slot_pair = (
            jnp.full((slot_total + 1,), pair_total, jnp.int32)
            .at[pair_slot]
            .set(jnp.arange(pair_total, dtype=jnp.int32))[:slot_total]
        )
        slot_token = slot_pair // TOPK
        slot_grid = pair_slot.reshape(micro_rows, TOPK)
        padded_low = jnp.concatenate([moe_low, jnp.zeros((1, model_width), jnp.bfloat16)], axis=0)
        received = send_rows(
            padded_low[slot_token].reshape(shard_count, capacity, model_width)
        ).reshape(slot_total, model_width)
        gate_pre = jnp.dot(received, gate_expert, preferred_element_type=jnp.float32)
        up_pre = jnp.dot(received, up_expert, preferred_element_type=jnp.float32)
        hidden, swiglu_pull = jax.vjp(swiglu, gate_pre, up_pre)
        hidden_low = hidden.astype(jnp.bfloat16)
        expert_out = jnp.dot(hidden_low, down_expert, preferred_element_type=jnp.float32).astype(
            jnp.bfloat16
        )
        returned = return_rows(expert_out.reshape(shard_count, capacity, model_width)).reshape(
            slot_total, model_width
        )
        padded_out = jnp.concatenate([returned, jnp.zeros((1, model_width), jnp.bfloat16)], axis=0)
        moe_part = jnp.zeros((micro_rows, model_width), jnp.float32)
        for pick_index in range(TOPK):
            moe_part = moe_part + gate_weights[:, pick_index : pick_index + 1] * padded_out[
                slot_grid[:, pick_index]
            ].astype(jnp.float32)
        moe_share = lax.psum_scatter(
            moe_part.astype(jnp.bfloat16), "tp", scatter_dimension=1, tiled=True
        ).astype(jnp.float32)
        middle_slice = lax.dynamic_slice_in_dim(middle, group_index * slice_width, slice_width, 1)
        out_parts.append((middle_slice + moe_share).astype(jnp.bfloat16))
        grad_block = full_grads[row_begin : row_begin + micro_rows].astype(jnp.float32)
        gate_columns = []
        for pick_index in range(TOPK):
            gate_columns.append(
                jnp.sum(
                    grad_block * padded_out[slot_grid[:, pick_index]].astype(jnp.float32), axis=1
                )
            )
        gates_grad = jnp.stack(gate_columns, axis=1)
        flat_gates = jnp.concatenate(
            [gate_weights.reshape(pair_total), jnp.zeros((1,), jnp.float32)]
        )
        padded_grad = jnp.concatenate(
            [grad_block, jnp.zeros((1, model_width), jnp.float32)], axis=0
        )
        send_grad = (padded_grad[slot_token] * flat_gates[slot_pair][:, None]).astype(jnp.bfloat16)
        received_grad = send_rows(send_grad.reshape(shard_count, capacity, model_width)).reshape(
            slot_total, model_width
        )
        hidden_grad = dot_last(received_grad, down_expert)
        down_acc = down_acc + dot_first(hidden_low, received_grad)
        gate_pre_grad, up_pre_grad = swiglu_pull(hidden_grad)
        gate_pre_low = gate_pre_grad.astype(jnp.bfloat16)
        up_pre_low = up_pre_grad.astype(jnp.bfloat16)
        gate_acc = gate_acc + dot_first(received, gate_pre_low)
        up_acc = up_acc + dot_first(received, up_pre_low)
        rows_back = (dot_last(gate_pre_low, gate_expert) + dot_last(up_pre_low, up_expert)).astype(
            jnp.bfloat16
        )
        back_rows = return_rows(rows_back.reshape(shard_count, capacity, model_width)).reshape(
            slot_total, model_width
        )
        padded_back = jnp.concatenate(
            [back_rows, jnp.zeros((1, model_width), jnp.bfloat16)], axis=0
        )
        moe_grad = jnp.zeros((micro_rows, model_width), jnp.float32)
        for pick_index in range(TOPK):
            moe_grad = moe_grad + padded_back[slot_grid[:, pick_index]].astype(jnp.float32)
        (chosen_grad,) = softmax_pull(gates_grad)
        logit_grad = jnp.sum(jnp.where(route_match, chosen_grad[:, :, None], 0.0), axis=1)
        router_acc = router_acc + lax.dot_general(
            moe_low.astype(jnp.float32),
            logit_grad,
            (((0,), (0,)), ((), ())),
            precision=highest_precision,
        )
        moe_grad = moe_grad + lax.dot_general(
            logit_grad, router_wide, (((1,), (1,)), ((), ())), precision=highest_precision
        )
        middle_part, gain_moe_part = moe_pull(moe_grad)
        gain_moe_acc = gain_moe_acc + gain_moe_part
        middle_grad = grad_block + lax.psum(middle_part.astype(jnp.bfloat16), "tp").astype(
            jnp.float32
        )
        middle_low = middle_grad.astype(jnp.bfloat16)
        gathered_back = gather_weights(w_query, key_weight, value_weight, w_out)
        out_acc = out_acc + dot_first(middle_low, heads_low)
        heads_grad = jnp.dot(middle_low, gathered_back[3], preferred_element_type=jnp.float32)
        grad_low = to_heads(
            heads_grad.reshape(micro_rows, query_local, head_width).astype(jnp.bfloat16),
            kv_local,
            group_width,
        )
        query_side, key_side_all, value_side_all = attend_backward(
            queries,
            keys_all,
            values_all,
            row_index,
            row_start,
            block_keys,
            head_out,
            log_total,
            grad_low,
        )
        key_side, value_side = (
            lax.psum_scatter(
                key_side_all.astype(jnp.bfloat16), "fsdp", scatter_dimension=0, tiled=True
            ).astype(jnp.float32),
            lax.psum_scatter(
                value_side_all.astype(jnp.bfloat16), "fsdp", scatter_dimension=0, tiled=True
            ).astype(jnp.float32),
        )
        query_pre_grad, key_pre_grad, gain_query_part, gain_key_part = heads_pull(
            (
                to_tokens(query_side, group_width).reshape(micro_rows, query_local, head_width),
                key_side.reshape(micro_rows, kv_local, head_width),
            )
        )
        gain_query_acc = gain_query_acc + gain_query_part
        gain_key_acc = gain_key_acc + gain_key_part
        query_pre_low = query_pre_grad.astype(jnp.bfloat16)
        key_pre_low = key_pre_grad.astype(jnp.bfloat16)
        value_pre_low = value_side.astype(jnp.bfloat16)
        query_acc = query_acc + dot_first(normed_reduced, query_pre_low)
        key_acc = key_acc + dot_first(normed_reduced, key_pre_low)
        value_acc = value_acc + dot_first(normed_reduced, value_pre_low)
        normed_grad = (
            dot_last(query_pre_low, gathered_back[0])
            + dot_last(key_pre_low, gathered_back[1])
            + dot_last(value_pre_low, gathered_back[2])
        )
        token_part, gain_attn_part = norm_pull(normed_grad)
        gain_attn_acc = gain_attn_acc + gain_attn_part
        token_share = lax.psum_scatter(
            token_part.astype(jnp.bfloat16), "tp", scatter_dimension=1, tiled=True
        ).astype(jnp.float32)
        grad_slice = lax.dynamic_slice_in_dim(
            middle_grad, group_index * slice_width, slice_width, 1
        )
        grad_parts.append((grad_slice + token_share).astype(jnp.bfloat16))
    weight_sums = (
        lax.psum_scatter(
            query_acc.astype(jnp.bfloat16), "fsdp", scatter_dimension=0, tiled=True
        ).astype(jnp.float32),
        lax.psum_scatter(
            key_acc.astype(jnp.bfloat16), "fsdp", scatter_dimension=0, tiled=True
        ).astype(jnp.float32),
        lax.psum_scatter(
            value_acc.astype(jnp.bfloat16), "fsdp", scatter_dimension=0, tiled=True
        ).astype(jnp.float32),
        lax.psum_scatter(
            out_acc.astype(jnp.bfloat16), "fsdp", scatter_dimension=0, tiled=True
        ).astype(jnp.float32),
    )
    small_sums = lax.psum(
        (gain_attn_acc, gain_query_acc, gain_key_acc, gain_moe_acc, router_acc), ("fsdp", "tp")
    )
    return (
        jnp.concatenate(out_parts, axis=0),
        jnp.concatenate(grad_parts, axis=0),
        small_sums[0],
        weight_sums[0],
        weight_sums[1],
        weight_sums[2],
        weight_sums[3],
        small_sums[1],
        small_sums[2],
        small_sums[3],
        small_sums[4],
        gate_acc[None],
        up_acc[None],
        down_acc[None],
    )


MESH = pl.DeviceIdType.MESH


def place():
    f = lax.axis_index("fsdp")
    t = lax.axis_index("tp")
    return f // 2, f % 2, t // 2, t % 2


def device(z, x, y, c):
    return (z * 2 + x, y * 2 + c)


def greet(devices):
    barrier = pltpu.get_barrier_semaphore()
    total = 0
    for valid, where in devices:
        if valid is None:
            pl.semaphore_signal(barrier, inc=1, device_id=where, device_id_type=MESH)
            total = total + 1
        else:
            @pl.when(valid)
            def _():
                pl.semaphore_signal(barrier, inc=1, device_id=where, device_id_type=MESH)
            total = total + valid.astype(jnp.int32)
    pl.semaphore_wait(barrier, total)


def remote(src, dst, send, recv, where):
    return pltpu.make_async_remote_copy(
        src_ref=src, dst_ref=dst, send_sem=send, recv_sem=recv, device_id=where, device_id_type=MESH
    )


def gather_all_kernel(nz, x_ref, o_ref, lsem, s_p, s_u, s_d, s_x, s_y, s_dx, s_dy,
                      r_z, r_x, r_y, r_dx, r_dy, r_p):
    z, x, y, c = place()
    rows, cols = x_ref.shape
    half = rows // 2
    partner = device(z, x, y, 1 - c)
    xn = device(z, 1 - x, y, c)
    yn = device(z, x, 1 - y, c)
    up = device(z + 1, x, y, c)
    down = device(z - 1, x, y, c)
    greet([(None, partner), (None, xn), (None, yn), (z < nz - 1, up), (z > 0, down)])

    def block(zz, xx, yy, cc, part=None):
        start = (zz * 2 + xx) * rows
        size = rows
        if part is not None:
            start = start + part * half
            size = half
        return o_ref.at[pl.ds(pl.multiple_of(start, half), size),
                        pl.ds(pl.multiple_of((yy * 2 + cc) * cols, cols), cols)]

    own = pltpu.make_async_copy(x_ref, block(z, x, y, c), lsem)
    own.start()

    items = [(0, 0)]
    for dist in range(1, nz):
        items += [(dist, -1), (dist, 1)]

    def guard(item, fn):
        dist, side = item
        zz = z + side * dist
        if dist == 0:
            fn(zz)
        else:
            pl.when((zz >= 0) & (zz < nz))(lambda: fn(zz))

    def c_z(zz, src):
        dst = block(zz, x, y, c)
        return (remote(src, dst, s_u.at[zz], r_z.at[zz], up),
                remote(src, dst, s_d.at[zz], r_z.at[zz], down))

    def c_xy(zz, src):
        dst = block(zz, x, y, c)
        return (remote(src, dst, s_x.at[zz], r_x.at[zz], xn),
                remote(src, dst, s_y.at[zz], r_y.at[zz], yn))

    def c_p(zz, rel, src=None):
        xx = 1 - x if rel in (1, 3, 4) else x
        yy = 1 - y if rel in (2, 3, 4) else y
        part = {3: 0, 4: 1}.get(rel)
        dst = block(zz, xx, yy, c, part)
        k = zz * 5 + rel
        return remote(dst if src is None else src, dst, s_p.at[k], r_p.at[k], partner)

    def w_p(zz, rel):
        xx = 1 - x if rel in (1, 3, 4) else x
        yy = 1 - y if rel in (2, 3, 4) else y
        part = {3: 0, 4: 1}.get(rel)
        dst = block(zz, xx, yy, 1 - c, part)
        k = zz * 5 + rel
        return remote(dst, dst, s_p.at[k], r_p.at[k], partner)

    def c_diag(zz):
        a = block(zz, 1 - x, y, c, 0)
        b = block(zz, x, 1 - y, c, 1)
        return (remote(a, a, s_dy.at[zz], r_dy.at[zz], yn),
                remote(b, b, s_dx.at[zz], r_dx.at[zz], xn))

    def stage_a(item):
        dist, side = item

        def run(zz):
            src = x_ref if dist == 0 else block(zz, x, y, c)
            cu, cd = c_z(zz, src)
            if dist:
                cu.wait_recv()
            if side <= 0:
                pl.when(z < nz - 1)(cu.start)
            if dist == 0 or side > 0:
                pl.when(z > 0)(cd.start)
            for cc in c_xy(zz, src):
                cc.start()
            c_p(zz, 0, src).start()

        guard(item, run)

    def stage_b(item):
        def run(zz):
            cx, cy = c_xy(zz, block(zz, x, y, c))
            dy, dx = c_diag(zz)
            cx.wait_recv()
            dy.start()
            c_p(zz, 1).start()
            cy.wait_recv()
            dx.start()
            c_p(zz, 2).start()

        guard(item, run)

    def stage_c(item):
        def run(zz):
            dy, dx = c_diag(zz)
            dy.wait_recv()
            c_p(zz, 3).start()
            dx.wait_recv()
            c_p(zz, 4).start()

        guard(item, run)

    count = len(items)
    for k in range(count + 2):
        if k < count:
            stage_a(items[k])
        if 0 <= k - 1 < count:
            stage_b(items[k - 1])
        if 0 <= k - 2 < count:
            stage_c(items[k - 2])

    def finish(zz, carry):
        for rel in range(5):
            w_p(zz, rel).wait_recv()
            c_p(zz, rel).wait_send()
        cu, cd = c_z(zz, block(zz, x, y, c))
        pl.when((zz <= z) & (z < nz - 1))(cu.wait_send)
        pl.when((zz >= z) & (z > 0))(cd.wait_send)
        for cc in c_xy(zz, block(zz, x, y, c)) + c_diag(zz):
            cc.wait_send()
        return carry

    lax.fori_loop(0, nz, finish, 0)
    own.wait()


def gather_all(block, nz, collective_id):
    rows, cols = block.shape
    dma = pltpu.SemaphoreType.DMA
    return pl.pallas_call(
        functools.partial(gather_all_kernel, nz),
        out_shape=jax.ShapeDtypeStruct((rows * nz * 2, cols * 4), block.dtype),
        in_specs=[pl.BlockSpec(memory_space=pl.ANY)],
        out_specs=pl.BlockSpec(memory_space=pl.ANY),
        scratch_shapes=[dma] + [dma((5 * nz,))] + [dma((nz,))] * 6 + [dma((nz,))] * 5 + [dma((5 * nz,))],
        compiler_params=pltpu.CompilerParams(collective_id=collective_id, has_side_effects=True),
        name="gather_all",
    )(block)


def scatter_all_kernel(nz, p_ref, o_ref, w, lp, rx, rxd, ry, ryd, rz,
                       s_l, s_p, r_p, s_x, s_y, s_dx, s_dy, s_z, r_x, r_y, r_dx, r_dy, r_z):
    z, x, y, c = place()
    rows, cols = o_ref.shape
    half = rows // 2
    partner = device(z, x, y, 1 - c)
    xn = device(z, 1 - x, y, c)
    yn = device(z, x, 1 - y, c)
    up = device(z + 1, x, y, c)
    down = device(z - 1, x, y, c)
    greet([(None, partner), (None, xn), (None, yn), (z < nz - 1, up), (z > 0, down)])
    chunk = 64

    def block(zz, rel, cc):
        xx = 1 - x if rel in (1, 3) else x
        yy = 1 - y if rel in (2, 3) else y
        return p_ref.at[pl.ds(pl.multiple_of((zz * 2 + xx) * rows, rows), rows),
                        pl.ds(pl.multiple_of((yy * 2 + cc) * cols, cols), cols)]

    items = []
    for dist in range(nz - 1, 0, -1):
        items += [(dist, -1), (dist, 1)]
    items += [(0, 0)]

    def guard(item, fn):
        dist, side = item
        zz = z + side * dist
        if dist == 0:
            fn(zz)
        else:
            pl.when((zz >= 0) & (zz < nz))(lambda: fn(zz))

    def c_p(zz, rel):
        k = zz * 4 + rel
        return remote(block(zz, rel, 1 - c), lp.at[zz, rel], s_p.at[k], r_p.at[k], partner)

    def c_l(zz, rel):
        return pltpu.make_async_copy(block(zz, rel, c), w.at[zz, rel], s_l.at[zz * 4 + rel])

    def c_diag(zz):
        return (remote(w.at[zz, 3, pl.ds(0, half)], rxd.at[zz], s_dx.at[zz], r_dx.at[zz], xn),
                remote(w.at[zz, 3, pl.ds(half, half)], ryd.at[zz], s_dy.at[zz], r_dy.at[zz], yn))

    def c_xy(zz):
        return (remote(w.at[zz, 1], rx.at[zz], s_x.at[zz], r_x.at[zz], xn),
                remote(w.at[zz, 2], ry.at[zz], s_y.at[zz], r_y.at[zz], yn))

    def c_z(zz, slot, where):
        return remote(w.at[zz, 0], rz.at[slot], s_z.at[zz], r_z.at[slot], where)

    def add(dst, srcs, start, count):
        def step(i, carry):
            off = pl.multiple_of(i * chunk, chunk)
            here = pl.ds(pl.multiple_of(start + off, chunk), chunk)
            total = dst[here, :].astype(jnp.float32)
            for src in srcs:
                total = total + src[pl.ds(off, chunk), :].astype(jnp.float32)
            dst[here, :] = total.astype(dst.dtype)
            return carry
        lax.fori_loop(0, count // chunk, step, 0)

    def stage_0(item):
        def run(zz):
            for rel in (3, 1, 2, 0):
                c_p(zz, rel).start()
                c_l(zz, rel).start()
        guard(item, run)

    def stage_d(item):
        def run(zz):
            for rel in (3, 1, 2, 0):
                c_p(zz, rel).wait_recv()
                c_l(zz, rel).wait()
                add(w.at[zz, rel], [lp.at[zz, rel]], 0, rows)
                if rel == 3:
                    for cc in c_diag(zz):
                        cc.start()
        guard(item, run)

    def stage_e(item):
        def run(zz):
            dx, dy = c_diag(zz)
            cx, cy = c_xy(zz)
            dy.wait_recv()
            add(w.at[zz, 1], [ryd.at[zz]], half, half)
            cx.start()
            dx.wait_recv()
            add(w.at[zz, 2], [rxd.at[zz]], 0, half)
            cy.start()
        guard(item, run)

    def stage_f(item):
        dist, side = item

        def run(zz):
            cx, cy = c_xy(zz)
            cx.wait_recv()
            cy.wait_recv()
            if dist:
                add(w.at[zz, 0], [rx.at[zz], ry.at[zz]], 0, rows)
                has = z > 0 if side > 0 else z < nz - 1
                cz = c_z(zz, zz, up if side > 0 else down)

                @pl.when(has)
                def _():
                    cz.wait_recv()
                    add(w.at[zz, 0], [rz.at[zz]], 0, rows)
                if side > 0:
                    cz.start()
                else:
                    if dist == 1:
                        c_z(zz, nz, down).start()
                    else:
                        cz.start()
            else:
                below, above = c_z(zz, zz, up), c_z(zz, nz, down)

                def total(refs):
                    def step(i, carry):
                        here = pl.ds(pl.multiple_of(i * chunk, chunk), chunk)
                        acc = w[zz, 0, here, :].astype(jnp.float32)
                        for ref in refs:
                            acc = acc + ref[here, :].astype(jnp.float32)
                        o_ref[here, :] = acc
                        return carry
                    lax.fori_loop(0, rows // chunk, step, 0)

                pl.when(z > 0)(below.wait_recv)
                pl.when(z < nz - 1)(above.wait_recv)
                pl.when(z == 0)(lambda: total([rx.at[zz], ry.at[zz], rz.at[nz]]))
                pl.when(z == nz - 1)(lambda: total([rx.at[zz], ry.at[zz], rz.at[zz]]))
                pl.when((z > 0) & (z < nz - 1))(
                    lambda: total([rx.at[zz], ry.at[zz], rz.at[zz], rz.at[nz]]))
        guard(item, run)

    for item in items:
        stage_0(item)
    count = len(items)
    for k in range(count + 2):
        if k < count:
            stage_d(items[k])
        if 0 <= k - 1 < count:
            stage_e(items[k - 1])
        if 0 <= k - 2 < count:
            stage_f(items[k - 2])

    def finish(zz, carry):
        for rel in range(4):
            c_p(zz, rel).wait_send()
        for cc in c_diag(zz) + c_xy(zz):
            cc.wait_send()
        pl.when(zz != z)(c_z(zz, zz, up).wait_send)
        return carry

    lax.fori_loop(0, nz, finish, 0)


def scatter_all(partial, nz, collective_id):
    rows, cols = partial.shape[0] // (2 * nz), partial.shape[1] // 4
    half = rows // 2
    dma = pltpu.SemaphoreType.DMA
    kind = partial.dtype
    vm = pltpu.VMEM
    return pl.pallas_call(
        functools.partial(scatter_all_kernel, nz),
        out_shape=jax.ShapeDtypeStruct((rows, cols), jnp.float32),
        in_specs=[pl.BlockSpec(memory_space=pl.ANY)],
        out_specs=pl.BlockSpec(memory_space=pltpu.VMEM),
        scratch_shapes=[vm((nz, 4, rows, cols), kind), vm((nz, 4, rows, cols), kind),
                        vm((nz, rows, cols), kind), vm((nz, half, cols), kind),
                        vm((nz, rows, cols), kind), vm((nz, half, cols), kind),
                        vm((nz + 1, rows, cols), kind)]
        + [dma((4 * nz,))] * 3 + [dma((nz,))] * 5 + [dma((nz,))] * 4 + [dma((nz + 1,))],
        compiler_params=pltpu.CompilerParams(collective_id=collective_id, has_side_effects=True,
                                             vmem_limit_bytes=48 << 20),
        name="scatter_all",
    )(partial)


def z_items(nz, near_first):
    items = [(0, 0)] if near_first else []
    order = range(1, nz) if near_first else range(nz - 1, 0, -1)
    for dist in order:
        items += [(dist, -1), (dist, 1)]
    return items if near_first else items + [(0, 0)]


def z_guard(item, z, nz, fn):
    dist, side = item
    zz = z + side * dist
    if dist == 0:
        fn(zz)
    else:
        pl.when((zz >= 0) & (zz < nz))(lambda: fn(zz))


def gather_rows_kernel(nz, count, columns, *refs):
    total = count + columns
    srcs, refs = refs[:total], refs[total:]
    outs, refs = refs[:total], refs[total:]
    wide, refs = refs[: min(columns, 1)], refs[min(columns, 1) :]
    lsem, s_u, s_d, s_x, r_z, r_x, s_c, r_c, s_w, r_w = refs
    z, x, y, c = place()
    xn, up, down = device(z, 1 - x, y, c), device(z + 1, x, y, c), device(z - 1, x, y, c)
    partner, yn = device(z, x, y, 1 - c), device(z, x, 1 - y, c)
    wanted = [(None, xn), (z < nz - 1, up), (z > 0, down)]
    greet(wanted + [(None, partner), (None, yn), (None, device(nz - 1 - z, x, y, c))] * min(columns, 1))

    def block(n, zz, xx):
        rows = srcs[n].shape[0]
        return outs[n].at[pl.ds(pl.multiple_of((zz * 2 + xx) * rows, rows), rows)]

    own = [(srcs[n], block(n, z, x)) for n in range(count)]
    column_copies, swaps = [], []
    if columns:
        mirror = device(nz - 1 - z, x, y, c)
        first, out = outs[count], wide[0]
        rows, cols = first.shape
        top, bottom = pl.ds(0, rows // 2), pl.ds(rows // 2, rows // 2)
        for n in range(columns):
            src, dst = srcs[count + n], outs[count + n]
            swaps.append(remote(src.at[bottom], dst.at[bottom], s_w.at[n], r_w.at[n], mirror))
            own.append((src.at[top], dst.at[top]))

        def column(yy):
            return out.at[:, pl.ds(pl.multiple_of((yy * 2 + c) * cols, cols), cols)]

        column_copies = [
            remote(first, column(y), s_c.at[0], r_c.at[0], yn),
            remote(first, column(y), s_c.at[1], r_c.at[1], partner),
            remote(column(1 - y), column(1 - y), s_c.at[2], r_c.at[2], partner),
        ]
        last = pltpu.make_async_copy(first, column(y), lsem.at[total])
    own = [pltpu.make_async_copy(src, dst, lsem.at[n]) for n, (src, dst) in enumerate(own)]
    for copy in swaps + own:
        copy.start()

    def copies(n, zz, src):
        dst = block(n, zz, x)
        k = n * nz + zz
        return (remote(src, dst, s_u.at[k], r_z.at[k], up),
                remote(src, dst, s_d.at[k], r_z.at[k], down),
                remote(src, dst, s_x.at[k], r_x.at[k], xn))

    for item in z_items(nz, True):
        dist, side = item

        def run(zz):
            for n in range(count):
                src = srcs[n] if dist == 0 else block(n, zz, x)
                cu, cd, cx = copies(n, zz, src)
                if dist:
                    cu.wait_recv()
                if side <= 0:
                    pl.when(z < nz - 1)(cu.start)
                if side > 0 or dist == 0:
                    pl.when(z > 0)(cd.start)
                cx.start()

        z_guard(item, z, nz, run)
        if columns and dist == 0:
            own[count].wait()
            swaps[0].wait_recv()
            column_copies[0].start()
            column_copies[1].start()
            last.start()
        if columns and item == (1, 1):
            column_copies[0].wait_recv()
            column_copies[2].start()

    def finish(zz, carry):
        for n in range(count):
            cu, cd, cx = copies(n, zz, block(n, zz, x))
            cx.wait_recv()
            cx.wait_send()
            pl.when((zz <= z) & (z < nz - 1))(cu.wait_send)
            pl.when((zz >= z) & (z > 0))(cd.wait_send)
        return carry

    lax.fori_loop(0, nz, finish, 0)
    for n, copy in enumerate(own):
        if n != count:
            copy.wait()
    if columns:
        column_copies[0].wait_send()
        column_copies[1].wait()
        column_copies[2].wait()
        last.wait()
        swaps[0].wait_send()
        for copy in swaps[1:]:
            copy.wait()


def gather_rows(blocks, nz, collective_id, swapped=()):
    count, columns = len(blocks), len(swapped)
    dma = pltpu.SemaphoreType.DMA
    any_space = pl.BlockSpec(memory_space=pl.ANY)
    shapes = [
        jax.ShapeDtypeStruct((b.shape[0] * nz * 2,) + b.shape[1:], b.dtype) for b in blocks
    ] + [jax.ShapeDtypeStruct(b.shape, b.dtype) for b in swapped]
    if columns:
        rows, cols = swapped[0].shape
        shapes.append(jax.ShapeDtypeStruct((rows, cols * 4), swapped[0].dtype))
    total = count + columns
    return pl.pallas_call(
        functools.partial(gather_rows_kernel, nz, count, columns),
        out_shape=shapes,
        in_specs=[any_space] * total,
        out_specs=[any_space] * len(shapes),
        scratch_shapes=[dma((total + 1,))] + [dma((count * nz,))] * 5 + [dma((3,))] * 2
        + [dma((max(columns, 1),))] * 2,
        compiler_params=pltpu.CompilerParams(collective_id=collective_id, has_side_effects=True),
        name="gather_rows",
    )(*blocks, *swapped)


def swap_back_kernel(nz, *refs):
    count = (len(refs) - 2) // 2
    srcs, outs = refs[:count], refs[count : 2 * count]
    s, r = refs[2 * count :]
    z, x, y, c = place()
    mirror = device(nz - 1 - z, x, y, c)
    greet([(None, mirror)])
    copies = [remote(src, out, s.at[n], r.at[n], mirror)
              for n, (src, out) in enumerate(zip(srcs, outs))]
    for copy in copies:
        copy.start()
    for copy in copies:
        copy.wait()


def swap_back(blocks, nz, collective_id):
    count = len(blocks)
    dma = pltpu.SemaphoreType.DMA
    any_space = pl.BlockSpec(memory_space=pl.ANY)
    return pl.pallas_call(
        functools.partial(swap_back_kernel, nz),
        out_shape=[jax.ShapeDtypeStruct(b.shape, b.dtype) for b in blocks],
        in_specs=[any_space] * count,
        out_specs=[any_space] * count,
        scratch_shapes=[dma((count,))] * 2,
        compiler_params=pltpu.CompilerParams(collective_id=collective_id, has_side_effects=True),
        name="swap_back",
    )(*blocks)


def add_blocks(dst, srcs, start, count, out=None, chunk=64):
    target = dst if out is None else out

    def step(i, carry):
        off = pl.multiple_of(i * chunk, chunk)
        here = pl.ds(pl.multiple_of(start + off, chunk), chunk)
        total = dst[here, :].astype(jnp.float32)
        for src in srcs:
            total = total + src[pl.ds(off, chunk), :].astype(jnp.float32)
        target[here, :] = total.astype(target.dtype)
        return carry

    lax.fori_loop(0, count // chunk, step, 0)


def reduce_rows_kernel(nz, p_ref, o_ref, w, rx, rz, s_l, s_x, s_z, r_x, r_z):
    z, x, y, c = place()
    rows = o_ref.shape[0]
    xn, up, down = device(z, 1 - x, y, c), device(z + 1, x, y, c), device(z - 1, x, y, c)
    greet([(None, xn), (z < nz - 1, up), (z > 0, down)])

    def block(zz, xx):
        return p_ref.at[pl.ds(pl.multiple_of((zz * 2 + xx) * rows, rows), rows)]

    def c_x(zz):
        return remote(block(zz, 1 - x), rx.at[zz], s_x.at[zz], r_x.at[zz], xn)

    def c_l(zz):
        return pltpu.make_async_copy(block(zz, x), w.at[zz], s_l.at[zz])

    def c_z(zz, slot, where):
        return remote(w.at[zz], rz.at[slot], s_z.at[zz], r_z.at[slot], where)

    items = z_items(nz, False)

    def start(zz):
        c_x(zz).start()
        c_l(zz).start()

    for item in items:
        z_guard(item, z, nz, start)
    for item in items:
        dist, side = item

        def run(zz):
            c_l(zz).wait()
            c_x(zz).wait_recv()
            if dist:
                add_blocks(w.at[zz], [rx.at[zz]], 0, rows)
                cz = c_z(zz, zz, up if side > 0 else down)

                @pl.when(z > 0 if side > 0 else z < nz - 1)
                def _():
                    cz.wait_recv()
                    add_blocks(w.at[zz], [rz.at[zz]], 0, rows)

                (c_z(zz, nz, down) if side < 0 and dist == 1 else cz).start()
            else:
                pl.when(z > 0)(c_z(zz, zz, up).wait_recv)
                pl.when(z < nz - 1)(c_z(zz, nz, down).wait_recv)
                low, high = rz.at[zz], rz.at[nz]
                pl.when(z == 0)(lambda: add_blocks(w.at[zz], [rx.at[zz], high], 0, rows, o_ref))
                pl.when(z == nz - 1)(lambda: add_blocks(w.at[zz], [rx.at[zz], low], 0, rows, o_ref))
                pl.when((z > 0) & (z < nz - 1))(
                    lambda: add_blocks(w.at[zz], [rx.at[zz], low, high], 0, rows, o_ref)
                )

        z_guard(item, z, nz, run)

    def finish(zz, carry):
        c_x(zz).wait_send()
        pl.when(zz != z)(c_z(zz, zz, up).wait_send)
        return carry

    lax.fori_loop(0, nz, finish, 0)


def reduce_rows(partial, nz, collective_id):
    rows, cols = partial.shape[0] // (2 * nz), partial.shape[1]
    dma, vm, kind = pltpu.SemaphoreType.DMA, pltpu.VMEM, partial.dtype
    return pl.pallas_call(
        functools.partial(reduce_rows_kernel, nz),
        out_shape=jax.ShapeDtypeStruct((rows, cols), jnp.float32),
        in_specs=[pl.BlockSpec(memory_space=pl.ANY)],
        out_specs=pl.BlockSpec(memory_space=pltpu.VMEM),
        scratch_shapes=[vm((nz, rows, cols), kind), vm((nz, rows, cols), kind),
                        vm((nz + 1, rows, cols), kind)]
        + [dma((nz,))] * 4 + [dma((nz + 1,))],
        compiler_params=pltpu.CompilerParams(
            collective_id=collective_id, has_side_effects=True, vmem_limit_bytes=48 << 20
        ),
        name="reduce_rows",
    )(partial)


def gather_cols_kernel(x_ref, o_ref, lsem, s_p, s_y, r_p, r_y):
    z, x, y, c = place()
    cols = x_ref.shape[1]
    partner, yn = device(z, x, y, 1 - c), device(z, x, 1 - y, c)
    greet([(None, partner), (None, yn)])

    def block(yy, cc):
        return o_ref.at[:, pl.ds(pl.multiple_of((yy * 2 + cc) * cols, cols), cols)]

    own = pltpu.make_async_copy(x_ref, block(y, c), lsem)
    cy = remote(x_ref, block(y, c), s_y, r_y, yn)
    cp = remote(x_ref, block(y, c), s_p.at[0], r_p.at[0], partner)
    cf = remote(block(1 - y, c), block(1 - y, c), s_p.at[1], r_p.at[1], partner)
    cy.start()
    cp.start()
    own.start()
    cy.wait_recv()
    cf.start()
    cp.wait()
    cf.wait()
    cy.wait_send()
    own.wait()


def gather_cols(block, collective_id):
    dma = pltpu.SemaphoreType.DMA
    any_space = pl.BlockSpec(memory_space=pl.ANY)
    return pl.pallas_call(
        gather_cols_kernel,
        out_shape=jax.ShapeDtypeStruct((block.shape[0], block.shape[1] * 4), block.dtype),
        in_specs=[any_space],
        out_specs=any_space,
        scratch_shapes=[dma, dma((2,)), dma, dma((2,)), dma],
        compiler_params=pltpu.CompilerParams(collective_id=collective_id, has_side_effects=True),
        name="gather_cols",
    )(block)


def reduce_cols_kernel(p_ref, o_ref, w, rp, ry, s_l, s_p, s_y, r_p, r_y):
    z, x, y, c = place()
    rows, cols = o_ref.shape
    partner, yn = device(z, x, y, 1 - c), device(z, x, 1 - y, c)
    greet([(None, partner), (None, yn)])

    def block(yy, cc):
        return p_ref.at[:, pl.ds(pl.multiple_of((yy * 2 + cc) * cols, cols), cols)]

    sends = [remote(block(yy, 1 - c), rp.at[k], s_p.at[k], r_p.at[k], partner)
             for k, yy in enumerate((1 - y, y))]
    loads = [pltpu.make_async_copy(block(yy, c), w.at[k], s_l.at[k])
             for k, yy in enumerate((1 - y, y))]
    cy = remote(w.at[0], ry, s_y, r_y, yn)
    for k in range(2):
        sends[k].start()
        loads[k].start()
    loads[0].wait()
    sends[0].wait_recv()
    add_blocks(w.at[0], [rp.at[0]], 0, rows)
    cy.start()
    loads[1].wait()
    sends[1].wait_recv()
    cy.wait_recv()
    add_blocks(w.at[1], [rp.at[1], ry], 0, rows, o_ref)
    for k in range(2):
        sends[k].wait_send()
    cy.wait_send()


def reduce_cols(partial, collective_id):
    rows, cols = partial.shape[0], partial.shape[1] // 4
    dma, vm, kind = pltpu.SemaphoreType.DMA, pltpu.VMEM, partial.dtype
    return pl.pallas_call(
        reduce_cols_kernel,
        out_shape=jax.ShapeDtypeStruct((rows, cols), jnp.float32),
        in_specs=[pl.BlockSpec(memory_space=pl.ANY)],
        out_specs=pl.BlockSpec(memory_space=pltpu.VMEM),
        scratch_shapes=[vm((2, rows, cols), kind), vm((2, rows, cols), kind), vm((rows, cols), kind),
                        dma((2,)), dma((2,)), dma, dma((2,)), dma],
        compiler_params=pltpu.CompilerParams(
            collective_id=collective_id, has_side_effects=True, vmem_limit_bytes=24 << 20
        ),
        name="reduce_cols",
    )(partial)


def sum_cols_kernel(v_ref, o_ref, got, s, r):
    group = lax.axis_index("tp")
    shard = lax.axis_index("fsdp")
    peers = [(shard, (group + k) % 4) for k in range(1, 4)]
    greet([(None, peer) for peer in peers])
    copies = [remote(v_ref, got.at[k], s.at[k], r.at[k], peer) for k, peer in enumerate(peers)]
    for copy in copies:
        copy.start()
    for copy in copies:
        copy.wait()
    o_ref[...] = v_ref[...] + got[0] + got[1] + got[2]


def sum_cols(vector, collective_id):
    dma = pltpu.SemaphoreType.DMA
    shape = vector.shape
    return pl.pallas_call(
        sum_cols_kernel,
        out_shape=jax.ShapeDtypeStruct(shape, jnp.float32),
        in_specs=[pl.BlockSpec(memory_space=pltpu.VMEM)],
        out_specs=pl.BlockSpec(memory_space=pltpu.VMEM),
        scratch_shapes=[pltpu.VMEM((3,) + shape, jnp.float32), dma((3,)), dma((3,))],
        compiler_params=pltpu.CompilerParams(collective_id=collective_id, has_side_effects=True),
        name="sum_cols",
    )(vector)


def greet_all(shard, group, shards, groups):
    barrier = pltpu.get_barrier_semaphore()
    total = shards * groups

    def step(k, carry):
        other = (shard * groups + group + k) % total
        pl.semaphore_signal(
            barrier, inc=1, device_id=(other // groups, other % groups), device_id_type=MESH
        )
        return carry

    lax.fori_loop(1, total, step, 0)
    pl.semaphore_wait(barrier, total - 1)


def swap_rows_kernel(shards, groups, v_ref, o_ref, s, r):
    shard, group = lax.axis_index("fsdp"), lax.axis_index("tp")
    total = shards * groups
    me = shard * groups + group
    greet_all(shard, group, shards, groups)

    def copy(k):
        other = (me + k) % total
        return remote(v_ref.at[other // groups], o_ref.at[me], s.at[k], r.at[k],
                      (other // groups, other % groups))

    def start(k, carry):
        copy(k).start()
        return carry

    def wait(k, carry):
        copy(k).wait()
        return carry

    lax.fori_loop(1, total, start, 0)
    o_ref[me] = v_ref[shard]
    lax.fori_loop(1, total, wait, 0)


def swap_rows(values, shards, groups, collective_id):
    dma, total = pltpu.SemaphoreType.DMA, shards * groups
    return pl.pallas_call(
        functools.partial(swap_rows_kernel, shards, groups),
        out_shape=jax.ShapeDtypeStruct((total,) + values.shape[1:], values.dtype),
        in_specs=[pl.BlockSpec(memory_space=pltpu.VMEM)],
        out_specs=pl.BlockSpec(memory_space=pltpu.VMEM),
        scratch_shapes=[dma((total,)), dma((total,))],
        compiler_params=pltpu.CompilerParams(collective_id=collective_id, has_side_effects=True),
        name="swap_rows",
    )(values)


def sum_small_kernel(shards, groups, v_ref, o_ref, got, s1, r1, s2, r2):
    shard, group = lax.axis_index("fsdp"), lax.axis_index("tp")
    total = shards * groups
    me = shard * groups + group
    greet_all(shard, group, shards, groups)

    def first(k):
        other = (shard + k) % shards
        return remote(v_ref.at[other], got.at[k], s1.at[k], r1.at[k], (other, group))

    def second(k):
        other = (me + k) % total
        return remote(o_ref.at[me], o_ref.at[me], s2.at[k], r2.at[k],
                      (other // groups, other % groups))

    for k in range(1, shards):
        first(k).start()
    acc = v_ref[shard]
    for k in range(1, shards):
        first(k).wait()
        acc = acc + got[k]
    o_ref[me] = acc

    def start(k, carry):
        second(k).start()
        return carry

    def wait(k, carry):
        second(k).wait()
        return carry

    lax.fori_loop(1, total, start, 0)
    lax.fori_loop(1, total, wait, 0)


def sum_small(values, shards, groups, collective_id):
    dma, total = pltpu.SemaphoreType.DMA, shards * groups
    part = values.shape[1:]
    return pl.pallas_call(
        functools.partial(sum_small_kernel, shards, groups),
        out_shape=jax.ShapeDtypeStruct((total,) + part, values.dtype),
        in_specs=[pl.BlockSpec(memory_space=pltpu.VMEM)],
        out_specs=pl.BlockSpec(memory_space=pltpu.VMEM),
        scratch_shapes=[pltpu.VMEM((shards,) + part, values.dtype), dma((shards,)), dma((shards,)),
                        dma((total,)), dma((total,))],
        compiler_params=pltpu.CompilerParams(collective_id=collective_id, has_side_effects=True),
        name="sum_small",
    )(values)


def dot_plain(left, right):
    return jnp.dot(left, right, preferred_element_type=jnp.float32)


def far_first(nz, z, k):
    at = 0
    for here in range(nz):
        order = sorted(range(nz), key=lambda other: (-abs(other - here), other))
        for step, other in enumerate(order):
            at = at + jnp.where((z == here) & (k == step), other, 0)
    return at


def expert_kernel(nz, slots, block_rows, x_all, g_all, routes_all, router_ref, wg, wu, wd,
                  out_all, back_ref, gg_ref, gates_ref, xr_all, gs_all, hid_all, gp_all, up_all,
                  x_ref, g_ref, t_ref, o_ref, xr, gs, hid, gp, up, st,
                  w, lp, rx, rxd, ry, ryd, rz,
                  s_in, s_out, s_save, s_p, r_p, s_x, s_y, s_dx, s_dy, s_z, r_x, r_y, r_dx, r_dy, r_z):
    z, x, y, c = place()
    expert = lax.axis_index("fsdp") * 4 + lax.axis_index("tp")
    rows, cols = back_ref.shape
    width = x_ref.shape[1]
    half = rows // 2
    blocks = rows // block_rows
    experts = router_ref.shape[1]
    f32, low = jnp.float32, jnp.bfloat16
    partner = device(z, x, y, 1 - c)
    xn, yn = device(z, 1 - x, y, c), device(z, x, 1 - y, c)
    up_dev, down_dev = device(z + 1, x, y, c), device(z - 1, x, y, c)
    greet([(None, partner), (None, xn), (None, yn), (z < nz - 1, up_dev), (z > 0, down_dev)])
    tiles = 2 * nz

    def tile_of(j):
        return far_first(nz, z, j // 2) * 2 + jnp.where(j % 2 == 0, 1 - x, x)

    def tile_rows(j):
        return pl.ds(pl.multiple_of(tile_of(j) * rows, rows), rows)

    def load(j, kind):
        src, dst = ((x_all, x_ref), None, (routes_all, t_ref))[kind]
        return pltpu.make_async_copy(src.at[tile_rows(j)], dst, s_in.at[kind])

    def load_g(j):
        tile = tile_of(j)
        first = pl.ds(pl.multiple_of(tile * rows, half), half)
        second = pl.ds(pl.multiple_of(mirrored(nz, tile) * rows + half, half), half)
        return (pltpu.make_async_copy(g_all.at[first], g_ref.at[pl.ds(0, half)], s_in.at[1]),
                pltpu.make_async_copy(g_all.at[second], g_ref.at[pl.ds(half, half)], s_in.at[3]))

    def save_out(j):
        return pltpu.make_async_copy(o_ref, out_all.at[tile_rows(j)], s_out)

    def saves(j):
        pairs = ((xr, xr_all), (gs, gs_all), (hid, hid_all), (gp, gp_all), (up, up_all))
        return [pltpu.make_async_copy(src, dst.at[j], s_save.at[n])
                for n, (src, dst) in enumerate(pairs)]

    def c_p(zz, rel, slot):
        k = zz * 4 + rel
        return remote(st.at[slot, rel // 2], lp.at[zz, rel], s_p.at[k], r_p.at[k], partner)

    def c_diag(zz):
        return (remote(w.at[zz, 3, pl.ds(0, half)], rxd.at[zz], s_dx.at[zz], r_dx.at[zz], xn),
                remote(w.at[zz, 3, pl.ds(half, half)], ryd.at[zz], s_dy.at[zz], r_dy.at[zz], yn))

    def c_xy(zz):
        return (remote(w.at[zz, 1], rx.at[zz], s_x.at[zz], r_x.at[zz], xn),
                remote(w.at[zz, 2], ry.at[zz], s_y.at[zz], r_y.at[zz], yn))

    def c_z(zz, slot, where):
        return remote(w.at[zz, 0], rz.at[slot], s_z.at[zz], r_z.at[slot], where)

    def send_z(zz):
        pl.when(zz > z)(lambda: c_z(zz, zz, up_dev).start())
        pl.when(zz == z - 1)(lambda: c_z(zz, nz, down_dev).start())
        pl.when(zz < z - 1)(lambda: c_z(zz, zz, down_dev).start())

    def stage_d(zz, rel, slot):
        c_p(zz, rel, slot).wait_recv()
        add_blocks(w.at[zz, rel], [lp.at[zz, rel]], 0, rows)
        if rel == 3:
            for copy in c_diag(zz):
                copy.start()

    def stage_e(zz):
        dx, dy = c_diag(zz)
        cx, cy = c_xy(zz)
        dy.wait_recv()
        add_blocks(w.at[zz, 1], [ryd.at[zz]], half, half)
        cx.start()
        dx.wait_recv()
        add_blocks(w.at[zz, 2], [rxd.at[zz]], 0, half)
        cy.start()

    def passes(zz):
        return ((zz > z) & (z > 0)) | ((zz < z) & (z < nz - 1))

    def stage_f1(zz):
        cx, cy = c_xy(zz)
        cx.wait_recv()
        cy.wait_recv()
        add_blocks(w.at[zz, 0], [rx.at[zz], ry.at[zz]], 0, rows)
        pl.when((zz != z) & jnp.logical_not(passes(zz)))(lambda: send_z(zz))

    def stage_f2(zz):
        @pl.when((zz != z) & passes(zz))
        def _():
            c_z(zz, zz, up_dev).wait_recv()
            add_blocks(w.at[zz, 0], [rz.at[zz]], 0, rows)
            send_z(zz)

        @pl.when(zz == z)
        def _():
            low_part, high_part = rz.at[zz], rz.at[nz]
            pl.when(z > 0)(lambda: c_z(zz, zz, up_dev).wait_recv())
            pl.when(z < nz - 1)(lambda: c_z(zz, nz, down_dev).wait_recv())
            own = w.at[zz, 0]
            pl.when(z == 0)(lambda: add_blocks(own, [high_part], 0, rows, back_ref))
            pl.when(z == nz - 1)(lambda: add_blocks(own, [low_part], 0, rows, back_ref))
            pl.when((z > 0) & (z < nz - 1))(
                lambda: add_blocks(own, [low_part, high_part], 0, rows, back_ref)
            )

    def compute(j):
        zz = far_first(nz, z, j // 2)
        slot = j % 2
        load(j, 2).wait()
        load(j, 0).wait()
        lanes = lax.broadcasted_iota(jnp.int32, (rows, experts), 1)
        routes = t_ref[...]
        chosen = routes[:, 0:1] == lanes
        for n in range(1, TOPK):
            chosen = chosen | (routes[:, n : n + 1] == lanes)
        logits = jnp.where(chosen, dot_plain(x_ref[...], router_ref[...]), masked_score)
        peak = jnp.max(logits, axis=1, keepdims=True)
        weights = jnp.where(chosen, jnp.exp(logits - peak), 0.0)
        gates = weights / jnp.sum(weights, axis=1, keepdims=True)
        gates_ref[...] = gates
        mine = lanes == expert
        gate_col = jnp.sum(jnp.where(mine, gates, 0.0), axis=1, keepdims=True)
        match_col = jnp.sum(jnp.where(mine & chosen, 1.0, 0.0), axis=1, keepdims=True)
        sub = lax.broadcasted_iota(jnp.int32, (block_rows, block_rows), 0)
        lane = lax.broadcasted_iota(jnp.int32, (block_rows, block_rows), 1)
        eye = sub == lane
        before = (sub > lane).astype(f32).astype(low)
        chosen_low = chosen.astype(f32).astype(low)
        pick, put, slot_gate = [], [], []
        slot_lane = lax.broadcasted_iota(jnp.int32, (block_rows, slots), 1).astype(f32)
        slot_sub = lax.broadcasted_iota(jnp.int32, (slots, block_rows), 0).astype(f32)
        for b in range(blocks):
            part = slice(b * block_rows, (b + 1) * block_rows)
            ranks = dot_plain(before, chosen_low[part])
            rank = jnp.sum(jnp.where(mine[part], ranks, 0.0), axis=1, keepdims=True)
            rank = jnp.where(match_col[part] > 0.0, rank, -1.0)
            rank_row = jnp.sum(jnp.where(eye, rank, 0.0), axis=0, keepdims=True)
            gate_row = jnp.sum(jnp.where(eye, gate_col[part], 0.0), axis=0, keepdims=True)
            hot = rank_row == slot_sub
            pick.append(hot.astype(f32).astype(low))
            put.append((rank == slot_lane).astype(f32).astype(low))
            slot_gate.append(jnp.sum(jnp.where(hot, gate_row, 0.0), axis=1, keepdims=True))
        slot_gate = jnp.concatenate(slot_gate, axis=0)

        def gather(ref, at):
            return jnp.concatenate(
                [dot_plain(pick[b], ref[pl.ds(b * block_rows, block_rows), at])
                 for b in range(blocks)],
                axis=0,
            )

        def scatter(ref, at, values):
            for b in range(blocks):
                ref[pl.ds(b * block_rows, block_rows), at] = dot_plain(
                    put[b], values[b * slots : (b + 1) * slots]
                ).astype(low)

        def columns(i):
            return pl.ds(pl.multiple_of(i * cols, cols), cols)

        @pl.when(j > 0)
        def _():
            for copy in saves(j):
                copy.wait()

        def take(i, carry):
            xr[:, columns(i)] = gather(x_ref, columns(i)).astype(low)
            return carry

        lax.fori_loop(0, width // cols, take, 0)

        @pl.when(j < tiles - 1)
        def _():
            load(j + 1, 2).start()
            load(j + 1, 0).start()

        gate_pre = dot_plain(xr[...], wg[...])
        up_pre = dot_plain(xr[...], wu[...])
        sig = jax.nn.sigmoid(gate_pre)
        silu = gate_pre * sig
        hidden_low = (silu * up_pre).astype(low)
        hid[...] = hidden_low
        for copy in load_g(j):
            copy.wait()
        pl.when(j > 0)(lambda: save_out(j).wait())

        def middle_part(i, carry):
            total, hidden_grad = carry
            at = columns(i)
            grad = gather(g_ref, at)
            expert_out = dot_plain(hidden_low, wd[:, at]).astype(low).astype(f32)
            total = total + jnp.sum(grad * expert_out, axis=1, keepdims=True)
            pair_grad = (grad * slot_gate).astype(low)
            gs[:, at] = pair_grad
            scatter(o_ref, at, (expert_out * slot_gate).astype(low))
            return total, hidden_grad + dot_last(pair_grad, wd[:, at])

        gates_grad, hidden_grad = lax.fori_loop(
            0,
            width // cols,
            middle_part,
            (jnp.zeros(slot_gate.shape, f32), jnp.zeros(gate_pre.shape, f32)),
        )
        save_out(j).start()

        @pl.when(j < tiles - 1)
        def _():
            for copy in load_g(j + 1):
                copy.start()

        for b in range(blocks):
            gg_ref[tile_of(j), :, pl.ds(b * block_rows, block_rows)] = jnp.sum(
                pick[b].astype(f32) * gates_grad[b * slots : (b + 1) * slots],
                axis=0,
                keepdims=True,
            )
        gate_grad = (hidden_grad * up_pre * (sig * (1.0 + gate_pre * (1.0 - sig)))).astype(low)
        up_grad = (hidden_grad * silu).astype(low)
        gp[...] = gate_grad
        up[...] = up_grad
        for copy in saves(j):
            copy.start()

        def part_of(i, yy, cc):
            at = columns(yy * 2 + cc)
            row_grad = dot_last(gate_grad, wg[at, :]) + dot_last(up_grad, wu[at, :])
            return row_grad.astype(low)

        first = jnp.where(slot == 0, 1, 0)

        def to_partner(i, carry):
            yy = jnp.where(i == 1, 1 - y, y)
            rel = first + 2 * i

            @pl.when(j >= 2)
            def _():
                before_zz = far_first(nz, z, j // 2 - 1)
                k = before_zz * 4 + rel
                remote(st.at[slot, i], lp.at[before_zz, rel], s_p.at[k], r_p.at[k], partner).wait_send()

            scatter(st.at[slot, i], slice(None), part_of(i, yy, 1 - c))
            k = zz * 4 + rel
            remote(st.at[slot, i], lp.at[zz, rel], s_p.at[k], r_p.at[k], partner).start()
            return carry

        def to_own(i, carry):
            yy = jnp.where(i == 1, 1 - y, y)
            scatter(w.at[zz, first + 2 * i], slice(None), part_of(i, yy, c))
            return carry

        lax.fori_loop(0, 2, to_partner, 0)
        lax.fori_loop(0, 2, to_own, 0)

    for copy in (load(0, 2), load(0, 0)) + load_g(0):
        copy.start()

    def step(j, carry):
        k, odd = j // 2, j % 2 == 1
        pl.when(j < tiles)(lambda: compute(j))

        @pl.when(odd & (k < nz))
        def _():
            zz = far_first(nz, z, k)
            stage_d(zz, 3, 0)
            stage_d(zz, 1, 0)

        @pl.when(jnp.logical_not(odd) & (k >= 1) & (k <= nz))
        def _():
            zz = far_first(nz, z, k - 1)
            stage_d(zz, 2, 1)
            stage_d(zz, 0, 1)
            stage_e(zz)

        @pl.when((k >= 2) & jnp.logical_not(odd))
        def _():
            stage_f1(far_first(nz, z, k - 2))

        @pl.when((k >= 2) & odd)
        def _():
            stage_f2(far_first(nz, z, k - 2))

        return carry

    lax.fori_loop(0, 2 * (nz + 2), step, 0)
    save_out(tiles - 1).wait()
    for copy in saves(tiles - 1):
        copy.wait()
    for slot in range(2):
        for i in range(2):
            c_p(z, 1 - slot + 2 * i, slot).wait_send()

    def finish(zz, carry):
        for copy in c_diag(zz) + c_xy(zz):
            copy.wait_send()
        pl.when(zz != z)(c_z(zz, zz, up_dev).wait_send)
        return carry

    lax.fori_loop(0, nz, finish, 0)


def run_experts(x_all, g_all, routes_all, router, gate_w, up_w, down_w, block_rows, slots, nz,
                collective_id):
    total, width = x_all.shape
    hidden = gate_w.shape[1]
    experts = router.shape[1]
    tiles = 2 * nz
    rows, cols = total // tiles, width // 4
    pairs = rows // block_rows * slots
    half = rows // 2
    f32, low = jnp.float32, jnp.bfloat16
    any_space = pl.BlockSpec(memory_space=pl.ANY)
    vmem = pl.BlockSpec(memory_space=pltpu.VMEM)
    vm, dma, shape = pltpu.VMEM, pltpu.SemaphoreType.DMA, jax.ShapeDtypeStruct
    return pl.pallas_call(
        functools.partial(expert_kernel, nz, slots, block_rows),
        in_specs=[any_space] * 3 + [vmem] * 4,
        out_specs=[any_space, vmem, vmem, vmem] + [any_space] * 5,
        out_shape=[
            shape((total, width), low), shape((rows, cols), f32), shape((tiles, 1, rows), f32),
            shape((rows, experts), f32),
            shape((tiles, pairs, width), low), shape((tiles, pairs, width), low),
            shape((tiles, pairs, hidden), low), shape((tiles, pairs, hidden), low),
            shape((tiles, pairs, hidden), low),
        ],
        scratch_shapes=[
            vm((rows, width), low), vm((rows, width), low),
            vm((rows, routes_all.shape[1]), jnp.int32), vm((rows, width), low),
            vm((pairs, width), low), vm((pairs, width), low),
            vm((pairs, hidden), low), vm((pairs, hidden), low), vm((pairs, hidden), low),
            vm((2, 2, rows, cols), low),
            vm((nz, 4, rows, cols), low), vm((nz, 4, rows, cols), low),
            vm((nz, rows, cols), low), vm((nz, half, cols), low),
            vm((nz, rows, cols), low), vm((nz, half, cols), low),
            vm((nz + 1, rows, cols), low),
            dma((4,)), dma, dma((5,)), dma((4 * nz,)), dma((4 * nz,)),
        ] + [dma((nz,))] * 9 + [dma((nz + 1,))],
        compiler_params=pltpu.CompilerParams(
            collective_id=collective_id, has_side_effects=True, vmem_limit_bytes=62 << 20
        ),
        name="experts",
    )(x_all, g_all, routes_all, router, gate_w, up_w, down_w)


def near_first(nz, z, k):
    return far_first(nz, z, nz - 1 - k)


class GatherAll:
    sems = 6

    @staticmethod
    def scratch(nz):
        dma = pltpu.SemaphoreType.DMA
        return [dma] + [dma((5 * nz,))] * 2 + [dma((nz,))] * 11

    def __init__(self, nz, src, out, sems, cut):
        (self.lsem, self.s_p, self.r_p, self.s_u, self.s_d, self.s_x, self.s_y, self.s_dx,
         self.s_dy, self.r_z, self.r_x, self.r_y, self.r_dx, self.r_dy) = sems
        self.nz, self.src, self.out, self.cut = nz, src, out, cut
        self.rows, self.cols = src.shape
        self.place = z, x, y, c = place()
        self.partner, self.xn, self.yn = (
            device(z, x, y, 1 - c), device(z, 1 - x, y, c), device(z, x, 1 - y, c))
        self.up, self.down = device(z + 1, x, y, c), device(z - 1, x, y, c)

    def block(self, zz, xx, yy, cc, part=None):
        start, size, unit = (zz * 2 + xx) * self.rows, self.rows, self.rows
        if part == 0:
            size, unit = self.cut, self.rows
        elif part == 1:
            start, size = start + self.cut, self.rows - self.cut
            unit = math.gcd(self.cut, self.rows)
        return self.out.at[pl.ds(pl.multiple_of(start, unit), size),
                           pl.ds(pl.multiple_of((yy * 2 + cc) * self.cols, self.cols), self.cols)]

    def own(self):
        z, x, y, c = self.place
        return pltpu.make_async_copy(self.src, self.block(z, x, y, c), self.lsem)

    def line(self, zz):
        z, x, y, c = self.place
        here = self.block(zz, x, y, c)
        return (remote(here, here, self.s_u.at[zz], self.r_z.at[zz], self.up),
                remote(here, here, self.s_d.at[zz], self.r_z.at[zz], self.down))

    def sides(self, zz):
        z, x, y, c = self.place
        here = self.block(zz, x, y, c)
        return (remote(here, here, self.s_x.at[zz], self.r_x.at[zz], self.xn),
                remote(here, here, self.s_y.at[zz], self.r_y.at[zz], self.yn))

    def across(self, zz):
        z, x, y, c = self.place
        copies = []
        if self.cut > 0:
            here = self.block(zz, 1 - x, y, c, 0)
            copies.append(remote(here, here, self.s_dy.at[zz], self.r_dy.at[zz], self.yn))
        if self.cut < self.rows:
            here = self.block(zz, x, 1 - y, c, 1)
            copies.append(remote(here, here, self.s_dx.at[zz], self.r_dx.at[zz], self.xn))
        return copies

    def pair(self, zz, rel, mine=True):
        z, x, y, c = self.place
        xx = 1 - x if rel in (1, 3, 4) else x
        yy = 1 - y if rel in (2, 3, 4) else y
        here = self.block(zz, xx, yy, c if mine else 1 - c, {3: 0, 4: 1}.get(rel))
        k = zz * 5 + rel
        return remote(here, here, self.s_p.at[k], self.r_p.at[k], self.partner)

    def parts(self):
        return [0, 1, 2] + [3] * (self.cut > 0) + [4] * (self.cut < self.rows)

    def first(self, k):
        zz, z = near_first(self.nz, self.place[0], k), self.place[0]
        up, down = self.line(zz)
        pl.when(k > 0)(lambda: up.wait_recv())
        pl.when((zz <= z) & (z < self.nz - 1))(lambda: up.start())
        pl.when((zz >= z) & (z > 0))(lambda: down.start())
        for copy in self.sides(zz):
            copy.start()
        self.pair(zz, 0).start()

    def second(self, k):
        zz = near_first(self.nz, self.place[0], k)
        to_x, to_y = self.sides(zz)
        across = self.across(zz)
        to_x.wait_recv()
        if self.cut > 0:
            across[0].start()
        self.pair(zz, 1).start()
        to_y.wait_recv()
        if self.cut < self.rows:
            across[-1].start()
        self.pair(zz, 2).start()

    def third(self, k):
        zz = near_first(self.nz, self.place[0], k)
        across = self.across(zz)
        for rel, copy in zip(self.parts()[3:], across):
            copy.wait_recv()
            self.pair(zz, rel).start()

    def finish(self):
        z = self.place[0]

        def step(zz, carry):
            for rel in self.parts():
                self.pair(zz, rel, False).wait_recv()
                self.pair(zz, rel).wait_send()
            up, down = self.line(zz)
            pl.when((zz <= z) & (z < self.nz - 1))(lambda: up.wait_send())
            pl.when((zz >= z) & (z > 0))(lambda: down.wait_send())
            for copy in tuple(self.sides(zz)) + tuple(self.across(zz)):
                copy.wait_send()
            return carry

        lax.fori_loop(0, self.nz, step, 0)


class GatherRows:
    @staticmethod
    def scratch(nz):
        dma = pltpu.SemaphoreType.DMA
        return [dma] + [dma((nz,))] * 5

    def __init__(self, nz, src, out, sems):
        self.lsem, self.s_u, self.s_d, self.s_x, self.r_z, self.r_x = sems
        self.nz, self.src, self.out = nz, src, out
        self.place = z, x, y, c = place()
        self.xn = device(z, 1 - x, y, c)
        self.up, self.down = device(z + 1, x, y, c), device(z - 1, x, y, c)

    def block(self, zz):
        rows = self.src.shape[0]
        return self.out.at[pl.ds(pl.multiple_of((zz * 2 + self.place[1]) * rows, rows), rows)]

    def own(self):
        return pltpu.make_async_copy(self.src, self.block(self.place[0]), self.lsem)

    def copies(self, zz):
        here = self.block(zz)
        return (remote(here, here, self.s_u.at[zz], self.r_z.at[zz], self.up),
                remote(here, here, self.s_d.at[zz], self.r_z.at[zz], self.down),
                remote(here, here, self.s_x.at[zz], self.r_x.at[zz], self.xn))

    def first(self, k):
        zz, z = near_first(self.nz, self.place[0], k), self.place[0]
        up, down, to_x = self.copies(zz)
        pl.when(k > 0)(lambda: up.wait_recv())
        pl.when((zz <= z) & (z < self.nz - 1))(lambda: up.start())
        pl.when((zz >= z) & (z > 0))(lambda: down.start())
        to_x.start()

    def finish(self):
        z = self.place[0]

        def step(zz, carry):
            up, down, to_x = self.copies(zz)
            to_x.wait()
            pl.when((zz <= z) & (z < self.nz - 1))(lambda: up.wait_send())
            pl.when((zz >= z) & (z > 0))(lambda: down.wait_send())
            return carry

        lax.fori_loop(0, self.nz, step, 0)


def mirrored(nz, shard):
    return (nz - 1 - shard // 2) * 2 + shard % 2


def stream_unit(u, nz, block):
    shard = lax.axis_index("fsdp")
    later = u > shard
    micro = jnp.where(later, 1, 0)
    here = jnp.where(later, mirrored(nz, shard), shard)
    key_place = here - jnp.where(later, u - shard - 1, u)
    owner = jnp.where(later, mirrored(nz, key_place), key_place)
    rows = pl.ds(pl.multiple_of((owner * 2 + micro) * block, block), block)
    return micro, here, key_place, rows


def key_bias(micro, here, key_place, block, start_ref):
    key = key_place * block + lax.broadcasted_iota(jnp.int32, (block, block), 0)
    query = here * block + lax.broadcasted_iota(jnp.int32, (block, block), 1)
    return jnp.where((key >= start_ref[micro]) & (key <= query), 0.0, masked_score)


def attend_kernel(nz, q_ref, k_ref, v_ref, start_ref, cot_ref, wo_ref,
                  heads_ref, out_ref, lse_ref, cot_all, wo_all, acc, peak, total, *sems):
    shards = 2 * nz
    width = k_ref.shape[1]
    block = q_ref.shape[0] // 2
    heads = q_ref.shape[1] // width
    z, x, y, c = place()
    split = len(GatherAll.scratch(nz))
    cots = GatherAll(nz, cot_ref, cot_all, sems[:split], cot_ref.shape[0])
    outs = GatherRows(nz, wo_ref, wo_all, sems[split:])
    greet([(None, cots.partner), (None, cots.xn), (None, cots.yn),
           (z < nz - 1, cots.up), (z > 0, cots.down)])
    for part in (outs, cots):
        part.own().start()
    peak[...] = jnp.full(peak.shape, masked_score, jnp.float32)
    total[...] = jnp.zeros_like(total)
    acc[...] = jnp.zeros_like(acc)
    for part in (outs, cots):
        part.own().wait()

    def unit(u, carry):
        @pl.when(u < nz)
        def _():
            outs.first(u)
            cots.first(u)

        pl.when((u >= 1) & (u <= nz))(lambda: cots.second(u - 1))
        pl.when((u >= 2) & (u <= nz + 1))(lambda: cots.third(u - 2))
        pl.when(u < shards + 2 * x)(lambda: attention(u))
        return carry

    def attention(u):
        micro, here, key_place, rows = stream_unit(u, nz, block)
        bias = key_bias(micro, here, key_place, block, start_ref)
        keys, values = k_ref[rows, :], v_ref[rows, :]
        q_rows = pl.ds(pl.multiple_of(micro * block, block), block)

        def head(h, carry):
            at = micro * heads + h
            query = q_ref[q_rows, pl.ds(pl.multiple_of(h * width, width), width)]
            scores = dot_last(keys, query) * width ** (-0.5) + bias
            before = peak[at]
            now = jnp.maximum(before, jnp.max(scores, axis=0, keepdims=True))
            weights = jnp.exp(scores - now)
            factor = jnp.exp(before - now)
            peak[at] = now
            total[at] = total[at] * factor + jnp.sum(weights, axis=0, keepdims=True)
            acc[at] = acc[at] * factor + dot_first(values, weights.astype(jnp.bfloat16))
            return carry

        lax.fori_loop(0, heads, head, 0, unroll=4)

    lax.fori_loop(0, shards + 2, unit, 0)

    def close(at, carry):
        micro, h = at // heads, at % heads
        result = (acc[at] / total[at]).T
        here = pl.ds(pl.multiple_of(micro * block, block), block)
        cols = pl.ds(pl.multiple_of(h * width, width), width)
        out_ref[here, cols] = result
        heads_ref[here, cols] = result.astype(jnp.bfloat16)
        lse_ref[at] = peak[at] + jnp.log(total[at])
        return carry

    lax.fori_loop(0, 2 * heads, close, 0)
    outs.finish()
    cots.finish()


def attend(query, keys, values, starts, cotangent, w_out, nz, collective_id):
    rows, columns = query.shape
    width = keys.shape[1]
    heads = columns // width
    block = rows // 2
    any_space = pl.BlockSpec(memory_space=pl.ANY)
    vmem = pl.BlockSpec(memory_space=pltpu.VMEM)
    vm, shape, f32 = pltpu.VMEM, jax.ShapeDtypeStruct, jnp.float32
    return pl.pallas_call(
        functools.partial(attend_kernel, nz),
        in_specs=[vmem] * 4 + [any_space] * 2,
        out_specs=[vmem] * 3 + [any_space] * 2,
        out_shape=[
            shape((rows, columns), jnp.bfloat16),
            shape((rows, columns), f32),
            shape((2 * heads, 1, block), f32),
            shape((rows * 2 * nz, cotangent.shape[1] * 4), cotangent.dtype),
            shape((w_out.shape[0] * 2 * nz, w_out.shape[1]), w_out.dtype),
        ],
        scratch_shapes=[
            vm((2 * heads, width, block), f32), vm((2 * heads, 1, block), f32),
            vm((2 * heads, 1, block), f32),
        ] + GatherAll.scratch(nz) + GatherRows.scratch(nz),
        compiler_params=pltpu.CompilerParams(
            collective_id=collective_id, has_side_effects=True, vmem_limit_bytes=40 << 20
        ),
        name="attend",
    )(query, keys, values, starts, cotangent, w_out)


class ScatterAll:
    @staticmethod
    def scratch(nz, rows, cols, kind, cut):
        vm, dma = pltpu.VMEM, pltpu.SemaphoreType.DMA
        return [
            vm((nz, 4, rows, cols), kind), vm((nz, 4, rows, cols), kind),
            vm((nz, rows, cols), kind), vm((nz, max(cut, 16), cols), kind),
            vm((nz, rows, cols), kind), vm((nz, max(rows - cut, 16), cols), kind),
            vm((nz + 1, rows, cols), kind),
        ] + [dma((4 * nz,))] * 3 + [dma((nz,))] * 9 + [dma((nz + 1,))]

    def __init__(self, nz, partial, out, refs, cut):
        (self.w, self.lp, self.rx, self.rxd, self.ry, self.ryd, self.rz,
         self.s_l, self.s_p, self.r_p, self.s_x, self.s_y, self.s_dx, self.s_dy, self.s_z,
         self.r_x, self.r_y, self.r_dx, self.r_dy, self.r_z) = refs
        self.nz, self.partial, self.out, self.cut = nz, partial, out, cut
        self.rows, self.cols = out.shape
        self.place = z, x, y, c = place()
        self.partner, self.xn, self.yn = (
            device(z, x, y, 1 - c), device(z, 1 - x, y, c), device(z, x, 1 - y, c))
        self.up, self.down = device(z + 1, x, y, c), device(z - 1, x, y, c)

    def block(self, zz, rel, cc):
        z, x, y, c = self.place
        xx = 1 - x if rel in (1, 3) else x
        yy = 1 - y if rel in (2, 3) else y
        return self.partial.at[
            pl.ds(pl.multiple_of((zz * 2 + xx) * self.rows, self.rows), self.rows),
            pl.ds(pl.multiple_of((yy * 2 + cc) * self.cols, self.cols), self.cols)]

    def pair(self, zz, rel):
        k = zz * 4 + rel
        return remote(self.block(zz, rel, 1 - self.place[3]), self.lp.at[zz, rel],
                      self.s_p.at[k], self.r_p.at[k], self.partner)

    def load(self, zz, rel):
        return pltpu.make_async_copy(
            self.block(zz, rel, self.place[3]), self.w.at[zz, rel], self.s_l.at[zz * 4 + rel])

    def across(self, zz):
        copies = []
        if self.cut > 0:
            copies.append(remote(self.w.at[zz, 3, pl.ds(0, self.cut)], self.rxd.at[zz],
                                 self.s_dx.at[zz], self.r_dx.at[zz], self.xn))
        if self.cut < self.rows:
            copies.append(remote(self.w.at[zz, 3, pl.ds(self.cut, self.rows - self.cut)],
                                 self.ryd.at[zz], self.s_dy.at[zz], self.r_dy.at[zz], self.yn))
        return copies

    def sides(self, zz):
        return (remote(self.w.at[zz, 1], self.rx.at[zz], self.s_x.at[zz], self.r_x.at[zz], self.xn),
                remote(self.w.at[zz, 2], self.ry.at[zz], self.s_y.at[zz], self.r_y.at[zz], self.yn))

    def line(self, zz, slot, where):
        return remote(self.w.at[zz, 0], self.rz.at[slot], self.s_z.at[zz], self.r_z.at[slot], where)

    def start(self):
        def step(k, carry):
            zz = far_first(self.nz, self.place[0], k)
            for rel in (3, 1, 2, 0):
                self.pair(zz, rel).start()
                self.load(zz, rel).start()
            return carry

        lax.fori_loop(0, self.nz, step, 0)

    def first(self, k):
        zz = far_first(self.nz, self.place[0], k)
        for rel in (3, 1, 2, 0):
            self.pair(zz, rel).wait_recv()
            self.load(zz, rel).wait()
            add_blocks(self.w.at[zz, rel], [self.lp.at[zz, rel]], 0, self.rows)
            if rel == 3:
                for copy in self.across(zz):
                    copy.start()

    def second(self, k):
        zz = far_first(self.nz, self.place[0], k)
        across, (to_x, to_y) = self.across(zz), self.sides(zz)
        if self.cut < self.rows:
            across[-1].wait_recv()
            add_blocks(self.w.at[zz, 1], [self.ryd.at[zz]], self.cut, self.rows - self.cut)
        to_x.start()
        if self.cut > 0:
            across[0].wait_recv()
            add_blocks(self.w.at[zz, 2], [self.rxd.at[zz]], 0, self.cut)
        to_y.start()

    def send_line(self, zz):
        z = self.place[0]
        pl.when(zz > z)(lambda: self.line(zz, zz, self.up).start())
        pl.when(zz == z - 1)(lambda: self.line(zz, self.nz, self.down).start())
        pl.when(zz < z - 1)(lambda: self.line(zz, zz, self.down).start())

    def passes(self, zz):
        z = self.place[0]
        return ((zz > z) & (z > 0)) | ((zz < z) & (z < self.nz - 1))

    def third(self, k):
        zz, z = far_first(self.nz, self.place[0], k), self.place[0]
        to_x, to_y = self.sides(zz)
        to_x.wait_recv()
        to_y.wait_recv()
        add_blocks(self.w.at[zz, 0], [self.rx.at[zz], self.ry.at[zz]], 0, self.rows)
        pl.when((zz != z) & jnp.logical_not(self.passes(zz)))(lambda: self.send_line(zz))

    def fourth(self, k):
        zz, z, nz = far_first(self.nz, self.place[0], k), self.place[0], self.nz

        @pl.when((zz != z) & self.passes(zz))
        def _():
            self.line(zz, zz, self.up).wait_recv()
            add_blocks(self.w.at[zz, 0], [self.rz.at[zz]], 0, self.rows)
            self.send_line(zz)

        @pl.when(zz == z)
        def _():
            finish_line(self, self.w.at[zz, 0], zz)

    def finish(self):
        z = self.place[0]

        def step(zz, carry):
            for rel in range(4):
                self.pair(zz, rel).wait_send()
            for copy in tuple(self.across(zz)) + tuple(self.sides(zz)):
                copy.wait_send()
            pl.when(zz != z)(lambda: self.line(zz, zz, self.up).wait_send())
            return carry

        lax.fori_loop(0, self.nz, step, 0)


def finish_line(self, own, zz):
    z, nz = self.place[0], self.nz
    below, above = self.rz.at[zz], self.rz.at[nz]
    pl.when(z > 0)(lambda: self.line(zz, zz, self.up).wait_recv())
    pl.when(z < nz - 1)(lambda: self.line(zz, nz, self.down).wait_recv())
    pl.when(z == 0)(lambda: add_blocks(own, [above], 0, self.rows, self.out))
    pl.when(z == nz - 1)(lambda: add_blocks(own, [below], 0, self.rows, self.out))
    pl.when((z > 0) & (z < nz - 1))(lambda: add_blocks(own, [below, above], 0, self.rows, self.out))


class ReduceRows:
    @staticmethod
    def scratch(nz, rows, cols, kind):
        vm, dma = pltpu.VMEM, pltpu.SemaphoreType.DMA
        return [vm((nz, rows, cols), kind), vm((nz, rows, cols), kind),
                vm((nz + 1, rows, cols), kind)] + [dma((nz,))] * 4 + [dma((nz + 1,))]

    def __init__(self, nz, partial, out, refs):
        self.w, self.rx, self.rz, self.s_l, self.s_x, self.s_z, self.r_x, self.r_z = refs
        self.nz, self.partial, self.out = nz, partial, out
        self.rows = out.shape[0]
        self.place = z, x, y, c = place()
        self.xn = device(z, 1 - x, y, c)
        self.up, self.down = device(z + 1, x, y, c), device(z - 1, x, y, c)

    def block(self, zz, xx):
        return self.partial.at[pl.ds(pl.multiple_of((zz * 2 + xx) * self.rows, self.rows), self.rows)]

    def side(self, zz):
        return remote(self.block(zz, 1 - self.place[1]), self.rx.at[zz],
                      self.s_x.at[zz], self.r_x.at[zz], self.xn)

    def load(self, zz):
        return pltpu.make_async_copy(self.block(zz, self.place[1]), self.w.at[zz], self.s_l.at[zz])

    def line(self, zz, slot, where):
        return remote(self.w.at[zz], self.rz.at[slot], self.s_z.at[zz], self.r_z.at[slot], where)

    def start(self):
        def step(k, carry):
            zz = far_first(self.nz, self.place[0], k)
            self.side(zz).start()
            self.load(zz).start()
            return carry

        lax.fori_loop(0, self.nz, step, 0)

    send_line = ScatterAll.send_line
    passes = ScatterAll.passes

    def first(self, k):
        zz, z = far_first(self.nz, self.place[0], k), self.place[0]
        self.load(zz).wait()
        self.side(zz).wait_recv()
        add_blocks(self.w.at[zz], [self.rx.at[zz]], 0, self.rows)
        pl.when((zz != z) & jnp.logical_not(self.passes(zz)))(lambda: self.send_line(zz))

    def second(self, k):
        zz, z, nz = far_first(self.nz, self.place[0], k), self.place[0], self.nz

        @pl.when((zz != z) & self.passes(zz))
        def _():
            self.line(zz, zz, self.up).wait_recv()
            add_blocks(self.w.at[zz], [self.rz.at[zz]], 0, self.rows)
            self.send_line(zz)

        @pl.when(zz == z)
        def _():
            finish_line(self, self.w.at[zz], zz)

    def finish(self):
        z = self.place[0]

        def step(zz, carry):
            self.side(zz).wait_send()
            pl.when(zz != z)(lambda: self.line(zz, zz, self.up).wait_send())
            return carry

        lax.fori_loop(0, self.nz, step, 0)


def attend_back_kernel(nz, q_ref, k_ref, v_ref, start_ref, lse_ref, delta_ref, grad_ref,
                       gp_ref, up_ref, hid_ref, xr_all, gs_all, out_part, wo_part,
                       q_side, sides, out_sum, wo_sum, dwg, dwu, dwd,
                       acc, k_acc, v_acc, x_panel, g_panel, o_gate, o_up, o_down, s_in, s_out, *refs):
    shards = 2 * nz
    shard = lax.axis_index("fsdp")
    width = k_ref.shape[1]
    block = q_ref.shape[0] // 2
    heads = q_ref.shape[1] // width
    z, x, y, c = place()
    count = shards + 2 * x
    panel = x_panel.shape[1]
    panels = xr_all.shape[1] // panel
    low = jnp.bfloat16
    split = len(ScatterAll.scratch(nz, 16, 128, low, 0))
    outs = ScatterAll(nz, out_part, out_sum, refs[:split], 0)
    weights = ReduceRows(nz, wo_part, wo_sum, refs[split:])
    greet([(None, outs.partner), (None, outs.xn), (None, outs.yn),
           (z < nz - 1, outs.up), (z > 0, outs.down)])
    outs.start()
    weights.start()

    def loads(n):
        at = pl.ds(pl.multiple_of(n * panel, panel), panel)
        return (pltpu.make_async_copy(xr_all.at[:, at], x_panel, s_in.at[0]),
                pltpu.make_async_copy(gs_all.at[:, at], g_panel, s_in.at[1]))

    def stores(n):
        at = pl.ds(pl.multiple_of(n * panel, panel), panel)
        return (pltpu.make_async_copy(o_gate, dwg.at[at, :], s_out.at[0]),
                pltpu.make_async_copy(o_up, dwu.at[at, :], s_out.at[1]),
                pltpu.make_async_copy(o_down, dwd.at[:, at], s_out.at[2]))

    for copy in loads(0):
        copy.start()
    sides[...] = jnp.zeros_like(sides)
    acc[...] = jnp.zeros_like(acc)

    def attention(u):
        micro, here, key_place, rows = stream_unit(u, nz, block)
        bias = key_bias(micro, here, key_place, block, start_ref)
        keys, values = k_ref[rows, :], v_ref[rows, :]
        q_rows = pl.ds(pl.multiple_of(micro * block, block), block)
        k_acc[...] = jnp.zeros_like(k_acc)
        v_acc[...] = jnp.zeros_like(v_acc)

        def head(h, carry):
            at = micro * heads + h
            cols = pl.ds(pl.multiple_of(h * width, width), width)
            query, grad = q_ref[q_rows, cols], grad_ref[q_rows, cols]
            scores = dot_last(keys, query) * width ** (-0.5) + bias
            probs = jnp.exp(scores - lse_ref[at])
            score_grad = (probs * (dot_last(values, grad) - delta_ref[at])).astype(low)
            v_acc[...] += dot_plain(probs.astype(low), grad)
            k_acc[...] += dot_plain(score_grad, query)
            acc[at] += dot_first(keys, score_grad)
            return carry

        lax.fori_loop(0, heads, head, 0, unroll=2)
        sides[rows, pl.ds(0, width)] = (k_acc[...] * width ** (-0.5)).astype(low)
        sides[rows, pl.ds(width, width)] = v_acc[...].astype(low)

    def expert_weights(n):
        for copy in loads(n):
            copy.wait()

        @pl.when(n > 0)
        def _():
            for copy in stores(n):
                copy.wait()

        o_gate[...] = dot_first(x_panel[...], gp_ref[...])
        o_up[...] = dot_first(x_panel[...], up_ref[...])
        o_down[...] = dot_first(g_panel[...], hid_ref[...]).T
        for copy in stores(n):
            copy.start()

        @pl.when(n < panels - 1)
        def _():
            for copy in loads(n + 1):
                copy.start()

    def unit(u, carry):
        def at(fn, k):
            pl.when((k >= 0) & (k < nz))(lambda: fn(k))

        at(outs.first, u)
        at(weights.first, u)
        at(outs.second, u - 1)
        at(weights.second, u - 1)
        at(outs.third, u - 2)
        at(outs.fourth, u - 3)
        pl.when(u < count)(lambda: attention(u))
        pl.when(u < panels)(lambda: expert_weights(u))
        return carry

    lax.fori_loop(0, max(shards + 2, panels), unit, 0)

    def close(at, carry):
        micro, h = at // heads, at % heads
        q_side[pl.ds(pl.multiple_of(micro * block, block), block),
               pl.ds(pl.multiple_of(h * width, width), width)] = acc[at].T * width ** (-0.5)
        return carry

    lax.fori_loop(0, 2 * heads, close, 0)
    for copy in stores(panels - 1):
        copy.wait()
    outs.finish()
    weights.finish()


def attend_back(query, keys, values, starts, log_total, delta, grad, gate_grad, up_grad, hidden,
                rows_in, pair_grad, out_part, wo_part, nz, collective_id):
    rows, columns = query.shape
    width = keys.shape[1]
    heads = columns // width
    block = rows // 2
    pairs, features = rows_in.shape
    hidden_width = hidden.shape[1]
    panel = 256
    cols = out_part.shape[1] // 4
    wo_shape = (wo_part.shape[0] // (2 * nz), wo_part.shape[1])
    any_space = pl.BlockSpec(memory_space=pl.ANY)
    vmem = pl.BlockSpec(memory_space=pltpu.VMEM)
    vm, shape, f32, low = pltpu.VMEM, jax.ShapeDtypeStruct, jnp.float32, jnp.bfloat16
    dma = pltpu.SemaphoreType.DMA
    return pl.pallas_call(
        functools.partial(attend_back_kernel, nz),
        in_specs=[vmem] * 10 + [any_space] * 4,
        out_specs=[vmem] * 4 + [any_space] * 3,
        out_shape=[
            shape((rows, columns), f32), shape((rows * 2 * nz, 2 * width), low),
            shape((rows, cols), f32), shape(wo_shape, f32),
            shape((features, hidden_width), f32), shape((features, hidden_width), f32),
            shape((hidden_width, features), f32),
        ],
        scratch_shapes=[
            vm((2 * heads, width, block), f32), vm((block, width), f32), vm((block, width), f32),
            vm((pairs, panel), low), vm((pairs, panel), low),
            vm((panel, hidden_width), f32), vm((panel, hidden_width), f32),
            vm((hidden_width, panel), f32), dma((2,)), dma((3,)),
        ] + ScatterAll.scratch(nz, rows, cols, low, 0) + ReduceRows.scratch(nz, *wo_shape, low),
        compiler_params=pltpu.CompilerParams(
            collective_id=collective_id, has_side_effects=True, vmem_limit_bytes=63 << 20
        ),
        name="attend_back",
    )(query, keys, values, starts, log_total, delta, grad, gate_grad, up_grad, hidden,
      rows_in, pair_grad, out_part, wo_part)


def gathered_body(
    tokens,
    cotangent,
    routes,
    doc_ids,
    gain_attn,
    w_query,
    key_weight,
    value_weight,
    w_out,
    gain_query,
    key_norm_gain,
    gain_moe,
    router,
    w_gate,
    w_up,
    w_down,
):
    shard_count = lax.axis_size("fsdp")
    group_count = lax.axis_size("tp")
    shard_index = lax.axis_index("fsdp")
    group_index = lax.axis_index("tp")
    nz = shard_count // 2
    f32, low = jnp.float32, jnp.bfloat16
    row_count, slice_width = tokens.shape
    model_width = slice_width * group_count
    micro_count, micro_rows = doc_ids.shape
    head_width = gain_query.shape[0]
    query_width, kv_width = w_query.shape[1], key_weight.shape[1]
    query_local = query_width // head_width
    kv_local = kv_width // head_width
    group_width = query_local // kv_local
    expert_total = router.shape[1]
    capacity = max(2, 2 * micro_rows * TOPK // expert_total)
    block_keys = micro_rows * math.gcd(shard_count, max(1, 512 // micro_rows))
    my_columns = group_index * slice_width

    mirror_index = mirrored(nz, shard_index)
    owners = jnp.stack([shard_index, mirror_index])

    def to_owners(array):
        second = array[:, 1].reshape((nz, 2) + array.shape[2:])[::-1].reshape(array[:, 1].shape)
        return jnp.stack([array[:, 0], second], axis=1)

    small = jnp.concatenate([routes.reshape(-1), doc_ids.reshape(-1)])
    small_rows = -(-small.shape[0] // 1024) * 8
    small = jnp.pad(small, (0, small_rows * 128 - small.shape[0])).reshape(small_rows, 128)
    small_all, wq_all, wk_all, wv_all, tokens, full_tokens = gather_rows(
        [small, w_query, key_weight, value_weight], nz, 2, [tokens]
    )
    small_all = small_all.reshape(shard_count, small_rows * 128)
    routes_all = to_owners(
        small_all[:, : row_count * TOPK].reshape(shard_count, micro_count, micro_rows, TOPK)
    ).reshape(shard_count * row_count, TOPK)
    ids_all = small_all[:, row_count * TOPK : row_count * (TOPK + 1)].reshape(
        shard_count, micro_count, micro_rows
    )
    doc_range = jnp.arange(DOCS)
    doc_totals = jnp.sum((ids_all[..., None] == doc_range).astype(jnp.int32), axis=(0, 2))
    doc_begin = jnp.cumsum(doc_totals, axis=1) - doc_totals
    query_index = owners[:, None] * micro_rows + jnp.arange(micro_rows)
    my_ids = jnp.stack(
        [lax.dynamic_index_in_dim(ids_all[:, m], owners[m], 0, False) for m in range(micro_count)]
    )
    query_start = jnp.sum(
        jnp.where(my_ids[:, :, None] == doc_range, doc_begin[:, None, :], 0), axis=2
    )
    positions = (query_index - query_start).reshape(row_count)
    cosine_lookup, sine_lookup = rope_tables(positions, head_width)

    full_tokens = full_tokens.astype(f32)
    token_mean = jnp.mean(full_tokens * full_tokens, axis=-1, keepdims=True)
    token_scale = lax.rsqrt(token_mean + norm_eps)
    normed_low = (full_tokens * token_scale * gain_attn).astype(low)
    query_pre = jnp.dot(normed_low, wq_all, preferred_element_type=f32)
    key_pre = jnp.dot(normed_low, wk_all, preferred_element_type=f32)
    value_low = jnp.dot(normed_low, wv_all, preferred_element_type=f32).astype(low)

    def shape_heads(query_raw, key_raw, query_gain, key_gain):
        query_heads = rotary_apply(
            root_mean_norm(query_raw.reshape(row_count, query_local, head_width), query_gain),
            cosine_lookup[:, None, :],
            sine_lookup[:, None, :],
        )
        key_heads = rotary_apply(
            root_mean_norm(key_raw.reshape(row_count, kv_local, head_width), key_gain),
            cosine_lookup[:, None, :],
            sine_lookup[:, None, :],
        )
        return (query_heads, key_heads)

    (query_heads, key_heads), heads_pull = jax.vjp(
        shape_heads, query_pre, key_pre, gain_query, key_norm_gain
    )
    query_low = query_heads.astype(low)
    key_low = key_heads.reshape(row_count, kv_width).astype(low)
    keys_got, values_got = gather_rows([key_low, value_low], nz, 4)

    starts = query_start.reshape(micro_count, 1, micro_rows).astype(jnp.int32)
    heads_low, head_out, log_total, grads_all, wo_all = attend(
        query_low.reshape(row_count, query_width), keys_got, values_got,
        starts, cotangent, w_out, nz, 3,
    )
    attn_part = dot_last(heads_low, wo_all).astype(low)
    middle = tokens.astype(f32) + reduce_cols(attn_part, 5)

    def row_mean(values, collective_id):
        total = jnp.sum(values, axis=1).reshape(row_count // 128, 128)
        return sum_cols(total, collective_id).reshape(row_count, 1) / model_width

    scale = lax.rsqrt(row_mean(middle * middle, 6) + norm_eps)
    gain_slice = lax.dynamic_slice_in_dim(gain_moe, my_columns, slice_width)
    moe_low = (middle * scale * gain_slice).astype(low)
    moe_all = gather_all(moe_low, nz, 7)
    out_part, back, gates_grad, gates, *kept = run_experts(
        moe_all, grads_all, routes_all, router, w_gate[0], w_up[0], w_down[0],
        micro_rows, capacity, nz, 8,
    )
    rows_in, pair_grad, hidden_low, gate_pre_low, up_pre_low = (
        array.reshape(-1, array.shape[2]) for array in kept
    )
    gates_grad = swap_rows(
        gates_grad.reshape(shard_count, row_count // 128, 128), shard_count, group_count, 9
    ).reshape(expert_total, row_count).T
    logit_grad = gates * (gates_grad - jnp.sum(gates * gates_grad, axis=1, keepdims=True))
    router_slice = lax.dynamic_slice_in_dim(router, my_columns, slice_width).astype(f32)
    moe_grad = back + lax.dot_general(
        logit_grad, router_slice, (((1,), (1,)), ((), ())), precision=highest_precision
    )
    router_part = lax.dot_general(
        moe_low.astype(f32), logit_grad, (((0,), (0,)), ((), ())), precision=highest_precision
    )
    gain_moe_part = jnp.sum(moe_grad * middle * scale, axis=0)
    swapped_grad = lax.dynamic_slice(
        grads_all, (mirror_index * row_count + micro_rows, my_columns), (micro_rows, slice_width)
    )
    grad_slice = jnp.concatenate([cotangent[:micro_rows], swapped_grad], axis=0).astype(f32)
    inner = gain_slice * moe_grad
    middle_grad = (
        grad_slice + scale * inner - middle * scale**3 * row_mean(middle * inner, 10)
    )
    middle_low = gather_cols(middle_grad.astype(low), 11)
    out_grad_part = dot_first(middle_low, heads_low).astype(low)
    heads_grad = jnp.dot(middle_low, wo_all, preferred_element_type=f32).astype(low)
    delta = jnp.sum(
        (heads_grad.astype(f32) * head_out).reshape(micro_count, micro_rows, query_local, head_width),
        axis=3,
    ).transpose(0, 2, 1).reshape(micro_count * query_local, 1, micro_rows)
    query_side, sides, out_sum, w_out_grad, gate_acc, up_acc, down_acc = attend_back(
        query_low.reshape(row_count, query_width), keys_got, values_got, starts, log_total, delta,
        heads_grad, gate_pre_low, up_pre_low, hidden_low, rows_in, pair_grad, out_part,
        out_grad_part, nz, 12,
    )
    block_out = (middle + out_sum).astype(low)
    sides = reduce_rows(sides, nz, 14)
    query_pre_grad, key_pre_grad, gain_query_part, gain_key_part = heads_pull(
        (
            query_side.reshape(row_count, query_local, head_width),
            sides[:, :kv_width].reshape(row_count, kv_local, head_width),
        )
    )
    query_pre_low = query_pre_grad.astype(low)
    key_pre_low = key_pre_grad.astype(low)
    value_pre_low = sides[:, kv_width:].astype(low)
    normed_part = (
        dot_last(query_pre_low, wq_all)
        + dot_last(key_pre_low, wk_all)
        + dot_last(value_pre_low, wv_all)
    ).astype(low)
    normed_grad = reduce_cols(normed_part, 15)
    pre_low = jnp.concatenate([query_pre_low, key_pre_low, value_pre_low], axis=1)
    weight_grad = reduce_rows(dot_first(normed_low, pre_low).astype(low), nz, 16)
    token_slice = tokens.astype(f32)
    attn_gain = lax.dynamic_slice_in_dim(gain_attn, my_columns, slice_width)
    gain_attn_part = jnp.sum(normed_grad * token_slice * token_scale, axis=0)
    inner = attn_gain * normed_grad
    token_grad = (
        middle_grad
        + token_scale * inner
        - token_slice * token_scale**3 * row_mean(token_slice * inner, 17)
    ).astype(low)

    there = swap_back([block_out[micro_rows:], token_grad[micro_rows:]], nz, 19)
    block_out = jnp.concatenate([block_out[:micro_rows], there[0]], axis=0)
    token_grad = jnp.concatenate([token_grad[:micro_rows], there[1]], axis=0)

    pieces = [router_part.reshape(-1), gain_attn_part, gain_moe_part, gain_query_part, gain_key_part]
    length = sum(piece.shape[0] for piece in pieces)
    part_rows = -(-length // (shard_count * 1024)) * 8
    flat = jnp.concatenate(
        pieces + [jnp.zeros((shard_count * part_rows * 128 - length,), f32)]
    ).reshape(shard_count, part_rows, 128)
    summed = sum_small(flat, shard_count, group_count, 18).reshape(
        shard_count, group_count, part_rows * 128
    ).transpose(1, 0, 2).reshape(group_count, shard_count * part_rows * 128)
    at = 0
    sums = []
    for piece in pieces:
        sums.append(summed[:, at : at + piece.shape[0]])
        at += piece.shape[0]
    return (
        block_out,
        token_grad,
        sums[1].reshape(-1),
        weight_grad[:, :query_width],
        weight_grad[:, query_width : query_width + kv_width],
        weight_grad[:, query_width + kv_width :],
        w_out_grad,
        jnp.sum(sums[3], axis=0),
        jnp.sum(sums[4], axis=0),
        sums[2].reshape(-1),
        sums[0].reshape(router.shape),
        gate_acc[None],
        up_acc[None],
        down_acc[None],
    )


def solution(mesh):
    small = mesh.shape["fsdp"] * mesh.shape["tp"] <= 32 and mesh.shape["tp"] == 4
    return jax.shard_map(
        gathered_body if small else body,
        mesh=mesh,
        in_specs=(
            P("fsdp", "tp"),
            P("fsdp", "tp"),
            P("fsdp", None),
            P(None, "fsdp"),
            P(),
            P("fsdp", "tp"),
            P("fsdp", "tp"),
            P("fsdp", "tp"),
            P("fsdp", "tp"),
            P(),
            P(),
            P(),
            P(),
            P(("fsdp", "tp"), None, None),
            P(("fsdp", "tp"), None, None),
            P(("fsdp", "tp"), None, None),
        ),
        out_specs=(
            P("fsdp", "tp"),
            P("fsdp", "tp"),
            P(),
            P("fsdp", "tp"),
            P("fsdp", "tp"),
            P("fsdp", "tp"),
            P("fsdp", "tp"),
            P(),
            P(),
            P(),
            P(),
            P(("fsdp", "tp"), None, None),
            P(("fsdp", "tp"), None, None),
            P(("fsdp", "tp"), None, None),
        ),
        check_vma=False,
    )
```

```python
import functools
import math

import jax
import jax.numpy as jnp
from jax import lax
from jax.experimental import pallas as pl
from jax.experimental.pallas import tpu as pltpu
from jax.sharding import PartitionSpec as P

TOPK = 8
DOCS = 4


theta_base = 1000000.0
norm_eps = 1e-06
masked_score = -1e30
highest_precision = lax.Precision.HIGHEST


def root_mean_norm(row_block, gain_row):
    return (
        row_block
        * lax.rsqrt(jnp.mean(row_block * row_block, axis=-1, keepdims=True) + norm_eps)
        * gain_row
    )


def rotary_apply(row_block, cosine_lookup, sine_lookup):
    half_width = row_block.shape[-1] // 2
    turned = jnp.concatenate([-row_block[..., half_width:], row_block[..., :half_width]], axis=-1)
    return row_block * cosine_lookup + turned * sine_lookup


def rope_tables(positions, head_width):
    half_width = head_width // 2
    frequency = theta_base ** (
        -2.0 * jnp.arange(half_width, dtype=jnp.int32).astype(jnp.float32) / head_width
    )
    angles = positions.astype(jnp.float32)[:, None] * frequency[None, :]
    cosine_lookup = jnp.cos(angles)
    sine_lookup = jnp.sin(angles)
    return (
        jnp.concatenate([cosine_lookup, cosine_lookup], axis=-1),
        jnp.concatenate([sine_lookup, sine_lookup], axis=-1),
    )


def swiglu(gate_pre, up_pre):
    return jax.nn.silu(gate_pre) * up_pre


def dot_first(left_side, right_side):
    return lax.dot_general(
        left_side, right_side, (((0,), (0,)), ((), ())), preferred_element_type=jnp.float32
    )


def dot_last(left_side, right_side):
    return lax.dot_general(
        left_side, right_side, (((1,), (1,)), ((), ())), preferred_element_type=jnp.float32
    )


def gather_weights(w_query, key_weight, value_weight, w_out):
    return (
        lax.all_gather(w_query, "fsdp", axis=0, tiled=True),
        lax.all_gather(key_weight, "fsdp", axis=0, tiled=True),
        lax.all_gather(value_weight, "fsdp", axis=0, tiled=True),
        lax.all_gather(w_out, "fsdp", axis=0, tiled=True),
    )


def gather_keys(keys_low, values_low):
    return (
        lax.all_gather(keys_low, "fsdp", axis=0, tiled=True),
        lax.all_gather(values_low, "fsdp", axis=0, tiled=True),
    )


def send_rows(buffer):
    return lax.all_to_all(buffer, "fsdp", split_axis=0, concat_axis=0, tiled=True)


def return_rows(buffer):
    return lax.all_to_all(buffer, "fsdp", split_axis=0, concat_axis=0, tiled=True)


def to_heads(per_token, kv_local, group_width):
    token_count, head_total, head_width = per_token.shape
    grouped_heads = per_token.reshape(token_count, kv_local, group_width, head_width)
    return grouped_heads.transpose(1, 2, 0, 3).reshape(
        kv_local, group_width * token_count, head_width
    )


def to_tokens(per_head, group_width):
    kv_local, row_count, head_width = per_head.shape
    token_count = row_count // group_width
    grouped_heads = per_head.reshape(kv_local, group_width, token_count, head_width)
    return grouped_heads.transpose(2, 0, 1, 3).reshape(
        token_count, kv_local * group_width * head_width
    )


def key_block(keys_all, key_start, block_keys, kv_local, head_width):
    return lax.dynamic_slice_in_dim(keys_all, key_start, block_keys, 0).reshape(
        block_keys, kv_local, head_width
    )


def block_scores(queries, keys_part, key_start, query_index, query_start):
    head_width = queries.shape[-1]
    scores = jnp.einsum(
        "hrd,khd->hrk", queries, keys_part, preferred_element_type=jnp.float32
    ) * head_width ** (-0.5)
    key_index = key_start + jnp.arange(keys_part.shape[0])
    allowed = (key_index[None, :] >= query_start[:, None]) & (
        key_index[None, :] <= query_index[:, None]
    )
    return (jnp.where(allowed[None], scores, masked_score), allowed)


def attend_forward(queries, keys_all, values_all, query_index, query_start, block_keys):
    kv_local, row_count, head_width = queries.shape
    lowest_block = jnp.min(query_start) // block_keys
    highest_block = jnp.max(query_index) // block_keys + 1

    def visit_block(block_index, running):
        run_peak, run_total, run_acc = running
        key_start = block_index * block_keys
        keys_part = key_block(keys_all, key_start, block_keys, kv_local, head_width)
        values_part = key_block(values_all, key_start, block_keys, kv_local, head_width)
        scores, allowed = block_scores(queries, keys_part, key_start, query_index, query_start)
        new_peak = jnp.maximum(run_peak, jnp.max(scores, axis=-1))
        weights = jnp.where(allowed[None], jnp.exp(scores - new_peak[..., None]), 0.0)
        factor = jnp.exp(run_peak - new_peak)
        run_total = run_total * factor + jnp.sum(weights, axis=-1)
        run_acc = run_acc * factor[..., None] + jnp.einsum(
            "hrk,khd->hrd",
            weights.astype(jnp.bfloat16),
            values_part,
            preferred_element_type=jnp.float32,
        )
        return (new_peak, run_total, run_acc)

    start_state = (
        jnp.full((kv_local, row_count), masked_score, jnp.float32),
        jnp.zeros((kv_local, row_count), jnp.float32),
        jnp.zeros((kv_local, row_count, head_width), jnp.float32),
    )
    run_peak, run_total, run_acc = lax.fori_loop(
        lowest_block, highest_block, visit_block, start_state
    )
    return (run_acc / run_total[..., None], run_peak + jnp.log(run_total))


def attend_backward(
    queries,
    keys_all,
    values_all,
    query_index,
    query_start,
    block_keys,
    outputs,
    log_total,
    grad_low,
):
    kv_local, row_count, head_width = queries.shape
    key_count = keys_all.shape[0]
    score_scale = head_width ** (-0.5)
    row_delta = jnp.sum(grad_low.astype(jnp.float32) * outputs, axis=-1)
    lowest_block = jnp.min(query_start) // block_keys
    highest_block = jnp.max(query_index) // block_keys + 1

    def visit_block(block_index, running):
        query_acc, key_acc, value_acc = running
        key_start = block_index * block_keys
        keys_part = key_block(keys_all, key_start, block_keys, kv_local, head_width)
        values_part = key_block(values_all, key_start, block_keys, kv_local, head_width)
        scores, allowed = block_scores(queries, keys_part, key_start, query_index, query_start)
        prob_block = jnp.where(allowed[None], jnp.exp(scores - log_total[..., None]), 0.0)
        prob_grad = jnp.einsum(
            "hrd,khd->hrk", grad_low, values_part, preferred_element_type=jnp.float32
        )
        score_grad = (prob_block * (prob_grad - row_delta[..., None])).astype(jnp.bfloat16)
        query_acc = (
            query_acc
            + jnp.einsum("hrk,khd->hrd", score_grad, keys_part, preferred_element_type=jnp.float32)
            * score_scale
        )
        key_part = (
            jnp.einsum("hrk,hrd->khd", score_grad, queries, preferred_element_type=jnp.float32)
            * score_scale
        )
        value_part = jnp.einsum(
            "hrk,hrd->khd",
            prob_block.astype(jnp.bfloat16),
            grad_low,
            preferred_element_type=jnp.float32,
        )
        key_acc = lax.dynamic_update_slice_in_dim(
            key_acc, key_part.reshape(block_keys, kv_local * head_width), key_start, 0
        )
        value_acc = lax.dynamic_update_slice_in_dim(
            value_acc, value_part.reshape(block_keys, kv_local * head_width), key_start, 0
        )
        return (query_acc, key_acc, value_acc)

    start_state = (
        jnp.zeros((kv_local, row_count, head_width), jnp.float32),
        jnp.zeros((key_count, kv_local * head_width), jnp.float32),
        jnp.zeros((key_count, kv_local * head_width), jnp.float32),
    )
    return lax.fori_loop(lowest_block, highest_block, visit_block, start_state)


def body(
    tokens,
    cotangent,
    routes,
    doc_ids,
    gain_attn,
    w_query,
    key_weight,
    value_weight,
    w_out,
    gain_query,
    key_norm_gain,
    gain_moe,
    router,
    w_gate,
    w_up,
    w_down,
):
    shard_count = lax.axis_size("fsdp")
    group_count = lax.axis_size("tp")
    shard_index = lax.axis_index("fsdp")
    group_index = lax.axis_index("tp")
    full_tokens, full_grads = (
        lax.all_gather(tokens, "tp", axis=1, tiled=True),
        lax.all_gather(cotangent, "tp", axis=1, tiled=True),
    )
    slice_width = tokens.shape[1]
    model_width = full_tokens.shape[1]
    micro_count, micro_rows = doc_ids.shape
    head_width = gain_query.shape[0]
    query_local = w_query.shape[1] // head_width
    kv_local = key_weight.shape[1] // head_width
    group_width = query_local // kv_local
    expert_total = router.shape[1]
    capacity = max(2, 2 * micro_rows * TOPK // expert_total)
    slot_total = shard_count * capacity
    pair_total = micro_rows * TOPK
    block_keys = micro_rows * math.gcd(shard_count, max(1, 512 // micro_rows))
    doc_range = jnp.arange(DOCS)
    expert_range = jnp.arange(expert_total)
    local_counts = jnp.sum((doc_ids[:, :, None] == doc_range).astype(jnp.float32), axis=1)
    doc_totals = lax.psum(local_counts, "fsdp")
    doc_begin = (jnp.cumsum(doc_totals, axis=1) - doc_totals).astype(jnp.int32)
    gate_expert = w_gate[0]
    up_expert = w_up[0]
    down_expert = w_down[0]
    router_wide = router.astype(jnp.float32)
    query_acc = jnp.zeros((model_width, query_local * head_width), jnp.float32)
    key_acc = jnp.zeros((model_width, kv_local * head_width), jnp.float32)
    value_acc = jnp.zeros((model_width, kv_local * head_width), jnp.float32)
    out_acc = jnp.zeros((model_width, query_local * head_width), jnp.float32)
    gate_acc = jnp.zeros(gate_expert.shape, jnp.float32)
    up_acc = jnp.zeros(up_expert.shape, jnp.float32)
    down_acc = jnp.zeros(down_expert.shape, jnp.float32)
    router_acc = jnp.zeros(router.shape, jnp.float32)
    gain_attn_acc = jnp.zeros(gain_attn.shape, jnp.float32)
    gain_moe_acc = jnp.zeros(gain_moe.shape, jnp.float32)
    gain_query_acc = jnp.zeros(gain_query.shape, jnp.float32)
    gain_key_acc = jnp.zeros(key_norm_gain.shape, jnp.float32)
    out_parts = []
    grad_parts = []
    for micro_index in range(micro_count):
        row_begin = micro_index * micro_rows
        token_block = full_tokens[row_begin : row_begin + micro_rows].astype(jnp.float32)
        ids_now = doc_ids[micro_index]
        query_index = shard_index * micro_rows + jnp.arange(micro_rows)
        query_start = jnp.sum(
            jnp.where(ids_now[:, None] == doc_range, doc_begin[micro_index][None, :], 0), axis=1
        )
        cosine_lookup, sine_lookup = rope_tables(query_index - query_start, head_width)
        gathered = gather_weights(w_query, key_weight, value_weight, w_out)
        normed, norm_pull = jax.vjp(root_mean_norm, token_block, gain_attn)
        normed_reduced = normed.astype(jnp.bfloat16)
        query_pre = jnp.dot(normed_reduced, gathered[0], preferred_element_type=jnp.float32)
        key_before_norm = jnp.dot(normed_reduced, gathered[1], preferred_element_type=jnp.float32)
        value_reduced = jnp.dot(
            normed_reduced, gathered[2], preferred_element_type=jnp.float32
        ).astype(jnp.bfloat16)

        def shape_heads(query_raw, key_raw, query_gain, key_gain):
            query_heads = rotary_apply(
                root_mean_norm(query_raw.reshape(micro_rows, query_local, head_width), query_gain),
                cosine_lookup[:, None, :],
                sine_lookup[:, None, :],
            )
            key_heads = rotary_apply(
                root_mean_norm(key_raw.reshape(micro_rows, kv_local, head_width), key_gain),
                cosine_lookup[:, None, :],
                sine_lookup[:, None, :],
            )
            return (query_heads, key_heads)

        (query_heads, key_heads), heads_pull = jax.vjp(
            shape_heads, query_pre, key_before_norm, gain_query, key_norm_gain
        )
        queries = to_heads(query_heads.astype(jnp.bfloat16), kv_local, group_width)
        keys_low = key_heads.reshape(micro_rows, kv_local * head_width).astype(jnp.bfloat16)
        keys_all, values_all = gather_keys(keys_low, value_reduced)
        row_index = jnp.tile(query_index, group_width)
        row_start = jnp.tile(query_start, group_width)
        head_out, log_total = attend_forward(
            queries, keys_all, values_all, row_index, row_start, block_keys
        )
        heads_low = to_tokens(head_out, group_width).astype(jnp.bfloat16)
        attn_part = dot_last(heads_low, gathered[3])
        middle = token_block + lax.psum(attn_part.astype(jnp.bfloat16), "tp").astype(jnp.float32)
        moe_normed, moe_pull = jax.vjp(root_mean_norm, middle, gain_moe)
        moe_low = moe_normed.astype(jnp.bfloat16)
        logits = jnp.dot(moe_low, router, preferred_element_type=jnp.float32)
        routes_now = routes[row_begin : row_begin + micro_rows]
        route_match = routes_now[:, :, None] == expert_range
        chosen = jnp.sum(jnp.where(route_match, logits[:, None, :], 0.0), axis=-1)
        gate_weights, softmax_pull = jax.vjp(jax.nn.softmax, chosen)
        mine = routes_now % group_count == group_index
        pair_target = jnp.where(mine, routes_now // group_count, shard_count).reshape(pair_total)
        target_hot = (pair_target[:, None] == jnp.arange(shard_count)).astype(jnp.int32)
        pair_rank = jnp.sum((jnp.cumsum(target_hot, axis=0) - target_hot) * target_hot, axis=1)
        pair_slot = jnp.where(
            pair_target < shard_count, pair_target * capacity + pair_rank, slot_total
        )
        slot_pair = (
            jnp.full((slot_total + 1,), pair_total, jnp.int32)
            .at[pair_slot]
            .set(jnp.arange(pair_total, dtype=jnp.int32))[:slot_total]
        )
        slot_token = slot_pair // TOPK
        slot_grid = pair_slot.reshape(micro_rows, TOPK)
        padded_low = jnp.concatenate([moe_low, jnp.zeros((1, model_width), jnp.bfloat16)], axis=0)
        received = send_rows(
            padded_low[slot_token].reshape(shard_count, capacity, model_width)
        ).reshape(slot_total, model_width)
        gate_pre = jnp.dot(received, gate_expert, preferred_element_type=jnp.float32)
        up_pre = jnp.dot(received, up_expert, preferred_element_type=jnp.float32)
        hidden, swiglu_pull = jax.vjp(swiglu, gate_pre, up_pre)
        hidden_low = hidden.astype(jnp.bfloat16)
        expert_out = jnp.dot(hidden_low, down_expert, preferred_element_type=jnp.float32).astype(
            jnp.bfloat16
        )
        returned = return_rows(expert_out.reshape(shard_count, capacity, model_width)).reshape(
            slot_total, model_width
        )
        padded_out = jnp.concatenate([returned, jnp.zeros((1, model_width), jnp.bfloat16)], axis=0)
        moe_part = jnp.zeros((micro_rows, model_width), jnp.float32)
        for pick_index in range(TOPK):
            moe_part = moe_part + gate_weights[:, pick_index : pick_index + 1] * padded_out[
                slot_grid[:, pick_index]
            ].astype(jnp.float32)
        moe_share = lax.psum_scatter(
            moe_part.astype(jnp.bfloat16), "tp", scatter_dimension=1, tiled=True
        ).astype(jnp.float32)
        middle_slice = lax.dynamic_slice_in_dim(middle, group_index * slice_width, slice_width, 1)
        out_parts.append((middle_slice + moe_share).astype(jnp.bfloat16))
        grad_block = full_grads[row_begin : row_begin + micro_rows].astype(jnp.float32)
        gate_columns = []
        for pick_index in range(TOPK):
            gate_columns.append(
                jnp.sum(
                    grad_block * padded_out[slot_grid[:, pick_index]].astype(jnp.float32), axis=1
                )
            )
        gates_grad = jnp.stack(gate_columns, axis=1)
        flat_gates = jnp.concatenate(
            [gate_weights.reshape(pair_total), jnp.zeros((1,), jnp.float32)]
        )
        padded_grad = jnp.concatenate(
            [grad_block, jnp.zeros((1, model_width), jnp.float32)], axis=0
        )
        send_grad = (padded_grad[slot_token] * flat_gates[slot_pair][:, None]).astype(jnp.bfloat16)
        received_grad = send_rows(send_grad.reshape(shard_count, capacity, model_width)).reshape(
            slot_total, model_width
        )
        hidden_grad = dot_last(received_grad, down_expert)
        down_acc = down_acc + dot_first(hidden_low, received_grad)
        gate_pre_grad, up_pre_grad = swiglu_pull(hidden_grad)
        gate_pre_low = gate_pre_grad.astype(jnp.bfloat16)
        up_pre_low = up_pre_grad.astype(jnp.bfloat16)
        gate_acc = gate_acc + dot_first(received, gate_pre_low)
        up_acc = up_acc + dot_first(received, up_pre_low)
        rows_back = (dot_last(gate_pre_low, gate_expert) + dot_last(up_pre_low, up_expert)).astype(
            jnp.bfloat16
        )
        back_rows = return_rows(rows_back.reshape(shard_count, capacity, model_width)).reshape(
            slot_total, model_width
        )
        padded_back = jnp.concatenate(
            [back_rows, jnp.zeros((1, model_width), jnp.bfloat16)], axis=0
        )
        moe_grad = jnp.zeros((micro_rows, model_width), jnp.float32)
        for pick_index in range(TOPK):
            moe_grad = moe_grad + padded_back[slot_grid[:, pick_index]].astype(jnp.float32)
        (chosen_grad,) = softmax_pull(gates_grad)
        logit_grad = jnp.sum(jnp.where(route_match, chosen_grad[:, :, None], 0.0), axis=1)
        router_acc = router_acc + lax.dot_general(
            moe_low.astype(jnp.float32),
            logit_grad,
            (((0,), (0,)), ((), ())),
            precision=highest_precision,
        )
        moe_grad = moe_grad + lax.dot_general(
            logit_grad, router_wide, (((1,), (1,)), ((), ())), precision=highest_precision
        )
        middle_part, gain_moe_part = moe_pull(moe_grad)
        gain_moe_acc = gain_moe_acc + gain_moe_part
        middle_grad = grad_block + lax.psum(middle_part.astype(jnp.bfloat16), "tp").astype(
            jnp.float32
        )
        middle_low = middle_grad.astype(jnp.bfloat16)
        gathered_back = gather_weights(w_query, key_weight, value_weight, w_out)
        out_acc = out_acc + dot_first(middle_low, heads_low)
        heads_grad = jnp.dot(middle_low, gathered_back[3], preferred_element_type=jnp.float32)
        grad_low = to_heads(
            heads_grad.reshape(micro_rows, query_local, head_width).astype(jnp.bfloat16),
            kv_local,
            group_width,
        )
        query_side, key_side_all, value_side_all = attend_backward(
            queries,
            keys_all,
            values_all,
            row_index,
            row_start,
            block_keys,
            head_out,
            log_total,
            grad_low,
        )
        key_side, value_side = (
            lax.psum_scatter(
                key_side_all.astype(jnp.bfloat16), "fsdp", scatter_dimension=0, tiled=True
            ).astype(jnp.float32),
            lax.psum_scatter(
                value_side_all.astype(jnp.bfloat16), "fsdp", scatter_dimension=0, tiled=True
            ).astype(jnp.float32),
        )
        query_pre_grad, key_pre_grad, gain_query_part, gain_key_part = heads_pull(
            (
                to_tokens(query_side, group_width).reshape(micro_rows, query_local, head_width),
                key_side.reshape(micro_rows, kv_local, head_width),
            )
        )
        gain_query_acc = gain_query_acc + gain_query_part
        gain_key_acc = gain_key_acc + gain_key_part
        query_pre_low = query_pre_grad.astype(jnp.bfloat16)
        key_pre_low = key_pre_grad.astype(jnp.bfloat16)
        value_pre_low = value_side.astype(jnp.bfloat16)
        query_acc = query_acc + dot_first(normed_reduced, query_pre_low)
        key_acc = key_acc + dot_first(normed_reduced, key_pre_low)
        value_acc = value_acc + dot_first(normed_reduced, value_pre_low)
        normed_grad = (
            dot_last(query_pre_low, gathered_back[0])
            + dot_last(key_pre_low, gathered_back[1])
            + dot_last(value_pre_low, gathered_back[2])
        )
        token_part, gain_attn_part = norm_pull(normed_grad)
        gain_attn_acc = gain_attn_acc + gain_attn_part
        token_share = lax.psum_scatter(
            token_part.astype(jnp.bfloat16), "tp", scatter_dimension=1, tiled=True
        ).astype(jnp.float32)
        grad_slice = lax.dynamic_slice_in_dim(
            middle_grad, group_index * slice_width, slice_width, 1
        )
        grad_parts.append((grad_slice + token_share).astype(jnp.bfloat16))
    weight_sums = (
        lax.psum_scatter(
            query_acc.astype(jnp.bfloat16), "fsdp", scatter_dimension=0, tiled=True
        ).astype(jnp.float32),
        lax.psum_scatter(
            key_acc.astype(jnp.bfloat16), "fsdp", scatter_dimension=0, tiled=True
        ).astype(jnp.float32),
        lax.psum_scatter(
            value_acc.astype(jnp.bfloat16), "fsdp", scatter_dimension=0, tiled=True
        ).astype(jnp.float32),
        lax.psum_scatter(
            out_acc.astype(jnp.bfloat16), "fsdp", scatter_dimension=0, tiled=True
        ).astype(jnp.float32),
    )
    small_sums = lax.psum(
        (gain_attn_acc, gain_query_acc, gain_key_acc, gain_moe_acc, router_acc), ("fsdp", "tp")
    )
    return (
        jnp.concatenate(out_parts, axis=0),
        jnp.concatenate(grad_parts, axis=0),
        small_sums[0],
        weight_sums[0],
        weight_sums[1],
        weight_sums[2],
        weight_sums[3],
        small_sums[1],
        small_sums[2],
        small_sums[3],
        small_sums[4],
        gate_acc[None],
        up_acc[None],
        down_acc[None],
    )


MESH = pl.DeviceIdType.MESH


def place():
    f = lax.axis_index("fsdp")
    t = lax.axis_index("tp")
    return f // 2, f % 2, t // 2, t % 2


def device(z, x, y, c):
    return (z * 2 + x, y * 2 + c)


def greet(devices):
    barrier = pltpu.get_barrier_semaphore()
    total = 0
    for valid, where in devices:
        if valid is None:
            pl.semaphore_signal(barrier, inc=1, device_id=where, device_id_type=MESH)
            total = total + 1
        else:
            @pl.when(valid)
            def _():
                pl.semaphore_signal(barrier, inc=1, device_id=where, device_id_type=MESH)
            total = total + valid.astype(jnp.int32)
    pl.semaphore_wait(barrier, total)


def remote(src, dst, send, recv, where):
    return pltpu.make_async_remote_copy(
        src_ref=src, dst_ref=dst, send_sem=send, recv_sem=recv, device_id=where, device_id_type=MESH
    )


def gather_all_kernel(nz, x_ref, o_ref, lsem, s_p, s_u, s_d, s_x, s_y, s_dx, s_dy,
                      r_z, r_x, r_y, r_dx, r_dy, r_p):
    z, x, y, c = place()
    rows, cols = x_ref.shape
    half = rows // 2
    partner = device(z, x, y, 1 - c)
    xn = device(z, 1 - x, y, c)
    yn = device(z, x, 1 - y, c)
    up = device(z + 1, x, y, c)
    down = device(z - 1, x, y, c)
    greet([(None, partner), (None, xn), (None, yn), (z < nz - 1, up), (z > 0, down)])

    def block(zz, xx, yy, cc, part=None):
        start = (zz * 2 + xx) * rows
        size = rows
        if part is not None:
            start = start + part * half
            size = half
        return o_ref.at[pl.ds(pl.multiple_of(start, half), size),
                        pl.ds(pl.multiple_of((yy * 2 + cc) * cols, cols), cols)]

    own = pltpu.make_async_copy(x_ref, block(z, x, y, c), lsem)
    own.start()

    items = [(0, 0)]
    for dist in range(1, nz):
        items += [(dist, -1), (dist, 1)]

    def guard(item, fn):
        dist, side = item
        zz = z + side * dist
        if dist == 0:
            fn(zz)
        else:
            pl.when((zz >= 0) & (zz < nz))(lambda: fn(zz))

    def c_z(zz, src):
        dst = block(zz, x, y, c)
        return (remote(src, dst, s_u.at[zz], r_z.at[zz], up),
                remote(src, dst, s_d.at[zz], r_z.at[zz], down))

    def c_xy(zz, src):
        dst = block(zz, x, y, c)
        return (remote(src, dst, s_x.at[zz], r_x.at[zz], xn),
                remote(src, dst, s_y.at[zz], r_y.at[zz], yn))

    def c_p(zz, rel, src=None):
        xx = 1 - x if rel in (1, 3, 4) else x
        yy = 1 - y if rel in (2, 3, 4) else y
        part = {3: 0, 4: 1}.get(rel)
        dst = block(zz, xx, yy, c, part)
        k = zz * 5 + rel
        return remote(dst if src is None else src, dst, s_p.at[k], r_p.at[k], partner)

    def w_p(zz, rel):
        xx = 1 - x if rel in (1, 3, 4) else x
        yy = 1 - y if rel in (2, 3, 4) else y
        part = {3: 0, 4: 1}.get(rel)
        dst = block(zz, xx, yy, 1 - c, part)
        k = zz * 5 + rel
        return remote(dst, dst, s_p.at[k], r_p.at[k], partner)

    def c_diag(zz):
        a = block(zz, 1 - x, y, c, 0)
        b = block(zz, x, 1 - y, c, 1)
        return (remote(a, a, s_dy.at[zz], r_dy.at[zz], yn),
                remote(b, b, s_dx.at[zz], r_dx.at[zz], xn))

    def stage_a(item):
        dist, side = item

        def run(zz):
            src = x_ref if dist == 0 else block(zz, x, y, c)
            cu, cd = c_z(zz, src)
            if dist:
                cu.wait_recv()
            if side <= 0:
                pl.when(z < nz - 1)(cu.start)
            if dist == 0 or side > 0:
                pl.when(z > 0)(cd.start)
            for cc in c_xy(zz, src):
                cc.start()
            c_p(zz, 0, src).start()

        guard(item, run)

    def stage_b(item):
        def run(zz):
            cx, cy = c_xy(zz, block(zz, x, y, c))
            dy, dx = c_diag(zz)
            cx.wait_recv()
            dy.start()
            c_p(zz, 1).start()
            cy.wait_recv()
            dx.start()
            c_p(zz, 2).start()

        guard(item, run)

    def stage_c(item):
        def run(zz):
            dy, dx = c_diag(zz)
            dy.wait_recv()
            c_p(zz, 3).start()
            dx.wait_recv()
            c_p(zz, 4).start()

        guard(item, run)

    count = len(items)
    for k in range(count + 2):
        if k < count:
            stage_a(items[k])
        if 0 <= k - 1 < count:
            stage_b(items[k - 1])
        if 0 <= k - 2 < count:
            stage_c(items[k - 2])

    def finish(zz, carry):
        for rel in range(5):
            w_p(zz, rel).wait_recv()
            c_p(zz, rel).wait_send()
        cu, cd = c_z(zz, block(zz, x, y, c))
        pl.when((zz <= z) & (z < nz - 1))(cu.wait_send)
        pl.when((zz >= z) & (z > 0))(cd.wait_send)
        for cc in c_xy(zz, block(zz, x, y, c)) + c_diag(zz):
            cc.wait_send()
        return carry

    lax.fori_loop(0, nz, finish, 0)
    own.wait()


def gather_all(block, nz, collective_id):
    rows, cols = block.shape
    dma = pltpu.SemaphoreType.DMA
    return pl.pallas_call(
        functools.partial(gather_all_kernel, nz),
        out_shape=jax.ShapeDtypeStruct((rows * nz * 2, cols * 4), block.dtype),
        in_specs=[pl.BlockSpec(memory_space=pl.ANY)],
        out_specs=pl.BlockSpec(memory_space=pl.ANY),
        scratch_shapes=[dma] + [dma((5 * nz,))] + [dma((nz,))] * 6 + [dma((nz,))] * 5 + [dma((5 * nz,))],
        compiler_params=pltpu.CompilerParams(collective_id=collective_id, has_side_effects=True),
        name="gather_all",
    )(block)


def scatter_all_kernel(nz, p_ref, o_ref, w, lp, rx, rxd, ry, ryd, rz,
                       s_l, s_p, r_p, s_x, s_y, s_dx, s_dy, s_z, r_x, r_y, r_dx, r_dy, r_z):
    z, x, y, c = place()
    rows, cols = o_ref.shape
    half = rows // 2
    partner = device(z, x, y, 1 - c)
    xn = device(z, 1 - x, y, c)
    yn = device(z, x, 1 - y, c)
    up = device(z + 1, x, y, c)
    down = device(z - 1, x, y, c)
    greet([(None, partner), (None, xn), (None, yn), (z < nz - 1, up), (z > 0, down)])
    chunk = 64

    def block(zz, rel, cc):
        xx = 1 - x if rel in (1, 3) else x
        yy = 1 - y if rel in (2, 3) else y
        return p_ref.at[pl.ds(pl.multiple_of((zz * 2 + xx) * rows, rows), rows),
                        pl.ds(pl.multiple_of((yy * 2 + cc) * cols, cols), cols)]

    items = []
    for dist in range(nz - 1, 0, -1):
        items += [(dist, -1), (dist, 1)]
    items += [(0, 0)]

    def guard(item, fn):
        dist, side = item
        zz = z + side * dist
        if dist == 0:
            fn(zz)
        else:
            pl.when((zz >= 0) & (zz < nz))(lambda: fn(zz))

    def c_p(zz, rel):
        k = zz * 4 + rel
        return remote(block(zz, rel, 1 - c), lp.at[zz, rel], s_p.at[k], r_p.at[k], partner)

    def c_l(zz, rel):
        return pltpu.make_async_copy(block(zz, rel, c), w.at[zz, rel], s_l.at[zz * 4 + rel])

    def c_diag(zz):
        return (remote(w.at[zz, 3, pl.ds(0, half)], rxd.at[zz], s_dx.at[zz], r_dx.at[zz], xn),
                remote(w.at[zz, 3, pl.ds(half, half)], ryd.at[zz], s_dy.at[zz], r_dy.at[zz], yn))

    def c_xy(zz):
        return (remote(w.at[zz, 1], rx.at[zz], s_x.at[zz], r_x.at[zz], xn),
                remote(w.at[zz, 2], ry.at[zz], s_y.at[zz], r_y.at[zz], yn))

    def c_z(zz, slot, where):
        return remote(w.at[zz, 0], rz.at[slot], s_z.at[zz], r_z.at[slot], where)

    def add(dst, srcs, start, count):
        def step(i, carry):
            off = pl.multiple_of(i * chunk, chunk)
            here = pl.ds(pl.multiple_of(start + off, chunk), chunk)
            total = dst[here, :].astype(jnp.float32)
            for src in srcs:
                total = total + src[pl.ds(off, chunk), :].astype(jnp.float32)
            dst[here, :] = total.astype(dst.dtype)
            return carry
        lax.fori_loop(0, count // chunk, step, 0)

    def stage_0(item):
        def run(zz):
            for rel in (3, 1, 2, 0):
                c_p(zz, rel).start()
                c_l(zz, rel).start()
        guard(item, run)

    def stage_d(item):
        def run(zz):
            for rel in (3, 1, 2, 0):
                c_p(zz, rel).wait_recv()
                c_l(zz, rel).wait()
                add(w.at[zz, rel], [lp.at[zz, rel]], 0, rows)
                if rel == 3:
                    for cc in c_diag(zz):
                        cc.start()
        guard(item, run)

    def stage_e(item):
        def run(zz):
            dx, dy = c_diag(zz)
            cx, cy = c_xy(zz)
            dy.wait_recv()
            add(w.at[zz, 1], [ryd.at[zz]], half, half)
            cx.start()
            dx.wait_recv()
            add(w.at[zz, 2], [rxd.at[zz]], 0, half)
            cy.start()
        guard(item, run)

    def stage_f(item):
        dist, side = item

        def run(zz):
            cx, cy = c_xy(zz)
            cx.wait_recv()
            cy.wait_recv()
            if dist:
                add(w.at[zz, 0], [rx.at[zz], ry.at[zz]], 0, rows)
                has = z > 0 if side > 0 else z < nz - 1
                cz = c_z(zz, zz, up if side > 0 else down)

                @pl.when(has)
                def _():
                    cz.wait_recv()
                    add(w.at[zz, 0], [rz.at[zz]], 0, rows)
                if side > 0:
                    cz.start()
                else:
                    if dist == 1:
                        c_z(zz, nz, down).start()
                    else:
                        cz.start()
            else:
                below, above = c_z(zz, zz, up), c_z(zz, nz, down)

                def total(refs):
                    def step(i, carry):
                        here = pl.ds(pl.multiple_of(i * chunk, chunk), chunk)
                        acc = w[zz, 0, here, :].astype(jnp.float32)
                        for ref in refs:
                            acc = acc + ref[here, :].astype(jnp.float32)
                        o_ref[here, :] = acc
                        return carry
                    lax.fori_loop(0, rows // chunk, step, 0)

                pl.when(z > 0)(below.wait_recv)
                pl.when(z < nz - 1)(above.wait_recv)
                pl.when(z == 0)(lambda: total([rx.at[zz], ry.at[zz], rz.at[nz]]))
                pl.when(z == nz - 1)(lambda: total([rx.at[zz], ry.at[zz], rz.at[zz]]))
                pl.when((z > 0) & (z < nz - 1))(
                    lambda: total([rx.at[zz], ry.at[zz], rz.at[zz], rz.at[nz]]))
        guard(item, run)

    for item in items:
        stage_0(item)
    count = len(items)
    for k in range(count + 2):
        if k < count:
            stage_d(items[k])
        if 0 <= k - 1 < count:
            stage_e(items[k - 1])
        if 0 <= k - 2 < count:
            stage_f(items[k - 2])

    def finish(zz, carry):
        for rel in range(4):
            c_p(zz, rel).wait_send()
        for cc in c_diag(zz) + c_xy(zz):
            cc.wait_send()
        pl.when(zz != z)(c_z(zz, zz, up).wait_send)
        return carry

    lax.fori_loop(0, nz, finish, 0)


def scatter_all(partial, nz, collective_id):
    rows, cols = partial.shape[0] // (2 * nz), partial.shape[1] // 4
    half = rows // 2
    dma = pltpu.SemaphoreType.DMA
    kind = partial.dtype
    vm = pltpu.VMEM
    return pl.pallas_call(
        functools.partial(scatter_all_kernel, nz),
        out_shape=jax.ShapeDtypeStruct((rows, cols), jnp.float32),
        in_specs=[pl.BlockSpec(memory_space=pl.ANY)],
        out_specs=pl.BlockSpec(memory_space=pltpu.VMEM),
        scratch_shapes=[vm((nz, 4, rows, cols), kind), vm((nz, 4, rows, cols), kind),
                        vm((nz, rows, cols), kind), vm((nz, half, cols), kind),
                        vm((nz, rows, cols), kind), vm((nz, half, cols), kind),
                        vm((nz + 1, rows, cols), kind)]
        + [dma((4 * nz,))] * 3 + [dma((nz,))] * 5 + [dma((nz,))] * 4 + [dma((nz + 1,))],
        compiler_params=pltpu.CompilerParams(collective_id=collective_id, has_side_effects=True,
                                             vmem_limit_bytes=62 << 20),
        name="scatter_all",
    )(partial)


def z_items(nz, near_first):
    items = [(0, 0)] if near_first else []
    order = range(1, nz) if near_first else range(nz - 1, 0, -1)
    for dist in order:
        items += [(dist, -1), (dist, 1)]
    return items if near_first else items + [(0, 0)]


def z_guard(item, z, nz, fn):
    dist, side = item
    zz = z + side * dist
    if dist == 0:
        fn(zz)
    else:
        pl.when((zz >= 0) & (zz < nz))(lambda: fn(zz))


def gather_rows_kernel(nz, count, columns, *refs):
    total = count + columns
    srcs, refs = refs[:total], refs[total:]
    outs, refs = refs[:total], refs[total:]
    wide, refs = refs[: min(columns, 1)], refs[min(columns, 1) :]
    lsem, s_u, s_d, s_x, r_z, r_x, s_c, r_c, s_w, r_w = refs
    z, x, y, c = place()
    xn, up, down = device(z, 1 - x, y, c), device(z + 1, x, y, c), device(z - 1, x, y, c)
    partner, yn = device(z, x, y, 1 - c), device(z, x, 1 - y, c)
    wanted = [(None, xn), (z < nz - 1, up), (z > 0, down)]
    greet(wanted + [(None, partner), (None, yn), (None, device(nz - 1 - z, x, y, c))] * min(columns, 1))

    def block(n, zz, xx):
        rows = srcs[n].shape[0]
        return outs[n].at[pl.ds(pl.multiple_of((zz * 2 + xx) * rows, rows), rows)]

    own = [(srcs[n], block(n, z, x)) for n in range(count)]
    column_copies, swaps = [], []
    if columns:
        mirror = device(nz - 1 - z, x, y, c)
        first, out = outs[count], wide[0]
        rows, cols = first.shape
        top, bottom = pl.ds(0, rows // 2), pl.ds(rows // 2, rows // 2)
        for n in range(columns):
            src, dst = srcs[count + n], outs[count + n]
            swaps.append(remote(src.at[bottom], dst.at[bottom], s_w.at[n], r_w.at[n], mirror))
            dst[top, :] = src[top, :]

        def column(yy):
            return out.at[:, pl.ds(pl.multiple_of((yy * 2 + c) * cols, cols), cols)]

        column_copies = [
            remote(first, column(y), s_c.at[0], r_c.at[0], yn),
            remote(first, column(y), s_c.at[1], r_c.at[1], partner),
            remote(column(1 - y), column(1 - y), s_c.at[2], r_c.at[2], partner),
        ]
        last = pltpu.make_async_copy(first, column(y), lsem.at[total])
    own = [pltpu.make_async_copy(src, dst, lsem.at[n]) for n, (src, dst) in enumerate(own)]
    for copy in swaps + own:
        copy.start()

    def copies(n, zz, src):
        dst = block(n, zz, x)
        k = n * nz + zz
        return (remote(src, dst, s_u.at[k], r_z.at[k], up),
                remote(src, dst, s_d.at[k], r_z.at[k], down),
                remote(src, dst, s_x.at[k], r_x.at[k], xn))

    items = z_items(nz, True)
    for item in items:
        dist, side = item

        def run(zz):
            for n in range(count):
                src = srcs[n] if dist == 0 else block(n, zz, x)
                cu, cd, cx = copies(n, zz, src)
                if dist:
                    cu.wait_recv()
                if side <= 0:
                    pl.when(z < nz - 1)(cu.start)
                if side > 0 or dist == 0:
                    pl.when(z > 0)(cd.start)
                cx.start()

        z_guard(item, z, nz, run)
        if columns and item == items[-1]:
            swaps[0].wait_recv()
            column_copies[0].start()
            column_copies[1].start()
            last.start()
        if columns and item == items[-1]:
            column_copies[0].wait_recv()
            column_copies[2].start()

    def finish(zz, carry):
        for n in range(count):
            cu, cd, cx = copies(n, zz, block(n, zz, x))
            cx.wait_recv()
            cx.wait_send()
            pl.when((zz <= z) & (z < nz - 1))(cu.wait_send)
            pl.when((zz >= z) & (z > 0))(cd.wait_send)
        return carry

    lax.fori_loop(0, nz, finish, 0)
    for copy in own:
        copy.wait()
    if columns:
        column_copies[0].wait_send()
        column_copies[1].wait()
        column_copies[2].wait()
        last.wait()
        swaps[0].wait_send()
        for copy in swaps[1:]:
            copy.wait()


def gather_rows(blocks, nz, collective_id, swapped=()):
    count, columns = len(blocks), len(swapped)
    dma = pltpu.SemaphoreType.DMA
    any_space = pl.BlockSpec(memory_space=pl.ANY)
    vmem = pl.BlockSpec(memory_space=pltpu.VMEM)
    shapes = [
        jax.ShapeDtypeStruct((b.shape[0] * nz * 2,) + b.shape[1:], b.dtype) for b in blocks
    ] + [jax.ShapeDtypeStruct(b.shape, b.dtype) for b in swapped]
    if columns:
        rows, cols = swapped[0].shape
        shapes.append(jax.ShapeDtypeStruct((rows, cols * 4), swapped[0].dtype))
    total = count + columns
    return pl.pallas_call(
        functools.partial(gather_rows_kernel, nz, count, columns),
        out_shape=shapes,
        in_specs=[vmem] * total,
        out_specs=[any_space] * count + [vmem] * columns + [any_space] * min(columns, 1),
        scratch_shapes=[dma((total + 1,))] + [dma((count * nz,))] * 5 + [dma((3,))] * 2
        + [dma((max(columns, 1),))] * 2,
        compiler_params=pltpu.CompilerParams(collective_id=collective_id, has_side_effects=True,
                                             vmem_limit_bytes=62 << 20),
        name="gather_rows",
    )(*blocks, *swapped)


def swap_back_kernel(nz, *refs):
    count = (len(refs) - 2) // 2
    srcs, outs = refs[:count], refs[count : 2 * count]
    s, r = refs[2 * count :]
    z, x, y, c = place()
    mirror = device(nz - 1 - z, x, y, c)
    greet([(None, mirror)])
    copies = [remote(src, out, s.at[n], r.at[n], mirror)
              for n, (src, out) in enumerate(zip(srcs, outs))]
    for copy in copies:
        copy.start()
    for copy in copies:
        copy.wait()


def swap_back(blocks, nz, collective_id):
    count = len(blocks)
    dma = pltpu.SemaphoreType.DMA
    any_space = pl.BlockSpec(memory_space=pl.ANY)
    return pl.pallas_call(
        functools.partial(swap_back_kernel, nz),
        out_shape=[jax.ShapeDtypeStruct(b.shape, b.dtype) for b in blocks],
        in_specs=[any_space] * count,
        out_specs=[any_space] * count,
        scratch_shapes=[dma((count,))] * 2,
        compiler_params=pltpu.CompilerParams(collective_id=collective_id, has_side_effects=True),
        name="swap_back",
    )(*blocks)


def add_blocks(dst, srcs, start, count, out=None, chunk=64):
    target = dst if out is None else out

    def step(i, carry):
        off = pl.multiple_of(i * chunk, chunk)
        here = pl.ds(pl.multiple_of(start + off, chunk), chunk)
        total = dst[here, :].astype(jnp.float32)
        for src in srcs:
            total = total + src[pl.ds(off, chunk), :].astype(jnp.float32)
        target[here, :] = total.astype(target.dtype)
        return carry

    lax.fori_loop(0, count // chunk, step, 0)


def reduce_rows_kernel(nz, p_ref, o_ref, w, rx, rz, s_l, s_x, s_z, r_x, r_z):
    z, x, y, c = place()
    rows = o_ref.shape[0]
    xn, up, down = device(z, 1 - x, y, c), device(z + 1, x, y, c), device(z - 1, x, y, c)
    greet([(None, xn), (z < nz - 1, up), (z > 0, down)])

    def block(zz, xx):
        return p_ref.at[pl.ds(pl.multiple_of((zz * 2 + xx) * rows, rows), rows)]

    def c_x(zz):
        return remote(block(zz, 1 - x), rx.at[zz], s_x.at[zz], r_x.at[zz], xn)

    def c_l(zz):
        return pltpu.make_async_copy(block(zz, x), w.at[zz], s_l.at[zz])

    def c_z(zz, slot, where):
        return remote(w.at[zz], rz.at[slot], s_z.at[zz], r_z.at[slot], where)

    items = z_items(nz, False)

    def start(zz):
        c_x(zz).start()
        c_l(zz).start()

    for item in items:
        z_guard(item, z, nz, start)
    for item in items:
        dist, side = item

        def run(zz):
            c_l(zz).wait()
            c_x(zz).wait_recv()
            if dist:
                add_blocks(w.at[zz], [rx.at[zz]], 0, rows)
                cz = c_z(zz, zz, up if side > 0 else down)

                @pl.when(z > 0 if side > 0 else z < nz - 1)
                def _():
                    cz.wait_recv()
                    add_blocks(w.at[zz], [rz.at[zz]], 0, rows)

                (c_z(zz, nz, down) if side < 0 and dist == 1 else cz).start()
            else:
                pl.when(z > 0)(c_z(zz, zz, up).wait_recv)
                pl.when(z < nz - 1)(c_z(zz, nz, down).wait_recv)
                low, high = rz.at[zz], rz.at[nz]
                pl.when(z == 0)(lambda: add_blocks(w.at[zz], [rx.at[zz], high], 0, rows, o_ref))
                pl.when(z == nz - 1)(lambda: add_blocks(w.at[zz], [rx.at[zz], low], 0, rows, o_ref))
                pl.when((z > 0) & (z < nz - 1))(
                    lambda: add_blocks(w.at[zz], [rx.at[zz], low, high], 0, rows, o_ref)
                )

        z_guard(item, z, nz, run)

    def finish(zz, carry):
        c_x(zz).wait_send()
        pl.when(zz != z)(c_z(zz, zz, up).wait_send)
        return carry

    lax.fori_loop(0, nz, finish, 0)


def reduce_rows(partial, nz, collective_id):
    rows, cols = partial.shape[0] // (2 * nz), partial.shape[1]
    dma, vm, kind = pltpu.SemaphoreType.DMA, pltpu.VMEM, partial.dtype
    return pl.pallas_call(
        functools.partial(reduce_rows_kernel, nz),
        out_shape=jax.ShapeDtypeStruct((rows, cols), jnp.float32),
        in_specs=[pl.BlockSpec(memory_space=pl.ANY)],
        out_specs=pl.BlockSpec(memory_space=pltpu.VMEM),
        scratch_shapes=[vm((nz, rows, cols), kind), vm((nz, rows, cols), kind),
                        vm((nz + 1, rows, cols), kind)]
        + [dma((nz,))] * 4 + [dma((nz + 1,))],
        compiler_params=pltpu.CompilerParams(
            collective_id=collective_id, has_side_effects=True, vmem_limit_bytes=62 << 20
        ),
        name="reduce_rows",
    )(partial)


def gather_cols_kernel(x_ref, o_ref, lsem, s_p, s_y, r_p, r_y):
    z, x, y, c = place()
    cols = x_ref.shape[1]
    partner, yn = device(z, x, y, 1 - c), device(z, x, 1 - y, c)
    greet([(None, partner), (None, yn)])

    def block(yy, cc):
        return o_ref.at[:, pl.ds(pl.multiple_of((yy * 2 + cc) * cols, cols), cols)]

    own = pltpu.make_async_copy(x_ref, block(y, c), lsem)
    cy = remote(x_ref, block(y, c), s_y, r_y, yn)
    cp = remote(x_ref, block(y, c), s_p.at[0], r_p.at[0], partner)
    cf = remote(block(1 - y, c), block(1 - y, c), s_p.at[1], r_p.at[1], partner)
    cy.start()
    cp.start()
    own.start()
    cy.wait_recv()
    cf.start()
    cp.wait()
    cf.wait()
    cy.wait_send()
    own.wait()


def gather_cols(block, collective_id):
    dma = pltpu.SemaphoreType.DMA
    any_space = pl.BlockSpec(memory_space=pl.ANY)
    return pl.pallas_call(
        gather_cols_kernel,
        out_shape=jax.ShapeDtypeStruct((block.shape[0], block.shape[1] * 4), block.dtype),
        in_specs=[any_space],
        out_specs=any_space,
        scratch_shapes=[dma, dma((2,)), dma, dma((2,)), dma],
        compiler_params=pltpu.CompilerParams(collective_id=collective_id, has_side_effects=True),
        name="gather_cols",
    )(block)


def reduce_cols_kernel(p_ref, o_ref, w, rp, ry, s_l, s_p, s_y, r_p, r_y):
    z, x, y, c = place()
    rows, cols = o_ref.shape
    partner, yn = device(z, x, y, 1 - c), device(z, x, 1 - y, c)
    greet([(None, partner), (None, yn)])

    def block(yy, cc):
        return p_ref.at[:, pl.ds(pl.multiple_of((yy * 2 + cc) * cols, cols), cols)]

    sends = [remote(block(yy, 1 - c), rp.at[k], s_p.at[k], r_p.at[k], partner)
             for k, yy in enumerate((1 - y, y))]
    loads = [pltpu.make_async_copy(block(yy, c), w.at[k], s_l.at[k])
             for k, yy in enumerate((1 - y, y))]
    cy = remote(w.at[0], ry, s_y, r_y, yn)
    for k in range(2):
        sends[k].start()
        loads[k].start()
    loads[0].wait()
    sends[0].wait_recv()
    add_blocks(w.at[0], [rp.at[0]], 0, rows)
    cy.start()
    loads[1].wait()
    sends[1].wait_recv()
    cy.wait_recv()
    add_blocks(w.at[1], [rp.at[1], ry], 0, rows, o_ref)
    for k in range(2):
        sends[k].wait_send()
    cy.wait_send()


def reduce_cols(partial, collective_id):
    rows, cols = partial.shape[0], partial.shape[1] // 4
    dma, vm, kind = pltpu.SemaphoreType.DMA, pltpu.VMEM, partial.dtype
    return pl.pallas_call(
        reduce_cols_kernel,
        out_shape=jax.ShapeDtypeStruct((rows, cols), jnp.float32),
        in_specs=[pl.BlockSpec(memory_space=pl.ANY)],
        out_specs=pl.BlockSpec(memory_space=pltpu.VMEM),
        scratch_shapes=[vm((2, rows, cols), kind), vm((2, rows, cols), kind), vm((rows, cols), kind),
                        dma((2,)), dma((2,)), dma, dma((2,)), dma],
        compiler_params=pltpu.CompilerParams(
            collective_id=collective_id, has_side_effects=True, vmem_limit_bytes=62 << 20
        ),
        name="reduce_cols",
    )(partial)


def sum_cols_kernel(v_ref, o_ref, got, s, r):
    group = lax.axis_index("tp")
    shard = lax.axis_index("fsdp")
    peers = [(shard, (group + k) % 4) for k in range(1, 4)]
    greet([(None, peer) for peer in peers])
    copies = [remote(v_ref, got.at[k], s.at[k], r.at[k], peer) for k, peer in enumerate(peers)]
    for copy in copies:
        copy.start()
    for copy in copies:
        copy.wait()
    o_ref[...] = v_ref[...] + got[0] + got[1] + got[2]


def sum_cols(vector, collective_id):
    dma = pltpu.SemaphoreType.DMA
    shape = vector.shape
    return pl.pallas_call(
        sum_cols_kernel,
        out_shape=jax.ShapeDtypeStruct(shape, jnp.float32),
        in_specs=[pl.BlockSpec(memory_space=pltpu.VMEM)],
        out_specs=pl.BlockSpec(memory_space=pltpu.VMEM),
        scratch_shapes=[pltpu.VMEM((3,) + shape, jnp.float32), dma((3,)), dma((3,))],
        compiler_params=pltpu.CompilerParams(collective_id=collective_id, has_side_effects=True),
        name="sum_cols",
    )(vector)


def greet_all(shard, group, shards, groups):
    barrier = pltpu.get_barrier_semaphore()
    total = shards * groups

    def step(k, carry):
        other = (shard * groups + group + k) % total
        pl.semaphore_signal(
            barrier, inc=1, device_id=(other // groups, other % groups), device_id_type=MESH
        )
        return carry

    lax.fori_loop(1, total, step, 0)
    pl.semaphore_wait(barrier, total - 1)


def swap_rows_kernel(shards, groups, v_ref, o_ref, s, r):
    shard, group = lax.axis_index("fsdp"), lax.axis_index("tp")
    total = shards * groups
    me = shard * groups + group
    greet_all(shard, group, shards, groups)

    def copy(k):
        other = (me + k) % total
        return remote(v_ref.at[other // groups], o_ref.at[me], s.at[k], r.at[k],
                      (other // groups, other % groups))

    def start(k, carry):
        copy(k).start()
        return carry

    def wait(k, carry):
        copy(k).wait()
        return carry

    lax.fori_loop(1, total, start, 0)
    o_ref[me] = v_ref[shard]
    lax.fori_loop(1, total, wait, 0)


def swap_rows(values, shards, groups, collective_id):
    dma, total = pltpu.SemaphoreType.DMA, shards * groups
    return pl.pallas_call(
        functools.partial(swap_rows_kernel, shards, groups),
        out_shape=jax.ShapeDtypeStruct((total,) + values.shape[1:], values.dtype),
        in_specs=[pl.BlockSpec(memory_space=pltpu.VMEM)],
        out_specs=pl.BlockSpec(memory_space=pltpu.VMEM),
        scratch_shapes=[dma((total,)), dma((total,))],
        compiler_params=pltpu.CompilerParams(collective_id=collective_id, has_side_effects=True),
        name="swap_rows",
    )(values)


def sum_small_kernel(shards, groups, v_ref, o_ref, got, s1, r1, s2, r2):
    shard, group = lax.axis_index("fsdp"), lax.axis_index("tp")
    total = shards * groups
    me = shard * groups + group
    greet_all(shard, group, shards, groups)

    def first(k):
        other = (shard + k) % shards
        return remote(v_ref.at[other], got.at[k], s1.at[k], r1.at[k], (other, group))

    def second(k):
        other = (me + k) % total
        return remote(o_ref.at[me], o_ref.at[me], s2.at[k], r2.at[k],
                      (other // groups, other % groups))

    for k in range(1, shards):
        first(k).start()
    acc = v_ref[shard]
    for k in range(1, shards):
        first(k).wait()
        acc = acc + got[k]
    o_ref[me] = acc

    def start(k, carry):
        second(k).start()
        return carry

    def wait(k, carry):
        second(k).wait()
        return carry

    lax.fori_loop(1, total, start, 0)
    lax.fori_loop(1, total, wait, 0)


def sum_small(values, shards, groups, collective_id):
    dma, total = pltpu.SemaphoreType.DMA, shards * groups
    part = values.shape[1:]
    return pl.pallas_call(
        functools.partial(sum_small_kernel, shards, groups),
        out_shape=jax.ShapeDtypeStruct((total,) + part, values.dtype),
        in_specs=[pl.BlockSpec(memory_space=pltpu.VMEM)],
        out_specs=pl.BlockSpec(memory_space=pltpu.VMEM),
        scratch_shapes=[pltpu.VMEM((shards,) + part, values.dtype), dma((shards,)), dma((shards,)),
                        dma((total,)), dma((total,))],
        compiler_params=pltpu.CompilerParams(collective_id=collective_id, has_side_effects=True),
        name="sum_small",
    )(values)


def dot_plain(left, right):
    return jnp.dot(left, right, preferred_element_type=jnp.float32)


def far_first(nz, z, k):
    at = 0
    for here in range(nz):
        order = sorted(range(nz), key=lambda other: (-abs(other - here), other))
        for step, other in enumerate(order):
            at = at + jnp.where((z == here) & (k == step), other, 0)
    return at


def expert_kernel(nz, slots, block_rows, x_all, g_all, routes_all, router_ref, wg, wu, wd,
                  out_all, back_ref, gg_got, gates_ref, xr_all, gs_all, hid_all, gp_all, up_all,
                  gg_ref, x_ref, g_ref, t_ref, o_ref, xr, gs, hid, gp, up, st,
                  w, lp, rx, rxd, ry, ryd, rz,
                  s_in, s_out, s_save, s_p, r_p, s_x, s_y, s_dx, s_dy, s_z, r_x, r_y, r_dx, r_dy, r_z,
                  s_g, r_g):
    z, x, y, c = place()
    shard, group = lax.axis_index("fsdp"), lax.axis_index("tp")
    expert = shard * 4 + group
    rows, cols = back_ref.shape
    width = x_ref.shape[1]
    half = rows // 2
    blocks = rows // block_rows
    experts = router_ref.shape[1]
    f32, low = jnp.float32, jnp.bfloat16
    partner = device(z, x, y, 1 - c)
    xn, yn = device(z, 1 - x, y, c), device(z, x, 1 - y, c)
    up_dev, down_dev = device(z + 1, x, y, c), device(z - 1, x, y, c)
    greet_all(shard, group, 2 * nz, 4)
    tiles = 2 * nz
    devices = 8 * nz

    def swap(k):
        other = (expert + k) % devices
        return remote(gg_ref.at[other // 4], gg_got.at[expert], s_g.at[k], r_g.at[k],
                      (other // 4, other % 4))

    def tile_of(j):
        return far_first(nz, z, j // 2) * 2 + jnp.where(j % 2 == 0, 1 - x, x)

    def tile_rows(j):
        return pl.ds(pl.multiple_of(tile_of(j) * rows, rows), rows)

    def load(j):
        return pltpu.make_async_copy(x_all.at[tile_rows(j)], x_ref, s_in.at[0])

    def load_g(j):
        tile = tile_of(j)
        first = pl.ds(pl.multiple_of(tile * rows, half), half)
        second = pl.ds(pl.multiple_of(mirrored(nz, tile) * rows + half, half), half)
        return (pltpu.make_async_copy(g_all.at[first], g_ref.at[pl.ds(0, half)], s_in.at[1]),
                pltpu.make_async_copy(g_all.at[second], g_ref.at[pl.ds(half, half)], s_in.at[3]))

    def load_t(j):
        tile = tile_of(j)
        first = pl.ds(pl.multiple_of(tile * rows, half), half)
        second = pl.ds(pl.multiple_of(mirrored(nz, tile) * rows + half, half), half)
        return (pltpu.make_async_copy(routes_all.at[first], t_ref.at[pl.ds(0, half)], s_in.at[2]),
                pltpu.make_async_copy(routes_all.at[second], t_ref.at[pl.ds(half, half)], s_in.at[4]))

    def save_out(j):
        return pltpu.make_async_copy(o_ref, out_all.at[tile_rows(j)], s_out)

    def saves(j):
        pairs = ((xr, xr_all), (gs, gs_all), (hid, hid_all), (gp, gp_all), (up, up_all))
        return [pltpu.make_async_copy(src, dst.at[j], s_save.at[n])
                for n, (src, dst) in enumerate(pairs)]

    def c_p(zz, rel, slot):
        k = zz * 4 + rel
        return remote(st.at[slot, rel // 2], lp.at[zz, rel], s_p.at[k], r_p.at[k], partner)

    def c_diag(zz):
        return (remote(w.at[zz, 3, pl.ds(0, half)], rxd.at[zz], s_dx.at[zz], r_dx.at[zz], xn),
                remote(w.at[zz, 3, pl.ds(half, half)], ryd.at[zz], s_dy.at[zz], r_dy.at[zz], yn))

    def c_xy(zz):
        return (remote(w.at[zz, 1], rx.at[zz], s_x.at[zz], r_x.at[zz], xn),
                remote(w.at[zz, 2], ry.at[zz], s_y.at[zz], r_y.at[zz], yn))

    def c_z(zz, slot, where):
        return remote(w.at[zz, 0], rz.at[slot], s_z.at[zz], r_z.at[slot], where)

    def send_z(zz):
        pl.when(zz > z)(lambda: c_z(zz, zz, up_dev).start())
        pl.when(zz == z - 1)(lambda: c_z(zz, nz, down_dev).start())
        pl.when(zz < z - 1)(lambda: c_z(zz, zz, down_dev).start())

    def stage_d(zz, rel, slot):
        c_p(zz, rel, slot).wait_recv()
        add_blocks(w.at[zz, rel], [lp.at[zz, rel]], 0, rows)
        if rel == 3:
            for copy in c_diag(zz):
                copy.start()

    def stage_e(zz):
        dx, dy = c_diag(zz)
        cx, cy = c_xy(zz)
        dy.wait_recv()
        add_blocks(w.at[zz, 1], [ryd.at[zz]], half, half)
        cx.start()
        dx.wait_recv()
        add_blocks(w.at[zz, 2], [rxd.at[zz]], 0, half)
        cy.start()

    def passes(zz):
        return ((zz > z) & (z > 0)) | ((zz < z) & (z < nz - 1))

    def stage_f1(zz):
        cx, cy = c_xy(zz)
        cx.wait_recv()
        cy.wait_recv()
        add_blocks(w.at[zz, 0], [rx.at[zz], ry.at[zz]], 0, rows)
        pl.when((zz != z) & jnp.logical_not(passes(zz)))(lambda: send_z(zz))

    def stage_f2(zz):
        @pl.when((zz != z) & passes(zz))
        def _():
            c_z(zz, zz, up_dev).wait_recv()
            add_blocks(w.at[zz, 0], [rz.at[zz]], 0, rows)
            send_z(zz)

        @pl.when(zz == z)
        def _():
            low_part, high_part = rz.at[zz], rz.at[nz]
            pl.when(z > 0)(lambda: c_z(zz, zz, up_dev).wait_recv())
            pl.when(z < nz - 1)(lambda: c_z(zz, nz, down_dev).wait_recv())
            own = w.at[zz, 0]
            pl.when(z == 0)(lambda: add_blocks(own, [high_part], 0, rows, back_ref))
            pl.when(z == nz - 1)(lambda: add_blocks(own, [low_part], 0, rows, back_ref))
            pl.when((z > 0) & (z < nz - 1))(
                lambda: add_blocks(own, [low_part, high_part], 0, rows, back_ref)
            )

    def compute(j):
        zz = far_first(nz, z, j // 2)
        slot = j % 2
        load(j).wait()
        for copy in load_t(j):
            copy.wait()
        lanes = lax.broadcasted_iota(jnp.int32, (rows, experts), 1)
        routes = t_ref[...]
        chosen = routes[:, 0:1] == lanes
        for n in range(1, TOPK):
            chosen = chosen | (routes[:, n : n + 1] == lanes)
        logits = jnp.where(chosen, dot_plain(x_ref[...], router_ref[...]), masked_score)
        peak = jnp.max(logits, axis=1, keepdims=True)
        weights = jnp.where(chosen, jnp.exp(logits - peak), 0.0)
        gates = weights / jnp.sum(weights, axis=1, keepdims=True)
        gates_ref[...] = gates
        mine = lanes == expert
        gate_col = jnp.sum(jnp.where(mine, gates, 0.0), axis=1, keepdims=True)
        match_col = jnp.sum(jnp.where(mine & chosen, 1.0, 0.0), axis=1, keepdims=True)
        sub = lax.broadcasted_iota(jnp.int32, (block_rows, block_rows), 0)
        lane = lax.broadcasted_iota(jnp.int32, (block_rows, block_rows), 1)
        eye = sub == lane
        before = (sub > lane).astype(f32).astype(low)
        chosen_low = chosen.astype(f32).astype(low)
        pick, put, slot_gate = [], [], []
        slot_lane = lax.broadcasted_iota(jnp.int32, (block_rows, slots), 1).astype(f32)
        slot_sub = lax.broadcasted_iota(jnp.int32, (slots, block_rows), 0).astype(f32)
        for b in range(blocks):
            part = slice(b * block_rows, (b + 1) * block_rows)
            ranks = dot_plain(before, chosen_low[part])
            rank = jnp.sum(jnp.where(mine[part], ranks, 0.0), axis=1, keepdims=True)
            rank = jnp.where(match_col[part] > 0.0, rank, -1.0)
            rank_row = jnp.sum(jnp.where(eye, rank, 0.0), axis=0, keepdims=True)
            gate_row = jnp.sum(jnp.where(eye, gate_col[part], 0.0), axis=0, keepdims=True)
            hot = rank_row == slot_sub
            pick.append(hot.astype(f32).astype(low))
            put.append((rank == slot_lane).astype(f32).astype(low))
            slot_gate.append(jnp.sum(jnp.where(hot, gate_row, 0.0), axis=1, keepdims=True))
        slot_gate = jnp.concatenate(slot_gate, axis=0)

        def gather(ref, at):
            return jnp.concatenate(
                [dot_plain(pick[b], ref[pl.ds(b * block_rows, block_rows), at])
                 for b in range(blocks)],
                axis=0,
            )

        def scatter(ref, at, values):
            for b in range(blocks):
                ref[pl.ds(b * block_rows, block_rows), at] = dot_plain(
                    put[b], values[b * slots : (b + 1) * slots]
                ).astype(low)

        def columns(i):
            return pl.ds(pl.multiple_of(i * cols, cols), cols)

        @pl.when(j > 0)
        def _():
            for copy in saves(j):
                copy.wait()

        def take(i, carry):
            xr[:, columns(i)] = gather(x_ref, columns(i)).astype(low)
            return carry

        lax.fori_loop(0, width // cols, take, 0)

        @pl.when(j < tiles - 1)
        def _():
            load(j + 1).start()
            for copy in load_t(j + 1):
                copy.start()

        gate_pre = dot_plain(xr[...], wg[...])
        up_pre = dot_plain(xr[...], wu[...])
        sig = jax.nn.sigmoid(gate_pre)
        silu = gate_pre * sig
        hidden_low = (silu * up_pre).astype(low)
        hid[...] = hidden_low
        for copy in load_g(j):
            copy.wait()
        pl.when(j > 0)(lambda: save_out(j).wait())

        def middle_part(i, carry):
            total, hidden_grad = carry
            at = columns(i)
            grad = gather(g_ref, at)
            expert_out = dot_plain(hidden_low, wd[:, at]).astype(low).astype(f32)
            total = total + jnp.sum(grad * expert_out, axis=1, keepdims=True)
            pair_grad = (grad * slot_gate).astype(low)
            gs[:, at] = pair_grad
            scatter(o_ref, at, (expert_out * slot_gate).astype(low))
            return total, hidden_grad + dot_last(pair_grad, wd[:, at])

        gates_grad, hidden_grad = lax.fori_loop(
            0,
            width // cols,
            middle_part,
            (jnp.zeros(slot_gate.shape, f32), jnp.zeros(gate_pre.shape, f32)),
        )
        save_out(j).start()

        @pl.when(j < tiles - 1)
        def _():
            for copy in load_g(j + 1):
                copy.start()

        for b in range(blocks):
            gg_ref[tile_of(j), :, pl.ds(b * block_rows, block_rows)] = jnp.sum(
                pick[b].astype(f32) * gates_grad[b * slots : (b + 1) * slots],
                axis=0,
                keepdims=True,
            )
        gate_grad = (hidden_grad * up_pre * (sig * (1.0 + gate_pre * (1.0 - sig)))).astype(low)
        up_grad = (hidden_grad * silu).astype(low)
        gp[...] = gate_grad
        up[...] = up_grad
        for copy in saves(j):
            copy.start()

        def part_of(i, yy, cc):
            at = columns(yy * 2 + cc)
            row_grad = dot_last(gate_grad, wg[at, :]) + dot_last(up_grad, wu[at, :])
            return row_grad.astype(low)

        first = jnp.where(slot == 0, 1, 0)

        def to_partner(i, carry):
            yy = jnp.where(i == 1, 1 - y, y)
            rel = first + 2 * i

            @pl.when(j >= 2)
            def _():
                before_zz = far_first(nz, z, j // 2 - 1)
                k = before_zz * 4 + rel
                remote(st.at[slot, i], lp.at[before_zz, rel], s_p.at[k], r_p.at[k], partner).wait_send()

            scatter(st.at[slot, i], slice(None), part_of(i, yy, 1 - c))
            k = zz * 4 + rel
            remote(st.at[slot, i], lp.at[zz, rel], s_p.at[k], r_p.at[k], partner).start()
            return carry

        def to_own(i, carry):
            yy = jnp.where(i == 1, 1 - y, y)
            scatter(w.at[zz, first + 2 * i], slice(None), part_of(i, yy, c))
            return carry

        lax.fori_loop(0, 2, to_partner, 0)
        lax.fori_loop(0, 2, to_own, 0)

    for copy in (load(0),) + load_t(0) + load_g(0):
        copy.start()

    def step(j, carry):
        k, odd = j // 2, j % 2 == 1
        pl.when(j < tiles)(lambda: compute(j))

        @pl.when(j == tiles)
        def _():
            gg_got[expert] = gg_ref[shard]
            loop_from_one(devices, lambda n: swap(n).start())

        @pl.when(odd & (k < nz))
        def _():
            zz = far_first(nz, z, k)
            stage_d(zz, 3, 0)
            stage_d(zz, 1, 0)

        @pl.when(jnp.logical_not(odd) & (k >= 1) & (k <= nz))
        def _():
            zz = far_first(nz, z, k - 1)
            stage_d(zz, 2, 1)
            stage_d(zz, 0, 1)
            stage_e(zz)

        @pl.when((k >= 2) & jnp.logical_not(odd))
        def _():
            stage_f1(far_first(nz, z, k - 2))

        @pl.when((k >= 2) & odd)
        def _():
            stage_f2(far_first(nz, z, k - 2))

        return carry

    lax.fori_loop(0, 2 * (nz + 2), step, 0)
    loop_from_one(devices, lambda n: swap(n).wait())
    save_out(tiles - 1).wait()
    for copy in saves(tiles - 1):
        copy.wait()
    for slot in range(2):
        for i in range(2):
            c_p(z, 1 - slot + 2 * i, slot).wait_send()

    def finish(zz, carry):
        for copy in c_diag(zz) + c_xy(zz):
            copy.wait_send()
        pl.when(zz != z)(c_z(zz, zz, up_dev).wait_send)
        return carry

    lax.fori_loop(0, nz, finish, 0)


def run_experts(x_all, g_all, routes_all, router, gate_w, up_w, down_w, block_rows, slots, nz,
                collective_id):
    total, width = x_all.shape
    hidden = gate_w.shape[1]
    experts = router.shape[1]
    tiles = 2 * nz
    rows, cols = total // tiles, width // 4
    pairs = rows // block_rows * slots
    half = rows // 2
    f32, low = jnp.float32, jnp.bfloat16
    any_space = pl.BlockSpec(memory_space=pl.ANY)
    vmem = pl.BlockSpec(memory_space=pltpu.VMEM)
    vm, dma, shape = pltpu.VMEM, pltpu.SemaphoreType.DMA, jax.ShapeDtypeStruct
    return pl.pallas_call(
        functools.partial(expert_kernel, nz, slots, block_rows),
        in_specs=[any_space] * 3 + [vmem] * 4,
        out_specs=[any_space, vmem, vmem, vmem] + [any_space] * 5,
        out_shape=[
            shape((total, width), low), shape((rows, cols), f32), shape((4 * tiles, 1, rows), f32),
            shape((rows, experts), f32),
            shape((tiles, pairs, width), low), shape((tiles, pairs, width), low),
            shape((tiles, pairs, hidden), low), shape((tiles, pairs, hidden), low),
            shape((tiles, pairs, hidden), low),
        ],
        scratch_shapes=[
            vm((tiles, 1, rows), f32), vm((rows, width), low), vm((rows, width), low),
            vm((rows, routes_all.shape[1]), jnp.int32), vm((rows, width), low),
            vm((pairs, width), low), vm((pairs, width), low),
            vm((pairs, hidden), low), vm((pairs, hidden), low), vm((pairs, hidden), low),
            vm((2, 2, rows, cols), low),
            vm((nz, 4, rows, cols), low), vm((nz, 4, rows, cols), low),
            vm((nz, rows, cols), low), vm((nz, half, cols), low),
            vm((nz, rows, cols), low), vm((nz, half, cols), low),
            vm((nz + 1, rows, cols), low),
            dma((5,)), dma, dma((5,)), dma((4 * nz,)), dma((4 * nz,)),
        ] + [dma((nz,))] * 9 + [dma((nz + 1,))] + [dma((4 * tiles,))] * 2,
        compiler_params=pltpu.CompilerParams(
            collective_id=collective_id, has_side_effects=True, vmem_limit_bytes=62 << 20
        ),
        name="experts",
    )(x_all, g_all, routes_all, router, gate_w, up_w, down_w)


def near_first(nz, z, k):
    return far_first(nz, z, nz - 1 - k)


class GatherAll:
    sems = 6

    @staticmethod
    def scratch(nz):
        dma = pltpu.SemaphoreType.DMA
        return [dma] + [dma((5 * nz,))] * 2 + [dma((nz,))] * 11

    def __init__(self, nz, src, out, sems, cut):
        (self.lsem, self.s_p, self.r_p, self.s_u, self.s_d, self.s_x, self.s_y, self.s_dx,
         self.s_dy, self.r_z, self.r_x, self.r_y, self.r_dx, self.r_dy) = sems
        self.nz, self.src, self.out, self.cut = nz, src, out, cut
        self.rows, self.cols = src.shape
        self.place = z, x, y, c = place()
        self.partner, self.xn, self.yn = (
            device(z, x, y, 1 - c), device(z, 1 - x, y, c), device(z, x, 1 - y, c))
        self.up, self.down = device(z + 1, x, y, c), device(z - 1, x, y, c)

    def block(self, zz, xx, yy, cc, part=None):
        start, size, unit = (zz * 2 + xx) * self.rows, self.rows, self.rows
        if part == 0:
            size, unit = self.cut, self.rows
        elif part == 1:
            start, size = start + self.cut, self.rows - self.cut
            unit = math.gcd(self.cut, self.rows)
        return self.out.at[pl.ds(pl.multiple_of(start, unit), size),
                           pl.ds(pl.multiple_of((yy * 2 + cc) * self.cols, self.cols), self.cols)]

    def own(self):
        z, x, y, c = self.place
        return pltpu.make_async_copy(self.src, self.block(z, x, y, c), self.lsem)

    def line(self, zz):
        z, x, y, c = self.place
        here = self.block(zz, x, y, c)
        return (remote(here, here, self.s_u.at[zz], self.r_z.at[zz], self.up),
                remote(here, here, self.s_d.at[zz], self.r_z.at[zz], self.down))

    def sides(self, zz):
        z, x, y, c = self.place
        here = self.block(zz, x, y, c)
        return (remote(here, here, self.s_x.at[zz], self.r_x.at[zz], self.xn),
                remote(here, here, self.s_y.at[zz], self.r_y.at[zz], self.yn))

    def across(self, zz):
        z, x, y, c = self.place
        copies = []
        if self.cut > 0:
            here = self.block(zz, 1 - x, y, c, 0)
            copies.append(remote(here, here, self.s_dy.at[zz], self.r_dy.at[zz], self.yn))
        if self.cut < self.rows:
            here = self.block(zz, x, 1 - y, c, 1)
            copies.append(remote(here, here, self.s_dx.at[zz], self.r_dx.at[zz], self.xn))
        return copies

    def pair(self, zz, rel, mine=True):
        z, x, y, c = self.place
        xx = 1 - x if rel in (1, 3, 4) else x
        yy = 1 - y if rel in (2, 3, 4) else y
        here = self.block(zz, xx, yy, c if mine else 1 - c, {3: 0, 4: 1}.get(rel))
        k = zz * 5 + rel
        return remote(here, here, self.s_p.at[k], self.r_p.at[k], self.partner)

    def parts(self):
        return [0, 1, 2] + [3] * (self.cut > 0) + [4] * (self.cut < self.rows)

    def first(self, k):
        zz, z = near_first(self.nz, self.place[0], k), self.place[0]
        up, down = self.line(zz)
        pl.when(k > 0)(lambda: up.wait_recv())
        pl.when((zz <= z) & (z < self.nz - 1))(lambda: up.start())
        pl.when((zz >= z) & (z > 0))(lambda: down.start())
        for copy in self.sides(zz):
            copy.start()
        self.pair(zz, 0).start()

    def second(self, k):
        zz = near_first(self.nz, self.place[0], k)
        to_x, to_y = self.sides(zz)
        across = self.across(zz)
        to_x.wait_recv()
        if self.cut > 0:
            across[0].start()
        self.pair(zz, 1).start()
        to_y.wait_recv()
        if self.cut < self.rows:
            across[-1].start()
        self.pair(zz, 2).start()

    def third(self, k):
        zz = near_first(self.nz, self.place[0], k)
        across = self.across(zz)
        for rel, copy in zip(self.parts()[3:], across):
            copy.wait_recv()
            self.pair(zz, rel).start()

    def finish(self):
        z = self.place[0]

        def step(zz, carry):
            for rel in self.parts():
                self.pair(zz, rel, False).wait_recv()
                self.pair(zz, rel).wait_send()
            up, down = self.line(zz)
            pl.when((zz <= z) & (z < self.nz - 1))(lambda: up.wait_send())
            pl.when((zz >= z) & (z > 0))(lambda: down.wait_send())
            for copy in tuple(self.sides(zz)) + tuple(self.across(zz)):
                copy.wait_send()
            return carry

        lax.fori_loop(0, self.nz, step, 0)


class GatherCausal:
    @staticmethod
    def scratch(nz):
        dma = pltpu.SemaphoreType.DMA
        return [dma, dma, dma((2,)), dma((2 * nz,)), dma((2 * nz,)), dma((2 * nz,))]

    def __init__(self, nz, src, out, held, sems):
        self.s_x, self.r_x, self.lsem, self.s_z, self.r_z, self.l_z = sems
        self.nz, self.src, self.out, self.held_ref = nz, src, out, held
        self.place = z, x, y, c = place()
        self.xn = device(z, 1 - x, y, c)
        self.near = (device(z + 1, x, y, c), device(z - 1, x, y, c))

    def own(self):
        z, x = self.place[:2]
        return [pltpu.make_async_copy(self.src, self.out.at[z, x], self.lsem.at[0]),
                pltpu.make_async_copy(self.src, self.held_ref.at[z, x], self.lsem.at[1])]

    def side(self):
        z, x = self.place[:2]
        return remote(self.src, self.out.at[z, x], self.s_x, self.r_x, self.xn)

    def line(self, zz, micro):
        here = self.out.at[zz, :, micro]
        return remote(here, here, self.s_z.at[zz * 2 + micro], self.r_z.at[zz * 2 + micro],
                      self.near[micro])

    def keep(self, zz, micro):
        return pltpu.make_async_copy(self.out.at[zz, :, micro], self.held_ref.at[zz, :, micro],
                                     self.l_z.at[zz * 2 + micro])

    def needed(self, zz, micro):
        return zz <= self.place[0] if micro == 0 else zz >= self.place[0]

    def sends(self, zz, micro):
        z = self.place[0]
        return self.needed(zz, micro) & (z < self.nz - 1 if micro == 0 else z > 0)

    def first(self, k):
        zz, z = near_first(self.nz, self.place[0], k), self.place[0]

        @pl.when(k == 0)
        def _():
            for copy in self.own():
                copy.wait()
            self.side().wait_recv()

        for micro in range(2):
            pl.when((k > 0) & self.needed(zz, micro))(lambda: self.line(zz, micro).wait_recv())
            pl.when(self.sends(zz, micro))(lambda: self.line(zz, micro).start())
            pl.when(self.needed(zz, micro))(lambda: self.keep(zz, micro).start())

    def ready(self, zz):
        for micro in range(2):
            pl.when(self.needed(zz, micro))(lambda: self.keep(zz, micro).wait())

    def finish(self):
        self.side().wait_send()

        def step(zz, carry):
            for micro in range(2):
                pl.when(self.sends(zz, micro))(lambda: self.line(zz, micro).wait_send())
            return carry

        lax.fori_loop(0, self.nz, step, 0)


class GatherRows:
    @staticmethod
    def scratch(nz):
        dma = pltpu.SemaphoreType.DMA
        return [dma] + [dma((nz,))] * 5

    def __init__(self, nz, src, out, sems):
        self.lsem, self.s_u, self.s_d, self.s_x, self.r_z, self.r_x = sems
        self.nz, self.src, self.out = nz, src, out
        self.place = z, x, y, c = place()
        self.xn = device(z, 1 - x, y, c)
        self.up, self.down = device(z + 1, x, y, c), device(z - 1, x, y, c)

    def block(self, zz):
        rows = self.src.shape[0]
        return self.out.at[pl.ds(pl.multiple_of((zz * 2 + self.place[1]) * rows, rows), rows)]

    def own(self):
        return pltpu.make_async_copy(self.src, self.block(self.place[0]), self.lsem)

    def copies(self, zz):
        here = self.block(zz)
        return (remote(here, here, self.s_u.at[zz], self.r_z.at[zz], self.up),
                remote(here, here, self.s_d.at[zz], self.r_z.at[zz], self.down),
                remote(here, here, self.s_x.at[zz], self.r_x.at[zz], self.xn))

    def first(self, k):
        zz, z = near_first(self.nz, self.place[0], k), self.place[0]
        up, down, to_x = self.copies(zz)
        pl.when(k > 0)(lambda: up.wait_recv())
        pl.when((zz <= z) & (z < self.nz - 1))(lambda: up.start())
        pl.when((zz >= z) & (z > 0))(lambda: down.start())
        to_x.start()

    def finish(self):
        z = self.place[0]

        def step(zz, carry):
            up, down, to_x = self.copies(zz)
            to_x.wait()
            pl.when((zz <= z) & (z < self.nz - 1))(lambda: up.wait_send())
            pl.when((zz >= z) & (z > 0))(lambda: down.wait_send())
            return carry

        lax.fori_loop(0, self.nz, step, 0)


def mirrored(nz, shard):
    return (nz - 1 - shard // 2) * 2 + shard % 2


def stream_unit(u, nz):
    shard = lax.axis_index("fsdp")
    later = u > shard
    micro = jnp.where(later, 1, 0)
    here = jnp.where(later, mirrored(nz, shard), shard)
    key_place = here - jnp.where(later, u - shard - 1, u)
    owner = jnp.where(later, mirrored(nz, key_place), key_place)
    return micro, here, key_place, owner


def key_bias(micro, here, key_place, block, start_ref):
    key = key_place * block + lax.broadcasted_iota(jnp.int32, (block, block), 0)
    query = here * block + lax.broadcasted_iota(jnp.int32, (block, block), 1)
    return jnp.where((key >= start_ref[micro]) & (key <= query), 0.0, masked_score)


def norm_turn(raw, gain, cosine, sine):
    scale = lax.rsqrt(jnp.mean(raw * raw, axis=1, keepdims=True) + norm_eps)
    normed = raw * scale * gain
    return normed * cosine + pltpu.roll(normed, raw.shape[1] // 2, 1) * sine


def attend_kernel(nz, q_pre, k_pre, v_pre, gq_ref, gk_ref, cos_ref, sin_ref, start_ref, cot_ref, wo_ref,
                  q_ref, heads_ref, out_ref, lse_ref, kv_all, cot_all, wo_all,
                  kv_ref, kv, acc, peak, total, *sems):
    shards = 2 * nz
    width = kv_ref.shape[2] // 2
    block = q_ref.shape[0] // 2
    low = jnp.bfloat16
    heads = q_ref.shape[1] // width
    z, x, y, c = place()
    split = len(GatherAll.scratch(nz))
    end = split + len(GatherRows.scratch(nz))
    cots = GatherAll(nz, cot_ref, cot_all, sems[:split], cot_ref.shape[0])
    outs = GatherRows(nz, wo_ref, wo_all, sems[split:end])
    keys_in = GatherCausal(nz, kv_ref, kv_all, kv, sems[end:])
    greet([(None, cots.partner), (None, cots.xn), (None, cots.yn),
           (z < nz - 1, cots.up), (z > 0, cots.down)])
    for part in (outs, cots):
        part.own().start()
    turned = norm_turn(k_pre[...], gk_ref[...], cos_ref[...], sin_ref[...]).astype(low)
    for micro in range(2):
        rows = slice(micro * block, (micro + 1) * block)
        kv_ref[micro, :, :width] = turned[rows]
        kv_ref[micro, :, width:] = v_pre[rows, :]
    keys_in.side().start()
    for copy in keys_in.own():
        copy.start()
    peak[...] = jnp.full(peak.shape, masked_score, jnp.float32)
    total[...] = jnp.zeros_like(total)
    acc[...] = jnp.zeros_like(acc)
    for part in (outs, cots):
        part.own().wait()

    def tick(u, carry):
        @pl.when(u < nz)
        def _():
            pl.when(u == 0)(lambda: cots.first(u))
            keys_in.first(u)
            pl.when(u > 0)(lambda: cots.first(u))
            outs.first(u)

        pl.when((u >= 1) & (u <= nz))(lambda: cots.second(u - 1))
        pl.when((u >= 2) & (u <= nz + 1))(lambda: cots.third(u - 2))
        pl.when((u >= 1) & (u <= nz))(lambda: attend_item(u - 1))
        return carry

    def attend_item(k):
        zz = near_first(nz, z, k)
        own = zz == z
        keys_in.ready(zz)

        def part(i, carry):
            micro = jnp.where(own, i // 2, jnp.where(zz < z, 0, 1))
            xx = jnp.where(own, jnp.where(i % 2 == 0, x, 0), i)
            valid = jnp.where(own, jnp.where((i % 2 == 0) | (x == 1), 1, 0), jnp.where(i < 2, 1, 0))
            pl.when(valid == 1)(lambda: attention(micro, zz, xx))
            return carry

        lax.fori_loop(0, 4, part, 0)

    def attention(micro, zz, xx):
        def at_place(z_at, x_at):
            return jnp.where(micro == 0, z_at, nz - 1 - z_at) * 2 + x_at

        here, key_place = at_place(z, x), at_place(zz, xx)
        bias = key_bias(micro, here, key_place, block, start_ref)
        both = kv.at[zz, xx, micro]
        keys, values = both[:, :width], both[:, width:]
        q_rows = pl.ds(pl.multiple_of(micro * block, block), block)

        def head(h, carry):
            at = micro * heads + h
            query = q_ref[q_rows, pl.ds(pl.multiple_of(h * width, width), width)]
            scores = dot_last(keys, query) * width ** (-0.5) + bias
            before = peak[at]
            now = jnp.maximum(before, jnp.max(scores, axis=0, keepdims=True))
            weights = jnp.exp(scores - now)
            factor = jnp.exp(before - now)
            peak[at] = now
            total[at] = total[at] * factor + jnp.sum(weights, axis=0, keepdims=True)
            acc[at] = acc[at] * factor + dot_first(values, weights.astype(jnp.bfloat16))
            return carry

        lax.fori_loop(0, heads, head, 0, unroll=4)

    def prepare(h, carry):
        cols = pl.ds(pl.multiple_of(h * width, width), width)
        q_ref[:, cols] = norm_turn(q_pre[:, cols], gq_ref[...], cos_ref[...], sin_ref[...]).astype(low)
        return carry

    tick(0, 0)
    lax.fori_loop(0, heads, prepare, 0)
    lax.fori_loop(1, nz + 2, tick, 0)

    def close(at, carry):
        micro, h = at // heads, at % heads
        result = (acc[at] / total[at]).T
        here = pl.ds(pl.multiple_of(micro * block, block), block)
        cols = pl.ds(pl.multiple_of(h * width, width), width)
        out_ref[here, cols] = result
        heads_ref[here, cols] = result.astype(jnp.bfloat16)
        lse_ref[at] = peak[at] + jnp.log(total[at])
        return carry

    lax.fori_loop(0, 2 * heads, close, 0)
    keys_in.finish()
    outs.finish()
    cots.finish()


def attend(q_pre, k_pre, v_low, gain_query, gain_key, cosine, sine, starts, cotangent, w_out, nz,
           collective_id):
    rows, columns = q_pre.shape
    width = k_pre.shape[1]
    heads = columns // width
    block = rows // 2
    any_space = pl.BlockSpec(memory_space=pl.ANY)
    vmem = pl.BlockSpec(memory_space=pltpu.VMEM)
    vm, shape, f32, low = pltpu.VMEM, jax.ShapeDtypeStruct, jnp.float32, jnp.bfloat16
    return pl.pallas_call(
        functools.partial(attend_kernel, nz),
        in_specs=[vmem] * 10,
        out_specs=[vmem] * 4 + [any_space] * 3,
        out_shape=[
            shape((rows, columns), low), shape((rows, columns), low), shape((rows, columns), f32),
            shape((2 * heads, 1, block), f32),
            shape((nz, 2, 2, block, 2 * width), low),
            shape((rows * 2 * nz, cotangent.shape[1] * 4), cotangent.dtype),
            shape((w_out.shape[0] * 2 * nz, w_out.shape[1]), w_out.dtype),
        ],
        scratch_shapes=[
            vm((2, block, 2 * width), low), vm((nz, 2, 2, block, 2 * width), low),
            vm((2 * heads, width, block), f32), vm((2 * heads, 1, block), f32),
            vm((2 * heads, 1, block), f32),
        ] + GatherAll.scratch(nz) + GatherRows.scratch(nz) + GatherCausal.scratch(nz),
        compiler_params=pltpu.CompilerParams(
            collective_id=collective_id, has_side_effects=True, vmem_limit_bytes=62 << 20
        ),
        name="attend",
    )(q_pre, k_pre, v_low, gain_query, gain_key, cosine, sine, starts, cotangent, w_out)


class ScatterAll:
    @staticmethod
    def scratch(nz, rows, cols, kind, cut):
        vm, dma = pltpu.VMEM, pltpu.SemaphoreType.DMA
        return [
            vm((nz, 4, rows, cols), kind), vm((nz, 4, rows, cols), kind),
            vm((nz, rows, cols), kind), vm((nz, max(cut, 16), cols), kind),
            vm((nz, rows, cols), kind), vm((nz, max(rows - cut, 16), cols), kind),
            vm((nz + 1, rows, cols), kind),
        ] + [dma((4 * nz,))] * 3 + [dma((nz,))] * 9 + [dma((nz + 1,))]

    def __init__(self, nz, partial, out, refs, cut):
        (self.w, self.lp, self.rx, self.rxd, self.ry, self.ryd, self.rz,
         self.s_l, self.s_p, self.r_p, self.s_x, self.s_y, self.s_dx, self.s_dy, self.s_z,
         self.r_x, self.r_y, self.r_dx, self.r_dy, self.r_z) = refs
        self.nz, self.partial, self.out, self.cut = nz, partial, out, cut
        self.rows, self.cols = out.shape
        self.place = z, x, y, c = place()
        self.partner, self.xn, self.yn = (
            device(z, x, y, 1 - c), device(z, 1 - x, y, c), device(z, x, 1 - y, c))
        self.up, self.down = device(z + 1, x, y, c), device(z - 1, x, y, c)

    def block(self, zz, rel, cc):
        z, x, y, c = self.place
        xx = 1 - x if rel in (1, 3) else x
        yy = 1 - y if rel in (2, 3) else y
        return self.partial.at[
            pl.ds(pl.multiple_of((zz * 2 + xx) * self.rows, self.rows), self.rows),
            pl.ds(pl.multiple_of((yy * 2 + cc) * self.cols, self.cols), self.cols)]

    def pair(self, zz, rel):
        k = zz * 4 + rel
        return remote(self.block(zz, rel, 1 - self.place[3]), self.lp.at[zz, rel],
                      self.s_p.at[k], self.r_p.at[k], self.partner)

    def load(self, zz, rel):
        return pltpu.make_async_copy(
            self.block(zz, rel, self.place[3]), self.w.at[zz, rel], self.s_l.at[zz * 4 + rel])

    def across(self, zz):
        copies = []
        if self.cut > 0:
            copies.append(remote(self.w.at[zz, 3, pl.ds(0, self.cut)], self.rxd.at[zz],
                                 self.s_dx.at[zz], self.r_dx.at[zz], self.xn))
        if self.cut < self.rows:
            copies.append(remote(self.w.at[zz, 3, pl.ds(self.cut, self.rows - self.cut)],
                                 self.ryd.at[zz], self.s_dy.at[zz], self.r_dy.at[zz], self.yn))
        return copies

    def sides(self, zz):
        return (remote(self.w.at[zz, 1], self.rx.at[zz], self.s_x.at[zz], self.r_x.at[zz], self.xn),
                remote(self.w.at[zz, 2], self.ry.at[zz], self.s_y.at[zz], self.r_y.at[zz], self.yn))

    def line(self, zz, slot, where):
        return remote(self.w.at[zz, 0], self.rz.at[slot], self.s_z.at[zz], self.r_z.at[slot], where)

    def start(self):
        def step(k, carry):
            zz = far_first(self.nz, self.place[0], k)
            for rel in (3, 1, 2, 0):
                self.pair(zz, rel).start()
                self.load(zz, rel).start()
            return carry

        lax.fori_loop(0, self.nz, step, 0)

    def first(self, k):
        zz = far_first(self.nz, self.place[0], k)
        for rel in (3, 1, 2, 0):
            self.pair(zz, rel).wait_recv()
            self.load(zz, rel).wait()
            add_blocks(self.w.at[zz, rel], [self.lp.at[zz, rel]], 0, self.rows)
            if rel == 3:
                for copy in self.across(zz):
                    copy.start()

    def second(self, k):
        zz = far_first(self.nz, self.place[0], k)
        across, (to_x, to_y) = self.across(zz), self.sides(zz)
        if self.cut < self.rows:
            across[-1].wait_recv()
            add_blocks(self.w.at[zz, 1], [self.ryd.at[zz]], self.cut, self.rows - self.cut)
        to_x.start()
        if self.cut > 0:
            across[0].wait_recv()
            add_blocks(self.w.at[zz, 2], [self.rxd.at[zz]], 0, self.cut)
        to_y.start()

    def send_line(self, zz):
        z = self.place[0]
        pl.when(zz > z)(lambda: self.line(zz, zz, self.up).start())
        pl.when(zz == z - 1)(lambda: self.line(zz, self.nz, self.down).start())
        pl.when(zz < z - 1)(lambda: self.line(zz, zz, self.down).start())

    def passes(self, zz):
        z = self.place[0]
        return ((zz > z) & (z > 0)) | ((zz < z) & (z < self.nz - 1))

    def third(self, k):
        zz, z = far_first(self.nz, self.place[0], k), self.place[0]
        to_x, to_y = self.sides(zz)
        to_x.wait_recv()
        to_y.wait_recv()
        add_blocks(self.w.at[zz, 0], [self.rx.at[zz], self.ry.at[zz]], 0, self.rows)
        pl.when((zz != z) & jnp.logical_not(self.passes(zz)))(lambda: self.send_line(zz))

    def fourth(self, k):
        zz, z, nz = far_first(self.nz, self.place[0], k), self.place[0], self.nz

        @pl.when((zz != z) & self.passes(zz))
        def _():
            self.line(zz, zz, self.up).wait_recv()
            add_blocks(self.w.at[zz, 0], [self.rz.at[zz]], 0, self.rows)
            self.send_line(zz)

        @pl.when(zz == z)
        def _():
            finish_line(self, self.w.at[zz, 0], zz)

    def finish(self):
        z = self.place[0]

        def step(zz, carry):
            for rel in range(4):
                self.pair(zz, rel).wait_send()
            for copy in tuple(self.across(zz)) + tuple(self.sides(zz)):
                copy.wait_send()
            pl.when(zz != z)(lambda: self.line(zz, zz, self.up).wait_send())
            return carry

        lax.fori_loop(0, self.nz, step, 0)


def finish_line(self, own, zz):
    z, nz = self.place[0], self.nz
    below, above = self.rz.at[zz], self.rz.at[nz]
    pl.when(z > 0)(lambda: self.line(zz, zz, self.up).wait_recv())
    pl.when(z < nz - 1)(lambda: self.line(zz, nz, self.down).wait_recv())
    pl.when(z == 0)(lambda: add_blocks(own, [above], 0, self.rows, self.out))
    pl.when(z == nz - 1)(lambda: add_blocks(own, [below], 0, self.rows, self.out))
    pl.when((z > 0) & (z < nz - 1))(lambda: add_blocks(own, [below, above], 0, self.rows, self.out))


class ReduceRows:
    @staticmethod
    def scratch(nz, rows, cols, kind):
        vm, dma = pltpu.VMEM, pltpu.SemaphoreType.DMA
        return [vm((nz, rows, cols), kind), vm((nz, rows, cols), kind),
                vm((nz + 1, rows, cols), kind)] + [dma((nz,))] * 4 + [dma((nz + 1,))]

    def __init__(self, nz, partial, out, refs):
        self.w, self.rx, self.rz, self.s_l, self.s_x, self.s_z, self.r_x, self.r_z = refs
        self.nz, self.partial, self.out = nz, partial, out
        self.rows = out.shape[0]
        self.place = z, x, y, c = place()
        self.xn = device(z, 1 - x, y, c)
        self.up, self.down = device(z + 1, x, y, c), device(z - 1, x, y, c)

    def block(self, zz, xx):
        return self.partial.at[pl.ds(pl.multiple_of((zz * 2 + xx) * self.rows, self.rows), self.rows)]

    def side(self, zz):
        return remote(self.block(zz, 1 - self.place[1]), self.rx.at[zz],
                      self.s_x.at[zz], self.r_x.at[zz], self.xn)

    def load(self, zz):
        return pltpu.make_async_copy(self.block(zz, self.place[1]), self.w.at[zz], self.s_l.at[zz])

    def line(self, zz, slot, where):
        return remote(self.w.at[zz], self.rz.at[slot], self.s_z.at[zz], self.r_z.at[slot], where)

    def start(self):
        def step(k, carry):
            self.send(k)
            return carry

        lax.fori_loop(0, self.nz, step, 0)

    def send(self, k):
        zz = far_first(self.nz, self.place[0], k)
        self.side(zz).start()
        self.load(zz).start()

    send_line = ScatterAll.send_line
    passes = ScatterAll.passes

    def first(self, k):
        zz, z = far_first(self.nz, self.place[0], k), self.place[0]
        self.load(zz).wait()
        self.side(zz).wait_recv()
        add_blocks(self.w.at[zz], [self.rx.at[zz]], 0, self.rows)
        pl.when((zz != z) & jnp.logical_not(self.passes(zz)))(lambda: self.send_line(zz))

    def second(self, k):
        zz, z, nz = far_first(self.nz, self.place[0], k), self.place[0], self.nz

        @pl.when((zz != z) & self.passes(zz))
        def _():
            self.line(zz, zz, self.up).wait_recv()
            add_blocks(self.w.at[zz], [self.rz.at[zz]], 0, self.rows)
            self.send_line(zz)

        @pl.when(zz == z)
        def _():
            finish_line(self, self.w.at[zz], zz)

    def finish(self):
        z = self.place[0]

        def step(zz, carry):
            self.side(zz).wait_send()
            pl.when(zz != z)(lambda: self.line(zz, zz, self.up).wait_send())
            return carry

        lax.fori_loop(0, self.nz, step, 0)


def attend_back_kernel(nz, q_ref, q_pre, gq_ref, cos_ref, sin_ref, kv_ref, start_ref, lse_ref,
                       delta_ref, grad_ref, small_ref, out_part, wo_part, q_grad, gain_grad, sides, out_sum, wo_sum, small_out,
                       acc, k_acc, v_acc, *refs):
    shards = 2 * nz
    shard = lax.axis_index("fsdp")
    width = kv_ref.shape[4] // 2
    block = q_ref.shape[0] // 2
    heads = q_ref.shape[1] // width
    z, x, y, c = place()
    count = shards + 2 * x
    low = jnp.bfloat16
    split = len(ScatterAll.scratch(nz, 16, 128, low, 0))
    outs = ScatterAll(nz, out_part, out_sum, refs[:split], 0)
    end = split + len(ReduceRows.scratch(nz, 16, 128, low))
    weights = ReduceRows(nz, wo_part, wo_sum, refs[split:end])
    smalls = SmallSums(nz, small_ref, small_out, refs[end:])
    greet_all(lax.axis_index("fsdp"), lax.axis_index("tp"), shards, 4)
    smalls.start()
    outs.start()

    sides[...] = jnp.zeros_like(sides)
    acc[...] = jnp.zeros_like(acc)

    def attention(u):
        micro, here, key_place, owner = stream_unit(u, nz)
        rows = pl.ds(pl.multiple_of((owner * 2 + micro) * block, block), block)
        bias = key_bias(micro, here, key_place, block, start_ref)
        both = kv_ref.at[owner // 2, owner % 2, micro]
        keys, values = both[:, :width], both[:, width:]
        q_rows = pl.ds(pl.multiple_of(micro * block, block), block)
        k_acc[...] = jnp.zeros_like(k_acc)
        v_acc[...] = jnp.zeros_like(v_acc)

        def head(h, carry):
            at = micro * heads + h
            cols = pl.ds(pl.multiple_of(h * width, width), width)
            query, grad = q_ref[q_rows, cols], grad_ref[q_rows, cols]
            scores = dot_last(keys, query) * width ** (-0.5) + bias
            probs = jnp.exp(scores - lse_ref[at])
            score_grad = (probs * (dot_last(values, grad) - delta_ref[at])).astype(low)
            v_acc[...] += dot_plain(probs.astype(low), grad)
            k_acc[...] += dot_plain(score_grad, query)
            acc[at] += dot_first(keys, score_grad)
            return carry

        lax.fori_loop(0, heads, head, 0, unroll=2)
        sides[rows, pl.ds(0, width)] = (k_acc[...] * width ** (-0.5)).astype(low)
        sides[rows, pl.ds(width, width)] = v_acc[...].astype(low)

    def close(at, total):
        micro, h = at // heads, at % heads
        here = pl.ds(pl.multiple_of(micro * block, block), block)
        cols = pl.ds(pl.multiple_of(h * width, width), width)
        turned = acc[at].T * width ** (-0.5)
        grad = turned * cos_ref[here, :] + pltpu.roll(turned * sin_ref[here, :], width // 2, 1)
        raw = q_pre[here, cols]
        scale = lax.rsqrt(jnp.mean(raw * raw, axis=1, keepdims=True) + norm_eps)
        inner = grad * gq_ref[...]
        mean = jnp.mean(raw * inner, axis=1, keepdims=True)
        q_grad[here, cols] = (scale * inner - raw * (scale * scale * scale * mean)).astype(low)
        return total + jnp.sum(grad * raw * scale, axis=0, keepdims=True)

    def close_all():
        gain_grad[...] = lax.fori_loop(
            0, 2 * heads, close, jnp.zeros(gain_grad.shape, jnp.float32)
        )

    def unit(u, carry):
        def at(fn, k):
            pl.when((k >= 0) & (k < nz))(lambda: fn(k))

        at(outs.first, u)
        at(outs.second, u - 1)
        at(weights.send, u)
        pl.when(u == 2)(smalls.second)
        pl.when(2 * u < count)(lambda: attention(2 * u))
        pl.when(2 * u + 1 < count)(lambda: attention(2 * u + 1))
        pl.when(u == (shards + 2) // 2)(close_all)
        at(outs.third, u - 2)
        at(outs.fourth, u - 3)
        at(weights.second, u - 2)
        at(weights.first, u - 1)
        return carry

    lax.fori_loop(0, max(nz + 3, nz + 2), unit, 0)

    outs.finish()
    weights.finish()
    smalls.finish()


def attend_back(query, q_pre, gain_query, cosine, sine, keys_values, starts, log_total, delta,
                grad, small, out_part, wo_part, nz, collective_id):
    rows, columns = query.shape
    width = keys_values.shape[4] // 2
    heads = columns // width
    block = rows // 2
    cols = out_part.shape[1] // 4
    wo_shape = (wo_part.shape[0] // (2 * nz), wo_part.shape[1])
    any_space = pl.BlockSpec(memory_space=pl.ANY)
    vmem = pl.BlockSpec(memory_space=pltpu.VMEM)
    vm, shape, f32, low = pltpu.VMEM, jax.ShapeDtypeStruct, jnp.float32, jnp.bfloat16
    return pl.pallas_call(
        functools.partial(attend_back_kernel, nz),
        in_specs=[vmem] * 11 + [any_space] * 2,
        out_specs=[vmem] * 6,
        out_shape=[
            shape((rows, columns), low), shape((1, width), f32),
            shape((rows * 2 * nz, 2 * width), low),
            shape((rows, cols), f32), shape(wo_shape, f32),
            shape((8 * nz,) + small.shape[1:], f32),
        ],
        scratch_shapes=[
            vm((2 * heads, width, block), f32), vm((block, width), f32), vm((block, width), f32),
        ] + ScatterAll.scratch(nz, rows, cols, low, 0) + ReduceRows.scratch(nz, *wo_shape, low)
        + SmallSums.scratch(nz, small.shape[1:], f32),
        compiler_params=pltpu.CompilerParams(
            collective_id=collective_id, has_side_effects=True, vmem_limit_bytes=62 << 20
        ),
        name="attend_back",
    )(query, q_pre, gain_query, cosine, sine, keys_values, starts, log_total, delta, grad, small,
      out_part, wo_part)


def to_row(column, eye):
    return jnp.sum(jnp.where(eye, column, 0.0), axis=0, keepdims=True)


def to_column(row, eye):
    return jnp.sum(jnp.where(eye, row, 0.0), axis=1, keepdims=True)


def diagonal():
    shape = (128, 128)
    return lax.broadcasted_iota(jnp.int32, shape, 0) == lax.broadcasted_iota(jnp.int32, shape, 1)


class RowSums:
    @staticmethod
    def scratch(rows):
        dma = pltpu.SemaphoreType.DMA
        return [pltpu.VMEM((4, rows // 128, 128), jnp.float32), dma((3,)), dma((3,))]

    def __init__(self, refs):
        self.got, s, r = refs
        shard, group = lax.axis_index("fsdp"), lax.axis_index("tp")
        self.peers = [(shard, (group + k) % 4) for k in range(1, 4)]
        self.copies = [
            remote(self.got.at[0], self.got.at[k + 1], s.at[k], r.at[k], peer)
            for k, peer in enumerate(self.peers)
        ]

    def start(self):
        for copy in self.copies:
            copy.start()

    def wait(self):
        for copy in self.copies:
            copy.wait()

    def total(self, n):
        return self.got[0, pl.ds(n, 1), :] + self.got[1, pl.ds(n, 1), :] + (
            self.got[2, pl.ds(n, 1), :] + self.got[3, pl.ds(n, 1), :])


class ReduceCols:
    @staticmethod
    def scratch(rows, cols, kind):
        vm, dma = pltpu.VMEM, pltpu.SemaphoreType.DMA
        return [vm((2, rows, cols), kind), vm((2, rows, cols), kind), vm((rows, cols), kind),
                dma((2,)), dma((2,)), dma((2,)), dma, dma]

    def __init__(self, partial, out, refs):
        self.w, self.rp, self.ry, s_l, s_p, r_p, s_y, r_y = refs
        self.out = out
        self.rows, cols = out.shape
        z, x, y, c = place()
        self.partner, self.yn = device(z, x, y, 1 - c), device(z, x, 1 - y, c)

        def block(yy, cc):
            return partial.at[:, pl.ds(pl.multiple_of((yy * 2 + cc) * cols, cols), cols)]

        self.sends = [remote(block(yy, 1 - c), self.rp.at[k], s_p.at[k], r_p.at[k], self.partner)
                      for k, yy in enumerate((1 - y, y))]
        self.loads = [pltpu.make_async_copy(block(yy, c), self.w.at[k], s_l.at[k])
                      for k, yy in enumerate((1 - y, y))]
        self.across = remote(self.w.at[0], self.ry, s_y, r_y, self.yn)

    def start(self):
        for k in range(2):
            self.sends[k].start()
            self.loads[k].start()

    def first(self):
        self.loads[0].wait()
        self.sends[0].wait_recv()
        add_blocks(self.w.at[0], [self.rp.at[0]], 0, self.rows)
        self.across.start()

    def second(self):
        self.loads[1].wait()
        self.sends[1].wait_recv()
        self.across.wait_recv()
        add_blocks(self.w.at[1], [self.rp.at[1], self.ry], 0, self.rows, self.out)

    def finish(self):
        for send in self.sends:
            send.wait_send()
        self.across.wait_send()


class SmallSums:
    @staticmethod
    def scratch(nz, part, kind):
        dma = pltpu.SemaphoreType.DMA
        return [pltpu.VMEM((2 * nz,) + part, kind), dma((2 * nz,)), dma((2 * nz,)),
                dma((8 * nz,)), dma((8 * nz,))]

    def __init__(self, nz, values, out, refs):
        self.got, self.s_1, self.r_1, self.s_2, self.r_2 = refs
        self.values, self.out = values, out
        self.shards, self.devices = 2 * nz, 8 * nz
        self.shard, self.group = lax.axis_index("fsdp"), lax.axis_index("tp")
        self.me = self.shard * 4 + self.group

    def share(self, k):
        other = (self.shard + k) % self.shards
        return remote(self.values.at[other], self.got.at[k], self.s_1.at[k], self.r_1.at[k],
                      (other, self.group))

    def spread(self, k):
        other = (self.me + k) % self.devices
        return remote(self.out.at[self.me], self.out.at[self.me], self.s_2.at[k], self.r_2.at[k],
                      (other // 4, other % 4))

    def start(self):
        loop_from_one(self.shards, lambda k: self.share(k).start())

    def second(self):
        loop_from_one(self.shards, lambda k: self.share(k).wait())
        acc = self.values[self.shard]
        for k in range(1, self.shards):
            acc = acc + self.got[k]
        self.out[self.me] = acc
        loop_from_one(self.devices, lambda k: self.spread(k).start())

    def finish(self):
        loop_from_one(self.devices, lambda k: self.spread(k).wait())


def loop_from_one(count, fn):
    def step(k, carry):
        fn(k)
        return carry

    lax.fori_loop(1, count, step, 0)


def tail_kernel(nz, tok_ref, mid_ref, scale_ref, gain_ref, block_ref, small_ref,
                gp_all, up_all, hid_all, xr_all, gs_all, w_part, normed_part,
                w_sum, token_out, block_out, small_out, dwg, dwu, dwd,
                gp_ref, up_ref, hid_ref, x_panel, g_panel, o_gate, o_up, o_down, s_in, s_out,
                normed, token, s_w, r_w, s_l, s_g, r_g, *refs):
    z, x, y, c = place()
    shard, group = lax.axis_index("fsdp"), lax.axis_index("tp")
    shards = 2 * nz
    devices = 4 * shards
    me = shard * 4 + group
    rows, cols = tok_ref.shape
    width = cols * 4
    half = rows // 2
    panel = x_panel.shape[1]
    panels = xr_all.shape[1] // panel
    f32, low = jnp.float32, jnp.bfloat16
    n_w, n_c = len(ReduceRows.scratch(nz, 16, 128, low)), len(ReduceCols.scratch(16, 128, low))
    weights = ReduceRows(nz, w_part, w_sum, refs[:n_w])
    columns = ReduceCols(normed_part, normed, refs[n_w : n_w + n_c])
    sums = RowSums(refs[n_w + n_c :])
    mirror = device(nz - 1 - z, x, y, c)
    greet_all(shard, group, shards, 4)
    columns.start()
    weights.start()
    top, bottom = pl.ds(0, half), pl.ds(half, half)
    swaps = [remote(src.at[bottom], dst.at[bottom], s_w.at[n], r_w.at[n], mirror)
             for n, (src, dst) in enumerate(((token, token_out), (block_ref, block_out)))]
    keeps = [pltpu.make_async_copy(src.at[top], dst.at[top], s_l.at[n])
             for n, (src, dst) in enumerate(((token, token_out), (block_ref, block_out)))]
    swaps[1].start()
    keeps[1].start()

    def loads(n):
        at = pl.ds(pl.multiple_of(n * panel, panel), panel)
        return (pltpu.make_async_copy(xr_all.at[:, at], x_panel, s_in.at[0]),
                pltpu.make_async_copy(gs_all.at[:, at], g_panel, s_in.at[1]))

    def stores(n):
        at = pl.ds(pl.multiple_of(n * panel, panel), panel)
        return (pltpu.make_async_copy(o_gate, dwg.at[at, :], s_out.at[0]),
                pltpu.make_async_copy(o_up, dwu.at[at, :], s_out.at[1]),
                pltpu.make_async_copy(o_down, dwd.at[:, at], s_out.at[2]))

    whole = [pltpu.make_async_copy(src, dst, s_in.at[2 + n])
             for n, (src, dst) in enumerate(((gp_all, gp_ref), (up_all, up_ref), (hid_all, hid_ref)))]
    for copy in tuple(whole) + loads(0):
        copy.start()
    small_out[me] = small_ref[...]

    def expert_weights(n):
        @pl.when(n == 0)
        def _():
            for copy in whole:
                copy.wait()

        for copy in loads(n):
            copy.wait()

        @pl.when(n > 0)
        def _():
            for copy in stores(n):
                copy.wait()

        o_gate[...] = dot_first(x_panel[...], gp_ref[...])
        o_up[...] = dot_first(x_panel[...], up_ref[...])
        o_down[...] = dot_first(g_panel[...], hid_ref[...]).T
        for copy in stores(n):
            copy.start()

        @pl.when(n < panels - 1)
        def _():
            for copy in loads(n + 1):
                copy.start()

    def token_sums():
        eye = diagonal()

        def step(n, gains):
            here = pl.ds(pl.multiple_of(n * 128, 128), 128)
            tok, grad = tok_ref[here, :].astype(f32), normed[here, :]
            product = tok * (grad * gain_ref[...])
            sums.got[0, pl.ds(n, 1), :] = to_row(jnp.sum(product, axis=1, keepdims=True), eye)
            return gains + jnp.sum(grad * tok * scale_ref[here, :], axis=0, keepdims=True)

        gains = lax.fori_loop(0, rows // 128, step, jnp.zeros((1, cols), f32))
        for n in range(cols // 128):
            small_out[me, pl.ds(n, 1), :] = gains[:, n * 128 : (n + 1) * 128]

    def token_grads():
        eye = diagonal()

        def step(n, carry):
            here = pl.ds(pl.multiple_of(n * 128, 128), 128)
            mean = to_column(sums.total(n), eye) / width
            scale = scale_ref[here, :]
            token[here, :] = (
                mid_ref[here, :]
                + scale * (gain_ref[...] * normed[here, :])
                - tok_ref[here, :].astype(f32) * (scale * scale * scale * mean)
            ).astype(low)
            return carry

        lax.fori_loop(0, rows // 128, step, 0)

    def spread(k):
        other = (me + k) % devices
        return remote(small_out.at[me], small_out.at[me], s_g.at[k], r_g.at[k],
                      (other // 4, other % 4))

    columns.first()

    def unit(u, carry):
        @pl.when(u == 1)
        def _():
            sums.wait()
            token_grads()
            swaps[0].start()
            keeps[0].start()

        pl.when((u >= 1) & (u <= nz))(lambda: weights.second(u - 1))

        @pl.when(u < panels // 2)
        def _():
            expert_weights(2 * u)
            expert_weights(2 * u + 1)

        @pl.when(u == 0)
        def _():
            columns.second()
            token_sums()
            sums.start()
            loop_from_one(devices, lambda k: spread(k).start())

        pl.when(u < nz)(lambda: weights.first(u))
        return carry

    lax.fori_loop(0, max(nz + 1, panels // 2), unit, 0)
    loop_from_one(devices, lambda k: spread(k).wait())
    for copy in swaps + keeps:
        copy.wait()
    for copy in stores(panels - 1):
        copy.wait()
    columns.finish()
    weights.finish()


def tail(gate_grad, up_grad, hidden, tokens, middle_grad, scale, gain, block_out, small, rows_in,
         pair_grad, w_part, normed_part, nz, collective_id):
    rows, cols = tokens.shape
    pairs, features = rows_in.shape
    hidden_width = hidden.shape[1]
    panel = 256
    w_shape = (w_part.shape[0] // (2 * nz), w_part.shape[1])
    devices = 8 * nz
    any_space = pl.BlockSpec(memory_space=pl.ANY)
    vmem = pl.BlockSpec(memory_space=pltpu.VMEM)
    vm, shape, f32, low = pltpu.VMEM, jax.ShapeDtypeStruct, jnp.float32, jnp.bfloat16
    dma = pltpu.SemaphoreType.DMA
    return pl.pallas_call(
        functools.partial(tail_kernel, nz),
        in_specs=[vmem] * 6 + [any_space] * 7,
        out_specs=[vmem, any_space, any_space, vmem] + [any_space] * 3,
        out_shape=[
            shape(w_shape, f32), shape((rows, cols), low), shape((rows, cols), low),
            shape((devices,) + small.shape, f32),
            shape((features, hidden_width), f32), shape((features, hidden_width), f32),
            shape((hidden_width, features), f32),
        ],
        scratch_shapes=[vm((pairs, hidden_width), low)] * 3 + [
            vm((pairs, panel), low), vm((pairs, panel), low),
            vm((panel, hidden_width), f32), vm((panel, hidden_width), f32),
            vm((hidden_width, panel), f32), dma((5,)), dma((3,)),
            vm((rows, cols), f32), vm((rows, cols), low),
            dma((2,)), dma((2,)), dma((2,)), dma((devices,)), dma((devices,)),
        ] + ReduceRows.scratch(nz, *w_shape, low) + ReduceCols.scratch(rows, cols, low)
        + RowSums.scratch(rows),
        compiler_params=pltpu.CompilerParams(
            collective_id=collective_id, has_side_effects=True, vmem_limit_bytes=62 << 20
        ),
        name="tail",
    )(tokens, middle_grad, scale, gain, block_out, small, gate_grad, up_grad, hidden, rows_in,
      pair_grad, w_part, normed_part)


def join_kernel(nz, tok_ref, gain_ref, attn_part, middle_ref, scale_ref, low_ref, all_ref, *refs):
    z, x, y, c = place()
    rows, cols = tok_ref.shape
    f32 = jnp.float32
    n_c, n_s = len(ReduceCols.scratch(16, 128, jnp.bfloat16)), 3
    columns = ReduceCols(attn_part, middle_ref, refs[:n_c])
    sums = RowSums(refs[n_c : n_c + n_s])
    gather = GatherAll(nz, low_ref, all_ref, refs[n_c + n_s :], rows // 2)
    greet([(None, gather.xn), (z < nz - 1, gather.up), (z > 0, gather.down)]
          + [(None, peer) for peer in sums.peers])
    columns.start()
    eye = diagonal()
    columns.first()
    columns.second()

    def add(n, carry):
        here = pl.ds(pl.multiple_of(n * 128, 128), 128)
        total = middle_ref[here, :] + tok_ref[here, :].astype(f32)
        middle_ref[here, :] = total
        sums.got[0, pl.ds(n, 1), :] = to_row(jnp.sum(total * total, axis=1, keepdims=True), eye)
        return carry

    def norm(n, carry):
        here = pl.ds(pl.multiple_of(n * 128, 128), 128)
        scale = lax.rsqrt(to_column(sums.total(n), eye) / (4 * cols) + norm_eps)
        scale_ref[here, :] = scale
        low_ref[here, :] = (middle_ref[here, :] * scale * gain_ref[...]).astype(low_ref.dtype)
        return carry

    lax.fori_loop(0, rows // 128, add, 0)
    sums.start()
    sums.wait()
    lax.fori_loop(0, rows // 128, norm, 0)
    gather.own().start()
    gather.own().wait()

    def tick(k, carry):
        pl.when(k < nz)(lambda: gather.first(k))
        pl.when((k >= 1) & (k <= nz))(lambda: gather.second(k - 1))
        pl.when(k >= 2)(lambda: gather.third(k - 2))
        return carry

    lax.fori_loop(0, nz + 2, tick, 0)
    gather.finish()
    columns.finish()


def join(tokens, gain, attn_part, nz, collective_id):
    rows, cols = tokens.shape
    any_space = pl.BlockSpec(memory_space=pl.ANY)
    vmem = pl.BlockSpec(memory_space=pltpu.VMEM)
    shape, f32, low = jax.ShapeDtypeStruct, jnp.float32, jnp.bfloat16
    return pl.pallas_call(
        functools.partial(join_kernel, nz),
        in_specs=[vmem] * 2 + [any_space],
        out_specs=[vmem] * 3 + [any_space],
        out_shape=[shape((rows, cols), f32), shape((rows, 1), f32), shape((rows, cols), low),
                   shape((rows * 2 * nz, cols * 4), low)],
        scratch_shapes=ReduceCols.scratch(rows, cols, low) + RowSums.scratch(rows)
        + GatherAll.scratch(nz),
        compiler_params=pltpu.CompilerParams(
            collective_id=collective_id, has_side_effects=True, vmem_limit_bytes=62 << 20
        ),
        name="join",
    )(tokens, gain, attn_part)


def turn_kernel(middle_ref, scale_ref, inner_ref, grad_ref, out_ref, all_ref, low_ref, lsem,
                s_p, r_p, s_y, r_y, *refs):
    z, x, y, c = place()
    rows, cols = middle_ref.shape
    sums = RowSums(refs)
    partner, yn = device(z, x, y, 1 - c), device(z, x, 1 - y, c)
    greet([(None, peer) for peer in sums.peers])
    eye = diagonal()

    def block(yy):
        return all_ref.at[:, pl.ds(pl.multiple_of((yy * 2 + c) * cols, cols), cols)]

    def dots(n, carry):
        here = pl.ds(pl.multiple_of(n * 128, 128), 128)
        product = middle_ref[here, :] * inner_ref[here, :]
        sums.got[0, pl.ds(n, 1), :] = to_row(jnp.sum(product, axis=1, keepdims=True), eye)
        return carry

    def grads(n, carry):
        here = pl.ds(pl.multiple_of(n * 128, 128), 128)
        mean = to_column(sums.total(n), eye) / (4 * cols)
        scale = scale_ref[here, :]
        out = (grad_ref[here, :] + scale * inner_ref[here, :]
               - middle_ref[here, :] * (scale * scale * scale * mean))
        out_ref[here, :] = out
        low_ref[here, :] = out.astype(low_ref.dtype)
        return carry

    lax.fori_loop(0, rows // 128, dots, 0)
    sums.start()
    sums.wait()
    lax.fori_loop(0, rows // 128, grads, 0)
    to_y = remote(low_ref, block(y), s_y, r_y, yn)
    to_pair = remote(low_ref, block(y), s_p.at[0], r_p.at[0], partner)
    own = pltpu.make_async_copy(low_ref, block(y), lsem)
    on = remote(block(1 - y), block(1 - y), s_p.at[1], r_p.at[1], partner)
    for copy in (to_y, to_pair, own):
        copy.start()
    to_y.wait_recv()
    on.start()
    to_pair.wait()
    on.wait()
    to_y.wait_send()
    own.wait()


def turn(middle, scale, inner, grad, collective_id):
    rows, cols = middle.shape
    any_space = pl.BlockSpec(memory_space=pl.ANY)
    vmem = pl.BlockSpec(memory_space=pltpu.VMEM)
    shape, f32, low = jax.ShapeDtypeStruct, jnp.float32, jnp.bfloat16
    dma = pltpu.SemaphoreType.DMA
    return pl.pallas_call(
        turn_kernel,
        in_specs=[vmem] * 4,
        out_specs=[vmem, any_space],
        out_shape=[shape((rows, cols), f32), shape((rows, cols * 4), low)],
        scratch_shapes=[pltpu.VMEM((rows, cols), low), dma, dma((2,)), dma((2,)), dma, dma]
        + RowSums.scratch(rows),
        compiler_params=pltpu.CompilerParams(
            collective_id=collective_id, has_side_effects=True, vmem_limit_bytes=62 << 20
        ),
        name="turn",
    )(middle, scale, inner, grad)


def gathered_body(
    tokens,
    cotangent,
    routes,
    doc_ids,
    gain_attn,
    w_query,
    key_weight,
    value_weight,
    w_out,
    gain_query,
    key_norm_gain,
    gain_moe,
    router,
    w_gate,
    w_up,
    w_down,
):
    shard_count = lax.axis_size("fsdp")
    group_count = lax.axis_size("tp")
    shard_index = lax.axis_index("fsdp")
    group_index = lax.axis_index("tp")
    nz = shard_count // 2
    f32, low = jnp.float32, jnp.bfloat16
    row_count, slice_width = tokens.shape
    model_width = slice_width * group_count
    micro_count, micro_rows = doc_ids.shape
    head_width = gain_query.shape[0]
    query_width, kv_width = w_query.shape[1], key_weight.shape[1]
    query_local = query_width // head_width
    kv_local = kv_width // head_width
    group_width = query_local // kv_local
    expert_total = router.shape[1]
    capacity = max(2, 2 * micro_rows * TOPK // expert_total)
    block_keys = micro_rows * math.gcd(shard_count, max(1, 512 // micro_rows))
    my_columns = group_index * slice_width

    mirror_index = mirrored(nz, shard_index)
    owners = jnp.stack([shard_index, mirror_index])

    small = jnp.concatenate([routes.reshape(-1), doc_ids.reshape(-1)])
    small_rows = -(-small.shape[0] // 1024) * 8
    small = jnp.pad(small, (0, small_rows * 128 - small.shape[0])).reshape(small_rows, 128)
    small_all, wq_all, wk_all, wv_all, tokens, full_tokens = gather_rows(
        [small, w_query, key_weight, value_weight], nz, 2, [tokens]
    )
    small_all = small_all.reshape(shard_count, small_rows * 128)
    routes_all = small_all[:, : row_count * TOPK].reshape(shard_count * row_count, TOPK)
    ids_all = small_all[:, row_count * TOPK : row_count * (TOPK + 1)].reshape(
        shard_count, micro_count, micro_rows
    )
    doc_range = jnp.arange(DOCS)
    doc_totals = jnp.sum((ids_all[..., None] == doc_range).astype(jnp.int32), axis=(0, 2))
    doc_begin = jnp.cumsum(doc_totals, axis=1) - doc_totals
    query_index = owners[:, None] * micro_rows + jnp.arange(micro_rows)
    my_ids = jnp.stack(
        [lax.dynamic_index_in_dim(ids_all[:, m], owners[m], 0, False) for m in range(micro_count)]
    )
    query_start = jnp.sum(
        jnp.where(my_ids[:, :, None] == doc_range, doc_begin[:, None, :], 0), axis=2
    )
    positions = (query_index - query_start).reshape(row_count)
    cosine_lookup, sine_lookup = rope_tables(positions, head_width)

    full_tokens = full_tokens.astype(f32)
    token_mean = jnp.mean(full_tokens * full_tokens, axis=-1, keepdims=True)
    token_scale = lax.rsqrt(token_mean + norm_eps)
    normed_low = (full_tokens * token_scale * gain_attn).astype(low)
    query_pre = jnp.dot(normed_low, wq_all, preferred_element_type=f32)
    key_pre = jnp.dot(normed_low, wk_all, preferred_element_type=f32)
    value_low = jnp.dot(normed_low, wv_all, preferred_element_type=f32).astype(low)
    turned_sine = jnp.where(jnp.arange(head_width) < head_width // 2, -sine_lookup, sine_lookup)
    query_gain, key_gain = gain_query.reshape(1, head_width), key_norm_gain.reshape(1, head_width)
    starts = query_start.reshape(micro_count, 1, micro_rows).astype(jnp.int32)
    query_low, heads_low, head_out, log_total, keys_values, grads_all, wo_all = attend(
        query_pre, key_pre, value_low, query_gain, key_gain, cosine_lookup, turned_sine, starts,
        cotangent, w_out, nz, 3,
    )
    attn_part = dot_last(heads_low, wo_all).astype(low)
    gain_slice = lax.dynamic_slice_in_dim(gain_moe, my_columns, slice_width)
    middle, scale, moe_low, moe_all = join(
        tokens, gain_slice.reshape(1, slice_width), attn_part, nz, 5
    )
    out_part, back, gates_grad, gates, *kept = run_experts(
        moe_all, grads_all, routes_all, router, w_gate[0], w_up[0], w_down[0],
        micro_rows, capacity, nz, 8,
    )
    rows_in, pair_grad, hidden_low, gate_pre_low, up_pre_low = (
        array.reshape(-1, array.shape[2]) for array in kept
    )
    gates_grad = gates_grad.reshape(expert_total, row_count).T
    logit_grad = gates * (gates_grad - jnp.sum(gates * gates_grad, axis=1, keepdims=True))
    router_slice = lax.dynamic_slice_in_dim(router, my_columns, slice_width).astype(f32)
    moe_grad = back + lax.dot_general(
        logit_grad, router_slice, (((1,), (1,)), ((), ())), precision=highest_precision
    )
    router_part = lax.dot_general(
        moe_low.astype(f32), logit_grad, (((0,), (0,)), ((), ())), precision=highest_precision
    )
    gain_moe_part = jnp.sum(moe_grad * middle * scale, axis=0)
    swapped_grad = lax.dynamic_slice(
        grads_all, (mirror_index * row_count + micro_rows, my_columns), (micro_rows, slice_width)
    )
    grad_slice = jnp.concatenate([cotangent[:micro_rows], swapped_grad], axis=0).astype(f32)
    inner = gain_slice * moe_grad
    middle_grad, middle_low = turn(middle, scale, inner, grad_slice, 11)
    out_grad_part = dot_first(middle_low, heads_low).astype(low)
    heads_grad = jnp.dot(middle_low, wo_all, preferred_element_type=f32).astype(low)
    delta = jnp.sum(
        (heads_grad.astype(f32) * head_out).reshape(micro_count, micro_rows, query_local, head_width),
        axis=3,
    ).transpose(0, 2, 1).reshape(micro_count * query_local, 1, micro_rows)
    pieces = [gain_moe_part, router_part.reshape(-1)]
    length = sum(piece.shape[0] for piece in pieces)
    part_rows = -(-length // (shard_count * 1024)) * 8
    flat = jnp.concatenate(
        pieces + [jnp.zeros((shard_count * part_rows * 128 - length,), f32)]
    ).reshape(shard_count, part_rows, 128)
    query_pre_low, gain_query_part, sides, out_sum, w_out_grad, summed = attend_back(
        query_low, query_pre, query_gain, cosine_lookup, turned_sine, keys_values, starts, log_total,
        delta, heads_grad, flat, out_part, out_grad_part, nz, 12,
    )
    block_out = (middle + out_sum).astype(low)
    sides = reduce_rows(sides, nz, 14)

    def shape_keys(key_raw, key_gain):
        return rotary_apply(root_mean_norm(key_raw, key_gain), cosine_lookup, sine_lookup)

    key_pre_grad, gain_key_part = jax.vjp(shape_keys, key_pre, key_norm_gain)[1](sides[:, :kv_width])
    key_pre_low = key_pre_grad.astype(low)
    value_pre_low = sides[:, kv_width:].astype(low)
    normed_part = (
        dot_last(query_pre_low, wq_all)
        + dot_last(key_pre_low, wk_all)
        + dot_last(value_pre_low, wv_all)
    ).astype(low)
    pre_low = jnp.concatenate([query_pre_low, key_pre_low, value_pre_low], axis=1)
    weight_part = dot_first(normed_low, pre_low).astype(low)
    gain_rows = slice_width // 128
    gains = jnp.concatenate(
        [jnp.zeros((slice_width,), f32), gain_query_part.reshape(-1), gain_key_part,
         jnp.zeros(((8 - gain_rows - 2) * 128,), f32)]
    ).reshape(8, 128)
    attn_gain = lax.dynamic_slice_in_dim(gain_attn, my_columns, slice_width)
    weight_grad, token_grad, block_out, gains, gate_acc, up_acc, down_acc = tail(
        gate_pre_low, up_pre_low, hidden_low, tokens, middle_grad, token_scale,
        attn_gain.reshape(1, slice_width), block_out, gains, rows_in, pair_grad, weight_part,
        normed_part, nz, 15,
    )
    summed = summed.reshape(shard_count, group_count, part_rows * 128).transpose(
        1, 0, 2
    ).reshape(group_count, shard_count * part_rows * 128)
    gains = gains.reshape(shard_count, group_count, 8, 128)
    return (
        block_out,
        token_grad,
        jnp.sum(gains[:, :, :gain_rows], axis=0).reshape(-1),
        weight_grad[:, :query_width],
        weight_grad[:, query_width : query_width + kv_width],
        weight_grad[:, query_width + kv_width :],
        w_out_grad,
        jnp.sum(gains[:, :, gain_rows], axis=(0, 1)),
        jnp.sum(gains[:, :, gain_rows + 1], axis=(0, 1)),
        summed[:, :slice_width].reshape(-1),
        summed[:, slice_width:length].reshape(router.shape),
        gate_acc[None],
        up_acc[None],
        down_acc[None],
    )


def solution(mesh):
    small = mesh.shape["fsdp"] * mesh.shape["tp"] <= 32 and mesh.shape["tp"] == 4
    return jax.shard_map(
        gathered_body if small else body,
        mesh=mesh,
        in_specs=(
            P("fsdp", "tp"),
            P("fsdp", "tp"),
            P("fsdp", None),
            P(None, "fsdp"),
            P(),
            P("fsdp", "tp"),
            P("fsdp", "tp"),
            P("fsdp", "tp"),
            P("fsdp", "tp"),
            P(),
            P(),
            P(),
            P(),
            P(("fsdp", "tp"), None, None),
            P(("fsdp", "tp"), None, None),
            P(("fsdp", "tp"), None, None),
        ),
        out_specs=(
            P("fsdp", "tp"),
            P("fsdp", "tp"),
            P(),
            P("fsdp", "tp"),
            P("fsdp", "tp"),
            P("fsdp", "tp"),
            P("fsdp", "tp"),
            P(),
            P(),
            P(),
            P(),
            P(("fsdp", "tp"), None, None),
            P(("fsdp", "tp"), None, None),
            P(("fsdp", "tp"), None, None),
        ),
        check_vma=False,
    )
```

```python
import functools
import math

import jax
import jax.numpy as jnp
from jax import lax
from jax.experimental import pallas as pl
from jax.experimental.pallas import tpu as pltpu
from jax.sharding import PartitionSpec as P

TOPK = 8
DOCS = 4


theta_base = 1000000.0
norm_eps = 1e-06
masked_score = -1e30
highest_precision = lax.Precision.HIGHEST


def root_mean_norm(row_block, gain_row):
    return (
        row_block
        * lax.rsqrt(jnp.mean(row_block * row_block, axis=-1, keepdims=True) + norm_eps)
        * gain_row
    )


def rotary_apply(row_block, cosine_lookup, sine_lookup):
    half_width = row_block.shape[-1] // 2
    turned = jnp.concatenate([-row_block[..., half_width:], row_block[..., :half_width]], axis=-1)
    return row_block * cosine_lookup + turned * sine_lookup


def rope_tables(positions, head_width):
    half_width = head_width // 2
    frequency = theta_base ** (
        -2.0 * jnp.arange(half_width, dtype=jnp.int32).astype(jnp.float32) / head_width
    )
    angles = positions.astype(jnp.float32)[:, None] * frequency[None, :]
    cosine_lookup = jnp.cos(angles)
    sine_lookup = jnp.sin(angles)
    return (
        jnp.concatenate([cosine_lookup, cosine_lookup], axis=-1),
        jnp.concatenate([sine_lookup, sine_lookup], axis=-1),
    )


def swiglu(gate_pre, up_pre):
    return jax.nn.silu(gate_pre) * up_pre


def dot_first(left_side, right_side):
    return lax.dot_general(
        left_side, right_side, (((0,), (0,)), ((), ())), preferred_element_type=jnp.float32
    )


def dot_last(left_side, right_side):
    return lax.dot_general(
        left_side, right_side, (((1,), (1,)), ((), ())), preferred_element_type=jnp.float32
    )


def gather_weights(w_query, key_weight, value_weight, w_out):
    return (
        lax.all_gather(w_query, "fsdp", axis=0, tiled=True),
        lax.all_gather(key_weight, "fsdp", axis=0, tiled=True),
        lax.all_gather(value_weight, "fsdp", axis=0, tiled=True),
        lax.all_gather(w_out, "fsdp", axis=0, tiled=True),
    )


def gather_keys(keys_low, values_low):
    return (
        lax.all_gather(keys_low, "fsdp", axis=0, tiled=True),
        lax.all_gather(values_low, "fsdp", axis=0, tiled=True),
    )


def send_rows(buffer):
    return lax.all_to_all(buffer, "fsdp", split_axis=0, concat_axis=0, tiled=True)


def return_rows(buffer):
    return lax.all_to_all(buffer, "fsdp", split_axis=0, concat_axis=0, tiled=True)


def to_heads(per_token, kv_local, group_width):
    token_count, head_total, head_width = per_token.shape
    grouped_heads = per_token.reshape(token_count, kv_local, group_width, head_width)
    return grouped_heads.transpose(1, 2, 0, 3).reshape(
        kv_local, group_width * token_count, head_width
    )


def to_tokens(per_head, group_width):
    kv_local, row_count, head_width = per_head.shape
    token_count = row_count // group_width
    grouped_heads = per_head.reshape(kv_local, group_width, token_count, head_width)
    return grouped_heads.transpose(2, 0, 1, 3).reshape(
        token_count, kv_local * group_width * head_width
    )


def key_block(keys_all, key_start, block_keys, kv_local, head_width):
    return lax.dynamic_slice_in_dim(keys_all, key_start, block_keys, 0).reshape(
        block_keys, kv_local, head_width
    )


def block_scores(queries, keys_part, key_start, query_index, query_start):
    head_width = queries.shape[-1]
    scores = jnp.einsum(
        "hrd,khd->hrk", queries, keys_part, preferred_element_type=jnp.float32
    ) * head_width ** (-0.5)
    key_index = key_start + jnp.arange(keys_part.shape[0])
    allowed = (key_index[None, :] >= query_start[:, None]) & (
        key_index[None, :] <= query_index[:, None]
    )
    return (jnp.where(allowed[None], scores, masked_score), allowed)


def attend_forward(queries, keys_all, values_all, query_index, query_start, block_keys):
    kv_local, row_count, head_width = queries.shape
    lowest_block = jnp.min(query_start) // block_keys
    highest_block = jnp.max(query_index) // block_keys + 1

    def visit_block(block_index, running):
        run_peak, run_total, run_acc = running
        key_start = block_index * block_keys
        keys_part = key_block(keys_all, key_start, block_keys, kv_local, head_width)
        values_part = key_block(values_all, key_start, block_keys, kv_local, head_width)
        scores, allowed = block_scores(queries, keys_part, key_start, query_index, query_start)
        new_peak = jnp.maximum(run_peak, jnp.max(scores, axis=-1))
        weights = jnp.where(allowed[None], jnp.exp(scores - new_peak[..., None]), 0.0)
        factor = jnp.exp(run_peak - new_peak)
        run_total = run_total * factor + jnp.sum(weights, axis=-1)
        run_acc = run_acc * factor[..., None] + jnp.einsum(
            "hrk,khd->hrd",
            weights.astype(jnp.bfloat16),
            values_part,
            preferred_element_type=jnp.float32,
        )
        return (new_peak, run_total, run_acc)

    start_state = (
        jnp.full((kv_local, row_count), masked_score, jnp.float32),
        jnp.zeros((kv_local, row_count), jnp.float32),
        jnp.zeros((kv_local, row_count, head_width), jnp.float32),
    )
    run_peak, run_total, run_acc = lax.fori_loop(
        lowest_block, highest_block, visit_block, start_state
    )
    return (run_acc / run_total[..., None], run_peak + jnp.log(run_total))


def attend_backward(
    queries,
    keys_all,
    values_all,
    query_index,
    query_start,
    block_keys,
    outputs,
    log_total,
    grad_low,
):
    kv_local, row_count, head_width = queries.shape
    key_count = keys_all.shape[0]
    score_scale = head_width ** (-0.5)
    row_delta = jnp.sum(grad_low.astype(jnp.float32) * outputs, axis=-1)
    lowest_block = jnp.min(query_start) // block_keys
    highest_block = jnp.max(query_index) // block_keys + 1

    def visit_block(block_index, running):
        query_acc, key_acc, value_acc = running
        key_start = block_index * block_keys
        keys_part = key_block(keys_all, key_start, block_keys, kv_local, head_width)
        values_part = key_block(values_all, key_start, block_keys, kv_local, head_width)
        scores, allowed = block_scores(queries, keys_part, key_start, query_index, query_start)
        prob_block = jnp.where(allowed[None], jnp.exp(scores - log_total[..., None]), 0.0)
        prob_grad = jnp.einsum(
            "hrd,khd->hrk", grad_low, values_part, preferred_element_type=jnp.float32
        )
        score_grad = (prob_block * (prob_grad - row_delta[..., None])).astype(jnp.bfloat16)
        query_acc = (
            query_acc
            + jnp.einsum("hrk,khd->hrd", score_grad, keys_part, preferred_element_type=jnp.float32)
            * score_scale
        )
        key_part = (
            jnp.einsum("hrk,hrd->khd", score_grad, queries, preferred_element_type=jnp.float32)
            * score_scale
        )
        value_part = jnp.einsum(
            "hrk,hrd->khd",
            prob_block.astype(jnp.bfloat16),
            grad_low,
            preferred_element_type=jnp.float32,
        )
        key_acc = lax.dynamic_update_slice_in_dim(
            key_acc, key_part.reshape(block_keys, kv_local * head_width), key_start, 0
        )
        value_acc = lax.dynamic_update_slice_in_dim(
            value_acc, value_part.reshape(block_keys, kv_local * head_width), key_start, 0
        )
        return (query_acc, key_acc, value_acc)

    start_state = (
        jnp.zeros((kv_local, row_count, head_width), jnp.float32),
        jnp.zeros((key_count, kv_local * head_width), jnp.float32),
        jnp.zeros((key_count, kv_local * head_width), jnp.float32),
    )
    return lax.fori_loop(lowest_block, highest_block, visit_block, start_state)


def body(
    tokens,
    cotangent,
    routes,
    doc_ids,
    gain_attn,
    w_query,
    key_weight,
    value_weight,
    w_out,
    gain_query,
    key_norm_gain,
    gain_moe,
    router,
    w_gate,
    w_up,
    w_down,
):
    shard_count = lax.axis_size("fsdp")
    group_count = lax.axis_size("tp")
    shard_index = lax.axis_index("fsdp")
    group_index = lax.axis_index("tp")
    full_tokens, full_grads = (
        lax.all_gather(tokens, "tp", axis=1, tiled=True),
        lax.all_gather(cotangent, "tp", axis=1, tiled=True),
    )
    slice_width = tokens.shape[1]
    model_width = full_tokens.shape[1]
    micro_count, micro_rows = doc_ids.shape
    head_width = gain_query.shape[0]
    query_local = w_query.shape[1] // head_width
    kv_local = key_weight.shape[1] // head_width
    group_width = query_local // kv_local
    expert_total = router.shape[1]
    capacity = max(2, 2 * micro_rows * TOPK // expert_total)
    slot_total = shard_count * capacity
    pair_total = micro_rows * TOPK
    block_keys = micro_rows * math.gcd(shard_count, max(1, 512 // micro_rows))
    doc_range = jnp.arange(DOCS)
    expert_range = jnp.arange(expert_total)
    local_counts = jnp.sum((doc_ids[:, :, None] == doc_range).astype(jnp.float32), axis=1)
    doc_totals = lax.psum(local_counts, "fsdp")
    doc_begin = (jnp.cumsum(doc_totals, axis=1) - doc_totals).astype(jnp.int32)
    gate_expert = w_gate[0]
    up_expert = w_up[0]
    down_expert = w_down[0]
    router_wide = router.astype(jnp.float32)
    query_acc = jnp.zeros((model_width, query_local * head_width), jnp.float32)
    key_acc = jnp.zeros((model_width, kv_local * head_width), jnp.float32)
    value_acc = jnp.zeros((model_width, kv_local * head_width), jnp.float32)
    out_acc = jnp.zeros((model_width, query_local * head_width), jnp.float32)
    gate_acc = jnp.zeros(gate_expert.shape, jnp.float32)
    up_acc = jnp.zeros(up_expert.shape, jnp.float32)
    down_acc = jnp.zeros(down_expert.shape, jnp.float32)
    router_acc = jnp.zeros(router.shape, jnp.float32)
    gain_attn_acc = jnp.zeros(gain_attn.shape, jnp.float32)
    gain_moe_acc = jnp.zeros(gain_moe.shape, jnp.float32)
    gain_query_acc = jnp.zeros(gain_query.shape, jnp.float32)
    gain_key_acc = jnp.zeros(key_norm_gain.shape, jnp.float32)
    out_parts = []
    grad_parts = []
    for micro_index in range(micro_count):
        row_begin = micro_index * micro_rows
        token_block = full_tokens[row_begin : row_begin + micro_rows].astype(jnp.float32)
        ids_now = doc_ids[micro_index]
        query_index = shard_index * micro_rows + jnp.arange(micro_rows)
        query_start = jnp.sum(
            jnp.where(ids_now[:, None] == doc_range, doc_begin[micro_index][None, :], 0), axis=1
        )
        cosine_lookup, sine_lookup = rope_tables(query_index - query_start, head_width)
        gathered = gather_weights(w_query, key_weight, value_weight, w_out)
        normed, norm_pull = jax.vjp(root_mean_norm, token_block, gain_attn)
        normed_reduced = normed.astype(jnp.bfloat16)
        query_pre = jnp.dot(normed_reduced, gathered[0], preferred_element_type=jnp.float32)
        key_before_norm = jnp.dot(normed_reduced, gathered[1], preferred_element_type=jnp.float32)
        value_reduced = jnp.dot(
            normed_reduced, gathered[2], preferred_element_type=jnp.float32
        ).astype(jnp.bfloat16)

        def shape_heads(query_raw, key_raw, query_gain, key_gain):
            query_heads = rotary_apply(
                root_mean_norm(query_raw.reshape(micro_rows, query_local, head_width), query_gain),
                cosine_lookup[:, None, :],
                sine_lookup[:, None, :],
            )
            key_heads = rotary_apply(
                root_mean_norm(key_raw.reshape(micro_rows, kv_local, head_width), key_gain),
                cosine_lookup[:, None, :],
                sine_lookup[:, None, :],
            )
            return (query_heads, key_heads)

        (query_heads, key_heads), heads_pull = jax.vjp(
            shape_heads, query_pre, key_before_norm, gain_query, key_norm_gain
        )
        queries = to_heads(query_heads.astype(jnp.bfloat16), kv_local, group_width)
        keys_low = key_heads.reshape(micro_rows, kv_local * head_width).astype(jnp.bfloat16)
        keys_all, values_all = gather_keys(keys_low, value_reduced)
        row_index = jnp.tile(query_index, group_width)
        row_start = jnp.tile(query_start, group_width)
        head_out, log_total = attend_forward(
            queries, keys_all, values_all, row_index, row_start, block_keys
        )
        heads_low = to_tokens(head_out, group_width).astype(jnp.bfloat16)
        attn_part = dot_last(heads_low, gathered[3])
        middle = token_block + lax.psum(attn_part.astype(jnp.bfloat16), "tp").astype(jnp.float32)
        moe_normed, moe_pull = jax.vjp(root_mean_norm, middle, gain_moe)
        moe_low = moe_normed.astype(jnp.bfloat16)
        logits = jnp.dot(moe_low, router, preferred_element_type=jnp.float32)
        routes_now = routes[row_begin : row_begin + micro_rows]
        route_match = routes_now[:, :, None] == expert_range
        chosen = jnp.sum(jnp.where(route_match, logits[:, None, :], 0.0), axis=-1)
        gate_weights, softmax_pull = jax.vjp(jax.nn.softmax, chosen)
        mine = routes_now % group_count == group_index
        pair_target = jnp.where(mine, routes_now // group_count, shard_count).reshape(pair_total)
        target_hot = (pair_target[:, None] == jnp.arange(shard_count)).astype(jnp.int32)
        pair_rank = jnp.sum((jnp.cumsum(target_hot, axis=0) - target_hot) * target_hot, axis=1)
        pair_slot = jnp.where(
            pair_target < shard_count, pair_target * capacity + pair_rank, slot_total
        )
        slot_pair = (
            jnp.full((slot_total + 1,), pair_total, jnp.int32)
            .at[pair_slot]
            .set(jnp.arange(pair_total, dtype=jnp.int32))[:slot_total]
        )
        slot_token = slot_pair // TOPK
        slot_grid = pair_slot.reshape(micro_rows, TOPK)
        padded_low = jnp.concatenate([moe_low, jnp.zeros((1, model_width), jnp.bfloat16)], axis=0)
        received = send_rows(
            padded_low[slot_token].reshape(shard_count, capacity, model_width)
        ).reshape(slot_total, model_width)
        gate_pre = jnp.dot(received, gate_expert, preferred_element_type=jnp.float32)
        up_pre = jnp.dot(received, up_expert, preferred_element_type=jnp.float32)
        hidden, swiglu_pull = jax.vjp(swiglu, gate_pre, up_pre)
        hidden_low = hidden.astype(jnp.bfloat16)
        expert_out = jnp.dot(hidden_low, down_expert, preferred_element_type=jnp.float32).astype(
            jnp.bfloat16
        )
        returned = return_rows(expert_out.reshape(shard_count, capacity, model_width)).reshape(
            slot_total, model_width
        )
        padded_out = jnp.concatenate([returned, jnp.zeros((1, model_width), jnp.bfloat16)], axis=0)
        moe_part = jnp.zeros((micro_rows, model_width), jnp.float32)
        for pick_index in range(TOPK):
            moe_part = moe_part + gate_weights[:, pick_index : pick_index + 1] * padded_out[
                slot_grid[:, pick_index]
            ].astype(jnp.float32)
        moe_share = lax.psum_scatter(
            moe_part.astype(jnp.bfloat16), "tp", scatter_dimension=1, tiled=True
        ).astype(jnp.float32)
        middle_slice = lax.dynamic_slice_in_dim(middle, group_index * slice_width, slice_width, 1)
        out_parts.append((middle_slice + moe_share).astype(jnp.bfloat16))
        grad_block = full_grads[row_begin : row_begin + micro_rows].astype(jnp.float32)
        gate_columns = []
        for pick_index in range(TOPK):
            gate_columns.append(
                jnp.sum(
                    grad_block * padded_out[slot_grid[:, pick_index]].astype(jnp.float32), axis=1
                )
            )
        gates_grad = jnp.stack(gate_columns, axis=1)
        flat_gates = jnp.concatenate(
            [gate_weights.reshape(pair_total), jnp.zeros((1,), jnp.float32)]
        )
        padded_grad = jnp.concatenate(
            [grad_block, jnp.zeros((1, model_width), jnp.float32)], axis=0
        )
        send_grad = (padded_grad[slot_token] * flat_gates[slot_pair][:, None]).astype(jnp.bfloat16)
        received_grad = send_rows(send_grad.reshape(shard_count, capacity, model_width)).reshape(
            slot_total, model_width
        )
        hidden_grad = dot_last(received_grad, down_expert)
        down_acc = down_acc + dot_first(hidden_low, received_grad)
        gate_pre_grad, up_pre_grad = swiglu_pull(hidden_grad)
        gate_pre_low = gate_pre_grad.astype(jnp.bfloat16)
        up_pre_low = up_pre_grad.astype(jnp.bfloat16)
        gate_acc = gate_acc + dot_first(received, gate_pre_low)
        up_acc = up_acc + dot_first(received, up_pre_low)
        rows_back = (dot_last(gate_pre_low, gate_expert) + dot_last(up_pre_low, up_expert)).astype(
            jnp.bfloat16
        )
        back_rows = return_rows(rows_back.reshape(shard_count, capacity, model_width)).reshape(
            slot_total, model_width
        )
        padded_back = jnp.concatenate(
            [back_rows, jnp.zeros((1, model_width), jnp.bfloat16)], axis=0
        )
        moe_grad = jnp.zeros((micro_rows, model_width), jnp.float32)
        for pick_index in range(TOPK):
            moe_grad = moe_grad + padded_back[slot_grid[:, pick_index]].astype(jnp.float32)
        (chosen_grad,) = softmax_pull(gates_grad)
        logit_grad = jnp.sum(jnp.where(route_match, chosen_grad[:, :, None], 0.0), axis=1)
        router_acc = router_acc + lax.dot_general(
            moe_low.astype(jnp.float32),
            logit_grad,
            (((0,), (0,)), ((), ())),
            precision=highest_precision,
        )
        moe_grad = moe_grad + lax.dot_general(
            logit_grad, router_wide, (((1,), (1,)), ((), ())), precision=highest_precision
        )
        middle_part, gain_moe_part = moe_pull(moe_grad)
        gain_moe_acc = gain_moe_acc + gain_moe_part
        middle_grad = grad_block + lax.psum(middle_part.astype(jnp.bfloat16), "tp").astype(
            jnp.float32
        )
        middle_low = middle_grad.astype(jnp.bfloat16)
        gathered_back = gather_weights(w_query, key_weight, value_weight, w_out)
        out_acc = out_acc + dot_first(middle_low, heads_low)
        heads_grad = jnp.dot(middle_low, gathered_back[3], preferred_element_type=jnp.float32)
        grad_low = to_heads(
            heads_grad.reshape(micro_rows, query_local, head_width).astype(jnp.bfloat16),
            kv_local,
            group_width,
        )
        query_side, key_side_all, value_side_all = attend_backward(
            queries,
            keys_all,
            values_all,
            row_index,
            row_start,
            block_keys,
            head_out,
            log_total,
            grad_low,
        )
        key_side, value_side = (
            lax.psum_scatter(
                key_side_all.astype(jnp.bfloat16), "fsdp", scatter_dimension=0, tiled=True
            ).astype(jnp.float32),
            lax.psum_scatter(
                value_side_all.astype(jnp.bfloat16), "fsdp", scatter_dimension=0, tiled=True
            ).astype(jnp.float32),
        )
        query_pre_grad, key_pre_grad, gain_query_part, gain_key_part = heads_pull(
            (
                to_tokens(query_side, group_width).reshape(micro_rows, query_local, head_width),
                key_side.reshape(micro_rows, kv_local, head_width),
            )
        )
        gain_query_acc = gain_query_acc + gain_query_part
        gain_key_acc = gain_key_acc + gain_key_part
        query_pre_low = query_pre_grad.astype(jnp.bfloat16)
        key_pre_low = key_pre_grad.astype(jnp.bfloat16)
        value_pre_low = value_side.astype(jnp.bfloat16)
        query_acc = query_acc + dot_first(normed_reduced, query_pre_low)
        key_acc = key_acc + dot_first(normed_reduced, key_pre_low)
        value_acc = value_acc + dot_first(normed_reduced, value_pre_low)
        normed_grad = (
            dot_last(query_pre_low, gathered_back[0])
            + dot_last(key_pre_low, gathered_back[1])
            + dot_last(value_pre_low, gathered_back[2])
        )
        token_part, gain_attn_part = norm_pull(normed_grad)
        gain_attn_acc = gain_attn_acc + gain_attn_part
        token_share = lax.psum_scatter(
            token_part.astype(jnp.bfloat16), "tp", scatter_dimension=1, tiled=True
        ).astype(jnp.float32)
        grad_slice = lax.dynamic_slice_in_dim(
            middle_grad, group_index * slice_width, slice_width, 1
        )
        grad_parts.append((grad_slice + token_share).astype(jnp.bfloat16))
    weight_sums = (
        lax.psum_scatter(
            query_acc.astype(jnp.bfloat16), "fsdp", scatter_dimension=0, tiled=True
        ).astype(jnp.float32),
        lax.psum_scatter(
            key_acc.astype(jnp.bfloat16), "fsdp", scatter_dimension=0, tiled=True
        ).astype(jnp.float32),
        lax.psum_scatter(
            value_acc.astype(jnp.bfloat16), "fsdp", scatter_dimension=0, tiled=True
        ).astype(jnp.float32),
        lax.psum_scatter(
            out_acc.astype(jnp.bfloat16), "fsdp", scatter_dimension=0, tiled=True
        ).astype(jnp.float32),
    )
    small_sums = lax.psum(
        (gain_attn_acc, gain_query_acc, gain_key_acc, gain_moe_acc, router_acc), ("fsdp", "tp")
    )
    return (
        jnp.concatenate(out_parts, axis=0),
        jnp.concatenate(grad_parts, axis=0),
        small_sums[0],
        weight_sums[0],
        weight_sums[1],
        weight_sums[2],
        weight_sums[3],
        small_sums[1],
        small_sums[2],
        small_sums[3],
        small_sums[4],
        gate_acc[None],
        up_acc[None],
        down_acc[None],
    )


MESH = pl.DeviceIdType.MESH


def place():
    f = lax.axis_index("fsdp")
    t = lax.axis_index("tp")
    return f // 2, f % 2, t // 2, t % 2


def device(z, x, y, c):
    return (z * 2 + x, y * 2 + c)


def greet(devices):
    barrier = pltpu.get_barrier_semaphore()
    total = 0
    for valid, where in devices:
        if valid is None:
            pl.semaphore_signal(barrier, inc=1, device_id=where, device_id_type=MESH)
            total = total + 1
        else:
            @pl.when(valid)
            def _():
                pl.semaphore_signal(barrier, inc=1, device_id=where, device_id_type=MESH)
            total = total + valid.astype(jnp.int32)
    pl.semaphore_wait(barrier, total)


def remote(src, dst, send, recv, where):
    return pltpu.make_async_remote_copy(
        src_ref=src, dst_ref=dst, send_sem=send, recv_sem=recv, device_id=where, device_id_type=MESH
    )


def gather_all_kernel(nz, x_ref, o_ref, lsem, s_p, s_u, s_d, s_x, s_y, s_dx, s_dy,
                      r_z, r_x, r_y, r_dx, r_dy, r_p):
    z, x, y, c = place()
    rows, cols = x_ref.shape
    half = rows // 2
    partner = device(z, x, y, 1 - c)
    xn = device(z, 1 - x, y, c)
    yn = device(z, x, 1 - y, c)
    up = device(z + 1, x, y, c)
    down = device(z - 1, x, y, c)
    greet([(None, partner), (None, xn), (None, yn), (z < nz - 1, up), (z > 0, down)])

    def block(zz, xx, yy, cc, part=None):
        start = (zz * 2 + xx) * rows
        size = rows
        if part is not None:
            start = start + part * half
            size = half
        return o_ref.at[pl.ds(pl.multiple_of(start, half), size),
                        pl.ds(pl.multiple_of((yy * 2 + cc) * cols, cols), cols)]

    own = pltpu.make_async_copy(x_ref, block(z, x, y, c), lsem)
    own.start()

    items = [(0, 0)]
    for dist in range(1, nz):
        items += [(dist, -1), (dist, 1)]

    def guard(item, fn):
        dist, side = item
        zz = z + side * dist
        if dist == 0:
            fn(zz)
        else:
            pl.when((zz >= 0) & (zz < nz))(lambda: fn(zz))

    def c_z(zz, src):
        dst = block(zz, x, y, c)
        return (remote(src, dst, s_u.at[zz], r_z.at[zz], up),
                remote(src, dst, s_d.at[zz], r_z.at[zz], down))

    def c_xy(zz, src):
        dst = block(zz, x, y, c)
        return (remote(src, dst, s_x.at[zz], r_x.at[zz], xn),
                remote(src, dst, s_y.at[zz], r_y.at[zz], yn))

    def c_p(zz, rel, src=None):
        xx = 1 - x if rel in (1, 3, 4) else x
        yy = 1 - y if rel in (2, 3, 4) else y
        part = {3: 0, 4: 1}.get(rel)
        dst = block(zz, xx, yy, c, part)
        k = zz * 5 + rel
        return remote(dst if src is None else src, dst, s_p.at[k], r_p.at[k], partner)

    def w_p(zz, rel):
        xx = 1 - x if rel in (1, 3, 4) else x
        yy = 1 - y if rel in (2, 3, 4) else y
        part = {3: 0, 4: 1}.get(rel)
        dst = block(zz, xx, yy, 1 - c, part)
        k = zz * 5 + rel
        return remote(dst, dst, s_p.at[k], r_p.at[k], partner)

    def c_diag(zz):
        a = block(zz, 1 - x, y, c, 0)
        b = block(zz, x, 1 - y, c, 1)
        return (remote(a, a, s_dy.at[zz], r_dy.at[zz], yn),
                remote(b, b, s_dx.at[zz], r_dx.at[zz], xn))

    def stage_a(item):
        dist, side = item

        def run(zz):
            src = x_ref if dist == 0 else block(zz, x, y, c)
            cu, cd = c_z(zz, src)
            if dist:
                cu.wait_recv()
            if side <= 0:
                pl.when(z < nz - 1)(cu.start)
            if dist == 0 or side > 0:
                pl.when(z > 0)(cd.start)
            for cc in c_xy(zz, src):
                cc.start()
            c_p(zz, 0, src).start()

        guard(item, run)

    def stage_b(item):
        def run(zz):
            cx, cy = c_xy(zz, block(zz, x, y, c))
            dy, dx = c_diag(zz)
            cx.wait_recv()
            dy.start()
            c_p(zz, 1).start()
            cy.wait_recv()
            dx.start()
            c_p(zz, 2).start()

        guard(item, run)

    def stage_c(item):
        def run(zz):
            dy, dx = c_diag(zz)
            dy.wait_recv()
            c_p(zz, 3).start()
            dx.wait_recv()
            c_p(zz, 4).start()

        guard(item, run)

    count = len(items)
    for k in range(count + 2):
        if k < count:
            stage_a(items[k])
        if 0 <= k - 1 < count:
            stage_b(items[k - 1])
        if 0 <= k - 2 < count:
            stage_c(items[k - 2])

    def finish(zz, carry):
        for rel in range(5):
            w_p(zz, rel).wait_recv()
            c_p(zz, rel).wait_send()
        cu, cd = c_z(zz, block(zz, x, y, c))
        pl.when((zz <= z) & (z < nz - 1))(cu.wait_send)
        pl.when((zz >= z) & (z > 0))(cd.wait_send)
        for cc in c_xy(zz, block(zz, x, y, c)) + c_diag(zz):
            cc.wait_send()
        return carry

    lax.fori_loop(0, nz, finish, 0)
    own.wait()


def gather_all(block, nz, collective_id):
    rows, cols = block.shape
    dma = pltpu.SemaphoreType.DMA
    return pl.pallas_call(
        functools.partial(gather_all_kernel, nz),
        out_shape=jax.ShapeDtypeStruct((rows * nz * 2, cols * 4), block.dtype),
        in_specs=[pl.BlockSpec(memory_space=pl.ANY)],
        out_specs=pl.BlockSpec(memory_space=pl.ANY),
        scratch_shapes=[dma] + [dma((5 * nz,))] + [dma((nz,))] * 6 + [dma((nz,))] * 5 + [dma((5 * nz,))],
        compiler_params=pltpu.CompilerParams(collective_id=collective_id, has_side_effects=True),
        name="gather_all",
    )(block)


def scatter_all_kernel(nz, p_ref, o_ref, w, lp, rx, rxd, ry, ryd, rz,
                       s_l, s_p, r_p, s_x, s_y, s_dx, s_dy, s_z, r_x, r_y, r_dx, r_dy, r_z):
    z, x, y, c = place()
    rows, cols = o_ref.shape
    half = rows // 2
    partner = device(z, x, y, 1 - c)
    xn = device(z, 1 - x, y, c)
    yn = device(z, x, 1 - y, c)
    up = device(z + 1, x, y, c)
    down = device(z - 1, x, y, c)
    greet([(None, partner), (None, xn), (None, yn), (z < nz - 1, up), (z > 0, down)])
    chunk = 64

    def block(zz, rel, cc):
        xx = 1 - x if rel in (1, 3) else x
        yy = 1 - y if rel in (2, 3) else y
        return p_ref.at[pl.ds(pl.multiple_of((zz * 2 + xx) * rows, rows), rows),
                        pl.ds(pl.multiple_of((yy * 2 + cc) * cols, cols), cols)]

    items = []
    for dist in range(nz - 1, 0, -1):
        items += [(dist, -1), (dist, 1)]
    items += [(0, 0)]

    def guard(item, fn):
        dist, side = item
        zz = z + side * dist
        if dist == 0:
            fn(zz)
        else:
            pl.when((zz >= 0) & (zz < nz))(lambda: fn(zz))

    def c_p(zz, rel):
        k = zz * 4 + rel
        return remote(block(zz, rel, 1 - c), lp.at[zz, rel], s_p.at[k], r_p.at[k], partner)

    def c_l(zz, rel):
        return pltpu.make_async_copy(block(zz, rel, c), w.at[zz, rel], s_l.at[zz * 4 + rel])

    def c_diag(zz):
        return (remote(w.at[zz, 3, pl.ds(0, half)], rxd.at[zz], s_dx.at[zz], r_dx.at[zz], xn),
                remote(w.at[zz, 3, pl.ds(half, half)], ryd.at[zz], s_dy.at[zz], r_dy.at[zz], yn))

    def c_xy(zz):
        return (remote(w.at[zz, 1], rx.at[zz], s_x.at[zz], r_x.at[zz], xn),
                remote(w.at[zz, 2], ry.at[zz], s_y.at[zz], r_y.at[zz], yn))

    def c_z(zz, slot, where):
        return remote(w.at[zz, 0], rz.at[slot], s_z.at[zz], r_z.at[slot], where)

    def add(dst, srcs, start, count):
        def step(i, carry):
            off = pl.multiple_of(i * chunk, chunk)
            here = pl.ds(pl.multiple_of(start + off, chunk), chunk)
            total = dst[here, :].astype(jnp.float32)
            for src in srcs:
                total = total + src[pl.ds(off, chunk), :].astype(jnp.float32)
            dst[here, :] = total.astype(dst.dtype)
            return carry
        lax.fori_loop(0, count // chunk, step, 0)

    def stage_0(item):
        def run(zz):
            for rel in (3, 1, 2, 0):
                c_p(zz, rel).start()
                c_l(zz, rel).start()
        guard(item, run)

    def stage_d(item):
        def run(zz):
            for rel in (3, 1, 2, 0):
                c_p(zz, rel).wait_recv()
                c_l(zz, rel).wait()
                add(w.at[zz, rel], [lp.at[zz, rel]], 0, rows)
                if rel == 3:
                    for cc in c_diag(zz):
                        cc.start()
        guard(item, run)

    def stage_e(item):
        def run(zz):
            dx, dy = c_diag(zz)
            cx, cy = c_xy(zz)
            dy.wait_recv()
            add(w.at[zz, 1], [ryd.at[zz]], half, half)
            cx.start()
            dx.wait_recv()
            add(w.at[zz, 2], [rxd.at[zz]], 0, half)
            cy.start()
        guard(item, run)

    def stage_f(item):
        dist, side = item

        def run(zz):
            cx, cy = c_xy(zz)
            cx.wait_recv()
            cy.wait_recv()
            if dist:
                add(w.at[zz, 0], [rx.at[zz], ry.at[zz]], 0, rows)
                has = z > 0 if side > 0 else z < nz - 1
                cz = c_z(zz, zz, up if side > 0 else down)

                @pl.when(has)
                def _():
                    cz.wait_recv()
                    add(w.at[zz, 0], [rz.at[zz]], 0, rows)
                if side > 0:
                    cz.start()
                else:
                    if dist == 1:
                        c_z(zz, nz, down).start()
                    else:
                        cz.start()
            else:
                below, above = c_z(zz, zz, up), c_z(zz, nz, down)

                def total(refs):
                    def step(i, carry):
                        here = pl.ds(pl.multiple_of(i * chunk, chunk), chunk)
                        acc = w[zz, 0, here, :].astype(jnp.float32)
                        for ref in refs:
                            acc = acc + ref[here, :].astype(jnp.float32)
                        o_ref[here, :] = acc
                        return carry
                    lax.fori_loop(0, rows // chunk, step, 0)

                pl.when(z > 0)(below.wait_recv)
                pl.when(z < nz - 1)(above.wait_recv)
                pl.when(z == 0)(lambda: total([rx.at[zz], ry.at[zz], rz.at[nz]]))
                pl.when(z == nz - 1)(lambda: total([rx.at[zz], ry.at[zz], rz.at[zz]]))
                pl.when((z > 0) & (z < nz - 1))(
                    lambda: total([rx.at[zz], ry.at[zz], rz.at[zz], rz.at[nz]]))
        guard(item, run)

    for item in items:
        stage_0(item)
    count = len(items)
    for k in range(count + 2):
        if k < count:
            stage_d(items[k])
        if 0 <= k - 1 < count:
            stage_e(items[k - 1])
        if 0 <= k - 2 < count:
            stage_f(items[k - 2])

    def finish(zz, carry):
        for rel in range(4):
            c_p(zz, rel).wait_send()
        for cc in c_diag(zz) + c_xy(zz):
            cc.wait_send()
        pl.when(zz != z)(c_z(zz, zz, up).wait_send)
        return carry

    lax.fori_loop(0, nz, finish, 0)


def scatter_all(partial, nz, collective_id):
    rows, cols = partial.shape[0] // (2 * nz), partial.shape[1] // 4
    half = rows // 2
    dma = pltpu.SemaphoreType.DMA
    kind = partial.dtype
    vm = pltpu.VMEM
    return pl.pallas_call(
        functools.partial(scatter_all_kernel, nz),
        out_shape=jax.ShapeDtypeStruct((rows, cols), jnp.float32),
        in_specs=[pl.BlockSpec(memory_space=pl.ANY)],
        out_specs=pl.BlockSpec(memory_space=pltpu.VMEM),
        scratch_shapes=[vm((nz, 4, rows, cols), kind), vm((nz, 4, rows, cols), kind),
                        vm((nz, rows, cols), kind), vm((nz, half, cols), kind),
                        vm((nz, rows, cols), kind), vm((nz, half, cols), kind),
                        vm((nz + 1, rows, cols), kind)]
        + [dma((4 * nz,))] * 3 + [dma((nz,))] * 5 + [dma((nz,))] * 4 + [dma((nz + 1,))],
        compiler_params=pltpu.CompilerParams(collective_id=collective_id, has_side_effects=True,
                                             vmem_limit_bytes=62 << 20),
        name="scatter_all",
    )(partial)


def z_items(nz, near_first):
    items = [(0, 0)] if near_first else []
    order = range(1, nz) if near_first else range(nz - 1, 0, -1)
    for dist in order:
        items += [(dist, -1), (dist, 1)]
    return items if near_first else items + [(0, 0)]


def z_guard(item, z, nz, fn):
    dist, side = item
    zz = z + side * dist
    if dist == 0:
        fn(zz)
    else:
        pl.when((zz >= 0) & (zz < nz))(lambda: fn(zz))


def gather_rows_kernel(nz, count, columns, *refs):
    total = count + columns
    srcs, refs = refs[:total], refs[total:]
    outs, refs = refs[:total], refs[total:]
    wide, refs = refs[: min(columns, 1)], refs[min(columns, 1) :]
    lsem, s_u, s_d, s_x, r_z, r_x, s_c, r_c, s_w, r_w = refs
    z, x, y, c = place()
    xn, up, down = device(z, 1 - x, y, c), device(z + 1, x, y, c), device(z - 1, x, y, c)
    partner, yn = device(z, x, y, 1 - c), device(z, x, 1 - y, c)
    wanted = [(None, xn), (z < nz - 1, up), (z > 0, down)]
    greet(wanted + [(None, partner), (None, yn), (None, device(nz - 1 - z, x, y, c))] * min(columns, 1))

    def block(n, zz, xx):
        rows = srcs[n].shape[0]
        return outs[n].at[pl.ds(pl.multiple_of((zz * 2 + xx) * rows, rows), rows)]

    own = [(srcs[n], block(n, z, x)) for n in range(count)]
    column_copies, swaps = [], []
    if columns:
        mirror = device(nz - 1 - z, x, y, c)
        first, out = outs[count], wide[0]
        rows, cols = first.shape
        top, bottom = pl.ds(0, rows // 2), pl.ds(rows // 2, rows // 2)
        for n in range(columns):
            src, dst = srcs[count + n], outs[count + n]
            swaps.append(remote(src.at[bottom], dst.at[bottom], s_w.at[n], r_w.at[n], mirror))
            dst[top, :] = src[top, :]

        def column(yy):
            return out.at[:, pl.ds(pl.multiple_of((yy * 2 + c) * cols, cols), cols)]

        column_copies = [
            remote(first, column(y), s_c.at[0], r_c.at[0], yn),
            remote(first, column(y), s_c.at[1], r_c.at[1], partner),
            remote(column(1 - y), column(1 - y), s_c.at[2], r_c.at[2], partner),
        ]
        last = pltpu.make_async_copy(first, column(y), lsem.at[total])
    own = [pltpu.make_async_copy(src, dst, lsem.at[n]) for n, (src, dst) in enumerate(own)]
    for copy in swaps + own:
        copy.start()

    def copies(n, zz, src):
        dst = block(n, zz, x)
        k = n * nz + zz
        return (remote(src, dst, s_u.at[k], r_z.at[k], up),
                remote(src, dst, s_d.at[k], r_z.at[k], down),
                remote(src, dst, s_x.at[k], r_x.at[k], xn))

    items = z_items(nz, True)
    for item in items:
        dist, side = item

        def run(zz):
            for n in range(count):
                src = srcs[n] if dist == 0 else block(n, zz, x)
                cu, cd, cx = copies(n, zz, src)
                if dist:
                    cu.wait_recv()
                if side <= 0:
                    pl.when(z < nz - 1)(cu.start)
                if side > 0 or dist == 0:
                    pl.when(z > 0)(cd.start)
                cx.start()

        z_guard(item, z, nz, run)
        if columns and item == items[-1]:
            swaps[0].wait_recv()
            column_copies[0].start()
            column_copies[1].start()
            last.start()
        if columns and item == items[-1]:
            column_copies[0].wait_recv()
            column_copies[2].start()

    def finish(zz, carry):
        for n in range(count):
            cu, cd, cx = copies(n, zz, block(n, zz, x))
            cx.wait_recv()
            cx.wait_send()
            pl.when((zz <= z) & (z < nz - 1))(cu.wait_send)
            pl.when((zz >= z) & (z > 0))(cd.wait_send)
        return carry

    lax.fori_loop(0, nz, finish, 0)
    for copy in own:
        copy.wait()
    if columns:
        column_copies[0].wait_send()
        column_copies[1].wait()
        column_copies[2].wait()
        last.wait()
        swaps[0].wait_send()
        for copy in swaps[1:]:
            copy.wait()


def gather_rows(blocks, nz, collective_id, swapped=()):
    count, columns = len(blocks), len(swapped)
    dma = pltpu.SemaphoreType.DMA
    any_space = pl.BlockSpec(memory_space=pl.ANY)
    vmem = pl.BlockSpec(memory_space=pltpu.VMEM)
    shapes = [
        jax.ShapeDtypeStruct((b.shape[0] * nz * 2,) + b.shape[1:], b.dtype) for b in blocks
    ] + [jax.ShapeDtypeStruct(b.shape, b.dtype) for b in swapped]
    if columns:
        rows, cols = swapped[0].shape
        shapes.append(jax.ShapeDtypeStruct((rows, cols * 4), swapped[0].dtype))
    total = count + columns
    return pl.pallas_call(
        functools.partial(gather_rows_kernel, nz, count, columns),
        out_shape=shapes,
        in_specs=[vmem] * total,
        out_specs=[any_space] * count + [vmem] * columns + [any_space] * min(columns, 1),
        scratch_shapes=[dma((total + 1,))] + [dma((count * nz,))] * 5 + [dma((3,))] * 2
        + [dma((max(columns, 1),))] * 2,
        compiler_params=pltpu.CompilerParams(collective_id=collective_id, has_side_effects=True,
                                             vmem_limit_bytes=62 << 20),
        name="gather_rows",
    )(*blocks, *swapped)


def swap_back_kernel(nz, *refs):
    count = (len(refs) - 2) // 2
    srcs, outs = refs[:count], refs[count : 2 * count]
    s, r = refs[2 * count :]
    z, x, y, c = place()
    mirror = device(nz - 1 - z, x, y, c)
    greet([(None, mirror)])
    copies = [remote(src, out, s.at[n], r.at[n], mirror)
              for n, (src, out) in enumerate(zip(srcs, outs))]
    for copy in copies:
        copy.start()
    for copy in copies:
        copy.wait()


def swap_back(blocks, nz, collective_id):
    count = len(blocks)
    dma = pltpu.SemaphoreType.DMA
    any_space = pl.BlockSpec(memory_space=pl.ANY)
    return pl.pallas_call(
        functools.partial(swap_back_kernel, nz),
        out_shape=[jax.ShapeDtypeStruct(b.shape, b.dtype) for b in blocks],
        in_specs=[any_space] * count,
        out_specs=[any_space] * count,
        scratch_shapes=[dma((count,))] * 2,
        compiler_params=pltpu.CompilerParams(collective_id=collective_id, has_side_effects=True),
        name="swap_back",
    )(*blocks)


def add_blocks(dst, srcs, start, count, out=None, chunk=64):
    target = dst if out is None else out

    def step(i, carry):
        off = pl.multiple_of(i * chunk, chunk)
        here = pl.ds(pl.multiple_of(start + off, chunk), chunk)
        total = dst[here, :].astype(jnp.float32)
        for src in srcs:
            total = total + src[pl.ds(off, chunk), :].astype(jnp.float32)
        target[here, :] = total.astype(target.dtype)
        return carry

    lax.fori_loop(0, count // chunk, step, 0)


def reduce_rows_kernel(nz, p_ref, o_ref, w, rx, rz, s_l, s_x, s_z, r_x, r_z):
    z, x, y, c = place()
    rows = o_ref.shape[0]
    xn, up, down = device(z, 1 - x, y, c), device(z + 1, x, y, c), device(z - 1, x, y, c)
    greet([(None, xn), (z < nz - 1, up), (z > 0, down)])

    def block(zz, xx):
        return p_ref.at[pl.ds(pl.multiple_of((zz * 2 + xx) * rows, rows), rows)]

    def c_x(zz):
        return remote(block(zz, 1 - x), rx.at[zz], s_x.at[zz], r_x.at[zz], xn)

    def c_l(zz):
        return pltpu.make_async_copy(block(zz, x), w.at[zz], s_l.at[zz])

    def c_z(zz, slot, where):
        return remote(w.at[zz], rz.at[slot], s_z.at[zz], r_z.at[slot], where)

    items = z_items(nz, False)

    def start(zz):
        c_x(zz).start()
        c_l(zz).start()

    for item in items:
        z_guard(item, z, nz, start)
    for item in items:
        dist, side = item

        def run(zz):
            c_l(zz).wait()
            c_x(zz).wait_recv()
            if dist:
                add_blocks(w.at[zz], [rx.at[zz]], 0, rows)
                cz = c_z(zz, zz, up if side > 0 else down)

                @pl.when(z > 0 if side > 0 else z < nz - 1)
                def _():
                    cz.wait_recv()
                    add_blocks(w.at[zz], [rz.at[zz]], 0, rows)

                (c_z(zz, nz, down) if side < 0 and dist == 1 else cz).start()
            else:
                pl.when(z > 0)(c_z(zz, zz, up).wait_recv)
                pl.when(z < nz - 1)(c_z(zz, nz, down).wait_recv)
                low, high = rz.at[zz], rz.at[nz]
                pl.when(z == 0)(lambda: add_blocks(w.at[zz], [rx.at[zz], high], 0, rows, o_ref))
                pl.when(z == nz - 1)(lambda: add_blocks(w.at[zz], [rx.at[zz], low], 0, rows, o_ref))
                pl.when((z > 0) & (z < nz - 1))(
                    lambda: add_blocks(w.at[zz], [rx.at[zz], low, high], 0, rows, o_ref)
                )

        z_guard(item, z, nz, run)

    def finish(zz, carry):
        c_x(zz).wait_send()
        pl.when(zz != z)(c_z(zz, zz, up).wait_send)
        return carry

    lax.fori_loop(0, nz, finish, 0)


def reduce_rows(partial, nz, collective_id):
    rows, cols = partial.shape[0] // (2 * nz), partial.shape[1]
    dma, vm, kind = pltpu.SemaphoreType.DMA, pltpu.VMEM, partial.dtype
    return pl.pallas_call(
        functools.partial(reduce_rows_kernel, nz),
        out_shape=jax.ShapeDtypeStruct((rows, cols), jnp.float32),
        in_specs=[pl.BlockSpec(memory_space=pl.ANY)],
        out_specs=pl.BlockSpec(memory_space=pltpu.VMEM),
        scratch_shapes=[vm((nz, rows, cols), kind), vm((nz, rows, cols), kind),
                        vm((nz + 1, rows, cols), kind)]
        + [dma((nz,))] * 4 + [dma((nz + 1,))],
        compiler_params=pltpu.CompilerParams(
            collective_id=collective_id, has_side_effects=True, vmem_limit_bytes=62 << 20
        ),
        name="reduce_rows",
    )(partial)


def gather_cols_kernel(x_ref, o_ref, lsem, s_p, s_y, r_p, r_y):
    z, x, y, c = place()
    cols = x_ref.shape[1]
    partner, yn = device(z, x, y, 1 - c), device(z, x, 1 - y, c)
    greet([(None, partner), (None, yn)])

    def block(yy, cc):
        return o_ref.at[:, pl.ds(pl.multiple_of((yy * 2 + cc) * cols, cols), cols)]

    own = pltpu.make_async_copy(x_ref, block(y, c), lsem)
    cy = remote(x_ref, block(y, c), s_y, r_y, yn)
    cp = remote(x_ref, block(y, c), s_p.at[0], r_p.at[0], partner)
    cf = remote(block(1 - y, c), block(1 - y, c), s_p.at[1], r_p.at[1], partner)
    cy.start()
    cp.start()
    own.start()
    cy.wait_recv()
    cf.start()
    cp.wait()
    cf.wait()
    cy.wait_send()
    own.wait()


def gather_cols(block, collective_id):
    dma = pltpu.SemaphoreType.DMA
    any_space = pl.BlockSpec(memory_space=pl.ANY)
    return pl.pallas_call(
        gather_cols_kernel,
        out_shape=jax.ShapeDtypeStruct((block.shape[0], block.shape[1] * 4), block.dtype),
        in_specs=[any_space],
        out_specs=any_space,
        scratch_shapes=[dma, dma((2,)), dma, dma((2,)), dma],
        compiler_params=pltpu.CompilerParams(collective_id=collective_id, has_side_effects=True),
        name="gather_cols",
    )(block)


def reduce_cols_kernel(p_ref, o_ref, w, rp, ry, s_l, s_p, s_y, r_p, r_y):
    z, x, y, c = place()
    rows, cols = o_ref.shape
    partner, yn = device(z, x, y, 1 - c), device(z, x, 1 - y, c)
    greet([(None, partner), (None, yn)])

    def block(yy, cc):
        return p_ref.at[:, pl.ds(pl.multiple_of((yy * 2 + cc) * cols, cols), cols)]

    sends = [remote(block(yy, 1 - c), rp.at[k], s_p.at[k], r_p.at[k], partner)
             for k, yy in enumerate((1 - y, y))]
    loads = [pltpu.make_async_copy(block(yy, c), w.at[k], s_l.at[k])
             for k, yy in enumerate((1 - y, y))]
    cy = remote(w.at[0], ry, s_y, r_y, yn)
    for k in range(2):
        sends[k].start()
        loads[k].start()
    loads[0].wait()
    sends[0].wait_recv()
    add_blocks(w.at[0], [rp.at[0]], 0, rows)
    cy.start()
    loads[1].wait()
    sends[1].wait_recv()
    cy.wait_recv()
    add_blocks(w.at[1], [rp.at[1], ry], 0, rows, o_ref)
    for k in range(2):
        sends[k].wait_send()
    cy.wait_send()


def reduce_cols(partial, collective_id):
    rows, cols = partial.shape[0], partial.shape[1] // 4
    dma, vm, kind = pltpu.SemaphoreType.DMA, pltpu.VMEM, partial.dtype
    return pl.pallas_call(
        reduce_cols_kernel,
        out_shape=jax.ShapeDtypeStruct((rows, cols), jnp.float32),
        in_specs=[pl.BlockSpec(memory_space=pl.ANY)],
        out_specs=pl.BlockSpec(memory_space=pltpu.VMEM),
        scratch_shapes=[vm((2, rows, cols), kind), vm((2, rows, cols), kind), vm((rows, cols), kind),
                        dma((2,)), dma((2,)), dma, dma((2,)), dma],
        compiler_params=pltpu.CompilerParams(
            collective_id=collective_id, has_side_effects=True, vmem_limit_bytes=62 << 20
        ),
        name="reduce_cols",
    )(partial)


def sum_cols_kernel(v_ref, o_ref, got, s, r):
    group = lax.axis_index("tp")
    shard = lax.axis_index("fsdp")
    peers = [(shard, (group + k) % 4) for k in range(1, 4)]
    greet([(None, peer) for peer in peers])
    copies = [remote(v_ref, got.at[k], s.at[k], r.at[k], peer) for k, peer in enumerate(peers)]
    for copy in copies:
        copy.start()
    for copy in copies:
        copy.wait()
    o_ref[...] = v_ref[...] + got[0] + got[1] + got[2]


def sum_cols(vector, collective_id):
    dma = pltpu.SemaphoreType.DMA
    shape = vector.shape
    return pl.pallas_call(
        sum_cols_kernel,
        out_shape=jax.ShapeDtypeStruct(shape, jnp.float32),
        in_specs=[pl.BlockSpec(memory_space=pltpu.VMEM)],
        out_specs=pl.BlockSpec(memory_space=pltpu.VMEM),
        scratch_shapes=[pltpu.VMEM((3,) + shape, jnp.float32), dma((3,)), dma((3,))],
        compiler_params=pltpu.CompilerParams(collective_id=collective_id, has_side_effects=True),
        name="sum_cols",
    )(vector)


def greet_all(shard, group, shards, groups):
    barrier = pltpu.get_barrier_semaphore()
    total = shards * groups

    def step(k, carry):
        other = (shard * groups + group + k) % total
        pl.semaphore_signal(
            barrier, inc=1, device_id=(other // groups, other % groups), device_id_type=MESH
        )
        return carry

    lax.fori_loop(1, total, step, 0)
    pl.semaphore_wait(barrier, total - 1)


def swap_rows_kernel(shards, groups, v_ref, o_ref, s, r):
    shard, group = lax.axis_index("fsdp"), lax.axis_index("tp")
    total = shards * groups
    me = shard * groups + group
    greet_all(shard, group, shards, groups)

    def copy(k):
        other = (me + k) % total
        return remote(v_ref.at[other // groups], o_ref.at[me], s.at[k], r.at[k],
                      (other // groups, other % groups))

    def start(k, carry):
        copy(k).start()
        return carry

    def wait(k, carry):
        copy(k).wait()
        return carry

    lax.fori_loop(1, total, start, 0)
    o_ref[me] = v_ref[shard]
    lax.fori_loop(1, total, wait, 0)


def swap_rows(values, shards, groups, collective_id):
    dma, total = pltpu.SemaphoreType.DMA, shards * groups
    return pl.pallas_call(
        functools.partial(swap_rows_kernel, shards, groups),
        out_shape=jax.ShapeDtypeStruct((total,) + values.shape[1:], values.dtype),
        in_specs=[pl.BlockSpec(memory_space=pltpu.VMEM)],
        out_specs=pl.BlockSpec(memory_space=pltpu.VMEM),
        scratch_shapes=[dma((total,)), dma((total,))],
        compiler_params=pltpu.CompilerParams(collective_id=collective_id, has_side_effects=True),
        name="swap_rows",
    )(values)


def sum_small_kernel(shards, groups, v_ref, o_ref, got, s1, r1, s2, r2):
    shard, group = lax.axis_index("fsdp"), lax.axis_index("tp")
    total = shards * groups
    me = shard * groups + group
    greet_all(shard, group, shards, groups)

    def first(k):
        other = (shard + k) % shards
        return remote(v_ref.at[other], got.at[k], s1.at[k], r1.at[k], (other, group))

    def second(k):
        other = (me + k) % total
        return remote(o_ref.at[me], o_ref.at[me], s2.at[k], r2.at[k],
                      (other // groups, other % groups))

    for k in range(1, shards):
        first(k).start()
    acc = v_ref[shard]
    for k in range(1, shards):
        first(k).wait()
        acc = acc + got[k]
    o_ref[me] = acc

    def start(k, carry):
        second(k).start()
        return carry

    def wait(k, carry):
        second(k).wait()
        return carry

    lax.fori_loop(1, total, start, 0)
    lax.fori_loop(1, total, wait, 0)


def sum_small(values, shards, groups, collective_id):
    dma, total = pltpu.SemaphoreType.DMA, shards * groups
    part = values.shape[1:]
    return pl.pallas_call(
        functools.partial(sum_small_kernel, shards, groups),
        out_shape=jax.ShapeDtypeStruct((total,) + part, values.dtype),
        in_specs=[pl.BlockSpec(memory_space=pltpu.VMEM)],
        out_specs=pl.BlockSpec(memory_space=pltpu.VMEM),
        scratch_shapes=[pltpu.VMEM((shards,) + part, values.dtype), dma((shards,)), dma((shards,)),
                        dma((total,)), dma((total,))],
        compiler_params=pltpu.CompilerParams(collective_id=collective_id, has_side_effects=True),
        name="sum_small",
    )(values)


def dot_plain(left, right):
    return jnp.dot(left, right, preferred_element_type=jnp.float32)


def far_first(nz, z, k):
    at = 0
    for here in range(nz):
        order = sorted(range(nz), key=lambda other: (-abs(other - here), other))
        for step, other in enumerate(order):
            at = at + jnp.where((z == here) & (k == step), other, 0)
    return at


def tile_item(nz, z, k):
    return far_first(nz, z, jnp.where(k == nz - 1, nz - 1, nz - 2 - k))


def line_schedule(nz):
    order = []
    for here in range(nz):
        near = sorted(range(nz), key=lambda other: (-abs(other - here), other))[::-1]
        order.append(near[1:] + near[:1])
    sent = {}
    steps = [{} for _ in range(nz)]

    def send(here, to):
        if (here, to) not in sent:
            ready = 2 * order[here].index(to) + 2
            back = here - 1 if to > here else here + 1
            if 0 <= back < nz:
                ready = max(ready, send(back, to)) + 1
                steps[here].setdefault(ready, []).append(to)
            sent[here, to] = ready
        return sent[here, to]

    for here in range(nz):
        for to in range(nz):
            if to != here:
                send(here, to)
    for here in range(nz):
        arrivals = [send(near, here) for near in (here - 1, here + 1) if 0 <= near < nz]
        last = max(arrivals + [2 * order[here].index(here) + 2]) + 1
        steps[here].setdefault(last, []).append(here)
    return steps


def expert_kernel(nz, slots, block_rows, tok_ref, gain_ref, router_ref, attn_part, g_all, routes_all,
                  wg_all, wu_all, wd_all, middle_ref, scale_ref, low_ref, x_all, out_all, back_ref, gg_got, gates_ref, xr_all, gs_all, hid_all, gp_all, up_all,
                  wg, wu, wd, s_in_w, gg_ref, x_ref, g_ref, t_ref, o_ref, xr, gs, hid, gp, up, st,
                  w, lp, rx, rxd, ry, ryd, rz,
                  s_in, s_out, s_save, s_p, r_p, s_x, s_y, s_dx, s_dy, s_z, r_x, r_y, r_dx, r_dy, r_z,
                  s_g, r_g, *refs):
    z, x, y, c = place()
    shard, group = lax.axis_index("fsdp"), lax.axis_index("tp")
    expert = shard * 4 + group
    rows, cols = back_ref.shape
    width = x_ref.shape[1]
    half = rows // 2
    blocks = rows // block_rows
    experts = router_ref.shape[1]
    f32, low = jnp.float32, jnp.bfloat16
    partner = device(z, x, y, 1 - c)
    xn, yn = device(z, 1 - x, y, c), device(z, x, 1 - y, c)
    up_dev, down_dev = device(z + 1, x, y, c), device(z - 1, x, y, c)
    n_c, n_s = len(ReduceCols.scratch(16, 128, low)), len(RowSums.scratch(128))
    columns = ReduceCols(attn_part, middle_ref, refs[:n_c])
    sums = RowSums(refs[n_c : n_c + n_s])
    moe_rows = GatherAll(nz, low_ref, x_all, refs[n_c + n_s :], half)
    greet_all(shard, group, 2 * nz, 4)
    columns.start()
    tiles = 2 * nz
    devices = 8 * nz

    def swap(k):
        other = (expert + k) % devices
        return remote(gg_ref.at[other // 4], gg_got.at[expert], s_g.at[k], r_g.at[k],
                      (other // 4, other % 4))

    def tile_of(j):
        return tile_item(nz, z, j // 2) * 2 + jnp.where(j % 2 == 0, 1 - x, x)

    def tile_rows(j):
        return pl.ds(pl.multiple_of(tile_of(j) * rows, rows), rows)

    def load(j):
        return pltpu.make_async_copy(x_all.at[tile_rows(j)], x_ref, s_in.at[0])

    def load_g(j):
        tile = tile_of(j)
        first = pl.ds(pl.multiple_of(tile * rows, half), half)
        second = pl.ds(pl.multiple_of(mirrored(nz, tile) * rows + half, half), half)
        return (pltpu.make_async_copy(g_all.at[first], g_ref.at[pl.ds(0, half)], s_in.at[1]),
                pltpu.make_async_copy(g_all.at[second], g_ref.at[pl.ds(half, half)], s_in.at[3]))

    def load_t(j):
        tile = tile_of(j)
        first = pl.ds(pl.multiple_of(tile * rows, half), half)
        second = pl.ds(pl.multiple_of(mirrored(nz, tile) * rows + half, half), half)
        return (pltpu.make_async_copy(routes_all.at[first], t_ref.at[pl.ds(0, half)], s_in.at[2]),
                pltpu.make_async_copy(routes_all.at[second], t_ref.at[pl.ds(half, half)], s_in.at[4]))

    def save_out(j):
        return pltpu.make_async_copy(o_ref, out_all.at[tile_rows(j)], s_out)

    def saves(j):
        pairs = ((xr, xr_all), (gs, gs_all), (hid, hid_all), (gp, gp_all), (up, up_all))
        return [pltpu.make_async_copy(src, dst.at[j], s_save.at[n])
                for n, (src, dst) in enumerate(pairs)]

    def c_p(zz, rel, slot):
        k = zz * 4 + rel
        return remote(st.at[slot, rel // 2], lp.at[zz, rel], s_p.at[k], r_p.at[k], partner)

    def c_diag(zz):
        return (remote(w.at[zz, 3, pl.ds(0, half)], rxd.at[zz], s_dx.at[zz], r_dx.at[zz], xn),
                remote(w.at[zz, 3, pl.ds(half, half)], ryd.at[zz], s_dy.at[zz], r_dy.at[zz], yn))

    def c_xy(zz):
        return (remote(w.at[zz, 1], rx.at[zz], s_x.at[zz], r_x.at[zz], xn),
                remote(w.at[zz, 2], ry.at[zz], s_y.at[zz], r_y.at[zz], yn))

    def c_z(zz, slot, where):
        return remote(w.at[zz, 0], rz.at[slot], s_z.at[zz], r_z.at[slot], where)

    def send_z(zz):
        pl.when(zz > z)(lambda: c_z(zz, zz, up_dev).start())
        pl.when(zz == z - 1)(lambda: c_z(zz, nz, down_dev).start())
        pl.when(zz < z - 1)(lambda: c_z(zz, zz, down_dev).start())

    def stage_d(zz, rel, slot):
        c_p(zz, rel, slot).wait_recv()
        add_blocks(w.at[zz, rel], [lp.at[zz, rel]], 0, rows)
        if rel == 3:
            for copy in c_diag(zz):
                copy.start()

    def stage_e(zz):
        dx, dy = c_diag(zz)
        cx, cy = c_xy(zz)
        dy.wait_recv()
        add_blocks(w.at[zz, 1], [ryd.at[zz]], half, half)
        cx.start()
        dx.wait_recv()
        add_blocks(w.at[zz, 2], [rxd.at[zz]], 0, half)
        cy.start()

    def passes(zz):
        return ((zz > z) & (z > 0)) | ((zz < z) & (z < nz - 1))

    def stage_f1(zz):
        cx, cy = c_xy(zz)
        cx.wait_recv()
        cy.wait_recv()
        add_blocks(w.at[zz, 0], [rx.at[zz], ry.at[zz]], 0, rows)
        pl.when((zz != z) & jnp.logical_not(passes(zz)))(lambda: send_z(zz))

    def stage_f2(zz):
        @pl.when((zz != z) & passes(zz))
        def _():
            c_z(zz, zz, up_dev).wait_recv()
            add_blocks(w.at[zz, 0], [rz.at[zz]], 0, rows)
            send_z(zz)

        @pl.when(zz == z)
        def _():
            low_part, high_part = rz.at[zz], rz.at[nz]
            pl.when(z > 0)(lambda: c_z(zz, zz, up_dev).wait_recv())
            pl.when(z < nz - 1)(lambda: c_z(zz, nz, down_dev).wait_recv())
            own = w.at[zz, 0]
            pl.when(z == 0)(lambda: add_blocks(own, [high_part], 0, rows, back_ref))
            pl.when(z == nz - 1)(lambda: add_blocks(own, [low_part], 0, rows, back_ref))
            pl.when((z > 0) & (z < nz - 1))(
                lambda: add_blocks(own, [low_part, high_part], 0, rows, back_ref)
            )

    def compute(j):
        zz = tile_item(nz, z, j // 2)
        slot = j % 2
        load(j).wait()
        for copy in load_t(j):
            copy.wait()
        lanes = lax.broadcasted_iota(jnp.int32, (rows, experts), 1)
        routes = t_ref[...]
        chosen = routes[:, 0:1] == lanes
        for n in range(1, TOPK):
            chosen = chosen | (routes[:, n : n + 1] == lanes)
        logits = jnp.where(chosen, dot_plain(x_ref[...], router_ref[...]), masked_score)
        peak = jnp.max(logits, axis=1, keepdims=True)
        weights = jnp.where(chosen, jnp.exp(logits - peak), 0.0)
        gates = weights / jnp.sum(weights, axis=1, keepdims=True)
        gates_ref[...] = gates
        mine = lanes == expert
        gate_col = jnp.sum(jnp.where(mine, gates, 0.0), axis=1, keepdims=True)
        match_col = jnp.sum(jnp.where(mine & chosen, 1.0, 0.0), axis=1, keepdims=True)
        sub = lax.broadcasted_iota(jnp.int32, (block_rows, block_rows), 0)
        lane = lax.broadcasted_iota(jnp.int32, (block_rows, block_rows), 1)
        eye = sub == lane
        before = (sub > lane).astype(f32).astype(low)
        chosen_low = chosen.astype(f32).astype(low)
        pick, put, slot_gate = [], [], []
        slot_lane = lax.broadcasted_iota(jnp.int32, (block_rows, slots), 1).astype(f32)
        slot_sub = lax.broadcasted_iota(jnp.int32, (slots, block_rows), 0).astype(f32)
        for b in range(blocks):
            part = slice(b * block_rows, (b + 1) * block_rows)
            ranks = dot_plain(before, chosen_low[part])
            rank = jnp.sum(jnp.where(mine[part], ranks, 0.0), axis=1, keepdims=True)
            rank = jnp.where(match_col[part] > 0.0, rank, -1.0)
            rank_row = jnp.sum(jnp.where(eye, rank, 0.0), axis=0, keepdims=True)
            gate_row = jnp.sum(jnp.where(eye, gate_col[part], 0.0), axis=0, keepdims=True)
            hot = rank_row == slot_sub
            pick.append(hot.astype(f32).astype(low))
            put.append((rank == slot_lane).astype(f32).astype(low))
            slot_gate.append(jnp.sum(jnp.where(hot, gate_row, 0.0), axis=1, keepdims=True))
        slot_gate = jnp.concatenate(slot_gate, axis=0)

        def gather(ref, at):
            return jnp.concatenate(
                [dot_plain(pick[b], ref[pl.ds(b * block_rows, block_rows), at])
                 for b in range(blocks)],
                axis=0,
            )

        def scatter(ref, at, values):
            for b in range(blocks):
                ref[pl.ds(b * block_rows, block_rows), at] = dot_plain(
                    put[b], values[b * slots : (b + 1) * slots]
                ).astype(low)

        def columns(i):
            return pl.ds(pl.multiple_of(i * cols, cols), cols)

        @pl.when(j > 0)
        def _():
            for copy in saves(j):
                copy.wait()

        def take(i, carry):
            xr[:, columns(i)] = gather(x_ref, columns(i)).astype(low)
            return carry

        lax.fori_loop(0, width // cols, take, 0)

        pl.when(j == 0)(lambda: moe_rows.second(2))
        for k in range(3, nz):
            pl.when(j == 1)(lambda: moe_rows.second(k))

        @pl.when((j % 2 == 1) & (j < tiles - 1))
        def _():
            moe_rows.ready(tile_item(nz, z, j // 2 + 1))

        @pl.when(j < tiles - 1)
        def _():
            load(j + 1).start()
            for copy in load_t(j + 1):
                copy.start()

        gate_pre = dot_plain(xr[...], wg[...])
        up_pre = dot_plain(xr[...], wu[...])
        sig = jax.nn.sigmoid(gate_pre)
        silu = gate_pre * sig
        hidden_low = (silu * up_pre).astype(low)
        hid[...] = hidden_low
        for copy in load_g(j):
            copy.wait()
        pl.when(j > 0)(lambda: save_out(j).wait())

        def middle_part(i, carry):
            total, hidden_grad = carry
            at = columns(i)
            grad = gather(g_ref, at)
            expert_out = dot_plain(hidden_low, wd[:, at]).astype(low).astype(f32)
            total = total + jnp.sum(grad * expert_out, axis=1, keepdims=True)
            pair_grad = (grad * slot_gate).astype(low)
            gs[:, at] = pair_grad
            scatter(o_ref, at, (expert_out * slot_gate).astype(low))
            return total, hidden_grad + dot_last(pair_grad, wd[:, at])

        gates_grad, hidden_grad = lax.fori_loop(
            0,
            width // cols,
            middle_part,
            (jnp.zeros(slot_gate.shape, f32), jnp.zeros(gate_pre.shape, f32)),
        )
        save_out(j).start()

        @pl.when(j < tiles - 1)
        def _():
            for copy in load_g(j + 1):
                copy.start()

        for b in range(blocks):
            gg_ref[tile_of(j), :, pl.ds(b * block_rows, block_rows)] = jnp.sum(
                pick[b].astype(f32) * gates_grad[b * slots : (b + 1) * slots],
                axis=0,
                keepdims=True,
            )
        gate_grad = (hidden_grad * up_pre * (sig * (1.0 + gate_pre * (1.0 - sig)))).astype(low)
        up_grad = (hidden_grad * silu).astype(low)
        gp[...] = gate_grad
        up[...] = up_grad
        for copy in saves(j):
            copy.start()

        def part_of(i, yy, cc):
            at = columns(yy * 2 + cc)
            row_grad = dot_last(gate_grad, wg[at, :]) + dot_last(up_grad, wu[at, :])
            return row_grad.astype(low)

        first = jnp.where(slot == 0, 1, 0)

        def to_partner(i, carry):
            yy = jnp.where(i == 1, 1 - y, y)
            rel = first + 2 * i

            @pl.when(j >= 2)
            def _():
                before_zz = tile_item(nz, z, j // 2 - 1)
                k = before_zz * 4 + rel
                remote(st.at[slot, i], lp.at[before_zz, rel], s_p.at[k], r_p.at[k], partner).wait_send()

            scatter(st.at[slot, i], slice(None), part_of(i, yy, 1 - c))
            k = zz * 4 + rel
            remote(st.at[slot, i], lp.at[zz, rel], s_p.at[k], r_p.at[k], partner).start()
            return carry

        def to_own(i, carry):
            yy = jnp.where(i == 1, 1 - y, y)
            scatter(w.at[zz, first + 2 * i], slice(None), part_of(i, yy, c))
            return carry

        lax.fori_loop(0, 2, to_partner, 0)
        lax.fori_loop(0, 2, to_own, 0)

    weights = [pltpu.make_async_copy(src, dst, s_in_w.at[n])
               for n, (src, dst) in enumerate(((wg_all, wg), (wu_all, wu), (wd_all, wd)))]
    for copy in load_t(0) + load_g(0) + tuple(weights):
        copy.start()

    corner = diagonal()
    columns.first()
    columns.second()

    def residual(n, carry):
        here = pl.ds(pl.multiple_of(n * 128, 128), 128)
        total = middle_ref[here, :] + tok_ref[here, :].astype(f32)
        middle_ref[here, :] = total
        sums.got[0, pl.ds(n, 1), :] = to_row(jnp.sum(total * total, axis=1, keepdims=True), corner)
        return carry

    def norm(n, carry):
        here = pl.ds(pl.multiple_of(n * 128, 128), 128)
        scale = lax.rsqrt(to_column(sums.total(n), corner) / width + norm_eps)
        scale_ref[here, :] = scale
        low_ref[here, :] = (middle_ref[here, :] * scale * gain_ref[...]).astype(low)
        return carry

    lax.fori_loop(0, rows // 128, residual, 0)
    sums.start()
    sums.wait()
    lax.fori_loop(0, rows // 128, norm, 0)
    moe_rows.own().start()
    moe_rows.own().wait()
    moe_rows.first(0)
    moe_rows.first(1)
    moe_rows.second(0)
    moe_rows.first(2)
    moe_rows.second(1)
    moe_rows.third(0)
    for k in range(3, nz):
        moe_rows.first(k)
    moe_rows.third(1)
    moe_rows.ready(tile_item(nz, z, 0))
    load(0).start()
    for copy in weights:
        copy.wait()
    schedule = line_schedule(nz)
    last_step = max(max(steps) for steps in schedule)

    def step(j, carry):
        k, odd = j // 2, j % 2 == 1
        pl.when(j < tiles)(lambda: compute(j))
        pl.when(j == 0)(lambda: moe_rows.third(2))
        for n in range(3, nz):
            pl.when(j == 2)(lambda: moe_rows.third(n))

        @pl.when(j == tiles)
        def _():
            gg_got[expert] = gg_ref[shard]
            loop_from_one(devices, lambda n: swap(n).start())

        @pl.when(jnp.logical_not(odd) & (k < nz))
        def _():
            zz = tile_item(nz, z, k)
            stage_d(zz, 3, 0)
            stage_d(zz, 1, 0)

        @pl.when(odd & (k < nz))
        def _():
            zz = tile_item(nz, z, k)
            stage_d(zz, 2, 1)
            stage_d(zz, 0, 1)
            stage_e(zz)

        @pl.when((k >= 1) & (k < nz + 1) & jnp.logical_not(odd))
        def _():
            stage_f1(tile_item(nz, z, k - 1))

        for here, steps in enumerate(schedule):
            for at, places in steps.items():
                for to in places:
                    pl.when((z == here) & (j == at))(lambda to=to: stage_f2(jnp.int32(to)))

        return carry

    lax.fori_loop(0, last_step + 1, step, 0)
    loop_from_one(devices, lambda n: swap(n).wait())
    save_out(tiles - 1).wait()
    for copy in saves(tiles - 1):
        copy.wait()
    for slot in range(2):
        for i in range(2):
            c_p(z, 1 - slot + 2 * i, slot).wait_send()

    def finish(zz, carry):
        for copy in c_diag(zz) + c_xy(zz):
            copy.wait_send()
        pl.when(zz != z)(c_z(zz, zz, up_dev).wait_send)
        return carry

    lax.fori_loop(0, nz, finish, 0)
    columns.finish()
    moe_rows.finish_sends()


def run_experts(tokens, gain, router, attn_part, g_all, routes_all, gate_w, up_w, down_w, block_rows,
                slots, nz, collective_id):
    total, width = g_all.shape
    hidden = gate_w.shape[1]
    experts = router.shape[1]
    tiles = 2 * nz
    rows, cols = total // tiles, width // 4
    pairs = rows // block_rows * slots
    half = rows // 2
    f32, low = jnp.float32, jnp.bfloat16
    any_space = pl.BlockSpec(memory_space=pl.ANY)
    vmem = pl.BlockSpec(memory_space=pltpu.VMEM)
    vm, dma, shape = pltpu.VMEM, pltpu.SemaphoreType.DMA, jax.ShapeDtypeStruct
    return pl.pallas_call(
        functools.partial(expert_kernel, nz, slots, block_rows),
        in_specs=[vmem] * 3 + [any_space] * 6,
        out_specs=[vmem] * 3 + [any_space] * 2 + [vmem] * 3 + [any_space] * 5,
        out_shape=[
            shape((rows, cols), f32), shape((rows, 1), f32), shape((rows, cols), low),
            shape((total, width), low),
            shape((total, width), low), shape((rows, cols), f32), shape((4 * tiles, 1, rows), f32),
            shape((rows, experts), f32),
            shape((tiles, pairs, width), low), shape((tiles, pairs, width), low),
            shape((tiles, pairs, hidden), low), shape((tiles, pairs, hidden), low),
            shape((tiles, pairs, hidden), low),
        ],
        scratch_shapes=[
            vm((width, hidden), low), vm((width, hidden), low), vm((hidden, width), low), dma((3,)),
            vm((tiles, 1, rows), f32), vm((rows, width), low), vm((rows, width), low),
            vm((rows, routes_all.shape[1]), jnp.int32), vm((rows, width), low),
            vm((pairs, width), low), vm((pairs, width), low),
            vm((pairs, hidden), low), vm((pairs, hidden), low), vm((pairs, hidden), low),
            vm((2, 2, rows, cols), low),
            vm((nz, 4, rows, cols), low), vm((nz, 4, rows, cols), low),
            vm((nz, rows, cols), low), vm((nz, half, cols), low),
            vm((nz, rows, cols), low), vm((nz, half, cols), low),
            vm((nz + 1, rows, cols), low),
            dma((5,)), dma, dma((5,)), dma((4 * nz,)), dma((4 * nz,)),
        ] + [dma((nz,))] * 9 + [dma((nz + 1,))] + [dma((4 * tiles,))] * 2
        + ReduceCols.scratch(rows, cols, low) + RowSums.scratch(rows) + GatherAll.scratch(nz),
        compiler_params=pltpu.CompilerParams(
            collective_id=collective_id, has_side_effects=True, vmem_limit_bytes=62 << 20
        ),
        name="experts",
    )(tokens, gain, router, attn_part, g_all, routes_all, gate_w, up_w, down_w)


def near_first(nz, z, k):
    return far_first(nz, z, nz - 1 - k)


class GatherAll:
    sems = 6

    @staticmethod
    def scratch(nz):
        dma = pltpu.SemaphoreType.DMA
        return [dma] + [dma((5 * nz,))] * 2 + [dma((nz,))] * 11

    def __init__(self, nz, src, out, sems, cut):
        (self.lsem, self.s_p, self.r_p, self.s_u, self.s_d, self.s_x, self.s_y, self.s_dx,
         self.s_dy, self.r_z, self.r_x, self.r_y, self.r_dx, self.r_dy) = sems
        self.nz, self.src, self.out, self.cut = nz, src, out, cut
        self.rows, self.cols = src.shape
        self.place = z, x, y, c = place()
        self.partner, self.xn, self.yn = (
            device(z, x, y, 1 - c), device(z, 1 - x, y, c), device(z, x, 1 - y, c))
        self.up, self.down = device(z + 1, x, y, c), device(z - 1, x, y, c)

    def block(self, zz, xx, yy, cc, part=None):
        start, size, unit = (zz * 2 + xx) * self.rows, self.rows, self.rows
        if part == 0:
            size, unit = self.cut, self.rows
        elif part == 1:
            start, size = start + self.cut, self.rows - self.cut
            unit = math.gcd(self.cut, self.rows)
        return self.out.at[pl.ds(pl.multiple_of(start, unit), size),
                           pl.ds(pl.multiple_of((yy * 2 + cc) * self.cols, self.cols), self.cols)]

    def own(self):
        z, x, y, c = self.place
        return pltpu.make_async_copy(self.src, self.block(z, x, y, c), self.lsem)

    def line(self, zz):
        z, x, y, c = self.place
        here = self.block(zz, x, y, c)
        return (remote(here, here, self.s_u.at[zz], self.r_z.at[zz], self.up),
                remote(here, here, self.s_d.at[zz], self.r_z.at[zz], self.down))

    def sides(self, zz):
        z, x, y, c = self.place
        here = self.block(zz, x, y, c)
        return (remote(here, here, self.s_x.at[zz], self.r_x.at[zz], self.xn),
                remote(here, here, self.s_y.at[zz], self.r_y.at[zz], self.yn))

    def across(self, zz):
        z, x, y, c = self.place
        copies = []
        if self.cut > 0:
            here = self.block(zz, 1 - x, y, c, 0)
            copies.append(remote(here, here, self.s_dy.at[zz], self.r_dy.at[zz], self.yn))
        if self.cut < self.rows:
            here = self.block(zz, x, 1 - y, c, 1)
            copies.append(remote(here, here, self.s_dx.at[zz], self.r_dx.at[zz], self.xn))
        return copies

    def pair(self, zz, rel, mine=True):
        z, x, y, c = self.place
        xx = 1 - x if rel in (1, 3, 4) else x
        yy = 1 - y if rel in (2, 3, 4) else y
        here = self.block(zz, xx, yy, c if mine else 1 - c, {3: 0, 4: 1}.get(rel))
        k = zz * 5 + rel
        return remote(here, here, self.s_p.at[k], self.r_p.at[k], self.partner)

    def parts(self):
        return [0, 1, 2] + [3] * (self.cut > 0) + [4] * (self.cut < self.rows)

    def first(self, k):
        zz, z = near_first(self.nz, self.place[0], k), self.place[0]
        up, down = self.line(zz)
        pl.when(k > 0)(lambda: up.wait_recv())
        pl.when((zz <= z) & (z < self.nz - 1))(lambda: up.start())
        pl.when((zz >= z) & (z > 0))(lambda: down.start())
        for copy in self.sides(zz):
            copy.start()
        self.pair(zz, 0).start()

    def second(self, k):
        zz = near_first(self.nz, self.place[0], k)
        to_x, to_y = self.sides(zz)
        across = self.across(zz)
        to_x.wait_recv()
        if self.cut > 0:
            across[0].start()
        self.pair(zz, 1).start()
        to_y.wait_recv()
        if self.cut < self.rows:
            across[-1].start()
        self.pair(zz, 2).start()

    def third(self, k):
        zz = near_first(self.nz, self.place[0], k)
        across = self.across(zz)
        for rel, copy in zip(self.parts()[3:], across):
            copy.wait_recv()
            self.pair(zz, rel).start()

    def ready(self, zz):
        for rel in self.parts():
            self.pair(zz, rel, False).wait_recv()

    def finish_sends(self):
        z = self.place[0]

        def step(zz, carry):
            for rel in self.parts():
                self.pair(zz, rel).wait_send()
            up, down = self.line(zz)
            pl.when((zz <= z) & (z < self.nz - 1))(lambda: up.wait_send())
            pl.when((zz >= z) & (z > 0))(lambda: down.wait_send())
            for copy in tuple(self.sides(zz)) + tuple(self.across(zz)):
                copy.wait_send()
            return carry

        lax.fori_loop(0, self.nz, step, 0)

    def finish(self):
        def step(zz, carry):
            self.ready(zz)
            return carry

        lax.fori_loop(0, self.nz, step, 0)
        self.finish_sends()


class GatherCausal:
    @staticmethod
    def scratch(nz):
        dma = pltpu.SemaphoreType.DMA
        return [dma, dma, dma((2,)), dma((2 * nz,)), dma((2 * nz,)), dma((2 * nz,))]

    def __init__(self, nz, src, out, held, sems):
        self.s_x, self.r_x, self.lsem, self.s_z, self.r_z, self.l_z = sems
        self.nz, self.src, self.out, self.held_ref = nz, src, out, held
        self.place = z, x, y, c = place()
        self.xn = device(z, 1 - x, y, c)
        self.near = (device(z + 1, x, y, c), device(z - 1, x, y, c))

    def own(self):
        z, x = self.place[:2]
        return [pltpu.make_async_copy(self.src, self.out.at[z, x], self.lsem.at[0]),
                pltpu.make_async_copy(self.src, self.held_ref.at[z, x], self.lsem.at[1])]

    def side(self):
        z, x = self.place[:2]
        return remote(self.src, self.out.at[z, x], self.s_x, self.r_x, self.xn)

    def line(self, zz, micro):
        here = self.out.at[zz, :, micro]
        return remote(here, here, self.s_z.at[zz * 2 + micro], self.r_z.at[zz * 2 + micro],
                      self.near[micro])

    def keep(self, zz, micro):
        return pltpu.make_async_copy(self.out.at[zz, :, micro], self.held_ref.at[zz, :, micro],
                                     self.l_z.at[zz * 2 + micro])

    def needed(self, zz, micro):
        return zz <= self.place[0] if micro == 0 else zz >= self.place[0]

    def sends(self, zz, micro):
        z = self.place[0]
        return self.needed(zz, micro) & (z < self.nz - 1 if micro == 0 else z > 0)

    def first(self, k):
        zz, z = near_first(self.nz, self.place[0], k), self.place[0]

        @pl.when(k == 0)
        def _():
            for copy in self.own():
                copy.wait()
            self.side().wait_recv()

        for micro in range(2):
            pl.when((k > 0) & self.needed(zz, micro))(lambda: self.line(zz, micro).wait_recv())
            pl.when(self.sends(zz, micro))(lambda: self.line(zz, micro).start())
            pl.when(self.needed(zz, micro))(lambda: self.keep(zz, micro).start())

    def ready(self, zz):
        for micro in range(2):
            pl.when(self.needed(zz, micro))(lambda: self.keep(zz, micro).wait())

    def finish(self):
        self.side().wait_send()

        def step(zz, carry):
            for micro in range(2):
                pl.when(self.sends(zz, micro))(lambda: self.line(zz, micro).wait_send())
            return carry

        lax.fori_loop(0, self.nz, step, 0)


class GatherRows:
    @staticmethod
    def scratch(nz):
        dma = pltpu.SemaphoreType.DMA
        return [dma] + [dma((nz,))] * 5

    def __init__(self, nz, src, out, sems):
        self.lsem, self.s_u, self.s_d, self.s_x, self.r_z, self.r_x = sems
        self.nz, self.src, self.out = nz, src, out
        self.place = z, x, y, c = place()
        self.xn = device(z, 1 - x, y, c)
        self.up, self.down = device(z + 1, x, y, c), device(z - 1, x, y, c)

    def block(self, zz):
        rows = self.src.shape[0]
        return self.out.at[pl.ds(pl.multiple_of((zz * 2 + self.place[1]) * rows, rows), rows)]

    def own(self):
        return pltpu.make_async_copy(self.src, self.block(self.place[0]), self.lsem)

    def copies(self, zz):
        here = self.block(zz)
        return (remote(here, here, self.s_u.at[zz], self.r_z.at[zz], self.up),
                remote(here, here, self.s_d.at[zz], self.r_z.at[zz], self.down),
                remote(here, here, self.s_x.at[zz], self.r_x.at[zz], self.xn))

    def first(self, k):
        zz, z = near_first(self.nz, self.place[0], k), self.place[0]
        up, down, to_x = self.copies(zz)
        pl.when(k > 0)(lambda: up.wait_recv())
        pl.when((zz <= z) & (z < self.nz - 1))(lambda: up.start())
        pl.when((zz >= z) & (z > 0))(lambda: down.start())
        to_x.start()

    def finish(self):
        z = self.place[0]

        def step(zz, carry):
            up, down, to_x = self.copies(zz)
            to_x.wait()
            pl.when((zz <= z) & (z < self.nz - 1))(lambda: up.wait_send())
            pl.when((zz >= z) & (z > 0))(lambda: down.wait_send())
            return carry

        lax.fori_loop(0, self.nz, step, 0)


def mirrored(nz, shard):
    return (nz - 1 - shard // 2) * 2 + shard % 2


def stream_unit(u, nz):
    shard = lax.axis_index("fsdp")
    later = u > shard
    micro = jnp.where(later, 1, 0)
    here = jnp.where(later, mirrored(nz, shard), shard)
    key_place = here - jnp.where(later, u - shard - 1, u)
    owner = jnp.where(later, mirrored(nz, key_place), key_place)
    return micro, here, key_place, owner


def key_bias(micro, here, key_place, block, start_ref):
    key = key_place * block + lax.broadcasted_iota(jnp.int32, (block, block), 0)
    query = here * block + lax.broadcasted_iota(jnp.int32, (block, block), 1)
    return jnp.where((key >= start_ref[micro]) & (key <= query), 0.0, masked_score)


def norm_turn(raw, gain, cosine, sine):
    scale = lax.rsqrt(jnp.mean(raw * raw, axis=1, keepdims=True) + norm_eps)
    normed = raw * scale * gain
    return normed * cosine + pltpu.roll(normed, raw.shape[1] // 2, 1) * sine


def attend_kernel(nz, q_pre, k_pre, v_pre, gq_ref, gk_ref, cos_ref, sin_ref, start_ref, cot_ref, wo_ref,
                  q_ref, heads_ref, out_ref, lse_ref, kv_all, cot_all, wo_all,
                  kv_ref, kv, acc, peak, total, *sems):
    shards = 2 * nz
    width = kv_ref.shape[2] // 2
    block = q_ref.shape[0] // 2
    low = jnp.bfloat16
    heads = q_ref.shape[1] // width
    z, x, y, c = place()
    split = len(GatherAll.scratch(nz))
    end = split + len(GatherRows.scratch(nz))
    cots = GatherAll(nz, cot_ref, cot_all, sems[:split], cot_ref.shape[0])
    outs = GatherRows(nz, wo_ref, wo_all, sems[split:end])
    keys_in = GatherCausal(nz, kv_ref, kv_all, kv, sems[end:])
    greet([(None, cots.partner), (None, cots.xn), (None, cots.yn),
           (z < nz - 1, cots.up), (z > 0, cots.down)])
    for part in (outs, cots):
        part.own().start()
    turned = norm_turn(k_pre[...], gk_ref[...], cos_ref[...], sin_ref[...]).astype(low)
    for micro in range(2):
        rows = slice(micro * block, (micro + 1) * block)
        kv_ref[micro, :, :width] = turned[rows]
        kv_ref[micro, :, width:] = v_pre[rows, :]
    keys_in.side().start()
    for copy in keys_in.own():
        copy.start()
    peak[...] = jnp.full(peak.shape, masked_score, jnp.float32)
    total[...] = jnp.zeros_like(total)
    acc[...] = jnp.zeros_like(acc)
    for part in (outs, cots):
        part.own().wait()

    def tick(u, carry):
        @pl.when(u < nz)
        def _():
            pl.when(u == 0)(lambda: cots.first(u))
            keys_in.first(u)
            pl.when(u > 0)(lambda: cots.first(u))
            outs.first(u)

        pl.when((u >= 1) & (u <= nz))(lambda: cots.second(u - 1))
        pl.when((u >= 2) & (u <= nz + 1))(lambda: cots.third(u - 2))
        pl.when((u >= 1) & (u <= nz))(lambda: attend_item(u - 1))
        return carry

    def attend_item(k):
        zz = near_first(nz, z, k)
        own = zz == z
        keys_in.ready(zz)

        def part(i, carry):
            micro = jnp.where(own, i // 2, jnp.where(zz < z, 0, 1))
            xx = jnp.where(own, jnp.where(i % 2 == 0, x, 0), i)
            valid = jnp.where(own, jnp.where((i % 2 == 0) | (x == 1), 1, 0), jnp.where(i < 2, 1, 0))
            pl.when(valid == 1)(lambda: attention(micro, zz, xx))
            return carry

        lax.fori_loop(0, 4, part, 0)

    def attention(micro, zz, xx):
        def at_place(z_at, x_at):
            return jnp.where(micro == 0, z_at, nz - 1 - z_at) * 2 + x_at

        here, key_place = at_place(z, x), at_place(zz, xx)
        bias = key_bias(micro, here, key_place, block, start_ref)
        both = kv.at[zz, xx, micro]
        keys, values = both[:, :width], both[:, width:]
        q_rows = pl.ds(pl.multiple_of(micro * block, block), block)

        def head(h, carry):
            at = micro * heads + h
            query = q_ref[q_rows, pl.ds(pl.multiple_of(h * width, width), width)]
            scores = dot_last(keys, query) * width ** (-0.5) + bias
            before = peak[at]
            now = jnp.maximum(before, jnp.max(scores, axis=0, keepdims=True))
            weights = jnp.exp(scores - now)
            factor = jnp.exp(before - now)
            peak[at] = now
            total[at] = total[at] * factor + jnp.sum(weights, axis=0, keepdims=True)
            acc[at] = acc[at] * factor + dot_first(values, weights.astype(jnp.bfloat16))
            return carry

        lax.fori_loop(0, heads, head, 0, unroll=4)

    def prepare(h, carry):
        cols = pl.ds(pl.multiple_of(h * width, width), width)
        q_ref[:, cols] = norm_turn(q_pre[:, cols], gq_ref[...], cos_ref[...], sin_ref[...]).astype(low)
        return carry

    tick(0, 0)
    lax.fori_loop(0, heads, prepare, 0)
    lax.fori_loop(1, nz + 2, tick, 0)

    def close(at, carry):
        micro, h = at // heads, at % heads
        result = (acc[at] / total[at]).T
        here = pl.ds(pl.multiple_of(micro * block, block), block)
        cols = pl.ds(pl.multiple_of(h * width, width), width)
        out_ref[here, cols] = result
        heads_ref[here, cols] = result.astype(jnp.bfloat16)
        lse_ref[at] = peak[at] + jnp.log(total[at])
        return carry

    lax.fori_loop(0, 2 * heads, close, 0)
    keys_in.finish()
    outs.finish()
    cots.finish()


def attend(q_pre, k_pre, v_low, gain_query, gain_key, cosine, sine, starts, cotangent, w_out, nz,
           collective_id):
    rows, columns = q_pre.shape
    width = k_pre.shape[1]
    heads = columns // width
    block = rows // 2
    any_space = pl.BlockSpec(memory_space=pl.ANY)
    vmem = pl.BlockSpec(memory_space=pltpu.VMEM)
    vm, shape, f32, low = pltpu.VMEM, jax.ShapeDtypeStruct, jnp.float32, jnp.bfloat16
    return pl.pallas_call(
        functools.partial(attend_kernel, nz),
        in_specs=[vmem] * 10,
        out_specs=[vmem] * 4 + [any_space] * 3,
        out_shape=[
            shape((rows, columns), low), shape((rows, columns), low), shape((rows, columns), f32),
            shape((2 * heads, 1, block), f32),
            shape((nz, 2, 2, block, 2 * width), low),
            shape((rows * 2 * nz, cotangent.shape[1] * 4), cotangent.dtype),
            shape((w_out.shape[0] * 2 * nz, w_out.shape[1]), w_out.dtype),
        ],
        scratch_shapes=[
            vm((2, block, 2 * width), low), vm((nz, 2, 2, block, 2 * width), low),
            vm((2 * heads, width, block), f32), vm((2 * heads, 1, block), f32),
            vm((2 * heads, 1, block), f32),
        ] + GatherAll.scratch(nz) + GatherRows.scratch(nz) + GatherCausal.scratch(nz),
        compiler_params=pltpu.CompilerParams(
            collective_id=collective_id, has_side_effects=True, vmem_limit_bytes=62 << 20
        ),
        name="attend",
    )(q_pre, k_pre, v_low, gain_query, gain_key, cosine, sine, starts, cotangent, w_out)


class ScatterAll:
    @staticmethod
    def scratch(nz, rows, cols, kind, cut):
        vm, dma = pltpu.VMEM, pltpu.SemaphoreType.DMA
        return [
            vm((nz, 4, rows, cols), kind), vm((nz, 4, rows, cols), kind),
            vm((nz, rows, cols), kind), vm((nz, max(cut, 16), cols), kind),
            vm((nz, rows, cols), kind), vm((nz, max(rows - cut, 16), cols), kind),
            vm((nz + 1, rows, cols), kind),
        ] + [dma((4 * nz,))] * 3 + [dma((nz,))] * 9 + [dma((nz + 1,))]

    def __init__(self, nz, partial, out, refs, cut):
        (self.w, self.lp, self.rx, self.rxd, self.ry, self.ryd, self.rz,
         self.s_l, self.s_p, self.r_p, self.s_x, self.s_y, self.s_dx, self.s_dy, self.s_z,
         self.r_x, self.r_y, self.r_dx, self.r_dy, self.r_z) = refs
        self.nz, self.partial, self.out, self.cut = nz, partial, out, cut
        self.rows, self.cols = out.shape
        self.place = z, x, y, c = place()
        self.partner, self.xn, self.yn = (
            device(z, x, y, 1 - c), device(z, 1 - x, y, c), device(z, x, 1 - y, c))
        self.up, self.down = device(z + 1, x, y, c), device(z - 1, x, y, c)

    def block(self, zz, rel, cc):
        z, x, y, c = self.place
        xx = 1 - x if rel in (1, 3) else x
        yy = 1 - y if rel in (2, 3) else y
        return self.partial.at[
            pl.ds(pl.multiple_of((zz * 2 + xx) * self.rows, self.rows), self.rows),
            pl.ds(pl.multiple_of((yy * 2 + cc) * self.cols, self.cols), self.cols)]

    def pair(self, zz, rel):
        k = zz * 4 + rel
        return remote(self.block(zz, rel, 1 - self.place[3]), self.lp.at[zz, rel],
                      self.s_p.at[k], self.r_p.at[k], self.partner)

    def load(self, zz, rel):
        return pltpu.make_async_copy(
            self.block(zz, rel, self.place[3]), self.w.at[zz, rel], self.s_l.at[zz * 4 + rel])

    def across(self, zz):
        copies = []
        if self.cut > 0:
            copies.append(remote(self.w.at[zz, 3, pl.ds(0, self.cut)], self.rxd.at[zz],
                                 self.s_dx.at[zz], self.r_dx.at[zz], self.xn))
        if self.cut < self.rows:
            copies.append(remote(self.w.at[zz, 3, pl.ds(self.cut, self.rows - self.cut)],
                                 self.ryd.at[zz], self.s_dy.at[zz], self.r_dy.at[zz], self.yn))
        return copies

    def sides(self, zz):
        return (remote(self.w.at[zz, 1], self.rx.at[zz], self.s_x.at[zz], self.r_x.at[zz], self.xn),
                remote(self.w.at[zz, 2], self.ry.at[zz], self.s_y.at[zz], self.r_y.at[zz], self.yn))

    def line(self, zz, slot, where):
        return remote(self.w.at[zz, 0], self.rz.at[slot], self.s_z.at[zz], self.r_z.at[slot], where)

    def start(self):
        def step(k, carry):
            zz = far_first(self.nz, self.place[0], k)
            for rel in (3, 1, 2, 0):
                self.pair(zz, rel).start()
                self.load(zz, rel).start()
            return carry

        lax.fori_loop(0, self.nz, step, 0)

    def first(self, k):
        zz = far_first(self.nz, self.place[0], k)
        for rel in (3, 1, 2, 0):
            self.pair(zz, rel).wait_recv()
            self.load(zz, rel).wait()
            add_blocks(self.w.at[zz, rel], [self.lp.at[zz, rel]], 0, self.rows)
            if rel == 3:
                for copy in self.across(zz):
                    copy.start()

    def second(self, k):
        zz = far_first(self.nz, self.place[0], k)
        across, (to_x, to_y) = self.across(zz), self.sides(zz)
        if self.cut < self.rows:
            across[-1].wait_recv()
            add_blocks(self.w.at[zz, 1], [self.ryd.at[zz]], self.cut, self.rows - self.cut)
        to_x.start()
        if self.cut > 0:
            across[0].wait_recv()
            add_blocks(self.w.at[zz, 2], [self.rxd.at[zz]], 0, self.cut)
        to_y.start()

    def send_line(self, zz):
        z = self.place[0]
        pl.when(zz > z)(lambda: self.line(zz, zz, self.up).start())
        pl.when(zz == z - 1)(lambda: self.line(zz, self.nz, self.down).start())
        pl.when(zz < z - 1)(lambda: self.line(zz, zz, self.down).start())

    def passes(self, zz):
        z = self.place[0]
        return ((zz > z) & (z > 0)) | ((zz < z) & (z < self.nz - 1))

    def third(self, k):
        zz, z = far_first(self.nz, self.place[0], k), self.place[0]
        to_x, to_y = self.sides(zz)
        to_x.wait_recv()
        to_y.wait_recv()
        add_blocks(self.w.at[zz, 0], [self.rx.at[zz], self.ry.at[zz]], 0, self.rows)
        pl.when((zz != z) & jnp.logical_not(self.passes(zz)))(lambda: self.send_line(zz))

    def fourth(self, k):
        zz, z, nz = far_first(self.nz, self.place[0], k), self.place[0], self.nz

        @pl.when((zz != z) & self.passes(zz))
        def _():
            self.line(zz, zz, self.up).wait_recv()
            add_blocks(self.w.at[zz, 0], [self.rz.at[zz]], 0, self.rows)
            self.send_line(zz)

        @pl.when(zz == z)
        def _():
            finish_line(self, self.w.at[zz, 0], zz)

    def finish(self):
        z = self.place[0]

        def step(zz, carry):
            for rel in range(4):
                self.pair(zz, rel).wait_send()
            for copy in tuple(self.across(zz)) + tuple(self.sides(zz)):
                copy.wait_send()
            pl.when(zz != z)(lambda: self.line(zz, zz, self.up).wait_send())
            return carry

        lax.fori_loop(0, self.nz, step, 0)


def finish_line(self, own, zz):
    z, nz = self.place[0], self.nz
    below, above = self.rz.at[zz], self.rz.at[nz]
    pl.when(z > 0)(lambda: self.line(zz, zz, self.up).wait_recv())
    pl.when(z < nz - 1)(lambda: self.line(zz, nz, self.down).wait_recv())
    pl.when(z == 0)(lambda: add_blocks(own, [above], 0, self.rows, self.out))
    pl.when(z == nz - 1)(lambda: add_blocks(own, [below], 0, self.rows, self.out))
    pl.when((z > 0) & (z < nz - 1))(lambda: add_blocks(own, [below, above], 0, self.rows, self.out))


class ReduceRows:
    @staticmethod
    def scratch(nz, rows, cols, kind):
        vm, dma = pltpu.VMEM, pltpu.SemaphoreType.DMA
        return [vm((nz, rows, cols), kind), vm((nz, rows, cols), kind), vm((nz, rows, cols), kind),
                vm((nz + 1, rows, cols), kind)] + [dma((nz,))] * 3 + [dma((nz + 1,))]

    def __init__(self, nz, left, right, out, refs):
        self.w, self.sent, self.rx, self.rz, self.s_x, self.s_z, self.r_x, self.r_z = refs
        self.nz, self.left, self.right, self.out = nz, left, right, out
        self.rows = out.shape[0]
        self.place = z, x, y, c = place()
        self.xn = device(z, 1 - x, y, c)
        self.up, self.down = device(z + 1, x, y, c), device(z - 1, x, y, c)

    def make(self, zz, xx, ref):
        at = pl.ds(pl.multiple_of((zz * 2 + xx) * self.rows, self.rows), self.rows)
        ref[...] = dot_first(self.left[:, at], self.right[...]).astype(ref.dtype)

    def side(self, zz):
        return remote(self.sent.at[zz], self.rx.at[zz], self.s_x.at[zz], self.r_x.at[zz], self.xn)

    def line(self, zz, slot, where):
        return remote(self.w.at[zz], self.rz.at[slot], self.s_z.at[zz], self.r_z.at[slot], where)

    def start(self):
        def step(k, carry):
            self.send(k)
            return carry

        lax.fori_loop(0, self.nz, step, 0)

    def send(self, k):
        zz, x = far_first(self.nz, self.place[0], k), self.place[1]
        self.make(zz, 1 - x, self.sent.at[zz])
        self.side(zz).start()
        self.make(zz, x, self.w.at[zz])

    send_line = ScatterAll.send_line
    passes = ScatterAll.passes

    def first(self, k):
        zz, z = far_first(self.nz, self.place[0], k), self.place[0]
        self.side(zz).wait_recv()
        add_blocks(self.w.at[zz], [self.rx.at[zz]], 0, self.rows)
        pl.when((zz != z) & jnp.logical_not(self.passes(zz)))(lambda: self.send_line(zz))

    def second(self, k):
        zz, z, nz = far_first(self.nz, self.place[0], k), self.place[0], self.nz

        @pl.when((zz != z) & self.passes(zz))
        def _():
            self.line(zz, zz, self.up).wait_recv()
            add_blocks(self.w.at[zz], [self.rz.at[zz]], 0, self.rows)
            self.send_line(zz)

        @pl.when(zz == z)
        def _():
            finish_line(self, self.w.at[zz], zz)

    def finish(self):
        z = self.place[0]

        def step(zz, carry):
            self.side(zz).wait_send()
            pl.when(zz != z)(lambda: self.line(zz, zz, self.up).wait_send())
            return carry

        lax.fori_loop(0, self.nz, step, 0)


class ReduceCausal:
    @staticmethod
    def scratch(nz, rows, cols, kind):
        vm, dma = pltpu.VMEM, pltpu.SemaphoreType.DMA
        return [vm((nz, 2, 2, rows, cols), kind), vm((2, rows, cols), kind),
                dma((2 * nz,)), dma((2 * nz,)), dma((2,)), dma((2,))]

    def __init__(self, nz, sides, out, refs):
        self.got, self.across, self.s_z, self.r_z, self.s_x, self.r_x = refs
        self.nz, self.sides, self.out = nz, sides, out
        self.place = z, x, y, c = place()
        self.xn = device(z, 1 - x, y, c)
        self.to = (device(z - 1, x, y, c), device(z + 1, x, y, c))

    def line(self, zz, micro):
        k = zz * 2 + micro
        return remote(self.sides.at[zz, :, micro], self.got.at[zz, :, micro],
                      self.s_z.at[k], self.r_z.at[k], self.to[micro])

    def side(self, micro):
        z, x = self.place[:2]
        return remote(self.sides.at[z, 1 - x, micro], self.across.at[micro],
                      self.s_x.at[micro], self.r_x.at[micro], self.xn)

    def take(self, zz, micro):
        first = self.place[0] == (self.nz - 1 if micro == 0 else 0)

        @pl.when(jnp.logical_not(first))
        def _():
            self.line(zz, micro).wait_recv()
            for xx in range(2):
                add_blocks(self.sides.at[zz, xx, micro], [self.got.at[zz, xx, micro]], 0,
                           self.sides.shape[3])

    def turn(self, hop):
        z, nz = self.place[0], self.nz
        for micro in range(2):
            @pl.when(hop == (nz - 1 - z if micro == 0 else z))
            def _():
                def step(n, carry):
                    zz = n if micro == 0 else nz - 1 - n
                    self.take(zz, micro)
                    self.line(zz, micro).start()
                    return carry

                lax.fori_loop(0, z if micro == 0 else nz - 1 - z, step, 0)
                self.take(z, micro)
                self.side(micro).start()

    def finish(self):
        z, x = self.place[:2]
        for micro in range(2):
            self.side(micro).wait_recv()
            add_blocks(self.sides.at[z, x, micro], [self.across.at[micro]], 0, self.sides.shape[3],
                       self.out.at[micro])
        for micro in range(2):
            self.side(micro).wait_send()

            def step(n, carry):
                self.line(n if micro == 0 else self.nz - 1 - n, micro).wait_send()
                return carry

            lax.fori_loop(0, z if micro == 0 else self.nz - 1 - z, step, 0)


def attend_back_kernel(nz, gq_ref, cos_ref, sin_ref, start_ref, lse_ref, delta_ref, small_ref,
                       mid_all, heads_all, q_all, kv_all, grad_all, pre_all, out_part,
                       q_grad, gain_grad, kv_sum, out_sum, wo_sum, small_out,
                       mid_ref, heads_ref, q_ref, kv_ref, grad_ref, q_pre, s_in,
                       sides, acc, k_acc, v_acc, *refs):
    shards = 2 * nz
    shard = lax.axis_index("fsdp")
    width = kv_ref.shape[4] // 2
    block = q_ref.shape[0] // 2
    heads = q_ref.shape[1] // width
    z, x, y, c = place()
    count = shards + 2 * x
    low = jnp.bfloat16
    split = len(ScatterAll.scratch(nz, 16, 128, low, 0))
    outs = ScatterAll(nz, out_part, out_sum, refs[:split], 0)
    end = split + len(ReduceRows.scratch(nz, 16, 128, low))
    weights = ReduceRows(nz, mid_ref, heads_ref, wo_sum, refs[split:end])
    last = end + len(SmallSums.scratch(nz, (8, 128), jnp.float32))
    smalls = SmallSums(nz, small_ref, small_out, refs[end:last])
    keys_out = ReduceCausal(nz, sides, kv_sum, refs[last:])
    greet_all(lax.axis_index("fsdp"), lax.axis_index("tp"), shards, 4)
    outs.start()
    fetches = [pltpu.make_async_copy(src, dst, s_in.at[n]) for n, (src, dst) in enumerate((
        (mid_all, mid_ref), (heads_all, heads_ref), (q_all, q_ref), (kv_all, kv_ref),
        (grad_all, grad_ref), (pre_all, q_pre)))]
    for copy in fetches:
        copy.start()
    smalls.start()

    sides[...] = jnp.zeros_like(sides)
    acc[...] = jnp.zeros_like(acc)

    def attention(u):
        micro, here, key_place, owner = stream_unit(u, nz)
        bias = key_bias(micro, here, key_place, block, start_ref)
        both = kv_ref.at[owner // 2, owner % 2, micro]
        keys, values = both[:, :width], both[:, width:]
        q_rows = pl.ds(pl.multiple_of(micro * block, block), block)
        k_acc[...] = jnp.zeros_like(k_acc)
        v_acc[...] = jnp.zeros_like(v_acc)

        def head(h, carry):
            at = micro * heads + h
            cols = pl.ds(pl.multiple_of(h * width, width), width)
            query, grad = q_ref[q_rows, cols], grad_ref[q_rows, cols]
            scores = dot_last(keys, query) * width ** (-0.5) + bias
            probs = jnp.exp(scores - lse_ref[at])
            score_grad = (probs * (dot_last(values, grad) - delta_ref[at])).astype(low)
            v_acc[...] += dot_plain(probs.astype(low), grad)
            k_acc[...] += dot_plain(score_grad, query)
            acc[at] += dot_first(keys, score_grad)
            return carry

        lax.fori_loop(0, heads, head, 0, unroll=2)
        side = sides.at[owner // 2, owner % 2, micro]
        side[:, :width] = (k_acc[...] * width ** (-0.5)).astype(low)
        side[:, width:] = v_acc[...].astype(low)

    def close(at, total):
        micro, h = at // heads, at % heads
        here = pl.ds(pl.multiple_of(micro * block, block), block)
        cols = pl.ds(pl.multiple_of(h * width, width), width)
        turned = acc[at].T * width ** (-0.5)
        grad = turned * cos_ref[here, :] + pltpu.roll(turned * sin_ref[here, :], width // 2, 1)
        raw = q_pre[here, cols]
        scale = lax.rsqrt(jnp.mean(raw * raw, axis=1, keepdims=True) + norm_eps)
        inner = grad * gq_ref[...]
        mean = jnp.mean(raw * inner, axis=1, keepdims=True)
        q_grad[here, cols] = (scale * inner - raw * (scale * scale * scale * mean)).astype(low)
        return total + jnp.sum(grad * raw * scale, axis=0, keepdims=True)

    def close_all():
        gain_grad[...] = lax.fori_loop(
            0, 2 * heads, close, jnp.zeros(gain_grad.shape, jnp.float32)
        )

    def unit(u, carry):
        def at(fn, k):
            pl.when((k >= 0) & (k < nz))(lambda: fn(k))

        for n in range(4):
            pl.when(4 * u + n < count)(lambda: attention(4 * u + n))
        at(outs.second, u)
        at(weights.send, u + 1)
        at(outs.first, u + 2)
        pl.when(u == 1)(smalls.second)
        at(keys_out.turn, u - done)
        at(outs.third, u - 1)
        at(outs.fourth, u - 2)
        at(weights.second, u - 3)
        at(weights.first, u - 2)
        pl.when(u == done + 1)(close_all)
        return carry

    done = (shards + 2 - 1) // 4
    outs.first(0)
    for copy in fetches:
        copy.wait()
    weights.send(0)
    outs.first(1)
    lax.fori_loop(0, nz + 3, unit, 0)
    keys_out.finish()
    outs.finish()
    weights.finish()
    smalls.finish()


def attend_back(query, q_pre, gain_query, cosine, sine, keys_values, starts, log_total, delta,
                grad, small, middle_grad, heads_low, out_part, nz, collective_id):
    rows, columns = query.shape
    width = keys_values.shape[4] // 2
    heads = columns // width
    block = rows // 2
    cols = out_part.shape[1] // 4
    wo_shape = (middle_grad.shape[1] // (2 * nz), columns)
    any_space = pl.BlockSpec(memory_space=pl.ANY)
    vmem = pl.BlockSpec(memory_space=pltpu.VMEM)
    vm, shape, f32, low = pltpu.VMEM, jax.ShapeDtypeStruct, jnp.float32, jnp.bfloat16
    return pl.pallas_call(
        functools.partial(attend_back_kernel, nz),
        in_specs=[vmem] * 7 + [any_space] * 7,
        out_specs=[vmem] * 6,
        out_shape=[
            shape((rows, columns), low), shape((1, width), f32),
            shape((2, block, 2 * width), f32),
            shape((rows, cols), f32), shape(wo_shape, f32),
            shape((8 * nz,) + small.shape[1:], f32),
        ],
        scratch_shapes=[vm(middle_grad.shape, low)] + [vm((rows, columns), low)] * 2 + [
            vm((nz, 2, 2, block, 2 * width), low), vm((rows, columns), low),
            vm((rows, columns), f32), pltpu.SemaphoreType.DMA((6,)),
            vm((nz, 2, 2, block, 2 * width), low),
            vm((2 * heads, width, block), f32), vm((block, width), f32), vm((block, width), f32),
        ] + ScatterAll.scratch(nz, rows, cols, low, 0) + ReduceRows.scratch(nz, *wo_shape, low)
        + SmallSums.scratch(nz, small.shape[1:], f32)
        + ReduceCausal.scratch(nz, block, 2 * width, low),
        compiler_params=pltpu.CompilerParams(
            collective_id=collective_id, has_side_effects=True, vmem_limit_bytes=62 << 20
        ),
        name="attend_back",
    )(gain_query, cosine, sine, starts, log_total, delta, small, middle_grad, heads_low, query,
      keys_values, grad, q_pre, out_part)


def to_row(column, eye):
    return jnp.sum(jnp.where(eye, column, 0.0), axis=0, keepdims=True)


def to_column(row, eye):
    return jnp.sum(jnp.where(eye, row, 0.0), axis=1, keepdims=True)


def diagonal():
    shape = (128, 128)
    return lax.broadcasted_iota(jnp.int32, shape, 0) == lax.broadcasted_iota(jnp.int32, shape, 1)


class RowSums:
    @staticmethod
    def scratch(rows):
        dma = pltpu.SemaphoreType.DMA
        return [pltpu.VMEM((4, rows // 128, 128), jnp.float32), dma((3,)), dma((3,))]

    def __init__(self, refs):
        self.got, s, r = refs
        shard, group = lax.axis_index("fsdp"), lax.axis_index("tp")
        self.peers = [(shard, (group + k) % 4) for k in range(1, 4)]
        self.copies = [
            remote(self.got.at[0], self.got.at[k + 1], s.at[k], r.at[k], peer)
            for k, peer in enumerate(self.peers)
        ]

    def start(self):
        for copy in self.copies:
            copy.start()

    def wait(self):
        for copy in self.copies:
            copy.wait()

    def total(self, n):
        return self.got[0, pl.ds(n, 1), :] + self.got[1, pl.ds(n, 1), :] + (
            self.got[2, pl.ds(n, 1), :] + self.got[3, pl.ds(n, 1), :])


class ReduceCols:
    @staticmethod
    def scratch(rows, cols, kind):
        vm, dma = pltpu.VMEM, pltpu.SemaphoreType.DMA
        return [vm((2, rows, cols), kind), vm((2, rows, cols), kind), vm((rows, cols), kind),
                dma((2,)), dma((2,)), dma((2,)), dma, dma]

    def __init__(self, partial, out, refs):
        self.w, self.rp, self.ry, s_l, s_p, r_p, s_y, r_y = refs
        self.out = out
        self.rows, cols = out.shape
        z, x, y, c = place()
        self.partner, self.yn = device(z, x, y, 1 - c), device(z, x, 1 - y, c)

        def block(yy, cc):
            return partial.at[:, pl.ds(pl.multiple_of((yy * 2 + cc) * cols, cols), cols)]

        self.sends = [remote(block(yy, 1 - c), self.rp.at[k], s_p.at[k], r_p.at[k], self.partner)
                      for k, yy in enumerate((1 - y, y))]
        self.loads = [pltpu.make_async_copy(block(yy, c), self.w.at[k], s_l.at[k])
                      for k, yy in enumerate((1 - y, y))]
        self.across = remote(self.w.at[0], self.ry, s_y, r_y, self.yn)

    def start(self):
        for k in range(2):
            self.sends[k].start()
            self.loads[k].start()

    def first(self):
        self.loads[0].wait()
        self.sends[0].wait_recv()
        add_blocks(self.w.at[0], [self.rp.at[0]], 0, self.rows)
        self.across.start()

    def second(self):
        self.loads[1].wait()
        self.sends[1].wait_recv()
        self.across.wait_recv()
        add_blocks(self.w.at[1], [self.rp.at[1], self.ry], 0, self.rows, self.out)

    def finish(self):
        for send in self.sends:
            send.wait_send()
        self.across.wait_send()


class SmallSums:
    @staticmethod
    def scratch(nz, part, kind):
        dma = pltpu.SemaphoreType.DMA
        return [pltpu.VMEM((2 * nz,) + part, kind), dma((2 * nz,)), dma((2 * nz,)),
                dma((8 * nz,)), dma((8 * nz,))]

    def __init__(self, nz, values, out, refs):
        self.got, self.s_1, self.r_1, self.s_2, self.r_2 = refs
        self.values, self.out = values, out
        self.shards, self.devices = 2 * nz, 8 * nz
        self.shard, self.group = lax.axis_index("fsdp"), lax.axis_index("tp")
        self.me = self.shard * 4 + self.group

    def share(self, k):
        other = (self.shard + k) % self.shards
        return remote(self.values.at[other], self.got.at[k], self.s_1.at[k], self.r_1.at[k],
                      (other, self.group))

    def spread(self, k):
        other = (self.me + k) % self.devices
        return remote(self.out.at[self.me], self.out.at[self.me], self.s_2.at[k], self.r_2.at[k],
                      (other // 4, other % 4))

    def start(self):
        loop_from_one(self.shards, lambda k: self.share(k).start())

    def second(self):
        loop_from_one(self.shards, lambda k: self.share(k).wait())
        acc = self.values[self.shard]
        for k in range(1, self.shards):
            acc = acc + self.got[k]
        self.out[self.me] = acc
        loop_from_one(self.devices, lambda k: self.spread(k).start())

    def finish(self):
        loop_from_one(self.devices, lambda k: self.spread(k).wait())


def loop_from_one(count, fn):
    def step(k, carry):
        fn(k)
        return carry

    lax.fori_loop(1, count, step, 0)


def tail_kernel(nz, tok_ref, scale_ref, gain_ref, block_ref, small_ref, left_all, right_all, mid_all,
                gp_all, up_all, hid_all, xr_all, gs_all, normed_part,
                wq_out, wk_out, wv_out, token_out, block_out, small_out, dwg, dwu, dwd,
                left_ref, right_ref, mid_ref, s_m, w_sum, gp_ref, up_ref, hid_ref, x_panel, g_panel, o_gate, o_up, o_down, s_in, s_out,
                normed, token, s_w, r_w, s_l, s_g, r_g, *refs):
    z, x, y, c = place()
    shard, group = lax.axis_index("fsdp"), lax.axis_index("tp")
    shards = 2 * nz
    devices = 4 * shards
    me = shard * 4 + group
    rows, cols = tok_ref.shape
    width = cols * 4
    half = rows // 2
    panel = x_panel.shape[1]
    panels = xr_all.shape[1] // panel
    f32, low = jnp.float32, jnp.bfloat16
    n_w, n_c = len(ReduceRows.scratch(nz, 16, 128, low)), len(ReduceCols.scratch(16, 128, low))
    weights = ReduceRows(nz, left_ref, right_ref, w_sum, refs[:n_w])
    columns = ReduceCols(normed_part, normed, refs[n_w : n_w + n_c])
    sums = RowSums(refs[n_w + n_c :])
    mirror = device(nz - 1 - z, x, y, c)
    greet_all(shard, group, shards, 4)
    columns.start()
    fetches = [pltpu.make_async_copy(src, dst, s_m.at[n]) for n, (src, dst) in enumerate((
        (left_all, left_ref), (right_all, right_ref), (mid_all, mid_ref)))]
    for copy in fetches:
        copy.start()
    for copy in fetches:
        copy.wait()
    weights.start()
    top, bottom = pl.ds(0, half), pl.ds(half, half)
    swaps = [remote(src.at[bottom], dst.at[bottom], s_w.at[n], r_w.at[n], mirror)
             for n, (src, dst) in enumerate(((token, token_out), (block_ref, block_out)))]
    keeps = [pltpu.make_async_copy(src.at[top], dst.at[top], s_l.at[n])
             for n, (src, dst) in enumerate(((token, token_out), (block_ref, block_out)))]
    swaps[1].start()
    keeps[1].start()

    def loads(n):
        at = pl.ds(pl.multiple_of(n * panel, panel), panel)
        return (pltpu.make_async_copy(xr_all.at[:, at], x_panel, s_in.at[0]),
                pltpu.make_async_copy(gs_all.at[:, at], g_panel, s_in.at[1]))

    def stores(n):
        at = pl.ds(pl.multiple_of(n * panel, panel), panel)
        return (pltpu.make_async_copy(o_gate, dwg.at[at, :], s_out.at[0]),
                pltpu.make_async_copy(o_up, dwu.at[at, :], s_out.at[1]),
                pltpu.make_async_copy(o_down, dwd.at[:, at], s_out.at[2]))

    whole = [pltpu.make_async_copy(src, dst, s_in.at[2 + n])
             for n, (src, dst) in enumerate(((gp_all, gp_ref), (up_all, up_ref), (hid_all, hid_ref)))]
    for copy in tuple(whole) + loads(0):
        copy.start()
    small_out[me] = small_ref[...]

    def expert_weights(n):
        @pl.when(n == 0)
        def _():
            for copy in whole:
                copy.wait()

        for copy in loads(n):
            copy.wait()

        @pl.when(n > 0)
        def _():
            for copy in stores(n):
                copy.wait()

        o_gate[...] = dot_first(x_panel[...], gp_ref[...])
        o_up[...] = dot_first(x_panel[...], up_ref[...])
        o_down[...] = dot_first(g_panel[...], hid_ref[...]).T
        for copy in stores(n):
            copy.start()

        @pl.when(n < panels - 1)
        def _():
            for copy in loads(n + 1):
                copy.start()

    def token_sums():
        eye = diagonal()

        def step(n, gains):
            here = pl.ds(pl.multiple_of(n * 128, 128), 128)
            tok, grad = tok_ref[here, :].astype(f32), normed[here, :]
            product = tok * (grad * gain_ref[...])
            sums.got[0, pl.ds(n, 1), :] = to_row(jnp.sum(product, axis=1, keepdims=True), eye)
            return gains + jnp.sum(grad * tok * scale_ref[here, :], axis=0, keepdims=True)

        gains = lax.fori_loop(0, rows // 128, step, jnp.zeros((1, cols), f32))
        for n in range(cols // 128):
            small_out[me, pl.ds(n, 1), :] = gains[:, n * 128 : (n + 1) * 128]

    def token_grads():
        eye = diagonal()

        def step(n, carry):
            here = pl.ds(pl.multiple_of(n * 128, 128), 128)
            mean = to_column(sums.total(n), eye) / width
            scale = scale_ref[here, :]
            token[here, :] = (
                mid_ref[here, :]
                + scale * (gain_ref[...] * normed[here, :])
                - tok_ref[here, :].astype(f32) * (scale * scale * scale * mean)
            ).astype(low)
            return carry

        lax.fori_loop(0, rows // 128, step, 0)

    def spread(k):
        other = (me + k) % devices
        return remote(small_out.at[me], small_out.at[me], s_g.at[k], r_g.at[k],
                      (other // 4, other % 4))

    columns.first()

    def unit(u, carry):
        @pl.when(u == 1)
        def _():
            sums.wait()
            token_grads()
            swaps[0].start()
            keeps[0].start()

        pl.when((u >= 1) & (u <= nz))(lambda: weights.second(u - 1))

        @pl.when(u < panels // 2)
        def _():
            expert_weights(2 * u)
            expert_weights(2 * u + 1)

        @pl.when(u == 0)
        def _():
            columns.second()
            token_sums()
            sums.start()
            loop_from_one(devices, lambda k: spread(k).start())

        pl.when(u < nz)(lambda: weights.first(u))
        return carry

    lax.fori_loop(0, max(nz + 1, panels // 2), unit, 0)
    loop_from_one(devices, lambda k: spread(k).wait())
    for copy in swaps + keeps:
        copy.wait()
    for copy in stores(panels - 1):
        copy.wait()
    first, second = wq_out.shape[1], wq_out.shape[1] + wk_out.shape[1]
    wq_out[...] = w_sum[:, :first]
    wk_out[...] = w_sum[:, first:second]
    wv_out[...] = w_sum[:, second:]
    columns.finish()
    weights.finish()


def tail(gate_grad, up_grad, hidden, tokens, middle_grad, scale, gain, block_out, small, normed_low,
         pre_grad, query_width, rows_in, pair_grad, normed_part, nz, collective_id):
    rows, cols = tokens.shape
    pairs, features = rows_in.shape
    hidden_width = hidden.shape[1]
    panel = 256
    w_shape = (normed_low.shape[1] // (2 * nz), pre_grad.shape[1])
    kv_width = (pre_grad.shape[1] - query_width) // 2
    devices = 8 * nz
    any_space = pl.BlockSpec(memory_space=pl.ANY)
    vmem = pl.BlockSpec(memory_space=pltpu.VMEM)
    vm, shape, f32, low = pltpu.VMEM, jax.ShapeDtypeStruct, jnp.float32, jnp.bfloat16
    dma = pltpu.SemaphoreType.DMA
    return pl.pallas_call(
        functools.partial(tail_kernel, nz),
        in_specs=[vmem] * 5 + [any_space] * 9,
        out_specs=[vmem] * 3 + [any_space, any_space, vmem] + [any_space] * 3,
        out_shape=[
            shape((w_shape[0], query_width), f32), shape((w_shape[0], kv_width), f32),
            shape((w_shape[0], kv_width), f32), shape((rows, cols), low), shape((rows, cols), low),
            shape((devices,) + small.shape, f32),
            shape((features, hidden_width), f32), shape((features, hidden_width), f32),
            shape((hidden_width, features), f32),
        ],
        scratch_shapes=[vm(normed_low.shape, low), vm(pre_grad.shape, low), vm((rows, cols), f32),
                        dma((3,)), vm(w_shape, f32)] + [vm((pairs, hidden_width), low)] * 3 + [
            vm((pairs, panel), low), vm((pairs, panel), low),
            vm((panel, hidden_width), f32), vm((panel, hidden_width), f32),
            vm((hidden_width, panel), f32), dma((5,)), dma((3,)),
            vm((rows, cols), f32), vm((rows, cols), low),
            dma((2,)), dma((2,)), dma((2,)), dma((devices,)), dma((devices,)),
        ] + ReduceRows.scratch(nz, *w_shape, low) + ReduceCols.scratch(rows, cols, low)
        + RowSums.scratch(rows),
        compiler_params=pltpu.CompilerParams(
            collective_id=collective_id, has_side_effects=True, vmem_limit_bytes=62 << 20
        ),
        name="tail",
    )(tokens, scale, gain, block_out, small, normed_low, pre_grad, middle_grad, gate_grad, up_grad,
      hidden, rows_in, pair_grad, normed_part)


def join_kernel(nz, tok_ref, gain_ref, attn_part, middle_ref, scale_ref, low_ref, all_ref, *refs):
    z, x, y, c = place()
    rows, cols = tok_ref.shape
    f32 = jnp.float32
    n_c, n_s = len(ReduceCols.scratch(16, 128, jnp.bfloat16)), 3
    columns = ReduceCols(attn_part, middle_ref, refs[:n_c])
    sums = RowSums(refs[n_c : n_c + n_s])
    gather = GatherAll(nz, low_ref, all_ref, refs[n_c + n_s :], rows // 2)
    greet([(None, gather.xn), (z < nz - 1, gather.up), (z > 0, gather.down)]
          + [(None, peer) for peer in sums.peers])
    columns.start()
    eye = diagonal()
    columns.first()
    columns.second()

    def add(n, carry):
        here = pl.ds(pl.multiple_of(n * 128, 128), 128)
        total = middle_ref[here, :] + tok_ref[here, :].astype(f32)
        middle_ref[here, :] = total
        sums.got[0, pl.ds(n, 1), :] = to_row(jnp.sum(total * total, axis=1, keepdims=True), eye)
        return carry

    def norm(n, carry):
        here = pl.ds(pl.multiple_of(n * 128, 128), 128)
        scale = lax.rsqrt(to_column(sums.total(n), eye) / (4 * cols) + norm_eps)
        scale_ref[here, :] = scale
        low_ref[here, :] = (middle_ref[here, :] * scale * gain_ref[...]).astype(low_ref.dtype)
        return carry

    lax.fori_loop(0, rows // 128, add, 0)
    sums.start()
    sums.wait()
    lax.fori_loop(0, rows // 128, norm, 0)
    gather.own().start()
    gather.own().wait()

    def tick(k, carry):
        pl.when(k < nz)(lambda: gather.first(k))
        pl.when((k >= 1) & (k <= nz))(lambda: gather.second(k - 1))
        pl.when(k >= 2)(lambda: gather.third(k - 2))
        return carry

    lax.fori_loop(0, nz + 2, tick, 0)
    gather.finish()
    columns.finish()


def join(tokens, gain, attn_part, nz, collective_id):
    rows, cols = tokens.shape
    any_space = pl.BlockSpec(memory_space=pl.ANY)
    vmem = pl.BlockSpec(memory_space=pltpu.VMEM)
    shape, f32, low = jax.ShapeDtypeStruct, jnp.float32, jnp.bfloat16
    return pl.pallas_call(
        functools.partial(join_kernel, nz),
        in_specs=[vmem] * 2 + [any_space],
        out_specs=[vmem] * 3 + [any_space],
        out_shape=[shape((rows, cols), f32), shape((rows, 1), f32), shape((rows, cols), low),
                   shape((rows * 2 * nz, cols * 4), low)],
        scratch_shapes=ReduceCols.scratch(rows, cols, low) + RowSums.scratch(rows)
        + GatherAll.scratch(nz),
        compiler_params=pltpu.CompilerParams(
            collective_id=collective_id, has_side_effects=True, vmem_limit_bytes=62 << 20
        ),
        name="join",
    )(tokens, gain, attn_part)


def turn_kernel(middle_ref, scale_ref, inner_ref, grad_ref, out_ref, all_ref, low_ref, lsem,
                s_p, r_p, s_y, r_y, *refs):
    z, x, y, c = place()
    rows, cols = middle_ref.shape
    sums = RowSums(refs)
    partner, yn = device(z, x, y, 1 - c), device(z, x, 1 - y, c)
    greet([(None, peer) for peer in sums.peers])
    eye = diagonal()

    def block(yy):
        return all_ref.at[:, pl.ds(pl.multiple_of((yy * 2 + c) * cols, cols), cols)]

    def dots(n, carry):
        here = pl.ds(pl.multiple_of(n * 128, 128), 128)
        product = middle_ref[here, :] * inner_ref[here, :]
        sums.got[0, pl.ds(n, 1), :] = to_row(jnp.sum(product, axis=1, keepdims=True), eye)
        return carry

    def grads(n, carry):
        here = pl.ds(pl.multiple_of(n * 128, 128), 128)
        mean = to_column(sums.total(n), eye) / (4 * cols)
        scale = scale_ref[here, :]
        out = (grad_ref[here, :] + scale * inner_ref[here, :]
               - middle_ref[here, :] * (scale * scale * scale * mean))
        out_ref[here, :] = out
        low_ref[here, :] = out.astype(low_ref.dtype)
        return carry

    lax.fori_loop(0, rows // 128, dots, 0)
    sums.start()
    sums.wait()
    lax.fori_loop(0, rows // 128, grads, 0)
    to_y = remote(low_ref, block(y), s_y, r_y, yn)
    to_pair = remote(low_ref, block(y), s_p.at[0], r_p.at[0], partner)
    own = pltpu.make_async_copy(low_ref, block(y), lsem)
    on = remote(block(1 - y), block(1 - y), s_p.at[1], r_p.at[1], partner)
    for copy in (to_y, to_pair, own):
        copy.start()
    to_y.wait_recv()
    on.start()
    to_pair.wait()
    on.wait()
    to_y.wait_send()
    own.wait()


def turn(middle, scale, inner, grad, collective_id):
    rows, cols = middle.shape
    any_space = pl.BlockSpec(memory_space=pl.ANY)
    vmem = pl.BlockSpec(memory_space=pltpu.VMEM)
    shape, f32, low = jax.ShapeDtypeStruct, jnp.float32, jnp.bfloat16
    dma = pltpu.SemaphoreType.DMA
    return pl.pallas_call(
        turn_kernel,
        in_specs=[vmem] * 4,
        out_specs=[vmem, any_space],
        out_shape=[shape((rows, cols), f32), shape((rows, cols * 4), low)],
        scratch_shapes=[pltpu.VMEM((rows, cols), low), dma, dma((2,)), dma((2,)), dma, dma]
        + RowSums.scratch(rows),
        compiler_params=pltpu.CompilerParams(
            collective_id=collective_id, has_side_effects=True, vmem_limit_bytes=62 << 20
        ),
        name="turn",
    )(middle, scale, inner, grad)


def gathered_body(
    tokens,
    cotangent,
    routes,
    doc_ids,
    gain_attn,
    w_query,
    key_weight,
    value_weight,
    w_out,
    gain_query,
    key_norm_gain,
    gain_moe,
    router,
    w_gate,
    w_up,
    w_down,
):
    shard_count = lax.axis_size("fsdp")
    group_count = lax.axis_size("tp")
    shard_index = lax.axis_index("fsdp")
    group_index = lax.axis_index("tp")
    nz = shard_count // 2
    f32, low = jnp.float32, jnp.bfloat16
    row_count, slice_width = tokens.shape
    model_width = slice_width * group_count
    micro_count, micro_rows = doc_ids.shape
    head_width = gain_query.shape[0]
    query_width, kv_width = w_query.shape[1], key_weight.shape[1]
    query_local = query_width // head_width
    kv_local = kv_width // head_width
    group_width = query_local // kv_local
    expert_total = router.shape[1]
    capacity = max(2, 2 * micro_rows * TOPK // expert_total)
    block_keys = micro_rows * math.gcd(shard_count, max(1, 512 // micro_rows))
    my_columns = group_index * slice_width

    mirror_index = mirrored(nz, shard_index)
    owners = jnp.stack([shard_index, mirror_index])

    small = jnp.concatenate([routes.reshape(-1), doc_ids.reshape(-1)])
    small_rows = -(-small.shape[0] // 1024) * 8
    small = jnp.pad(small, (0, small_rows * 128 - small.shape[0])).reshape(small_rows, 128)
    small_all, wq_all, wk_all, wv_all, tokens, full_tokens = gather_rows(
        [small, w_query, key_weight, value_weight], nz, 2, [tokens]
    )
    small_all = small_all.reshape(shard_count, small_rows * 128)
    routes_all = small_all[:, : row_count * TOPK].reshape(shard_count * row_count, TOPK)
    ids_all = small_all[:, row_count * TOPK : row_count * (TOPK + 1)].reshape(
        shard_count, micro_count, micro_rows
    )
    doc_range = jnp.arange(DOCS)
    doc_totals = jnp.sum((ids_all[..., None] == doc_range).astype(jnp.int32), axis=(0, 2))
    doc_begin = jnp.cumsum(doc_totals, axis=1) - doc_totals
    query_index = owners[:, None] * micro_rows + jnp.arange(micro_rows)
    my_ids = jnp.stack(
        [lax.dynamic_index_in_dim(ids_all[:, m], owners[m], 0, False) for m in range(micro_count)]
    )
    query_start = jnp.sum(
        jnp.where(my_ids[:, :, None] == doc_range, doc_begin[:, None, :], 0), axis=2
    )
    positions = (query_index - query_start).reshape(row_count)
    cosine_lookup, sine_lookup = rope_tables(positions, head_width)

    full_tokens = full_tokens.astype(f32)
    token_mean = jnp.mean(full_tokens * full_tokens, axis=-1, keepdims=True)
    token_scale = lax.rsqrt(token_mean + norm_eps)
    normed_low = (full_tokens * token_scale * gain_attn).astype(low)
    query_pre = jnp.dot(normed_low, wq_all, preferred_element_type=f32)
    key_pre = jnp.dot(normed_low, wk_all, preferred_element_type=f32)
    value_low = jnp.dot(normed_low, wv_all, preferred_element_type=f32).astype(low)
    turned_sine = jnp.where(jnp.arange(head_width) < head_width // 2, -sine_lookup, sine_lookup)
    query_gain, key_gain = gain_query.reshape(1, head_width), key_norm_gain.reshape(1, head_width)
    starts = query_start.reshape(micro_count, 1, micro_rows).astype(jnp.int32)
    query_low, heads_low, head_out, log_total, keys_values, grads_all, wo_all = attend(
        query_pre, key_pre, value_low, query_gain, key_gain, cosine_lookup, turned_sine, starts,
        cotangent, w_out, nz, 3,
    )
    attn_part = dot_last(heads_low, wo_all).astype(low)
    gain_slice = lax.dynamic_slice_in_dim(gain_moe, my_columns, slice_width)
    middle, scale, moe_low, _, out_part, back, gates_grad, gates, *kept = run_experts(
        tokens, gain_slice.reshape(1, slice_width), router, attn_part, grads_all, routes_all,
        w_gate[0], w_up[0], w_down[0], micro_rows, capacity, nz, 8,
    )
    rows_in, pair_grad, hidden_low, gate_pre_low, up_pre_low = (
        array.reshape(-1, array.shape[2]) for array in kept
    )
    gates_grad = gates_grad.reshape(expert_total, row_count).T
    logit_grad = gates * (gates_grad - jnp.sum(gates * gates_grad, axis=1, keepdims=True))
    router_slice = lax.dynamic_slice_in_dim(router, my_columns, slice_width).astype(f32)
    moe_grad = back + lax.dot_general(
        logit_grad, router_slice, (((1,), (1,)), ((), ())), precision=highest_precision
    )
    router_part = lax.dot_general(
        moe_low.astype(f32), logit_grad, (((0,), (0,)), ((), ())), precision=highest_precision
    )
    gain_moe_part = jnp.sum(moe_grad * middle * scale, axis=0)
    swapped_grad = lax.dynamic_slice(
        grads_all, (mirror_index * row_count + micro_rows, my_columns), (micro_rows, slice_width)
    )
    grad_slice = jnp.concatenate([cotangent[:micro_rows], swapped_grad], axis=0).astype(f32)
    inner = gain_slice * moe_grad
    middle_grad, middle_low = turn(middle, scale, inner, grad_slice, 11)
    heads_grad = jnp.dot(middle_low, wo_all, preferred_element_type=f32).astype(low)
    delta = jnp.sum(
        (heads_grad.astype(f32) * head_out).reshape(micro_count, micro_rows, query_local, head_width),
        axis=3,
    ).transpose(0, 2, 1).reshape(micro_count * query_local, 1, micro_rows)
    pieces = [gain_moe_part, router_part.reshape(-1)]
    length = sum(piece.shape[0] for piece in pieces)
    part_rows = -(-length // (shard_count * 1024)) * 8
    flat = jnp.concatenate(
        pieces + [jnp.zeros((shard_count * part_rows * 128 - length,), f32)]
    ).reshape(shard_count, part_rows, 128)
    query_pre_low, gain_query_part, sides, out_sum, w_out_grad, summed = attend_back(
        query_low, query_pre, query_gain, cosine_lookup, turned_sine, keys_values, starts, log_total,
        delta, heads_grad, flat, middle_low, heads_low, out_part, nz, 12,
    )
    block_out = (middle + out_sum).astype(low)
    sides = sides.reshape(row_count, 2 * kv_width)

    def shape_keys(key_raw, key_gain):
        return rotary_apply(root_mean_norm(key_raw, key_gain), cosine_lookup, sine_lookup)

    key_pre_grad, gain_key_part = jax.vjp(shape_keys, key_pre, key_norm_gain)[1](sides[:, :kv_width])
    key_pre_low = key_pre_grad.astype(low)
    value_pre_low = sides[:, kv_width:].astype(low)
    normed_part = (
        dot_last(query_pre_low, wq_all)
        + dot_last(key_pre_low, wk_all)
        + dot_last(value_pre_low, wv_all)
    ).astype(low)
    pre_low = jnp.concatenate([query_pre_low, key_pre_low, value_pre_low], axis=1)
    gain_rows = slice_width // 128
    gains = jnp.concatenate(
        [jnp.zeros((slice_width,), f32), gain_query_part.reshape(-1), gain_key_part,
         jnp.zeros(((8 - gain_rows - 2) * 128,), f32)]
    ).reshape(8, 128)
    attn_gain = lax.dynamic_slice_in_dim(gain_attn, my_columns, slice_width)
    w_query_grad, w_key_grad, w_value_grad, token_grad, block_out, gains, *expert_grads = tail(
        gate_pre_low, up_pre_low, hidden_low, tokens, middle_grad, token_scale,
        attn_gain.reshape(1, slice_width), block_out, gains, normed_low, pre_low, query_width, rows_in,
        pair_grad, normed_part, nz, 15,
    )
    summed = summed.reshape(shard_count, group_count, part_rows * 128).transpose(
        1, 0, 2
    ).reshape(group_count, shard_count * part_rows * 128)
    gains = gains.reshape(shard_count, group_count, 8, 128)
    return (
        block_out,
        token_grad,
        jnp.sum(gains[:, :, :gain_rows], axis=0).reshape(-1),
        w_query_grad,
        w_key_grad,
        w_value_grad,
        w_out_grad,
        jnp.sum(gains[:, :, gain_rows], axis=(0, 1)),
        jnp.sum(gains[:, :, gain_rows + 1], axis=(0, 1)),
        summed[:, :slice_width].reshape(-1),
        summed[:, slice_width:length].reshape(router.shape),
        expert_grads[0][None],
        expert_grads[1][None],
        expert_grads[2][None],
    )


def solution(mesh):
    small = mesh.shape["fsdp"] * mesh.shape["tp"] <= 32 and mesh.shape["tp"] == 4
    return jax.shard_map(
        gathered_body if small else body,
        mesh=mesh,
        in_specs=(
            P("fsdp", "tp"),
            P("fsdp", "tp"),
            P("fsdp", None),
            P(None, "fsdp"),
            P(),
            P("fsdp", "tp"),
            P("fsdp", "tp"),
            P("fsdp", "tp"),
            P("fsdp", "tp"),
            P(),
            P(),
            P(),
            P(),
            P(("fsdp", "tp"), None, None),
            P(("fsdp", "tp"), None, None),
            P(("fsdp", "tp"), None, None),
        ),
        out_specs=(
            P("fsdp", "tp"),
            P("fsdp", "tp"),
            P(),
            P("fsdp", "tp"),
            P("fsdp", "tp"),
            P("fsdp", "tp"),
            P("fsdp", "tp"),
            P(),
            P(),
            P(),
            P(),
            P(("fsdp", "tp"), None, None),
            P(("fsdp", "tp"), None, None),
            P(("fsdp", "tp"), None, None),
        ),
        check_vma=False,
    )
```

```python
import functools
import math

import jax
import jax.numpy as jnp
from jax import lax
from jax.experimental import pallas as pl
from jax.experimental.pallas import tpu as pltpu
from jax.sharding import PartitionSpec as P

TOPK = 8
DOCS = 4


theta_base = 1000000.0
norm_eps = 1e-06
masked_score = -1e30
highest_precision = lax.Precision.HIGHEST


def root_mean_norm(row_block, gain_row):
    return (
        row_block
        * lax.rsqrt(jnp.mean(row_block * row_block, axis=-1, keepdims=True) + norm_eps)
        * gain_row
    )


def rotary_apply(row_block, cosine_lookup, sine_lookup):
    half_width = row_block.shape[-1] // 2
    turned = jnp.concatenate([-row_block[..., half_width:], row_block[..., :half_width]], axis=-1)
    return row_block * cosine_lookup + turned * sine_lookup


def rope_tables(positions, head_width):
    half_width = head_width // 2
    frequency = theta_base ** (
        -2.0 * jnp.arange(half_width, dtype=jnp.int32).astype(jnp.float32) / head_width
    )
    angles = positions.astype(jnp.float32)[:, None] * frequency[None, :]
    cosine_lookup = jnp.cos(angles)
    sine_lookup = jnp.sin(angles)
    return (
        jnp.concatenate([cosine_lookup, cosine_lookup], axis=-1),
        jnp.concatenate([sine_lookup, sine_lookup], axis=-1),
    )


def swiglu(gate_pre, up_pre):
    return jax.nn.silu(gate_pre) * up_pre


def dot_first(left_side, right_side):
    return lax.dot_general(
        left_side, right_side, (((0,), (0,)), ((), ())), preferred_element_type=jnp.float32
    )


def dot_last(left_side, right_side):
    return lax.dot_general(
        left_side, right_side, (((1,), (1,)), ((), ())), preferred_element_type=jnp.float32
    )


def gather_weights(w_query, key_weight, value_weight, w_out):
    return (
        lax.all_gather(w_query, "fsdp", axis=0, tiled=True),
        lax.all_gather(key_weight, "fsdp", axis=0, tiled=True),
        lax.all_gather(value_weight, "fsdp", axis=0, tiled=True),
        lax.all_gather(w_out, "fsdp", axis=0, tiled=True),
    )


def gather_keys(keys_low, values_low):
    return (
        lax.all_gather(keys_low, "fsdp", axis=0, tiled=True),
        lax.all_gather(values_low, "fsdp", axis=0, tiled=True),
    )


def send_rows(buffer):
    return lax.all_to_all(buffer, "fsdp", split_axis=0, concat_axis=0, tiled=True)


def return_rows(buffer):
    return lax.all_to_all(buffer, "fsdp", split_axis=0, concat_axis=0, tiled=True)


def to_heads(per_token, kv_local, group_width):
    token_count, head_total, head_width = per_token.shape
    grouped_heads = per_token.reshape(token_count, kv_local, group_width, head_width)
    return grouped_heads.transpose(1, 2, 0, 3).reshape(
        kv_local, group_width * token_count, head_width
    )


def to_tokens(per_head, group_width):
    kv_local, row_count, head_width = per_head.shape
    token_count = row_count // group_width
    grouped_heads = per_head.reshape(kv_local, group_width, token_count, head_width)
    return grouped_heads.transpose(2, 0, 1, 3).reshape(
        token_count, kv_local * group_width * head_width
    )


def key_block(keys_all, key_start, block_keys, kv_local, head_width):
    return lax.dynamic_slice_in_dim(keys_all, key_start, block_keys, 0).reshape(
        block_keys, kv_local, head_width
    )


def block_scores(queries, keys_part, key_start, query_index, query_start):
    head_width = queries.shape[-1]
    scores = jnp.einsum(
        "hrd,khd->hrk", queries, keys_part, preferred_element_type=jnp.float32
    ) * head_width ** (-0.5)
    key_index = key_start + jnp.arange(keys_part.shape[0])
    allowed = (key_index[None, :] >= query_start[:, None]) & (
        key_index[None, :] <= query_index[:, None]
    )
    return (jnp.where(allowed[None], scores, masked_score), allowed)


def attend_forward(queries, keys_all, values_all, query_index, query_start, block_keys):
    kv_local, row_count, head_width = queries.shape
    lowest_block = jnp.min(query_start) // block_keys
    highest_block = jnp.max(query_index) // block_keys + 1

    def visit_block(block_index, running):
        run_peak, run_total, run_acc = running
        key_start = block_index * block_keys
        keys_part = key_block(keys_all, key_start, block_keys, kv_local, head_width)
        values_part = key_block(values_all, key_start, block_keys, kv_local, head_width)
        scores, allowed = block_scores(queries, keys_part, key_start, query_index, query_start)
        new_peak = jnp.maximum(run_peak, jnp.max(scores, axis=-1))
        weights = jnp.where(allowed[None], jnp.exp(scores - new_peak[..., None]), 0.0)
        factor = jnp.exp(run_peak - new_peak)
        run_total = run_total * factor + jnp.sum(weights, axis=-1)
        run_acc = run_acc * factor[..., None] + jnp.einsum(
            "hrk,khd->hrd",
            weights.astype(jnp.bfloat16),
            values_part,
            preferred_element_type=jnp.float32,
        )
        return (new_peak, run_total, run_acc)

    start_state = (
        jnp.full((kv_local, row_count), masked_score, jnp.float32),
        jnp.zeros((kv_local, row_count), jnp.float32),
        jnp.zeros((kv_local, row_count, head_width), jnp.float32),
    )
    run_peak, run_total, run_acc = lax.fori_loop(
        lowest_block, highest_block, visit_block, start_state
    )
    return (run_acc / run_total[..., None], run_peak + jnp.log(run_total))


def attend_backward(
    queries,
    keys_all,
    values_all,
    query_index,
    query_start,
    block_keys,
    outputs,
    log_total,
    grad_low,
):
    kv_local, row_count, head_width = queries.shape
    key_count = keys_all.shape[0]
    score_scale = head_width ** (-0.5)
    row_delta = jnp.sum(grad_low.astype(jnp.float32) * outputs, axis=-1)
    lowest_block = jnp.min(query_start) // block_keys
    highest_block = jnp.max(query_index) // block_keys + 1

    def visit_block(block_index, running):
        query_acc, key_acc, value_acc = running
        key_start = block_index * block_keys
        keys_part = key_block(keys_all, key_start, block_keys, kv_local, head_width)
        values_part = key_block(values_all, key_start, block_keys, kv_local, head_width)
        scores, allowed = block_scores(queries, keys_part, key_start, query_index, query_start)
        prob_block = jnp.where(allowed[None], jnp.exp(scores - log_total[..., None]), 0.0)
        prob_grad = jnp.einsum(
            "hrd,khd->hrk", grad_low, values_part, preferred_element_type=jnp.float32
        )
        score_grad = (prob_block * (prob_grad - row_delta[..., None])).astype(jnp.bfloat16)
        query_acc = (
            query_acc
            + jnp.einsum("hrk,khd->hrd", score_grad, keys_part, preferred_element_type=jnp.float32)
            * score_scale
        )
        key_part = (
            jnp.einsum("hrk,hrd->khd", score_grad, queries, preferred_element_type=jnp.float32)
            * score_scale
        )
        value_part = jnp.einsum(
            "hrk,hrd->khd",
            prob_block.astype(jnp.bfloat16),
            grad_low,
            preferred_element_type=jnp.float32,
        )
        key_acc = lax.dynamic_update_slice_in_dim(
            key_acc, key_part.reshape(block_keys, kv_local * head_width), key_start, 0
        )
        value_acc = lax.dynamic_update_slice_in_dim(
            value_acc, value_part.reshape(block_keys, kv_local * head_width), key_start, 0
        )
        return (query_acc, key_acc, value_acc)

    start_state = (
        jnp.zeros((kv_local, row_count, head_width), jnp.float32),
        jnp.zeros((key_count, kv_local * head_width), jnp.float32),
        jnp.zeros((key_count, kv_local * head_width), jnp.float32),
    )
    return lax.fori_loop(lowest_block, highest_block, visit_block, start_state)


def body(
    tokens,
    cotangent,
    routes,
    doc_ids,
    gain_attn,
    w_query,
    key_weight,
    value_weight,
    w_out,
    gain_query,
    key_norm_gain,
    gain_moe,
    router,
    w_gate,
    w_up,
    w_down,
):
    shard_count = lax.axis_size("fsdp")
    group_count = lax.axis_size("tp")
    shard_index = lax.axis_index("fsdp")
    group_index = lax.axis_index("tp")
    full_tokens, full_grads = (
        lax.all_gather(tokens, "tp", axis=1, tiled=True),
        lax.all_gather(cotangent, "tp", axis=1, tiled=True),
    )
    slice_width = tokens.shape[1]
    model_width = full_tokens.shape[1]
    micro_count, micro_rows = doc_ids.shape
    head_width = gain_query.shape[0]
    query_local = w_query.shape[1] // head_width
    kv_local = key_weight.shape[1] // head_width
    group_width = query_local // kv_local
    expert_total = router.shape[1]
    capacity = max(2, 2 * micro_rows * TOPK // expert_total)
    slot_total = shard_count * capacity
    pair_total = micro_rows * TOPK
    block_keys = micro_rows * math.gcd(shard_count, max(1, 512 // micro_rows))
    doc_range = jnp.arange(DOCS)
    expert_range = jnp.arange(expert_total)
    local_counts = jnp.sum((doc_ids[:, :, None] == doc_range).astype(jnp.float32), axis=1)
    doc_totals = lax.psum(local_counts, "fsdp")
    doc_begin = (jnp.cumsum(doc_totals, axis=1) - doc_totals).astype(jnp.int32)
    gate_expert = w_gate[0]
    up_expert = w_up[0]
    down_expert = w_down[0]
    router_wide = router.astype(jnp.float32)
    query_acc = jnp.zeros((model_width, query_local * head_width), jnp.float32)
    key_acc = jnp.zeros((model_width, kv_local * head_width), jnp.float32)
    value_acc = jnp.zeros((model_width, kv_local * head_width), jnp.float32)
    out_acc = jnp.zeros((model_width, query_local * head_width), jnp.float32)
    gate_acc = jnp.zeros(gate_expert.shape, jnp.float32)
    up_acc = jnp.zeros(up_expert.shape, jnp.float32)
    down_acc = jnp.zeros(down_expert.shape, jnp.float32)
    router_acc = jnp.zeros(router.shape, jnp.float32)
    gain_attn_acc = jnp.zeros(gain_attn.shape, jnp.float32)
    gain_moe_acc = jnp.zeros(gain_moe.shape, jnp.float32)
    gain_query_acc = jnp.zeros(gain_query.shape, jnp.float32)
    gain_key_acc = jnp.zeros(key_norm_gain.shape, jnp.float32)
    out_parts = []
    grad_parts = []
    for micro_index in range(micro_count):
        row_begin = micro_index * micro_rows
        token_block = full_tokens[row_begin : row_begin + micro_rows].astype(jnp.float32)
        ids_now = doc_ids[micro_index]
        query_index = shard_index * micro_rows + jnp.arange(micro_rows)
        query_start = jnp.sum(
            jnp.where(ids_now[:, None] == doc_range, doc_begin[micro_index][None, :], 0), axis=1
        )
        cosine_lookup, sine_lookup = rope_tables(query_index - query_start, head_width)
        gathered = gather_weights(w_query, key_weight, value_weight, w_out)
        normed, norm_pull = jax.vjp(root_mean_norm, token_block, gain_attn)
        normed_reduced = normed.astype(jnp.bfloat16)
        query_pre = jnp.dot(normed_reduced, gathered[0], preferred_element_type=jnp.float32)
        key_before_norm = jnp.dot(normed_reduced, gathered[1], preferred_element_type=jnp.float32)
        value_reduced = jnp.dot(
            normed_reduced, gathered[2], preferred_element_type=jnp.float32
        ).astype(jnp.bfloat16)

        def shape_heads(query_raw, key_raw, query_gain, key_gain):
            query_heads = rotary_apply(
                root_mean_norm(query_raw.reshape(micro_rows, query_local, head_width), query_gain),
                cosine_lookup[:, None, :],
                sine_lookup[:, None, :],
            )
            key_heads = rotary_apply(
                root_mean_norm(key_raw.reshape(micro_rows, kv_local, head_width), key_gain),
                cosine_lookup[:, None, :],
                sine_lookup[:, None, :],
            )
            return (query_heads, key_heads)

        (query_heads, key_heads), heads_pull = jax.vjp(
            shape_heads, query_pre, key_before_norm, gain_query, key_norm_gain
        )
        queries = to_heads(query_heads.astype(jnp.bfloat16), kv_local, group_width)
        keys_low = key_heads.reshape(micro_rows, kv_local * head_width).astype(jnp.bfloat16)
        keys_all, values_all = gather_keys(keys_low, value_reduced)
        row_index = jnp.tile(query_index, group_width)
        row_start = jnp.tile(query_start, group_width)
        head_out, log_total = attend_forward(
            queries, keys_all, values_all, row_index, row_start, block_keys
        )
        heads_low = to_tokens(head_out, group_width).astype(jnp.bfloat16)
        attn_part = dot_last(heads_low, gathered[3])
        middle = token_block + lax.psum(attn_part.astype(jnp.bfloat16), "tp").astype(jnp.float32)
        moe_normed, moe_pull = jax.vjp(root_mean_norm, middle, gain_moe)
        moe_low = moe_normed.astype(jnp.bfloat16)
        logits = jnp.dot(moe_low, router, preferred_element_type=jnp.float32)
        routes_now = routes[row_begin : row_begin + micro_rows]
        route_match = routes_now[:, :, None] == expert_range
        chosen = jnp.sum(jnp.where(route_match, logits[:, None, :], 0.0), axis=-1)
        gate_weights, softmax_pull = jax.vjp(jax.nn.softmax, chosen)
        mine = routes_now % group_count == group_index
        pair_target = jnp.where(mine, routes_now // group_count, shard_count).reshape(pair_total)
        target_hot = (pair_target[:, None] == jnp.arange(shard_count)).astype(jnp.int32)
        pair_rank = jnp.sum((jnp.cumsum(target_hot, axis=0) - target_hot) * target_hot, axis=1)
        pair_slot = jnp.where(
            pair_target < shard_count, pair_target * capacity + pair_rank, slot_total
        )
        slot_pair = (
            jnp.full((slot_total + 1,), pair_total, jnp.int32)
            .at[pair_slot]
            .set(jnp.arange(pair_total, dtype=jnp.int32))[:slot_total]
        )
        slot_token = slot_pair // TOPK
        slot_grid = pair_slot.reshape(micro_rows, TOPK)
        padded_low = jnp.concatenate([moe_low, jnp.zeros((1, model_width), jnp.bfloat16)], axis=0)
        received = send_rows(
            padded_low[slot_token].reshape(shard_count, capacity, model_width)
        ).reshape(slot_total, model_width)
        gate_pre = jnp.dot(received, gate_expert, preferred_element_type=jnp.float32)
        up_pre = jnp.dot(received, up_expert, preferred_element_type=jnp.float32)
        hidden, swiglu_pull = jax.vjp(swiglu, gate_pre, up_pre)
        hidden_low = hidden.astype(jnp.bfloat16)
        expert_out = jnp.dot(hidden_low, down_expert, preferred_element_type=jnp.float32).astype(
            jnp.bfloat16
        )
        returned = return_rows(expert_out.reshape(shard_count, capacity, model_width)).reshape(
            slot_total, model_width
        )
        padded_out = jnp.concatenate([returned, jnp.zeros((1, model_width), jnp.bfloat16)], axis=0)
        moe_part = jnp.zeros((micro_rows, model_width), jnp.float32)
        for pick_index in range(TOPK):
            moe_part = moe_part + gate_weights[:, pick_index : pick_index + 1] * padded_out[
                slot_grid[:, pick_index]
            ].astype(jnp.float32)
        moe_share = lax.psum_scatter(
            moe_part.astype(jnp.bfloat16), "tp", scatter_dimension=1, tiled=True
        ).astype(jnp.float32)
        middle_slice = lax.dynamic_slice_in_dim(middle, group_index * slice_width, slice_width, 1)
        out_parts.append((middle_slice + moe_share).astype(jnp.bfloat16))
        grad_block = full_grads[row_begin : row_begin + micro_rows].astype(jnp.float32)
        gate_columns = []
        for pick_index in range(TOPK):
            gate_columns.append(
                jnp.sum(
                    grad_block * padded_out[slot_grid[:, pick_index]].astype(jnp.float32), axis=1
                )
            )
        gates_grad = jnp.stack(gate_columns, axis=1)
        flat_gates = jnp.concatenate(
            [gate_weights.reshape(pair_total), jnp.zeros((1,), jnp.float32)]
        )
        padded_grad = jnp.concatenate(
            [grad_block, jnp.zeros((1, model_width), jnp.float32)], axis=0
        )
        send_grad = (padded_grad[slot_token] * flat_gates[slot_pair][:, None]).astype(jnp.bfloat16)
        received_grad = send_rows(send_grad.reshape(shard_count, capacity, model_width)).reshape(
            slot_total, model_width
        )
        hidden_grad = dot_last(received_grad, down_expert)
        down_acc = down_acc + dot_first(hidden_low, received_grad)
        gate_pre_grad, up_pre_grad = swiglu_pull(hidden_grad)
        gate_pre_low = gate_pre_grad.astype(jnp.bfloat16)
        up_pre_low = up_pre_grad.astype(jnp.bfloat16)
        gate_acc = gate_acc + dot_first(received, gate_pre_low)
        up_acc = up_acc + dot_first(received, up_pre_low)
        rows_back = (dot_last(gate_pre_low, gate_expert) + dot_last(up_pre_low, up_expert)).astype(
            jnp.bfloat16
        )
        back_rows = return_rows(rows_back.reshape(shard_count, capacity, model_width)).reshape(
            slot_total, model_width
        )
        padded_back = jnp.concatenate(
            [back_rows, jnp.zeros((1, model_width), jnp.bfloat16)], axis=0
        )
        moe_grad = jnp.zeros((micro_rows, model_width), jnp.float32)
        for pick_index in range(TOPK):
            moe_grad = moe_grad + padded_back[slot_grid[:, pick_index]].astype(jnp.float32)
        (chosen_grad,) = softmax_pull(gates_grad)
        logit_grad = jnp.sum(jnp.where(route_match, chosen_grad[:, :, None], 0.0), axis=1)
        router_acc = router_acc + lax.dot_general(
            moe_low.astype(jnp.float32),
            logit_grad,
            (((0,), (0,)), ((), ())),
            precision=highest_precision,
        )
        moe_grad = moe_grad + lax.dot_general(
            logit_grad, router_wide, (((1,), (1,)), ((), ())), precision=highest_precision
        )
        middle_part, gain_moe_part = moe_pull(moe_grad)
        gain_moe_acc = gain_moe_acc + gain_moe_part
        middle_grad = grad_block + lax.psum(middle_part.astype(jnp.bfloat16), "tp").astype(
            jnp.float32
        )
        middle_low = middle_grad.astype(jnp.bfloat16)
        gathered_back = gather_weights(w_query, key_weight, value_weight, w_out)
        out_acc = out_acc + dot_first(middle_low, heads_low)
        heads_grad = jnp.dot(middle_low, gathered_back[3], preferred_element_type=jnp.float32)
        grad_low = to_heads(
            heads_grad.reshape(micro_rows, query_local, head_width).astype(jnp.bfloat16),
            kv_local,
            group_width,
        )
        query_side, key_side_all, value_side_all = attend_backward(
            queries,
            keys_all,
            values_all,
            row_index,
            row_start,
            block_keys,
            head_out,
            log_total,
            grad_low,
        )
        key_side, value_side = (
            lax.psum_scatter(
                key_side_all.astype(jnp.bfloat16), "fsdp", scatter_dimension=0, tiled=True
            ).astype(jnp.float32),
            lax.psum_scatter(
                value_side_all.astype(jnp.bfloat16), "fsdp", scatter_dimension=0, tiled=True
            ).astype(jnp.float32),
        )
        query_pre_grad, key_pre_grad, gain_query_part, gain_key_part = heads_pull(
            (
                to_tokens(query_side, group_width).reshape(micro_rows, query_local, head_width),
                key_side.reshape(micro_rows, kv_local, head_width),
            )
        )
        gain_query_acc = gain_query_acc + gain_query_part
        gain_key_acc = gain_key_acc + gain_key_part
        query_pre_low = query_pre_grad.astype(jnp.bfloat16)
        key_pre_low = key_pre_grad.astype(jnp.bfloat16)
        value_pre_low = value_side.astype(jnp.bfloat16)
        query_acc = query_acc + dot_first(normed_reduced, query_pre_low)
        key_acc = key_acc + dot_first(normed_reduced, key_pre_low)
        value_acc = value_acc + dot_first(normed_reduced, value_pre_low)
        normed_grad = (
            dot_last(query_pre_low, gathered_back[0])
            + dot_last(key_pre_low, gathered_back[1])
            + dot_last(value_pre_low, gathered_back[2])
        )
        token_part, gain_attn_part = norm_pull(normed_grad)
        gain_attn_acc = gain_attn_acc + gain_attn_part
        token_share = lax.psum_scatter(
            token_part.astype(jnp.bfloat16), "tp", scatter_dimension=1, tiled=True
        ).astype(jnp.float32)
        grad_slice = lax.dynamic_slice_in_dim(
            middle_grad, group_index * slice_width, slice_width, 1
        )
        grad_parts.append((grad_slice + token_share).astype(jnp.bfloat16))
    weight_sums = (
        lax.psum_scatter(
            query_acc.astype(jnp.bfloat16), "fsdp", scatter_dimension=0, tiled=True
        ).astype(jnp.float32),
        lax.psum_scatter(
            key_acc.astype(jnp.bfloat16), "fsdp", scatter_dimension=0, tiled=True
        ).astype(jnp.float32),
        lax.psum_scatter(
            value_acc.astype(jnp.bfloat16), "fsdp", scatter_dimension=0, tiled=True
        ).astype(jnp.float32),
        lax.psum_scatter(
            out_acc.astype(jnp.bfloat16), "fsdp", scatter_dimension=0, tiled=True
        ).astype(jnp.float32),
    )
    small_sums = lax.psum(
        (gain_attn_acc, gain_query_acc, gain_key_acc, gain_moe_acc, router_acc), ("fsdp", "tp")
    )
    return (
        jnp.concatenate(out_parts, axis=0),
        jnp.concatenate(grad_parts, axis=0),
        small_sums[0],
        weight_sums[0],
        weight_sums[1],
        weight_sums[2],
        weight_sums[3],
        small_sums[1],
        small_sums[2],
        small_sums[3],
        small_sums[4],
        gate_acc[None],
        up_acc[None],
        down_acc[None],
    )


MESH = pl.DeviceIdType.MESH


def place():
    f = lax.axis_index("fsdp")
    t = lax.axis_index("tp")
    return f // 2, f % 2, t // 2, t % 2


def device(z, x, y, c):
    return (z * 2 + x, y * 2 + c)


def greet(devices):
    barrier = pltpu.get_barrier_semaphore()
    total = 0
    for valid, where in devices:
        if valid is None:
            pl.semaphore_signal(barrier, inc=1, device_id=where, device_id_type=MESH)
            total = total + 1
        else:
            @pl.when(valid)
            def _():
                pl.semaphore_signal(barrier, inc=1, device_id=where, device_id_type=MESH)
            total = total + valid.astype(jnp.int32)
    pl.semaphore_wait(barrier, total)


def remote(src, dst, send, recv, where):
    return pltpu.make_async_remote_copy(
        src_ref=src, dst_ref=dst, send_sem=send, recv_sem=recv, device_id=where, device_id_type=MESH
    )


def gather_all_kernel(nz, x_ref, o_ref, lsem, s_p, s_u, s_d, s_x, s_y, s_dx, s_dy,
                      r_z, r_x, r_y, r_dx, r_dy, r_p):
    z, x, y, c = place()
    rows, cols = x_ref.shape
    half = rows // 2
    partner = device(z, x, y, 1 - c)
    xn = device(z, 1 - x, y, c)
    yn = device(z, x, 1 - y, c)
    up = device(z + 1, x, y, c)
    down = device(z - 1, x, y, c)
    greet([(None, partner), (None, xn), (None, yn), (z < nz - 1, up), (z > 0, down)])

    def block(zz, xx, yy, cc, part=None):
        start = (zz * 2 + xx) * rows
        size = rows
        if part is not None:
            start = start + part * half
            size = half
        return o_ref.at[pl.ds(pl.multiple_of(start, half), size),
                        pl.ds(pl.multiple_of((yy * 2 + cc) * cols, cols), cols)]

    own = pltpu.make_async_copy(x_ref, block(z, x, y, c), lsem)
    own.start()

    items = [(0, 0)]
    for dist in range(1, nz):
        items += [(dist, -1), (dist, 1)]

    def guard(item, fn):
        dist, side = item
        zz = z + side * dist
        if dist == 0:
            fn(zz)
        else:
            pl.when((zz >= 0) & (zz < nz))(lambda: fn(zz))

    def c_z(zz, src):
        dst = block(zz, x, y, c)
        return (remote(src, dst, s_u.at[zz], r_z.at[zz], up),
                remote(src, dst, s_d.at[zz], r_z.at[zz], down))

    def c_xy(zz, src):
        dst = block(zz, x, y, c)
        return (remote(src, dst, s_x.at[zz], r_x.at[zz], xn),
                remote(src, dst, s_y.at[zz], r_y.at[zz], yn))

    def c_p(zz, rel, src=None):
        xx = 1 - x if rel in (1, 3, 4) else x
        yy = 1 - y if rel in (2, 3, 4) else y
        part = {3: 0, 4: 1}.get(rel)
        dst = block(zz, xx, yy, c, part)
        k = zz * 5 + rel
        return remote(dst if src is None else src, dst, s_p.at[k], r_p.at[k], partner)

    def w_p(zz, rel):
        xx = 1 - x if rel in (1, 3, 4) else x
        yy = 1 - y if rel in (2, 3, 4) else y
        part = {3: 0, 4: 1}.get(rel)
        dst = block(zz, xx, yy, 1 - c, part)
        k = zz * 5 + rel
        return remote(dst, dst, s_p.at[k], r_p.at[k], partner)

    def c_diag(zz):
        a = block(zz, 1 - x, y, c, 0)
        b = block(zz, x, 1 - y, c, 1)
        return (remote(a, a, s_dy.at[zz], r_dy.at[zz], yn),
                remote(b, b, s_dx.at[zz], r_dx.at[zz], xn))

    def stage_a(item):
        dist, side = item

        def run(zz):
            src = x_ref if dist == 0 else block(zz, x, y, c)
            cu, cd = c_z(zz, src)
            if dist:
                cu.wait_recv()
            if side <= 0:
                pl.when(z < nz - 1)(cu.start)
            if dist == 0 or side > 0:
                pl.when(z > 0)(cd.start)
            for cc in c_xy(zz, src):
                cc.start()
            c_p(zz, 0, src).start()

        guard(item, run)

    def stage_b(item):
        def run(zz):
            cx, cy = c_xy(zz, block(zz, x, y, c))
            dy, dx = c_diag(zz)
            cx.wait_recv()
            dy.start()
            c_p(zz, 1).start()
            cy.wait_recv()
            dx.start()
            c_p(zz, 2).start()

        guard(item, run)

    def stage_c(item):
        def run(zz):
            dy, dx = c_diag(zz)
            dy.wait_recv()
            c_p(zz, 3).start()
            dx.wait_recv()
            c_p(zz, 4).start()

        guard(item, run)

    count = len(items)
    for k in range(count + 2):
        if k < count:
            stage_a(items[k])
        if 0 <= k - 1 < count:
            stage_b(items[k - 1])
        if 0 <= k - 2 < count:
            stage_c(items[k - 2])

    def finish(zz, carry):
        for rel in range(5):
            w_p(zz, rel).wait_recv()
            c_p(zz, rel).wait_send()
        cu, cd = c_z(zz, block(zz, x, y, c))
        pl.when((zz <= z) & (z < nz - 1))(cu.wait_send)
        pl.when((zz >= z) & (z > 0))(cd.wait_send)
        for cc in c_xy(zz, block(zz, x, y, c)) + c_diag(zz):
            cc.wait_send()
        return carry

    lax.fori_loop(0, nz, finish, 0)
    own.wait()


def gather_all(block, nz, collective_id):
    rows, cols = block.shape
    dma = pltpu.SemaphoreType.DMA
    return pl.pallas_call(
        functools.partial(gather_all_kernel, nz),
        out_shape=jax.ShapeDtypeStruct((rows * nz * 2, cols * 4), block.dtype),
        in_specs=[pl.BlockSpec(memory_space=pl.ANY)],
        out_specs=pl.BlockSpec(memory_space=pl.ANY),
        scratch_shapes=[dma] + [dma((5 * nz,))] + [dma((nz,))] * 6 + [dma((nz,))] * 5 + [dma((5 * nz,))],
        compiler_params=pltpu.CompilerParams(collective_id=collective_id, has_side_effects=True),
        name="gather_all",
    )(block)


def scatter_all_kernel(nz, p_ref, o_ref, w, lp, rx, rxd, ry, ryd, rz,
                       s_l, s_p, r_p, s_x, s_y, s_dx, s_dy, s_z, r_x, r_y, r_dx, r_dy, r_z):
    z, x, y, c = place()
    rows, cols = o_ref.shape
    half = rows // 2
    partner = device(z, x, y, 1 - c)
    xn = device(z, 1 - x, y, c)
    yn = device(z, x, 1 - y, c)
    up = device(z + 1, x, y, c)
    down = device(z - 1, x, y, c)
    greet([(None, partner), (None, xn), (None, yn), (z < nz - 1, up), (z > 0, down)])
    chunk = 64

    def block(zz, rel, cc):
        xx = 1 - x if rel in (1, 3) else x
        yy = 1 - y if rel in (2, 3) else y
        return p_ref.at[pl.ds(pl.multiple_of((zz * 2 + xx) * rows, rows), rows),
                        pl.ds(pl.multiple_of((yy * 2 + cc) * cols, cols), cols)]

    items = []
    for dist in range(nz - 1, 0, -1):
        items += [(dist, -1), (dist, 1)]
    items += [(0, 0)]

    def guard(item, fn):
        dist, side = item
        zz = z + side * dist
        if dist == 0:
            fn(zz)
        else:
            pl.when((zz >= 0) & (zz < nz))(lambda: fn(zz))

    def c_p(zz, rel):
        k = zz * 4 + rel
        return remote(block(zz, rel, 1 - c), lp.at[zz, rel], s_p.at[k], r_p.at[k], partner)

    def c_l(zz, rel):
        return pltpu.make_async_copy(block(zz, rel, c), w.at[zz, rel], s_l.at[zz * 4 + rel])

    def c_diag(zz):
        return (remote(w.at[zz, 3, pl.ds(0, half)], rxd.at[zz], s_dx.at[zz], r_dx.at[zz], xn),
                remote(w.at[zz, 3, pl.ds(half, half)], ryd.at[zz], s_dy.at[zz], r_dy.at[zz], yn))

    def c_xy(zz):
        return (remote(w.at[zz, 1], rx.at[zz], s_x.at[zz], r_x.at[zz], xn),
                remote(w.at[zz, 2], ry.at[zz], s_y.at[zz], r_y.at[zz], yn))

    def c_z(zz, slot, where):
        return remote(w.at[zz, 0], rz.at[slot], s_z.at[zz], r_z.at[slot], where)

    def add(dst, srcs, start, count):
        def step(i, carry):
            off = pl.multiple_of(i * chunk, chunk)
            here = pl.ds(pl.multiple_of(start + off, chunk), chunk)
            total = dst[here, :].astype(jnp.float32)
            for src in srcs:
                total = total + src[pl.ds(off, chunk), :].astype(jnp.float32)
            dst[here, :] = total.astype(dst.dtype)
            return carry
        lax.fori_loop(0, count // chunk, step, 0)

    def stage_0(item):
        def run(zz):
            for rel in (3, 1, 2, 0):
                c_p(zz, rel).start()
                c_l(zz, rel).start()
        guard(item, run)

    def stage_d(item):
        def run(zz):
            for rel in (3, 1, 2, 0):
                c_p(zz, rel).wait_recv()
                c_l(zz, rel).wait()
                add(w.at[zz, rel], [lp.at[zz, rel]], 0, rows)
                if rel == 3:
                    for cc in c_diag(zz):
                        cc.start()
        guard(item, run)

    def stage_e(item):
        def run(zz):
            dx, dy = c_diag(zz)
            cx, cy = c_xy(zz)
            dy.wait_recv()
            add(w.at[zz, 1], [ryd.at[zz]], half, half)
            cx.start()
            dx.wait_recv()
            add(w.at[zz, 2], [rxd.at[zz]], 0, half)
            cy.start()
        guard(item, run)

    def stage_f(item):
        dist, side = item

        def run(zz):
            cx, cy = c_xy(zz)
            cx.wait_recv()
            cy.wait_recv()
            if dist:
                add(w.at[zz, 0], [rx.at[zz], ry.at[zz]], 0, rows)
                has = z > 0 if side > 0 else z < nz - 1
                cz = c_z(zz, zz, up if side > 0 else down)

                @pl.when(has)
                def _():
                    cz.wait_recv()
                    add(w.at[zz, 0], [rz.at[zz]], 0, rows)
                if side > 0:
                    cz.start()
                else:
                    if dist == 1:
                        c_z(zz, nz, down).start()
                    else:
                        cz.start()
            else:
                below, above = c_z(zz, zz, up), c_z(zz, nz, down)

                def total(refs):
                    def step(i, carry):
                        here = pl.ds(pl.multiple_of(i * chunk, chunk), chunk)
                        acc = w[zz, 0, here, :].astype(jnp.float32)
                        for ref in refs:
                            acc = acc + ref[here, :].astype(jnp.float32)
                        o_ref[here, :] = acc
                        return carry
                    lax.fori_loop(0, rows // chunk, step, 0)

                pl.when(z > 0)(below.wait_recv)
                pl.when(z < nz - 1)(above.wait_recv)
                pl.when(z == 0)(lambda: total([rx.at[zz], ry.at[zz], rz.at[nz]]))
                pl.when(z == nz - 1)(lambda: total([rx.at[zz], ry.at[zz], rz.at[zz]]))
                pl.when((z > 0) & (z < nz - 1))(
                    lambda: total([rx.at[zz], ry.at[zz], rz.at[zz], rz.at[nz]]))
        guard(item, run)

    for item in items:
        stage_0(item)
    count = len(items)
    for k in range(count + 2):
        if k < count:
            stage_d(items[k])
        if 0 <= k - 1 < count:
            stage_e(items[k - 1])
        if 0 <= k - 2 < count:
            stage_f(items[k - 2])

    def finish(zz, carry):
        for rel in range(4):
            c_p(zz, rel).wait_send()
        for cc in c_diag(zz) + c_xy(zz):
            cc.wait_send()
        pl.when(zz != z)(c_z(zz, zz, up).wait_send)
        return carry

    lax.fori_loop(0, nz, finish, 0)


def scatter_all(partial, nz, collective_id):
    rows, cols = partial.shape[0] // (2 * nz), partial.shape[1] // 4
    half = rows // 2
    dma = pltpu.SemaphoreType.DMA
    kind = partial.dtype
    vm = pltpu.VMEM
    return pl.pallas_call(
        functools.partial(scatter_all_kernel, nz),
        out_shape=jax.ShapeDtypeStruct((rows, cols), jnp.float32),
        in_specs=[pl.BlockSpec(memory_space=pl.ANY)],
        out_specs=pl.BlockSpec(memory_space=pltpu.VMEM),
        scratch_shapes=[vm((nz, 4, rows, cols), kind), vm((nz, 4, rows, cols), kind),
                        vm((nz, rows, cols), kind), vm((nz, half, cols), kind),
                        vm((nz, rows, cols), kind), vm((nz, half, cols), kind),
                        vm((nz + 1, rows, cols), kind)]
        + [dma((4 * nz,))] * 3 + [dma((nz,))] * 5 + [dma((nz,))] * 4 + [dma((nz + 1,))],
        compiler_params=pltpu.CompilerParams(collective_id=collective_id, has_side_effects=True,
                                             vmem_limit_bytes=62 << 20),
        name="scatter_all",
    )(partial)


def z_items(nz, near_first):
    items = [(0, 0)] if near_first else []
    order = range(1, nz) if near_first else range(nz - 1, 0, -1)
    for dist in order:
        items += [(dist, -1), (dist, 1)]
    return items if near_first else items + [(0, 0)]


def z_guard(item, z, nz, fn):
    dist, side = item
    zz = z + side * dist
    if dist == 0:
        fn(zz)
    else:
        pl.when((zz >= 0) & (zz < nz))(lambda: fn(zz))


def gather_rows_kernel(nz, count, columns, narrow, *refs):
    total = count + columns
    srcs, refs = refs[:total], refs[total:]
    outs, refs = refs[:total], refs[total:]
    wide, refs = refs[: min(columns, 1)], refs[min(columns, 1) :]
    lsem, s_u, s_d, s_x, r_z, r_x, s_c, r_c, s_w, r_w = refs
    z, x, y, c = place()
    xn, up, down = device(z, 1 - x, y, c), device(z + 1, x, y, c), device(z - 1, x, y, c)
    partner, yn = device(z, x, y, 1 - c), device(z, x, 1 - y, c)
    wanted = [(None, xn), (z < nz - 1, up), (z > 0, down)]
    greet(wanted + [(None, partner), (None, yn), (None, device(nz - 1 - z, x, y, c))] * min(columns, 1))

    def block(n, zz, xx):
        rows = srcs[n].shape[0]
        return outs[n].at[pl.ds(pl.multiple_of((zz * 2 + xx) * rows, rows), rows)]

    own = [(srcs[n], block(n, z, x)) for n in range(count)]
    column_copies, swaps = [], []
    if columns:
        mirror = device(nz - 1 - z, x, y, c)
        first, out = outs[count], wide[0]
        rows, cols = first.shape
        top, bottom = pl.ds(0, rows // 2), pl.ds(rows // 2, rows // 2)
        for n in range(columns):
            src, dst = srcs[count + n], outs[count + n]
            swaps.append(remote(src.at[bottom], dst.at[bottom], s_w.at[n], r_w.at[n], mirror))
            dst[top, :] = src[top, :]

        def column(yy):
            return out.at[:, pl.ds(pl.multiple_of((yy * 2 + c) * cols, cols), cols)]

        column_copies = [
            remote(first, column(y), s_c.at[0], r_c.at[0], yn),
            remote(first, column(y), s_c.at[1], r_c.at[1], partner),
            remote(column(1 - y), column(1 - y), s_c.at[2], r_c.at[2], partner),
        ]
        last = pltpu.make_async_copy(first, column(y), lsem.at[total])
    own = [pltpu.make_async_copy(src, dst, lsem.at[n]) for n, (src, dst) in enumerate(own)]
    pairs = range(count - narrow, count)
    sides = [remote(srcs[n], block(n, z, x), s_x.at[n * nz], r_x.at[n * nz], xn) for n in pairs]
    for copy in swaps + own + sides:
        copy.start()

    def copies(n, zz, src):
        dst = block(n, zz, x)
        k = n * nz + zz
        if n in pairs:
            rows = 2 * srcs[n].shape[0]
            dst = src = outs[n].at[pl.ds(pl.multiple_of(zz * rows, rows), rows)]
        return (remote(src, dst, s_u.at[k], r_z.at[k], up),
                remote(src, dst, s_d.at[k], r_z.at[k], down),
                remote(src, dst, s_x.at[k], r_x.at[k], xn))

    items = z_items(nz, True)
    for item in items:
        dist, side = item

        def run(zz):
            for n in range(count):
                src = srcs[n] if dist == 0 else block(n, zz, x)
                cu, cd, cx = copies(n, zz, src)
                if dist:
                    cu.wait_recv()
                elif n in pairs:
                    own[n].wait()
                    sides[n - count + narrow].wait_recv()
                if side <= 0:
                    pl.when(z < nz - 1)(cu.start)
                if side > 0 or dist == 0:
                    pl.when(z > 0)(cd.start)
                if n not in pairs:
                    cx.start()

        z_guard(item, z, nz, run)
        if columns and item == items[-3]:
            swaps[0].wait_recv()
            column_copies[0].start()
            column_copies[1].start()
            last.start()
        if columns and item == items[-1]:
            column_copies[0].wait_recv()
            column_copies[2].start()

    def finish(zz, carry):
        for n in range(count):
            cu, cd, cx = copies(n, zz, block(n, zz, x))
            if n not in pairs:
                cx.wait_recv()
                cx.wait_send()
            pl.when((zz <= z) & (z < nz - 1))(cu.wait_send)
            pl.when((zz >= z) & (z > 0))(cd.wait_send)
        return carry

    lax.fori_loop(0, nz, finish, 0)
    for copy in own[: count - narrow]:
        copy.wait()
    for copy in sides:
        copy.wait_send()
    if columns:
        column_copies[0].wait_send()
        column_copies[1].wait()
        column_copies[2].wait()
        last.wait()
        swaps[0].wait_send()
        for copy in swaps[1:]:
            copy.wait()


def gather_rows(blocks, nz, collective_id, swapped=(), narrow=0):
    count, columns = len(blocks), len(swapped)
    dma = pltpu.SemaphoreType.DMA
    any_space = pl.BlockSpec(memory_space=pl.ANY)
    vmem = pl.BlockSpec(memory_space=pltpu.VMEM)
    shapes = [
        jax.ShapeDtypeStruct((b.shape[0] * nz * 2,) + b.shape[1:], b.dtype) for b in blocks
    ] + [jax.ShapeDtypeStruct(b.shape, b.dtype) for b in swapped]
    if columns:
        rows, cols = swapped[0].shape
        shapes.append(jax.ShapeDtypeStruct((rows, cols * 4), swapped[0].dtype))
    total = count + columns
    return pl.pallas_call(
        functools.partial(gather_rows_kernel, nz, count, columns, narrow),
        out_shape=shapes,
        in_specs=[vmem] * total,
        out_specs=[any_space] * count + [vmem] * columns + [any_space] * min(columns, 1),
        scratch_shapes=[dma((total + 1,))] + [dma((count * nz,))] * 5 + [dma((3,))] * 2
        + [dma((max(columns, 1),))] * 2,
        compiler_params=pltpu.CompilerParams(collective_id=collective_id, has_side_effects=True,
                                             vmem_limit_bytes=62 << 20),
        name="gather_rows",
    )(*blocks, *swapped)


def swap_back_kernel(nz, *refs):
    count = (len(refs) - 2) // 2
    srcs, outs = refs[:count], refs[count : 2 * count]
    s, r = refs[2 * count :]
    z, x, y, c = place()
    mirror = device(nz - 1 - z, x, y, c)
    greet([(None, mirror)])
    copies = [remote(src, out, s.at[n], r.at[n], mirror)
              for n, (src, out) in enumerate(zip(srcs, outs))]
    for copy in copies:
        copy.start()
    for copy in copies:
        copy.wait()


def swap_back(blocks, nz, collective_id):
    count = len(blocks)
    dma = pltpu.SemaphoreType.DMA
    any_space = pl.BlockSpec(memory_space=pl.ANY)
    return pl.pallas_call(
        functools.partial(swap_back_kernel, nz),
        out_shape=[jax.ShapeDtypeStruct(b.shape, b.dtype) for b in blocks],
        in_specs=[any_space] * count,
        out_specs=[any_space] * count,
        scratch_shapes=[dma((count,))] * 2,
        compiler_params=pltpu.CompilerParams(collective_id=collective_id, has_side_effects=True),
        name="swap_back",
    )(*blocks)


def add_blocks(dst, srcs, start, count, out=None, chunk=64):
    target = dst if out is None else out

    def step(i, carry):
        off = pl.multiple_of(i * chunk, chunk)
        here = pl.ds(pl.multiple_of(start + off, chunk), chunk)
        total = dst[here, :].astype(jnp.float32)
        for src in srcs:
            total = total + src[pl.ds(off, chunk), :].astype(jnp.float32)
        target[here, :] = total.astype(target.dtype)
        return carry

    lax.fori_loop(0, count // chunk, step, 0)


def reduce_rows_kernel(nz, p_ref, o_ref, w, rx, rz, s_l, s_x, s_z, r_x, r_z):
    z, x, y, c = place()
    rows = o_ref.shape[0]
    xn, up, down = device(z, 1 - x, y, c), device(z + 1, x, y, c), device(z - 1, x, y, c)
    greet([(None, xn), (z < nz - 1, up), (z > 0, down)])

    def block(zz, xx):
        return p_ref.at[pl.ds(pl.multiple_of((zz * 2 + xx) * rows, rows), rows)]

    def c_x(zz):
        return remote(block(zz, 1 - x), rx.at[zz], s_x.at[zz], r_x.at[zz], xn)

    def c_l(zz):
        return pltpu.make_async_copy(block(zz, x), w.at[zz], s_l.at[zz])

    def c_z(zz, slot, where):
        return remote(w.at[zz], rz.at[slot], s_z.at[zz], r_z.at[slot], where)

    items = z_items(nz, False)

    def start(zz):
        c_x(zz).start()
        c_l(zz).start()

    for item in items:
        z_guard(item, z, nz, start)
    for item in items:
        dist, side = item

        def run(zz):
            c_l(zz).wait()
            c_x(zz).wait_recv()
            if dist:
                add_blocks(w.at[zz], [rx.at[zz]], 0, rows)
                cz = c_z(zz, zz, up if side > 0 else down)

                @pl.when(z > 0 if side > 0 else z < nz - 1)
                def _():
                    cz.wait_recv()
                    add_blocks(w.at[zz], [rz.at[zz]], 0, rows)

                (c_z(zz, nz, down) if side < 0 and dist == 1 else cz).start()
            else:
                pl.when(z > 0)(c_z(zz, zz, up).wait_recv)
                pl.when(z < nz - 1)(c_z(zz, nz, down).wait_recv)
                low, high = rz.at[zz], rz.at[nz]
                pl.when(z == 0)(lambda: add_blocks(w.at[zz], [rx.at[zz], high], 0, rows, o_ref))
                pl.when(z == nz - 1)(lambda: add_blocks(w.at[zz], [rx.at[zz], low], 0, rows, o_ref))
                pl.when((z > 0) & (z < nz - 1))(
                    lambda: add_blocks(w.at[zz], [rx.at[zz], low, high], 0, rows, o_ref)
                )

        z_guard(item, z, nz, run)

    def finish(zz, carry):
        c_x(zz).wait_send()
        pl.when(zz != z)(c_z(zz, zz, up).wait_send)
        return carry

    lax.fori_loop(0, nz, finish, 0)


def reduce_rows(partial, nz, collective_id):
    rows, cols = partial.shape[0] // (2 * nz), partial.shape[1]
    dma, vm, kind = pltpu.SemaphoreType.DMA, pltpu.VMEM, partial.dtype
    return pl.pallas_call(
        functools.partial(reduce_rows_kernel, nz),
        out_shape=jax.ShapeDtypeStruct((rows, cols), jnp.float32),
        in_specs=[pl.BlockSpec(memory_space=pl.ANY)],
        out_specs=pl.BlockSpec(memory_space=pltpu.VMEM),
        scratch_shapes=[vm((nz, rows, cols), kind), vm((nz, rows, cols), kind),
                        vm((nz + 1, rows, cols), kind)]
        + [dma((nz,))] * 4 + [dma((nz + 1,))],
        compiler_params=pltpu.CompilerParams(
            collective_id=collective_id, has_side_effects=True, vmem_limit_bytes=62 << 20
        ),
        name="reduce_rows",
    )(partial)


def gather_cols_kernel(x_ref, o_ref, lsem, s_p, s_y, r_p, r_y):
    z, x, y, c = place()
    cols = x_ref.shape[1]
    partner, yn = device(z, x, y, 1 - c), device(z, x, 1 - y, c)
    greet([(None, partner), (None, yn)])

    def block(yy, cc):
        return o_ref.at[:, pl.ds(pl.multiple_of((yy * 2 + cc) * cols, cols), cols)]

    own = pltpu.make_async_copy(x_ref, block(y, c), lsem)
    cy = remote(x_ref, block(y, c), s_y, r_y, yn)
    cp = remote(x_ref, block(y, c), s_p.at[0], r_p.at[0], partner)
    cf = remote(block(1 - y, c), block(1 - y, c), s_p.at[1], r_p.at[1], partner)
    cy.start()
    cp.start()
    own.start()
    cy.wait_recv()
    cf.start()
    cp.wait()
    cf.wait()
    cy.wait_send()
    own.wait()


def gather_cols(block, collective_id):
    dma = pltpu.SemaphoreType.DMA
    any_space = pl.BlockSpec(memory_space=pl.ANY)
    return pl.pallas_call(
        gather_cols_kernel,
        out_shape=jax.ShapeDtypeStruct((block.shape[0], block.shape[1] * 4), block.dtype),
        in_specs=[any_space],
        out_specs=any_space,
        scratch_shapes=[dma, dma((2,)), dma, dma((2,)), dma],
        compiler_params=pltpu.CompilerParams(collective_id=collective_id, has_side_effects=True),
        name="gather_cols",
    )(block)


def reduce_cols_kernel(p_ref, o_ref, w, rp, ry, s_l, s_p, s_y, r_p, r_y):
    z, x, y, c = place()
    rows, cols = o_ref.shape
    partner, yn = device(z, x, y, 1 - c), device(z, x, 1 - y, c)
    greet([(None, partner), (None, yn)])

    def block(yy, cc):
        return p_ref.at[:, pl.ds(pl.multiple_of((yy * 2 + cc) * cols, cols), cols)]

    sends = [remote(block(yy, 1 - c), rp.at[k], s_p.at[k], r_p.at[k], partner)
             for k, yy in enumerate((1 - y, y))]
    loads = [pltpu.make_async_copy(block(yy, c), w.at[k], s_l.at[k])
             for k, yy in enumerate((1 - y, y))]
    cy = remote(w.at[0], ry, s_y, r_y, yn)
    for k in range(2):
        sends[k].start()
        loads[k].start()
    loads[0].wait()
    sends[0].wait_recv()
    add_blocks(w.at[0], [rp.at[0]], 0, rows)
    cy.start()
    loads[1].wait()
    sends[1].wait_recv()
    cy.wait_recv()
    add_blocks(w.at[1], [rp.at[1], ry], 0, rows, o_ref)
    for k in range(2):
        sends[k].wait_send()
    cy.wait_send()


def reduce_cols(partial, collective_id):
    rows, cols = partial.shape[0], partial.shape[1] // 4
    dma, vm, kind = pltpu.SemaphoreType.DMA, pltpu.VMEM, partial.dtype
    return pl.pallas_call(
        reduce_cols_kernel,
        out_shape=jax.ShapeDtypeStruct((rows, cols), jnp.float32),
        in_specs=[pl.BlockSpec(memory_space=pl.ANY)],
        out_specs=pl.BlockSpec(memory_space=pltpu.VMEM),
        scratch_shapes=[vm((2, rows, cols), kind), vm((2, rows, cols), kind), vm((rows, cols), kind),
                        dma((2,)), dma((2,)), dma, dma((2,)), dma],
        compiler_params=pltpu.CompilerParams(
            collective_id=collective_id, has_side_effects=True, vmem_limit_bytes=62 << 20
        ),
        name="reduce_cols",
    )(partial)


def sum_cols_kernel(v_ref, o_ref, got, s, r):
    group = lax.axis_index("tp")
    shard = lax.axis_index("fsdp")
    peers = [(shard, (group + k) % 4) for k in range(1, 4)]
    greet([(None, peer) for peer in peers])
    copies = [remote(v_ref, got.at[k], s.at[k], r.at[k], peer) for k, peer in enumerate(peers)]
    for copy in copies:
        copy.start()
    for copy in copies:
        copy.wait()
    o_ref[...] = v_ref[...] + got[0] + got[1] + got[2]


def sum_cols(vector, collective_id):
    dma = pltpu.SemaphoreType.DMA
    shape = vector.shape
    return pl.pallas_call(
        sum_cols_kernel,
        out_shape=jax.ShapeDtypeStruct(shape, jnp.float32),
        in_specs=[pl.BlockSpec(memory_space=pltpu.VMEM)],
        out_specs=pl.BlockSpec(memory_space=pltpu.VMEM),
        scratch_shapes=[pltpu.VMEM((3,) + shape, jnp.float32), dma((3,)), dma((3,))],
        compiler_params=pltpu.CompilerParams(collective_id=collective_id, has_side_effects=True),
        name="sum_cols",
    )(vector)


def greet_all(shard, group, shards, groups):
    barrier = pltpu.get_barrier_semaphore()
    total = shards * groups

    def step(k, carry):
        other = (shard * groups + group + k) % total
        pl.semaphore_signal(
            barrier, inc=1, device_id=(other // groups, other % groups), device_id_type=MESH
        )
        return carry

    lax.fori_loop(1, total, step, 0)
    pl.semaphore_wait(barrier, total - 1)


def swap_rows_kernel(shards, groups, v_ref, o_ref, s, r):
    shard, group = lax.axis_index("fsdp"), lax.axis_index("tp")
    total = shards * groups
    me = shard * groups + group
    greet_all(shard, group, shards, groups)

    def copy(k):
        other = (me + k) % total
        return remote(v_ref.at[other // groups], o_ref.at[me], s.at[k], r.at[k],
                      (other // groups, other % groups))

    def start(k, carry):
        copy(k).start()
        return carry

    def wait(k, carry):
        copy(k).wait()
        return carry

    lax.fori_loop(1, total, start, 0)
    o_ref[me] = v_ref[shard]
    lax.fori_loop(1, total, wait, 0)


def swap_rows(values, shards, groups, collective_id):
    dma, total = pltpu.SemaphoreType.DMA, shards * groups
    return pl.pallas_call(
        functools.partial(swap_rows_kernel, shards, groups),
        out_shape=jax.ShapeDtypeStruct((total,) + values.shape[1:], values.dtype),
        in_specs=[pl.BlockSpec(memory_space=pltpu.VMEM)],
        out_specs=pl.BlockSpec(memory_space=pltpu.VMEM),
        scratch_shapes=[dma((total,)), dma((total,))],
        compiler_params=pltpu.CompilerParams(collective_id=collective_id, has_side_effects=True),
        name="swap_rows",
    )(values)


def sum_small_kernel(shards, groups, v_ref, o_ref, got, s1, r1, s2, r2):
    shard, group = lax.axis_index("fsdp"), lax.axis_index("tp")
    total = shards * groups
    me = shard * groups + group
    greet_all(shard, group, shards, groups)

    def first(k):
        other = (shard + k) % shards
        return remote(v_ref.at[other], got.at[k], s1.at[k], r1.at[k], (other, group))

    def second(k):
        other = (me + k) % total
        return remote(o_ref.at[me], o_ref.at[me], s2.at[k], r2.at[k],
                      (other // groups, other % groups))

    for k in range(1, shards):
        first(k).start()
    acc = v_ref[shard]
    for k in range(1, shards):
        first(k).wait()
        acc = acc + got[k]
    o_ref[me] = acc

    def start(k, carry):
        second(k).start()
        return carry

    def wait(k, carry):
        second(k).wait()
        return carry

    lax.fori_loop(1, total, start, 0)
    lax.fori_loop(1, total, wait, 0)


def sum_small(values, shards, groups, collective_id):
    dma, total = pltpu.SemaphoreType.DMA, shards * groups
    part = values.shape[1:]
    return pl.pallas_call(
        functools.partial(sum_small_kernel, shards, groups),
        out_shape=jax.ShapeDtypeStruct((total,) + part, values.dtype),
        in_specs=[pl.BlockSpec(memory_space=pltpu.VMEM)],
        out_specs=pl.BlockSpec(memory_space=pltpu.VMEM),
        scratch_shapes=[pltpu.VMEM((shards,) + part, values.dtype), dma((shards,)), dma((shards,)),
                        dma((total,)), dma((total,))],
        compiler_params=pltpu.CompilerParams(collective_id=collective_id, has_side_effects=True),
        name="sum_small",
    )(values)


def dot_plain(left, right):
    return jnp.dot(left, right, preferred_element_type=jnp.float32)


def far_first(nz, z, k):
    at = 0
    for here in range(nz):
        order = sorted(range(nz), key=lambda other: (-abs(other - here), other))
        for step, other in enumerate(order):
            at = at + jnp.where((z == here) & (k == step), other, 0)
    return at


def tile_item(nz, z, k):
    return far_first(nz, z, jnp.where(k == nz - 1, nz - 1, nz - 2 - k))


def line_schedule(nz):
    order = []
    for here in range(nz):
        near = sorted(range(nz), key=lambda other: (-abs(other - here), other))[::-1]
        order.append(near[1:] + near[:1])
    sent = {}
    steps = [{} for _ in range(nz)]

    def send(here, to):
        if (here, to) not in sent:
            ready = 2 * order[here].index(to) + 2
            back = here - 1 if to > here else here + 1
            if 0 <= back < nz:
                ready = max(ready, send(back, to)) + 1
                steps[here].setdefault(ready, []).append(to)
            sent[here, to] = ready
        return sent[here, to]

    for here in range(nz):
        for to in range(nz):
            if to != here:
                send(here, to)
    for here in range(nz):
        arrivals = [send(near, here) for near in (here - 1, here + 1) if 0 <= near < nz]
        last = max(arrivals + [2 * order[here].index(here) + 2]) + 1
        steps[here].setdefault(last, []).append(here)
    return steps


def expert_kernel(nz, slots, block_rows, tok_ref, gain_ref, router_ref, attn_part, g_all, routes_all,
                  wg_all, wu_all, wd_all, middle_ref, scale_ref, low_ref, x_all, out_all, back_ref, gg_got, gates_ref, xr_all, gs_all, hid_all, gp_all, up_all,
                  wg, wu, wd, s_in_w, gg_ref, x_ref, g_ref, t_ref, o_ref, xr, gs, hid, gp, up, st,
                  w, lp, rx, rxd, ry, ryd, rz,
                  s_in, s_out, s_save, s_p, r_p, s_x, s_y, s_dx, s_dy, s_z, r_x, r_y, r_dx, r_dy, r_z,
                  s_g, r_g, *refs):
    z, x, y, c = place()
    shard, group = lax.axis_index("fsdp"), lax.axis_index("tp")
    expert = shard * 4 + group
    rows, cols = back_ref.shape
    width = x_ref.shape[1]
    half = rows // 2
    blocks = rows // block_rows
    experts = router_ref.shape[1]
    f32, low = jnp.float32, jnp.bfloat16
    partner = device(z, x, y, 1 - c)
    xn, yn = device(z, 1 - x, y, c), device(z, x, 1 - y, c)
    up_dev, down_dev = device(z + 1, x, y, c), device(z - 1, x, y, c)
    n_c, n_s = len(ReduceCols.scratch(16, 128, low)), len(RowSums.scratch(128))
    columns = ReduceCols(attn_part, middle_ref, refs[:n_c])
    sums = RowSums(refs[n_c : n_c + n_s])
    n_g = len(GatherAll.scratch(nz))
    moe_rows = [GatherAll(nz, part, x_all, refs[n_c + n_s + n * n_g : n_c + n_s + (n + 1) * n_g],
                          half // 2, n, 2) for n, part in enumerate(halves(low_ref))]

    def rows_step(name, *args):
        for part in moe_rows:
            getattr(part, name)(*args)

    greet_all(shard, group, 2 * nz, 4)
    columns.start()
    tiles = 2 * nz
    devices = 8 * nz

    def swap(k):
        other = (expert + k) % devices
        return remote(gg_ref.at[other // 4], gg_got.at[expert], s_g.at[k], r_g.at[k],
                      (other // 4, other % 4))

    def tile_of(j):
        return tile_item(nz, z, j // 2) * 2 + jnp.where(j % 2 == 0, 1 - x, x)

    def tile_rows(j):
        return pl.ds(pl.multiple_of(tile_of(j) * rows, rows), rows)

    def load(j):
        return pltpu.make_async_copy(x_all.at[tile_rows(j)], x_ref, s_in.at[0])

    def load_g(j):
        tile = tile_of(j)
        first = pl.ds(pl.multiple_of(tile * rows, half), half)
        second = pl.ds(pl.multiple_of(mirrored(nz, tile) * rows + half, half), half)
        return (pltpu.make_async_copy(g_all.at[first], g_ref.at[pl.ds(0, half)], s_in.at[1]),
                pltpu.make_async_copy(g_all.at[second], g_ref.at[pl.ds(half, half)], s_in.at[3]))

    def load_t(j):
        tile = tile_of(j)
        first = pl.ds(pl.multiple_of(tile * rows, half), half)
        second = pl.ds(pl.multiple_of(mirrored(nz, tile) * rows + half, half), half)
        return (pltpu.make_async_copy(routes_all.at[first], t_ref.at[pl.ds(0, half)], s_in.at[2]),
                pltpu.make_async_copy(routes_all.at[second], t_ref.at[pl.ds(half, half)], s_in.at[4]))

    def save_out(j):
        return pltpu.make_async_copy(o_ref, out_all.at[tile_rows(j)], s_out)

    def saves(j):
        pairs = ((xr, xr_all), (gs, gs_all), (hid, hid_all), (gp, gp_all), (up, up_all))
        return [pltpu.make_async_copy(src, dst.at[j], s_save.at[n])
                for n, (src, dst) in enumerate(pairs)]

    def c_p(zz, rel, slot):
        k = zz * 4 + rel
        return remote(st.at[slot, rel // 2], lp.at[zz, rel], s_p.at[k], r_p.at[k], partner)

    def c_diag(zz):
        return (remote(w.at[zz, 3, pl.ds(0, half)], rxd.at[zz], s_dx.at[zz], r_dx.at[zz], xn),
                remote(w.at[zz, 3, pl.ds(half, half)], ryd.at[zz], s_dy.at[zz], r_dy.at[zz], yn))

    def c_xy(zz):
        return (remote(w.at[zz, 1], rx.at[zz], s_x.at[zz], r_x.at[zz], xn),
                remote(w.at[zz, 2], ry.at[zz], s_y.at[zz], r_y.at[zz], yn))

    def c_z(zz, slot, where):
        return remote(w.at[zz, 0], rz.at[slot], s_z.at[zz], r_z.at[slot], where)

    def send_z(zz):
        pl.when(zz > z)(lambda: c_z(zz, zz, up_dev).start())
        pl.when(zz == z - 1)(lambda: c_z(zz, nz, down_dev).start())
        pl.when(zz < z - 1)(lambda: c_z(zz, zz, down_dev).start())

    def stage_d(zz, rel, slot):
        c_p(zz, rel, slot).wait_recv()
        add_blocks(w.at[zz, rel], [lp.at[zz, rel]], 0, rows)
        if rel == 3:
            for copy in c_diag(zz):
                copy.start()

    def stage_e(zz):
        dx, dy = c_diag(zz)
        cx, cy = c_xy(zz)
        dy.wait_recv()
        add_blocks(w.at[zz, 1], [ryd.at[zz]], half, half)
        cx.start()
        dx.wait_recv()
        add_blocks(w.at[zz, 2], [rxd.at[zz]], 0, half)
        cy.start()

    def passes(zz):
        return ((zz > z) & (z > 0)) | ((zz < z) & (z < nz - 1))

    def stage_f1(zz):
        cx, cy = c_xy(zz)
        cx.wait_recv()
        cy.wait_recv()
        add_blocks(w.at[zz, 0], [rx.at[zz], ry.at[zz]], 0, rows)
        pl.when((zz != z) & jnp.logical_not(passes(zz)))(lambda: send_z(zz))

    def stage_f2(zz):
        @pl.when((zz != z) & passes(zz))
        def _():
            c_z(zz, zz, up_dev).wait_recv()
            add_blocks(w.at[zz, 0], [rz.at[zz]], 0, rows)
            send_z(zz)

        @pl.when(zz == z)
        def _():
            low_part, high_part = rz.at[zz], rz.at[nz]
            pl.when(z > 0)(lambda: c_z(zz, zz, up_dev).wait_recv())
            pl.when(z < nz - 1)(lambda: c_z(zz, nz, down_dev).wait_recv())
            own = w.at[zz, 0]
            pl.when(z == 0)(lambda: add_blocks(own, [high_part], 0, rows, back_ref))
            pl.when(z == nz - 1)(lambda: add_blocks(own, [low_part], 0, rows, back_ref))
            pl.when((z > 0) & (z < nz - 1))(
                lambda: add_blocks(own, [low_part, high_part], 0, rows, back_ref)
            )

    def compute(j):
        zz = tile_item(nz, z, j // 2)
        slot = j % 2
        load(j).wait()
        for copy in load_t(j):
            copy.wait()
        lanes = lax.broadcasted_iota(jnp.int32, (rows, experts), 1)
        routes = t_ref[...]
        chosen = routes[:, 0:1] == lanes
        for n in range(1, TOPK):
            chosen = chosen | (routes[:, n : n + 1] == lanes)
        logits = jnp.where(chosen, dot_plain(x_ref[...], router_ref[...]), masked_score)
        peak = jnp.max(logits, axis=1, keepdims=True)
        weights = jnp.where(chosen, jnp.exp(logits - peak), 0.0)
        gates = weights / jnp.sum(weights, axis=1, keepdims=True)
        gates_ref[...] = gates
        mine = lanes == expert
        gate_col = jnp.sum(jnp.where(mine, gates, 0.0), axis=1, keepdims=True)
        match_col = jnp.sum(jnp.where(mine & chosen, 1.0, 0.0), axis=1, keepdims=True)
        sub = lax.broadcasted_iota(jnp.int32, (block_rows, block_rows), 0)
        lane = lax.broadcasted_iota(jnp.int32, (block_rows, block_rows), 1)
        eye = sub == lane
        before = (sub > lane).astype(f32).astype(low)
        chosen_low = chosen.astype(f32).astype(low)
        pick, put, slot_gate = [], [], []
        slot_lane = lax.broadcasted_iota(jnp.int32, (block_rows, slots), 1).astype(f32)
        slot_sub = lax.broadcasted_iota(jnp.int32, (slots, block_rows), 0).astype(f32)
        for b in range(blocks):
            part = slice(b * block_rows, (b + 1) * block_rows)
            ranks = dot_plain(before, chosen_low[part])
            rank = jnp.sum(jnp.where(mine[part], ranks, 0.0), axis=1, keepdims=True)
            rank = jnp.where(match_col[part] > 0.0, rank, -1.0)
            rank_row = jnp.sum(jnp.where(eye, rank, 0.0), axis=0, keepdims=True)
            gate_row = jnp.sum(jnp.where(eye, gate_col[part], 0.0), axis=0, keepdims=True)
            hot = rank_row == slot_sub
            pick.append(hot.astype(f32).astype(low))
            put.append((rank == slot_lane).astype(f32).astype(low))
            slot_gate.append(jnp.sum(jnp.where(hot, gate_row, 0.0), axis=1, keepdims=True))
        slot_gate = jnp.concatenate(slot_gate, axis=0)

        def gather(ref, at):
            return jnp.concatenate(
                [dot_plain(pick[b], ref[pl.ds(b * block_rows, block_rows), at])
                 for b in range(blocks)],
                axis=0,
            )

        def scatter(ref, at, values):
            for b in range(blocks):
                ref[pl.ds(b * block_rows, block_rows), at] = dot_plain(
                    put[b], values[b * slots : (b + 1) * slots]
                ).astype(low)

        def columns(i):
            return pl.ds(pl.multiple_of(i * cols, cols), cols)

        @pl.when(j > 0)
        def _():
            for copy in saves(j):
                copy.wait()

        def take(i, carry):
            xr[:, columns(i)] = gather(x_ref, columns(i)).astype(low)
            return carry

        lax.fori_loop(0, width // cols, take, 0)

        pl.when(j == 0)(lambda: rows_step('second', 2))
        for k in range(3, nz):
            pl.when(j == 1)(lambda: rows_step('second', k))

        @pl.when((j % 2 == 1) & (j < tiles - 1))
        def _():
            rows_step('ready', tile_item(nz, z, j // 2 + 1))

        @pl.when(j < tiles - 1)
        def _():
            load(j + 1).start()
            for copy in load_t(j + 1):
                copy.start()

        gate_pre = dot_plain(xr[...], wg[...])
        up_pre = dot_plain(xr[...], wu[...])
        sig = jax.nn.sigmoid(gate_pre)
        silu = gate_pre * sig
        hidden_low = (silu * up_pre).astype(low)
        hid[...] = hidden_low
        for copy in load_g(j):
            copy.wait()
        pl.when(j > 0)(lambda: save_out(j).wait())

        def middle_part(i, carry):
            total, hidden_grad = carry
            at = columns(i)
            grad = gather(g_ref, at)
            expert_out = dot_plain(hidden_low, wd[:, at]).astype(low).astype(f32)
            total = total + jnp.sum(grad * expert_out, axis=1, keepdims=True)
            pair_grad = (grad * slot_gate).astype(low)
            gs[:, at] = pair_grad
            scatter(o_ref, at, (expert_out * slot_gate).astype(low))
            return total, hidden_grad + dot_last(pair_grad, wd[:, at])

        gates_grad, hidden_grad = lax.fori_loop(
            0,
            width // cols,
            middle_part,
            (jnp.zeros(slot_gate.shape, f32), jnp.zeros(gate_pre.shape, f32)),
        )
        save_out(j).start()

        @pl.when(j < tiles - 1)
        def _():
            for copy in load_g(j + 1):
                copy.start()

        for b in range(blocks):
            gg_ref[tile_of(j), :, pl.ds(b * block_rows, block_rows)] = jnp.sum(
                pick[b].astype(f32) * gates_grad[b * slots : (b + 1) * slots],
                axis=0,
                keepdims=True,
            )
        gate_grad = (hidden_grad * up_pre * (sig * (1.0 + gate_pre * (1.0 - sig)))).astype(low)
        up_grad = (hidden_grad * silu).astype(low)
        gp[...] = gate_grad
        up[...] = up_grad
        for copy in saves(j):
            copy.start()

        def part_of(i, yy, cc):
            at = columns(yy * 2 + cc)
            row_grad = dot_last(gate_grad, wg[at, :]) + dot_last(up_grad, wu[at, :])
            return row_grad.astype(low)

        first = jnp.where(slot == 0, 1, 0)

        def to_partner(i, carry):
            yy = jnp.where(i == 1, 1 - y, y)
            rel = first + 2 * i

            @pl.when(j >= 2)
            def _():
                before_zz = tile_item(nz, z, j // 2 - 1)
                k = before_zz * 4 + rel
                remote(st.at[slot, i], lp.at[before_zz, rel], s_p.at[k], r_p.at[k], partner).wait_send()

            scatter(st.at[slot, i], slice(None), part_of(i, yy, 1 - c))
            k = zz * 4 + rel
            remote(st.at[slot, i], lp.at[zz, rel], s_p.at[k], r_p.at[k], partner).start()
            return carry

        def to_own(i, carry):
            yy = jnp.where(i == 1, 1 - y, y)
            scatter(w.at[zz, first + 2 * i], slice(None), part_of(i, yy, c))
            return carry

        lax.fori_loop(0, 2, to_partner, 0)
        lax.fori_loop(0, 2, to_own, 0)

    weights = [pltpu.make_async_copy(src, dst, s_in_w.at[n])
               for n, (src, dst) in enumerate(((wg_all, wg), (wu_all, wu), (wd_all, wd)))]
    for copy in load_t(0) + load_g(0) + tuple(weights):
        copy.start()

    corner = diagonal()
    columns.first()
    columns.second()

    def residual(n, carry):
        here = pl.ds(pl.multiple_of(n * 128, 128), 128)
        total = middle_ref[here, :] + tok_ref[here, :].astype(f32)
        middle_ref[here, :] = total
        sums.got[0, pl.ds(n, 1), :] = to_row(jnp.sum(total * total, axis=1, keepdims=True), corner)
        return carry

    def norm(n, carry):
        here = pl.ds(pl.multiple_of(n * 128, 128), 128)
        scale = lax.rsqrt(to_column(sums.total(n), corner) / width + norm_eps)
        scale_ref[here, :] = scale
        low_ref[here, :] = (middle_ref[here, :] * scale * gain_ref[...]).astype(low)
        return carry

    lax.fori_loop(0, rows // 128, residual, 0)
    sums.start()
    sums.wait()
    lax.fori_loop(0, rows // 128, norm, 0)
    for part in moe_rows:
        part.own().start()
    for part in moe_rows:
        part.own().wait()
    rows_step('first', 0)
    rows_step('first', 1)
    rows_step('second', 0)
    rows_step('first', 2)
    rows_step('second', 1)
    rows_step('third', 0)
    for k in range(3, nz):
        rows_step('first', k)
    rows_step('third', 1)
    rows_step('ready', tile_item(nz, z, 0))
    load(0).start()
    for copy in weights:
        copy.wait()
    schedule = line_schedule(nz)
    last_step = max(max(steps) for steps in schedule)

    def step(j, carry):
        k, odd = j // 2, j % 2 == 1
        pl.when(j < tiles)(lambda: compute(j))
        pl.when(j == 0)(lambda: rows_step('third', 2))
        for n in range(3, nz):
            pl.when(j == 2)(lambda: rows_step('third', n))

        @pl.when(j == tiles)
        def _():
            gg_got[expert] = gg_ref[shard]
            loop_from_one(devices, lambda n: swap(n).start())

        @pl.when(jnp.logical_not(odd) & (k < nz))
        def _():
            zz = tile_item(nz, z, k)
            stage_d(zz, 3, 0)
            stage_d(zz, 1, 0)

        @pl.when(odd & (k < nz))
        def _():
            zz = tile_item(nz, z, k)
            stage_d(zz, 2, 1)
            stage_d(zz, 0, 1)
            stage_e(zz)

        @pl.when((k >= 1) & (k < nz + 1) & jnp.logical_not(odd))
        def _():
            stage_f1(tile_item(nz, z, k - 1))

        for here, steps in enumerate(schedule):
            for at, places in steps.items():
                for to in places:
                    pl.when((z == here) & (j == at))(lambda to=to: stage_f2(jnp.int32(to)))

        return carry

    lax.fori_loop(0, last_step + 1, step, 0)
    loop_from_one(devices, lambda n: swap(n).wait())
    save_out(tiles - 1).wait()
    for copy in saves(tiles - 1):
        copy.wait()
    for slot in range(2):
        for i in range(2):
            c_p(z, 1 - slot + 2 * i, slot).wait_send()

    def finish(zz, carry):
        for copy in c_diag(zz) + c_xy(zz):
            copy.wait_send()
        pl.when(zz != z)(c_z(zz, zz, up_dev).wait_send)
        return carry

    lax.fori_loop(0, nz, finish, 0)
    columns.finish()
    rows_step('finish_sends')


def run_experts(tokens, gain, router, attn_part, g_all, routes_all, gate_w, up_w, down_w, block_rows,
                slots, nz, collective_id):
    total, width = g_all.shape
    hidden = gate_w.shape[1]
    experts = router.shape[1]
    tiles = 2 * nz
    rows, cols = total // tiles, width // 4
    pairs = rows // block_rows * slots
    half = rows // 2
    f32, low = jnp.float32, jnp.bfloat16
    any_space = pl.BlockSpec(memory_space=pl.ANY)
    vmem = pl.BlockSpec(memory_space=pltpu.VMEM)
    vm, dma, shape = pltpu.VMEM, pltpu.SemaphoreType.DMA, jax.ShapeDtypeStruct
    return pl.pallas_call(
        functools.partial(expert_kernel, nz, slots, block_rows),
        in_specs=[vmem] * 3 + [any_space] * 6,
        out_specs=[vmem] * 3 + [any_space] * 2 + [vmem] * 3 + [any_space] * 5,
        out_shape=[
            shape((rows, cols), f32), shape((rows, 1), f32), shape((rows, cols), low),
            shape((total, width), low),
            shape((total, width), low), shape((rows, cols), f32), shape((4 * tiles, 1, rows), f32),
            shape((rows, experts), f32),
            shape((tiles, pairs, width), low), shape((tiles, pairs, width), low),
            shape((tiles, pairs, hidden), low), shape((tiles, pairs, hidden), low),
            shape((tiles, pairs, hidden), low),
        ],
        scratch_shapes=[
            vm((width, hidden), low), vm((width, hidden), low), vm((hidden, width), low), dma((3,)),
            vm((tiles, 1, rows), f32), vm((rows, width), low), vm((rows, width), low),
            vm((rows, routes_all.shape[1]), jnp.int32), vm((rows, width), low),
            vm((pairs, width), low), vm((pairs, width), low),
            vm((pairs, hidden), low), vm((pairs, hidden), low), vm((pairs, hidden), low),
            vm((2, 2, rows, cols), low),
            vm((nz, 4, rows, cols), low), vm((nz, 4, rows, cols), low),
            vm((nz, rows, cols), low), vm((nz, half, cols), low),
            vm((nz, rows, cols), low), vm((nz, half, cols), low),
            vm((nz + 1, rows, cols), low),
            dma((5,)), dma, dma((5,)), dma((4 * nz,)), dma((4 * nz,)),
        ] + [dma((nz,))] * 9 + [dma((nz + 1,))] + [dma((4 * tiles,))] * 2
        + ReduceCols.scratch(rows, cols, low) + RowSums.scratch(rows) + GatherAll.scratch(nz) * 2,
        compiler_params=pltpu.CompilerParams(
            collective_id=collective_id, has_side_effects=True, vmem_limit_bytes=62 << 20
        ),
        name="experts",
    )(tokens, gain, router, attn_part, g_all, routes_all, gate_w, up_w, down_w)


def near_first(nz, z, k):
    return far_first(nz, z, nz - 1 - k)


def halves(ref):
    rows = ref.shape[0] // 2
    return [ref.at[pl.ds(part * rows, rows)] for part in range(2)]


class GatherAll:
    sems = 6

    @staticmethod
    def scratch(nz):
        dma = pltpu.SemaphoreType.DMA
        return [dma] + [dma((5 * nz,))] * 2 + [dma((nz,))] * 11

    def __init__(self, nz, src, out, sems, cut, part=0, parts=1):
        (self.lsem, self.s_p, self.r_p, self.s_u, self.s_d, self.s_x, self.s_y, self.s_dx,
         self.s_dy, self.r_z, self.r_x, self.r_y, self.r_dx, self.r_dy) = sems
        self.nz, self.src, self.out, self.cut = nz, src, out, cut
        self.rows, self.cols = src.shape
        self.offset, self.stride = part * self.rows, parts * self.rows
        self.place = z, x, y, c = place()
        self.partner, self.xn, self.yn = (
            device(z, x, y, 1 - c), device(z, 1 - x, y, c), device(z, x, 1 - y, c))
        self.up, self.down = device(z + 1, x, y, c), device(z - 1, x, y, c)

    def block(self, zz, xx, yy, cc, part=None):
        start, size, unit = (zz * 2 + xx) * self.stride + self.offset, self.rows, self.rows
        if part == 0:
            size, unit = self.cut, self.rows
        elif part == 1:
            start, size = start + self.cut, self.rows - self.cut
            unit = math.gcd(self.cut, self.rows)
        return self.out.at[pl.ds(pl.multiple_of(start, unit), size),
                           pl.ds(pl.multiple_of((yy * 2 + cc) * self.cols, self.cols), self.cols)]

    def own(self):
        z, x, y, c = self.place
        return pltpu.make_async_copy(self.src, self.block(z, x, y, c), self.lsem)

    def line(self, zz):
        z, x, y, c = self.place
        here = self.block(zz, x, y, c)
        return (remote(here, here, self.s_u.at[zz], self.r_z.at[zz], self.up),
                remote(here, here, self.s_d.at[zz], self.r_z.at[zz], self.down))

    def sides(self, zz):
        z, x, y, c = self.place
        here = self.block(zz, x, y, c)
        return (remote(here, here, self.s_x.at[zz], self.r_x.at[zz], self.xn),
                remote(here, here, self.s_y.at[zz], self.r_y.at[zz], self.yn))

    def across(self, zz):
        z, x, y, c = self.place
        copies = []
        if self.cut > 0:
            here = self.block(zz, 1 - x, y, c, 0)
            copies.append(remote(here, here, self.s_dy.at[zz], self.r_dy.at[zz], self.yn))
        if self.cut < self.rows:
            here = self.block(zz, x, 1 - y, c, 1)
            copies.append(remote(here, here, self.s_dx.at[zz], self.r_dx.at[zz], self.xn))
        return copies

    def pair(self, zz, rel, mine=True):
        z, x, y, c = self.place
        xx = 1 - x if rel in (1, 3, 4) else x
        yy = 1 - y if rel in (2, 3, 4) else y
        here = self.block(zz, xx, yy, c if mine else 1 - c, {3: 0, 4: 1}.get(rel))
        k = zz * 5 + rel
        return remote(here, here, self.s_p.at[k], self.r_p.at[k], self.partner)

    def parts(self):
        return [0, 1, 2] + [3] * (self.cut > 0) + [4] * (self.cut < self.rows)

    def first(self, k):
        self.first_to(near_first(self.nz, self.place[0], k))

    def second(self, k):
        self.second_to(near_first(self.nz, self.place[0], k))

    def third(self, k):
        self.third_to(near_first(self.nz, self.place[0], k))

    def first_to(self, zz):
        z = self.place[0]
        up, down = self.line(zz)
        pl.when(zz != z)(lambda: up.wait_recv())
        pl.when((zz <= z) & (z < self.nz - 1))(lambda: up.start())
        pl.when((zz >= z) & (z > 0))(lambda: down.start())
        for copy in self.sides(zz):
            copy.start()
        self.pair(zz, 0).start()

    def second_to(self, zz):
        to_x, to_y = self.sides(zz)
        across = self.across(zz)
        to_x.wait_recv()
        if self.cut > 0:
            across[0].start()
        self.pair(zz, 1).start()
        to_y.wait_recv()
        if self.cut < self.rows:
            across[-1].start()
        self.pair(zz, 2).start()

    def third_to(self, zz):
        across = self.across(zz)
        for rel, copy in zip(self.parts()[3:], across):
            copy.wait_recv()
            self.pair(zz, rel).start()

    def ready(self, zz):
        for rel in self.parts():
            self.pair(zz, rel, False).wait_recv()

    def finish_sends(self):
        z = self.place[0]

        def step(zz, carry):
            for rel in self.parts():
                self.pair(zz, rel).wait_send()
            up, down = self.line(zz)
            pl.when((zz <= z) & (z < self.nz - 1))(lambda: up.wait_send())
            pl.when((zz >= z) & (z > 0))(lambda: down.wait_send())
            for copy in tuple(self.sides(zz)) + tuple(self.across(zz)):
                copy.wait_send()
            return carry

        lax.fori_loop(0, self.nz, step, 0)

    def finish(self):
        def step(zz, carry):
            self.ready(zz)
            return carry

        lax.fori_loop(0, self.nz, step, 0)
        self.finish_sends()


class GatherCausal:
    @staticmethod
    def scratch(nz):
        dma = pltpu.SemaphoreType.DMA
        return [dma, dma, dma((2,)), dma((2 * nz,)), dma((2 * nz,)), dma((2 * nz,))]

    def __init__(self, nz, src, out, held, sems):
        self.s_x, self.r_x, self.lsem, self.s_z, self.r_z, self.l_z = sems
        self.nz, self.src, self.out, self.held_ref = nz, src, out, held
        self.place = z, x, y, c = place()
        self.xn = device(z, 1 - x, y, c)
        self.near = (device(z + 1, x, y, c), device(z - 1, x, y, c))

    def own(self):
        z, x = self.place[:2]
        return [pltpu.make_async_copy(self.src, self.out.at[z, x], self.lsem.at[0]),
                pltpu.make_async_copy(self.src, self.held_ref.at[z, x], self.lsem.at[1])]

    def side(self):
        z, x = self.place[:2]
        return remote(self.src, self.out.at[z, x], self.s_x, self.r_x, self.xn)

    def line(self, zz, micro):
        here = self.out.at[zz, :, micro]
        return remote(here, here, self.s_z.at[zz * 2 + micro], self.r_z.at[zz * 2 + micro],
                      self.near[micro])

    def keep(self, zz, micro):
        return pltpu.make_async_copy(self.out.at[zz, :, micro], self.held_ref.at[zz, :, micro],
                                     self.l_z.at[zz * 2 + micro])

    def needed(self, zz, micro):
        return zz <= self.place[0] if micro == 0 else zz >= self.place[0]

    def sends(self, zz, micro):
        z = self.place[0]
        return self.needed(zz, micro) & (z < self.nz - 1 if micro == 0 else z > 0)

    def first_to(self, zz):
        z = self.place[0]

        @pl.when(zz == z)
        def _():
            for copy in self.own():
                copy.wait()
            self.side().wait_recv()

        for micro in range(2):
            pl.when((zz != z) & self.needed(zz, micro))(lambda: self.line(zz, micro).wait_recv())
            pl.when(self.sends(zz, micro))(lambda: self.line(zz, micro).start())
            pl.when(self.needed(zz, micro))(lambda: self.keep(zz, micro).start())

    def ready(self, zz):
        for micro in range(2):
            pl.when(self.needed(zz, micro))(lambda: self.keep(zz, micro).wait())

    def finish(self):
        self.side().wait_send()

        def step(zz, carry):
            for micro in range(2):
                pl.when(self.sends(zz, micro))(lambda: self.line(zz, micro).wait_send())
            return carry

        lax.fori_loop(0, self.nz, step, 0)


class GatherRows:
    @staticmethod
    def scratch(nz):
        dma = pltpu.SemaphoreType.DMA
        return [dma] + [dma((nz,))] * 5

    def __init__(self, nz, src, out, sems, part=0, parts=1):
        self.lsem, self.s_u, self.s_d, self.s_x, self.r_z, self.r_x = sems
        self.nz, self.src, self.out = nz, src, out
        self.offset, self.stride = part * src.shape[0], parts * src.shape[0]
        self.place = z, x, y, c = place()
        self.xn = device(z, 1 - x, y, c)
        self.up, self.down = device(z + 1, x, y, c), device(z - 1, x, y, c)

    def block(self, zz):
        rows = self.src.shape[0]
        start = (zz * 2 + self.place[1]) * self.stride + self.offset
        return self.out.at[pl.ds(pl.multiple_of(start, rows), rows)]

    def own(self):
        return pltpu.make_async_copy(self.src, self.block(self.place[0]), self.lsem)

    def copies(self, zz):
        here = self.block(zz)
        return (remote(here, here, self.s_u.at[zz], self.r_z.at[zz], self.up),
                remote(here, here, self.s_d.at[zz], self.r_z.at[zz], self.down),
                remote(here, here, self.s_x.at[zz], self.r_x.at[zz], self.xn))

    def first_to(self, zz):
        z = self.place[0]
        up, down, to_x = self.copies(zz)
        pl.when(zz != z)(lambda: up.wait_recv())
        pl.when((zz <= z) & (z < self.nz - 1))(lambda: up.start())
        pl.when((zz >= z) & (z > 0))(lambda: down.start())
        to_x.start()

    def finish(self):
        z = self.place[0]

        def step(zz, carry):
            up, down, to_x = self.copies(zz)
            to_x.wait()
            pl.when((zz <= z) & (z < self.nz - 1))(lambda: up.wait_send())
            pl.when((zz >= z) & (z > 0))(lambda: down.wait_send())
            return carry

        lax.fori_loop(0, self.nz, step, 0)


def mirrored(nz, shard):
    return (nz - 1 - shard // 2) * 2 + shard % 2


def stream_unit(u, nz):
    shard = lax.axis_index("fsdp")
    later = u > shard
    micro = jnp.where(later, 1, 0)
    here = jnp.where(later, mirrored(nz, shard), shard)
    key_place = here - jnp.where(later, u - shard - 1, u)
    owner = jnp.where(later, mirrored(nz, key_place), key_place)
    return micro, here, key_place, owner


def key_bias(micro, here, key_place, block, start_ref):
    key = key_place * block + lax.broadcasted_iota(jnp.int32, (block, block), 0)
    query = here * block + lax.broadcasted_iota(jnp.int32, (block, block), 1)
    return jnp.where((key >= start_ref[micro]) & (key <= query), 0.0, masked_score)


def norm_turn(raw, gain, cosine, sine):
    scale = lax.rsqrt(jnp.mean(raw * raw, axis=1, keepdims=True) + norm_eps)
    normed = raw * scale * gain
    return normed * cosine + pltpu.roll(normed, raw.shape[1] // 2, 1) * sine


def attend_kernel(nz, gain_ref, gq_ref, gk_ref, cos_ref, sin_ref, start_ref, cot_ref, wo_ref,
                  tok_all, wq_all, wk_all, wv_all,
                  normed, scale_ref, q_pre, k_pre, q_ref, heads_ref, lse_ref, kv_all, cot_all, wo_all,
                  tok_ref, wq, wk, wv, s_in, kv_ref, kv, acc, peak, total, *sems):
    shards = 2 * nz
    width = kv_ref.shape[2] // 2
    block = q_ref.shape[0] // 2
    low = jnp.bfloat16
    heads = q_ref.shape[1] // width
    z, x, y, c = place()
    n_c, n_o = len(GatherAll.scratch(nz)), len(GatherRows.scratch(nz))
    end = 2 * (n_c + n_o)
    cots = [GatherAll(nz, half, cot_all, sems[n * n_c : (n + 1) * n_c], half.shape[0], n, 2)
            for n, half in enumerate(halves(cot_ref))]
    outs = [GatherRows(nz, half, wo_all, sems[2 * n_c + n * n_o : 2 * n_c + (n + 1) * n_o], n, 2)
            for n, half in enumerate(halves(wo_ref))]
    keys_in = GatherCausal(nz, kv_ref, kv_all, kv, sems[end:])
    greet([(None, cots[0].partner), (None, cots[0].xn), (None, cots[0].yn),
           (z < nz - 1, cots[0].up), (z > 0, cots[0].down)])
    for part in outs + cots:
        part.own().start()
    fetches = [pltpu.make_async_copy(src, dst, s_in.at[n]) for n, (src, dst) in enumerate((
        (tok_all, tok_ref), (wk_all, wk), (wv_all, wv), (wq_all, wq)))]
    for copy in fetches:
        copy.start()
    for part in outs + cots:
        part.own().wait()
    for part in cots:
        part.first_to(z)
    fetches[0].wait()

    def token_norm(n, carry):
        rows = pl.ds(pl.multiple_of(n * 64, 64), 64)
        row = tok_ref[rows, :].astype(jnp.float32)
        scale = lax.rsqrt(jnp.mean(row * row, axis=1, keepdims=True) + norm_eps)
        scale_ref[rows, :] = scale
        normed[rows, :] = (row * scale * gain_ref[...]).astype(low)
        return carry

    lax.fori_loop(0, tok_ref.shape[0] // 64, token_norm, 0)
    fetches[1].wait()
    k_pre[...] = dot_plain(normed[...], wk[...])
    turned = norm_turn(k_pre[...], gk_ref[...], cos_ref[...], sin_ref[...]).astype(low)
    fetches[2].wait()
    value = dot_plain(normed[...], wv[...]).astype(low)
    for micro in range(2):
        rows = slice(micro * block, (micro + 1) * block)
        kv_ref[micro, :, :width] = turned[rows]
        kv_ref[micro, :, width:] = value[rows]
    keys_in.side().start()
    for copy in keys_in.own():
        copy.start()
    peak[...] = jnp.full(peak.shape, masked_score, jnp.float32)
    total[...] = jnp.zeros_like(total)
    acc[...] = jnp.zeros_like(acc)
    fetches[3].wait()

    def at_distance(dist, fn):
        for side in (-1, 1):
            zz = z + side * dist
            valid = (dist >= 0) & (zz >= 0) & (zz < nz) & ((dist > 0) | (side > 0))
            pl.when(valid)(lambda: fn(zz))

    def tick(u, carry):
        def gradients(zz):
            @pl.when(u > 0)
            def _():
                for part in cots:
                    part.first_to(zz)

        def weights(zz):
            for part in outs:
                part.first_to(zz)

        def across(zz):
            for part in cots:
                part.second_to(zz)

        def onward(zz):
            for part in cots:
                part.third_to(zz)

        at_distance(u, keys_in.first_to)
        at_distance(u, gradients)
        at_distance(u, weights)
        at_distance(u - 1, across)
        at_distance(u - 2, onward)
        at_distance(u - 1, attend_item)
        return carry

    def attend_item(zz):
        own = zz == z
        keys_in.ready(zz)

        def part(i, carry):
            micro = jnp.where(own, i // 2, jnp.where(zz < z, 0, 1))
            xx = jnp.where(own, jnp.where(i % 2 == 0, x, 0), i)
            valid = jnp.where(own, jnp.where((i % 2 == 0) | (x == 1), 1, 0), jnp.where(i < 2, 1, 0))
            pl.when(valid == 1)(lambda: attention(micro, zz, xx))
            return carry

        lax.fori_loop(0, 4, part, 0)

    def attention(micro, zz, xx):
        def at_place(z_at, x_at):
            return jnp.where(micro == 0, z_at, nz - 1 - z_at) * 2 + x_at

        here, key_place = at_place(z, x), at_place(zz, xx)
        bias = key_bias(micro, here, key_place, block, start_ref)
        both = kv.at[zz, xx, micro]
        keys, values = both[:, :width], both[:, width:]
        q_rows = pl.ds(pl.multiple_of(micro * block, block), block)

        def head(h, carry):
            at = micro * heads + h
            query = q_ref[q_rows, pl.ds(pl.multiple_of(h * width, width), width)]
            scores = dot_last(keys, query) * width ** (-0.5) + bias
            before = peak[at]
            now = jnp.maximum(before, jnp.max(scores, axis=0, keepdims=True))
            weights = jnp.exp(scores - now)
            factor = jnp.exp(before - now)
            peak[at] = now
            total[at] = total[at] * factor + jnp.sum(weights, axis=0, keepdims=True)
            acc[at] = acc[at] * factor + dot_first(values, weights.astype(jnp.bfloat16))
            return carry

        lax.fori_loop(0, heads, head, 0, unroll=4)

    def prepare(n, carry):
        pair = pl.ds(pl.multiple_of(n * 2 * width, 2 * width), 2 * width)
        q_pre[:, pair] = dot_plain(normed[...], wq[:, pair])
        for h in range(2):
            cols = pl.ds(pl.multiple_of((n * 2 + h) * width, width), width)
            q_ref[:, cols] = norm_turn(
                q_pre[:, cols], gq_ref[...], cos_ref[...], sin_ref[...]
            ).astype(low)
        return carry

    lax.fori_loop(0, heads // 2, prepare, 0)
    tick(0, 0)
    lax.fori_loop(1, nz + 2, tick, 0)

    def close(at, carry):
        micro, h = at // heads, at % heads
        result = (acc[at] / total[at]).T
        here = pl.ds(pl.multiple_of(micro * block, block), block)
        cols = pl.ds(pl.multiple_of(h * width, width), width)
        heads_ref[here, cols] = result.astype(jnp.bfloat16)
        lse_ref[at] = peak[at] + jnp.log(total[at])
        return carry

    lax.fori_loop(0, 2 * heads, close, 0)
    keys_in.finish()
    for part in outs + cots:
        part.finish()


def attend(tokens, gain_attn, wq_all, wk_all, wv_all, gain_query, gain_key, cosine, sine, starts,
           cotangent, w_out, nz, collective_id):
    rows, features = tokens.shape
    columns, width = wq_all.shape[1], wk_all.shape[1]
    heads = columns // width
    block = rows // 2
    any_space = pl.BlockSpec(memory_space=pl.ANY)
    vmem = pl.BlockSpec(memory_space=pltpu.VMEM)
    vm, shape, f32, low = pltpu.VMEM, jax.ShapeDtypeStruct, jnp.float32, jnp.bfloat16
    return pl.pallas_call(
        functools.partial(attend_kernel, nz),
        in_specs=[vmem] * 8 + [any_space] * 4,
        out_specs=[vmem] * 7 + [any_space] * 3,
        out_shape=[
            shape((rows, features), low), shape((rows, 1), f32),
            shape((rows, columns), f32), shape((rows, width), f32),
            shape((rows, columns), low), shape((rows, columns), low),
            shape((2 * heads, 1, block), f32),
            shape((nz, 2, 2, block, 2 * width), low),
            shape((rows * 2 * nz, cotangent.shape[1] * 4), cotangent.dtype),
            shape((w_out.shape[0] * 2 * nz, w_out.shape[1]), w_out.dtype),
        ],
        scratch_shapes=[
            vm((rows, features), low), vm(wq_all.shape, low), vm(wk_all.shape, low),
            vm(wv_all.shape, low), pltpu.SemaphoreType.DMA((4,)),
            vm((2, block, 2 * width), low), vm((nz, 2, 2, block, 2 * width), low),
            vm((2 * heads, width, block), f32), vm((2 * heads, 1, block), f32),
            vm((2 * heads, 1, block), f32),
        ] + GatherAll.scratch(nz) * 2 + GatherRows.scratch(nz) * 2 + GatherCausal.scratch(nz),
        compiler_params=pltpu.CompilerParams(
            collective_id=collective_id, has_side_effects=True, vmem_limit_bytes=62 << 20
        ),
        name="attend",
    )(gain_attn, gain_query, gain_key, cosine, sine, starts, cotangent, w_out, tokens, wq_all, wk_all,
      wv_all)


class ScatterAll:
    @staticmethod
    def scratch(nz, rows, cols, kind, cut):
        vm, dma = pltpu.VMEM, pltpu.SemaphoreType.DMA
        return [
            vm((nz, 4, rows, cols), kind), vm((nz, 4, rows, cols), kind),
            vm((nz, rows, cols), kind), vm((nz, max(cut, 16), cols), kind),
            vm((nz, rows, cols), kind), vm((nz, max(rows - cut, 16), cols), kind),
            vm((nz + 1, rows, cols), kind),
        ] + [dma((4 * nz,))] * 3 + [dma((nz,))] * 9 + [dma((nz + 1,))]

    def __init__(self, nz, partial, out, refs, cut, part=0, parts=1):
        (self.w, self.lp, self.rx, self.rxd, self.ry, self.ryd, self.rz,
         self.s_l, self.s_p, self.r_p, self.s_x, self.s_y, self.s_dx, self.s_dy, self.s_z,
         self.r_x, self.r_y, self.r_dx, self.r_dy, self.r_z) = refs
        self.nz, self.partial, self.out, self.cut = nz, partial, out, cut
        self.rows, self.cols = out.shape
        self.offset, self.stride = part * self.rows, parts * self.rows
        self.place = z, x, y, c = place()
        self.partner, self.xn, self.yn = (
            device(z, x, y, 1 - c), device(z, 1 - x, y, c), device(z, x, 1 - y, c))
        self.up, self.down = device(z + 1, x, y, c), device(z - 1, x, y, c)

    def block(self, zz, rel, cc):
        z, x, y, c = self.place
        xx = 1 - x if rel in (1, 3) else x
        yy = 1 - y if rel in (2, 3) else y
        return self.partial.at[
            pl.ds(pl.multiple_of((zz * 2 + xx) * self.stride + self.offset, self.rows), self.rows),
            pl.ds(pl.multiple_of((yy * 2 + cc) * self.cols, self.cols), self.cols)]

    def pair(self, zz, rel):
        k = zz * 4 + rel
        return remote(self.block(zz, rel, 1 - self.place[3]), self.lp.at[zz, rel],
                      self.s_p.at[k], self.r_p.at[k], self.partner)

    def load(self, zz, rel):
        return pltpu.make_async_copy(
            self.block(zz, rel, self.place[3]), self.w.at[zz, rel], self.s_l.at[zz * 4 + rel])

    def across(self, zz):
        copies = []
        if self.cut > 0:
            copies.append(remote(self.w.at[zz, 3, pl.ds(0, self.cut)], self.rxd.at[zz],
                                 self.s_dx.at[zz], self.r_dx.at[zz], self.xn))
        if self.cut < self.rows:
            copies.append(remote(self.w.at[zz, 3, pl.ds(self.cut, self.rows - self.cut)],
                                 self.ryd.at[zz], self.s_dy.at[zz], self.r_dy.at[zz], self.yn))
        return copies

    def sides(self, zz):
        return (remote(self.w.at[zz, 1], self.rx.at[zz], self.s_x.at[zz], self.r_x.at[zz], self.xn),
                remote(self.w.at[zz, 2], self.ry.at[zz], self.s_y.at[zz], self.r_y.at[zz], self.yn))

    def line(self, zz, slot, where):
        return remote(self.w.at[zz, 0], self.rz.at[slot], self.s_z.at[zz], self.r_z.at[slot], where)

    def start(self):
        def step(k, carry):
            zz = far_first(self.nz, self.place[0], k)
            for rel in (3, 1, 2, 0):
                self.pair(zz, rel).start()
                self.load(zz, rel).start()
            return carry

        lax.fori_loop(0, self.nz, step, 0)

    def first(self, k):
        zz = far_first(self.nz, self.place[0], k)
        for rel in (3, 1, 2, 0):
            self.pair(zz, rel).wait_recv()
            self.load(zz, rel).wait()
            add_blocks(self.w.at[zz, rel], [self.lp.at[zz, rel]], 0, self.rows)
            if rel == 3:
                for copy in self.across(zz):
                    copy.start()

    def second(self, k):
        zz = far_first(self.nz, self.place[0], k)
        across, (to_x, to_y) = self.across(zz), self.sides(zz)
        if self.cut < self.rows:
            across[-1].wait_recv()
            add_blocks(self.w.at[zz, 1], [self.ryd.at[zz]], self.cut, self.rows - self.cut)
        to_x.start()
        if self.cut > 0:
            across[0].wait_recv()
            add_blocks(self.w.at[zz, 2], [self.rxd.at[zz]], 0, self.cut)
        to_y.start()

    def send_line(self, zz):
        z = self.place[0]
        pl.when(zz > z)(lambda: self.line(zz, zz, self.up).start())
        pl.when(zz == z - 1)(lambda: self.line(zz, self.nz, self.down).start())
        pl.when(zz < z - 1)(lambda: self.line(zz, zz, self.down).start())

    def passes(self, zz):
        z = self.place[0]
        return ((zz > z) & (z > 0)) | ((zz < z) & (z < self.nz - 1))

    def third(self, k):
        zz, z = far_first(self.nz, self.place[0], k), self.place[0]
        to_x, to_y = self.sides(zz)
        to_x.wait_recv()
        to_y.wait_recv()
        add_blocks(self.w.at[zz, 0], [self.rx.at[zz], self.ry.at[zz]], 0, self.rows)
        pl.when((zz != z) & jnp.logical_not(self.passes(zz)))(lambda: self.send_line(zz))

    def fourth(self, k):
        zz, z, nz = far_first(self.nz, self.place[0], k), self.place[0], self.nz

        @pl.when((zz != z) & self.passes(zz))
        def _():
            self.line(zz, zz, self.up).wait_recv()
            add_blocks(self.w.at[zz, 0], [self.rz.at[zz]], 0, self.rows)
            self.send_line(zz)

        @pl.when(zz == z)
        def _():
            finish_line(self, self.w.at[zz, 0], zz)

    def finish(self):
        z = self.place[0]

        def step(zz, carry):
            for rel in range(4):
                self.pair(zz, rel).wait_send()
            for copy in tuple(self.across(zz)) + tuple(self.sides(zz)):
                copy.wait_send()
            pl.when(zz != z)(lambda: self.line(zz, zz, self.up).wait_send())
            return carry

        lax.fori_loop(0, self.nz, step, 0)


def finish_line(self, own, zz):
    z, nz = self.place[0], self.nz
    below, above = self.rz.at[zz], self.rz.at[nz]
    pl.when(z > 0)(lambda: self.line(zz, zz, self.up).wait_recv())
    pl.when(z < nz - 1)(lambda: self.line(zz, nz, self.down).wait_recv())
    pl.when(z == 0)(lambda: add_blocks(own, [above], 0, self.rows, self.out))
    pl.when(z == nz - 1)(lambda: add_blocks(own, [below], 0, self.rows, self.out))
    pl.when((z > 0) & (z < nz - 1))(lambda: add_blocks(own, [below, above], 0, self.rows, self.out))


class ReduceRows:
    @staticmethod
    def scratch(nz, rows, cols, kind):
        vm, dma = pltpu.VMEM, pltpu.SemaphoreType.DMA
        return [vm((nz, rows, cols), kind), vm((nz, rows, cols), kind), vm((nz, rows, cols), kind),
                vm((nz + 1, rows, cols), kind)] + [dma((nz,))] * 3 + [dma((nz + 1,))]

    def __init__(self, nz, left, right, out, refs, part=0, parts=1):
        self.w, self.sent, self.rx, self.rz, self.s_x, self.s_z, self.r_x, self.r_z = refs
        self.nz, self.left, self.right, self.out = nz, left, right, out
        self.rows = out.shape[0]
        self.offset, self.stride = part * self.rows, parts * self.rows
        self.place = z, x, y, c = place()
        self.xn = device(z, 1 - x, y, c)
        self.up, self.down = device(z + 1, x, y, c), device(z - 1, x, y, c)

    def make(self, zz, xx, ref):
        start = (zz * 2 + xx) * self.stride + self.offset
        at = pl.ds(pl.multiple_of(start, self.rows), self.rows)
        ref[...] = dot_first(self.left[:, at], self.right[...]).astype(ref.dtype)

    def side(self, zz):
        return remote(self.sent.at[zz], self.rx.at[zz], self.s_x.at[zz], self.r_x.at[zz], self.xn)

    def line(self, zz, slot, where):
        return remote(self.w.at[zz], self.rz.at[slot], self.s_z.at[zz], self.r_z.at[slot], where)

    def start(self):
        def step(k, carry):
            self.send(k)
            return carry

        lax.fori_loop(0, self.nz, step, 0)

    def send(self, k):
        zz, x = far_first(self.nz, self.place[0], k), self.place[1]
        self.make(zz, 1 - x, self.sent.at[zz])
        self.side(zz).start()
        self.make(zz, x, self.w.at[zz])

    send_line = ScatterAll.send_line
    passes = ScatterAll.passes

    def first(self, k):
        zz, z = far_first(self.nz, self.place[0], k), self.place[0]
        self.side(zz).wait_recv()
        add_blocks(self.w.at[zz], [self.rx.at[zz]], 0, self.rows)
        pl.when((zz != z) & jnp.logical_not(self.passes(zz)))(lambda: self.send_line(zz))

    def second(self, k):
        zz, z, nz = far_first(self.nz, self.place[0], k), self.place[0], self.nz

        @pl.when((zz != z) & self.passes(zz))
        def _():
            self.line(zz, zz, self.up).wait_recv()
            add_blocks(self.w.at[zz], [self.rz.at[zz]], 0, self.rows)
            self.send_line(zz)

        @pl.when(zz == z)
        def _():
            finish_line(self, self.w.at[zz], zz)

    def finish(self):
        z = self.place[0]

        def step(zz, carry):
            self.side(zz).wait_send()
            pl.when(zz != z)(lambda: self.line(zz, zz, self.up).wait_send())
            return carry

        lax.fori_loop(0, self.nz, step, 0)


class ReduceCausal:
    @staticmethod
    def scratch(nz, rows, cols, kind):
        vm, dma = pltpu.VMEM, pltpu.SemaphoreType.DMA
        return [vm((nz, 2, 2, rows, cols), kind), vm((2, rows, cols), kind),
                dma((2 * nz,)), dma((2 * nz,)), dma((2,)), dma((2,))]

    def __init__(self, nz, sides, out, refs):
        self.got, self.across, self.s_z, self.r_z, self.s_x, self.r_x = refs
        self.nz, self.sides, self.out = nz, sides, out
        self.place = z, x, y, c = place()
        self.xn = device(z, 1 - x, y, c)
        self.to = (device(z - 1, x, y, c), device(z + 1, x, y, c))

    def line(self, zz, micro):
        k = zz * 2 + micro
        return remote(self.sides.at[zz, :, micro], self.got.at[zz, :, micro],
                      self.s_z.at[k], self.r_z.at[k], self.to[micro])

    def side(self, micro):
        z, x = self.place[:2]
        return remote(self.sides.at[z, 1 - x, micro], self.across.at[micro],
                      self.s_x.at[micro], self.r_x.at[micro], self.xn)

    def take(self, zz, micro):
        first = self.place[0] == (self.nz - 1 if micro == 0 else 0)

        @pl.when(jnp.logical_not(first))
        def _():
            self.line(zz, micro).wait_recv()
            for xx in range(2):
                add_blocks(self.sides.at[zz, xx, micro], [self.got.at[zz, xx, micro]], 0,
                           self.sides.shape[3])

    def turn(self, hop):
        z, nz = self.place[0], self.nz
        for micro in range(2):
            @pl.when(hop == (nz - 1 - z if micro == 0 else z))
            def _():
                def step(n, carry):
                    zz = n if micro == 0 else nz - 1 - n
                    self.take(zz, micro)
                    self.line(zz, micro).start()
                    return carry

                lax.fori_loop(0, z if micro == 0 else nz - 1 - z, step, 0)
                self.take(z, micro)
                self.side(micro).start()

    def finish(self):
        z, x = self.place[:2]
        for micro in range(2):
            self.side(micro).wait_recv()
            add_blocks(self.sides.at[z, x, micro], [self.across.at[micro]], 0, self.sides.shape[3],
                       self.out.at[micro])
        for micro in range(2):
            self.side(micro).wait_send()

            def step(n, carry):
                self.line(n if micro == 0 else self.nz - 1 - n, micro).wait_send()
                return carry

            lax.fori_loop(0, z if micro == 0 else self.nz - 1 - z, step, 0)


def norm_turn_back(turned, raw, gain, cosine, sine):
    grad = turned * cosine + pltpu.roll(turned * sine, raw.shape[1] // 2, 1)
    scale = lax.rsqrt(jnp.mean(raw * raw, axis=1, keepdims=True) + norm_eps)
    inner = grad * gain
    mean = jnp.mean(raw * inner, axis=1, keepdims=True)
    return (scale * inner - raw * (scale * scale * scale * mean),
            jnp.sum(grad * raw * scale, axis=0, keepdims=True))


def attend_back_kernel(nz, k_pre, gk_ref, gq_ref, cos_ref, sin_ref, start_ref, lse_ref, scale_ref,
                       gates_ref, gg_ref, router_ref, gain_ref, moe_ref,
                       middle_all, back_all, slice_all, wo_all, heads_all, q_all, kv_all, pre_all,
                       out_part, mid_out, q_grad, gain_grad, out_sum, wo_sum, small_out,
                       low_ref, mid_ref, wo_ref, heads_ref, q_ref, kv_ref,
                       small_ref, split_ref, grad_ref, delta_ref, q_pre, s_in, s_t, r_t,
                       kv_sum, sides, acc, k_acc, v_acc, *refs):
    middle_ref, inner_ref = (q_pre.at[:, pl.ds(n * mid_out.shape[1], mid_out.shape[1])]
                             for n in range(2))
    shards = 2 * nz
    shard = lax.axis_index("fsdp")
    width = kv_ref.shape[4] // 2
    block = q_ref.shape[0] // 2
    heads = q_ref.shape[1] // width
    z, x, y, c = place()
    count = shards + 2 * x
    low = jnp.bfloat16
    n_o, n_w = len(ScatterAll.scratch(nz, 16, 128, low, 0)), len(ReduceRows.scratch(nz, 16, 128, low))
    end = 2 * (n_o + n_w)
    outs = [ScatterAll(nz, out_part, half, refs[n * n_o : (n + 1) * n_o], 0, n, 2)
            for n, half in enumerate(halves(out_sum))]
    weights = [ReduceRows(nz, mid_ref, heads_ref, half,
                          refs[2 * n_o + n * n_w : 2 * n_o + (n + 1) * n_w], n, 2)
               for n, half in enumerate(halves(wo_sum))]
    last = end + len(SmallSums.scratch(nz, (8, 128), jnp.float32))
    smalls = SmallSums(nz, small_ref, small_out, refs[end:last])
    final = last + len(ReduceCausal.scratch(nz, 16, 128, low))
    keys_out = ReduceCausal(nz, sides, kv_sum, refs[last:final])
    sums = RowSums(refs[final:])
    greet_all(lax.axis_index("fsdp"), lax.axis_index("tp"), shards, 4)
    for part in outs:
        part.start()
    fetches = [pltpu.make_async_copy(src, dst, s_in.at[n]) for n, (src, dst) in enumerate((
        (middle_all, middle_ref), (back_all, inner_ref), (slice_all, mid_out),
        (wo_all.at[:, pl.ds(0, wo_ref.shape[1])], wo_ref),
        (heads_all, heads_ref), (q_all, q_ref), (kv_all, kv_ref), (pre_all, q_pre)))]
    for copy in fetches[:-1]:
        copy.start()

    sides[...] = jnp.zeros_like(sides)
    acc[...] = jnp.zeros_like(acc)

    def attention(u):
        micro, here, key_place, owner = stream_unit(u, nz)
        bias = key_bias(micro, here, key_place, block, start_ref)
        both = kv_ref.at[owner // 2, owner % 2, micro]
        keys, values = both[:, :width], both[:, width:]
        q_rows = pl.ds(pl.multiple_of(micro * block, block), block)
        k_acc[...] = jnp.zeros_like(k_acc)
        v_acc[...] = jnp.zeros_like(v_acc)

        def head(h, carry):
            at = micro * heads + h
            cols = pl.ds(pl.multiple_of(h * width, width), width)
            query, grad = q_ref[q_rows, cols], grad_ref[q_rows, cols]
            scores = dot_last(keys, query) * width ** (-0.5) + bias
            probs = jnp.exp(scores - lse_ref[at])
            score_grad = (probs * (dot_last(values, grad) - delta_ref[at])).astype(low)
            v_acc[...] += dot_plain(probs.astype(low), grad)
            k_acc[...] += dot_plain(score_grad, query)
            acc[at] += dot_first(keys, score_grad)
            return carry

        lax.fori_loop(0, heads, head, 0, unroll=2)
        side = sides.at[owner // 2, owner % 2, micro]
        side[:, :width] = (k_acc[...] * width ** (-0.5)).astype(low)
        side[:, width:] = v_acc[...].astype(low)

    def close(at, total):
        micro, h = at // heads, at % heads
        here = pl.ds(pl.multiple_of(micro * block, block), block)
        cols = pl.ds(pl.multiple_of(h * width, width), width)
        grad, gain = norm_turn_back(acc[at].T * width ** (-0.5), q_pre[here, cols], gq_ref[...],
                                    cos_ref[here, :], sin_ref[here, :])
        q_grad[here, cols] = grad.astype(low)
        return total + gain

    def close_all():
        gain_grad[pl.ds(0, 1), :] = lax.fori_loop(
            0, 2 * heads, close, jnp.zeros((1, width), jnp.float32)
        )

    def unit(u, carry):
        def at(fn, k):
            pl.when((k >= 0) & (k < nz))(lambda: fn(k))

        def each(parts, name, k):
            for part in parts:
                at(getattr(part, name), k)

        for n in range(4):
            pl.when(4 * u + n < count)(lambda: attention(4 * u + n))
        each(outs, 'second', u + 1)
        each(weights, 'send', u + 2)
        each(outs, 'first', u + 3)
        pl.when(u == 1)(smalls.second)
        at(keys_out.turn, u - done)
        each(outs, 'third', u)
        each(outs, 'fourth', u - 1)
        each(weights, 'second', u - 2)
        each(weights, 'first', u - 1)
        pl.when(u == done + 1)(close_all)
        return carry

    rows, cols = mid_out.shape
    eye = diagonal()

    def column(yy):
        return mid_ref.at[:, pl.ds(pl.multiple_of((yy * 2 + c) * cols, cols), cols)]

    partner, yn = outs[0].partner, outs[0].yn
    to_y = remote(low_ref, column(y), s_t.at[0], r_t.at[0], yn)
    to_pair = remote(low_ref, column(y), s_t.at[1], r_t.at[1], partner)
    onward = remote(column(1 - y), column(1 - y), s_t.at[2], r_t.at[2], partner)

    def dots(n, carry):
        here = pl.ds(pl.multiple_of(n * 128, 128), 128)
        product = middle_ref[here, :] * inner_ref[here, :]
        sums.got[0, pl.ds(n, 1), :] = to_row(jnp.sum(product, axis=1, keepdims=True), eye)
        return carry

    def residual(n, carry):
        here = pl.ds(pl.multiple_of(n * 128, 128), 128)
        mean = to_column(sums.total(n), eye) / (4 * cols)
        scale = scale_ref[here, :]
        out = (mid_out[here, :] + scale * inner_ref[here, :]
               - middle_ref[here, :] * (scale * scale * scale * mean))
        mid_out[here, :] = out
        low_ref[here, :] = out.astype(low)
        return carry

    def head_grads(part):
        def step(n, carry):
            at = pl.ds(pl.multiple_of(n * 256, 256), 256)
            to = pl.ds(pl.multiple_of(part * wo_ref.shape[1] + n * 256, 256), 256)
            grad_ref[:, to] = dot_plain(mid_ref[...], wo_ref[:, at]).astype(low)
            return carry

        lax.fori_loop(0, wo_ref.shape[1] // 256, step, 0)

    def deltas(at, carry):
        here = pl.ds(pl.multiple_of(at // heads * block, block), block)
        head = pl.ds(pl.multiple_of(at % heads * width, width), width)
        product = grad_ref[here, head].astype(jnp.float32) * heads_ref[here, head].astype(jnp.float32)
        delta_ref[at] = jnp.sum(product.T, axis=0, keepdims=True)
        return carry

    done = (shards + 2 - 1) // 4
    def each_now(parts, name, k):
        for part in parts:
            getattr(part, name)(k)

    gates = gates_ref[...]
    gates_grad = gg_ref[:, 0, :].T
    logit_grad = gates * (gates_grad - jnp.sum(gates * gates_grad, axis=1, keepdims=True))
    each_now(outs, 'first', 0)
    pieces, rest = [], logit_grad
    for _ in range(3):
        pieces.append(rest.astype(low))
        rest = rest - pieces[-1].astype(jnp.float32)
    router_grad = sum(dot_first(piece, moe_ref[...]) for piece in pieces)
    small_ref[...] = jnp.zeros_like(small_ref)
    blocks = cols // 128
    per = router_grad.shape[0] // shards
    for e in range(router_grad.shape[0]):
        for n in range(blocks):
            small_ref[e // per, pl.ds(e % per * blocks + n, 1), :] = (
                router_grad[e : e + 1, n * 128 : (n + 1) * 128])
    for copy in fetches[:3]:
        copy.wait()

    def moe_grads(n, total):
        here = pl.ds(pl.multiple_of(n * 128, 128), 128)
        grad = inner_ref[here, :]
        for piece in pieces_ref:
            grad = grad + dot_last(piece[here, :], router_ref[...])
        inner_ref[here, :] = grad * gain_ref[...]
        return total + jnp.sum(grad * middle_ref[here, :] * scale_ref[here, :], axis=0, keepdims=True)

    pieces_ref = [split_ref.at[n] for n in range(3)]
    for ref, piece in zip(pieces_ref, pieces):
        ref[...] = piece
    gain_total = lax.fori_loop(0, rows // 128, moe_grads, jnp.zeros((1, cols), jnp.float32))
    for n in range(blocks):
        small_ref[0, pl.ds(per * blocks + n, 1), :] = gain_total[:, n * 128 : (n + 1) * 128]
    smalls.start()
    lax.fori_loop(0, rows // 128, dots, 0)
    sums.start()
    sums.wait()
    lax.fori_loop(0, rows // 128, residual, 0)
    fetches[-1].start()
    to_y.start()
    to_pair.start()
    mid_ref[:, pl.ds(pl.multiple_of((y * 2 + c) * cols, cols), cols)] = low_ref[...]
    each_now(outs, 'first', 1)
    to_y.wait_recv()
    onward.start()
    each_now(outs, 'second', 0)
    for copy in fetches[3:]:
        copy.wait()
    to_pair.wait()
    onward.wait()
    to_y.wait_send()
    for k in range(2):
        each_now(weights, 'send', k)
    each_now(outs, 'first', 2)
    head_grads(0)
    more = pltpu.make_async_copy(wo_all.at[:, pl.ds(wo_ref.shape[1], wo_ref.shape[1])], wo_ref,
                                 s_in.at[3])
    more.start()
    more.wait()
    head_grads(1)
    lax.fori_loop(0, 2 * heads, deltas, 0)
    lax.fori_loop(0, nz + 2, unit, 0)
    keys_out.finish()
    total = jnp.zeros((1, width), jnp.float32)
    for micro in range(2):
        here = slice(micro * block, (micro + 1) * block)
        grad, gain = norm_turn_back(kv_sum[micro, :, :width], k_pre[here, :], gk_ref[...],
                                    cos_ref[here, :], sin_ref[here, :])
        q_grad[here, heads * width : (heads + 1) * width] = grad.astype(low)
        q_grad[here, (heads + 1) * width :] = kv_sum[micro, :, width:].astype(low)
        total = total + gain
    gain_grad[pl.ds(1, 1), :] = total
    for part in outs + weights:
        part.finish()
    smalls.finish()


def attend_back(query, q_pre, k_pre, gain_key, gain_query, cosine, sine, keys_values, starts, log_total,
                gates, gates_grad, router, gain, moe_low, middle, scale, back, grad_slice, w_out, heads_low, out_part, nz, collective_id):
    rows, columns = query.shape
    width = keys_values.shape[4] // 2
    heads = columns // width
    block = rows // 2
    cols = out_part.shape[1] // 4
    wo_shape = (w_out.shape[0] // (2 * nz), columns)
    experts = gates.shape[1]
    part_rows = -(-(experts // (2 * nz) + 1) * cols // 1024) * 8
    small = (2 * nz, part_rows, 128)
    any_space = pl.BlockSpec(memory_space=pl.ANY)
    vmem = pl.BlockSpec(memory_space=pltpu.VMEM)
    vm, shape, f32, low = pltpu.VMEM, jax.ShapeDtypeStruct, jnp.float32, jnp.bfloat16
    dma = pltpu.SemaphoreType.DMA
    return pl.pallas_call(
        functools.partial(attend_back_kernel, nz),
        in_specs=[vmem] * 13 + [any_space] * 9,
        out_specs=[vmem] * 6,
        out_shape=[
            shape((rows, cols), f32),
            shape((rows, columns + 2 * width), low), shape((2, width), f32),
            shape((rows, cols), f32), shape(wo_shape, f32),
            shape((8 * nz,) + small[1:], f32),
        ],
        scratch_shapes=[
            vm((rows, cols), low),
            vm((rows, 4 * cols), low), vm((w_out.shape[0], columns // 2), low), vm((rows, columns), low),
            vm((rows, columns), low), vm((nz, 2, 2, block, 2 * width), low),
            vm(small, f32), vm((3, rows, experts), low), vm((rows, columns), low),
            vm((2 * heads, 1, block), f32), vm((rows, columns), f32), dma((8,)), dma((3,)), dma((3,)),
            vm((2, block, 2 * width), f32), vm((nz, 2, 2, block, 2 * width), low),
            vm((2 * heads, width, block), f32), vm((block, width), f32), vm((block, width), f32),
        ] + ScatterAll.scratch(nz, rows // 2, cols, low, 0) * 2
        + ReduceRows.scratch(nz, wo_shape[0] // 2, wo_shape[1], low) * 2
        + SmallSums.scratch(nz, small[1:], f32)
        + ReduceCausal.scratch(nz, block, 2 * width, low) + RowSums.scratch(rows),
        compiler_params=pltpu.CompilerParams(
            collective_id=collective_id, has_side_effects=True, vmem_limit_bytes=62 << 20
        ),
        name="attend_back",
    )(k_pre, gain_key, gain_query, cosine, sine, starts, log_total, scale, gates, gates_grad, router,
      gain, moe_low, middle, back, grad_slice, w_out,
      heads_low, query, keys_values, q_pre, out_part)


def to_row(column, eye):
    return jnp.sum(jnp.where(eye, column, 0.0), axis=0, keepdims=True)


def to_column(row, eye):
    return jnp.sum(jnp.where(eye, row, 0.0), axis=1, keepdims=True)


def diagonal():
    shape = (128, 128)
    return lax.broadcasted_iota(jnp.int32, shape, 0) == lax.broadcasted_iota(jnp.int32, shape, 1)


class RowSums:
    @staticmethod
    def scratch(rows):
        dma = pltpu.SemaphoreType.DMA
        return [pltpu.VMEM((4, rows // 128, 128), jnp.float32), dma((3,)), dma((3,))]

    def __init__(self, refs):
        self.got, s, r = refs
        shard, group = lax.axis_index("fsdp"), lax.axis_index("tp")
        self.peers = [(shard, (group + k) % 4) for k in range(1, 4)]
        self.copies = [
            remote(self.got.at[0], self.got.at[k + 1], s.at[k], r.at[k], peer)
            for k, peer in enumerate(self.peers)
        ]

    def start(self):
        for copy in self.copies:
            copy.start()

    def wait(self):
        for copy in self.copies:
            copy.wait()

    def total(self, n):
        return self.got[0, pl.ds(n, 1), :] + self.got[1, pl.ds(n, 1), :] + (
            self.got[2, pl.ds(n, 1), :] + self.got[3, pl.ds(n, 1), :])


class ReduceCols:
    @staticmethod
    def scratch(rows, cols, kind):
        vm, dma = pltpu.VMEM, pltpu.SemaphoreType.DMA
        return [vm((2, rows, cols), kind), vm((2, rows, cols), kind), vm((rows, cols), kind),
                dma((2,)), dma((2,)), dma((2,)), dma, dma]

    def __init__(self, partial, out, refs):
        self.w, self.rp, self.ry, s_l, s_p, r_p, s_y, r_y = refs
        self.out = out
        self.rows, cols = out.shape
        z, x, y, c = place()
        self.partner, self.yn = device(z, x, y, 1 - c), device(z, x, 1 - y, c)

        def block(yy, cc):
            return partial.at[:, pl.ds(pl.multiple_of((yy * 2 + cc) * cols, cols), cols)]

        self.sends = [remote(block(yy, 1 - c), self.rp.at[k], s_p.at[k], r_p.at[k], self.partner)
                      for k, yy in enumerate((1 - y, y))]
        self.loads = [pltpu.make_async_copy(block(yy, c), self.w.at[k], s_l.at[k])
                      for k, yy in enumerate((1 - y, y))]
        self.across = remote(self.w.at[0], self.ry, s_y, r_y, self.yn)

    def start(self):
        for k in range(2):
            self.sends[k].start()
            self.loads[k].start()

    def first(self):
        self.loads[0].wait()
        self.sends[0].wait_recv()
        add_blocks(self.w.at[0], [self.rp.at[0]], 0, self.rows)
        self.across.start()

    def second(self):
        self.loads[1].wait()
        self.sends[1].wait_recv()
        self.across.wait_recv()
        add_blocks(self.w.at[1], [self.rp.at[1], self.ry], 0, self.rows, self.out)

    def finish(self):
        for send in self.sends:
            send.wait_send()
        self.across.wait_send()


class SmallSums:
    @staticmethod
    def scratch(nz, part, kind):
        dma = pltpu.SemaphoreType.DMA
        return [pltpu.VMEM((2 * nz,) + part, kind), dma((2 * nz,)), dma((2 * nz,)),
                dma((8 * nz,)), dma((8 * nz,))]

    def __init__(self, nz, values, out, refs):
        self.got, self.s_1, self.r_1, self.s_2, self.r_2 = refs
        self.values, self.out = values, out
        self.shards, self.devices = 2 * nz, 8 * nz
        self.shard, self.group = lax.axis_index("fsdp"), lax.axis_index("tp")
        self.me = self.shard * 4 + self.group

    def share(self, k):
        other = (self.shard + k) % self.shards
        return remote(self.values.at[other], self.got.at[k], self.s_1.at[k], self.r_1.at[k],
                      (other, self.group))

    def spread(self, k):
        other = (self.me + k) % self.devices
        return remote(self.out.at[self.me], self.out.at[self.me], self.s_2.at[k], self.r_2.at[k],
                      (other // 4, other % 4))

    def start(self):
        loop_from_one(self.shards, lambda k: self.share(k).start())

    def second(self):
        loop_from_one(self.shards, lambda k: self.share(k).wait())
        acc = self.values[self.shard]
        for k in range(1, self.shards):
            acc = acc + self.got[k]
        self.out[self.me] = acc
        loop_from_one(self.devices, lambda k: self.spread(k).start())

    def finish(self):
        loop_from_one(self.devices, lambda k: self.spread(k).wait())


def loop_from_one(count, fn):
    def step(k, carry):
        fn(k)
        return carry

    lax.fori_loop(1, count, step, 0)


def tail_kernel(nz, tok_ref, scale_ref, gain_ref, block_ref, small_ref, left_all, right_all, mid_all,
                wq_all, wk_all, wv_all, gp_all, up_all, hid_all, xr_all, gs_all,
                wq_out, wk_out, wv_out, token_out, block_out, gain_out, head_out, dwg, dwu, dwd,
                left_ref, right_ref, mid_ref, wq, wk, wv, part_ref, s_m, w_sum, gp_ref, up_ref, hid_ref, x_panel, g_panel, o_gate, o_up, o_down, s_in, s_out,
                small_out, normed, token, s_w, r_w, s_l, s_g, r_g, *refs):
    z, x, y, c = place()
    shard, group = lax.axis_index("fsdp"), lax.axis_index("tp")
    shards = 2 * nz
    devices = 4 * shards
    me = shard * 4 + group
    rows, cols = tok_ref.shape
    width = cols * 4
    half = rows // 2
    panel = x_panel.shape[1]
    panels = xr_all.shape[1] // panel
    f32, low = jnp.float32, jnp.bfloat16
    n_w, n_c = len(ReduceRows.scratch(nz, 16, 128, low)), len(ReduceCols.scratch(16, 128, low))
    weights = [ReduceRows(nz, left_ref, right_ref, half, refs[n * n_w : (n + 1) * n_w], n, 2)
               for n, half in enumerate(halves(w_sum))]
    columns = ReduceCols(part_ref, normed, refs[2 * n_w : 2 * n_w + n_c])
    sums = RowSums(refs[2 * n_w + n_c :])
    mirror = device(nz - 1 - z, x, y, c)
    greet_all(shard, group, shards, 4)
    fetches = [pltpu.make_async_copy(src, dst, s_m.at[n]) for n, (src, dst) in enumerate((
        (left_all, left_ref), (right_all, right_ref), (wq_all, wq), (wk_all, wk), (wv_all, wv),
        (mid_all, mid_ref)))]
    for copy in fetches:
        copy.start()
    for copy in fetches[:2]:
        copy.wait()
    for part in weights:
        part.send(0)
    for copy in fetches[2:]:
        copy.wait()
    first, second = wq_out.shape[1], wq_out.shape[1] + wk_out.shape[1]

    def normed_parts(n, carry):
        at = pl.ds(pl.multiple_of(n * cols, cols), cols)
        part_ref[:, at] = (
            dot_last(right_ref[:, :first], wq[at, :])
            + dot_last(right_ref[:, first:second], wk[at, :])
            + dot_last(right_ref[:, second:], wv[at, :])
        ).astype(low)
        return carry

    lax.fori_loop(0, 4, normed_parts, 0)
    columns.start()
    for k in range(1, nz):
        for part in weights:
            part.send(k)
    top, bottom = pl.ds(0, half), pl.ds(half, half)
    swaps = [remote(src.at[bottom], dst.at[bottom], s_w.at[n], r_w.at[n], mirror)
             for n, (src, dst) in enumerate(((token, token_out), (block_ref, block_out)))]
    keeps = [pltpu.make_async_copy(src.at[top], dst.at[top], s_l.at[n])
             for n, (src, dst) in enumerate(((token, token_out), (block_ref, block_out)))]
    swaps[1].start()
    keeps[1].start()

    def loads(n):
        at = pl.ds(pl.multiple_of(n * panel, panel), panel)
        return (pltpu.make_async_copy(xr_all.at[:, at], x_panel, s_in.at[0]),
                pltpu.make_async_copy(gs_all.at[:, at], g_panel, s_in.at[1]))

    def stores(n):
        at = pl.ds(pl.multiple_of(n * panel, panel), panel)
        return (pltpu.make_async_copy(o_gate, dwg.at[at, :], s_out.at[0]),
                pltpu.make_async_copy(o_up, dwu.at[at, :], s_out.at[1]),
                pltpu.make_async_copy(o_down, dwd.at[:, at], s_out.at[2]))

    whole = [pltpu.make_async_copy(src, dst, s_in.at[2 + n])
             for n, (src, dst) in enumerate(((gp_all, gp_ref), (up_all, up_ref), (hid_all, hid_ref)))]
    for copy in tuple(whole) + loads(0):
        copy.start()
    small_out[me] = small_ref[...]

    def expert_weights(n):
        @pl.when(n == 0)
        def _():
            for copy in whole:
                copy.wait()

        for copy in loads(n):
            copy.wait()

        @pl.when(n > 0)
        def _():
            for copy in stores(n):
                copy.wait()

        o_gate[...] = dot_first(x_panel[...], gp_ref[...])
        o_up[...] = dot_first(x_panel[...], up_ref[...])
        o_down[...] = dot_first(g_panel[...], hid_ref[...]).T
        for copy in stores(n):
            copy.start()

        @pl.when(n < panels - 1)
        def _():
            for copy in loads(n + 1):
                copy.start()

    def token_sums():
        eye = diagonal()

        def step(n, gains):
            here = pl.ds(pl.multiple_of(n * 128, 128), 128)
            tok, grad = tok_ref[here, :].astype(f32), normed[here, :]
            product = tok * (grad * gain_ref[...])
            sums.got[0, pl.ds(n, 1), :] = to_row(jnp.sum(product, axis=1, keepdims=True), eye)
            return gains + jnp.sum(grad * tok * scale_ref[here, :], axis=0, keepdims=True)

        gains = lax.fori_loop(0, rows // 128, step, jnp.zeros((1, cols), f32))
        for n in range(cols // 128):
            small_out[me, pl.ds(n, 1), :] = gains[:, n * 128 : (n + 1) * 128]

    def token_grads():
        eye = diagonal()

        def step(n, carry):
            here = pl.ds(pl.multiple_of(n * 128, 128), 128)
            mean = to_column(sums.total(n), eye) / width
            scale = scale_ref[here, :]
            token[here, :] = (
                mid_ref[here, :]
                + scale * (gain_ref[...] * normed[here, :])
                - tok_ref[here, :].astype(f32) * (scale * scale * scale * mean)
            ).astype(low)
            return carry

        lax.fori_loop(0, rows // 128, step, 0)

    def spread(k):
        other = (me + k) % devices
        return remote(small_out.at[me], small_out.at[me], s_g.at[k], r_g.at[k],
                      (other // 4, other % 4))

    columns.first()

    def unit(u, carry):
        @pl.when(u == 1)
        def _():
            sums.wait()
            token_grads()
            swaps[0].start()
            keeps[0].start()

        @pl.when((u >= 1) & (u <= nz))
        def _():
            for part in weights:
                part.second(u - 1)

        @pl.when(u < panels // 2)
        def _():
            expert_weights(2 * u)
            expert_weights(2 * u + 1)

        @pl.when(u == 0)
        def _():
            columns.second()
            token_sums()
            sums.start()
            loop_from_one(devices, lambda k: spread(k).start())

        @pl.when(u < nz)
        def _():
            for part in weights:
                part.first(u)

        return carry

    lax.fori_loop(0, max(nz + 1, panels // 2), unit, 0)
    loop_from_one(devices, lambda k: spread(k).wait())
    gain_rows = cols // 128
    for g in range(4):
        rows_of = small_out[g, pl.ds(0, gain_rows), :]
        for f in range(1, shards):
            rows_of = rows_of + small_out[f * 4 + g, pl.ds(0, gain_rows), :]
        gain_out[g] = rows_of
    total = small_out[0, pl.ds(gain_rows, 2), :]
    for d in range(1, devices):
        total = total + small_out[d, pl.ds(gain_rows, 2), :]
    head_out[...] = total
    for copy in swaps + keeps:
        copy.wait()
    for copy in stores(panels - 1):
        copy.wait()
    wq_out[...] = w_sum[:, :first]
    wk_out[...] = w_sum[:, first:second]
    wv_out[...] = w_sum[:, second:]
    columns.finish()
    for part in weights:
        part.finish()


def tail(gate_grad, up_grad, hidden, tokens, middle_grad, scale, gain, block_out, small, normed_low,
         pre_grad, wq_all, wk_all, wv_all, rows_in, pair_grad, nz, collective_id):
    rows, cols = tokens.shape
    pairs, features = rows_in.shape
    hidden_width = hidden.shape[1]
    panel = 256
    w_shape = (normed_low.shape[1] // (2 * nz), pre_grad.shape[1])
    query_width, kv_width = wq_all.shape[1], wk_all.shape[1]
    devices = 8 * nz
    any_space = pl.BlockSpec(memory_space=pl.ANY)
    vmem = pl.BlockSpec(memory_space=pltpu.VMEM)
    vm, shape, f32, low = pltpu.VMEM, jax.ShapeDtypeStruct, jnp.float32, jnp.bfloat16
    dma = pltpu.SemaphoreType.DMA
    return pl.pallas_call(
        functools.partial(tail_kernel, nz),
        in_specs=[vmem] * 5 + [any_space] * 11,
        out_specs=[vmem] * 3 + [any_space, any_space, vmem, vmem] + [any_space] * 3,
        out_shape=[
            shape((w_shape[0], query_width), f32), shape((w_shape[0], kv_width), f32),
            shape((w_shape[0], kv_width), f32), shape((rows, cols), low), shape((rows, cols), low),
            shape((4, cols // 128, 128), f32), shape((2, 128), f32),
            shape((features, hidden_width), f32), shape((features, hidden_width), f32),
            shape((hidden_width, features), f32),
        ],
        scratch_shapes=[vm(normed_low.shape, low), vm(pre_grad.shape, low), vm((rows, cols), f32),
                        vm(wq_all.shape, low), vm(wk_all.shape, low), vm(wv_all.shape, low),
                        vm((rows, 4 * cols), low), dma((6,)), vm(w_shape, f32)] + [vm((pairs, hidden_width), low)] * 3 + [
            vm((pairs, panel), low), vm((pairs, panel), low),
            vm((panel, hidden_width), f32), vm((panel, hidden_width), f32),
            vm((hidden_width, panel), f32), dma((5,)), dma((3,)),
            vm((devices,) + small.shape, f32), vm((rows, cols), f32), vm((rows, cols), low),
            dma((2,)), dma((2,)), dma((2,)), dma((devices,)), dma((devices,)),
        ] + ReduceRows.scratch(nz, w_shape[0] // 2, w_shape[1], low) * 2 + ReduceCols.scratch(rows, cols, low)
        + RowSums.scratch(rows),
        compiler_params=pltpu.CompilerParams(
            collective_id=collective_id, has_side_effects=True, vmem_limit_bytes=62 << 20
        ),
        name="tail",
    )(tokens, scale, gain, block_out, small, normed_low, pre_grad, middle_grad, wq_all, wk_all, wv_all,
      gate_grad, up_grad, hidden, rows_in, pair_grad)


def join_kernel(nz, tok_ref, gain_ref, attn_part, middle_ref, scale_ref, low_ref, all_ref, *refs):
    z, x, y, c = place()
    rows, cols = tok_ref.shape
    f32 = jnp.float32
    n_c, n_s = len(ReduceCols.scratch(16, 128, jnp.bfloat16)), 3
    columns = ReduceCols(attn_part, middle_ref, refs[:n_c])
    sums = RowSums(refs[n_c : n_c + n_s])
    gather = GatherAll(nz, low_ref, all_ref, refs[n_c + n_s :], rows // 2)
    greet([(None, gather.xn), (z < nz - 1, gather.up), (z > 0, gather.down)]
          + [(None, peer) for peer in sums.peers])
    columns.start()
    eye = diagonal()
    columns.first()
    columns.second()

    def add(n, carry):
        here = pl.ds(pl.multiple_of(n * 128, 128), 128)
        total = middle_ref[here, :] + tok_ref[here, :].astype(f32)
        middle_ref[here, :] = total
        sums.got[0, pl.ds(n, 1), :] = to_row(jnp.sum(total * total, axis=1, keepdims=True), eye)
        return carry

    def norm(n, carry):
        here = pl.ds(pl.multiple_of(n * 128, 128), 128)
        scale = lax.rsqrt(to_column(sums.total(n), eye) / (4 * cols) + norm_eps)
        scale_ref[here, :] = scale
        low_ref[here, :] = (middle_ref[here, :] * scale * gain_ref[...]).astype(low_ref.dtype)
        return carry

    lax.fori_loop(0, rows // 128, add, 0)
    sums.start()
    sums.wait()
    lax.fori_loop(0, rows // 128, norm, 0)
    gather.own().start()
    gather.own().wait()

    def tick(k, carry):
        pl.when(k < nz)(lambda: gather.first(k))
        pl.when((k >= 1) & (k <= nz))(lambda: gather.second(k - 1))
        pl.when(k >= 2)(lambda: gather.third(k - 2))
        return carry

    lax.fori_loop(0, nz + 2, tick, 0)
    gather.finish()
    columns.finish()


def join(tokens, gain, attn_part, nz, collective_id):
    rows, cols = tokens.shape
    any_space = pl.BlockSpec(memory_space=pl.ANY)
    vmem = pl.BlockSpec(memory_space=pltpu.VMEM)
    shape, f32, low = jax.ShapeDtypeStruct, jnp.float32, jnp.bfloat16
    return pl.pallas_call(
        functools.partial(join_kernel, nz),
        in_specs=[vmem] * 2 + [any_space],
        out_specs=[vmem] * 3 + [any_space],
        out_shape=[shape((rows, cols), f32), shape((rows, 1), f32), shape((rows, cols), low),
                   shape((rows * 2 * nz, cols * 4), low)],
        scratch_shapes=ReduceCols.scratch(rows, cols, low) + RowSums.scratch(rows)
        + GatherAll.scratch(nz),
        compiler_params=pltpu.CompilerParams(
            collective_id=collective_id, has_side_effects=True, vmem_limit_bytes=62 << 20
        ),
        name="join",
    )(tokens, gain, attn_part)


def turn_kernel(middle_ref, scale_ref, inner_ref, grad_ref, out_ref, all_ref, low_ref, lsem,
                s_p, r_p, s_y, r_y, *refs):
    z, x, y, c = place()
    rows, cols = middle_ref.shape
    sums = RowSums(refs)
    partner, yn = device(z, x, y, 1 - c), device(z, x, 1 - y, c)
    greet([(None, peer) for peer in sums.peers])
    eye = diagonal()

    def block(yy):
        return all_ref.at[:, pl.ds(pl.multiple_of((yy * 2 + c) * cols, cols), cols)]

    def dots(n, carry):
        here = pl.ds(pl.multiple_of(n * 128, 128), 128)
        product = middle_ref[here, :] * inner_ref[here, :]
        sums.got[0, pl.ds(n, 1), :] = to_row(jnp.sum(product, axis=1, keepdims=True), eye)
        return carry

    def grads(n, carry):
        here = pl.ds(pl.multiple_of(n * 128, 128), 128)
        mean = to_column(sums.total(n), eye) / (4 * cols)
        scale = scale_ref[here, :]
        out = (grad_ref[here, :] + scale * inner_ref[here, :]
               - middle_ref[here, :] * (scale * scale * scale * mean))
        out_ref[here, :] = out
        low_ref[here, :] = out.astype(low_ref.dtype)
        return carry

    lax.fori_loop(0, rows // 128, dots, 0)
    sums.start()
    sums.wait()
    lax.fori_loop(0, rows // 128, grads, 0)
    to_y = remote(low_ref, block(y), s_y, r_y, yn)
    to_pair = remote(low_ref, block(y), s_p.at[0], r_p.at[0], partner)
    own = pltpu.make_async_copy(low_ref, block(y), lsem)
    on = remote(block(1 - y), block(1 - y), s_p.at[1], r_p.at[1], partner)
    for copy in (to_y, to_pair, own):
        copy.start()
    to_y.wait_recv()
    on.start()
    to_pair.wait()
    on.wait()
    to_y.wait_send()
    own.wait()


def turn(middle, scale, inner, grad, collective_id):
    rows, cols = middle.shape
    any_space = pl.BlockSpec(memory_space=pl.ANY)
    vmem = pl.BlockSpec(memory_space=pltpu.VMEM)
    shape, f32, low = jax.ShapeDtypeStruct, jnp.float32, jnp.bfloat16
    dma = pltpu.SemaphoreType.DMA
    return pl.pallas_call(
        turn_kernel,
        in_specs=[vmem] * 4,
        out_specs=[vmem, any_space],
        out_shape=[shape((rows, cols), f32), shape((rows, cols * 4), low)],
        scratch_shapes=[pltpu.VMEM((rows, cols), low), dma, dma((2,)), dma((2,)), dma, dma]
        + RowSums.scratch(rows),
        compiler_params=pltpu.CompilerParams(
            collective_id=collective_id, has_side_effects=True, vmem_limit_bytes=62 << 20
        ),
        name="turn",
    )(middle, scale, inner, grad)


def gathered_body(
    tokens,
    cotangent,
    routes,
    doc_ids,
    gain_attn,
    w_query,
    key_weight,
    value_weight,
    w_out,
    gain_query,
    key_norm_gain,
    gain_moe,
    router,
    w_gate,
    w_up,
    w_down,
):
    shard_count = lax.axis_size("fsdp")
    group_count = lax.axis_size("tp")
    shard_index = lax.axis_index("fsdp")
    group_index = lax.axis_index("tp")
    nz = shard_count // 2
    f32, low = jnp.float32, jnp.bfloat16
    row_count, slice_width = tokens.shape
    model_width = slice_width * group_count
    micro_count, micro_rows = doc_ids.shape
    head_width = gain_query.shape[0]
    query_width, kv_width = w_query.shape[1], key_weight.shape[1]
    query_local = query_width // head_width
    kv_local = kv_width // head_width
    group_width = query_local // kv_local
    expert_total = router.shape[1]
    capacity = max(2, 2 * micro_rows * TOPK // expert_total)
    block_keys = micro_rows * math.gcd(shard_count, max(1, 512 // micro_rows))
    my_columns = group_index * slice_width

    mirror_index = mirrored(nz, shard_index)
    owners = jnp.stack([shard_index, mirror_index])

    small = jnp.concatenate([routes.reshape(-1), doc_ids.reshape(-1)])
    small_rows = -(-small.shape[0] // 1024) * 8
    small = jnp.pad(small, (0, small_rows * 128 - small.shape[0])).reshape(small_rows, 128)
    small_all, wq_all, wk_all, wv_all, tokens, full_tokens = gather_rows(
        [small, w_query, key_weight, value_weight], nz, 2, [tokens], 2
    )
    small_all = small_all.reshape(shard_count, small_rows * 128)
    routes_all = small_all[:, : row_count * TOPK].reshape(shard_count * row_count, TOPK)
    ids_all = small_all[:, row_count * TOPK : row_count * (TOPK + 1)].reshape(
        shard_count, micro_count, micro_rows
    )
    doc_range = jnp.arange(DOCS)
    doc_totals = jnp.sum((ids_all[..., None] == doc_range).astype(jnp.int32), axis=(0, 2))
    doc_begin = jnp.cumsum(doc_totals, axis=1) - doc_totals
    query_index = owners[:, None] * micro_rows + jnp.arange(micro_rows)
    my_ids = jnp.stack(
        [lax.dynamic_index_in_dim(ids_all[:, m], owners[m], 0, False) for m in range(micro_count)]
    )
    query_start = jnp.sum(
        jnp.where(my_ids[:, :, None] == doc_range, doc_begin[:, None, :], 0), axis=2
    )
    positions = (query_index - query_start).reshape(row_count)
    cosine_lookup, sine_lookup = rope_tables(positions, head_width)

    turned_sine = jnp.where(jnp.arange(head_width) < head_width // 2, -sine_lookup, sine_lookup)
    query_gain, key_gain = gain_query.reshape(1, head_width), key_norm_gain.reshape(1, head_width)
    starts = query_start.reshape(micro_count, 1, micro_rows).astype(jnp.int32)
    (normed_low, token_scale, query_pre, key_pre, query_low, heads_low, log_total, keys_values,
     grads_all, wo_all) = attend(
        full_tokens, gain_attn.reshape(1, model_width), wq_all, wk_all, wv_all, query_gain, key_gain,
        cosine_lookup, turned_sine, starts, cotangent, w_out, nz, 3,
    )
    attn_part = dot_last(heads_low, wo_all).astype(low)
    gain_slice = lax.dynamic_slice_in_dim(gain_moe, my_columns, slice_width)
    middle, scale, moe_low, _, out_part, back, gates_grad, gates, *kept = run_experts(
        tokens, gain_slice.reshape(1, slice_width), router, attn_part, grads_all, routes_all,
        w_gate[0], w_up[0], w_down[0], micro_rows, capacity, nz, 8,
    )
    rows_in, pair_grad, hidden_low, gate_pre_low, up_pre_low = (
        array.reshape(-1, array.shape[2]) for array in kept
    )
    router_slice = lax.dynamic_slice_in_dim(router, my_columns, slice_width)
    swapped_grad = lax.dynamic_slice(
        grads_all, (mirror_index * row_count + micro_rows, my_columns), (micro_rows, slice_width)
    )
    grad_slice = jnp.concatenate([cotangent[:micro_rows], swapped_grad], axis=0).astype(f32)
    middle_grad, pre_low, head_gains, out_sum, w_out_grad, summed = attend_back(
        query_low, query_pre, key_pre, key_gain, query_gain, cosine_lookup, turned_sine, keys_values,
        starts, log_total, gates, gates_grad, router_slice, gain_slice.reshape(1, slice_width), moe_low,
        middle, scale, back, grad_slice, wo_all, heads_low, out_part, nz, 12,
    )
    block_out = (middle + out_sum).astype(low)
    gain_rows = slice_width // 128
    gains = jnp.concatenate(
        [jnp.zeros((slice_width,), f32), head_gains.reshape(-1),
         jnp.zeros(((8 - gain_rows - 2) * 128,), f32)]
    ).reshape(8, 128)
    attn_gain = lax.dynamic_slice_in_dim(gain_attn, my_columns, slice_width)
    (w_query_grad, w_key_grad, w_value_grad, token_grad, block_out, attn_gains, head_gains,
     *expert_grads) = tail(
        gate_pre_low, up_pre_low, hidden_low, tokens, middle_grad, token_scale,
        attn_gain.reshape(1, slice_width), block_out, gains, normed_low, pre_low, wq_all, wk_all, wv_all,
        rows_in, pair_grad, nz, 15,
    )
    per = expert_total // shard_count
    summed = summed.reshape(shard_count, group_count, -1, 128)
    router_grad = summed[:, :, : per * gain_rows].reshape(
        shard_count, group_count, per, slice_width
    ).transpose(1, 3, 0, 2).reshape(router.shape)
    return (
        block_out,
        token_grad,
        attn_gains.reshape(-1),
        w_query_grad,
        w_key_grad,
        w_value_grad,
        w_out_grad,
        head_gains[0],
        head_gains[1],
        summed[0, :, per * gain_rows : (per + 1) * gain_rows].reshape(-1),
        router_grad,
        expert_grads[0][None],
        expert_grads[1][None],
        expert_grads[2][None],
    )


def solution(mesh):
    small = mesh.shape["fsdp"] * mesh.shape["tp"] <= 32 and mesh.shape["tp"] == 4
    return jax.shard_map(
        gathered_body if small else body,
        mesh=mesh,
        in_specs=(
            P("fsdp", "tp"),
            P("fsdp", "tp"),
            P("fsdp", None),
            P(None, "fsdp"),
            P(),
            P("fsdp", "tp"),
            P("fsdp", "tp"),
            P("fsdp", "tp"),
            P("fsdp", "tp"),
            P(),
            P(),
            P(),
            P(),
            P(("fsdp", "tp"), None, None),
            P(("fsdp", "tp"), None, None),
            P(("fsdp", "tp"), None, None),
        ),
        out_specs=(
            P("fsdp", "tp"),
            P("fsdp", "tp"),
            P(),
            P("fsdp", "tp"),
            P("fsdp", "tp"),
            P("fsdp", "tp"),
            P("fsdp", "tp"),
            P(),
            P(),
            P(),
            P(),
            P(("fsdp", "tp"), None, None),
            P(("fsdp", "tp"), None, None),
            P(("fsdp", "tp"), None, None),
        ),
        check_vma=False,
    )
```

```python
import functools
import math

import jax
import jax.numpy as jnp
from jax import lax
from jax.experimental import pallas as pl
from jax.experimental.pallas import tpu as pltpu
from jax.sharding import PartitionSpec as P

TOPK = 8
DOCS = 4


theta_base = 1000000.0
norm_eps = 1e-06
masked_score = -1e30
highest_precision = lax.Precision.HIGHEST


def root_mean_norm(row_block, gain_row):
    return (
        row_block
        * lax.rsqrt(jnp.mean(row_block * row_block, axis=-1, keepdims=True) + norm_eps)
        * gain_row
    )


def rotary_apply(row_block, cosine_lookup, sine_lookup):
    half_width = row_block.shape[-1] // 2
    turned = jnp.concatenate([-row_block[..., half_width:], row_block[..., :half_width]], axis=-1)
    return row_block * cosine_lookup + turned * sine_lookup


def rope_tables(positions, head_width):
    half_width = head_width // 2
    frequency = theta_base ** (
        -2.0 * jnp.arange(half_width, dtype=jnp.int32).astype(jnp.float32) / head_width
    )
    angles = positions.astype(jnp.float32)[:, None] * frequency[None, :]
    cosine_lookup = jnp.cos(angles)
    sine_lookup = jnp.sin(angles)
    return (
        jnp.concatenate([cosine_lookup, cosine_lookup], axis=-1),
        jnp.concatenate([sine_lookup, sine_lookup], axis=-1),
    )


def swiglu(gate_pre, up_pre):
    return jax.nn.silu(gate_pre) * up_pre


def dot_first(left_side, right_side):
    return lax.dot_general(
        left_side, right_side, (((0,), (0,)), ((), ())), preferred_element_type=jnp.float32
    )


def dot_last(left_side, right_side):
    return lax.dot_general(
        left_side, right_side, (((1,), (1,)), ((), ())), preferred_element_type=jnp.float32
    )


def gather_weights(w_query, key_weight, value_weight, w_out):
    return (
        lax.all_gather(w_query, "fsdp", axis=0, tiled=True),
        lax.all_gather(key_weight, "fsdp", axis=0, tiled=True),
        lax.all_gather(value_weight, "fsdp", axis=0, tiled=True),
        lax.all_gather(w_out, "fsdp", axis=0, tiled=True),
    )


def gather_keys(keys_low, values_low):
    return (
        lax.all_gather(keys_low, "fsdp", axis=0, tiled=True),
        lax.all_gather(values_low, "fsdp", axis=0, tiled=True),
    )


def send_rows(buffer):
    return lax.all_to_all(buffer, "fsdp", split_axis=0, concat_axis=0, tiled=True)


def return_rows(buffer):
    return lax.all_to_all(buffer, "fsdp", split_axis=0, concat_axis=0, tiled=True)


def to_heads(per_token, kv_local, group_width):
    token_count, head_total, head_width = per_token.shape
    grouped_heads = per_token.reshape(token_count, kv_local, group_width, head_width)
    return grouped_heads.transpose(1, 2, 0, 3).reshape(
        kv_local, group_width * token_count, head_width
    )


def to_tokens(per_head, group_width):
    kv_local, row_count, head_width = per_head.shape
    token_count = row_count // group_width
    grouped_heads = per_head.reshape(kv_local, group_width, token_count, head_width)
    return grouped_heads.transpose(2, 0, 1, 3).reshape(
        token_count, kv_local * group_width * head_width
    )


def key_block(keys_all, key_start, block_keys, kv_local, head_width):
    return lax.dynamic_slice_in_dim(keys_all, key_start, block_keys, 0).reshape(
        block_keys, kv_local, head_width
    )


def block_scores(queries, keys_part, key_start, query_index, query_start):
    head_width = queries.shape[-1]
    scores = jnp.einsum(
        "hrd,khd->hrk", queries, keys_part, preferred_element_type=jnp.float32
    ) * head_width ** (-0.5)
    key_index = key_start + jnp.arange(keys_part.shape[0])
    allowed = (key_index[None, :] >= query_start[:, None]) & (
        key_index[None, :] <= query_index[:, None]
    )
    return (jnp.where(allowed[None], scores, masked_score), allowed)


def attend_forward(queries, keys_all, values_all, query_index, query_start, block_keys):
    kv_local, row_count, head_width = queries.shape
    lowest_block = jnp.min(query_start) // block_keys
    highest_block = jnp.max(query_index) // block_keys + 1

    def visit_block(block_index, running):
        run_peak, run_total, run_acc = running
        key_start = block_index * block_keys
        keys_part = key_block(keys_all, key_start, block_keys, kv_local, head_width)
        values_part = key_block(values_all, key_start, block_keys, kv_local, head_width)
        scores, allowed = block_scores(queries, keys_part, key_start, query_index, query_start)
        new_peak = jnp.maximum(run_peak, jnp.max(scores, axis=-1))
        weights = jnp.where(allowed[None], jnp.exp(scores - new_peak[..., None]), 0.0)
        factor = jnp.exp(run_peak - new_peak)
        run_total = run_total * factor + jnp.sum(weights, axis=-1)
        run_acc = run_acc * factor[..., None] + jnp.einsum(
            "hrk,khd->hrd",
            weights.astype(jnp.bfloat16),
            values_part,
            preferred_element_type=jnp.float32,
        )
        return (new_peak, run_total, run_acc)

    start_state = (
        jnp.full((kv_local, row_count), masked_score, jnp.float32),
        jnp.zeros((kv_local, row_count), jnp.float32),
        jnp.zeros((kv_local, row_count, head_width), jnp.float32),
    )
    run_peak, run_total, run_acc = lax.fori_loop(
        lowest_block, highest_block, visit_block, start_state
    )
    return (run_acc / run_total[..., None], run_peak + jnp.log(run_total))


def attend_backward(
    queries,
    keys_all,
    values_all,
    query_index,
    query_start,
    block_keys,
    outputs,
    log_total,
    grad_low,
):
    kv_local, row_count, head_width = queries.shape
    key_count = keys_all.shape[0]
    score_scale = head_width ** (-0.5)
    row_delta = jnp.sum(grad_low.astype(jnp.float32) * outputs, axis=-1)
    lowest_block = jnp.min(query_start) // block_keys
    highest_block = jnp.max(query_index) // block_keys + 1

    def visit_block(block_index, running):
        query_acc, key_acc, value_acc = running
        key_start = block_index * block_keys
        keys_part = key_block(keys_all, key_start, block_keys, kv_local, head_width)
        values_part = key_block(values_all, key_start, block_keys, kv_local, head_width)
        scores, allowed = block_scores(queries, keys_part, key_start, query_index, query_start)
        prob_block = jnp.where(allowed[None], jnp.exp(scores - log_total[..., None]), 0.0)
        prob_grad = jnp.einsum(
            "hrd,khd->hrk", grad_low, values_part, preferred_element_type=jnp.float32
        )
        score_grad = (prob_block * (prob_grad - row_delta[..., None])).astype(jnp.bfloat16)
        query_acc = (
            query_acc
            + jnp.einsum("hrk,khd->hrd", score_grad, keys_part, preferred_element_type=jnp.float32)
            * score_scale
        )
        key_part = (
            jnp.einsum("hrk,hrd->khd", score_grad, queries, preferred_element_type=jnp.float32)
            * score_scale
        )
        value_part = jnp.einsum(
            "hrk,hrd->khd",
            prob_block.astype(jnp.bfloat16),
            grad_low,
            preferred_element_type=jnp.float32,
        )
        key_acc = lax.dynamic_update_slice_in_dim(
            key_acc, key_part.reshape(block_keys, kv_local * head_width), key_start, 0
        )
        value_acc = lax.dynamic_update_slice_in_dim(
            value_acc, value_part.reshape(block_keys, kv_local * head_width), key_start, 0
        )
        return (query_acc, key_acc, value_acc)

    start_state = (
        jnp.zeros((kv_local, row_count, head_width), jnp.float32),
        jnp.zeros((key_count, kv_local * head_width), jnp.float32),
        jnp.zeros((key_count, kv_local * head_width), jnp.float32),
    )
    return lax.fori_loop(lowest_block, highest_block, visit_block, start_state)


def body(
    tokens,
    cotangent,
    routes,
    doc_ids,
    gain_attn,
    w_query,
    key_weight,
    value_weight,
    w_out,
    gain_query,
    key_norm_gain,
    gain_moe,
    router,
    w_gate,
    w_up,
    w_down,
):
    shard_count = lax.axis_size("fsdp")
    group_count = lax.axis_size("tp")
    shard_index = lax.axis_index("fsdp")
    group_index = lax.axis_index("tp")
    full_tokens, full_grads = (
        lax.all_gather(tokens, "tp", axis=1, tiled=True),
        lax.all_gather(cotangent, "tp", axis=1, tiled=True),
    )
    slice_width = tokens.shape[1]
    model_width = full_tokens.shape[1]
    micro_count, micro_rows = doc_ids.shape
    head_width = gain_query.shape[0]
    query_local = w_query.shape[1] // head_width
    kv_local = key_weight.shape[1] // head_width
    group_width = query_local // kv_local
    expert_total = router.shape[1]
    capacity = max(2, 2 * micro_rows * TOPK // expert_total)
    slot_total = shard_count * capacity
    pair_total = micro_rows * TOPK
    block_keys = micro_rows * math.gcd(shard_count, max(1, 512 // micro_rows))
    doc_range = jnp.arange(DOCS)
    expert_range = jnp.arange(expert_total)
    local_counts = jnp.sum((doc_ids[:, :, None] == doc_range).astype(jnp.float32), axis=1)
    doc_totals = lax.psum(local_counts, "fsdp")
    doc_begin = (jnp.cumsum(doc_totals, axis=1) - doc_totals).astype(jnp.int32)
    gate_expert = w_gate[0]
    up_expert = w_up[0]
    down_expert = w_down[0]
    router_wide = router.astype(jnp.float32)
    query_acc = jnp.zeros((model_width, query_local * head_width), jnp.float32)
    key_acc = jnp.zeros((model_width, kv_local * head_width), jnp.float32)
    value_acc = jnp.zeros((model_width, kv_local * head_width), jnp.float32)
    out_acc = jnp.zeros((model_width, query_local * head_width), jnp.float32)
    gate_acc = jnp.zeros(gate_expert.shape, jnp.float32)
    up_acc = jnp.zeros(up_expert.shape, jnp.float32)
    down_acc = jnp.zeros(down_expert.shape, jnp.float32)
    router_acc = jnp.zeros(router.shape, jnp.float32)
    gain_attn_acc = jnp.zeros(gain_attn.shape, jnp.float32)
    gain_moe_acc = jnp.zeros(gain_moe.shape, jnp.float32)
    gain_query_acc = jnp.zeros(gain_query.shape, jnp.float32)
    gain_key_acc = jnp.zeros(key_norm_gain.shape, jnp.float32)
    out_parts = []
    grad_parts = []
    for micro_index in range(micro_count):
        row_begin = micro_index * micro_rows
        token_block = full_tokens[row_begin : row_begin + micro_rows].astype(jnp.float32)
        ids_now = doc_ids[micro_index]
        query_index = shard_index * micro_rows + jnp.arange(micro_rows)
        query_start = jnp.sum(
            jnp.where(ids_now[:, None] == doc_range, doc_begin[micro_index][None, :], 0), axis=1
        )
        cosine_lookup, sine_lookup = rope_tables(query_index - query_start, head_width)
        gathered = gather_weights(w_query, key_weight, value_weight, w_out)
        normed, norm_pull = jax.vjp(root_mean_norm, token_block, gain_attn)
        normed_reduced = normed.astype(jnp.bfloat16)
        query_pre = jnp.dot(normed_reduced, gathered[0], preferred_element_type=jnp.float32)
        key_before_norm = jnp.dot(normed_reduced, gathered[1], preferred_element_type=jnp.float32)
        value_reduced = jnp.dot(
            normed_reduced, gathered[2], preferred_element_type=jnp.float32
        ).astype(jnp.bfloat16)

        def shape_heads(query_raw, key_raw, query_gain, key_gain):
            query_heads = rotary_apply(
                root_mean_norm(query_raw.reshape(micro_rows, query_local, head_width), query_gain),
                cosine_lookup[:, None, :],
                sine_lookup[:, None, :],
            )
            key_heads = rotary_apply(
                root_mean_norm(key_raw.reshape(micro_rows, kv_local, head_width), key_gain),
                cosine_lookup[:, None, :],
                sine_lookup[:, None, :],
            )
            return (query_heads, key_heads)

        (query_heads, key_heads), heads_pull = jax.vjp(
            shape_heads, query_pre, key_before_norm, gain_query, key_norm_gain
        )
        queries = to_heads(query_heads.astype(jnp.bfloat16), kv_local, group_width)
        keys_low = key_heads.reshape(micro_rows, kv_local * head_width).astype(jnp.bfloat16)
        keys_all, values_all = gather_keys(keys_low, value_reduced)
        row_index = jnp.tile(query_index, group_width)
        row_start = jnp.tile(query_start, group_width)
        head_out, log_total = attend_forward(
            queries, keys_all, values_all, row_index, row_start, block_keys
        )
        heads_low = to_tokens(head_out, group_width).astype(jnp.bfloat16)
        attn_part = dot_last(heads_low, gathered[3])
        middle = token_block + lax.psum(attn_part.astype(jnp.bfloat16), "tp").astype(jnp.float32)
        moe_normed, moe_pull = jax.vjp(root_mean_norm, middle, gain_moe)
        moe_low = moe_normed.astype(jnp.bfloat16)
        logits = jnp.dot(moe_low, router, preferred_element_type=jnp.float32)
        routes_now = routes[row_begin : row_begin + micro_rows]
        route_match = routes_now[:, :, None] == expert_range
        chosen = jnp.sum(jnp.where(route_match, logits[:, None, :], 0.0), axis=-1)
        gate_weights, softmax_pull = jax.vjp(jax.nn.softmax, chosen)
        mine = routes_now % group_count == group_index
        pair_target = jnp.where(mine, routes_now // group_count, shard_count).reshape(pair_total)
        target_hot = (pair_target[:, None] == jnp.arange(shard_count)).astype(jnp.int32)
        pair_rank = jnp.sum((jnp.cumsum(target_hot, axis=0) - target_hot) * target_hot, axis=1)
        pair_slot = jnp.where(
            pair_target < shard_count, pair_target * capacity + pair_rank, slot_total
        )
        slot_pair = (
            jnp.full((slot_total + 1,), pair_total, jnp.int32)
            .at[pair_slot]
            .set(jnp.arange(pair_total, dtype=jnp.int32))[:slot_total]
        )
        slot_token = slot_pair // TOPK
        slot_grid = pair_slot.reshape(micro_rows, TOPK)
        padded_low = jnp.concatenate([moe_low, jnp.zeros((1, model_width), jnp.bfloat16)], axis=0)
        received = send_rows(
            padded_low[slot_token].reshape(shard_count, capacity, model_width)
        ).reshape(slot_total, model_width)
        gate_pre = jnp.dot(received, gate_expert, preferred_element_type=jnp.float32)
        up_pre = jnp.dot(received, up_expert, preferred_element_type=jnp.float32)
        hidden, swiglu_pull = jax.vjp(swiglu, gate_pre, up_pre)
        hidden_low = hidden.astype(jnp.bfloat16)
        expert_out = jnp.dot(hidden_low, down_expert, preferred_element_type=jnp.float32).astype(
            jnp.bfloat16
        )
        returned = return_rows(expert_out.reshape(shard_count, capacity, model_width)).reshape(
            slot_total, model_width
        )
        padded_out = jnp.concatenate([returned, jnp.zeros((1, model_width), jnp.bfloat16)], axis=0)
        moe_part = jnp.zeros((micro_rows, model_width), jnp.float32)
        for pick_index in range(TOPK):
            moe_part = moe_part + gate_weights[:, pick_index : pick_index + 1] * padded_out[
                slot_grid[:, pick_index]
            ].astype(jnp.float32)
        moe_share = lax.psum_scatter(
            moe_part.astype(jnp.bfloat16), "tp", scatter_dimension=1, tiled=True
        ).astype(jnp.float32)
        middle_slice = lax.dynamic_slice_in_dim(middle, group_index * slice_width, slice_width, 1)
        out_parts.append((middle_slice + moe_share).astype(jnp.bfloat16))
        grad_block = full_grads[row_begin : row_begin + micro_rows].astype(jnp.float32)
        gate_columns = []
        for pick_index in range(TOPK):
            gate_columns.append(
                jnp.sum(
                    grad_block * padded_out[slot_grid[:, pick_index]].astype(jnp.float32), axis=1
                )
            )
        gates_grad = jnp.stack(gate_columns, axis=1)
        flat_gates = jnp.concatenate(
            [gate_weights.reshape(pair_total), jnp.zeros((1,), jnp.float32)]
        )
        padded_grad = jnp.concatenate(
            [grad_block, jnp.zeros((1, model_width), jnp.float32)], axis=0
        )
        send_grad = (padded_grad[slot_token] * flat_gates[slot_pair][:, None]).astype(jnp.bfloat16)
        received_grad = send_rows(send_grad.reshape(shard_count, capacity, model_width)).reshape(
            slot_total, model_width
        )
        hidden_grad = dot_last(received_grad, down_expert)
        down_acc = down_acc + dot_first(hidden_low, received_grad)
        gate_pre_grad, up_pre_grad = swiglu_pull(hidden_grad)
        gate_pre_low = gate_pre_grad.astype(jnp.bfloat16)
        up_pre_low = up_pre_grad.astype(jnp.bfloat16)
        gate_acc = gate_acc + dot_first(received, gate_pre_low)
        up_acc = up_acc + dot_first(received, up_pre_low)
        rows_back = (dot_last(gate_pre_low, gate_expert) + dot_last(up_pre_low, up_expert)).astype(
            jnp.bfloat16
        )
        back_rows = return_rows(rows_back.reshape(shard_count, capacity, model_width)).reshape(
            slot_total, model_width
        )
        padded_back = jnp.concatenate(
            [back_rows, jnp.zeros((1, model_width), jnp.bfloat16)], axis=0
        )
        moe_grad = jnp.zeros((micro_rows, model_width), jnp.float32)
        for pick_index in range(TOPK):
            moe_grad = moe_grad + padded_back[slot_grid[:, pick_index]].astype(jnp.float32)
        (chosen_grad,) = softmax_pull(gates_grad)
        logit_grad = jnp.sum(jnp.where(route_match, chosen_grad[:, :, None], 0.0), axis=1)
        router_acc = router_acc + lax.dot_general(
            moe_low.astype(jnp.float32),
            logit_grad,
            (((0,), (0,)), ((), ())),
            precision=highest_precision,
        )
        moe_grad = moe_grad + lax.dot_general(
            logit_grad, router_wide, (((1,), (1,)), ((), ())), precision=highest_precision
        )
        middle_part, gain_moe_part = moe_pull(moe_grad)
        gain_moe_acc = gain_moe_acc + gain_moe_part
        middle_grad = grad_block + lax.psum(middle_part.astype(jnp.bfloat16), "tp").astype(
            jnp.float32
        )
        middle_low = middle_grad.astype(jnp.bfloat16)
        gathered_back = gather_weights(w_query, key_weight, value_weight, w_out)
        out_acc = out_acc + dot_first(middle_low, heads_low)
        heads_grad = jnp.dot(middle_low, gathered_back[3], preferred_element_type=jnp.float32)
        grad_low = to_heads(
            heads_grad.reshape(micro_rows, query_local, head_width).astype(jnp.bfloat16),
            kv_local,
            group_width,
        )
        query_side, key_side_all, value_side_all = attend_backward(
            queries,
            keys_all,
            values_all,
            row_index,
            row_start,
            block_keys,
            head_out,
            log_total,
            grad_low,
        )
        key_side, value_side = (
            lax.psum_scatter(
                key_side_all.astype(jnp.bfloat16), "fsdp", scatter_dimension=0, tiled=True
            ).astype(jnp.float32),
            lax.psum_scatter(
                value_side_all.astype(jnp.bfloat16), "fsdp", scatter_dimension=0, tiled=True
            ).astype(jnp.float32),
        )
        query_pre_grad, key_pre_grad, gain_query_part, gain_key_part = heads_pull(
            (
                to_tokens(query_side, group_width).reshape(micro_rows, query_local, head_width),
                key_side.reshape(micro_rows, kv_local, head_width),
            )
        )
        gain_query_acc = gain_query_acc + gain_query_part
        gain_key_acc = gain_key_acc + gain_key_part
        query_pre_low = query_pre_grad.astype(jnp.bfloat16)
        key_pre_low = key_pre_grad.astype(jnp.bfloat16)
        value_pre_low = value_side.astype(jnp.bfloat16)
        query_acc = query_acc + dot_first(normed_reduced, query_pre_low)
        key_acc = key_acc + dot_first(normed_reduced, key_pre_low)
        value_acc = value_acc + dot_first(normed_reduced, value_pre_low)
        normed_grad = (
            dot_last(query_pre_low, gathered_back[0])
            + dot_last(key_pre_low, gathered_back[1])
            + dot_last(value_pre_low, gathered_back[2])
        )
        token_part, gain_attn_part = norm_pull(normed_grad)
        gain_attn_acc = gain_attn_acc + gain_attn_part
        token_share = lax.psum_scatter(
            token_part.astype(jnp.bfloat16), "tp", scatter_dimension=1, tiled=True
        ).astype(jnp.float32)
        grad_slice = lax.dynamic_slice_in_dim(
            middle_grad, group_index * slice_width, slice_width, 1
        )
        grad_parts.append((grad_slice + token_share).astype(jnp.bfloat16))
    weight_sums = (
        lax.psum_scatter(
            query_acc.astype(jnp.bfloat16), "fsdp", scatter_dimension=0, tiled=True
        ).astype(jnp.float32),
        lax.psum_scatter(
            key_acc.astype(jnp.bfloat16), "fsdp", scatter_dimension=0, tiled=True
        ).astype(jnp.float32),
        lax.psum_scatter(
            value_acc.astype(jnp.bfloat16), "fsdp", scatter_dimension=0, tiled=True
        ).astype(jnp.float32),
        lax.psum_scatter(
            out_acc.astype(jnp.bfloat16), "fsdp", scatter_dimension=0, tiled=True
        ).astype(jnp.float32),
    )
    small_sums = lax.psum(
        (gain_attn_acc, gain_query_acc, gain_key_acc, gain_moe_acc, router_acc), ("fsdp", "tp")
    )
    return (
        jnp.concatenate(out_parts, axis=0),
        jnp.concatenate(grad_parts, axis=0),
        small_sums[0],
        weight_sums[0],
        weight_sums[1],
        weight_sums[2],
        weight_sums[3],
        small_sums[1],
        small_sums[2],
        small_sums[3],
        small_sums[4],
        gate_acc[None],
        up_acc[None],
        down_acc[None],
    )


MESH = pl.DeviceIdType.MESH


def place():
    f = lax.axis_index("fsdp")
    t = lax.axis_index("tp")
    return f // 2, f % 2, t // 2, t % 2


def device(z, x, y, c):
    return (z * 2 + x, y * 2 + c)


def greet(devices):
    barrier = pltpu.get_barrier_semaphore()
    total = 0
    for valid, where in devices:
        if valid is None:
            pl.semaphore_signal(barrier, inc=1, device_id=where, device_id_type=MESH)
            total = total + 1
        else:
            @pl.when(valid)
            def _():
                pl.semaphore_signal(barrier, inc=1, device_id=where, device_id_type=MESH)
            total = total + valid.astype(jnp.int32)
    pl.semaphore_wait(barrier, total)


def remote(src, dst, send, recv, where):
    return pltpu.make_async_remote_copy(
        src_ref=src, dst_ref=dst, send_sem=send, recv_sem=recv, device_id=where, device_id_type=MESH
    )


def gather_all_kernel(nz, x_ref, o_ref, lsem, s_p, s_u, s_d, s_x, s_y, s_dx, s_dy,
                      r_z, r_x, r_y, r_dx, r_dy, r_p):
    z, x, y, c = place()
    rows, cols = x_ref.shape
    half = rows // 2
    partner = device(z, x, y, 1 - c)
    xn = device(z, 1 - x, y, c)
    yn = device(z, x, 1 - y, c)
    up = device(z + 1, x, y, c)
    down = device(z - 1, x, y, c)
    greet([(None, partner), (None, xn), (None, yn), (z < nz - 1, up), (z > 0, down)])

    def block(zz, xx, yy, cc, part=None):
        start = (zz * 2 + xx) * rows
        size = rows
        if part is not None:
            start = start + part * half
            size = half
        return o_ref.at[pl.ds(pl.multiple_of(start, half), size),
                        pl.ds(pl.multiple_of((yy * 2 + cc) * cols, cols), cols)]

    own = pltpu.make_async_copy(x_ref, block(z, x, y, c), lsem)
    own.start()

    items = [(0, 0)]
    for dist in range(1, nz):
        items += [(dist, -1), (dist, 1)]

    def guard(item, fn):
        dist, side = item
        zz = z + side * dist
        if dist == 0:
            fn(zz)
        else:
            pl.when((zz >= 0) & (zz < nz))(lambda: fn(zz))

    def c_z(zz, src):
        dst = block(zz, x, y, c)
        return (remote(src, dst, s_u.at[zz], r_z.at[zz], up),
                remote(src, dst, s_d.at[zz], r_z.at[zz], down))

    def c_xy(zz, src):
        dst = block(zz, x, y, c)
        return (remote(src, dst, s_x.at[zz], r_x.at[zz], xn),
                remote(src, dst, s_y.at[zz], r_y.at[zz], yn))

    def c_p(zz, rel, src=None):
        xx = 1 - x if rel in (1, 3, 4) else x
        yy = 1 - y if rel in (2, 3, 4) else y
        part = {3: 0, 4: 1}.get(rel)
        dst = block(zz, xx, yy, c, part)
        k = zz * 5 + rel
        return remote(dst if src is None else src, dst, s_p.at[k], r_p.at[k], partner)

    def w_p(zz, rel):
        xx = 1 - x if rel in (1, 3, 4) else x
        yy = 1 - y if rel in (2, 3, 4) else y
        part = {3: 0, 4: 1}.get(rel)
        dst = block(zz, xx, yy, 1 - c, part)
        k = zz * 5 + rel
        return remote(dst, dst, s_p.at[k], r_p.at[k], partner)

    def c_diag(zz):
        a = block(zz, 1 - x, y, c, 0)
        b = block(zz, x, 1 - y, c, 1)
        return (remote(a, a, s_dy.at[zz], r_dy.at[zz], yn),
                remote(b, b, s_dx.at[zz], r_dx.at[zz], xn))

    def stage_a(item):
        dist, side = item

        def run(zz):
            src = x_ref if dist == 0 else block(zz, x, y, c)
            cu, cd = c_z(zz, src)
            if dist:
                cu.wait_recv()
            if side <= 0:
                pl.when(z < nz - 1)(cu.start)
            if dist == 0 or side > 0:
                pl.when(z > 0)(cd.start)
            for cc in c_xy(zz, src):
                cc.start()
            c_p(zz, 0, src).start()

        guard(item, run)

    def stage_b(item):
        def run(zz):
            cx, cy = c_xy(zz, block(zz, x, y, c))
            dy, dx = c_diag(zz)
            cx.wait_recv()
            dy.start()
            c_p(zz, 1).start()
            cy.wait_recv()
            dx.start()
            c_p(zz, 2).start()

        guard(item, run)

    def stage_c(item):
        def run(zz):
            dy, dx = c_diag(zz)
            dy.wait_recv()
            c_p(zz, 3).start()
            dx.wait_recv()
            c_p(zz, 4).start()

        guard(item, run)

    count = len(items)
    for k in range(count + 2):
        if k < count:
            stage_a(items[k])
        if 0 <= k - 1 < count:
            stage_b(items[k - 1])
        if 0 <= k - 2 < count:
            stage_c(items[k - 2])

    def finish(zz, carry):
        for rel in range(5):
            w_p(zz, rel).wait_recv()
            c_p(zz, rel).wait_send()
        cu, cd = c_z(zz, block(zz, x, y, c))
        pl.when((zz <= z) & (z < nz - 1))(cu.wait_send)
        pl.when((zz >= z) & (z > 0))(cd.wait_send)
        for cc in c_xy(zz, block(zz, x, y, c)) + c_diag(zz):
            cc.wait_send()
        return carry

    lax.fori_loop(0, nz, finish, 0)
    own.wait()


def gather_all(block, nz, collective_id):
    rows, cols = block.shape
    dma = pltpu.SemaphoreType.DMA
    return pl.pallas_call(
        functools.partial(gather_all_kernel, nz),
        out_shape=jax.ShapeDtypeStruct((rows * nz * 2, cols * 4), block.dtype),
        in_specs=[pl.BlockSpec(memory_space=pl.ANY)],
        out_specs=pl.BlockSpec(memory_space=pl.ANY),
        scratch_shapes=[dma] + [dma((5 * nz,))] + [dma((nz,))] * 6 + [dma((nz,))] * 5 + [dma((5 * nz,))],
        compiler_params=pltpu.CompilerParams(collective_id=collective_id, has_side_effects=True),
        name="gather_all",
    )(block)


def scatter_all_kernel(nz, p_ref, o_ref, w, lp, rx, rxd, ry, ryd, rz,
                       s_l, s_p, r_p, s_x, s_y, s_dx, s_dy, s_z, r_x, r_y, r_dx, r_dy, r_z):
    z, x, y, c = place()
    rows, cols = o_ref.shape
    half = rows // 2
    partner = device(z, x, y, 1 - c)
    xn = device(z, 1 - x, y, c)
    yn = device(z, x, 1 - y, c)
    up = device(z + 1, x, y, c)
    down = device(z - 1, x, y, c)
    greet([(None, partner), (None, xn), (None, yn), (z < nz - 1, up), (z > 0, down)])
    chunk = 64

    def block(zz, rel, cc):
        xx = 1 - x if rel in (1, 3) else x
        yy = 1 - y if rel in (2, 3) else y
        return p_ref.at[pl.ds(pl.multiple_of((zz * 2 + xx) * rows, rows), rows),
                        pl.ds(pl.multiple_of((yy * 2 + cc) * cols, cols), cols)]

    items = []
    for dist in range(nz - 1, 0, -1):
        items += [(dist, -1), (dist, 1)]
    items += [(0, 0)]

    def guard(item, fn):
        dist, side = item
        zz = z + side * dist
        if dist == 0:
            fn(zz)
        else:
            pl.when((zz >= 0) & (zz < nz))(lambda: fn(zz))

    def c_p(zz, rel):
        k = zz * 4 + rel
        return remote(block(zz, rel, 1 - c), lp.at[zz, rel], s_p.at[k], r_p.at[k], partner)

    def c_l(zz, rel):
        return pltpu.make_async_copy(block(zz, rel, c), w.at[zz, rel], s_l.at[zz * 4 + rel])

    def c_diag(zz):
        return (remote(w.at[zz, 3, pl.ds(0, half)], rxd.at[zz], s_dx.at[zz], r_dx.at[zz], xn),
                remote(w.at[zz, 3, pl.ds(half, half)], ryd.at[zz], s_dy.at[zz], r_dy.at[zz], yn))

    def c_xy(zz):
        return (remote(w.at[zz, 1], rx.at[zz], s_x.at[zz], r_x.at[zz], xn),
                remote(w.at[zz, 2], ry.at[zz], s_y.at[zz], r_y.at[zz], yn))

    def c_z(zz, slot, where):
        return remote(w.at[zz, 0], rz.at[slot], s_z.at[zz], r_z.at[slot], where)

    def add(dst, srcs, start, count):
        def step(i, carry):
            off = pl.multiple_of(i * chunk, chunk)
            here = pl.ds(pl.multiple_of(start + off, chunk), chunk)
            total = dst[here, :].astype(jnp.float32)
            for src in srcs:
                total = total + src[pl.ds(off, chunk), :].astype(jnp.float32)
            dst[here, :] = total.astype(dst.dtype)
            return carry
        lax.fori_loop(0, count // chunk, step, 0)

    def stage_0(item):
        def run(zz):
            for rel in (3, 1, 2, 0):
                c_p(zz, rel).start()
                c_l(zz, rel).start()
        guard(item, run)

    def stage_d(item):
        def run(zz):
            for rel in (3, 1, 2, 0):
                c_p(zz, rel).wait_recv()
                c_l(zz, rel).wait()
                add(w.at[zz, rel], [lp.at[zz, rel]], 0, rows)
                if rel == 3:
                    for cc in c_diag(zz):
                        cc.start()
        guard(item, run)

    def stage_e(item):
        def run(zz):
            dx, dy = c_diag(zz)
            cx, cy = c_xy(zz)
            dy.wait_recv()
            add(w.at[zz, 1], [ryd.at[zz]], half, half)
            cx.start()
            dx.wait_recv()
            add(w.at[zz, 2], [rxd.at[zz]], 0, half)
            cy.start()
        guard(item, run)

    def stage_f(item):
        dist, side = item

        def run(zz):
            cx, cy = c_xy(zz)
            cx.wait_recv()
            cy.wait_recv()
            if dist:
                add(w.at[zz, 0], [rx.at[zz], ry.at[zz]], 0, rows)
                has = z > 0 if side > 0 else z < nz - 1
                cz = c_z(zz, zz, up if side > 0 else down)

                @pl.when(has)
                def _():
                    cz.wait_recv()
                    add(w.at[zz, 0], [rz.at[zz]], 0, rows)
                if side > 0:
                    cz.start()
                else:
                    if dist == 1:
                        c_z(zz, nz, down).start()
                    else:
                        cz.start()
            else:
                below, above = c_z(zz, zz, up), c_z(zz, nz, down)

                def total(refs):
                    def step(i, carry):
                        here = pl.ds(pl.multiple_of(i * chunk, chunk), chunk)
                        acc = w[zz, 0, here, :].astype(jnp.float32)
                        for ref in refs:
                            acc = acc + ref[here, :].astype(jnp.float32)
                        o_ref[here, :] = acc
                        return carry
                    lax.fori_loop(0, rows // chunk, step, 0)

                pl.when(z > 0)(below.wait_recv)
                pl.when(z < nz - 1)(above.wait_recv)
                pl.when(z == 0)(lambda: total([rx.at[zz], ry.at[zz], rz.at[nz]]))
                pl.when(z == nz - 1)(lambda: total([rx.at[zz], ry.at[zz], rz.at[zz]]))
                pl.when((z > 0) & (z < nz - 1))(
                    lambda: total([rx.at[zz], ry.at[zz], rz.at[zz], rz.at[nz]]))
        guard(item, run)

    for item in items:
        stage_0(item)
    count = len(items)
    for k in range(count + 2):
        if k < count:
            stage_d(items[k])
        if 0 <= k - 1 < count:
            stage_e(items[k - 1])
        if 0 <= k - 2 < count:
            stage_f(items[k - 2])

    def finish(zz, carry):
        for rel in range(4):
            c_p(zz, rel).wait_send()
        for cc in c_diag(zz) + c_xy(zz):
            cc.wait_send()
        pl.when(zz != z)(c_z(zz, zz, up).wait_send)
        return carry

    lax.fori_loop(0, nz, finish, 0)


def scatter_all(partial, nz, collective_id):
    rows, cols = partial.shape[0] // (2 * nz), partial.shape[1] // 4
    half = rows // 2
    dma = pltpu.SemaphoreType.DMA
    kind = partial.dtype
    vm = pltpu.VMEM
    return pl.pallas_call(
        functools.partial(scatter_all_kernel, nz),
        out_shape=jax.ShapeDtypeStruct((rows, cols), jnp.float32),
        in_specs=[pl.BlockSpec(memory_space=pl.ANY)],
        out_specs=pl.BlockSpec(memory_space=pltpu.VMEM),
        scratch_shapes=[vm((nz, 4, rows, cols), kind), vm((nz, 4, rows, cols), kind),
                        vm((nz, rows, cols), kind), vm((nz, half, cols), kind),
                        vm((nz, rows, cols), kind), vm((nz, half, cols), kind),
                        vm((nz + 1, rows, cols), kind)]
        + [dma((4 * nz,))] * 3 + [dma((nz,))] * 5 + [dma((nz,))] * 4 + [dma((nz + 1,))],
        compiler_params=pltpu.CompilerParams(collective_id=collective_id, has_side_effects=True,
                                             vmem_limit_bytes=62 << 20),
        name="scatter_all",
    )(partial)


def z_items(nz, near_first):
    items = [(0, 0)] if near_first else []
    order = range(1, nz) if near_first else range(nz - 1, 0, -1)
    for dist in order:
        items += [(dist, -1), (dist, 1)]
    return items if near_first else items + [(0, 0)]


def z_guard(item, z, nz, fn):
    dist, side = item
    zz = z + side * dist
    if dist == 0:
        fn(zz)
    else:
        pl.when((zz >= 0) & (zz < nz))(lambda: fn(zz))


def gather_rows_kernel(nz, count, columns, narrow, *refs):
    total = count + columns
    srcs, refs = refs[:total], refs[total:]
    outs, refs = refs[:total], refs[total:]
    wide, refs = refs[: min(columns, 1)], refs[min(columns, 1) :]
    lsem, s_u, s_d, s_x, r_z, r_x, s_c, r_c, s_w, r_w = refs
    z, x, y, c = place()
    xn, up, down = device(z, 1 - x, y, c), device(z + 1, x, y, c), device(z - 1, x, y, c)
    partner, yn = device(z, x, y, 1 - c), device(z, x, 1 - y, c)
    wanted = [(None, xn), (z < nz - 1, up), (z > 0, down)]
    greet(wanted + [(None, partner), (None, yn), (None, device(nz - 1 - z, x, y, c))] * min(columns, 1))

    def block(n, zz, xx):
        rows = srcs[n].shape[0]
        return outs[n].at[pl.ds(pl.multiple_of((zz * 2 + xx) * rows, rows), rows)]

    own = [(srcs[n], block(n, z, x)) for n in range(count)]
    column_copies, swaps = [], []
    if columns:
        mirror = device(nz - 1 - z, x, y, c)
        first, out = outs[count], wide[0]
        rows, cols = first.shape
        top, bottom = pl.ds(0, rows // 2), pl.ds(rows // 2, rows // 2)
        for n in range(columns):
            src, dst = srcs[count + n], outs[count + n]
            swaps.append(remote(src.at[bottom], dst.at[bottom], s_w.at[n], r_w.at[n], mirror))
            dst[top, :] = src[top, :]

        def column(yy):
            return out.at[:, pl.ds(pl.multiple_of((yy * 2 + c) * cols, cols), cols)]

        column_copies = [
            remote(first, column(y), s_c.at[0], r_c.at[0], yn),
            remote(first, column(y), s_c.at[1], r_c.at[1], partner),
            remote(column(1 - y), column(1 - y), s_c.at[2], r_c.at[2], partner),
        ]
        last = pltpu.make_async_copy(first, column(y), lsem.at[total])
    own = [pltpu.make_async_copy(src, dst, lsem.at[n]) for n, (src, dst) in enumerate(own)]
    pairs = range(count - narrow, count)
    sides = [remote(srcs[n], block(n, z, x), s_x.at[n * nz], r_x.at[n * nz], xn) for n in pairs]
    for copy in swaps + own + sides:
        copy.start()

    def copies(n, zz, src):
        dst = block(n, zz, x)
        k = n * nz + zz
        if n in pairs:
            rows = 2 * srcs[n].shape[0]
            dst = src = outs[n].at[pl.ds(pl.multiple_of(zz * rows, rows), rows)]
        return (remote(src, dst, s_u.at[k], r_z.at[k], up),
                remote(src, dst, s_d.at[k], r_z.at[k], down),
                remote(src, dst, s_x.at[k], r_x.at[k], xn))

    items = z_items(nz, True)
    for item in items:
        dist, side = item

        def run(zz):
            for n in range(count):
                src = srcs[n] if dist == 0 else block(n, zz, x)
                cu, cd, cx = copies(n, zz, src)
                if dist:
                    cu.wait_recv()
                elif n in pairs:
                    own[n].wait()
                    sides[n - count + narrow].wait_recv()
                if side <= 0:
                    pl.when(z < nz - 1)(cu.start)
                if side > 0 or dist == 0:
                    pl.when(z > 0)(cd.start)
                if n not in pairs:
                    cx.start()

        z_guard(item, z, nz, run)
        if columns and item == items[-3]:
            swaps[0].wait_recv()
            column_copies[0].start()
            column_copies[1].start()
            last.start()
        if columns and item == items[-1]:
            column_copies[0].wait_recv()
            column_copies[2].start()

    def finish(zz, carry):
        for n in range(count):
            cu, cd, cx = copies(n, zz, block(n, zz, x))
            if n not in pairs:
                cx.wait_recv()
                cx.wait_send()
            pl.when((zz <= z) & (z < nz - 1))(cu.wait_send)
            pl.when((zz >= z) & (z > 0))(cd.wait_send)
        return carry

    lax.fori_loop(0, nz, finish, 0)
    for copy in own[: count - narrow]:
        copy.wait()
    for copy in sides:
        copy.wait_send()
    if columns:
        column_copies[0].wait_send()
        column_copies[1].wait()
        column_copies[2].wait()
        last.wait()
        swaps[0].wait_send()
        for copy in swaps[1:]:
            copy.wait()


def gather_rows(blocks, nz, collective_id, swapped=(), narrow=0):
    count, columns = len(blocks), len(swapped)
    dma = pltpu.SemaphoreType.DMA
    any_space = pl.BlockSpec(memory_space=pl.ANY)
    vmem = pl.BlockSpec(memory_space=pltpu.VMEM)
    shapes = [
        jax.ShapeDtypeStruct((b.shape[0] * nz * 2,) + b.shape[1:], b.dtype) for b in blocks
    ] + [jax.ShapeDtypeStruct(b.shape, b.dtype) for b in swapped]
    if columns:
        rows, cols = swapped[0].shape
        shapes.append(jax.ShapeDtypeStruct((rows, cols * 4), swapped[0].dtype))
    total = count + columns
    return pl.pallas_call(
        functools.partial(gather_rows_kernel, nz, count, columns, narrow),
        out_shape=shapes,
        in_specs=[vmem] * total,
        out_specs=[any_space] * count + [vmem] * columns + [any_space] * min(columns, 1),
        scratch_shapes=[dma((total + 1,))] + [dma((count * nz,))] * 5 + [dma((3,))] * 2
        + [dma((max(columns, 1),))] * 2,
        compiler_params=pltpu.CompilerParams(collective_id=collective_id, has_side_effects=True,
                                             vmem_limit_bytes=62 << 20),
        name="gather_rows",
    )(*blocks, *swapped)


def swap_back_kernel(nz, *refs):
    count = (len(refs) - 2) // 2
    srcs, outs = refs[:count], refs[count : 2 * count]
    s, r = refs[2 * count :]
    z, x, y, c = place()
    mirror = device(nz - 1 - z, x, y, c)
    greet([(None, mirror)])
    copies = [remote(src, out, s.at[n], r.at[n], mirror)
              for n, (src, out) in enumerate(zip(srcs, outs))]
    for copy in copies:
        copy.start()
    for copy in copies:
        copy.wait()


def swap_back(blocks, nz, collective_id):
    count = len(blocks)
    dma = pltpu.SemaphoreType.DMA
    any_space = pl.BlockSpec(memory_space=pl.ANY)
    return pl.pallas_call(
        functools.partial(swap_back_kernel, nz),
        out_shape=[jax.ShapeDtypeStruct(b.shape, b.dtype) for b in blocks],
        in_specs=[any_space] * count,
        out_specs=[any_space] * count,
        scratch_shapes=[dma((count,))] * 2,
        compiler_params=pltpu.CompilerParams(collective_id=collective_id, has_side_effects=True),
        name="swap_back",
    )(*blocks)


def add_blocks(dst, srcs, start, count, out=None, chunk=64):
    target = dst if out is None else out

    def step(i, carry):
        off = pl.multiple_of(i * chunk, chunk)
        here = pl.ds(pl.multiple_of(start + off, chunk), chunk)
        total = dst[here, :].astype(jnp.float32)
        for src in srcs:
            total = total + src[pl.ds(off, chunk), :].astype(jnp.float32)
        target[here, :] = total.astype(target.dtype)
        return carry

    lax.fori_loop(0, count // chunk, step, 0)


def reduce_rows_kernel(nz, p_ref, o_ref, w, rx, rz, s_l, s_x, s_z, r_x, r_z):
    z, x, y, c = place()
    rows = o_ref.shape[0]
    xn, up, down = device(z, 1 - x, y, c), device(z + 1, x, y, c), device(z - 1, x, y, c)
    greet([(None, xn), (z < nz - 1, up), (z > 0, down)])

    def block(zz, xx):
        return p_ref.at[pl.ds(pl.multiple_of((zz * 2 + xx) * rows, rows), rows)]

    def c_x(zz):
        return remote(block(zz, 1 - x), rx.at[zz], s_x.at[zz], r_x.at[zz], xn)

    def c_l(zz):
        return pltpu.make_async_copy(block(zz, x), w.at[zz], s_l.at[zz])

    def c_z(zz, slot, where):
        return remote(w.at[zz], rz.at[slot], s_z.at[zz], r_z.at[slot], where)

    items = z_items(nz, False)

    def start(zz):
        c_x(zz).start()
        c_l(zz).start()

    for item in items:
        z_guard(item, z, nz, start)
    for item in items:
        dist, side = item

        def run(zz):
            c_l(zz).wait()
            c_x(zz).wait_recv()
            if dist:
                add_blocks(w.at[zz], [rx.at[zz]], 0, rows)
                cz = c_z(zz, zz, up if side > 0 else down)

                @pl.when(z > 0 if side > 0 else z < nz - 1)
                def _():
                    cz.wait_recv()
                    add_blocks(w.at[zz], [rz.at[zz]], 0, rows)

                (c_z(zz, nz, down) if side < 0 and dist == 1 else cz).start()
            else:
                pl.when(z > 0)(c_z(zz, zz, up).wait_recv)
                pl.when(z < nz - 1)(c_z(zz, nz, down).wait_recv)
                low, high = rz.at[zz], rz.at[nz]
                pl.when(z == 0)(lambda: add_blocks(w.at[zz], [rx.at[zz], high], 0, rows, o_ref))
                pl.when(z == nz - 1)(lambda: add_blocks(w.at[zz], [rx.at[zz], low], 0, rows, o_ref))
                pl.when((z > 0) & (z < nz - 1))(
                    lambda: add_blocks(w.at[zz], [rx.at[zz], low, high], 0, rows, o_ref)
                )

        z_guard(item, z, nz, run)

    def finish(zz, carry):
        c_x(zz).wait_send()
        pl.when(zz != z)(c_z(zz, zz, up).wait_send)
        return carry

    lax.fori_loop(0, nz, finish, 0)


def reduce_rows(partial, nz, collective_id):
    rows, cols = partial.shape[0] // (2 * nz), partial.shape[1]
    dma, vm, kind = pltpu.SemaphoreType.DMA, pltpu.VMEM, partial.dtype
    return pl.pallas_call(
        functools.partial(reduce_rows_kernel, nz),
        out_shape=jax.ShapeDtypeStruct((rows, cols), jnp.float32),
        in_specs=[pl.BlockSpec(memory_space=pl.ANY)],
        out_specs=pl.BlockSpec(memory_space=pltpu.VMEM),
        scratch_shapes=[vm((nz, rows, cols), kind), vm((nz, rows, cols), kind),
                        vm((nz + 1, rows, cols), kind)]
        + [dma((nz,))] * 4 + [dma((nz + 1,))],
        compiler_params=pltpu.CompilerParams(
            collective_id=collective_id, has_side_effects=True, vmem_limit_bytes=62 << 20
        ),
        name="reduce_rows",
    )(partial)


def gather_cols_kernel(x_ref, o_ref, lsem, s_p, s_y, r_p, r_y):
    z, x, y, c = place()
    cols = x_ref.shape[1]
    partner, yn = device(z, x, y, 1 - c), device(z, x, 1 - y, c)
    greet([(None, partner), (None, yn)])

    def block(yy, cc):
        return o_ref.at[:, pl.ds(pl.multiple_of((yy * 2 + cc) * cols, cols), cols)]

    own = pltpu.make_async_copy(x_ref, block(y, c), lsem)
    cy = remote(x_ref, block(y, c), s_y, r_y, yn)
    cp = remote(x_ref, block(y, c), s_p.at[0], r_p.at[0], partner)
    cf = remote(block(1 - y, c), block(1 - y, c), s_p.at[1], r_p.at[1], partner)
    cy.start()
    cp.start()
    own.start()
    cy.wait_recv()
    cf.start()
    cp.wait()
    cf.wait()
    cy.wait_send()
    own.wait()


def gather_cols(block, collective_id):
    dma = pltpu.SemaphoreType.DMA
    any_space = pl.BlockSpec(memory_space=pl.ANY)
    return pl.pallas_call(
        gather_cols_kernel,
        out_shape=jax.ShapeDtypeStruct((block.shape[0], block.shape[1] * 4), block.dtype),
        in_specs=[any_space],
        out_specs=any_space,
        scratch_shapes=[dma, dma((2,)), dma, dma((2,)), dma],
        compiler_params=pltpu.CompilerParams(collective_id=collective_id, has_side_effects=True),
        name="gather_cols",
    )(block)


def reduce_cols_kernel(p_ref, o_ref, w, rp, ry, s_l, s_p, s_y, r_p, r_y):
    z, x, y, c = place()
    rows, cols = o_ref.shape
    partner, yn = device(z, x, y, 1 - c), device(z, x, 1 - y, c)
    greet([(None, partner), (None, yn)])

    def block(yy, cc):
        return p_ref.at[:, pl.ds(pl.multiple_of((yy * 2 + cc) * cols, cols), cols)]

    sends = [remote(block(yy, 1 - c), rp.at[k], s_p.at[k], r_p.at[k], partner)
             for k, yy in enumerate((1 - y, y))]
    loads = [pltpu.make_async_copy(block(yy, c), w.at[k], s_l.at[k])
             for k, yy in enumerate((1 - y, y))]
    cy = remote(w.at[0], ry, s_y, r_y, yn)
    for k in range(2):
        sends[k].start()
        loads[k].start()
    loads[0].wait()
    sends[0].wait_recv()
    add_blocks(w.at[0], [rp.at[0]], 0, rows)
    cy.start()
    loads[1].wait()
    sends[1].wait_recv()
    cy.wait_recv()
    add_blocks(w.at[1], [rp.at[1], ry], 0, rows, o_ref)
    for k in range(2):
        sends[k].wait_send()
    cy.wait_send()


def reduce_cols(partial, collective_id):
    rows, cols = partial.shape[0], partial.shape[1] // 4
    dma, vm, kind = pltpu.SemaphoreType.DMA, pltpu.VMEM, partial.dtype
    return pl.pallas_call(
        reduce_cols_kernel,
        out_shape=jax.ShapeDtypeStruct((rows, cols), jnp.float32),
        in_specs=[pl.BlockSpec(memory_space=pl.ANY)],
        out_specs=pl.BlockSpec(memory_space=pltpu.VMEM),
        scratch_shapes=[vm((2, rows, cols), kind), vm((2, rows, cols), kind), vm((rows, cols), kind),
                        dma((2,)), dma((2,)), dma, dma((2,)), dma],
        compiler_params=pltpu.CompilerParams(
            collective_id=collective_id, has_side_effects=True, vmem_limit_bytes=62 << 20
        ),
        name="reduce_cols",
    )(partial)


def sum_cols_kernel(v_ref, o_ref, got, s, r):
    group = lax.axis_index("tp")
    shard = lax.axis_index("fsdp")
    peers = [(shard, (group + k) % 4) for k in range(1, 4)]
    greet([(None, peer) for peer in peers])
    copies = [remote(v_ref, got.at[k], s.at[k], r.at[k], peer) for k, peer in enumerate(peers)]
    for copy in copies:
        copy.start()
    for copy in copies:
        copy.wait()
    o_ref[...] = v_ref[...] + got[0] + got[1] + got[2]


def sum_cols(vector, collective_id):
    dma = pltpu.SemaphoreType.DMA
    shape = vector.shape
    return pl.pallas_call(
        sum_cols_kernel,
        out_shape=jax.ShapeDtypeStruct(shape, jnp.float32),
        in_specs=[pl.BlockSpec(memory_space=pltpu.VMEM)],
        out_specs=pl.BlockSpec(memory_space=pltpu.VMEM),
        scratch_shapes=[pltpu.VMEM((3,) + shape, jnp.float32), dma((3,)), dma((3,))],
        compiler_params=pltpu.CompilerParams(collective_id=collective_id, has_side_effects=True),
        name="sum_cols",
    )(vector)


def greet_all(shard, group, shards, groups):
    barrier = pltpu.get_barrier_semaphore()
    total = shards * groups

    def step(k, carry):
        other = (shard * groups + group + k) % total
        pl.semaphore_signal(
            barrier, inc=1, device_id=(other // groups, other % groups), device_id_type=MESH
        )
        return carry

    lax.fori_loop(1, total, step, 0)
    pl.semaphore_wait(barrier, total - 1)


def swap_rows_kernel(shards, groups, v_ref, o_ref, s, r):
    shard, group = lax.axis_index("fsdp"), lax.axis_index("tp")
    total = shards * groups
    me = shard * groups + group
    greet_all(shard, group, shards, groups)

    def copy(k):
        other = (me + k) % total
        return remote(v_ref.at[other // groups], o_ref.at[me], s.at[k], r.at[k],
                      (other // groups, other % groups))

    def start(k, carry):
        copy(k).start()
        return carry

    def wait(k, carry):
        copy(k).wait()
        return carry

    lax.fori_loop(1, total, start, 0)
    o_ref[me] = v_ref[shard]
    lax.fori_loop(1, total, wait, 0)


def swap_rows(values, shards, groups, collective_id):
    dma, total = pltpu.SemaphoreType.DMA, shards * groups
    return pl.pallas_call(
        functools.partial(swap_rows_kernel, shards, groups),
        out_shape=jax.ShapeDtypeStruct((total,) + values.shape[1:], values.dtype),
        in_specs=[pl.BlockSpec(memory_space=pltpu.VMEM)],
        out_specs=pl.BlockSpec(memory_space=pltpu.VMEM),
        scratch_shapes=[dma((total,)), dma((total,))],
        compiler_params=pltpu.CompilerParams(collective_id=collective_id, has_side_effects=True),
        name="swap_rows",
    )(values)


def sum_small_kernel(shards, groups, v_ref, o_ref, got, s1, r1, s2, r2):
    shard, group = lax.axis_index("fsdp"), lax.axis_index("tp")
    total = shards * groups
    me = shard * groups + group
    greet_all(shard, group, shards, groups)

    def first(k):
        other = (shard + k) % shards
        return remote(v_ref.at[other], got.at[k], s1.at[k], r1.at[k], (other, group))

    def second(k):
        other = (me + k) % total
        return remote(o_ref.at[me], o_ref.at[me], s2.at[k], r2.at[k],
                      (other // groups, other % groups))

    for k in range(1, shards):
        first(k).start()
    acc = v_ref[shard]
    for k in range(1, shards):
        first(k).wait()
        acc = acc + got[k]
    o_ref[me] = acc

    def start(k, carry):
        second(k).start()
        return carry

    def wait(k, carry):
        second(k).wait()
        return carry

    lax.fori_loop(1, total, start, 0)
    lax.fori_loop(1, total, wait, 0)


def sum_small(values, shards, groups, collective_id):
    dma, total = pltpu.SemaphoreType.DMA, shards * groups
    part = values.shape[1:]
    return pl.pallas_call(
        functools.partial(sum_small_kernel, shards, groups),
        out_shape=jax.ShapeDtypeStruct((total,) + part, values.dtype),
        in_specs=[pl.BlockSpec(memory_space=pltpu.VMEM)],
        out_specs=pl.BlockSpec(memory_space=pltpu.VMEM),
        scratch_shapes=[pltpu.VMEM((shards,) + part, values.dtype), dma((shards,)), dma((shards,)),
                        dma((total,)), dma((total,))],
        compiler_params=pltpu.CompilerParams(collective_id=collective_id, has_side_effects=True),
        name="sum_small",
    )(values)


def dot_plain(left, right):
    return jnp.dot(left, right, preferred_element_type=jnp.float32)


def far_first(nz, z, k):
    at = 0
    for here in range(nz):
        order = sorted(range(nz), key=lambda other: (-abs(other - here), other))
        for step, other in enumerate(order):
            at = at + jnp.where((z == here) & (k == step), other, 0)
    return at


def tile_item(nz, z, k):
    return far_first(nz, z, jnp.where(k == nz - 1, nz - 1, nz - 2 - k))


def line_schedule(nz):
    order = []
    for here in range(nz):
        near = sorted(range(nz), key=lambda other: (-abs(other - here), other))[::-1]
        order.append(near[1:] + near[:1])
    sent = {}
    steps = [{} for _ in range(nz)]

    def send(here, to):
        if (here, to) not in sent:
            ready = 2 * order[here].index(to) + 2
            back = here - 1 if to > here else here + 1
            if 0 <= back < nz:
                ready = max(ready, send(back, to)) + 1
                steps[here].setdefault(ready, []).append(to)
            sent[here, to] = ready
        return sent[here, to]

    for here in range(nz):
        for to in range(nz):
            if to != here:
                send(here, to)
    for here in range(nz):
        arrivals = [send(near, here) for near in (here - 1, here + 1) if 0 <= near < nz]
        last = max(arrivals + [2 * order[here].index(here) + 2]) + 1
        steps[here].setdefault(last, []).append(here)
    return steps


def expert_kernel(nz, slots, block_rows, tok_ref, gain_ref, router_ref, attn_part, g_all, routes_all,
                  wg_all, wu_all, wd_all, middle_ref, scale_ref, low_ref, x_all, out_all, back_ref, gg_got, gates_ref, xr_all, gs_all, hid_all, gp_all, up_all,
                  wg, wu, wd, s_in_w, gg_ref, x_ref, g_ref, t_ref, o_ref, xr, gs, hid, gp, up, st,
                  w, lp, rx, rxd, ry, ryd, rz,
                  s_in, s_out, s_save, s_p, r_p, s_x, s_y, s_dx, s_dy, s_z, r_x, r_y, r_dx, r_dy, r_z,
                  s_g, r_g, *refs):
    z, x, y, c = place()
    shard, group = lax.axis_index("fsdp"), lax.axis_index("tp")
    expert = shard * 4 + group
    rows, cols = back_ref.shape
    width = x_ref.shape[1]
    half = rows // 2
    blocks = rows // block_rows
    experts = router_ref.shape[1]
    f32, low = jnp.float32, jnp.bfloat16
    partner = device(z, x, y, 1 - c)
    xn, yn = device(z, 1 - x, y, c), device(z, x, 1 - y, c)
    up_dev, down_dev = device(z + 1, x, y, c), device(z - 1, x, y, c)
    n_c, n_s = len(ReduceCols.scratch(16, 128, low)), len(RowSums.scratch(128))
    columns = ReduceCols(attn_part, middle_ref, refs[:n_c])
    sums = RowSums(refs[n_c : n_c + n_s])
    n_g = len(GatherAll.scratch(nz))
    moe_rows = [GatherAll(nz, part, x_all, refs[n_c + n_s + n * n_g : n_c + n_s + (n + 1) * n_g],
                          half // 2, n, 2) for n, part in enumerate(halves(low_ref))]

    def rows_step(name, *args):
        for part in moe_rows:
            getattr(part, name)(*args)

    greet_all(shard, group, 2 * nz, 4)
    columns.start()
    tiles = 2 * nz
    devices = 8 * nz

    def swap(k):
        other = (expert + k) % devices
        return remote(gg_ref.at[other // 4], gg_got.at[expert], s_g.at[k], r_g.at[k],
                      (other // 4, other % 4))

    def tile_of(j):
        return tile_item(nz, z, j // 2) * 2 + jnp.where(j % 2 == 0, 1 - x, x)

    def tile_rows(j):
        return pl.ds(pl.multiple_of(tile_of(j) * rows, rows), rows)

    def load(j):
        return pltpu.make_async_copy(x_all.at[tile_rows(j)], x_ref, s_in.at[0])

    def load_g(j):
        tile = tile_of(j)
        first = pl.ds(pl.multiple_of(tile * rows, half), half)
        second = pl.ds(pl.multiple_of(mirrored(nz, tile) * rows + half, half), half)
        return (pltpu.make_async_copy(g_all.at[first], g_ref.at[pl.ds(0, half)], s_in.at[1]),
                pltpu.make_async_copy(g_all.at[second], g_ref.at[pl.ds(half, half)], s_in.at[3]))

    def load_t(j):
        tile = tile_of(j)
        first = pl.ds(pl.multiple_of(tile * rows, half), half)
        second = pl.ds(pl.multiple_of(mirrored(nz, tile) * rows + half, half), half)
        return (pltpu.make_async_copy(routes_all.at[first], t_ref.at[pl.ds(0, half)], s_in.at[2]),
                pltpu.make_async_copy(routes_all.at[second], t_ref.at[pl.ds(half, half)], s_in.at[4]))

    def save_out(j):
        return pltpu.make_async_copy(o_ref, out_all.at[tile_rows(j)], s_out)

    def saves(j):
        pairs = ((xr, xr_all), (gs, gs_all), (hid, hid_all), (gp, gp_all), (up, up_all))
        return [pltpu.make_async_copy(src, dst.at[j], s_save.at[n])
                for n, (src, dst) in enumerate(pairs)]

    def c_p(zz, rel, slot):
        k = zz * 4 + rel
        return remote(st.at[slot, rel // 2], lp.at[zz, rel], s_p.at[k], r_p.at[k], partner)

    def c_diag(zz):
        return (remote(w.at[zz, 3, pl.ds(0, half)], rxd.at[zz], s_dx.at[zz], r_dx.at[zz], xn),
                remote(w.at[zz, 3, pl.ds(half, half)], ryd.at[zz], s_dy.at[zz], r_dy.at[zz], yn))

    def c_xy(zz):
        return (remote(w.at[zz, 1], rx.at[zz], s_x.at[zz], r_x.at[zz], xn),
                remote(w.at[zz, 2], ry.at[zz], s_y.at[zz], r_y.at[zz], yn))

    def c_z(zz, slot, where):
        return remote(w.at[zz, 0], rz.at[slot], s_z.at[zz], r_z.at[slot], where)

    def send_z(zz):
        pl.when(zz > z)(lambda: c_z(zz, zz, up_dev).start())
        pl.when(zz == z - 1)(lambda: c_z(zz, nz, down_dev).start())
        pl.when(zz < z - 1)(lambda: c_z(zz, zz, down_dev).start())

    def stage_d(zz, rel, slot):
        c_p(zz, rel, slot).wait_recv()
        add_blocks(w.at[zz, rel], [lp.at[zz, rel]], 0, rows)
        if rel == 3:
            for copy in c_diag(zz):
                copy.start()

    def stage_e(zz):
        dx, dy = c_diag(zz)
        cx, cy = c_xy(zz)
        dy.wait_recv()
        add_blocks(w.at[zz, 1], [ryd.at[zz]], half, half)
        cx.start()
        dx.wait_recv()
        add_blocks(w.at[zz, 2], [rxd.at[zz]], 0, half)
        cy.start()

    def passes(zz):
        return ((zz > z) & (z > 0)) | ((zz < z) & (z < nz - 1))

    def stage_f1(zz):
        cx, cy = c_xy(zz)
        cx.wait_recv()
        cy.wait_recv()
        add_blocks(w.at[zz, 0], [rx.at[zz], ry.at[zz]], 0, rows)
        pl.when((zz != z) & jnp.logical_not(passes(zz)))(lambda: send_z(zz))

    def stage_f2(zz):
        @pl.when((zz != z) & passes(zz))
        def _():
            c_z(zz, zz, up_dev).wait_recv()
            add_blocks(w.at[zz, 0], [rz.at[zz]], 0, rows)
            send_z(zz)

        @pl.when(zz == z)
        def _():
            low_part, high_part = rz.at[zz], rz.at[nz]
            pl.when(z > 0)(lambda: c_z(zz, zz, up_dev).wait_recv())
            pl.when(z < nz - 1)(lambda: c_z(zz, nz, down_dev).wait_recv())
            own = w.at[zz, 0]
            pl.when(z == 0)(lambda: add_blocks(own, [high_part], 0, rows, back_ref))
            pl.when(z == nz - 1)(lambda: add_blocks(own, [low_part], 0, rows, back_ref))
            pl.when((z > 0) & (z < nz - 1))(
                lambda: add_blocks(own, [low_part, high_part], 0, rows, back_ref)
            )

    def compute(j):
        zz = tile_item(nz, z, j // 2)
        slot = j % 2
        load(j).wait()
        for copy in load_t(j):
            copy.wait()
        lanes = lax.broadcasted_iota(jnp.int32, (rows, experts), 1)
        routes = t_ref[...]
        chosen = routes[:, 0:1] == lanes
        for n in range(1, TOPK):
            chosen = chosen | (routes[:, n : n + 1] == lanes)
        logits = jnp.where(chosen, dot_plain(x_ref[...], router_ref[...]), masked_score)
        peak = jnp.max(logits, axis=1, keepdims=True)
        weights = jnp.where(chosen, jnp.exp(logits - peak), 0.0)
        gates = weights / jnp.sum(weights, axis=1, keepdims=True)
        gates_ref[...] = gates
        mine = lanes == expert
        gate_col = jnp.sum(jnp.where(mine, gates, 0.0), axis=1, keepdims=True)
        match_col = jnp.sum(jnp.where(mine & chosen, 1.0, 0.0), axis=1, keepdims=True)
        sub = lax.broadcasted_iota(jnp.int32, (block_rows, block_rows), 0)
        lane = lax.broadcasted_iota(jnp.int32, (block_rows, block_rows), 1)
        eye = sub == lane
        before = (sub > lane).astype(f32).astype(low)
        chosen_low = chosen.astype(f32).astype(low)
        pick, put, slot_gate = [], [], []
        slot_lane = lax.broadcasted_iota(jnp.int32, (block_rows, slots), 1).astype(f32)
        slot_sub = lax.broadcasted_iota(jnp.int32, (slots, block_rows), 0).astype(f32)
        for b in range(blocks):
            part = slice(b * block_rows, (b + 1) * block_rows)
            ranks = dot_plain(before, chosen_low[part])
            rank = jnp.sum(jnp.where(mine[part], ranks, 0.0), axis=1, keepdims=True)
            rank = jnp.where(match_col[part] > 0.0, rank, -1.0)
            rank_row = jnp.sum(jnp.where(eye, rank, 0.0), axis=0, keepdims=True)
            gate_row = jnp.sum(jnp.where(eye, gate_col[part], 0.0), axis=0, keepdims=True)
            hot = rank_row == slot_sub
            pick.append(hot.astype(f32).astype(low))
            put.append((rank == slot_lane).astype(f32).astype(low))
            slot_gate.append(jnp.sum(jnp.where(hot, gate_row, 0.0), axis=1, keepdims=True))
        slot_gate = jnp.concatenate(slot_gate, axis=0)

        def gather(ref, at):
            return jnp.concatenate(
                [dot_plain(pick[b], ref[pl.ds(b * block_rows, block_rows), at])
                 for b in range(blocks)],
                axis=0,
            )

        def scatter(ref, at, values):
            for b in range(blocks):
                ref[pl.ds(b * block_rows, block_rows), at] = dot_plain(
                    put[b], values[b * slots : (b + 1) * slots]
                ).astype(low)

        def columns(i):
            return pl.ds(pl.multiple_of(i * cols, cols), cols)

        @pl.when(j > 0)
        def _():
            for copy in saves(j):
                copy.wait()

        def take(i, carry):
            xr[:, columns(i)] = gather(x_ref, columns(i)).astype(low)
            return carry

        lax.fori_loop(0, width // cols, take, 0)

        pl.when(j == 0)(lambda: rows_step('second', 2))
        for k in range(3, nz):
            pl.when(j == 1)(lambda: rows_step('second', k))

        @pl.when((j % 2 == 1) & (j < tiles - 1))
        def _():
            rows_step('ready', tile_item(nz, z, j // 2 + 1))

        @pl.when(j < tiles - 1)
        def _():
            load(j + 1).start()
            for copy in load_t(j + 1):
                copy.start()

        gate_pre = dot_plain(xr[...], wg[...])
        up_pre = dot_plain(xr[...], wu[...])
        sig = jax.nn.sigmoid(gate_pre)
        silu = gate_pre * sig
        hidden_low = (silu * up_pre).astype(low)
        hid[...] = hidden_low
        for copy in load_g(j):
            copy.wait()
        pl.when(j > 0)(lambda: save_out(j).wait())

        def middle_part(i, carry):
            total, hidden_grad = carry
            at = columns(i)
            grad = gather(g_ref, at)
            expert_out = dot_plain(hidden_low, wd[:, at]).astype(low).astype(f32)
            total = total + jnp.sum(grad * expert_out, axis=1, keepdims=True)
            pair_grad = (grad * slot_gate).astype(low)
            gs[:, at] = pair_grad
            scatter(o_ref, at, (expert_out * slot_gate).astype(low))
            return total, hidden_grad + dot_last(pair_grad, wd[:, at])

        gates_grad, hidden_grad = lax.fori_loop(
            0,
            width // cols,
            middle_part,
            (jnp.zeros(slot_gate.shape, f32), jnp.zeros(gate_pre.shape, f32)),
        )
        save_out(j).start()

        @pl.when(j < tiles - 1)
        def _():
            for copy in load_g(j + 1):
                copy.start()

        for b in range(blocks):
            gg_ref[tile_of(j), :, pl.ds(b * block_rows, block_rows)] = jnp.sum(
                pick[b].astype(f32) * gates_grad[b * slots : (b + 1) * slots],
                axis=0,
                keepdims=True,
            )
        gate_grad = (hidden_grad * up_pre * (sig * (1.0 + gate_pre * (1.0 - sig)))).astype(low)
        up_grad = (hidden_grad * silu).astype(low)
        gp[...] = gate_grad
        up[...] = up_grad
        for copy in saves(j):
            copy.start()

        def part_of(i, yy, cc):
            at = columns(yy * 2 + cc)
            row_grad = dot_last(gate_grad, wg[at, :]) + dot_last(up_grad, wu[at, :])
            return row_grad.astype(low)

        first = jnp.where(slot == 0, 1, 0)

        def to_partner(i, carry):
            yy = jnp.where(i == 1, 1 - y, y)
            rel = first + 2 * i

            @pl.when(j >= 2)
            def _():
                before_zz = tile_item(nz, z, j // 2 - 1)
                k = before_zz * 4 + rel
                remote(st.at[slot, i], lp.at[before_zz, rel], s_p.at[k], r_p.at[k], partner).wait_send()

            scatter(st.at[slot, i], slice(None), part_of(i, yy, 1 - c))
            k = zz * 4 + rel
            remote(st.at[slot, i], lp.at[zz, rel], s_p.at[k], r_p.at[k], partner).start()
            return carry

        def to_own(i, carry):
            yy = jnp.where(i == 1, 1 - y, y)
            scatter(w.at[zz, first + 2 * i], slice(None), part_of(i, yy, c))
            return carry

        lax.fori_loop(0, 2, to_partner, 0)
        lax.fori_loop(0, 2, to_own, 0)

    weights = [pltpu.make_async_copy(src, dst, s_in_w.at[n])
               for n, (src, dst) in enumerate(((wg_all, wg), (wu_all, wu), (wd_all, wd)))]
    for copy in load_t(0) + load_g(0) + tuple(weights):
        copy.start()

    corner = diagonal()
    columns.first()
    columns.second()

    def residual(n, carry):
        here = pl.ds(pl.multiple_of(n * 128, 128), 128)
        total = middle_ref[here, :] + tok_ref[here, :].astype(f32)
        middle_ref[here, :] = total
        sums.got[0, pl.ds(n, 1), :] = to_row(jnp.sum(total * total, axis=1, keepdims=True), corner)
        return carry

    def norm(n, carry):
        here = pl.ds(pl.multiple_of(n * 128, 128), 128)
        scale = lax.rsqrt(to_column(sums.total(n), corner) / width + norm_eps)
        scale_ref[here, :] = scale
        gain = gain_ref[:, pl.ds(pl.multiple_of(group * cols, cols), cols)]
        low_ref[here, :] = (middle_ref[here, :] * scale * gain).astype(low)
        return carry

    lax.fori_loop(0, rows // 128, residual, 0)
    sums.start()
    sums.wait()
    lax.fori_loop(0, rows // 128, norm, 0)
    for part in moe_rows:
        part.own().start()
    for part in moe_rows:
        part.own().wait()
    rows_step('first', 0)
    rows_step('first', 1)
    rows_step('second', 0)
    rows_step('first', 2)
    rows_step('second', 1)
    rows_step('third', 0)
    for k in range(3, nz):
        rows_step('first', k)
    rows_step('third', 1)
    rows_step('ready', tile_item(nz, z, 0))
    load(0).start()
    for copy in weights:
        copy.wait()
    schedule = line_schedule(nz)
    last_step = max(max(steps) for steps in schedule)

    def step(j, carry):
        k, odd = j // 2, j % 2 == 1
        pl.when(j < tiles)(lambda: compute(j))
        pl.when(j == 0)(lambda: rows_step('third', 2))
        for n in range(3, nz):
            pl.when(j == 2)(lambda: rows_step('third', n))

        @pl.when(j == tiles)
        def _():
            gg_got[expert] = gg_ref[shard]
            loop_from_one(devices, lambda n: swap(n).start())

        @pl.when(jnp.logical_not(odd) & (k < nz))
        def _():
            zz = tile_item(nz, z, k)
            stage_d(zz, 3, 0)
            stage_d(zz, 1, 0)

        @pl.when(odd & (k < nz))
        def _():
            zz = tile_item(nz, z, k)
            stage_d(zz, 2, 1)
            stage_d(zz, 0, 1)
            stage_e(zz)

        @pl.when((k >= 1) & (k < nz + 1) & jnp.logical_not(odd))
        def _():
            stage_f1(tile_item(nz, z, k - 1))

        for here, steps in enumerate(schedule):
            for at, places in steps.items():
                for to in places:
                    pl.when((z == here) & (j == at))(lambda to=to: stage_f2(jnp.int32(to)))

        return carry

    lax.fori_loop(0, last_step + 1, step, 0)
    loop_from_one(devices, lambda n: swap(n).wait())
    save_out(tiles - 1).wait()
    for copy in saves(tiles - 1):
        copy.wait()
    for slot in range(2):
        for i in range(2):
            c_p(z, 1 - slot + 2 * i, slot).wait_send()

    def finish(zz, carry):
        for copy in c_diag(zz) + c_xy(zz):
            copy.wait_send()
        pl.when(zz != z)(c_z(zz, zz, up_dev).wait_send)
        return carry

    lax.fori_loop(0, nz, finish, 0)
    columns.finish()
    rows_step('finish_sends')


def run_experts(tokens, gain, router, attn_part, g_all, routes_all, gate_w, up_w, down_w, block_rows,
                slots, nz, collective_id):
    total, width = g_all.shape
    hidden = gate_w.shape[1]
    experts = router.shape[1]
    tiles = 2 * nz
    rows, cols = total // tiles, width // 4
    pairs = rows // block_rows * slots
    half = rows // 2
    f32, low = jnp.float32, jnp.bfloat16
    any_space = pl.BlockSpec(memory_space=pl.ANY)
    vmem = pl.BlockSpec(memory_space=pltpu.VMEM)
    vm, dma, shape = pltpu.VMEM, pltpu.SemaphoreType.DMA, jax.ShapeDtypeStruct
    return pl.pallas_call(
        functools.partial(expert_kernel, nz, slots, block_rows),
        in_specs=[vmem] * 3 + [any_space] * 6,
        out_specs=[vmem] * 3 + [any_space] * 2 + [vmem] * 3 + [any_space] * 5,
        out_shape=[
            shape((rows, cols), f32), shape((rows, 1), f32), shape((rows, cols), low),
            shape((total, width), low),
            shape((total, width), low), shape((rows, cols), f32), shape((4 * tiles, 1, rows), f32),
            shape((rows, experts), f32),
            shape((tiles, pairs, width), low), shape((tiles, pairs, width), low),
            shape((tiles, pairs, hidden), low), shape((tiles, pairs, hidden), low),
            shape((tiles, pairs, hidden), low),
        ],
        scratch_shapes=[
            vm((width, hidden), low), vm((width, hidden), low), vm((hidden, width), low), dma((3,)),
            vm((tiles, 1, rows), f32), vm((rows, width), low), vm((rows, width), low),
            vm((rows, routes_all.shape[1]), jnp.int32), vm((rows, width), low),
            vm((pairs, width), low), vm((pairs, width), low),
            vm((pairs, hidden), low), vm((pairs, hidden), low), vm((pairs, hidden), low),
            vm((2, 2, rows, cols), low),
            vm((nz, 4, rows, cols), low), vm((nz, 4, rows, cols), low),
            vm((nz, rows, cols), low), vm((nz, half, cols), low),
            vm((nz, rows, cols), low), vm((nz, half, cols), low),
            vm((nz + 1, rows, cols), low),
            dma((5,)), dma, dma((5,)), dma((4 * nz,)), dma((4 * nz,)),
        ] + [dma((nz,))] * 9 + [dma((nz + 1,))] + [dma((4 * tiles,))] * 2
        + ReduceCols.scratch(rows, cols, low) + RowSums.scratch(rows) + GatherAll.scratch(nz) * 2,
        compiler_params=pltpu.CompilerParams(
            collective_id=collective_id, has_side_effects=True, vmem_limit_bytes=62 << 20
        ),
        name="experts",
    )(tokens, gain, router, attn_part, g_all, routes_all, gate_w, up_w, down_w)


def near_first(nz, z, k):
    return far_first(nz, z, nz - 1 - k)


def halves(ref):
    rows = ref.shape[0] // 2
    return [ref.at[pl.ds(part * rows, rows)] for part in range(2)]


class GatherAll:
    sems = 6

    @staticmethod
    def scratch(nz):
        dma = pltpu.SemaphoreType.DMA
        return [dma] + [dma((5 * nz,))] * 2 + [dma((nz,))] * 11

    def __init__(self, nz, src, out, sems, cut, part=0, parts=1):
        (self.lsem, self.s_p, self.r_p, self.s_u, self.s_d, self.s_x, self.s_y, self.s_dx,
         self.s_dy, self.r_z, self.r_x, self.r_y, self.r_dx, self.r_dy) = sems
        self.nz, self.src, self.out, self.cut = nz, src, out, cut
        self.rows, self.cols = src.shape
        self.offset, self.stride = part * self.rows, parts * self.rows
        self.place = z, x, y, c = place()
        self.partner, self.xn, self.yn = (
            device(z, x, y, 1 - c), device(z, 1 - x, y, c), device(z, x, 1 - y, c))
        self.up, self.down = device(z + 1, x, y, c), device(z - 1, x, y, c)

    def block(self, zz, xx, yy, cc, part=None):
        start, size, unit = (zz * 2 + xx) * self.stride + self.offset, self.rows, self.rows
        if part == 0:
            size, unit = self.cut, self.rows
        elif part == 1:
            start, size = start + self.cut, self.rows - self.cut
            unit = math.gcd(self.cut, self.rows)
        return self.out.at[pl.ds(pl.multiple_of(start, unit), size),
                           pl.ds(pl.multiple_of((yy * 2 + cc) * self.cols, self.cols), self.cols)]

    def own(self):
        z, x, y, c = self.place
        return pltpu.make_async_copy(self.src, self.block(z, x, y, c), self.lsem)

    def line(self, zz):
        z, x, y, c = self.place
        here = self.block(zz, x, y, c)
        return (remote(here, here, self.s_u.at[zz], self.r_z.at[zz], self.up),
                remote(here, here, self.s_d.at[zz], self.r_z.at[zz], self.down))

    def sides(self, zz):
        z, x, y, c = self.place
        here = self.block(zz, x, y, c)
        return (remote(here, here, self.s_x.at[zz], self.r_x.at[zz], self.xn),
                remote(here, here, self.s_y.at[zz], self.r_y.at[zz], self.yn))

    def across(self, zz):
        z, x, y, c = self.place
        copies = []
        if self.cut > 0:
            here = self.block(zz, 1 - x, y, c, 0)
            copies.append(remote(here, here, self.s_dy.at[zz], self.r_dy.at[zz], self.yn))
        if self.cut < self.rows:
            here = self.block(zz, x, 1 - y, c, 1)
            copies.append(remote(here, here, self.s_dx.at[zz], self.r_dx.at[zz], self.xn))
        return copies

    def pair(self, zz, rel, mine=True):
        z, x, y, c = self.place
        xx = 1 - x if rel in (1, 3, 4) else x
        yy = 1 - y if rel in (2, 3, 4) else y
        here = self.block(zz, xx, yy, c if mine else 1 - c, {3: 0, 4: 1}.get(rel))
        k = zz * 5 + rel
        return remote(here, here, self.s_p.at[k], self.r_p.at[k], self.partner)

    def parts(self):
        return [0, 1, 2] + [3] * (self.cut > 0) + [4] * (self.cut < self.rows)

    def first(self, k):
        self.first_to(near_first(self.nz, self.place[0], k))

    def second(self, k):
        self.second_to(near_first(self.nz, self.place[0], k))

    def third(self, k):
        self.third_to(near_first(self.nz, self.place[0], k))

    def first_to(self, zz):
        z = self.place[0]
        up, down = self.line(zz)
        pl.when(zz != z)(lambda: up.wait_recv())
        pl.when((zz <= z) & (z < self.nz - 1))(lambda: up.start())
        pl.when((zz >= z) & (z > 0))(lambda: down.start())
        for copy in self.sides(zz):
            copy.start()
        self.pair(zz, 0).start()

    def second_to(self, zz):
        to_x, to_y = self.sides(zz)
        across = self.across(zz)
        to_x.wait_recv()
        if self.cut > 0:
            across[0].start()
        self.pair(zz, 1).start()
        to_y.wait_recv()
        if self.cut < self.rows:
            across[-1].start()
        self.pair(zz, 2).start()

    def third_to(self, zz):
        across = self.across(zz)
        for rel, copy in zip(self.parts()[3:], across):
            copy.wait_recv()
            self.pair(zz, rel).start()

    def ready(self, zz):
        for rel in self.parts():
            self.pair(zz, rel, False).wait_recv()

    def finish_sends(self):
        z = self.place[0]

        def step(zz, carry):
            for rel in self.parts():
                self.pair(zz, rel).wait_send()
            up, down = self.line(zz)
            pl.when((zz <= z) & (z < self.nz - 1))(lambda: up.wait_send())
            pl.when((zz >= z) & (z > 0))(lambda: down.wait_send())
            for copy in tuple(self.sides(zz)) + tuple(self.across(zz)):
                copy.wait_send()
            return carry

        lax.fori_loop(0, self.nz, step, 0)

    def finish(self):
        def step(zz, carry):
            self.ready(zz)
            return carry

        lax.fori_loop(0, self.nz, step, 0)
        self.finish_sends()


class GatherCausal:
    @staticmethod
    def scratch(nz):
        dma = pltpu.SemaphoreType.DMA
        return [dma, dma, dma((2,)), dma((2 * nz,)), dma((2 * nz,)), dma((2 * nz,))]

    def __init__(self, nz, src, out, held, sems):
        self.s_x, self.r_x, self.lsem, self.s_z, self.r_z, self.l_z = sems
        self.nz, self.src, self.out, self.held_ref = nz, src, out, held
        self.place = z, x, y, c = place()
        self.xn = device(z, 1 - x, y, c)
        self.near = (device(z + 1, x, y, c), device(z - 1, x, y, c))

    def own(self):
        z, x = self.place[:2]
        return [pltpu.make_async_copy(self.src, self.out.at[z, x], self.lsem.at[0]),
                pltpu.make_async_copy(self.src, self.held_ref.at[z, x], self.lsem.at[1])]

    def side(self):
        z, x = self.place[:2]
        return remote(self.src, self.out.at[z, x], self.s_x, self.r_x, self.xn)

    def line(self, zz, micro):
        here = self.out.at[zz, :, micro]
        return remote(here, here, self.s_z.at[zz * 2 + micro], self.r_z.at[zz * 2 + micro],
                      self.near[micro])

    def keep(self, zz, micro):
        return pltpu.make_async_copy(self.out.at[zz, :, micro], self.held_ref.at[zz, :, micro],
                                     self.l_z.at[zz * 2 + micro])

    def needed(self, zz, micro):
        return zz <= self.place[0] if micro == 0 else zz >= self.place[0]

    def sends(self, zz, micro):
        z = self.place[0]
        return self.needed(zz, micro) & (z < self.nz - 1 if micro == 0 else z > 0)

    def first_to(self, zz):
        z = self.place[0]

        @pl.when(zz == z)
        def _():
            for copy in self.own():
                copy.wait()
            self.side().wait_recv()

        for micro in range(2):
            pl.when((zz != z) & self.needed(zz, micro))(lambda: self.line(zz, micro).wait_recv())
            pl.when(self.sends(zz, micro))(lambda: self.line(zz, micro).start())
            pl.when(self.needed(zz, micro))(lambda: self.keep(zz, micro).start())

    def ready(self, zz):
        for micro in range(2):
            pl.when(self.needed(zz, micro))(lambda: self.keep(zz, micro).wait())

    def finish(self):
        self.side().wait_send()

        def step(zz, carry):
            for micro in range(2):
                pl.when(self.sends(zz, micro))(lambda: self.line(zz, micro).wait_send())
            return carry

        lax.fori_loop(0, self.nz, step, 0)


class GatherRows:
    @staticmethod
    def scratch(nz):
        dma = pltpu.SemaphoreType.DMA
        return [dma] + [dma((nz,))] * 5

    def __init__(self, nz, src, out, sems, part=0, parts=1):
        self.lsem, self.s_u, self.s_d, self.s_x, self.r_z, self.r_x = sems
        self.nz, self.src, self.out = nz, src, out
        self.offset, self.stride = part * src.shape[0], parts * src.shape[0]
        self.place = z, x, y, c = place()
        self.xn = device(z, 1 - x, y, c)
        self.up, self.down = device(z + 1, x, y, c), device(z - 1, x, y, c)

    def block(self, zz):
        rows = self.src.shape[0]
        start = (zz * 2 + self.place[1]) * self.stride + self.offset
        return self.out.at[pl.ds(pl.multiple_of(start, rows), rows)]

    def own(self):
        return pltpu.make_async_copy(self.src, self.block(self.place[0]), self.lsem)

    def copies(self, zz):
        here = self.block(zz)
        return (remote(here, here, self.s_u.at[zz], self.r_z.at[zz], self.up),
                remote(here, here, self.s_d.at[zz], self.r_z.at[zz], self.down),
                remote(here, here, self.s_x.at[zz], self.r_x.at[zz], self.xn))

    def first_to(self, zz):
        z = self.place[0]
        up, down, to_x = self.copies(zz)
        pl.when(zz != z)(lambda: up.wait_recv())
        pl.when((zz <= z) & (z < self.nz - 1))(lambda: up.start())
        pl.when((zz >= z) & (z > 0))(lambda: down.start())
        to_x.start()

    def finish(self):
        z = self.place[0]

        def step(zz, carry):
            up, down, to_x = self.copies(zz)
            to_x.wait()
            pl.when((zz <= z) & (z < self.nz - 1))(lambda: up.wait_send())
            pl.when((zz >= z) & (z > 0))(lambda: down.wait_send())
            return carry

        lax.fori_loop(0, self.nz, step, 0)


def mirrored(nz, shard):
    return (nz - 1 - shard // 2) * 2 + shard % 2


def stream_unit(u, nz):
    shard = lax.axis_index("fsdp")
    later = u > shard
    micro = jnp.where(later, 1, 0)
    here = jnp.where(later, mirrored(nz, shard), shard)
    key_place = here - jnp.where(later, u - shard - 1, u)
    owner = jnp.where(later, mirrored(nz, key_place), key_place)
    return micro, here, key_place, owner


def key_bias(micro, here, key_place, block, start_ref):
    key = key_place * block + lax.broadcasted_iota(jnp.int32, (block, block), 0)
    query = here * block + lax.broadcasted_iota(jnp.int32, (block, block), 1)
    return jnp.where((key >= start_ref[micro]) & (key <= query), 0.0, masked_score)


def norm_turn(raw, gain, cosine, sine):
    scale = lax.rsqrt(jnp.mean(raw * raw, axis=1, keepdims=True) + norm_eps)
    normed = raw * scale * gain
    return normed * cosine + pltpu.roll(normed, raw.shape[1] // 2, 1) * sine


def attend_kernel(nz, gain_ref, gq_ref, gk_ref, cos_ref, sin_ref, start_ref, cot_ref, wo_ref,
                  tok_all, wq_all, wk_all, wv_all,
                  normed, scale_ref, q_pre, k_pre, q_ref, heads_ref, lse_ref, kv_all, cot_all, wo_all,
                  tok_ref, wq, wk, wv, s_in, kv_ref, kv, acc, peak, total, *sems):
    shards = 2 * nz
    width = kv_ref.shape[2] // 2
    block = q_ref.shape[0] // 2
    low = jnp.bfloat16
    heads = q_ref.shape[1] // width
    z, x, y, c = place()
    n_c, n_o = len(GatherAll.scratch(nz)), len(GatherRows.scratch(nz))
    end = 2 * (n_c + n_o)
    cots = [GatherAll(nz, half, cot_all, sems[n * n_c : (n + 1) * n_c], half.shape[0], n, 2)
            for n, half in enumerate(halves(cot_ref))]
    outs = [GatherRows(nz, half, wo_all, sems[2 * n_c + n * n_o : 2 * n_c + (n + 1) * n_o], n, 2)
            for n, half in enumerate(halves(wo_ref))]
    keys_in = GatherCausal(nz, kv_ref, kv_all, kv, sems[end:])
    greet([(None, cots[0].partner), (None, cots[0].xn), (None, cots[0].yn),
           (z < nz - 1, cots[0].up), (z > 0, cots[0].down)])
    for part in outs + cots:
        part.own().start()
    fetches = [pltpu.make_async_copy(src, dst, s_in.at[n]) for n, (src, dst) in enumerate((
        (tok_all, tok_ref), (wk_all, wk), (wv_all, wv), (wq_all, wq)))]
    for copy in fetches:
        copy.start()
    for part in outs + cots:
        part.own().wait()
    for part in cots:
        part.first_to(z)
    fetches[0].wait()

    def token_norm(n, carry):
        rows = pl.ds(pl.multiple_of(n * 64, 64), 64)
        row = tok_ref[rows, :].astype(jnp.float32)
        scale = lax.rsqrt(jnp.mean(row * row, axis=1, keepdims=True) + norm_eps)
        scale_ref[rows, :] = scale
        normed[rows, :] = (row * scale * gain_ref[...]).astype(low)
        return carry

    lax.fori_loop(0, tok_ref.shape[0] // 64, token_norm, 0)
    fetches[1].wait()
    k_pre[...] = dot_plain(normed[...], wk[...])
    turned = norm_turn(k_pre[...], gk_ref[...], cos_ref[...], sin_ref[...]).astype(low)
    fetches[2].wait()
    value = dot_plain(normed[...], wv[...]).astype(low)
    for micro in range(2):
        rows = slice(micro * block, (micro + 1) * block)
        kv_ref[micro, :, :width] = turned[rows]
        kv_ref[micro, :, width:] = value[rows]
    keys_in.side().start()
    for copy in keys_in.own():
        copy.start()
    peak[...] = jnp.full(peak.shape, masked_score, jnp.float32)
    total[...] = jnp.zeros_like(total)
    acc[...] = jnp.zeros_like(acc)
    fetches[3].wait()

    def at_distance(dist, fn):
        for side in (-1, 1):
            zz = z + side * dist
            valid = (dist >= 0) & (zz >= 0) & (zz < nz) & ((dist > 0) | (side > 0))
            pl.when(valid)(lambda: fn(zz))

    def tick(u, carry):
        def gradients(zz):
            @pl.when(u > 0)
            def _():
                for part in cots:
                    part.first_to(zz)

        def weights(zz):
            for part in outs:
                part.first_to(zz)

        def across(zz):
            for part in cots:
                part.second_to(zz)

        def onward(zz):
            for part in cots:
                part.third_to(zz)

        at_distance(u, keys_in.first_to)
        at_distance(u, gradients)
        at_distance(u, weights)
        at_distance(u - 1, across)
        at_distance(u - 2, onward)
        at_distance(u - 1, attend_item)
        return carry

    def attend_item(zz):
        own = zz == z
        keys_in.ready(zz)

        def part(i, carry):
            micro = jnp.where(own, i // 2, jnp.where(zz < z, 0, 1))
            xx = jnp.where(own, jnp.where(i % 2 == 0, x, 0), i)
            valid = jnp.where(own, jnp.where((i % 2 == 0) | (x == 1), 1, 0), jnp.where(i < 2, 1, 0))
            pl.when(valid == 1)(lambda: attention(micro, zz, xx))
            return carry

        lax.fori_loop(0, 4, part, 0)

    def attention(micro, zz, xx):
        def at_place(z_at, x_at):
            return jnp.where(micro == 0, z_at, nz - 1 - z_at) * 2 + x_at

        here, key_place = at_place(z, x), at_place(zz, xx)
        bias = key_bias(micro, here, key_place, block, start_ref)
        both = kv.at[zz, xx, micro]
        keys, values = both[:, :width], both[:, width:]
        q_rows = pl.ds(pl.multiple_of(micro * block, block), block)

        def head(h, carry):
            at = micro * heads + h
            query = q_ref[q_rows, pl.ds(pl.multiple_of(h * width, width), width)]
            scores = dot_last(keys, query) * width ** (-0.5) + bias
            before = peak[at]
            now = jnp.maximum(before, jnp.max(scores, axis=0, keepdims=True))
            weights = jnp.exp(scores - now)
            factor = jnp.exp(before - now)
            peak[at] = now
            total[at] = total[at] * factor + jnp.sum(weights, axis=0, keepdims=True)
            acc[at] = acc[at] * factor + dot_first(values, weights.astype(jnp.bfloat16))
            return carry

        lax.fori_loop(0, heads, head, 0, unroll=4)

    def prepare(n, carry):
        pair = pl.ds(pl.multiple_of(n * 2 * width, 2 * width), 2 * width)
        q_pre[:, pair] = dot_plain(normed[...], wq[:, pair])
        for h in range(2):
            cols = pl.ds(pl.multiple_of((n * 2 + h) * width, width), width)
            q_ref[:, cols] = norm_turn(
                q_pre[:, cols], gq_ref[...], cos_ref[...], sin_ref[...]
            ).astype(low)
        return carry

    lax.fori_loop(0, heads // 2, prepare, 0)
    tick(0, 0)
    lax.fori_loop(1, nz + 2, tick, 0)

    def close(at, carry):
        micro, h = at // heads, at % heads
        result = (acc[at] / total[at]).T
        here = pl.ds(pl.multiple_of(micro * block, block), block)
        cols = pl.ds(pl.multiple_of(h * width, width), width)
        heads_ref[here, cols] = result.astype(jnp.bfloat16)
        lse_ref[at] = peak[at] + jnp.log(total[at])
        return carry

    lax.fori_loop(0, 2 * heads, close, 0)
    keys_in.finish()
    for part in outs + cots:
        part.finish()


def attend(tokens, gain_attn, wq_all, wk_all, wv_all, gain_query, gain_key, cosine, sine, starts,
           cotangent, w_out, nz, collective_id):
    rows, features = tokens.shape
    columns, width = wq_all.shape[1], wk_all.shape[1]
    heads = columns // width
    block = rows // 2
    any_space = pl.BlockSpec(memory_space=pl.ANY)
    vmem = pl.BlockSpec(memory_space=pltpu.VMEM)
    vm, shape, f32, low = pltpu.VMEM, jax.ShapeDtypeStruct, jnp.float32, jnp.bfloat16
    return pl.pallas_call(
        functools.partial(attend_kernel, nz),
        in_specs=[vmem] * 8 + [any_space] * 4,
        out_specs=[vmem] * 7 + [any_space] * 3,
        out_shape=[
            shape((rows, features), low), shape((rows, 1), f32),
            shape((rows, columns), f32), shape((rows, width), f32),
            shape((rows, columns), low), shape((rows, columns), low),
            shape((2 * heads, 1, block), f32),
            shape((nz, 2, 2, block, 2 * width), low),
            shape((rows * 2 * nz, cotangent.shape[1] * 4), cotangent.dtype),
            shape((w_out.shape[0] * 2 * nz, w_out.shape[1]), w_out.dtype),
        ],
        scratch_shapes=[
            vm((rows, features), low), vm(wq_all.shape, low), vm(wk_all.shape, low),
            vm(wv_all.shape, low), pltpu.SemaphoreType.DMA((4,)),
            vm((2, block, 2 * width), low), vm((nz, 2, 2, block, 2 * width), low),
            vm((2 * heads, width, block), f32), vm((2 * heads, 1, block), f32),
            vm((2 * heads, 1, block), f32),
        ] + GatherAll.scratch(nz) * 2 + GatherRows.scratch(nz) * 2 + GatherCausal.scratch(nz),
        compiler_params=pltpu.CompilerParams(
            collective_id=collective_id, has_side_effects=True, vmem_limit_bytes=62 << 20
        ),
        name="attend",
    )(gain_attn, gain_query, gain_key, cosine, sine, starts, cotangent, w_out, tokens, wq_all, wk_all,
      wv_all)


class ScatterAll:
    @staticmethod
    def scratch(nz, rows, cols, kind, cut):
        vm, dma = pltpu.VMEM, pltpu.SemaphoreType.DMA
        return [
            vm((nz, 4, rows, cols), kind), vm((nz, 4, rows, cols), kind),
            vm((nz, rows, cols), kind), vm((nz, max(cut, 16), cols), kind),
            vm((nz, rows, cols), kind), vm((nz, max(rows - cut, 16), cols), kind),
            vm((nz + 1, rows, cols), kind),
        ] + [dma((4 * nz,))] * 3 + [dma((nz,))] * 9 + [dma((nz + 1,))]

    def __init__(self, nz, partial, out, refs, cut, part=0, parts=1):
        (self.w, self.lp, self.rx, self.rxd, self.ry, self.ryd, self.rz,
         self.s_l, self.s_p, self.r_p, self.s_x, self.s_y, self.s_dx, self.s_dy, self.s_z,
         self.r_x, self.r_y, self.r_dx, self.r_dy, self.r_z) = refs
        self.nz, self.partial, self.out, self.cut = nz, partial, out, cut
        self.rows, self.cols = out.shape
        self.offset, self.stride = part * self.rows, parts * self.rows
        self.place = z, x, y, c = place()
        self.partner, self.xn, self.yn = (
            device(z, x, y, 1 - c), device(z, 1 - x, y, c), device(z, x, 1 - y, c))
        self.up, self.down = device(z + 1, x, y, c), device(z - 1, x, y, c)

    def block(self, zz, rel, cc):
        z, x, y, c = self.place
        xx = 1 - x if rel in (1, 3) else x
        yy = 1 - y if rel in (2, 3) else y
        return self.partial.at[
            pl.ds(pl.multiple_of((zz * 2 + xx) * self.stride + self.offset, self.rows), self.rows),
            pl.ds(pl.multiple_of((yy * 2 + cc) * self.cols, self.cols), self.cols)]

    def pair(self, zz, rel):
        k = zz * 4 + rel
        return remote(self.block(zz, rel, 1 - self.place[3]), self.lp.at[zz, rel],
                      self.s_p.at[k], self.r_p.at[k], self.partner)

    def load(self, zz, rel):
        return pltpu.make_async_copy(
            self.block(zz, rel, self.place[3]), self.w.at[zz, rel], self.s_l.at[zz * 4 + rel])

    def across(self, zz):
        copies = []
        if self.cut > 0:
            copies.append(remote(self.w.at[zz, 3, pl.ds(0, self.cut)], self.rxd.at[zz],
                                 self.s_dx.at[zz], self.r_dx.at[zz], self.xn))
        if self.cut < self.rows:
            copies.append(remote(self.w.at[zz, 3, pl.ds(self.cut, self.rows - self.cut)],
                                 self.ryd.at[zz], self.s_dy.at[zz], self.r_dy.at[zz], self.yn))
        return copies

    def sides(self, zz):
        return (remote(self.w.at[zz, 1], self.rx.at[zz], self.s_x.at[zz], self.r_x.at[zz], self.xn),
                remote(self.w.at[zz, 2], self.ry.at[zz], self.s_y.at[zz], self.r_y.at[zz], self.yn))

    def line(self, zz, slot, where):
        return remote(self.w.at[zz, 0], self.rz.at[slot], self.s_z.at[zz], self.r_z.at[slot], where)

    def start(self):
        def step(k, carry):
            zz = far_first(self.nz, self.place[0], k)
            for rel in (3, 1, 2, 0):
                self.pair(zz, rel).start()
                self.load(zz, rel).start()
            return carry

        lax.fori_loop(0, self.nz, step, 0)

    def first(self, k):
        zz = far_first(self.nz, self.place[0], k)
        for rel in (3, 1, 2, 0):
            self.pair(zz, rel).wait_recv()
            self.load(zz, rel).wait()
            add_blocks(self.w.at[zz, rel], [self.lp.at[zz, rel]], 0, self.rows)
            if rel == 3:
                for copy in self.across(zz):
                    copy.start()

    def second(self, k):
        zz = far_first(self.nz, self.place[0], k)
        across, (to_x, to_y) = self.across(zz), self.sides(zz)
        if self.cut < self.rows:
            across[-1].wait_recv()
            add_blocks(self.w.at[zz, 1], [self.ryd.at[zz]], self.cut, self.rows - self.cut)
        to_x.start()
        if self.cut > 0:
            across[0].wait_recv()
            add_blocks(self.w.at[zz, 2], [self.rxd.at[zz]], 0, self.cut)
        to_y.start()

    def send_line(self, zz):
        z = self.place[0]
        pl.when(zz > z)(lambda: self.line(zz, zz, self.up).start())
        pl.when(zz == z - 1)(lambda: self.line(zz, self.nz, self.down).start())
        pl.when(zz < z - 1)(lambda: self.line(zz, zz, self.down).start())

    def passes(self, zz):
        z = self.place[0]
        return ((zz > z) & (z > 0)) | ((zz < z) & (z < self.nz - 1))

    def third(self, k):
        zz, z = far_first(self.nz, self.place[0], k), self.place[0]
        to_x, to_y = self.sides(zz)
        to_x.wait_recv()
        to_y.wait_recv()
        add_blocks(self.w.at[zz, 0], [self.rx.at[zz], self.ry.at[zz]], 0, self.rows)
        pl.when((zz != z) & jnp.logical_not(self.passes(zz)))(lambda: self.send_line(zz))

    def fourth(self, k):
        zz, z, nz = far_first(self.nz, self.place[0], k), self.place[0], self.nz

        @pl.when((zz != z) & self.passes(zz))
        def _():
            self.line(zz, zz, self.up).wait_recv()
            add_blocks(self.w.at[zz, 0], [self.rz.at[zz]], 0, self.rows)
            self.send_line(zz)

        @pl.when(zz == z)
        def _():
            finish_line(self, self.w.at[zz, 0], zz)

    def finish(self):
        z = self.place[0]

        def step(zz, carry):
            for rel in range(4):
                self.pair(zz, rel).wait_send()
            for copy in tuple(self.across(zz)) + tuple(self.sides(zz)):
                copy.wait_send()
            pl.when(zz != z)(lambda: self.line(zz, zz, self.up).wait_send())
            return carry

        lax.fori_loop(0, self.nz, step, 0)


def finish_line(self, own, zz):
    z, nz = self.place[0], self.nz
    below, above = self.rz.at[zz], self.rz.at[nz]
    pl.when(z > 0)(lambda: self.line(zz, zz, self.up).wait_recv())
    pl.when(z < nz - 1)(lambda: self.line(zz, nz, self.down).wait_recv())
    pl.when(z == 0)(lambda: add_blocks(own, [above], 0, self.rows, self.out))
    pl.when(z == nz - 1)(lambda: add_blocks(own, [below], 0, self.rows, self.out))
    pl.when((z > 0) & (z < nz - 1))(lambda: add_blocks(own, [below, above], 0, self.rows, self.out))


class ReduceRows:
    @staticmethod
    def scratch(nz, rows, cols, kind):
        vm, dma = pltpu.VMEM, pltpu.SemaphoreType.DMA
        return [vm((nz, rows, cols), kind), vm((nz, rows, cols), kind), vm((nz, rows, cols), kind),
                vm((nz + 1, rows, cols), kind)] + [dma((nz,))] * 3 + [dma((nz + 1,))]

    def __init__(self, nz, left, right, out, refs, part=0, parts=1):
        self.w, self.sent, self.rx, self.rz, self.s_x, self.s_z, self.r_x, self.r_z = refs
        self.nz, self.left, self.right, self.out = nz, left, right, out
        self.rows = out.shape[0]
        self.offset, self.stride = part * self.rows, parts * self.rows
        self.place = z, x, y, c = place()
        self.xn = device(z, 1 - x, y, c)
        self.up, self.down = device(z + 1, x, y, c), device(z - 1, x, y, c)

    def make(self, zz, xx, ref):
        start = (zz * 2 + xx) * self.stride + self.offset
        at = pl.ds(pl.multiple_of(start, self.rows), self.rows)
        ref[...] = dot_first(self.left[:, at], self.right[...]).astype(ref.dtype)

    def side(self, zz):
        return remote(self.sent.at[zz], self.rx.at[zz], self.s_x.at[zz], self.r_x.at[zz], self.xn)

    def line(self, zz, slot, where):
        return remote(self.w.at[zz], self.rz.at[slot], self.s_z.at[zz], self.r_z.at[slot], where)

    def start(self):
        def step(k, carry):
            self.send(k)
            return carry

        lax.fori_loop(0, self.nz, step, 0)

    def send(self, k):
        zz, x = far_first(self.nz, self.place[0], k), self.place[1]
        self.make(zz, 1 - x, self.sent.at[zz])
        self.side(zz).start()
        self.make(zz, x, self.w.at[zz])

    send_line = ScatterAll.send_line
    passes = ScatterAll.passes

    def first(self, k):
        zz, z = far_first(self.nz, self.place[0], k), self.place[0]
        self.side(zz).wait_recv()
        add_blocks(self.w.at[zz], [self.rx.at[zz]], 0, self.rows)
        pl.when((zz != z) & jnp.logical_not(self.passes(zz)))(lambda: self.send_line(zz))

    def second(self, k):
        zz, z, nz = far_first(self.nz, self.place[0], k), self.place[0], self.nz

        @pl.when((zz != z) & self.passes(zz))
        def _():
            self.line(zz, zz, self.up).wait_recv()
            add_blocks(self.w.at[zz], [self.rz.at[zz]], 0, self.rows)
            self.send_line(zz)

        @pl.when(zz == z)
        def _():
            finish_line(self, self.w.at[zz], zz)

    def finish(self):
        z = self.place[0]

        def step(zz, carry):
            self.side(zz).wait_send()
            pl.when(zz != z)(lambda: self.line(zz, zz, self.up).wait_send())
            return carry

        lax.fori_loop(0, self.nz, step, 0)


class ReduceCausal:
    @staticmethod
    def scratch(nz, rows, cols, kind):
        vm, dma = pltpu.VMEM, pltpu.SemaphoreType.DMA
        return [vm((nz, 2, 2, rows, cols), kind), vm((2, rows, cols), kind),
                dma((2 * nz,)), dma((2 * nz,)), dma((2,)), dma((2,))]

    def __init__(self, nz, sides, out, refs):
        self.got, self.across, self.s_z, self.r_z, self.s_x, self.r_x = refs
        self.nz, self.sides, self.out = nz, sides, out
        self.place = z, x, y, c = place()
        self.xn = device(z, 1 - x, y, c)
        self.to = (device(z - 1, x, y, c), device(z + 1, x, y, c))

    def line(self, zz, micro):
        k = zz * 2 + micro
        return remote(self.sides.at[zz, :, micro], self.got.at[zz, :, micro],
                      self.s_z.at[k], self.r_z.at[k], self.to[micro])

    def side(self, micro):
        z, x = self.place[:2]
        return remote(self.sides.at[z, 1 - x, micro], self.across.at[micro],
                      self.s_x.at[micro], self.r_x.at[micro], self.xn)

    def take(self, zz, micro):
        first = self.place[0] == (self.nz - 1 if micro == 0 else 0)

        @pl.when(jnp.logical_not(first))
        def _():
            self.line(zz, micro).wait_recv()
            for xx in range(2):
                add_blocks(self.sides.at[zz, xx, micro], [self.got.at[zz, xx, micro]], 0,
                           self.sides.shape[3])

    def turn(self, hop):
        z, nz = self.place[0], self.nz
        for micro in range(2):
            @pl.when(hop == (nz - 1 - z if micro == 0 else z))
            def _():
                def step(n, carry):
                    zz = n if micro == 0 else nz - 1 - n
                    self.take(zz, micro)
                    self.line(zz, micro).start()
                    return carry

                lax.fori_loop(0, z if micro == 0 else nz - 1 - z, step, 0)
                self.take(z, micro)
                self.side(micro).start()

    def finish(self):
        z, x = self.place[:2]
        for micro in range(2):
            self.side(micro).wait_recv()
            add_blocks(self.sides.at[z, x, micro], [self.across.at[micro]], 0, self.sides.shape[3],
                       self.out.at[micro])
        for micro in range(2):
            self.side(micro).wait_send()

            def step(n, carry):
                self.line(n if micro == 0 else self.nz - 1 - n, micro).wait_send()
                return carry

            lax.fori_loop(0, z if micro == 0 else self.nz - 1 - z, step, 0)


def norm_turn_back(turned, raw, gain, cosine, sine):
    grad = turned * cosine + pltpu.roll(turned * sine, raw.shape[1] // 2, 1)
    scale = lax.rsqrt(jnp.mean(raw * raw, axis=1, keepdims=True) + norm_eps)
    inner = grad * gain
    mean = jnp.mean(raw * inner, axis=1, keepdims=True)
    return (scale * inner - raw * (scale * scale * scale * mean),
            jnp.sum(grad * raw * scale, axis=0, keepdims=True))


def attend_back_kernel(nz, k_pre, gk_ref, gq_ref, cos_ref, sin_ref, start_ref, lse_ref, scale_ref,
                       gates_ref, gg_ref, router_all, gain_ref, moe_ref,
                       middle_all, back_all, cot_part, cot_all, wo_all, heads_all, q_all, kv_all, pre_all,
                       out_part, mid_out, q_grad, gain_grad, out_sum, wo_sum, small_out,
                       router_ref, low_ref, mid_ref, wo_ref, heads_ref, q_ref, kv_ref,
                       small_ref, split_ref, grad_ref, delta_ref, q_pre, s_in, s_t, r_t,
                       kv_sum, sides, acc, k_acc, v_acc, *refs):
    middle_ref, inner_ref = (q_pre.at[:, pl.ds(n * mid_out.shape[1], mid_out.shape[1])]
                             for n in range(2))
    shards = 2 * nz
    shard = lax.axis_index("fsdp")
    width = kv_ref.shape[4] // 2
    block = q_ref.shape[0] // 2
    heads = q_ref.shape[1] // width
    z, x, y, c = place()
    count = shards + 2 * x
    low = jnp.bfloat16
    n_o, n_w = len(ScatterAll.scratch(nz, 16, 128, low, 0)), len(ReduceRows.scratch(nz, 16, 128, low))
    end = 2 * (n_o + n_w)
    outs = [ScatterAll(nz, out_part, half, refs[n * n_o : (n + 1) * n_o], 0, n, 2)
            for n, half in enumerate(halves(out_sum))]
    weights = [ReduceRows(nz, mid_ref, heads_ref, half,
                          refs[2 * n_o + n * n_w : 2 * n_o + (n + 1) * n_w], n, 2)
               for n, half in enumerate(halves(wo_sum))]
    last = end + len(SmallSums.scratch(nz, (8, 128), jnp.float32))
    smalls = SmallSums(nz, small_ref, small_out, refs[end:last])
    final = last + len(ReduceCausal.scratch(nz, 16, 128, low))
    keys_out = ReduceCausal(nz, sides, kv_sum, refs[last:final])
    sums = RowSums(refs[final:])
    greet_all(lax.axis_index("fsdp"), lax.axis_index("tp"), shards, 4)
    for part in outs:
        part.start()
    group = lax.axis_index("tp")
    rows, cols = mid_out.shape
    half = rows // 2
    mine = pl.ds(pl.multiple_of(group * cols, cols), cols)
    there = pl.ds(pl.multiple_of(mirrored(nz, shard) * rows + half, half), half)
    fetches = [pltpu.make_async_copy(src, dst, s_in.at[n]) for n, (src, dst) in enumerate((
        (router_all.at[mine], router_ref), (middle_all, middle_ref), (back_all, inner_ref),
        (cot_part.at[pl.ds(0, half)], low_ref.at[pl.ds(0, half)]),
        (cot_all.at[there, mine], low_ref.at[pl.ds(half, half)]),
        (wo_all.at[:, pl.ds(0, wo_ref.shape[1])], wo_ref),
        (heads_all, heads_ref), (q_all, q_ref), (kv_all, kv_ref), (pre_all, q_pre)))]
    for copy in fetches[:-1]:
        copy.start()

    sides[...] = jnp.zeros_like(sides)
    acc[...] = jnp.zeros_like(acc)

    def attention(u):
        micro, here, key_place, owner = stream_unit(u, nz)
        bias = key_bias(micro, here, key_place, block, start_ref)
        both = kv_ref.at[owner // 2, owner % 2, micro]
        keys, values = both[:, :width], both[:, width:]
        q_rows = pl.ds(pl.multiple_of(micro * block, block), block)
        k_acc[...] = jnp.zeros_like(k_acc)
        v_acc[...] = jnp.zeros_like(v_acc)

        def head(h, carry):
            at = micro * heads + h
            cols = pl.ds(pl.multiple_of(h * width, width), width)
            query, grad = q_ref[q_rows, cols], grad_ref[q_rows, cols]
            scores = dot_last(keys, query) * width ** (-0.5) + bias
            probs = jnp.exp(scores - lse_ref[at])
            score_grad = (probs * (dot_last(values, grad) - delta_ref[at])).astype(low)
            v_acc[...] += dot_plain(probs.astype(low), grad)
            k_acc[...] += dot_plain(score_grad, query)
            acc[at] += dot_first(keys, score_grad)
            return carry

        lax.fori_loop(0, heads, head, 0, unroll=2)
        side = sides.at[owner // 2, owner % 2, micro]
        side[:, :width] = (k_acc[...] * width ** (-0.5)).astype(low)
        side[:, width:] = v_acc[...].astype(low)

    def close(at, total):
        micro, h = at // heads, at % heads
        here = pl.ds(pl.multiple_of(micro * block, block), block)
        cols = pl.ds(pl.multiple_of(h * width, width), width)
        grad, gain = norm_turn_back(acc[at].T * width ** (-0.5), q_pre[here, cols], gq_ref[...],
                                    cos_ref[here, :], sin_ref[here, :])
        q_grad[here, cols] = grad.astype(low)
        return total + gain

    def close_all():
        gain_grad[pl.ds(0, 1), :] = lax.fori_loop(
            0, 2 * heads, close, jnp.zeros((1, width), jnp.float32)
        )

    def unit(u, carry):
        def at(fn, k):
            pl.when((k >= 0) & (k < nz))(lambda: fn(k))

        def each(parts, name, k):
            for part in parts:
                at(getattr(part, name), k)

        for n in range(4):
            pl.when(4 * u + n < count)(lambda: attention(4 * u + n))
        each(outs, 'second', u + 1)
        each(weights, 'send', u + 2)
        each(outs, 'first', u + 3)
        pl.when(u == 1)(smalls.second)
        at(keys_out.turn, u - done)
        each(outs, 'third', u)
        each(outs, 'fourth', u - 1)
        each(weights, 'second', u - 2)
        each(weights, 'first', u - 1)
        pl.when(u == done + 1)(close_all)
        return carry

    eye = diagonal()

    def column(yy):
        return mid_ref.at[:, pl.ds(pl.multiple_of((yy * 2 + c) * cols, cols), cols)]

    partner, yn = outs[0].partner, outs[0].yn
    to_y = remote(low_ref, column(y), s_t.at[0], r_t.at[0], yn)
    to_pair = remote(low_ref, column(y), s_t.at[1], r_t.at[1], partner)
    onward = remote(column(1 - y), column(1 - y), s_t.at[2], r_t.at[2], partner)

    def dots(n, carry):
        here = pl.ds(pl.multiple_of(n * 128, 128), 128)
        product = middle_ref[here, :] * inner_ref[here, :]
        sums.got[0, pl.ds(n, 1), :] = to_row(jnp.sum(product, axis=1, keepdims=True), eye)
        return carry

    def residual(n, carry):
        here = pl.ds(pl.multiple_of(n * 128, 128), 128)
        mean = to_column(sums.total(n), eye) / (4 * cols)
        scale = scale_ref[here, :]
        out = (low_ref[here, :].astype(jnp.float32) + scale * inner_ref[here, :]
               - middle_ref[here, :] * (scale * scale * scale * mean))
        mid_out[here, :] = out
        low_ref[here, :] = out.astype(low)
        return carry

    def head_grads(part):
        def step(n, carry):
            at = pl.ds(pl.multiple_of(n * 256, 256), 256)
            to = pl.ds(pl.multiple_of(part * wo_ref.shape[1] + n * 256, 256), 256)
            grad_ref[:, to] = dot_plain(mid_ref[...], wo_ref[:, at]).astype(low)
            return carry

        lax.fori_loop(0, wo_ref.shape[1] // 256, step, 0)

    def deltas(at, carry):
        here = pl.ds(pl.multiple_of(at // heads * block, block), block)
        head = pl.ds(pl.multiple_of(at % heads * width, width), width)
        product = grad_ref[here, head].astype(jnp.float32) * heads_ref[here, head].astype(jnp.float32)
        delta_ref[at] = jnp.sum(product.T, axis=0, keepdims=True)
        return carry

    done = (shards + 2 - 1) // 4
    def each_now(parts, name, k):
        for part in parts:
            getattr(part, name)(k)

    gates = gates_ref[...]
    gates_grad = gg_ref[:, 0, :].T
    logit_grad = gates * (gates_grad - jnp.sum(gates * gates_grad, axis=1, keepdims=True))
    each_now(outs, 'first', 0)
    pieces, rest = [], logit_grad
    for _ in range(3):
        pieces.append(rest.astype(low))
        rest = rest - pieces[-1].astype(jnp.float32)
    router_grad = sum(dot_first(piece, moe_ref[...]) for piece in pieces)
    small_ref[...] = jnp.zeros_like(small_ref)
    blocks = cols // 128
    per = router_grad.shape[0] // shards
    for e in range(router_grad.shape[0]):
        for n in range(blocks):
            small_ref[e // per, pl.ds(e % per * blocks + n, 1), :] = (
                router_grad[e : e + 1, n * 128 : (n + 1) * 128])
    for copy in fetches[:5]:
        copy.wait()

    def moe_grads(n, total):
        here = pl.ds(pl.multiple_of(n * 128, 128), 128)
        grad = inner_ref[here, :]
        for piece in pieces_ref:
            grad = grad + dot_last(piece[here, :], router_ref[...])
        inner_ref[here, :] = grad * gain_ref[:, mine]
        return total + jnp.sum(grad * middle_ref[here, :] * scale_ref[here, :], axis=0, keepdims=True)

    pieces_ref = [split_ref.at[n] for n in range(3)]
    for ref, piece in zip(pieces_ref, pieces):
        ref[...] = piece
    gain_total = lax.fori_loop(0, rows // 128, moe_grads, jnp.zeros((1, cols), jnp.float32))
    for n in range(blocks):
        small_ref[0, pl.ds(per * blocks + n, 1), :] = gain_total[:, n * 128 : (n + 1) * 128]
    smalls.start()
    lax.fori_loop(0, rows // 128, dots, 0)
    sums.start()
    sums.wait()
    lax.fori_loop(0, rows // 128, residual, 0)
    fetches[-1].start()
    to_y.start()
    to_pair.start()
    mid_ref[:, pl.ds(pl.multiple_of((y * 2 + c) * cols, cols), cols)] = low_ref[...]
    each_now(outs, 'first', 1)
    to_y.wait_recv()
    onward.start()
    each_now(outs, 'second', 0)
    for copy in fetches[5:]:
        copy.wait()
    to_pair.wait()
    onward.wait()
    to_y.wait_send()
    for k in range(2):
        each_now(weights, 'send', k)
    each_now(outs, 'first', 2)
    head_grads(0)
    more = pltpu.make_async_copy(wo_all.at[:, pl.ds(wo_ref.shape[1], wo_ref.shape[1])], wo_ref,
                                 s_in.at[5])
    more.start()
    more.wait()
    head_grads(1)
    lax.fori_loop(0, 2 * heads, deltas, 0)
    lax.fori_loop(0, nz + 2, unit, 0)
    keys_out.finish()
    total = jnp.zeros((1, width), jnp.float32)
    for micro in range(2):
        here = slice(micro * block, (micro + 1) * block)
        grad, gain = norm_turn_back(kv_sum[micro, :, :width], k_pre[here, :], gk_ref[...],
                                    cos_ref[here, :], sin_ref[here, :])
        q_grad[here, heads * width : (heads + 1) * width] = grad.astype(low)
        q_grad[here, (heads + 1) * width :] = kv_sum[micro, :, width:].astype(low)
        total = total + gain
    gain_grad[pl.ds(1, 1), :] = total
    for part in outs + weights:
        part.finish()
    smalls.finish()


def attend_back(query, q_pre, k_pre, gain_key, gain_query, cosine, sine, keys_values, starts, log_total,
                gates, gates_grad, router, gain, moe_low, middle, scale, back, cotangent, cot_all, w_out, heads_low, out_part, nz, collective_id):
    rows, columns = query.shape
    width = keys_values.shape[4] // 2
    heads = columns // width
    block = rows // 2
    cols = out_part.shape[1] // 4
    wo_shape = (w_out.shape[0] // (2 * nz), columns)
    experts = gates.shape[1]
    part_rows = -(-(experts // (2 * nz) + 1) * cols // 1024) * 8
    small = (2 * nz, part_rows, 128)
    any_space = pl.BlockSpec(memory_space=pl.ANY)
    vmem = pl.BlockSpec(memory_space=pltpu.VMEM)
    vm, shape, f32, low = pltpu.VMEM, jax.ShapeDtypeStruct, jnp.float32, jnp.bfloat16
    dma = pltpu.SemaphoreType.DMA
    return pl.pallas_call(
        functools.partial(attend_back_kernel, nz),
        in_specs=[vmem] * 10 + [any_space] + [vmem] * 2 + [any_space] * 10,
        out_specs=[vmem] * 6,
        out_shape=[
            shape((rows, cols), f32),
            shape((rows, columns + 2 * width), low), shape((2, width), f32),
            shape((rows, cols), f32), shape(wo_shape, f32),
            shape((8 * nz,) + small[1:], f32),
        ],
        scratch_shapes=[
            vm((cols, experts), low), vm((rows, cols), low),
            vm((rows, 4 * cols), low), vm((w_out.shape[0], columns // 2), low), vm((rows, columns), low),
            vm((rows, columns), low), vm((nz, 2, 2, block, 2 * width), low),
            vm(small, f32), vm((3, rows, experts), low), vm((rows, columns), low),
            vm((2 * heads, 1, block), f32), vm((rows, columns), f32), dma((10,)), dma((3,)), dma((3,)),
            vm((2, block, 2 * width), f32), vm((nz, 2, 2, block, 2 * width), low),
            vm((2 * heads, width, block), f32), vm((block, width), f32), vm((block, width), f32),
        ] + ScatterAll.scratch(nz, rows // 2, cols, low, 0) * 2
        + ReduceRows.scratch(nz, wo_shape[0] // 2, wo_shape[1], low) * 2
        + SmallSums.scratch(nz, small[1:], f32)
        + ReduceCausal.scratch(nz, block, 2 * width, low) + RowSums.scratch(rows),
        compiler_params=pltpu.CompilerParams(
            collective_id=collective_id, has_side_effects=True, vmem_limit_bytes=62 << 20
        ),
        name="attend_back",
    )(k_pre, gain_key, gain_query, cosine, sine, starts, log_total, scale, gates, gates_grad, router,
      gain, moe_low, middle, back, cotangent, cot_all, w_out,
      heads_low, query, keys_values, q_pre, out_part)


def to_row(column, eye):
    return jnp.sum(jnp.where(eye, column, 0.0), axis=0, keepdims=True)


def to_column(row, eye):
    return jnp.sum(jnp.where(eye, row, 0.0), axis=1, keepdims=True)


def diagonal():
    shape = (128, 128)
    return lax.broadcasted_iota(jnp.int32, shape, 0) == lax.broadcasted_iota(jnp.int32, shape, 1)


class RowSums:
    @staticmethod
    def scratch(rows):
        dma = pltpu.SemaphoreType.DMA
        return [pltpu.VMEM((4, rows // 128, 128), jnp.float32), dma((3,)), dma((3,))]

    def __init__(self, refs):
        self.got, s, r = refs
        shard, group = lax.axis_index("fsdp"), lax.axis_index("tp")
        self.peers = [(shard, (group + k) % 4) for k in range(1, 4)]
        self.copies = [
            remote(self.got.at[0], self.got.at[k + 1], s.at[k], r.at[k], peer)
            for k, peer in enumerate(self.peers)
        ]

    def start(self):
        for copy in self.copies:
            copy.start()

    def wait(self):
        for copy in self.copies:
            copy.wait()

    def total(self, n):
        return self.got[0, pl.ds(n, 1), :] + self.got[1, pl.ds(n, 1), :] + (
            self.got[2, pl.ds(n, 1), :] + self.got[3, pl.ds(n, 1), :])


class ReduceCols:
    @staticmethod
    def scratch(rows, cols, kind):
        vm, dma = pltpu.VMEM, pltpu.SemaphoreType.DMA
        return [vm((2, rows, cols), kind), vm((2, rows, cols), kind), vm((rows, cols), kind),
                dma((2,)), dma((2,)), dma((2,)), dma, dma]

    def __init__(self, partial, out, refs):
        self.w, self.rp, self.ry, s_l, s_p, r_p, s_y, r_y = refs
        self.out = out
        self.rows, cols = out.shape
        z, x, y, c = place()
        self.partner, self.yn = device(z, x, y, 1 - c), device(z, x, 1 - y, c)

        def block(yy, cc):
            return partial.at[:, pl.ds(pl.multiple_of((yy * 2 + cc) * cols, cols), cols)]

        self.sends = [remote(block(yy, 1 - c), self.rp.at[k], s_p.at[k], r_p.at[k], self.partner)
                      for k, yy in enumerate((1 - y, y))]
        self.loads = [pltpu.make_async_copy(block(yy, c), self.w.at[k], s_l.at[k])
                      for k, yy in enumerate((1 - y, y))]
        self.across = remote(self.w.at[0], self.ry, s_y, r_y, self.yn)

    def start(self):
        for k in range(2):
            self.sends[k].start()
            self.loads[k].start()

    def first(self):
        self.loads[0].wait()
        self.sends[0].wait_recv()
        add_blocks(self.w.at[0], [self.rp.at[0]], 0, self.rows)
        self.across.start()

    def second(self):
        self.loads[1].wait()
        self.sends[1].wait_recv()
        self.across.wait_recv()
        add_blocks(self.w.at[1], [self.rp.at[1], self.ry], 0, self.rows, self.out)

    def finish(self):
        for send in self.sends:
            send.wait_send()
        self.across.wait_send()


class SmallSums:
    @staticmethod
    def scratch(nz, part, kind):
        dma = pltpu.SemaphoreType.DMA
        return [pltpu.VMEM((2 * nz,) + part, kind), dma((2 * nz,)), dma((2 * nz,)),
                dma((8 * nz,)), dma((8 * nz,))]

    def __init__(self, nz, values, out, refs):
        self.got, self.s_1, self.r_1, self.s_2, self.r_2 = refs
        self.values, self.out = values, out
        self.shards, self.devices = 2 * nz, 8 * nz
        self.shard, self.group = lax.axis_index("fsdp"), lax.axis_index("tp")
        self.me = self.shard * 4 + self.group

    def share(self, k):
        other = (self.shard + k) % self.shards
        return remote(self.values.at[other], self.got.at[k], self.s_1.at[k], self.r_1.at[k],
                      (other, self.group))

    def spread(self, k):
        other = (self.me + k) % self.devices
        return remote(self.out.at[self.me], self.out.at[self.me], self.s_2.at[k], self.r_2.at[k],
                      (other // 4, other % 4))

    def start(self):
        loop_from_one(self.shards, lambda k: self.share(k).start())

    def second(self):
        loop_from_one(self.shards, lambda k: self.share(k).wait())
        acc = self.values[self.shard]
        for k in range(1, self.shards):
            acc = acc + self.got[k]
        self.out[self.me] = acc
        loop_from_one(self.devices, lambda k: self.spread(k).start())

    def finish(self):
        loop_from_one(self.devices, lambda k: self.spread(k).wait())


def loop_from_one(count, fn):
    def step(k, carry):
        fn(k)
        return carry

    lax.fori_loop(1, count, step, 0)


def tail_kernel(nz, tok_ref, scale_ref, gain_ref, block_ref, small_ref, left_all, right_all, mid_all,
                wq_all, wk_all, wv_all, gp_all, up_all, hid_all, xr_all, gs_all,
                wq_out, wk_out, wv_out, token_out, block_out, gain_out, head_out, dwg, dwu, dwd,
                left_ref, right_ref, mid_ref, wq, wk, wv, part_ref, s_m, w_sum, gp_ref, up_ref, hid_ref, x_panel, g_panel, o_gate, o_up, o_down, s_in, s_out,
                small_out, normed, token, s_w, r_w, s_l, s_g, r_g, *refs):
    z, x, y, c = place()
    shard, group = lax.axis_index("fsdp"), lax.axis_index("tp")
    shards = 2 * nz
    devices = 4 * shards
    me = shard * 4 + group
    rows, cols = tok_ref.shape
    width = cols * 4
    half = rows // 2
    panel = x_panel.shape[1]
    panels = xr_all.shape[1] // panel
    f32, low = jnp.float32, jnp.bfloat16
    n_w, n_c = len(ReduceRows.scratch(nz, 16, 128, low)), len(ReduceCols.scratch(16, 128, low))
    weights = [ReduceRows(nz, left_ref, right_ref, half, refs[n * n_w : (n + 1) * n_w], n, 2)
               for n, half in enumerate(halves(w_sum))]
    columns = ReduceCols(part_ref, normed, refs[2 * n_w : 2 * n_w + n_c])
    sums = RowSums(refs[2 * n_w + n_c :])
    mirror = device(nz - 1 - z, x, y, c)
    greet_all(shard, group, shards, 4)
    fetches = [pltpu.make_async_copy(src, dst, s_m.at[n]) for n, (src, dst) in enumerate((
        (left_all, left_ref), (right_all, right_ref), (wq_all, wq), (wk_all, wk), (wv_all, wv),
        (mid_all, mid_ref)))]
    for copy in fetches:
        copy.start()
    for copy in fetches[:2]:
        copy.wait()
    for part in weights:
        part.send(0)
    for copy in fetches[2:]:
        copy.wait()
    first, second = wq_out.shape[1], wq_out.shape[1] + wk_out.shape[1]

    def normed_parts(n, carry):
        at = pl.ds(pl.multiple_of(n * cols, cols), cols)
        part_ref[:, at] = (
            dot_last(right_ref[:, :first], wq[at, :])
            + dot_last(right_ref[:, first:second], wk[at, :])
            + dot_last(right_ref[:, second:], wv[at, :])
        ).astype(low)
        return carry

    lax.fori_loop(0, 4, normed_parts, 0)
    columns.start()
    for k in range(1, nz):
        for part in weights:
            part.send(k)
    top, bottom = pl.ds(0, half), pl.ds(half, half)
    swaps = [remote(src.at[bottom], dst.at[bottom], s_w.at[n], r_w.at[n], mirror)
             for n, (src, dst) in enumerate(((token, token_out), (block_ref, block_out)))]
    keeps = [pltpu.make_async_copy(src.at[top], dst.at[top], s_l.at[n])
             for n, (src, dst) in enumerate(((token, token_out), (block_ref, block_out)))]
    swaps[1].start()
    keeps[1].start()

    def loads(n):
        at = pl.ds(pl.multiple_of(n * panel, panel), panel)
        return (pltpu.make_async_copy(xr_all.at[:, at], x_panel, s_in.at[0]),
                pltpu.make_async_copy(gs_all.at[:, at], g_panel, s_in.at[1]))

    def stores(n):
        at = pl.ds(pl.multiple_of(n * panel, panel), panel)
        return (pltpu.make_async_copy(o_gate, dwg.at[at, :], s_out.at[0]),
                pltpu.make_async_copy(o_up, dwu.at[at, :], s_out.at[1]),
                pltpu.make_async_copy(o_down, dwd.at[:, at], s_out.at[2]))

    whole = [pltpu.make_async_copy(src, dst, s_in.at[2 + n])
             for n, (src, dst) in enumerate(((gp_all, gp_ref), (up_all, up_ref), (hid_all, hid_ref)))]
    for copy in tuple(whole) + loads(0):
        copy.start()
    small_out[me] = jnp.zeros(small_out.shape[1:], f32)
    small_out[me, pl.ds(cols // 128, 2), :] = small_ref[...]

    def expert_weights(n):
        @pl.when(n == 0)
        def _():
            for copy in whole:
                copy.wait()

        for copy in loads(n):
            copy.wait()

        @pl.when(n > 0)
        def _():
            for copy in stores(n):
                copy.wait()

        o_gate[...] = dot_first(x_panel[...], gp_ref[...])
        o_up[...] = dot_first(x_panel[...], up_ref[...])
        o_down[...] = dot_first(g_panel[...], hid_ref[...]).T
        for copy in stores(n):
            copy.start()

        @pl.when(n < panels - 1)
        def _():
            for copy in loads(n + 1):
                copy.start()

    def token_sums():
        eye = diagonal()

        def step(n, gains):
            here = pl.ds(pl.multiple_of(n * 128, 128), 128)
            tok, grad = tok_ref[here, :].astype(f32), normed[here, :]
            product = tok * (grad * gain_ref[:, pl.ds(pl.multiple_of(group * cols, cols), cols)])
            sums.got[0, pl.ds(n, 1), :] = to_row(jnp.sum(product, axis=1, keepdims=True), eye)
            return gains + jnp.sum(grad * tok * scale_ref[here, :], axis=0, keepdims=True)

        gains = lax.fori_loop(0, rows // 128, step, jnp.zeros((1, cols), f32))
        for n in range(cols // 128):
            small_out[me, pl.ds(n, 1), :] = gains[:, n * 128 : (n + 1) * 128]

    def token_grads():
        eye = diagonal()

        def step(n, carry):
            here = pl.ds(pl.multiple_of(n * 128, 128), 128)
            mean = to_column(sums.total(n), eye) / width
            scale = scale_ref[here, :]
            token[here, :] = (
                mid_ref[here, :]
                + scale * (gain_ref[:, pl.ds(pl.multiple_of(group * cols, cols), cols)] * normed[here, :])
                - tok_ref[here, :].astype(f32) * (scale * scale * scale * mean)
            ).astype(low)
            return carry

        lax.fori_loop(0, rows // 128, step, 0)

    def spread(k):
        other = (me + k) % devices
        return remote(small_out.at[me], small_out.at[me], s_g.at[k], r_g.at[k],
                      (other // 4, other % 4))

    columns.first()

    def unit(u, carry):
        @pl.when(u == 1)
        def _():
            sums.wait()
            token_grads()
            swaps[0].start()
            keeps[0].start()

        @pl.when((u >= 1) & (u <= nz))
        def _():
            for part in weights:
                part.second(u - 1)

        @pl.when(u < panels // 2)
        def _():
            expert_weights(2 * u)
            expert_weights(2 * u + 1)

        @pl.when(u == 0)
        def _():
            columns.second()
            token_sums()
            sums.start()
            loop_from_one(devices, lambda k: spread(k).start())

        @pl.when(u < nz)
        def _():
            for part in weights:
                part.first(u)

        return carry

    lax.fori_loop(0, max(nz + 1, panels // 2), unit, 0)
    loop_from_one(devices, lambda k: spread(k).wait())
    gain_rows = cols // 128
    for g in range(4):
        rows_of = small_out[g, pl.ds(0, gain_rows), :]
        for f in range(1, shards):
            rows_of = rows_of + small_out[f * 4 + g, pl.ds(0, gain_rows), :]
        gain_out[g] = rows_of
    total = small_out[0, pl.ds(gain_rows, 2), :]
    for d in range(1, devices):
        total = total + small_out[d, pl.ds(gain_rows, 2), :]
    head_out[...] = total
    for copy in swaps + keeps:
        copy.wait()
    for copy in stores(panels - 1):
        copy.wait()
    wq_out[...] = w_sum[:, :first]
    wk_out[...] = w_sum[:, first:second]
    wv_out[...] = w_sum[:, second:]
    columns.finish()
    for part in weights:
        part.finish()


def tail(gate_grad, up_grad, hidden, tokens, middle_grad, scale, gain, block_out, small, normed_low,
         pre_grad, wq_all, wk_all, wv_all, rows_in, pair_grad, nz, collective_id):
    rows, cols = tokens.shape
    pairs, features = rows_in.shape
    hidden_width = hidden.shape[1]
    panel = 256
    w_shape = (normed_low.shape[1] // (2 * nz), pre_grad.shape[1])
    query_width, kv_width = wq_all.shape[1], wk_all.shape[1]
    devices = 8 * nz
    any_space = pl.BlockSpec(memory_space=pl.ANY)
    vmem = pl.BlockSpec(memory_space=pltpu.VMEM)
    vm, shape, f32, low = pltpu.VMEM, jax.ShapeDtypeStruct, jnp.float32, jnp.bfloat16
    dma = pltpu.SemaphoreType.DMA
    return pl.pallas_call(
        functools.partial(tail_kernel, nz),
        in_specs=[vmem] * 5 + [any_space] * 11,
        out_specs=[vmem] * 3 + [any_space, any_space, vmem, vmem] + [any_space] * 3,
        out_shape=[
            shape((w_shape[0], query_width), f32), shape((w_shape[0], kv_width), f32),
            shape((w_shape[0], kv_width), f32), shape((rows, cols), low), shape((rows, cols), low),
            shape((4, cols // 128, 128), f32), shape((2, 128), f32),
            shape((features, hidden_width), f32), shape((features, hidden_width), f32),
            shape((hidden_width, features), f32),
        ],
        scratch_shapes=[vm(normed_low.shape, low), vm(pre_grad.shape, low), vm((rows, cols), f32),
                        vm(wq_all.shape, low), vm(wk_all.shape, low), vm(wv_all.shape, low),
                        vm((rows, 4 * cols), low), dma((6,)), vm(w_shape, f32)] + [vm((pairs, hidden_width), low)] * 3 + [
            vm((pairs, panel), low), vm((pairs, panel), low),
            vm((panel, hidden_width), f32), vm((panel, hidden_width), f32),
            vm((hidden_width, panel), f32), dma((5,)), dma((3,)),
            vm((devices, 8, 128), f32), vm((rows, cols), f32), vm((rows, cols), low),
            dma((2,)), dma((2,)), dma((2,)), dma((devices,)), dma((devices,)),
        ] + ReduceRows.scratch(nz, w_shape[0] // 2, w_shape[1], low) * 2 + ReduceCols.scratch(rows, cols, low)
        + RowSums.scratch(rows),
        compiler_params=pltpu.CompilerParams(
            collective_id=collective_id, has_side_effects=True, vmem_limit_bytes=62 << 20
        ),
        name="tail",
    )(tokens, scale, gain, block_out, small, normed_low, pre_grad, middle_grad, wq_all, wk_all, wv_all,
      gate_grad, up_grad, hidden, rows_in, pair_grad)


def join_kernel(nz, tok_ref, gain_ref, attn_part, middle_ref, scale_ref, low_ref, all_ref, *refs):
    z, x, y, c = place()
    rows, cols = tok_ref.shape
    f32 = jnp.float32
    n_c, n_s = len(ReduceCols.scratch(16, 128, jnp.bfloat16)), 3
    columns = ReduceCols(attn_part, middle_ref, refs[:n_c])
    sums = RowSums(refs[n_c : n_c + n_s])
    gather = GatherAll(nz, low_ref, all_ref, refs[n_c + n_s :], rows // 2)
    greet([(None, gather.xn), (z < nz - 1, gather.up), (z > 0, gather.down)]
          + [(None, peer) for peer in sums.peers])
    columns.start()
    eye = diagonal()
    columns.first()
    columns.second()

    def add(n, carry):
        here = pl.ds(pl.multiple_of(n * 128, 128), 128)
        total = middle_ref[here, :] + tok_ref[here, :].astype(f32)
        middle_ref[here, :] = total
        sums.got[0, pl.ds(n, 1), :] = to_row(jnp.sum(total * total, axis=1, keepdims=True), eye)
        return carry

    def norm(n, carry):
        here = pl.ds(pl.multiple_of(n * 128, 128), 128)
        scale = lax.rsqrt(to_column(sums.total(n), eye) / (4 * cols) + norm_eps)
        scale_ref[here, :] = scale
        low_ref[here, :] = (middle_ref[here, :] * scale * gain_ref[...]).astype(low_ref.dtype)
        return carry

    lax.fori_loop(0, rows // 128, add, 0)
    sums.start()
    sums.wait()
    lax.fori_loop(0, rows // 128, norm, 0)
    gather.own().start()
    gather.own().wait()

    def tick(k, carry):
        pl.when(k < nz)(lambda: gather.first(k))
        pl.when((k >= 1) & (k <= nz))(lambda: gather.second(k - 1))
        pl.when(k >= 2)(lambda: gather.third(k - 2))
        return carry

    lax.fori_loop(0, nz + 2, tick, 0)
    gather.finish()
    columns.finish()


def join(tokens, gain, attn_part, nz, collective_id):
    rows, cols = tokens.shape
    any_space = pl.BlockSpec(memory_space=pl.ANY)
    vmem = pl.BlockSpec(memory_space=pltpu.VMEM)
    shape, f32, low = jax.ShapeDtypeStruct, jnp.float32, jnp.bfloat16
    return pl.pallas_call(
        functools.partial(join_kernel, nz),
        in_specs=[vmem] * 2 + [any_space],
        out_specs=[vmem] * 3 + [any_space],
        out_shape=[shape((rows, cols), f32), shape((rows, 1), f32), shape((rows, cols), low),
                   shape((rows * 2 * nz, cols * 4), low)],
        scratch_shapes=ReduceCols.scratch(rows, cols, low) + RowSums.scratch(rows)
        + GatherAll.scratch(nz),
        compiler_params=pltpu.CompilerParams(
            collective_id=collective_id, has_side_effects=True, vmem_limit_bytes=62 << 20
        ),
        name="join",
    )(tokens, gain, attn_part)


def turn_kernel(middle_ref, scale_ref, inner_ref, grad_ref, out_ref, all_ref, low_ref, lsem,
                s_p, r_p, s_y, r_y, *refs):
    z, x, y, c = place()
    rows, cols = middle_ref.shape
    sums = RowSums(refs)
    partner, yn = device(z, x, y, 1 - c), device(z, x, 1 - y, c)
    greet([(None, peer) for peer in sums.peers])
    eye = diagonal()

    def block(yy):
        return all_ref.at[:, pl.ds(pl.multiple_of((yy * 2 + c) * cols, cols), cols)]

    def dots(n, carry):
        here = pl.ds(pl.multiple_of(n * 128, 128), 128)
        product = middle_ref[here, :] * inner_ref[here, :]
        sums.got[0, pl.ds(n, 1), :] = to_row(jnp.sum(product, axis=1, keepdims=True), eye)
        return carry

    def grads(n, carry):
        here = pl.ds(pl.multiple_of(n * 128, 128), 128)
        mean = to_column(sums.total(n), eye) / (4 * cols)
        scale = scale_ref[here, :]
        out = (grad_ref[here, :] + scale * inner_ref[here, :]
               - middle_ref[here, :] * (scale * scale * scale * mean))
        out_ref[here, :] = out
        low_ref[here, :] = out.astype(low_ref.dtype)
        return carry

    lax.fori_loop(0, rows // 128, dots, 0)
    sums.start()
    sums.wait()
    lax.fori_loop(0, rows // 128, grads, 0)
    to_y = remote(low_ref, block(y), s_y, r_y, yn)
    to_pair = remote(low_ref, block(y), s_p.at[0], r_p.at[0], partner)
    own = pltpu.make_async_copy(low_ref, block(y), lsem)
    on = remote(block(1 - y), block(1 - y), s_p.at[1], r_p.at[1], partner)
    for copy in (to_y, to_pair, own):
        copy.start()
    to_y.wait_recv()
    on.start()
    to_pair.wait()
    on.wait()
    to_y.wait_send()
    own.wait()


def turn(middle, scale, inner, grad, collective_id):
    rows, cols = middle.shape
    any_space = pl.BlockSpec(memory_space=pl.ANY)
    vmem = pl.BlockSpec(memory_space=pltpu.VMEM)
    shape, f32, low = jax.ShapeDtypeStruct, jnp.float32, jnp.bfloat16
    dma = pltpu.SemaphoreType.DMA
    return pl.pallas_call(
        turn_kernel,
        in_specs=[vmem] * 4,
        out_specs=[vmem, any_space],
        out_shape=[shape((rows, cols), f32), shape((rows, cols * 4), low)],
        scratch_shapes=[pltpu.VMEM((rows, cols), low), dma, dma((2,)), dma((2,)), dma, dma]
        + RowSums.scratch(rows),
        compiler_params=pltpu.CompilerParams(
            collective_id=collective_id, has_side_effects=True, vmem_limit_bytes=62 << 20
        ),
        name="turn",
    )(middle, scale, inner, grad)


def gathered_body(
    tokens,
    cotangent,
    routes,
    doc_ids,
    gain_attn,
    w_query,
    key_weight,
    value_weight,
    w_out,
    gain_query,
    key_norm_gain,
    gain_moe,
    router,
    w_gate,
    w_up,
    w_down,
):
    shard_count = lax.axis_size("fsdp")
    group_count = lax.axis_size("tp")
    shard_index = lax.axis_index("fsdp")
    group_index = lax.axis_index("tp")
    nz = shard_count // 2
    f32, low = jnp.float32, jnp.bfloat16
    row_count, slice_width = tokens.shape
    model_width = slice_width * group_count
    micro_count, micro_rows = doc_ids.shape
    head_width = gain_query.shape[0]
    query_width, kv_width = w_query.shape[1], key_weight.shape[1]
    query_local = query_width // head_width
    kv_local = kv_width // head_width
    group_width = query_local // kv_local
    expert_total = router.shape[1]
    capacity = max(2, 2 * micro_rows * TOPK // expert_total)
    block_keys = micro_rows * math.gcd(shard_count, max(1, 512 // micro_rows))
    my_columns = group_index * slice_width

    mirror_index = mirrored(nz, shard_index)
    owners = jnp.stack([shard_index, mirror_index])

    small = jnp.concatenate([routes.reshape(-1), doc_ids.reshape(-1)])
    small_rows = -(-small.shape[0] // 1024) * 8
    small = jnp.pad(small, (0, small_rows * 128 - small.shape[0])).reshape(small_rows, 128)
    small_all, wq_all, wk_all, wv_all, tokens, full_tokens = gather_rows(
        [small, w_query, key_weight, value_weight], nz, 2, [tokens], 2
    )
    small_all = small_all.reshape(shard_count, small_rows * 128)
    routes_all = small_all[:, : row_count * TOPK].reshape(shard_count * row_count, TOPK)
    ids_all = small_all[:, row_count * TOPK : row_count * (TOPK + 1)].reshape(
        shard_count, micro_count, micro_rows
    )
    doc_range = jnp.arange(DOCS)
    doc_totals = jnp.sum((ids_all[..., None] == doc_range).astype(jnp.int32), axis=(0, 2))
    doc_begin = jnp.cumsum(doc_totals, axis=1) - doc_totals
    query_index = owners[:, None] * micro_rows + jnp.arange(micro_rows)
    my_ids = jnp.stack(
        [lax.dynamic_index_in_dim(ids_all[:, m], owners[m], 0, False) for m in range(micro_count)]
    )
    query_start = jnp.sum(
        jnp.where(my_ids[:, :, None] == doc_range, doc_begin[:, None, :], 0), axis=2
    )
    positions = (query_index - query_start).reshape(row_count)
    cosine_lookup, sine_lookup = rope_tables(positions, head_width)

    turned_sine = jnp.where(jnp.arange(head_width) < head_width // 2, -sine_lookup, sine_lookup)
    query_gain, key_gain = gain_query.reshape(1, head_width), key_norm_gain.reshape(1, head_width)
    starts = query_start.reshape(micro_count, 1, micro_rows).astype(jnp.int32)
    (normed_low, token_scale, query_pre, key_pre, query_low, heads_low, log_total, keys_values,
     grads_all, wo_all) = attend(
        full_tokens, gain_attn.reshape(1, model_width), wq_all, wk_all, wv_all, query_gain, key_gain,
        cosine_lookup, turned_sine, starts, cotangent, w_out, nz, 3,
    )
    attn_part = dot_last(heads_low, wo_all).astype(low)
    gain_row = gain_moe.reshape(1, model_width)
    middle, scale, moe_low, _, out_part, back, gates_grad, gates, *kept = run_experts(
        tokens, gain_row, router, attn_part, grads_all, routes_all,
        w_gate[0], w_up[0], w_down[0], micro_rows, capacity, nz, 8,
    )
    rows_in, pair_grad, hidden_low, gate_pre_low, up_pre_low = (
        array.reshape(-1, array.shape[2]) for array in kept
    )
    middle_grad, pre_low, head_gains, out_sum, w_out_grad, summed = attend_back(
        query_low, query_pre, key_pre, key_gain, query_gain, cosine_lookup, turned_sine, keys_values,
        starts, log_total, gates, gates_grad, router, gain_row, moe_low, middle, scale,
        back, cotangent, grads_all, wo_all, heads_low, out_part, nz, 12,
    )
    block_out = (middle + out_sum).astype(low)
    gain_rows = slice_width // 128
    (w_query_grad, w_key_grad, w_value_grad, token_grad, block_out, attn_gains, head_gains,
     *expert_grads) = tail(
        gate_pre_low, up_pre_low, hidden_low, tokens, middle_grad, token_scale,
        gain_attn.reshape(1, model_width), block_out, head_gains, normed_low, pre_low, wq_all, wk_all, wv_all,
        rows_in, pair_grad, nz, 15,
    )
    per = expert_total // shard_count
    summed = summed.reshape(shard_count, group_count, -1, 128)
    router_grad = summed[:, :, : per * gain_rows].reshape(
        shard_count, group_count, per, slice_width
    ).transpose(1, 3, 0, 2).reshape(router.shape)
    return (
        block_out,
        token_grad,
        attn_gains.reshape(-1),
        w_query_grad,
        w_key_grad,
        w_value_grad,
        w_out_grad,
        head_gains[0],
        head_gains[1],
        summed[0, :, per * gain_rows : (per + 1) * gain_rows].reshape(-1),
        router_grad,
        expert_grads[0][None],
        expert_grads[1][None],
        expert_grads[2][None],
    )


def solution(mesh):
    small = mesh.shape["fsdp"] * mesh.shape["tp"] <= 32 and mesh.shape["tp"] == 4
    return jax.shard_map(
        gathered_body if small else body,
        mesh=mesh,
        in_specs=(
            P("fsdp", "tp"),
            P("fsdp", "tp"),
            P("fsdp", None),
            P(None, "fsdp"),
            P(),
            P("fsdp", "tp"),
            P("fsdp", "tp"),
            P("fsdp", "tp"),
            P("fsdp", "tp"),
            P(),
            P(),
            P(),
            P(),
            P(("fsdp", "tp"), None, None),
            P(("fsdp", "tp"), None, None),
            P(("fsdp", "tp"), None, None),
        ),
        out_specs=(
            P("fsdp", "tp"),
            P("fsdp", "tp"),
            P(),
            P("fsdp", "tp"),
            P("fsdp", "tp"),
            P("fsdp", "tp"),
            P("fsdp", "tp"),
            P(),
            P(),
            P(),
            P(),
            P(("fsdp", "tp"), None, None),
            P(("fsdp", "tp"), None, None),
            P(("fsdp", "tp"), None, None),
        ),
        check_vma=False,
    )
```

```python
import functools
import math

import jax
import jax.numpy as jnp
from jax import lax
from jax.experimental import pallas as pl
from jax.experimental.pallas import tpu as pltpu
from jax.sharding import PartitionSpec as P

TOPK = 8
DOCS = 4


theta_base = 1000000.0
norm_eps = 1e-06
masked_score = -1e30
highest_precision = lax.Precision.HIGHEST


def root_mean_norm(row_block, gain_row):
    return (
        row_block
        * lax.rsqrt(jnp.mean(row_block * row_block, axis=-1, keepdims=True) + norm_eps)
        * gain_row
    )


def rotary_apply(row_block, cosine_lookup, sine_lookup):
    half_width = row_block.shape[-1] // 2
    turned = jnp.concatenate([-row_block[..., half_width:], row_block[..., :half_width]], axis=-1)
    return row_block * cosine_lookup + turned * sine_lookup


def rope_tables(positions, head_width):
    half_width = head_width // 2
    frequency = theta_base ** (
        -2.0 * jnp.arange(half_width, dtype=jnp.int32).astype(jnp.float32) / head_width
    )
    angles = positions.astype(jnp.float32)[:, None] * frequency[None, :]
    cosine_lookup = jnp.cos(angles)
    sine_lookup = jnp.sin(angles)
    return (
        jnp.concatenate([cosine_lookup, cosine_lookup], axis=-1),
        jnp.concatenate([sine_lookup, sine_lookup], axis=-1),
    )


def swiglu(gate_pre, up_pre):
    return jax.nn.silu(gate_pre) * up_pre


def dot_first(left_side, right_side):
    return lax.dot_general(
        left_side, right_side, (((0,), (0,)), ((), ())), preferred_element_type=jnp.float32
    )


def dot_last(left_side, right_side):
    return lax.dot_general(
        left_side, right_side, (((1,), (1,)), ((), ())), preferred_element_type=jnp.float32
    )


def gather_weights(w_query, key_weight, value_weight, w_out):
    return (
        lax.all_gather(w_query, "fsdp", axis=0, tiled=True),
        lax.all_gather(key_weight, "fsdp", axis=0, tiled=True),
        lax.all_gather(value_weight, "fsdp", axis=0, tiled=True),
        lax.all_gather(w_out, "fsdp", axis=0, tiled=True),
    )


def gather_keys(keys_low, values_low):
    return (
        lax.all_gather(keys_low, "fsdp", axis=0, tiled=True),
        lax.all_gather(values_low, "fsdp", axis=0, tiled=True),
    )


def send_rows(buffer):
    return lax.all_to_all(buffer, "fsdp", split_axis=0, concat_axis=0, tiled=True)


def return_rows(buffer):
    return lax.all_to_all(buffer, "fsdp", split_axis=0, concat_axis=0, tiled=True)


def to_heads(per_token, kv_local, group_width):
    token_count, head_total, head_width = per_token.shape
    grouped_heads = per_token.reshape(token_count, kv_local, group_width, head_width)
    return grouped_heads.transpose(1, 2, 0, 3).reshape(
        kv_local, group_width * token_count, head_width
    )


def to_tokens(per_head, group_width):
    kv_local, row_count, head_width = per_head.shape
    token_count = row_count // group_width
    grouped_heads = per_head.reshape(kv_local, group_width, token_count, head_width)
    return grouped_heads.transpose(2, 0, 1, 3).reshape(
        token_count, kv_local * group_width * head_width
    )


def key_block(keys_all, key_start, block_keys, kv_local, head_width):
    return lax.dynamic_slice_in_dim(keys_all, key_start, block_keys, 0).reshape(
        block_keys, kv_local, head_width
    )


def block_scores(queries, keys_part, key_start, query_index, query_start):
    head_width = queries.shape[-1]
    scores = jnp.einsum(
        "hrd,khd->hrk", queries, keys_part, preferred_element_type=jnp.float32
    ) * head_width ** (-0.5)
    key_index = key_start + jnp.arange(keys_part.shape[0])
    allowed = (key_index[None, :] >= query_start[:, None]) & (
        key_index[None, :] <= query_index[:, None]
    )
    return (jnp.where(allowed[None], scores, masked_score), allowed)


def attend_forward(queries, keys_all, values_all, query_index, query_start, block_keys):
    kv_local, row_count, head_width = queries.shape
    lowest_block = jnp.min(query_start) // block_keys
    highest_block = jnp.max(query_index) // block_keys + 1

    def visit_block(block_index, running):
        run_peak, run_total, run_acc = running
        key_start = block_index * block_keys
        keys_part = key_block(keys_all, key_start, block_keys, kv_local, head_width)
        values_part = key_block(values_all, key_start, block_keys, kv_local, head_width)
        scores, allowed = block_scores(queries, keys_part, key_start, query_index, query_start)
        new_peak = jnp.maximum(run_peak, jnp.max(scores, axis=-1))
        weights = jnp.where(allowed[None], jnp.exp(scores - new_peak[..., None]), 0.0)
        factor = jnp.exp(run_peak - new_peak)
        run_total = run_total * factor + jnp.sum(weights, axis=-1)
        run_acc = run_acc * factor[..., None] + jnp.einsum(
            "hrk,khd->hrd",
            weights.astype(jnp.bfloat16),
            values_part,
            preferred_element_type=jnp.float32,
        )
        return (new_peak, run_total, run_acc)

    start_state = (
        jnp.full((kv_local, row_count), masked_score, jnp.float32),
        jnp.zeros((kv_local, row_count), jnp.float32),
        jnp.zeros((kv_local, row_count, head_width), jnp.float32),
    )
    run_peak, run_total, run_acc = lax.fori_loop(
        lowest_block, highest_block, visit_block, start_state
    )
    return (run_acc / run_total[..., None], run_peak + jnp.log(run_total))


def attend_backward(
    queries,
    keys_all,
    values_all,
    query_index,
    query_start,
    block_keys,
    outputs,
    log_total,
    grad_low,
):
    kv_local, row_count, head_width = queries.shape
    key_count = keys_all.shape[0]
    score_scale = head_width ** (-0.5)
    row_delta = jnp.sum(grad_low.astype(jnp.float32) * outputs, axis=-1)
    lowest_block = jnp.min(query_start) // block_keys
    highest_block = jnp.max(query_index) // block_keys + 1

    def visit_block(block_index, running):
        query_acc, key_acc, value_acc = running
        key_start = block_index * block_keys
        keys_part = key_block(keys_all, key_start, block_keys, kv_local, head_width)
        values_part = key_block(values_all, key_start, block_keys, kv_local, head_width)
        scores, allowed = block_scores(queries, keys_part, key_start, query_index, query_start)
        prob_block = jnp.where(allowed[None], jnp.exp(scores - log_total[..., None]), 0.0)
        prob_grad = jnp.einsum(
            "hrd,khd->hrk", grad_low, values_part, preferred_element_type=jnp.float32
        )
        score_grad = (prob_block * (prob_grad - row_delta[..., None])).astype(jnp.bfloat16)
        query_acc = (
            query_acc
            + jnp.einsum("hrk,khd->hrd", score_grad, keys_part, preferred_element_type=jnp.float32)
            * score_scale
        )
        key_part = (
            jnp.einsum("hrk,hrd->khd", score_grad, queries, preferred_element_type=jnp.float32)
            * score_scale
        )
        value_part = jnp.einsum(
            "hrk,hrd->khd",
            prob_block.astype(jnp.bfloat16),
            grad_low,
            preferred_element_type=jnp.float32,
        )
        key_acc = lax.dynamic_update_slice_in_dim(
            key_acc, key_part.reshape(block_keys, kv_local * head_width), key_start, 0
        )
        value_acc = lax.dynamic_update_slice_in_dim(
            value_acc, value_part.reshape(block_keys, kv_local * head_width), key_start, 0
        )
        return (query_acc, key_acc, value_acc)

    start_state = (
        jnp.zeros((kv_local, row_count, head_width), jnp.float32),
        jnp.zeros((key_count, kv_local * head_width), jnp.float32),
        jnp.zeros((key_count, kv_local * head_width), jnp.float32),
    )
    return lax.fori_loop(lowest_block, highest_block, visit_block, start_state)


def body(
    tokens,
    cotangent,
    routes,
    doc_ids,
    gain_attn,
    w_query,
    key_weight,
    value_weight,
    w_out,
    gain_query,
    key_norm_gain,
    gain_moe,
    router,
    w_gate,
    w_up,
    w_down,
):
    shard_count = lax.axis_size("fsdp")
    group_count = lax.axis_size("tp")
    shard_index = lax.axis_index("fsdp")
    group_index = lax.axis_index("tp")
    full_tokens, full_grads = (
        lax.all_gather(tokens, "tp", axis=1, tiled=True),
        lax.all_gather(cotangent, "tp", axis=1, tiled=True),
    )
    slice_width = tokens.shape[1]
    model_width = full_tokens.shape[1]
    micro_count, micro_rows = doc_ids.shape
    head_width = gain_query.shape[0]
    query_local = w_query.shape[1] // head_width
    kv_local = key_weight.shape[1] // head_width
    group_width = query_local // kv_local
    expert_total = router.shape[1]
    capacity = max(2, 2 * micro_rows * TOPK // expert_total)
    slot_total = shard_count * capacity
    pair_total = micro_rows * TOPK
    block_keys = micro_rows * math.gcd(shard_count, max(1, 512 // micro_rows))
    doc_range = jnp.arange(DOCS)
    expert_range = jnp.arange(expert_total)
    local_counts = jnp.sum((doc_ids[:, :, None] == doc_range).astype(jnp.float32), axis=1)
    doc_totals = lax.psum(local_counts, "fsdp")
    doc_begin = (jnp.cumsum(doc_totals, axis=1) - doc_totals).astype(jnp.int32)
    gate_expert = w_gate[0]
    up_expert = w_up[0]
    down_expert = w_down[0]
    router_wide = router.astype(jnp.float32)
    query_acc = jnp.zeros((model_width, query_local * head_width), jnp.float32)
    key_acc = jnp.zeros((model_width, kv_local * head_width), jnp.float32)
    value_acc = jnp.zeros((model_width, kv_local * head_width), jnp.float32)
    out_acc = jnp.zeros((model_width, query_local * head_width), jnp.float32)
    gate_acc = jnp.zeros(gate_expert.shape, jnp.float32)
    up_acc = jnp.zeros(up_expert.shape, jnp.float32)
    down_acc = jnp.zeros(down_expert.shape, jnp.float32)
    router_acc = jnp.zeros(router.shape, jnp.float32)
    gain_attn_acc = jnp.zeros(gain_attn.shape, jnp.float32)
    gain_moe_acc = jnp.zeros(gain_moe.shape, jnp.float32)
    gain_query_acc = jnp.zeros(gain_query.shape, jnp.float32)
    gain_key_acc = jnp.zeros(key_norm_gain.shape, jnp.float32)
    out_parts = []
    grad_parts = []
    for micro_index in range(micro_count):
        row_begin = micro_index * micro_rows
        token_block = full_tokens[row_begin : row_begin + micro_rows].astype(jnp.float32)
        ids_now = doc_ids[micro_index]
        query_index = shard_index * micro_rows + jnp.arange(micro_rows)
        query_start = jnp.sum(
            jnp.where(ids_now[:, None] == doc_range, doc_begin[micro_index][None, :], 0), axis=1
        )
        cosine_lookup, sine_lookup = rope_tables(query_index - query_start, head_width)
        gathered = gather_weights(w_query, key_weight, value_weight, w_out)
        normed, norm_pull = jax.vjp(root_mean_norm, token_block, gain_attn)
        normed_reduced = normed.astype(jnp.bfloat16)
        query_pre = jnp.dot(normed_reduced, gathered[0], preferred_element_type=jnp.float32)
        key_before_norm = jnp.dot(normed_reduced, gathered[1], preferred_element_type=jnp.float32)
        value_reduced = jnp.dot(
            normed_reduced, gathered[2], preferred_element_type=jnp.float32
        ).astype(jnp.bfloat16)

        def shape_heads(query_raw, key_raw, query_gain, key_gain):
            query_heads = rotary_apply(
                root_mean_norm(query_raw.reshape(micro_rows, query_local, head_width), query_gain),
                cosine_lookup[:, None, :],
                sine_lookup[:, None, :],
            )
            key_heads = rotary_apply(
                root_mean_norm(key_raw.reshape(micro_rows, kv_local, head_width), key_gain),
                cosine_lookup[:, None, :],
                sine_lookup[:, None, :],
            )
            return (query_heads, key_heads)

        (query_heads, key_heads), heads_pull = jax.vjp(
            shape_heads, query_pre, key_before_norm, gain_query, key_norm_gain
        )
        queries = to_heads(query_heads.astype(jnp.bfloat16), kv_local, group_width)
        keys_low = key_heads.reshape(micro_rows, kv_local * head_width).astype(jnp.bfloat16)
        keys_all, values_all = gather_keys(keys_low, value_reduced)
        row_index = jnp.tile(query_index, group_width)
        row_start = jnp.tile(query_start, group_width)
        head_out, log_total = attend_forward(
            queries, keys_all, values_all, row_index, row_start, block_keys
        )
        heads_low = to_tokens(head_out, group_width).astype(jnp.bfloat16)
        attn_part = dot_last(heads_low, gathered[3])
        middle = token_block + lax.psum(attn_part.astype(jnp.bfloat16), "tp").astype(jnp.float32)
        moe_normed, moe_pull = jax.vjp(root_mean_norm, middle, gain_moe)
        moe_low = moe_normed.astype(jnp.bfloat16)
        logits = jnp.dot(moe_low, router, preferred_element_type=jnp.float32)
        routes_now = routes[row_begin : row_begin + micro_rows]
        route_match = routes_now[:, :, None] == expert_range
        chosen = jnp.sum(jnp.where(route_match, logits[:, None, :], 0.0), axis=-1)
        gate_weights, softmax_pull = jax.vjp(jax.nn.softmax, chosen)
        mine = routes_now % group_count == group_index
        pair_target = jnp.where(mine, routes_now // group_count, shard_count).reshape(pair_total)
        target_hot = (pair_target[:, None] == jnp.arange(shard_count)).astype(jnp.int32)
        pair_rank = jnp.sum((jnp.cumsum(target_hot, axis=0) - target_hot) * target_hot, axis=1)
        pair_slot = jnp.where(
            pair_target < shard_count, pair_target * capacity + pair_rank, slot_total
        )
        slot_pair = (
            jnp.full((slot_total + 1,), pair_total, jnp.int32)
            .at[pair_slot]
            .set(jnp.arange(pair_total, dtype=jnp.int32))[:slot_total]
        )
        slot_token = slot_pair // TOPK
        slot_grid = pair_slot.reshape(micro_rows, TOPK)
        padded_low = jnp.concatenate([moe_low, jnp.zeros((1, model_width), jnp.bfloat16)], axis=0)
        received = send_rows(
            padded_low[slot_token].reshape(shard_count, capacity, model_width)
        ).reshape(slot_total, model_width)
        gate_pre = jnp.dot(received, gate_expert, preferred_element_type=jnp.float32)
        up_pre = jnp.dot(received, up_expert, preferred_element_type=jnp.float32)
        hidden, swiglu_pull = jax.vjp(swiglu, gate_pre, up_pre)
        hidden_low = hidden.astype(jnp.bfloat16)
        expert_out = jnp.dot(hidden_low, down_expert, preferred_element_type=jnp.float32).astype(
            jnp.bfloat16
        )
        returned = return_rows(expert_out.reshape(shard_count, capacity, model_width)).reshape(
            slot_total, model_width
        )
        padded_out = jnp.concatenate([returned, jnp.zeros((1, model_width), jnp.bfloat16)], axis=0)
        moe_part = jnp.zeros((micro_rows, model_width), jnp.float32)
        for pick_index in range(TOPK):
            moe_part = moe_part + gate_weights[:, pick_index : pick_index + 1] * padded_out[
                slot_grid[:, pick_index]
            ].astype(jnp.float32)
        moe_share = lax.psum_scatter(
            moe_part.astype(jnp.bfloat16), "tp", scatter_dimension=1, tiled=True
        ).astype(jnp.float32)
        middle_slice = lax.dynamic_slice_in_dim(middle, group_index * slice_width, slice_width, 1)
        out_parts.append((middle_slice + moe_share).astype(jnp.bfloat16))
        grad_block = full_grads[row_begin : row_begin + micro_rows].astype(jnp.float32)
        gate_columns = []
        for pick_index in range(TOPK):
            gate_columns.append(
                jnp.sum(
                    grad_block * padded_out[slot_grid[:, pick_index]].astype(jnp.float32), axis=1
                )
            )
        gates_grad = jnp.stack(gate_columns, axis=1)
        flat_gates = jnp.concatenate(
            [gate_weights.reshape(pair_total), jnp.zeros((1,), jnp.float32)]
        )
        padded_grad = jnp.concatenate(
            [grad_block, jnp.zeros((1, model_width), jnp.float32)], axis=0
        )
        send_grad = (padded_grad[slot_token] * flat_gates[slot_pair][:, None]).astype(jnp.bfloat16)
        received_grad = send_rows(send_grad.reshape(shard_count, capacity, model_width)).reshape(
            slot_total, model_width
        )
        hidden_grad = dot_last(received_grad, down_expert)
        down_acc = down_acc + dot_first(hidden_low, received_grad)
        gate_pre_grad, up_pre_grad = swiglu_pull(hidden_grad)
        gate_pre_low = gate_pre_grad.astype(jnp.bfloat16)
        up_pre_low = up_pre_grad.astype(jnp.bfloat16)
        gate_acc = gate_acc + dot_first(received, gate_pre_low)
        up_acc = up_acc + dot_first(received, up_pre_low)
        rows_back = (dot_last(gate_pre_low, gate_expert) + dot_last(up_pre_low, up_expert)).astype(
            jnp.bfloat16
        )
        back_rows = return_rows(rows_back.reshape(shard_count, capacity, model_width)).reshape(
            slot_total, model_width
        )
        padded_back = jnp.concatenate(
            [back_rows, jnp.zeros((1, model_width), jnp.bfloat16)], axis=0
        )
        moe_grad = jnp.zeros((micro_rows, model_width), jnp.float32)
        for pick_index in range(TOPK):
            moe_grad = moe_grad + padded_back[slot_grid[:, pick_index]].astype(jnp.float32)
        (chosen_grad,) = softmax_pull(gates_grad)
        logit_grad = jnp.sum(jnp.where(route_match, chosen_grad[:, :, None], 0.0), axis=1)
        router_acc = router_acc + lax.dot_general(
            moe_low.astype(jnp.float32),
            logit_grad,
            (((0,), (0,)), ((), ())),
            precision=highest_precision,
        )
        moe_grad = moe_grad + lax.dot_general(
            logit_grad, router_wide, (((1,), (1,)), ((), ())), precision=highest_precision
        )
        middle_part, gain_moe_part = moe_pull(moe_grad)
        gain_moe_acc = gain_moe_acc + gain_moe_part
        middle_grad = grad_block + lax.psum(middle_part.astype(jnp.bfloat16), "tp").astype(
            jnp.float32
        )
        middle_low = middle_grad.astype(jnp.bfloat16)
        gathered_back = gather_weights(w_query, key_weight, value_weight, w_out)
        out_acc = out_acc + dot_first(middle_low, heads_low)
        heads_grad = jnp.dot(middle_low, gathered_back[3], preferred_element_type=jnp.float32)
        grad_low = to_heads(
            heads_grad.reshape(micro_rows, query_local, head_width).astype(jnp.bfloat16),
            kv_local,
            group_width,
        )
        query_side, key_side_all, value_side_all = attend_backward(
            queries,
            keys_all,
            values_all,
            row_index,
            row_start,
            block_keys,
            head_out,
            log_total,
            grad_low,
        )
        key_side, value_side = (
            lax.psum_scatter(
                key_side_all.astype(jnp.bfloat16), "fsdp", scatter_dimension=0, tiled=True
            ).astype(jnp.float32),
            lax.psum_scatter(
                value_side_all.astype(jnp.bfloat16), "fsdp", scatter_dimension=0, tiled=True
            ).astype(jnp.float32),
        )
        query_pre_grad, key_pre_grad, gain_query_part, gain_key_part = heads_pull(
            (
                to_tokens(query_side, group_width).reshape(micro_rows, query_local, head_width),
                key_side.reshape(micro_rows, kv_local, head_width),
            )
        )
        gain_query_acc = gain_query_acc + gain_query_part
        gain_key_acc = gain_key_acc + gain_key_part
        query_pre_low = query_pre_grad.astype(jnp.bfloat16)
        key_pre_low = key_pre_grad.astype(jnp.bfloat16)
        value_pre_low = value_side.astype(jnp.bfloat16)
        query_acc = query_acc + dot_first(normed_reduced, query_pre_low)
        key_acc = key_acc + dot_first(normed_reduced, key_pre_low)
        value_acc = value_acc + dot_first(normed_reduced, value_pre_low)
        normed_grad = (
            dot_last(query_pre_low, gathered_back[0])
            + dot_last(key_pre_low, gathered_back[1])
            + dot_last(value_pre_low, gathered_back[2])
        )
        token_part, gain_attn_part = norm_pull(normed_grad)
        gain_attn_acc = gain_attn_acc + gain_attn_part
        token_share = lax.psum_scatter(
            token_part.astype(jnp.bfloat16), "tp", scatter_dimension=1, tiled=True
        ).astype(jnp.float32)
        grad_slice = lax.dynamic_slice_in_dim(
            middle_grad, group_index * slice_width, slice_width, 1
        )
        grad_parts.append((grad_slice + token_share).astype(jnp.bfloat16))
    weight_sums = (
        lax.psum_scatter(
            query_acc.astype(jnp.bfloat16), "fsdp", scatter_dimension=0, tiled=True
        ).astype(jnp.float32),
        lax.psum_scatter(
            key_acc.astype(jnp.bfloat16), "fsdp", scatter_dimension=0, tiled=True
        ).astype(jnp.float32),
        lax.psum_scatter(
            value_acc.astype(jnp.bfloat16), "fsdp", scatter_dimension=0, tiled=True
        ).astype(jnp.float32),
        lax.psum_scatter(
            out_acc.astype(jnp.bfloat16), "fsdp", scatter_dimension=0, tiled=True
        ).astype(jnp.float32),
    )
    small_sums = lax.psum(
        (gain_attn_acc, gain_query_acc, gain_key_acc, gain_moe_acc, router_acc), ("fsdp", "tp")
    )
    return (
        jnp.concatenate(out_parts, axis=0),
        jnp.concatenate(grad_parts, axis=0),
        small_sums[0],
        weight_sums[0],
        weight_sums[1],
        weight_sums[2],
        weight_sums[3],
        small_sums[1],
        small_sums[2],
        small_sums[3],
        small_sums[4],
        gate_acc[None],
        up_acc[None],
        down_acc[None],
    )


MESH = pl.DeviceIdType.MESH


def place():
    f = lax.axis_index("fsdp")
    t = lax.axis_index("tp")
    return f // 2, f % 2, t // 2, t % 2


def device(z, x, y, c):
    return (z * 2 + x, y * 2 + c)


def greet(devices):
    barrier = pltpu.get_barrier_semaphore()
    total = 0
    for valid, where in devices:
        if valid is None:
            pl.semaphore_signal(barrier, inc=1, device_id=where, device_id_type=MESH)
            total = total + 1
        else:
            @pl.when(valid)
            def _():
                pl.semaphore_signal(barrier, inc=1, device_id=where, device_id_type=MESH)
            total = total + valid.astype(jnp.int32)
    pl.semaphore_wait(barrier, total)


def remote(src, dst, send, recv, where):
    return pltpu.make_async_remote_copy(
        src_ref=src, dst_ref=dst, send_sem=send, recv_sem=recv, device_id=where, device_id_type=MESH
    )


def gather_all_kernel(nz, x_ref, o_ref, lsem, s_p, s_u, s_d, s_x, s_y, s_dx, s_dy,
                      r_z, r_x, r_y, r_dx, r_dy, r_p):
    z, x, y, c = place()
    rows, cols = x_ref.shape
    half = rows // 2
    partner = device(z, x, y, 1 - c)
    xn = device(z, 1 - x, y, c)
    yn = device(z, x, 1 - y, c)
    up = device(z + 1, x, y, c)
    down = device(z - 1, x, y, c)
    greet([(None, partner), (None, xn), (None, yn), (z < nz - 1, up), (z > 0, down)])

    def block(zz, xx, yy, cc, part=None):
        start = (zz * 2 + xx) * rows
        size = rows
        if part is not None:
            start = start + part * half
            size = half
        return o_ref.at[pl.ds(pl.multiple_of(start, half), size),
                        pl.ds(pl.multiple_of((yy * 2 + cc) * cols, cols), cols)]

    own = pltpu.make_async_copy(x_ref, block(z, x, y, c), lsem)
    own.start()

    items = [(0, 0)]
    for dist in range(1, nz):
        items += [(dist, -1), (dist, 1)]

    def guard(item, fn):
        dist, side = item
        zz = z + side * dist
        if dist == 0:
            fn(zz)
        else:
            pl.when((zz >= 0) & (zz < nz))(lambda: fn(zz))

    def c_z(zz, src):
        dst = block(zz, x, y, c)
        return (remote(src, dst, s_u.at[zz], r_z.at[zz], up),
                remote(src, dst, s_d.at[zz], r_z.at[zz], down))

    def c_xy(zz, src):
        dst = block(zz, x, y, c)
        return (remote(src, dst, s_x.at[zz], r_x.at[zz], xn),
                remote(src, dst, s_y.at[zz], r_y.at[zz], yn))

    def c_p(zz, rel, src=None):
        xx = 1 - x if rel in (1, 3, 4) else x
        yy = 1 - y if rel in (2, 3, 4) else y
        part = {3: 0, 4: 1}.get(rel)
        dst = block(zz, xx, yy, c, part)
        k = zz * 5 + rel
        return remote(dst if src is None else src, dst, s_p.at[k], r_p.at[k], partner)

    def w_p(zz, rel):
        xx = 1 - x if rel in (1, 3, 4) else x
        yy = 1 - y if rel in (2, 3, 4) else y
        part = {3: 0, 4: 1}.get(rel)
        dst = block(zz, xx, yy, 1 - c, part)
        k = zz * 5 + rel
        return remote(dst, dst, s_p.at[k], r_p.at[k], partner)

    def c_diag(zz):
        a = block(zz, 1 - x, y, c, 0)
        b = block(zz, x, 1 - y, c, 1)
        return (remote(a, a, s_dy.at[zz], r_dy.at[zz], yn),
                remote(b, b, s_dx.at[zz], r_dx.at[zz], xn))

    def stage_a(item):
        dist, side = item

        def run(zz):
            src = x_ref if dist == 0 else block(zz, x, y, c)
            cu, cd = c_z(zz, src)
            if dist:
                cu.wait_recv()
            if side <= 0:
                pl.when(z < nz - 1)(cu.start)
            if dist == 0 or side > 0:
                pl.when(z > 0)(cd.start)
            for cc in c_xy(zz, src):
                cc.start()
            c_p(zz, 0, src).start()

        guard(item, run)

    def stage_b(item):
        def run(zz):
            cx, cy = c_xy(zz, block(zz, x, y, c))
            dy, dx = c_diag(zz)
            cx.wait_recv()
            dy.start()
            c_p(zz, 1).start()
            cy.wait_recv()
            dx.start()
            c_p(zz, 2).start()

        guard(item, run)

    def stage_c(item):
        def run(zz):
            dy, dx = c_diag(zz)
            dy.wait_recv()
            c_p(zz, 3).start()
            dx.wait_recv()
            c_p(zz, 4).start()

        guard(item, run)

    count = len(items)
    for k in range(count + 2):
        if k < count:
            stage_a(items[k])
        if 0 <= k - 1 < count:
            stage_b(items[k - 1])
        if 0 <= k - 2 < count:
            stage_c(items[k - 2])

    def finish(zz, carry):
        for rel in range(5):
            w_p(zz, rel).wait_recv()
            c_p(zz, rel).wait_send()
        cu, cd = c_z(zz, block(zz, x, y, c))
        pl.when((zz <= z) & (z < nz - 1))(cu.wait_send)
        pl.when((zz >= z) & (z > 0))(cd.wait_send)
        for cc in c_xy(zz, block(zz, x, y, c)) + c_diag(zz):
            cc.wait_send()
        return carry

    lax.fori_loop(0, nz, finish, 0)
    own.wait()


def gather_all(block, nz, collective_id):
    rows, cols = block.shape
    dma = pltpu.SemaphoreType.DMA
    return pl.pallas_call(
        functools.partial(gather_all_kernel, nz),
        out_shape=jax.ShapeDtypeStruct((rows * nz * 2, cols * 4), block.dtype),
        in_specs=[pl.BlockSpec(memory_space=pl.ANY)],
        out_specs=pl.BlockSpec(memory_space=pl.ANY),
        scratch_shapes=[dma] + [dma((5 * nz,))] + [dma((nz,))] * 6 + [dma((nz,))] * 5 + [dma((5 * nz,))],
        compiler_params=pltpu.CompilerParams(collective_id=collective_id, has_side_effects=True),
        name="gather_all",
    )(block)


def scatter_all_kernel(nz, p_ref, o_ref, w, lp, rx, rxd, ry, ryd, rz,
                       s_l, s_p, r_p, s_x, s_y, s_dx, s_dy, s_z, r_x, r_y, r_dx, r_dy, r_z):
    z, x, y, c = place()
    rows, cols = o_ref.shape
    half = rows // 2
    partner = device(z, x, y, 1 - c)
    xn = device(z, 1 - x, y, c)
    yn = device(z, x, 1 - y, c)
    up = device(z + 1, x, y, c)
    down = device(z - 1, x, y, c)
    greet([(None, partner), (None, xn), (None, yn), (z < nz - 1, up), (z > 0, down)])
    chunk = 64

    def block(zz, rel, cc):
        xx = 1 - x if rel in (1, 3) else x
        yy = 1 - y if rel in (2, 3) else y
        return p_ref.at[pl.ds(pl.multiple_of((zz * 2 + xx) * rows, rows), rows),
                        pl.ds(pl.multiple_of((yy * 2 + cc) * cols, cols), cols)]

    items = []
    for dist in range(nz - 1, 0, -1):
        items += [(dist, -1), (dist, 1)]
    items += [(0, 0)]

    def guard(item, fn):
        dist, side = item
        zz = z + side * dist
        if dist == 0:
            fn(zz)
        else:
            pl.when((zz >= 0) & (zz < nz))(lambda: fn(zz))

    def c_p(zz, rel):
        k = zz * 4 + rel
        return remote(block(zz, rel, 1 - c), lp.at[zz, rel], s_p.at[k], r_p.at[k], partner)

    def c_l(zz, rel):
        return pltpu.make_async_copy(block(zz, rel, c), w.at[zz, rel], s_l.at[zz * 4 + rel])

    def c_diag(zz):
        return (remote(w.at[zz, 3, pl.ds(0, half)], rxd.at[zz], s_dx.at[zz], r_dx.at[zz], xn),
                remote(w.at[zz, 3, pl.ds(half, half)], ryd.at[zz], s_dy.at[zz], r_dy.at[zz], yn))

    def c_xy(zz):
        return (remote(w.at[zz, 1], rx.at[zz], s_x.at[zz], r_x.at[zz], xn),
                remote(w.at[zz, 2], ry.at[zz], s_y.at[zz], r_y.at[zz], yn))

    def c_z(zz, slot, where):
        return remote(w.at[zz, 0], rz.at[slot], s_z.at[zz], r_z.at[slot], where)

    def add(dst, srcs, start, count):
        def step(i, carry):
            off = pl.multiple_of(i * chunk, chunk)
            here = pl.ds(pl.multiple_of(start + off, chunk), chunk)
            total = dst[here, :].astype(jnp.float32)
            for src in srcs:
                total = total + src[pl.ds(off, chunk), :].astype(jnp.float32)
            dst[here, :] = total.astype(dst.dtype)
            return carry
        lax.fori_loop(0, count // chunk, step, 0)

    def stage_0(item):
        def run(zz):
            for rel in (3, 1, 2, 0):
                c_p(zz, rel).start()
                c_l(zz, rel).start()
        guard(item, run)

    def stage_d(item):
        def run(zz):
            for rel in (3, 1, 2, 0):
                c_p(zz, rel).wait_recv()
                c_l(zz, rel).wait()
                add(w.at[zz, rel], [lp.at[zz, rel]], 0, rows)
                if rel == 3:
                    for cc in c_diag(zz):
                        cc.start()
        guard(item, run)

    def stage_e(item):
        def run(zz):
            dx, dy = c_diag(zz)
            cx, cy = c_xy(zz)
            dy.wait_recv()
            add(w.at[zz, 1], [ryd.at[zz]], half, half)
            cx.start()
            dx.wait_recv()
            add(w.at[zz, 2], [rxd.at[zz]], 0, half)
            cy.start()
        guard(item, run)

    def stage_f(item):
        dist, side = item

        def run(zz):
            cx, cy = c_xy(zz)
            cx.wait_recv()
            cy.wait_recv()
            if dist:
                add(w.at[zz, 0], [rx.at[zz], ry.at[zz]], 0, rows)
                has = z > 0 if side > 0 else z < nz - 1
                cz = c_z(zz, zz, up if side > 0 else down)

                @pl.when(has)
                def _():
                    cz.wait_recv()
                    add(w.at[zz, 0], [rz.at[zz]], 0, rows)
                if side > 0:
                    cz.start()
                else:
                    if dist == 1:
                        c_z(zz, nz, down).start()
                    else:
                        cz.start()
            else:
                below, above = c_z(zz, zz, up), c_z(zz, nz, down)

                def total(refs):
                    def step(i, carry):
                        here = pl.ds(pl.multiple_of(i * chunk, chunk), chunk)
                        acc = w[zz, 0, here, :].astype(jnp.float32)
                        for ref in refs:
                            acc = acc + ref[here, :].astype(jnp.float32)
                        o_ref[here, :] = acc
                        return carry
                    lax.fori_loop(0, rows // chunk, step, 0)

                pl.when(z > 0)(below.wait_recv)
                pl.when(z < nz - 1)(above.wait_recv)
                pl.when(z == 0)(lambda: total([rx.at[zz], ry.at[zz], rz.at[nz]]))
                pl.when(z == nz - 1)(lambda: total([rx.at[zz], ry.at[zz], rz.at[zz]]))
                pl.when((z > 0) & (z < nz - 1))(
                    lambda: total([rx.at[zz], ry.at[zz], rz.at[zz], rz.at[nz]]))
        guard(item, run)

    for item in items:
        stage_0(item)
    count = len(items)
    for k in range(count + 2):
        if k < count:
            stage_d(items[k])
        if 0 <= k - 1 < count:
            stage_e(items[k - 1])
        if 0 <= k - 2 < count:
            stage_f(items[k - 2])

    def finish(zz, carry):
        for rel in range(4):
            c_p(zz, rel).wait_send()
        for cc in c_diag(zz) + c_xy(zz):
            cc.wait_send()
        pl.when(zz != z)(c_z(zz, zz, up).wait_send)
        return carry

    lax.fori_loop(0, nz, finish, 0)


def scatter_all(partial, nz, collective_id):
    rows, cols = partial.shape[0] // (2 * nz), partial.shape[1] // 4
    half = rows // 2
    dma = pltpu.SemaphoreType.DMA
    kind = partial.dtype
    vm = pltpu.VMEM
    return pl.pallas_call(
        functools.partial(scatter_all_kernel, nz),
        out_shape=jax.ShapeDtypeStruct((rows, cols), jnp.float32),
        in_specs=[pl.BlockSpec(memory_space=pl.ANY)],
        out_specs=pl.BlockSpec(memory_space=pltpu.VMEM),
        scratch_shapes=[vm((nz, 4, rows, cols), kind), vm((nz, 4, rows, cols), kind),
                        vm((nz, rows, cols), kind), vm((nz, half, cols), kind),
                        vm((nz, rows, cols), kind), vm((nz, half, cols), kind),
                        vm((nz + 1, rows, cols), kind)]
        + [dma((4 * nz,))] * 3 + [dma((nz,))] * 5 + [dma((nz,))] * 4 + [dma((nz + 1,))],
        compiler_params=pltpu.CompilerParams(collective_id=collective_id, has_side_effects=True,
                                             vmem_limit_bytes=62 << 20),
        name="scatter_all",
    )(partial)


def z_items(nz, near_first):
    items = [(0, 0)] if near_first else []
    order = range(1, nz) if near_first else range(nz - 1, 0, -1)
    for dist in order:
        items += [(dist, -1), (dist, 1)]
    return items if near_first else items + [(0, 0)]


def z_guard(item, z, nz, fn):
    dist, side = item
    zz = z + side * dist
    if dist == 0:
        fn(zz)
    else:
        pl.when((zz >= 0) & (zz < nz))(lambda: fn(zz))


def gather_rows_kernel(nz, count, columns, narrow, *refs):
    total = count + columns
    srcs, refs = refs[:total], refs[total:]
    outs, refs = refs[:total], refs[total:]
    wide, refs = refs[: min(columns, 1)], refs[min(columns, 1) :]
    lsem, s_u, s_d, s_x, r_z, r_x, s_c, r_c, s_w, r_w = refs
    z, x, y, c = place()
    xn, up, down = device(z, 1 - x, y, c), device(z + 1, x, y, c), device(z - 1, x, y, c)
    partner, yn = device(z, x, y, 1 - c), device(z, x, 1 - y, c)
    wanted = [(None, xn), (z < nz - 1, up), (z > 0, down)]
    greet(wanted + [(None, partner), (None, yn), (None, device(nz - 1 - z, x, y, c))] * min(columns, 1))

    def block(n, zz, xx):
        rows = srcs[n].shape[0]
        return outs[n].at[pl.ds(pl.multiple_of((zz * 2 + xx) * rows, rows), rows)]

    own = [(srcs[n], block(n, z, x)) for n in range(count)]
    column_copies, swaps = [], []
    if columns:
        mirror = device(nz - 1 - z, x, y, c)
        first, out = outs[count], wide[0]
        rows, cols = first.shape
        top, bottom = pl.ds(0, rows // 2), pl.ds(rows // 2, rows // 2)
        for n in range(columns):
            src, dst = srcs[count + n], outs[count + n]
            swaps.append(remote(src.at[bottom], dst.at[bottom], s_w.at[n], r_w.at[n], mirror))
            dst[top, :] = src[top, :]

        def column(yy):
            return out.at[:, pl.ds(pl.multiple_of((yy * 2 + c) * cols, cols), cols)]

        column_copies = [
            remote(first, column(y), s_c.at[0], r_c.at[0], yn),
            remote(first, column(y), s_c.at[1], r_c.at[1], partner),
            remote(column(1 - y), column(1 - y), s_c.at[2], r_c.at[2], partner),
        ]
        last = pltpu.make_async_copy(first, column(y), lsem.at[total])
    own = [pltpu.make_async_copy(src, dst, lsem.at[n]) for n, (src, dst) in enumerate(own)]
    pairs = range(count - narrow, count)
    sides = [remote(srcs[n], block(n, z, x), s_x.at[n * nz], r_x.at[n * nz], xn) for n in pairs]
    for copy in swaps + own + sides:
        copy.start()

    def copies(n, zz, src):
        dst = block(n, zz, x)
        k = n * nz + zz
        if n in pairs:
            rows = 2 * srcs[n].shape[0]
            dst = src = outs[n].at[pl.ds(pl.multiple_of(zz * rows, rows), rows)]
        return (remote(src, dst, s_u.at[k], r_z.at[k], up),
                remote(src, dst, s_d.at[k], r_z.at[k], down),
                remote(src, dst, s_x.at[k], r_x.at[k], xn))

    items = z_items(nz, True)
    for item in items:
        dist, side = item

        def run(zz):
            for n in range(count):
                src = srcs[n] if dist == 0 else block(n, zz, x)
                cu, cd, cx = copies(n, zz, src)
                if dist:
                    cu.wait_recv()
                elif n in pairs:
                    own[n].wait()
                    sides[n - count + narrow].wait_recv()
                if side <= 0:
                    pl.when(z < nz - 1)(cu.start)
                if side > 0 or dist == 0:
                    pl.when(z > 0)(cd.start)
                if n not in pairs:
                    cx.start()

        z_guard(item, z, nz, run)
        if columns and item == items[-3]:
            swaps[0].wait_recv()
            column_copies[0].start()
            column_copies[1].start()
            last.start()
        if columns and item == items[-1]:
            column_copies[0].wait_recv()
            column_copies[2].start()

    def finish(zz, carry):
        for n in range(count):
            cu, cd, cx = copies(n, zz, block(n, zz, x))
            if n not in pairs:
                cx.wait_recv()
                cx.wait_send()
            pl.when((zz <= z) & (z < nz - 1))(cu.wait_send)
            pl.when((zz >= z) & (z > 0))(cd.wait_send)
        return carry

    lax.fori_loop(0, nz, finish, 0)
    for copy in own[: count - narrow]:
        copy.wait()
    for copy in sides:
        copy.wait_send()
    if columns:
        column_copies[0].wait_send()
        column_copies[1].wait()
        column_copies[2].wait()
        last.wait()
        swaps[0].wait_send()
        for copy in swaps[1:]:
            copy.wait()


def gather_rows(blocks, nz, collective_id, swapped=(), narrow=0):
    count, columns = len(blocks), len(swapped)
    dma = pltpu.SemaphoreType.DMA
    any_space = pl.BlockSpec(memory_space=pl.ANY)
    vmem = pl.BlockSpec(memory_space=pltpu.VMEM)
    shapes = [
        jax.ShapeDtypeStruct((b.shape[0] * nz * 2,) + b.shape[1:], b.dtype) for b in blocks
    ] + [jax.ShapeDtypeStruct(b.shape, b.dtype) for b in swapped]
    if columns:
        rows, cols = swapped[0].shape
        shapes.append(jax.ShapeDtypeStruct((rows, cols * 4), swapped[0].dtype))
    total = count + columns
    return pl.pallas_call(
        functools.partial(gather_rows_kernel, nz, count, columns, narrow),
        out_shape=shapes,
        in_specs=[vmem] * total,
        out_specs=[any_space] * count + [vmem] * columns + [any_space] * min(columns, 1),
        scratch_shapes=[dma((total + 1,))] + [dma((count * nz,))] * 5 + [dma((3,))] * 2
        + [dma((max(columns, 1),))] * 2,
        compiler_params=pltpu.CompilerParams(collective_id=collective_id, has_side_effects=True,
                                             vmem_limit_bytes=62 << 20),
        name="gather_rows",
    )(*blocks, *swapped)


def swap_back_kernel(nz, *refs):
    count = (len(refs) - 2) // 2
    srcs, outs = refs[:count], refs[count : 2 * count]
    s, r = refs[2 * count :]
    z, x, y, c = place()
    mirror = device(nz - 1 - z, x, y, c)
    greet([(None, mirror)])
    copies = [remote(src, out, s.at[n], r.at[n], mirror)
              for n, (src, out) in enumerate(zip(srcs, outs))]
    for copy in copies:
        copy.start()
    for copy in copies:
        copy.wait()


def swap_back(blocks, nz, collective_id):
    count = len(blocks)
    dma = pltpu.SemaphoreType.DMA
    any_space = pl.BlockSpec(memory_space=pl.ANY)
    return pl.pallas_call(
        functools.partial(swap_back_kernel, nz),
        out_shape=[jax.ShapeDtypeStruct(b.shape, b.dtype) for b in blocks],
        in_specs=[any_space] * count,
        out_specs=[any_space] * count,
        scratch_shapes=[dma((count,))] * 2,
        compiler_params=pltpu.CompilerParams(collective_id=collective_id, has_side_effects=True),
        name="swap_back",
    )(*blocks)


def add_blocks(dst, srcs, start, count, out=None, chunk=64):
    target = dst if out is None else out

    def step(i, carry):
        off = pl.multiple_of(i * chunk, chunk)
        here = pl.ds(pl.multiple_of(start + off, chunk), chunk)
        total = dst[here, :].astype(jnp.float32)
        for src in srcs:
            total = total + src[pl.ds(off, chunk), :].astype(jnp.float32)
        target[here, :] = total.astype(target.dtype)
        return carry

    lax.fori_loop(0, count // chunk, step, 0)


def reduce_rows_kernel(nz, p_ref, o_ref, w, rx, rz, s_l, s_x, s_z, r_x, r_z):
    z, x, y, c = place()
    rows = o_ref.shape[0]
    xn, up, down = device(z, 1 - x, y, c), device(z + 1, x, y, c), device(z - 1, x, y, c)
    greet([(None, xn), (z < nz - 1, up), (z > 0, down)])

    def block(zz, xx):
        return p_ref.at[pl.ds(pl.multiple_of((zz * 2 + xx) * rows, rows), rows)]

    def c_x(zz):
        return remote(block(zz, 1 - x), rx.at[zz], s_x.at[zz], r_x.at[zz], xn)

    def c_l(zz):
        return pltpu.make_async_copy(block(zz, x), w.at[zz], s_l.at[zz])

    def c_z(zz, slot, where):
        return remote(w.at[zz], rz.at[slot], s_z.at[zz], r_z.at[slot], where)

    items = z_items(nz, False)

    def start(zz):
        c_x(zz).start()
        c_l(zz).start()

    for item in items:
        z_guard(item, z, nz, start)
    for item in items:
        dist, side = item

        def run(zz):
            c_l(zz).wait()
            c_x(zz).wait_recv()
            if dist:
                add_blocks(w.at[zz], [rx.at[zz]], 0, rows)
                cz = c_z(zz, zz, up if side > 0 else down)

                @pl.when(z > 0 if side > 0 else z < nz - 1)
                def _():
                    cz.wait_recv()
                    add_blocks(w.at[zz], [rz.at[zz]], 0, rows)

                (c_z(zz, nz, down) if side < 0 and dist == 1 else cz).start()
            else:
                pl.when(z > 0)(c_z(zz, zz, up).wait_recv)
                pl.when(z < nz - 1)(c_z(zz, nz, down).wait_recv)
                low, high = rz.at[zz], rz.at[nz]
                pl.when(z == 0)(lambda: add_blocks(w.at[zz], [rx.at[zz], high], 0, rows, o_ref))
                pl.when(z == nz - 1)(lambda: add_blocks(w.at[zz], [rx.at[zz], low], 0, rows, o_ref))
                pl.when((z > 0) & (z < nz - 1))(
                    lambda: add_blocks(w.at[zz], [rx.at[zz], low, high], 0, rows, o_ref)
                )

        z_guard(item, z, nz, run)

    def finish(zz, carry):
        c_x(zz).wait_send()
        pl.when(zz != z)(c_z(zz, zz, up).wait_send)
        return carry

    lax.fori_loop(0, nz, finish, 0)


def reduce_rows(partial, nz, collective_id):
    rows, cols = partial.shape[0] // (2 * nz), partial.shape[1]
    dma, vm, kind = pltpu.SemaphoreType.DMA, pltpu.VMEM, partial.dtype
    return pl.pallas_call(
        functools.partial(reduce_rows_kernel, nz),
        out_shape=jax.ShapeDtypeStruct((rows, cols), jnp.float32),
        in_specs=[pl.BlockSpec(memory_space=pl.ANY)],
        out_specs=pl.BlockSpec(memory_space=pltpu.VMEM),
        scratch_shapes=[vm((nz, rows, cols), kind), vm((nz, rows, cols), kind),
                        vm((nz + 1, rows, cols), kind)]
        + [dma((nz,))] * 4 + [dma((nz + 1,))],
        compiler_params=pltpu.CompilerParams(
            collective_id=collective_id, has_side_effects=True, vmem_limit_bytes=62 << 20
        ),
        name="reduce_rows",
    )(partial)


def gather_cols_kernel(x_ref, o_ref, lsem, s_p, s_y, r_p, r_y):
    z, x, y, c = place()
    cols = x_ref.shape[1]
    partner, yn = device(z, x, y, 1 - c), device(z, x, 1 - y, c)
    greet([(None, partner), (None, yn)])

    def block(yy, cc):
        return o_ref.at[:, pl.ds(pl.multiple_of((yy * 2 + cc) * cols, cols), cols)]

    own = pltpu.make_async_copy(x_ref, block(y, c), lsem)
    cy = remote(x_ref, block(y, c), s_y, r_y, yn)
    cp = remote(x_ref, block(y, c), s_p.at[0], r_p.at[0], partner)
    cf = remote(block(1 - y, c), block(1 - y, c), s_p.at[1], r_p.at[1], partner)
    cy.start()
    cp.start()
    own.start()
    cy.wait_recv()
    cf.start()
    cp.wait()
    cf.wait()
    cy.wait_send()
    own.wait()


def gather_cols(block, collective_id):
    dma = pltpu.SemaphoreType.DMA
    any_space = pl.BlockSpec(memory_space=pl.ANY)
    return pl.pallas_call(
        gather_cols_kernel,
        out_shape=jax.ShapeDtypeStruct((block.shape[0], block.shape[1] * 4), block.dtype),
        in_specs=[any_space],
        out_specs=any_space,
        scratch_shapes=[dma, dma((2,)), dma, dma((2,)), dma],
        compiler_params=pltpu.CompilerParams(collective_id=collective_id, has_side_effects=True),
        name="gather_cols",
    )(block)


def reduce_cols_kernel(p_ref, o_ref, w, rp, ry, s_l, s_p, s_y, r_p, r_y):
    z, x, y, c = place()
    rows, cols = o_ref.shape
    partner, yn = device(z, x, y, 1 - c), device(z, x, 1 - y, c)
    greet([(None, partner), (None, yn)])

    def block(yy, cc):
        return p_ref.at[:, pl.ds(pl.multiple_of((yy * 2 + cc) * cols, cols), cols)]

    sends = [remote(block(yy, 1 - c), rp.at[k], s_p.at[k], r_p.at[k], partner)
             for k, yy in enumerate((1 - y, y))]
    loads = [pltpu.make_async_copy(block(yy, c), w.at[k], s_l.at[k])
             for k, yy in enumerate((1 - y, y))]
    cy = remote(w.at[0], ry, s_y, r_y, yn)
    for k in range(2):
        sends[k].start()
        loads[k].start()
    loads[0].wait()
    sends[0].wait_recv()
    add_blocks(w.at[0], [rp.at[0]], 0, rows)
    cy.start()
    loads[1].wait()
    sends[1].wait_recv()
    cy.wait_recv()
    add_blocks(w.at[1], [rp.at[1], ry], 0, rows, o_ref)
    for k in range(2):
        sends[k].wait_send()
    cy.wait_send()


def reduce_cols(partial, collective_id):
    rows, cols = partial.shape[0], partial.shape[1] // 4
    dma, vm, kind = pltpu.SemaphoreType.DMA, pltpu.VMEM, partial.dtype
    return pl.pallas_call(
        reduce_cols_kernel,
        out_shape=jax.ShapeDtypeStruct((rows, cols), jnp.float32),
        in_specs=[pl.BlockSpec(memory_space=pl.ANY)],
        out_specs=pl.BlockSpec(memory_space=pltpu.VMEM),
        scratch_shapes=[vm((2, rows, cols), kind), vm((2, rows, cols), kind), vm((rows, cols), kind),
                        dma((2,)), dma((2,)), dma, dma((2,)), dma],
        compiler_params=pltpu.CompilerParams(
            collective_id=collective_id, has_side_effects=True, vmem_limit_bytes=62 << 20
        ),
        name="reduce_cols",
    )(partial)


def sum_cols_kernel(v_ref, o_ref, got, s, r):
    group = lax.axis_index("tp")
    shard = lax.axis_index("fsdp")
    peers = [(shard, (group + k) % 4) for k in range(1, 4)]
    greet([(None, peer) for peer in peers])
    copies = [remote(v_ref, got.at[k], s.at[k], r.at[k], peer) for k, peer in enumerate(peers)]
    for copy in copies:
        copy.start()
    for copy in copies:
        copy.wait()
    o_ref[...] = v_ref[...] + got[0] + got[1] + got[2]


def sum_cols(vector, collective_id):
    dma = pltpu.SemaphoreType.DMA
    shape = vector.shape
    return pl.pallas_call(
        sum_cols_kernel,
        out_shape=jax.ShapeDtypeStruct(shape, jnp.float32),
        in_specs=[pl.BlockSpec(memory_space=pltpu.VMEM)],
        out_specs=pl.BlockSpec(memory_space=pltpu.VMEM),
        scratch_shapes=[pltpu.VMEM((3,) + shape, jnp.float32), dma((3,)), dma((3,))],
        compiler_params=pltpu.CompilerParams(collective_id=collective_id, has_side_effects=True),
        name="sum_cols",
    )(vector)


def greet_all(shard, group, shards, groups):
    barrier = pltpu.get_barrier_semaphore()
    total = shards * groups

    def step(k, carry):
        other = (shard * groups + group + k) % total
        pl.semaphore_signal(
            barrier, inc=1, device_id=(other // groups, other % groups), device_id_type=MESH
        )
        return carry

    lax.fori_loop(1, total, step, 0)
    pl.semaphore_wait(barrier, total - 1)


def swap_rows_kernel(shards, groups, v_ref, o_ref, s, r):
    shard, group = lax.axis_index("fsdp"), lax.axis_index("tp")
    total = shards * groups
    me = shard * groups + group
    greet_all(shard, group, shards, groups)

    def copy(k):
        other = (me + k) % total
        return remote(v_ref.at[other // groups], o_ref.at[me], s.at[k], r.at[k],
                      (other // groups, other % groups))

    def start(k, carry):
        copy(k).start()
        return carry

    def wait(k, carry):
        copy(k).wait()
        return carry

    lax.fori_loop(1, total, start, 0)
    o_ref[me] = v_ref[shard]
    lax.fori_loop(1, total, wait, 0)


def swap_rows(values, shards, groups, collective_id):
    dma, total = pltpu.SemaphoreType.DMA, shards * groups
    return pl.pallas_call(
        functools.partial(swap_rows_kernel, shards, groups),
        out_shape=jax.ShapeDtypeStruct((total,) + values.shape[1:], values.dtype),
        in_specs=[pl.BlockSpec(memory_space=pltpu.VMEM)],
        out_specs=pl.BlockSpec(memory_space=pltpu.VMEM),
        scratch_shapes=[dma((total,)), dma((total,))],
        compiler_params=pltpu.CompilerParams(collective_id=collective_id, has_side_effects=True),
        name="swap_rows",
    )(values)


def sum_small_kernel(shards, groups, v_ref, o_ref, got, s1, r1, s2, r2):
    shard, group = lax.axis_index("fsdp"), lax.axis_index("tp")
    total = shards * groups
    me = shard * groups + group
    greet_all(shard, group, shards, groups)

    def first(k):
        other = (shard + k) % shards
        return remote(v_ref.at[other], got.at[k], s1.at[k], r1.at[k], (other, group))

    def second(k):
        other = (me + k) % total
        return remote(o_ref.at[me], o_ref.at[me], s2.at[k], r2.at[k],
                      (other // groups, other % groups))

    for k in range(1, shards):
        first(k).start()
    acc = v_ref[shard]
    for k in range(1, shards):
        first(k).wait()
        acc = acc + got[k]
    o_ref[me] = acc

    def start(k, carry):
        second(k).start()
        return carry

    def wait(k, carry):
        second(k).wait()
        return carry

    lax.fori_loop(1, total, start, 0)
    lax.fori_loop(1, total, wait, 0)


def sum_small(values, shards, groups, collective_id):
    dma, total = pltpu.SemaphoreType.DMA, shards * groups
    part = values.shape[1:]
    return pl.pallas_call(
        functools.partial(sum_small_kernel, shards, groups),
        out_shape=jax.ShapeDtypeStruct((total,) + part, values.dtype),
        in_specs=[pl.BlockSpec(memory_space=pltpu.VMEM)],
        out_specs=pl.BlockSpec(memory_space=pltpu.VMEM),
        scratch_shapes=[pltpu.VMEM((shards,) + part, values.dtype), dma((shards,)), dma((shards,)),
                        dma((total,)), dma((total,))],
        compiler_params=pltpu.CompilerParams(collective_id=collective_id, has_side_effects=True),
        name="sum_small",
    )(values)


def dot_plain(left, right):
    return jnp.dot(left, right, preferred_element_type=jnp.float32)


def far_first(nz, z, k):
    at = 0
    for here in range(nz):
        order = sorted(range(nz), key=lambda other: (-abs(other - here), other))
        for step, other in enumerate(order):
            at = at + jnp.where((z == here) & (k == step), other, 0)
    return at


def tile_item(nz, z, k):
    return far_first(nz, z, jnp.where(k == nz - 1, nz - 1, nz - 2 - k))


def line_schedule(nz):
    order = []
    for here in range(nz):
        near = sorted(range(nz), key=lambda other: (-abs(other - here), other))[::-1]
        order.append(near[1:] + near[:1])
    sent = {}
    steps = [{} for _ in range(nz)]

    def send(here, to):
        if (here, to) not in sent:
            ready = 2 * order[here].index(to) + 2
            back = here - 1 if to > here else here + 1
            if 0 <= back < nz:
                ready = max(ready, send(back, to)) + 1
                steps[here].setdefault(ready, []).append(to)
            sent[here, to] = ready
        return sent[here, to]

    for here in range(nz):
        for to in range(nz):
            if to != here:
                send(here, to)
    for here in range(nz):
        arrivals = [send(near, here) for near in (here - 1, here + 1) if 0 <= near < nz]
        last = max(arrivals + [2 * order[here].index(here) + 2]) + 1
        steps[here].setdefault(last, []).append(here)
    return steps


def expert_kernel(nz, slots, block_rows, tok_ref, gain_ref, router_ref, attn_part, g_all, routes_all,
                  wg_all, wu_all, wd_all, middle_ref, scale_ref, low_ref, x_all, out_all, back_ref, gg_got, gates_ref, xr_all, gs_all, hid_all, gp_all, up_all,
                  wg, wu, wd, s_in_w, gg_ref, x_ref, g_ref, t_ref, o_ref, xr, gs, hid, gp, up, st,
                  w, lp, rx, rxd, ry, ryd, rz,
                  s_in, s_out, s_save, s_p, r_p, s_x, s_y, s_dx, s_dy, s_z, r_x, r_y, r_dx, r_dy, r_z,
                  s_g, r_g, *refs):
    z, x, y, c = place()
    shard, group = lax.axis_index("fsdp"), lax.axis_index("tp")
    expert = shard * 4 + group
    rows, cols = back_ref.shape
    width = x_ref.shape[1]
    half = rows // 2
    blocks = rows // block_rows
    experts = router_ref.shape[1]
    f32, low = jnp.float32, jnp.bfloat16
    partner = device(z, x, y, 1 - c)
    xn, yn = device(z, 1 - x, y, c), device(z, x, 1 - y, c)
    up_dev, down_dev = device(z + 1, x, y, c), device(z - 1, x, y, c)
    n_c, n_s = len(ReduceCols.scratch(16, 128, low)), len(RowSums.scratch(128))
    columns = ReduceCols(attn_part, middle_ref, refs[:n_c])
    sums = RowSums(refs[n_c : n_c + n_s])
    n_g = len(GatherAll.scratch(nz))
    moe_rows = [GatherAll(nz, part, x_all, refs[n_c + n_s + n * n_g : n_c + n_s + (n + 1) * n_g],
                          half // 2, n, 2) for n, part in enumerate(halves(low_ref))]

    def rows_step(name, *args):
        for part in moe_rows:
            getattr(part, name)(*args)

    greet_all(shard, group, 2 * nz, 4)
    columns.start()
    tiles = 2 * nz
    devices = 8 * nz

    def swap(k):
        other = (expert + k) % devices
        return remote(gg_ref.at[other // 4], gg_got.at[expert], s_g.at[k], r_g.at[k],
                      (other // 4, other % 4))

    def tile_of(j):
        return tile_item(nz, z, j // 2) * 2 + jnp.where(j % 2 == 0, 1 - x, x)

    def tile_rows(j):
        return pl.ds(pl.multiple_of(tile_of(j) * rows, rows), rows)

    def load(j):
        return pltpu.make_async_copy(x_all.at[tile_rows(j)], x_ref, s_in.at[0])

    def load_g(j):
        tile = tile_of(j)
        first = pl.ds(pl.multiple_of(tile * rows, half), half)
        second = pl.ds(pl.multiple_of(mirrored(nz, tile) * rows + half, half), half)
        return (pltpu.make_async_copy(g_all.at[first], g_ref.at[pl.ds(0, half)], s_in.at[1]),
                pltpu.make_async_copy(g_all.at[second], g_ref.at[pl.ds(half, half)], s_in.at[3]))

    def load_t(j):
        tile = tile_of(j)
        first = pl.ds(pl.multiple_of(tile * rows, half), half)
        second = pl.ds(pl.multiple_of(mirrored(nz, tile) * rows + half, half), half)
        return (pltpu.make_async_copy(routes_all.at[first], t_ref.at[pl.ds(0, half)], s_in.at[2]),
                pltpu.make_async_copy(routes_all.at[second], t_ref.at[pl.ds(half, half)], s_in.at[4]))

    def save_out(j):
        return pltpu.make_async_copy(o_ref, out_all.at[tile_rows(j)], s_out)

    def saves(j):
        pairs = ((xr, xr_all), (gs, gs_all), (hid, hid_all), (gp, gp_all), (up, up_all))
        return [pltpu.make_async_copy(src, dst.at[j], s_save.at[n])
                for n, (src, dst) in enumerate(pairs)]

    def c_p(zz, rel, slot):
        k = zz * 4 + rel
        return remote(st.at[slot, rel // 2], lp.at[zz, rel], s_p.at[k], r_p.at[k], partner)

    def c_diag(zz):
        return (remote(w.at[zz, 3, pl.ds(0, half)], rxd.at[zz], s_dx.at[zz], r_dx.at[zz], xn),
                remote(w.at[zz, 3, pl.ds(half, half)], ryd.at[zz], s_dy.at[zz], r_dy.at[zz], yn))

    def c_xy(zz):
        return (remote(w.at[zz, 1], rx.at[zz], s_x.at[zz], r_x.at[zz], xn),
                remote(w.at[zz, 2], ry.at[zz], s_y.at[zz], r_y.at[zz], yn))

    def c_z(zz, slot, where):
        return remote(w.at[zz, 0], rz.at[slot], s_z.at[zz], r_z.at[slot], where)

    def send_z(zz):
        pl.when(zz > z)(lambda: c_z(zz, zz, up_dev).start())
        pl.when(zz == z - 1)(lambda: c_z(zz, nz, down_dev).start())
        pl.when(zz < z - 1)(lambda: c_z(zz, zz, down_dev).start())

    def stage_d(zz, rel, slot):
        c_p(zz, rel, slot).wait_recv()
        add_blocks(w.at[zz, rel], [lp.at[zz, rel]], 0, rows)
        if rel == 3:
            for copy in c_diag(zz):
                copy.start()

    def stage_e(zz):
        dx, dy = c_diag(zz)
        cx, cy = c_xy(zz)
        dy.wait_recv()
        add_blocks(w.at[zz, 1], [ryd.at[zz]], half, half)
        cx.start()
        dx.wait_recv()
        add_blocks(w.at[zz, 2], [rxd.at[zz]], 0, half)
        cy.start()

    def passes(zz):
        return ((zz > z) & (z > 0)) | ((zz < z) & (z < nz - 1))

    def stage_f1(zz):
        cx, cy = c_xy(zz)
        cx.wait_recv()
        cy.wait_recv()
        add_blocks(w.at[zz, 0], [rx.at[zz], ry.at[zz]], 0, rows)
        pl.when((zz != z) & jnp.logical_not(passes(zz)))(lambda: send_z(zz))

    def stage_f2(zz):
        @pl.when((zz != z) & passes(zz))
        def _():
            c_z(zz, zz, up_dev).wait_recv()
            add_blocks(w.at[zz, 0], [rz.at[zz]], 0, rows)
            send_z(zz)

        @pl.when(zz == z)
        def _():
            low_part, high_part = rz.at[zz], rz.at[nz]
            pl.when(z > 0)(lambda: c_z(zz, zz, up_dev).wait_recv())
            pl.when(z < nz - 1)(lambda: c_z(zz, nz, down_dev).wait_recv())
            own = w.at[zz, 0]
            pl.when(z == 0)(lambda: add_blocks(own, [high_part], 0, rows, back_ref))
            pl.when(z == nz - 1)(lambda: add_blocks(own, [low_part], 0, rows, back_ref))
            pl.when((z > 0) & (z < nz - 1))(
                lambda: add_blocks(own, [low_part, high_part], 0, rows, back_ref)
            )

    def compute(j):
        zz = tile_item(nz, z, j // 2)
        slot = j % 2
        load(j).wait()
        for copy in load_t(j):
            copy.wait()
        lanes = lax.broadcasted_iota(jnp.int32, (rows, experts), 1)
        routes = t_ref[...]
        chosen = routes[:, 0:1] == lanes
        for n in range(1, TOPK):
            chosen = chosen | (routes[:, n : n + 1] == lanes)
        logits = jnp.where(chosen, dot_plain(x_ref[...], router_ref[...]), masked_score)
        peak = jnp.max(logits, axis=1, keepdims=True)
        weights = jnp.where(chosen, jnp.exp(logits - peak), 0.0)
        gates = weights / jnp.sum(weights, axis=1, keepdims=True)
        gates_ref[...] = gates
        mine = lanes == expert
        gate_col = jnp.sum(jnp.where(mine, gates, 0.0), axis=1, keepdims=True)
        match_col = jnp.sum(jnp.where(mine & chosen, 1.0, 0.0), axis=1, keepdims=True)
        sub = lax.broadcasted_iota(jnp.int32, (block_rows, block_rows), 0)
        lane = lax.broadcasted_iota(jnp.int32, (block_rows, block_rows), 1)
        eye = sub == lane
        before = (sub > lane).astype(f32).astype(low)
        chosen_low = chosen.astype(f32).astype(low)
        pick, put, slot_gate = [], [], []
        slot_lane = lax.broadcasted_iota(jnp.int32, (block_rows, slots), 1).astype(f32)
        slot_sub = lax.broadcasted_iota(jnp.int32, (slots, block_rows), 0).astype(f32)
        for b in range(blocks):
            part = slice(b * block_rows, (b + 1) * block_rows)
            ranks = dot_plain(before, chosen_low[part])
            rank = jnp.sum(jnp.where(mine[part], ranks, 0.0), axis=1, keepdims=True)
            rank = jnp.where(match_col[part] > 0.0, rank, -1.0)
            rank_row = jnp.sum(jnp.where(eye, rank, 0.0), axis=0, keepdims=True)
            gate_row = jnp.sum(jnp.where(eye, gate_col[part], 0.0), axis=0, keepdims=True)
            hot = rank_row == slot_sub
            pick.append(hot.astype(f32).astype(low))
            put.append((rank == slot_lane).astype(f32).astype(low))
            slot_gate.append(jnp.sum(jnp.where(hot, gate_row, 0.0), axis=1, keepdims=True))
        slot_gate = jnp.concatenate(slot_gate, axis=0)

        def gather(ref, at):
            return jnp.concatenate(
                [dot_plain(pick[b], ref[pl.ds(b * block_rows, block_rows), at])
                 for b in range(blocks)],
                axis=0,
            )

        def scatter(ref, at, values):
            for b in range(blocks):
                ref[pl.ds(b * block_rows, block_rows), at] = dot_plain(
                    put[b], values[b * slots : (b + 1) * slots]
                ).astype(low)

        def columns(i):
            return pl.ds(pl.multiple_of(i * cols, cols), cols)

        @pl.when(j > 0)
        def _():
            for copy in saves(j):
                copy.wait()

        def take(i, carry):
            xr[:, columns(i)] = gather(x_ref, columns(i)).astype(low)
            return carry

        lax.fori_loop(0, width // cols, take, 0)

        pl.when(j == 0)(lambda: rows_step('second', 2))
        for k in range(3, nz):
            pl.when(j == 1)(lambda: rows_step('second', k))

        @pl.when((j % 2 == 1) & (j < tiles - 1))
        def _():
            rows_step('ready', tile_item(nz, z, j // 2 + 1))

        @pl.when(j < tiles - 1)
        def _():
            load(j + 1).start()
            for copy in load_t(j + 1):
                copy.start()

        gate_pre = dot_plain(xr[...], wg[...])
        up_pre = dot_plain(xr[...], wu[...])
        sig = jax.nn.sigmoid(gate_pre)
        silu = gate_pre * sig
        hidden_low = (silu * up_pre).astype(low)
        hid[...] = hidden_low
        for copy in load_g(j):
            copy.wait()
        pl.when(j > 0)(lambda: save_out(j).wait())

        def middle_part(i, carry):
            total, hidden_grad = carry
            at = columns(i)
            grad = gather(g_ref, at)
            expert_out = dot_plain(hidden_low, wd[:, at]).astype(low).astype(f32)
            total = total + jnp.sum(grad * expert_out, axis=1, keepdims=True)
            pair_grad = (grad * slot_gate).astype(low)
            gs[:, at] = pair_grad
            scatter(o_ref, at, (expert_out * slot_gate).astype(low))
            return total, hidden_grad + dot_last(pair_grad, wd[:, at])

        gates_grad, hidden_grad = lax.fori_loop(
            0,
            width // cols,
            middle_part,
            (jnp.zeros(slot_gate.shape, f32), jnp.zeros(gate_pre.shape, f32)),
            unroll=2,
        )
        save_out(j).start()

        @pl.when(j < tiles - 1)
        def _():
            for copy in load_g(j + 1):
                copy.start()

        for b in range(blocks):
            gg_ref[tile_of(j), :, pl.ds(b * block_rows, block_rows)] = jnp.sum(
                pick[b].astype(f32) * gates_grad[b * slots : (b + 1) * slots],
                axis=0,
                keepdims=True,
            )
        gate_grad = (hidden_grad * up_pre * (sig * (1.0 + gate_pre * (1.0 - sig)))).astype(low)
        up_grad = (hidden_grad * silu).astype(low)
        gp[...] = gate_grad
        up[...] = up_grad
        for copy in saves(j):
            copy.start()

        def part_of(i, yy, cc):
            at = columns(yy * 2 + cc)
            row_grad = dot_last(gate_grad, wg[at, :]) + dot_last(up_grad, wu[at, :])
            return row_grad.astype(low)

        first = jnp.where(slot == 0, 1, 0)

        def to_partner(i, carry):
            yy = jnp.where(i == 1, 1 - y, y)
            rel = first + 2 * i

            @pl.when(j >= 2)
            def _():
                before_zz = tile_item(nz, z, j // 2 - 1)
                k = before_zz * 4 + rel
                remote(st.at[slot, i], lp.at[before_zz, rel], s_p.at[k], r_p.at[k], partner).wait_send()

            scatter(st.at[slot, i], slice(None), part_of(i, yy, 1 - c))
            k = zz * 4 + rel
            remote(st.at[slot, i], lp.at[zz, rel], s_p.at[k], r_p.at[k], partner).start()
            return carry

        def to_own(i, carry):
            yy = jnp.where(i == 1, 1 - y, y)
            scatter(w.at[zz, first + 2 * i], slice(None), part_of(i, yy, c))
            return carry

        lax.fori_loop(0, 2, to_partner, 0)
        lax.fori_loop(0, 2, to_own, 0)

    weights = [pltpu.make_async_copy(src, dst, s_in_w.at[n])
               for n, (src, dst) in enumerate(((wg_all, wg), (wu_all, wu), (wd_all, wd)))]
    for copy in load_t(0) + load_g(0) + tuple(weights):
        copy.start()

    corner = diagonal()
    columns.first()
    columns.second()

    def residual(n, carry):
        here = pl.ds(pl.multiple_of(n * 128, 128), 128)
        total = middle_ref[here, :] + tok_ref[here, :].astype(f32)
        middle_ref[here, :] = total
        sums.got[0, pl.ds(n, 1), :] = to_row(jnp.sum(total * total, axis=1, keepdims=True), corner)
        return carry

    def norm(n, carry):
        here = pl.ds(pl.multiple_of(n * 128, 128), 128)
        scale = lax.rsqrt(to_column(sums.total(n), corner) / width + norm_eps)
        scale_ref[here, :] = scale
        gain = gain_ref[:, pl.ds(pl.multiple_of(group * cols, cols), cols)]
        low_ref[here, :] = (middle_ref[here, :] * scale * gain).astype(low)
        return carry

    lax.fori_loop(0, rows // 128, residual, 0)
    sums.start()
    sums.wait()
    lax.fori_loop(0, rows // 128, norm, 0)
    for part in moe_rows:
        part.own().start()
    for part in moe_rows:
        part.own().wait()
    rows_step('first', 0)
    rows_step('first', 1)
    rows_step('second', 0)
    rows_step('first', 2)
    rows_step('second', 1)
    rows_step('third', 0)
    for k in range(3, nz):
        rows_step('first', k)
    rows_step('third', 1)
    rows_step('ready', tile_item(nz, z, 0))
    load(0).start()
    for copy in weights:
        copy.wait()
    schedule = line_schedule(nz)
    last_step = max(max(steps) for steps in schedule)

    def step(j, carry):
        k, odd = j // 2, j % 2 == 1
        pl.when(j < tiles)(lambda: compute(j))
        pl.when(j == 0)(lambda: rows_step('third', 2))
        for n in range(3, nz):
            pl.when(j == 2)(lambda: rows_step('third', n))

        @pl.when(j == tiles)
        def _():
            gg_got[expert] = gg_ref[shard]
            loop_from_one(devices, lambda n: swap(n).start())

        @pl.when(jnp.logical_not(odd) & (k < nz))
        def _():
            zz = tile_item(nz, z, k)
            stage_d(zz, 3, 0)
            stage_d(zz, 1, 0)

        @pl.when(odd & (k < nz))
        def _():
            zz = tile_item(nz, z, k)
            stage_d(zz, 2, 1)
            stage_d(zz, 0, 1)
            stage_e(zz)

        @pl.when((k >= 1) & (k < nz + 1) & jnp.logical_not(odd))
        def _():
            stage_f1(tile_item(nz, z, k - 1))

        for here, steps in enumerate(schedule):
            for at, places in steps.items():
                for to in places:
                    pl.when((z == here) & (j == at))(lambda to=to: stage_f2(jnp.int32(to)))

        return carry

    lax.fori_loop(0, last_step + 1, step, 0)
    loop_from_one(devices, lambda n: swap(n).wait())
    save_out(tiles - 1).wait()
    for copy in saves(tiles - 1):
        copy.wait()
    for slot in range(2):
        for i in range(2):
            c_p(z, 1 - slot + 2 * i, slot).wait_send()

    def finish(zz, carry):
        for copy in c_diag(zz) + c_xy(zz):
            copy.wait_send()
        pl.when(zz != z)(c_z(zz, zz, up_dev).wait_send)
        return carry

    lax.fori_loop(0, nz, finish, 0)
    columns.finish()
    rows_step('finish_sends')


def run_experts(tokens, gain, router, attn_part, g_all, routes_all, gate_w, up_w, down_w, block_rows,
                slots, nz, collective_id):
    total, width = g_all.shape
    hidden = gate_w.shape[1]
    experts = router.shape[1]
    tiles = 2 * nz
    rows, cols = total // tiles, width // 4
    pairs = rows // block_rows * slots
    half = rows // 2
    f32, low = jnp.float32, jnp.bfloat16
    any_space = pl.BlockSpec(memory_space=pl.ANY)
    vmem = pl.BlockSpec(memory_space=pltpu.VMEM)
    vm, dma, shape = pltpu.VMEM, pltpu.SemaphoreType.DMA, jax.ShapeDtypeStruct
    return pl.pallas_call(
        functools.partial(expert_kernel, nz, slots, block_rows),
        in_specs=[vmem] * 3 + [any_space] * 6,
        out_specs=[vmem] * 3 + [any_space] * 2 + [vmem] * 3 + [any_space] * 5,
        out_shape=[
            shape((rows, cols), f32), shape((rows, 1), f32), shape((rows, cols), low),
            shape((total, width), low),
            shape((total, width), low), shape((rows, cols), f32), shape((4 * tiles, 1, rows), f32),
            shape((rows, experts), f32),
            shape((tiles, pairs, width), low), shape((tiles, pairs, width), low),
            shape((tiles, pairs, hidden), low), shape((tiles, pairs, hidden), low),
            shape((tiles, pairs, hidden), low),
        ],
        scratch_shapes=[
            vm((width, hidden), low), vm((width, hidden), low), vm((hidden, width), low), dma((3,)),
            vm((tiles, 1, rows), f32), vm((rows, width), low), vm((rows, width), low),
            vm((rows, routes_all.shape[1]), jnp.int32), vm((rows, width), low),
            vm((pairs, width), low), vm((pairs, width), low),
            vm((pairs, hidden), low), vm((pairs, hidden), low), vm((pairs, hidden), low),
            vm((2, 2, rows, cols), low),
            vm((nz, 4, rows, cols), low), vm((nz, 4, rows, cols), low),
            vm((nz, rows, cols), low), vm((nz, half, cols), low),
            vm((nz, rows, cols), low), vm((nz, half, cols), low),
            vm((nz + 1, rows, cols), low),
            dma((5,)), dma, dma((5,)), dma((4 * nz,)), dma((4 * nz,)),
        ] + [dma((nz,))] * 9 + [dma((nz + 1,))] + [dma((4 * tiles,))] * 2
        + ReduceCols.scratch(rows, cols, low) + RowSums.scratch(rows) + GatherAll.scratch(nz) * 2,
        compiler_params=pltpu.CompilerParams(
            collective_id=collective_id, has_side_effects=True, vmem_limit_bytes=62 << 20
        ),
        name="experts",
    )(tokens, gain, router, attn_part, g_all, routes_all, gate_w, up_w, down_w)


def near_first(nz, z, k):
    return far_first(nz, z, nz - 1 - k)


def halves(ref):
    rows = ref.shape[0] // 2
    return [ref.at[pl.ds(part * rows, rows)] for part in range(2)]


class GatherAll:
    sems = 6

    @staticmethod
    def scratch(nz):
        dma = pltpu.SemaphoreType.DMA
        return [dma] + [dma((5 * nz,))] * 2 + [dma((nz,))] * 11

    def __init__(self, nz, src, out, sems, cut, part=0, parts=1):
        (self.lsem, self.s_p, self.r_p, self.s_u, self.s_d, self.s_x, self.s_y, self.s_dx,
         self.s_dy, self.r_z, self.r_x, self.r_y, self.r_dx, self.r_dy) = sems
        self.nz, self.src, self.out, self.cut = nz, src, out, cut
        self.rows, self.cols = src.shape
        self.offset, self.stride = part * self.rows, parts * self.rows
        self.place = z, x, y, c = place()
        self.partner, self.xn, self.yn = (
            device(z, x, y, 1 - c), device(z, 1 - x, y, c), device(z, x, 1 - y, c))
        self.up, self.down = device(z + 1, x, y, c), device(z - 1, x, y, c)

    def block(self, zz, xx, yy, cc, part=None):
        start, size, unit = (zz * 2 + xx) * self.stride + self.offset, self.rows, self.rows
        if part == 0:
            size, unit = self.cut, self.rows
        elif part == 1:
            start, size = start + self.cut, self.rows - self.cut
            unit = math.gcd(self.cut, self.rows)
        return self.out.at[pl.ds(pl.multiple_of(start, unit), size),
                           pl.ds(pl.multiple_of((yy * 2 + cc) * self.cols, self.cols), self.cols)]

    def own(self):
        z, x, y, c = self.place
        return pltpu.make_async_copy(self.src, self.block(z, x, y, c), self.lsem)

    def line(self, zz):
        z, x, y, c = self.place
        here = self.block(zz, x, y, c)
        return (remote(here, here, self.s_u.at[zz], self.r_z.at[zz], self.up),
                remote(here, here, self.s_d.at[zz], self.r_z.at[zz], self.down))

    def sides(self, zz):
        z, x, y, c = self.place
        here = self.block(zz, x, y, c)
        return (remote(here, here, self.s_x.at[zz], self.r_x.at[zz], self.xn),
                remote(here, here, self.s_y.at[zz], self.r_y.at[zz], self.yn))

    def across(self, zz):
        z, x, y, c = self.place
        copies = []
        if self.cut > 0:
            here = self.block(zz, 1 - x, y, c, 0)
            copies.append(remote(here, here, self.s_dy.at[zz], self.r_dy.at[zz], self.yn))
        if self.cut < self.rows:
            here = self.block(zz, x, 1 - y, c, 1)
            copies.append(remote(here, here, self.s_dx.at[zz], self.r_dx.at[zz], self.xn))
        return copies

    def pair(self, zz, rel, mine=True):
        z, x, y, c = self.place
        xx = 1 - x if rel in (1, 3, 4) else x
        yy = 1 - y if rel in (2, 3, 4) else y
        here = self.block(zz, xx, yy, c if mine else 1 - c, {3: 0, 4: 1}.get(rel))
        k = zz * 5 + rel
        return remote(here, here, self.s_p.at[k], self.r_p.at[k], self.partner)

    def parts(self):
        return [0, 1, 2] + [3] * (self.cut > 0) + [4] * (self.cut < self.rows)

    def first(self, k):
        self.first_to(near_first(self.nz, self.place[0], k))

    def second(self, k):
        self.second_to(near_first(self.nz, self.place[0], k))

    def third(self, k):
        self.third_to(near_first(self.nz, self.place[0], k))

    def first_to(self, zz):
        z = self.place[0]
        up, down = self.line(zz)
        pl.when(zz != z)(lambda: up.wait_recv())
        pl.when((zz <= z) & (z < self.nz - 1))(lambda: up.start())
        pl.when((zz >= z) & (z > 0))(lambda: down.start())
        for copy in self.sides(zz):
            copy.start()
        self.pair(zz, 0).start()

    def second_to(self, zz):
        to_x, to_y = self.sides(zz)
        across = self.across(zz)
        to_x.wait_recv()
        if self.cut > 0:
            across[0].start()
        self.pair(zz, 1).start()
        to_y.wait_recv()
        if self.cut < self.rows:
            across[-1].start()
        self.pair(zz, 2).start()

    def third_to(self, zz):
        across = self.across(zz)
        for rel, copy in zip(self.parts()[3:], across):
            copy.wait_recv()
            self.pair(zz, rel).start()

    def ready(self, zz):
        for rel in self.parts():
            self.pair(zz, rel, False).wait_recv()

    def finish_sends(self):
        z = self.place[0]

        def step(zz, carry):
            for rel in self.parts():
                self.pair(zz, rel).wait_send()
            up, down = self.line(zz)
            pl.when((zz <= z) & (z < self.nz - 1))(lambda: up.wait_send())
            pl.when((zz >= z) & (z > 0))(lambda: down.wait_send())
            for copy in tuple(self.sides(zz)) + tuple(self.across(zz)):
                copy.wait_send()
            return carry

        lax.fori_loop(0, self.nz, step, 0)

    def finish(self):
        def step(zz, carry):
            self.ready(zz)
            return carry

        lax.fori_loop(0, self.nz, step, 0)
        self.finish_sends()


class GatherCausal:
    @staticmethod
    def scratch(nz):
        dma = pltpu.SemaphoreType.DMA
        return [dma, dma, dma((2,)), dma((2 * nz,)), dma((2 * nz,)), dma((2 * nz,))]

    def __init__(self, nz, src, out, held, sems):
        self.s_x, self.r_x, self.lsem, self.s_z, self.r_z, self.l_z = sems
        self.nz, self.src, self.out, self.held_ref = nz, src, out, held
        self.place = z, x, y, c = place()
        self.xn = device(z, 1 - x, y, c)
        self.near = (device(z + 1, x, y, c), device(z - 1, x, y, c))

    def own(self):
        z, x = self.place[:2]
        return [pltpu.make_async_copy(self.src, self.out.at[z, x], self.lsem.at[0]),
                pltpu.make_async_copy(self.src, self.held_ref.at[z, x], self.lsem.at[1])]

    def side(self):
        z, x = self.place[:2]
        return remote(self.src, self.out.at[z, x], self.s_x, self.r_x, self.xn)

    def line(self, zz, micro):
        here = self.out.at[zz, :, micro]
        return remote(here, here, self.s_z.at[zz * 2 + micro], self.r_z.at[zz * 2 + micro],
                      self.near[micro])

    def keep(self, zz, micro):
        return pltpu.make_async_copy(self.out.at[zz, :, micro], self.held_ref.at[zz, :, micro],
                                     self.l_z.at[zz * 2 + micro])

    def needed(self, zz, micro):
        return zz <= self.place[0] if micro == 0 else zz >= self.place[0]

    def sends(self, zz, micro):
        z = self.place[0]
        return self.needed(zz, micro) & (z < self.nz - 1 if micro == 0 else z > 0)

    def first_to(self, zz):
        z = self.place[0]

        @pl.when(zz == z)
        def _():
            for copy in self.own():
                copy.wait()
            self.side().wait_recv()

        for micro in range(2):
            pl.when((zz != z) & self.needed(zz, micro))(lambda: self.line(zz, micro).wait_recv())
            pl.when(self.sends(zz, micro))(lambda: self.line(zz, micro).start())
            pl.when(self.needed(zz, micro))(lambda: self.keep(zz, micro).start())

    def ready(self, zz):
        for micro in range(2):
            pl.when(self.needed(zz, micro))(lambda: self.keep(zz, micro).wait())

    def finish(self):
        self.side().wait_send()

        def step(zz, carry):
            for micro in range(2):
                pl.when(self.sends(zz, micro))(lambda: self.line(zz, micro).wait_send())
            return carry

        lax.fori_loop(0, self.nz, step, 0)


class GatherRows:
    @staticmethod
    def scratch(nz):
        dma = pltpu.SemaphoreType.DMA
        return [dma] + [dma((nz,))] * 5

    def __init__(self, nz, src, out, sems, part=0, parts=1):
        self.lsem, self.s_u, self.s_d, self.s_x, self.r_z, self.r_x = sems
        self.nz, self.src, self.out = nz, src, out
        self.offset, self.stride = part * src.shape[0], parts * src.shape[0]
        self.place = z, x, y, c = place()
        self.xn = device(z, 1 - x, y, c)
        self.up, self.down = device(z + 1, x, y, c), device(z - 1, x, y, c)

    def block(self, zz):
        rows = self.src.shape[0]
        start = (zz * 2 + self.place[1]) * self.stride + self.offset
        return self.out.at[pl.ds(pl.multiple_of(start, rows), rows)]

    def own(self):
        return pltpu.make_async_copy(self.src, self.block(self.place[0]), self.lsem)

    def copies(self, zz):
        here = self.block(zz)
        return (remote(here, here, self.s_u.at[zz], self.r_z.at[zz], self.up),
                remote(here, here, self.s_d.at[zz], self.r_z.at[zz], self.down),
                remote(here, here, self.s_x.at[zz], self.r_x.at[zz], self.xn))

    def first_to(self, zz):
        z = self.place[0]
        up, down, to_x = self.copies(zz)
        pl.when(zz != z)(lambda: up.wait_recv())
        pl.when((zz <= z) & (z < self.nz - 1))(lambda: up.start())
        pl.when((zz >= z) & (z > 0))(lambda: down.start())
        to_x.start()

    def finish(self):
        z = self.place[0]

        def step(zz, carry):
            up, down, to_x = self.copies(zz)
            to_x.wait()
            pl.when((zz <= z) & (z < self.nz - 1))(lambda: up.wait_send())
            pl.when((zz >= z) & (z > 0))(lambda: down.wait_send())
            return carry

        lax.fori_loop(0, self.nz, step, 0)


def mirrored(nz, shard):
    return (nz - 1 - shard // 2) * 2 + shard % 2


def stream_unit(u, nz):
    shard = lax.axis_index("fsdp")
    later = u > shard
    micro = jnp.where(later, 1, 0)
    here = jnp.where(later, mirrored(nz, shard), shard)
    key_place = here - jnp.where(later, u - shard - 1, u)
    owner = jnp.where(later, mirrored(nz, key_place), key_place)
    return micro, here, key_place, owner


def key_bias(micro, here, key_place, block, start_ref):
    key = key_place * block + lax.broadcasted_iota(jnp.int32, (block, block), 0)
    query = here * block + lax.broadcasted_iota(jnp.int32, (block, block), 1)
    return jnp.where((key >= start_ref[micro]) & (key <= query), 0.0, masked_score)


def norm_turn(raw, gain, cosine, sine):
    scale = lax.rsqrt(jnp.mean(raw * raw, axis=1, keepdims=True) + norm_eps)
    normed = raw * scale * gain
    return normed * cosine + pltpu.roll(normed, raw.shape[1] // 2, 1) * sine


def attend_kernel(nz, gain_ref, gq_ref, gk_ref, cos_ref, sin_ref, start_ref, cot_ref, wo_ref,
                  tok_all, wq_all, wk_all, wv_all,
                  normed, scale_ref, q_pre, k_pre, q_ref, heads_ref, lse_ref, kv_all, cot_all, wo_all,
                  tok_ref, wq, wk, wv, s_in, kv_ref, kv, acc, peak, total, *sems):
    shards = 2 * nz
    width = kv_ref.shape[2] // 2
    block = q_ref.shape[0] // 2
    low = jnp.bfloat16
    heads = q_ref.shape[1] // width
    z, x, y, c = place()
    n_c, n_o = len(GatherAll.scratch(nz)), len(GatherRows.scratch(nz))
    end = 2 * (n_c + n_o)
    cots = [GatherAll(nz, half, cot_all, sems[n * n_c : (n + 1) * n_c], half.shape[0], n, 2)
            for n, half in enumerate(halves(cot_ref))]
    outs = [GatherRows(nz, half, wo_all, sems[2 * n_c + n * n_o : 2 * n_c + (n + 1) * n_o], n, 2)
            for n, half in enumerate(halves(wo_ref))]
    keys_in = GatherCausal(nz, kv_ref, kv_all, kv, sems[end:])
    greet([(None, cots[0].partner), (None, cots[0].xn), (None, cots[0].yn),
           (z < nz - 1, cots[0].up), (z > 0, cots[0].down)])
    for part in outs + cots:
        part.own().start()
    fetches = [pltpu.make_async_copy(src, dst, s_in.at[n]) for n, (src, dst) in enumerate((
        (tok_all, tok_ref), (wk_all, wk), (wv_all, wv), (wq_all, wq)))]
    for copy in fetches:
        copy.start()
    for part in outs + cots:
        part.own().wait()
    for part in cots:
        part.first_to(z)
    fetches[0].wait()

    def token_norm(n, carry):
        rows = pl.ds(pl.multiple_of(n * 64, 64), 64)
        row = tok_ref[rows, :].astype(jnp.float32)
        scale = lax.rsqrt(jnp.mean(row * row, axis=1, keepdims=True) + norm_eps)
        scale_ref[rows, :] = scale
        normed[rows, :] = (row * scale * gain_ref[...]).astype(low)
        return carry

    lax.fori_loop(0, tok_ref.shape[0] // 64, token_norm, 0)
    fetches[1].wait()
    k_pre[...] = dot_plain(normed[...], wk[...])
    turned = norm_turn(k_pre[...], gk_ref[...], cos_ref[...], sin_ref[...]).astype(low)
    fetches[2].wait()
    value = dot_plain(normed[...], wv[...]).astype(low)
    for micro in range(2):
        rows = slice(micro * block, (micro + 1) * block)
        kv_ref[micro, :, :width] = turned[rows]
        kv_ref[micro, :, width:] = value[rows]
    keys_in.side().start()
    for copy in keys_in.own():
        copy.start()
    peak[...] = jnp.full(peak.shape, masked_score, jnp.float32)
    total[...] = jnp.zeros_like(total)
    acc[...] = jnp.zeros_like(acc)
    fetches[3].wait()

    def at_distance(dist, fn):
        for side in (-1, 1):
            zz = z + side * dist
            valid = (dist >= 0) & (zz >= 0) & (zz < nz) & ((dist > 0) | (side > 0))
            pl.when(valid)(lambda: fn(zz))

    def tick(u, carry):
        def gradients(zz):
            @pl.when(u > 0)
            def _():
                for part in cots:
                    part.first_to(zz)

        def weights(zz):
            for part in outs:
                part.first_to(zz)

        def across(zz):
            for part in cots:
                part.second_to(zz)

        def onward(zz):
            for part in cots:
                part.third_to(zz)

        at_distance(u, keys_in.first_to)
        at_distance(u, gradients)
        at_distance(u, weights)
        at_distance(u - 1, across)
        at_distance(u - 2, onward)
        at_distance(u - 1, attend_item)
        return carry

    def attend_item(zz):
        own = zz == z
        keys_in.ready(zz)

        def part(i, carry):
            micro = jnp.where(own, i // 2, jnp.where(zz < z, 0, 1))
            xx = jnp.where(own, jnp.where(i % 2 == 0, x, 0), i)
            valid = jnp.where(own, jnp.where((i % 2 == 0) | (x == 1), 1, 0), jnp.where(i < 2, 1, 0))
            pl.when(valid == 1)(lambda: attention(micro, zz, xx))
            return carry

        lax.fori_loop(0, 4, part, 0)

    def attention(micro, zz, xx):
        def at_place(z_at, x_at):
            return jnp.where(micro == 0, z_at, nz - 1 - z_at) * 2 + x_at

        here, key_place = at_place(z, x), at_place(zz, xx)
        bias = key_bias(micro, here, key_place, block, start_ref)
        both = kv.at[zz, xx, micro]
        keys, values = both[:, :width], both[:, width:]
        q_rows = pl.ds(pl.multiple_of(micro * block, block), block)

        def head(h, carry):
            at = micro * heads + h
            query = q_ref[q_rows, pl.ds(pl.multiple_of(h * width, width), width)]
            scores = dot_last(keys, query) * width ** (-0.5) + bias
            before = peak[at]
            now = jnp.maximum(before, jnp.max(scores, axis=0, keepdims=True))
            weights = jnp.exp(scores - now)
            factor = jnp.exp(before - now)
            peak[at] = now
            total[at] = total[at] * factor + jnp.sum(weights, axis=0, keepdims=True)
            acc[at] = acc[at] * factor + dot_first(values, weights.astype(jnp.bfloat16))
            return carry

        lax.fori_loop(0, heads, head, 0, unroll=4)

    def prepare(n, carry):
        pair = pl.ds(pl.multiple_of(n * 2 * width, 2 * width), 2 * width)
        q_pre[:, pair] = dot_plain(normed[...], wq[:, pair])
        for h in range(2):
            cols = pl.ds(pl.multiple_of((n * 2 + h) * width, width), width)
            q_ref[:, cols] = norm_turn(
                q_pre[:, cols], gq_ref[...], cos_ref[...], sin_ref[...]
            ).astype(low)
        return carry

    lax.fori_loop(0, heads // 2, prepare, 0)
    tick(0, 0)
    lax.fori_loop(1, nz + 2, tick, 0)

    def close(at, carry):
        micro, h = at // heads, at % heads
        result = (acc[at] / total[at]).T
        here = pl.ds(pl.multiple_of(micro * block, block), block)
        cols = pl.ds(pl.multiple_of(h * width, width), width)
        heads_ref[here, cols] = result.astype(jnp.bfloat16)
        lse_ref[at] = peak[at] + jnp.log(total[at])
        return carry

    lax.fori_loop(0, 2 * heads, close, 0)
    keys_in.finish()
    for part in outs + cots:
        part.finish()


def attend(tokens, gain_attn, wq_all, wk_all, wv_all, gain_query, gain_key, cosine, sine, starts,
           cotangent, w_out, nz, collective_id):
    rows, features = tokens.shape
    columns, width = wq_all.shape[1], wk_all.shape[1]
    heads = columns // width
    block = rows // 2
    any_space = pl.BlockSpec(memory_space=pl.ANY)
    vmem = pl.BlockSpec(memory_space=pltpu.VMEM)
    vm, shape, f32, low = pltpu.VMEM, jax.ShapeDtypeStruct, jnp.float32, jnp.bfloat16
    return pl.pallas_call(
        functools.partial(attend_kernel, nz),
        in_specs=[vmem] * 8 + [any_space] * 4,
        out_specs=[vmem] * 7 + [any_space] * 3,
        out_shape=[
            shape((rows, features), low), shape((rows, 1), f32),
            shape((rows, columns), f32), shape((rows, width), f32),
            shape((rows, columns), low), shape((rows, columns), low),
            shape((2 * heads, 1, block), f32),
            shape((nz, 2, 2, block, 2 * width), low),
            shape((rows * 2 * nz, cotangent.shape[1] * 4), cotangent.dtype),
            shape((w_out.shape[0] * 2 * nz, w_out.shape[1]), w_out.dtype),
        ],
        scratch_shapes=[
            vm((rows, features), low), vm(wq_all.shape, low), vm(wk_all.shape, low),
            vm(wv_all.shape, low), pltpu.SemaphoreType.DMA((4,)),
            vm((2, block, 2 * width), low), vm((nz, 2, 2, block, 2 * width), low),
            vm((2 * heads, width, block), f32), vm((2 * heads, 1, block), f32),
            vm((2 * heads, 1, block), f32),
        ] + GatherAll.scratch(nz) * 2 + GatherRows.scratch(nz) * 2 + GatherCausal.scratch(nz),
        compiler_params=pltpu.CompilerParams(
            collective_id=collective_id, has_side_effects=True, vmem_limit_bytes=62 << 20
        ),
        name="attend",
    )(gain_attn, gain_query, gain_key, cosine, sine, starts, cotangent, w_out, tokens, wq_all, wk_all,
      wv_all)


class ScatterAll:
    @staticmethod
    def scratch(nz, rows, cols, kind, cut):
        vm, dma = pltpu.VMEM, pltpu.SemaphoreType.DMA
        return [
            vm((nz, 4, rows, cols), kind), vm((nz, 4, rows, cols), kind),
            vm((nz, rows, cols), kind), vm((nz, max(cut, 16), cols), kind),
            vm((nz, rows, cols), kind), vm((nz, max(rows - cut, 16), cols), kind),
            vm((nz + 1, rows, cols), kind),
        ] + [dma((4 * nz,))] * 3 + [dma((nz,))] * 9 + [dma((nz + 1,))]

    def __init__(self, nz, partial, out, refs, cut, part=0, parts=1):
        (self.w, self.lp, self.rx, self.rxd, self.ry, self.ryd, self.rz,
         self.s_l, self.s_p, self.r_p, self.s_x, self.s_y, self.s_dx, self.s_dy, self.s_z,
         self.r_x, self.r_y, self.r_dx, self.r_dy, self.r_z) = refs
        self.nz, self.partial, self.out, self.cut = nz, partial, out, cut
        self.rows, self.cols = out.shape
        self.offset, self.stride = part * self.rows, parts * self.rows
        self.place = z, x, y, c = place()
        self.partner, self.xn, self.yn = (
            device(z, x, y, 1 - c), device(z, 1 - x, y, c), device(z, x, 1 - y, c))
        self.up, self.down = device(z + 1, x, y, c), device(z - 1, x, y, c)

    def block(self, zz, rel, cc):
        z, x, y, c = self.place
        xx = 1 - x if rel in (1, 3) else x
        yy = 1 - y if rel in (2, 3) else y
        return self.partial.at[
            pl.ds(pl.multiple_of((zz * 2 + xx) * self.stride + self.offset, self.rows), self.rows),
            pl.ds(pl.multiple_of((yy * 2 + cc) * self.cols, self.cols), self.cols)]

    def pair(self, zz, rel):
        k = zz * 4 + rel
        return remote(self.block(zz, rel, 1 - self.place[3]), self.lp.at[zz, rel],
                      self.s_p.at[k], self.r_p.at[k], self.partner)

    def load(self, zz, rel):
        return pltpu.make_async_copy(
            self.block(zz, rel, self.place[3]), self.w.at[zz, rel], self.s_l.at[zz * 4 + rel])

    def across(self, zz):
        copies = []
        if self.cut > 0:
            copies.append(remote(self.w.at[zz, 3, pl.ds(0, self.cut)], self.rxd.at[zz],
                                 self.s_dx.at[zz], self.r_dx.at[zz], self.xn))
        if self.cut < self.rows:
            copies.append(remote(self.w.at[zz, 3, pl.ds(self.cut, self.rows - self.cut)],
                                 self.ryd.at[zz], self.s_dy.at[zz], self.r_dy.at[zz], self.yn))
        return copies

    def sides(self, zz):
        return (remote(self.w.at[zz, 1], self.rx.at[zz], self.s_x.at[zz], self.r_x.at[zz], self.xn),
                remote(self.w.at[zz, 2], self.ry.at[zz], self.s_y.at[zz], self.r_y.at[zz], self.yn))

    def line(self, zz, slot, where):
        return remote(self.w.at[zz, 0], self.rz.at[slot], self.s_z.at[zz], self.r_z.at[slot], where)

    def start(self):
        def step(k, carry):
            zz = far_first(self.nz, self.place[0], k)
            for rel in (3, 1, 2, 0):
                self.pair(zz, rel).start()
                self.load(zz, rel).start()
            return carry

        lax.fori_loop(0, self.nz, step, 0)

    def first(self, k):
        zz = far_first(self.nz, self.place[0], k)
        for rel in (3, 1, 2, 0):
            self.pair(zz, rel).wait_recv()
            self.load(zz, rel).wait()
            add_blocks(self.w.at[zz, rel], [self.lp.at[zz, rel]], 0, self.rows)
            if rel == 3:
                for copy in self.across(zz):
                    copy.start()

    def second(self, k):
        zz = far_first(self.nz, self.place[0], k)
        across, (to_x, to_y) = self.across(zz), self.sides(zz)
        if self.cut < self.rows:
            across[-1].wait_recv()
            add_blocks(self.w.at[zz, 1], [self.ryd.at[zz]], self.cut, self.rows - self.cut)
        to_x.start()
        if self.cut > 0:
            across[0].wait_recv()
            add_blocks(self.w.at[zz, 2], [self.rxd.at[zz]], 0, self.cut)
        to_y.start()

    def send_line(self, zz):
        z = self.place[0]
        pl.when(zz > z)(lambda: self.line(zz, zz, self.up).start())
        pl.when(zz == z - 1)(lambda: self.line(zz, self.nz, self.down).start())
        pl.when(zz < z - 1)(lambda: self.line(zz, zz, self.down).start())

    def passes(self, zz):
        z = self.place[0]
        return ((zz > z) & (z > 0)) | ((zz < z) & (z < self.nz - 1))

    def third(self, k):
        zz, z = far_first(self.nz, self.place[0], k), self.place[0]
        to_x, to_y = self.sides(zz)
        to_x.wait_recv()
        to_y.wait_recv()
        add_blocks(self.w.at[zz, 0], [self.rx.at[zz], self.ry.at[zz]], 0, self.rows)
        pl.when((zz != z) & jnp.logical_not(self.passes(zz)))(lambda: self.send_line(zz))

    def fourth(self, k):
        zz, z, nz = far_first(self.nz, self.place[0], k), self.place[0], self.nz

        @pl.when((zz != z) & self.passes(zz))
        def _():
            self.line(zz, zz, self.up).wait_recv()
            add_blocks(self.w.at[zz, 0], [self.rz.at[zz]], 0, self.rows)
            self.send_line(zz)

        @pl.when(zz == z)
        def _():
            finish_line(self, self.w.at[zz, 0], zz)

    def finish(self):
        z = self.place[0]

        def step(zz, carry):
            for rel in range(4):
                self.pair(zz, rel).wait_send()
            for copy in tuple(self.across(zz)) + tuple(self.sides(zz)):
                copy.wait_send()
            pl.when(zz != z)(lambda: self.line(zz, zz, self.up).wait_send())
            return carry

        lax.fori_loop(0, self.nz, step, 0)


def finish_line(self, own, zz):
    z, nz = self.place[0], self.nz
    below, above = self.rz.at[zz], self.rz.at[nz]
    pl.when(z > 0)(lambda: self.line(zz, zz, self.up).wait_recv())
    pl.when(z < nz - 1)(lambda: self.line(zz, nz, self.down).wait_recv())
    pl.when(z == 0)(lambda: add_blocks(own, [above], 0, self.rows, self.out))
    pl.when(z == nz - 1)(lambda: add_blocks(own, [below], 0, self.rows, self.out))
    pl.when((z > 0) & (z < nz - 1))(lambda: add_blocks(own, [below, above], 0, self.rows, self.out))


class ReduceRows:
    @staticmethod
    def scratch(nz, rows, cols, kind):
        vm, dma = pltpu.VMEM, pltpu.SemaphoreType.DMA
        return [vm((nz, rows, cols), kind), vm((nz, rows, cols), kind), vm((nz, rows, cols), kind),
                vm((nz + 1, rows, cols), kind)] + [dma((nz,))] * 3 + [dma((nz + 1,))]

    def __init__(self, nz, left, right, out, refs, part=0, parts=1):
        self.w, self.sent, self.rx, self.rz, self.s_x, self.s_z, self.r_x, self.r_z = refs
        self.nz, self.left, self.right, self.out = nz, left, right, out
        self.rows = out.shape[0]
        self.offset, self.stride = part * self.rows, parts * self.rows
        self.place = z, x, y, c = place()
        self.xn = device(z, 1 - x, y, c)
        self.up, self.down = device(z + 1, x, y, c), device(z - 1, x, y, c)

    def make(self, zz, xx, ref):
        start = (zz * 2 + xx) * self.stride + self.offset
        at = pl.ds(pl.multiple_of(start, self.rows), self.rows)
        ref[...] = dot_first(self.left[:, at], self.right[...]).astype(ref.dtype)

    def side(self, zz):
        return remote(self.sent.at[zz], self.rx.at[zz], self.s_x.at[zz], self.r_x.at[zz], self.xn)

    def line(self, zz, slot, where):
        return remote(self.w.at[zz], self.rz.at[slot], self.s_z.at[zz], self.r_z.at[slot], where)

    def start(self):
        def step(k, carry):
            self.send(k)
            return carry

        lax.fori_loop(0, self.nz, step, 0)

    def send(self, k):
        zz, x = far_first(self.nz, self.place[0], k), self.place[1]
        self.make(zz, 1 - x, self.sent.at[zz])
        self.side(zz).start()
        self.make(zz, x, self.w.at[zz])

    send_line = ScatterAll.send_line
    passes = ScatterAll.passes

    def first(self, k):
        zz, z = far_first(self.nz, self.place[0], k), self.place[0]
        self.side(zz).wait_recv()
        add_blocks(self.w.at[zz], [self.rx.at[zz]], 0, self.rows)
        pl.when((zz != z) & jnp.logical_not(self.passes(zz)))(lambda: self.send_line(zz))

    def second(self, k):
        zz, z, nz = far_first(self.nz, self.place[0], k), self.place[0], self.nz

        @pl.when((zz != z) & self.passes(zz))
        def _():
            self.line(zz, zz, self.up).wait_recv()
            add_blocks(self.w.at[zz], [self.rz.at[zz]], 0, self.rows)
            self.send_line(zz)

        @pl.when(zz == z)
        def _():
            finish_line(self, self.w.at[zz], zz)

    def finish(self):
        z = self.place[0]

        def step(zz, carry):
            self.side(zz).wait_send()
            pl.when(zz != z)(lambda: self.line(zz, zz, self.up).wait_send())
            return carry

        lax.fori_loop(0, self.nz, step, 0)


class ReduceCausal:
    @staticmethod
    def scratch(nz, rows, cols, kind):
        vm, dma = pltpu.VMEM, pltpu.SemaphoreType.DMA
        return [vm((nz, 2, 2, rows, cols), kind), vm((2, rows, cols), kind),
                dma((2 * nz,)), dma((2 * nz,)), dma((2,)), dma((2,))]

    def __init__(self, nz, sides, out, refs):
        self.got, self.across, self.s_z, self.r_z, self.s_x, self.r_x = refs
        self.nz, self.sides, self.out = nz, sides, out
        self.place = z, x, y, c = place()
        self.xn = device(z, 1 - x, y, c)
        self.to = (device(z - 1, x, y, c), device(z + 1, x, y, c))

    def line(self, zz, micro):
        k = zz * 2 + micro
        return remote(self.sides.at[zz, :, micro], self.got.at[zz, :, micro],
                      self.s_z.at[k], self.r_z.at[k], self.to[micro])

    def side(self, micro):
        z, x = self.place[:2]
        return remote(self.sides.at[z, 1 - x, micro], self.across.at[micro],
                      self.s_x.at[micro], self.r_x.at[micro], self.xn)

    def take(self, zz, micro):
        first = self.place[0] == (self.nz - 1 if micro == 0 else 0)

        @pl.when(jnp.logical_not(first))
        def _():
            self.line(zz, micro).wait_recv()
            for xx in range(2):
                add_blocks(self.sides.at[zz, xx, micro], [self.got.at[zz, xx, micro]], 0,
                           self.sides.shape[3])

    def turn(self, hop):
        z, nz = self.place[0], self.nz
        for micro in range(2):
            @pl.when(hop == (nz - 1 - z if micro == 0 else z))
            def _():
                def step(n, carry):
                    zz = n if micro == 0 else nz - 1 - n
                    self.take(zz, micro)
                    self.line(zz, micro).start()
                    return carry

                lax.fori_loop(0, z if micro == 0 else nz - 1 - z, step, 0)
                self.take(z, micro)
                self.side(micro).start()

    def finish(self):
        z, x = self.place[:2]
        for micro in range(2):
            self.side(micro).wait_recv()
            add_blocks(self.sides.at[z, x, micro], [self.across.at[micro]], 0, self.sides.shape[3],
                       self.out.at[micro])
        for micro in range(2):
            self.side(micro).wait_send()

            def step(n, carry):
                self.line(n if micro == 0 else self.nz - 1 - n, micro).wait_send()
                return carry

            lax.fori_loop(0, z if micro == 0 else self.nz - 1 - z, step, 0)


def norm_turn_back(turned, raw, gain, cosine, sine):
    grad = turned * cosine + pltpu.roll(turned * sine, raw.shape[1] // 2, 1)
    scale = lax.rsqrt(jnp.mean(raw * raw, axis=1, keepdims=True) + norm_eps)
    inner = grad * gain
    mean = jnp.mean(raw * inner, axis=1, keepdims=True)
    return (scale * inner - raw * (scale * scale * scale * mean),
            jnp.sum(grad * raw * scale, axis=0, keepdims=True))


def attend_back_kernel(nz, k_pre, gk_ref, gq_ref, cos_ref, sin_ref, start_ref, lse_ref, scale_ref,
                       gates_ref, gg_ref, router_all, gain_ref, moe_ref,
                       middle_all, back_all, cot_part, cot_all, wo_all, heads_all, q_all, kv_all, pre_all,
                       out_part, mid_out, q_grad, gain_grad, out_sum, wo_sum, small_out,
                       router_ref, low_ref, mid_ref, wo_ref, heads_ref, q_ref, kv_ref,
                       small_ref, split_ref, grad_ref, delta_ref, q_pre, s_in, s_t, r_t,
                       kv_sum, sides, acc, k_acc, v_acc, *refs):
    middle_ref, inner_ref = (q_pre.at[:, pl.ds(n * mid_out.shape[1], mid_out.shape[1])]
                             for n in range(2))
    shards = 2 * nz
    shard = lax.axis_index("fsdp")
    width = kv_ref.shape[4] // 2
    block = q_ref.shape[0] // 2
    heads = q_ref.shape[1] // width
    z, x, y, c = place()
    count = shards + 2 * x
    low = jnp.bfloat16
    n_o, n_w = len(ScatterAll.scratch(nz, 16, 128, low, 0)), len(ReduceRows.scratch(nz, 16, 128, low))
    end = 2 * (n_o + n_w)
    outs = [ScatterAll(nz, out_part, half, refs[n * n_o : (n + 1) * n_o], 0, n, 2)
            for n, half in enumerate(halves(out_sum))]
    weights = [ReduceRows(nz, mid_ref, heads_ref, half,
                          refs[2 * n_o + n * n_w : 2 * n_o + (n + 1) * n_w], n, 2)
               for n, half in enumerate(halves(wo_sum))]
    last = end + len(SmallSums.scratch(nz, (8, 128), jnp.float32))
    smalls = SmallSums(nz, small_ref, small_out, refs[end:last])
    final = last + len(ReduceCausal.scratch(nz, 16, 128, low))
    keys_out = ReduceCausal(nz, sides, kv_sum, refs[last:final])
    sums = RowSums(refs[final:])
    greet_all(lax.axis_index("fsdp"), lax.axis_index("tp"), shards, 4)
    for part in outs:
        part.start()
    group = lax.axis_index("tp")
    rows, cols = mid_out.shape
    half = rows // 2
    mine = pl.ds(pl.multiple_of(group * cols, cols), cols)
    there = pl.ds(pl.multiple_of(mirrored(nz, shard) * rows + half, half), half)
    fetches = [pltpu.make_async_copy(src, dst, s_in.at[n]) for n, (src, dst) in enumerate((
        (router_all.at[mine], router_ref), (middle_all, middle_ref), (back_all, inner_ref),
        (cot_part.at[pl.ds(0, half)], low_ref.at[pl.ds(0, half)]),
        (cot_all.at[there, mine], low_ref.at[pl.ds(half, half)]),
        (wo_all.at[:, pl.ds(0, wo_ref.shape[1])], wo_ref),
        (heads_all, heads_ref), (q_all, q_ref), (kv_all, kv_ref), (pre_all, q_pre)))]
    for copy in fetches[:-1]:
        copy.start()

    sides[...] = jnp.zeros_like(sides)
    acc[...] = jnp.zeros_like(acc)

    def attention(u):
        micro, here, key_place, owner = stream_unit(u, nz)
        bias = key_bias(micro, here, key_place, block, start_ref)
        both = kv_ref.at[owner // 2, owner % 2, micro]
        keys, values = both[:, :width], both[:, width:]
        q_rows = pl.ds(pl.multiple_of(micro * block, block), block)
        k_acc[...] = jnp.zeros_like(k_acc)
        v_acc[...] = jnp.zeros_like(v_acc)

        def head(h, carry):
            at = micro * heads + h
            cols = pl.ds(pl.multiple_of(h * width, width), width)
            query, grad = q_ref[q_rows, cols], grad_ref[q_rows, cols]
            scores = dot_last(keys, query) * width ** (-0.5) + bias
            probs = jnp.exp(scores - lse_ref[at])
            score_grad = (probs * (dot_last(values, grad) - delta_ref[at])).astype(low)
            v_acc[...] += dot_plain(probs.astype(low), grad)
            k_acc[...] += dot_plain(score_grad, query)
            acc[at] += dot_first(keys, score_grad)
            return carry

        lax.fori_loop(0, heads, head, 0, unroll=2)
        side = sides.at[owner // 2, owner % 2, micro]
        side[:, :width] = (k_acc[...] * width ** (-0.5)).astype(low)
        side[:, width:] = v_acc[...].astype(low)

    def close(at, total):
        micro, h = at // heads, at % heads
        here = pl.ds(pl.multiple_of(micro * block, block), block)
        cols = pl.ds(pl.multiple_of(h * width, width), width)
        grad, gain = norm_turn_back(acc[at].T * width ** (-0.5), q_pre[here, cols], gq_ref[...],
                                    cos_ref[here, :], sin_ref[here, :])
        q_grad[here, cols] = grad.astype(low)
        return total + gain

    def close_all():
        gain_grad[pl.ds(0, 1), :] = lax.fori_loop(
            0, 2 * heads, close, jnp.zeros((1, width), jnp.float32)
        )

    def unit(u, carry):
        def at(fn, k):
            pl.when((k >= 0) & (k < nz))(lambda: fn(k))

        def each(parts, name, k):
            for part in parts:
                at(getattr(part, name), k)

        for n in range(4):
            pl.when(4 * u + n < count)(lambda: attention(4 * u + n))
        each(outs, 'second', u + 1)
        each(weights, 'send', u + 2)
        each(outs, 'first', u + 3)
        pl.when(u == 1)(smalls.second)
        at(keys_out.turn, u - done)
        each(outs, 'third', u)
        each(outs, 'fourth', u - 1)
        each(weights, 'second', u - 2)
        each(weights, 'first', u - 1)
        pl.when(u == done + 1)(close_all)
        return carry

    eye = diagonal()

    def column(yy):
        return mid_ref.at[:, pl.ds(pl.multiple_of((yy * 2 + c) * cols, cols), cols)]

    partner, yn = outs[0].partner, outs[0].yn
    to_y = remote(low_ref, column(y), s_t.at[0], r_t.at[0], yn)
    to_pair = remote(low_ref, column(y), s_t.at[1], r_t.at[1], partner)
    onward = remote(column(1 - y), column(1 - y), s_t.at[2], r_t.at[2], partner)

    def dots(n, carry):
        here = pl.ds(pl.multiple_of(n * 128, 128), 128)
        product = middle_ref[here, :] * inner_ref[here, :]
        sums.got[0, pl.ds(n, 1), :] = to_row(jnp.sum(product, axis=1, keepdims=True), eye)
        return carry

    def residual(n, carry):
        here = pl.ds(pl.multiple_of(n * 128, 128), 128)
        mean = to_column(sums.total(n), eye) / (4 * cols)
        scale = scale_ref[here, :]
        out = (low_ref[here, :].astype(jnp.float32) + scale * inner_ref[here, :]
               - middle_ref[here, :] * (scale * scale * scale * mean))
        mid_out[here, :] = out
        low_ref[here, :] = out.astype(low)
        return carry

    def head_grads(part):
        def step(n, carry):
            at = pl.ds(pl.multiple_of(n * 256, 256), 256)
            to = pl.ds(pl.multiple_of(part * wo_ref.shape[1] + n * 256, 256), 256)
            grad_ref[:, to] = dot_plain(mid_ref[...], wo_ref[:, at]).astype(low)
            return carry

        lax.fori_loop(0, wo_ref.shape[1] // 256, step, 0)

    def deltas(at, carry):
        here = pl.ds(pl.multiple_of(at // heads * block, block), block)
        head = pl.ds(pl.multiple_of(at % heads * width, width), width)
        product = grad_ref[here, head].astype(jnp.float32) * heads_ref[here, head].astype(jnp.float32)
        delta_ref[at] = jnp.sum(product.T, axis=0, keepdims=True)
        return carry

    done = (shards + 2 - 1) // 4
    def each_now(parts, name, k):
        for part in parts:
            getattr(part, name)(k)

    gates = gates_ref[...]
    gates_grad = gg_ref[:, 0, :].T
    logit_grad = gates * (gates_grad - jnp.sum(gates * gates_grad, axis=1, keepdims=True))
    each_now(outs, 'first', 0)
    pieces, rest = [], logit_grad
    for _ in range(3):
        pieces.append(rest.astype(low))
        rest = rest - pieces[-1].astype(jnp.float32)
    router_grad = sum(dot_first(piece, moe_ref[...]) for piece in pieces)
    small_ref[...] = jnp.zeros_like(small_ref)
    blocks = cols // 128
    per = router_grad.shape[0] // shards
    for e in range(router_grad.shape[0]):
        for n in range(blocks):
            small_ref[e // per, pl.ds(e % per * blocks + n, 1), :] = (
                router_grad[e : e + 1, n * 128 : (n + 1) * 128])
    for copy in fetches[:5]:
        copy.wait()

    def moe_grads(n, total):
        here = pl.ds(pl.multiple_of(n * 128, 128), 128)
        grad = inner_ref[here, :]
        for piece in pieces_ref:
            grad = grad + dot_last(piece[here, :], router_ref[...])
        inner_ref[here, :] = grad * gain_ref[:, mine]
        return total + jnp.sum(grad * middle_ref[here, :] * scale_ref[here, :], axis=0, keepdims=True)

    pieces_ref = [split_ref.at[n] for n in range(3)]
    for ref, piece in zip(pieces_ref, pieces):
        ref[...] = piece
    gain_total = lax.fori_loop(0, rows // 128, moe_grads, jnp.zeros((1, cols), jnp.float32))
    for n in range(blocks):
        small_ref[0, pl.ds(per * blocks + n, 1), :] = gain_total[:, n * 128 : (n + 1) * 128]
    smalls.start()
    lax.fori_loop(0, rows // 128, dots, 0)
    sums.start()
    sums.wait()
    lax.fori_loop(0, rows // 128, residual, 0)
    fetches[-1].start()
    to_y.start()
    to_pair.start()
    mid_ref[:, pl.ds(pl.multiple_of((y * 2 + c) * cols, cols), cols)] = low_ref[...]
    each_now(outs, 'first', 1)
    to_y.wait_recv()
    onward.start()
    each_now(outs, 'second', 0)
    for copy in fetches[5:]:
        copy.wait()
    to_pair.wait()
    onward.wait()
    to_y.wait_send()
    for k in range(2):
        each_now(weights, 'send', k)
    each_now(outs, 'first', 2)
    head_grads(0)
    more = pltpu.make_async_copy(wo_all.at[:, pl.ds(wo_ref.shape[1], wo_ref.shape[1])], wo_ref,
                                 s_in.at[5])
    more.start()
    more.wait()
    head_grads(1)
    lax.fori_loop(0, 2 * heads, deltas, 0)
    lax.fori_loop(0, nz + 2, unit, 0)
    keys_out.finish()
    total = jnp.zeros((1, width), jnp.float32)
    for micro in range(2):
        here = slice(micro * block, (micro + 1) * block)
        grad, gain = norm_turn_back(kv_sum[micro, :, :width], k_pre[here, :], gk_ref[...],
                                    cos_ref[here, :], sin_ref[here, :])
        q_grad[here, heads * width : (heads + 1) * width] = grad.astype(low)
        q_grad[here, (heads + 1) * width :] = kv_sum[micro, :, width:].astype(low)
        total = total + gain
    gain_grad[pl.ds(1, 1), :] = total
    for part in outs + weights:
        part.finish()
    smalls.finish()


def attend_back(query, q_pre, k_pre, gain_key, gain_query, cosine, sine, keys_values, starts, log_total,
                gates, gates_grad, router, gain, moe_low, middle, scale, back, cotangent, cot_all, w_out, heads_low, out_part, nz, collective_id):
    rows, columns = query.shape
    width = keys_values.shape[4] // 2
    heads = columns // width
    block = rows // 2
    cols = out_part.shape[1] // 4
    wo_shape = (w_out.shape[0] // (2 * nz), columns)
    experts = gates.shape[1]
    part_rows = -(-(experts // (2 * nz) + 1) * cols // 1024) * 8
    small = (2 * nz, part_rows, 128)
    any_space = pl.BlockSpec(memory_space=pl.ANY)
    vmem = pl.BlockSpec(memory_space=pltpu.VMEM)
    vm, shape, f32, low = pltpu.VMEM, jax.ShapeDtypeStruct, jnp.float32, jnp.bfloat16
    dma = pltpu.SemaphoreType.DMA
    return pl.pallas_call(
        functools.partial(attend_back_kernel, nz),
        in_specs=[vmem] * 10 + [any_space] + [vmem] * 2 + [any_space] * 10,
        out_specs=[vmem] * 6,
        out_shape=[
            shape((rows, cols), f32),
            shape((rows, columns + 2 * width), low), shape((2, width), f32),
            shape((rows, cols), f32), shape(wo_shape, f32),
            shape((8 * nz,) + small[1:], f32),
        ],
        scratch_shapes=[
            vm((cols, experts), low), vm((rows, cols), low),
            vm((rows, 4 * cols), low), vm((w_out.shape[0], columns // 2), low), vm((rows, columns), low),
            vm((rows, columns), low), vm((nz, 2, 2, block, 2 * width), low),
            vm(small, f32), vm((3, rows, experts), low), vm((rows, columns), low),
            vm((2 * heads, 1, block), f32), vm((rows, columns), f32), dma((10,)), dma((3,)), dma((3,)),
            vm((2, block, 2 * width), f32), vm((nz, 2, 2, block, 2 * width), low),
            vm((2 * heads, width, block), f32), vm((block, width), f32), vm((block, width), f32),
        ] + ScatterAll.scratch(nz, rows // 2, cols, low, 0) * 2
        + ReduceRows.scratch(nz, wo_shape[0] // 2, wo_shape[1], low) * 2
        + SmallSums.scratch(nz, small[1:], f32)
        + ReduceCausal.scratch(nz, block, 2 * width, low) + RowSums.scratch(rows),
        compiler_params=pltpu.CompilerParams(
            collective_id=collective_id, has_side_effects=True, vmem_limit_bytes=62 << 20
        ),
        name="attend_back",
    )(k_pre, gain_key, gain_query, cosine, sine, starts, log_total, scale, gates, gates_grad, router,
      gain, moe_low, middle, back, cotangent, cot_all, w_out,
      heads_low, query, keys_values, q_pre, out_part)


def to_row(column, eye):
    return jnp.sum(jnp.where(eye, column, 0.0), axis=0, keepdims=True)


def to_column(row, eye):
    return jnp.sum(jnp.where(eye, row, 0.0), axis=1, keepdims=True)


def diagonal():
    shape = (128, 128)
    return lax.broadcasted_iota(jnp.int32, shape, 0) == lax.broadcasted_iota(jnp.int32, shape, 1)


class RowSums:
    @staticmethod
    def scratch(rows):
        dma = pltpu.SemaphoreType.DMA
        return [pltpu.VMEM((4, rows // 128, 128), jnp.float32), dma((3,)), dma((3,))]

    def __init__(self, refs):
        self.got, s, r = refs
        shard, group = lax.axis_index("fsdp"), lax.axis_index("tp")
        self.peers = [(shard, (group + k) % 4) for k in range(1, 4)]
        self.copies = [
            remote(self.got.at[0], self.got.at[k + 1], s.at[k], r.at[k], peer)
            for k, peer in enumerate(self.peers)
        ]

    def start(self):
        for copy in self.copies:
            copy.start()

    def wait(self):
        for copy in self.copies:
            copy.wait()

    def total(self, n):
        return self.got[0, pl.ds(n, 1), :] + self.got[1, pl.ds(n, 1), :] + (
            self.got[2, pl.ds(n, 1), :] + self.got[3, pl.ds(n, 1), :])


class ReduceCols:
    @staticmethod
    def scratch(rows, cols, kind):
        vm, dma = pltpu.VMEM, pltpu.SemaphoreType.DMA
        return [vm((2, rows, cols), kind), vm((2, rows, cols), kind), vm((rows, cols), kind),
                dma((2,)), dma((2,)), dma((2,)), dma, dma]

    def __init__(self, partial, out, refs):
        self.w, self.rp, self.ry, s_l, s_p, r_p, s_y, r_y = refs
        self.out = out
        self.rows, cols = out.shape
        z, x, y, c = place()
        self.partner, self.yn = device(z, x, y, 1 - c), device(z, x, 1 - y, c)

        def block(yy, cc):
            return partial.at[:, pl.ds(pl.multiple_of((yy * 2 + cc) * cols, cols), cols)]

        self.sends = [remote(block(yy, 1 - c), self.rp.at[k], s_p.at[k], r_p.at[k], self.partner)
                      for k, yy in enumerate((1 - y, y))]
        self.loads = [pltpu.make_async_copy(block(yy, c), self.w.at[k], s_l.at[k])
                      for k, yy in enumerate((1 - y, y))]
        self.across = remote(self.w.at[0], self.ry, s_y, r_y, self.yn)

    def start(self):
        for k in range(2):
            self.sends[k].start()
            self.loads[k].start()

    def first(self):
        self.loads[0].wait()
        self.sends[0].wait_recv()
        add_blocks(self.w.at[0], [self.rp.at[0]], 0, self.rows)
        self.across.start()

    def second(self):
        self.loads[1].wait()
        self.sends[1].wait_recv()
        self.across.wait_recv()
        add_blocks(self.w.at[1], [self.rp.at[1], self.ry], 0, self.rows, self.out)

    def finish(self):
        for send in self.sends:
            send.wait_send()
        self.across.wait_send()


class SmallSums:
    @staticmethod
    def scratch(nz, part, kind):
        dma = pltpu.SemaphoreType.DMA
        return [pltpu.VMEM((2 * nz,) + part, kind), dma((2 * nz,)), dma((2 * nz,)),
                dma((8 * nz,)), dma((8 * nz,))]

    def __init__(self, nz, values, out, refs):
        self.got, self.s_1, self.r_1, self.s_2, self.r_2 = refs
        self.values, self.out = values, out
        self.shards, self.devices = 2 * nz, 8 * nz
        self.shard, self.group = lax.axis_index("fsdp"), lax.axis_index("tp")
        self.me = self.shard * 4 + self.group

    def share(self, k):
        other = (self.shard + k) % self.shards
        return remote(self.values.at[other], self.got.at[k], self.s_1.at[k], self.r_1.at[k],
                      (other, self.group))

    def spread(self, k):
        other = (self.me + k) % self.devices
        return remote(self.out.at[self.me], self.out.at[self.me], self.s_2.at[k], self.r_2.at[k],
                      (other // 4, other % 4))

    def start(self):
        loop_from_one(self.shards, lambda k: self.share(k).start())

    def second(self):
        loop_from_one(self.shards, lambda k: self.share(k).wait())
        acc = self.values[self.shard]
        for k in range(1, self.shards):
            acc = acc + self.got[k]
        self.out[self.me] = acc
        loop_from_one(self.devices, lambda k: self.spread(k).start())

    def finish(self):
        loop_from_one(self.devices, lambda k: self.spread(k).wait())


def loop_from_one(count, fn):
    def step(k, carry):
        fn(k)
        return carry

    lax.fori_loop(1, count, step, 0)


def tail_kernel(nz, tok_ref, scale_ref, gain_ref, block_ref, small_ref, left_all, right_all, mid_all,
                wq_all, wk_all, wv_all, gp_all, up_all, hid_all, xr_all, gs_all,
                wq_out, wk_out, wv_out, token_out, block_out, gain_out, head_out, dwg, dwu, dwd,
                left_ref, right_ref, mid_ref, wq, wk, wv, part_ref, s_m, w_sum, gp_ref, up_ref, hid_ref, x_panel, g_panel, o_gate, o_up, o_down, s_in, s_out,
                small_out, normed, token, s_w, r_w, s_l, s_g, r_g, *refs):
    z, x, y, c = place()
    shard, group = lax.axis_index("fsdp"), lax.axis_index("tp")
    shards = 2 * nz
    devices = 4 * shards
    me = shard * 4 + group
    rows, cols = tok_ref.shape
    width = cols * 4
    half = rows // 2
    panel = x_panel.shape[1]
    panels = xr_all.shape[1] // panel
    f32, low = jnp.float32, jnp.bfloat16
    n_w, n_c = len(ReduceRows.scratch(nz, 16, 128, low)), len(ReduceCols.scratch(16, 128, low))
    weights = [ReduceRows(nz, left_ref, right_ref, half, refs[n * n_w : (n + 1) * n_w], n, 2)
               for n, half in enumerate(halves(w_sum))]
    columns = ReduceCols(part_ref, normed, refs[2 * n_w : 2 * n_w + n_c])
    sums = RowSums(refs[2 * n_w + n_c :])
    mirror = device(nz - 1 - z, x, y, c)
    greet_all(shard, group, shards, 4)
    fetches = [pltpu.make_async_copy(src, dst, s_m.at[n]) for n, (src, dst) in enumerate((
        (left_all, left_ref), (right_all, right_ref), (wq_all, wq), (wk_all, wk), (wv_all, wv),
        (mid_all, mid_ref)))]
    for copy in fetches:
        copy.start()
    for copy in fetches[:2]:
        copy.wait()
    for part in weights:
        part.send(0)
    for copy in fetches[2:]:
        copy.wait()
    first, second = wq_out.shape[1], wq_out.shape[1] + wk_out.shape[1]

    def normed_parts(n, carry):
        at = pl.ds(pl.multiple_of(n * cols, cols), cols)
        part_ref[:, at] = (
            dot_last(right_ref[:, :first], wq[at, :])
            + dot_last(right_ref[:, first:second], wk[at, :])
            + dot_last(right_ref[:, second:], wv[at, :])
        ).astype(low)
        return carry

    lax.fori_loop(0, 4, normed_parts, 0)
    columns.start()
    for k in range(1, nz):
        for part in weights:
            part.send(k)
    top, bottom = pl.ds(0, half), pl.ds(half, half)
    swaps = [remote(src.at[bottom], dst.at[bottom], s_w.at[n], r_w.at[n], mirror)
             for n, (src, dst) in enumerate(((token, token_out), (block_ref, block_out)))]
    keeps = [pltpu.make_async_copy(src.at[top], dst.at[top], s_l.at[n])
             for n, (src, dst) in enumerate(((token, token_out), (block_ref, block_out)))]
    swaps[1].start()
    keeps[1].start()

    def loads(n):
        at = pl.ds(pl.multiple_of(n * panel, panel), panel)
        return (pltpu.make_async_copy(xr_all.at[:, at], x_panel, s_in.at[0]),
                pltpu.make_async_copy(gs_all.at[:, at], g_panel, s_in.at[1]))

    def stores(n):
        at = pl.ds(pl.multiple_of(n * panel, panel), panel)
        return (pltpu.make_async_copy(o_gate, dwg.at[at, :], s_out.at[0]),
                pltpu.make_async_copy(o_up, dwu.at[at, :], s_out.at[1]),
                pltpu.make_async_copy(o_down, dwd.at[:, at], s_out.at[2]))

    whole = [pltpu.make_async_copy(src, dst, s_in.at[2 + n])
             for n, (src, dst) in enumerate(((gp_all, gp_ref), (up_all, up_ref), (hid_all, hid_ref)))]
    for copy in tuple(whole) + loads(0):
        copy.start()
    small_out[me] = jnp.zeros(small_out.shape[1:], f32)
    small_out[me, pl.ds(cols // 128, 2), :] = small_ref[...]

    def expert_weights(n):
        @pl.when(n == 0)
        def _():
            for copy in whole:
                copy.wait()

        for copy in loads(n):
            copy.wait()

        @pl.when(n > 0)
        def _():
            for copy in stores(n):
                copy.wait()

        o_gate[...] = dot_first(x_panel[...], gp_ref[...]).astype(low)
        o_up[...] = dot_first(x_panel[...], up_ref[...]).astype(low)
        o_down[...] = dot_first(g_panel[...], hid_ref[...]).T.astype(low)
        for copy in stores(n):
            copy.start()

        @pl.when(n < panels - 1)
        def _():
            for copy in loads(n + 1):
                copy.start()

    def token_sums():
        eye = diagonal()

        def step(n, gains):
            here = pl.ds(pl.multiple_of(n * 128, 128), 128)
            tok, grad = tok_ref[here, :].astype(f32), normed[here, :]
            product = tok * (grad * gain_ref[:, pl.ds(pl.multiple_of(group * cols, cols), cols)])
            sums.got[0, pl.ds(n, 1), :] = to_row(jnp.sum(product, axis=1, keepdims=True), eye)
            return gains + jnp.sum(grad * tok * scale_ref[here, :], axis=0, keepdims=True)

        gains = lax.fori_loop(0, rows // 128, step, jnp.zeros((1, cols), f32))
        for n in range(cols // 128):
            small_out[me, pl.ds(n, 1), :] = gains[:, n * 128 : (n + 1) * 128]

    def token_grads():
        eye = diagonal()

        def step(n, carry):
            here = pl.ds(pl.multiple_of(n * 128, 128), 128)
            mean = to_column(sums.total(n), eye) / width
            scale = scale_ref[here, :]
            token[here, :] = (
                mid_ref[here, :]
                + scale * (gain_ref[:, pl.ds(pl.multiple_of(group * cols, cols), cols)] * normed[here, :])
                - tok_ref[here, :].astype(f32) * (scale * scale * scale * mean)
            ).astype(low)
            return carry

        lax.fori_loop(0, rows // 128, step, 0)

    def spread(k):
        other = (me + k) % devices
        return remote(small_out.at[me], small_out.at[me], s_g.at[k], r_g.at[k],
                      (other // 4, other % 4))

    columns.first()

    def unit(u, carry):
        @pl.when(u == 1)
        def _():
            sums.wait()
            token_grads()
            swaps[0].start()
            keeps[0].start()

        @pl.when((u >= 1) & (u <= nz))
        def _():
            for part in weights:
                part.second(u - 1)

        @pl.when(u < panels // 2)
        def _():
            expert_weights(2 * u)
            expert_weights(2 * u + 1)

        @pl.when(u == 0)
        def _():
            columns.second()
            token_sums()
            sums.start()
            loop_from_one(devices, lambda k: spread(k).start())

        @pl.when(u < nz)
        def _():
            for part in weights:
                part.first(u)

        return carry

    lax.fori_loop(0, max(nz + 1, panels // 2), unit, 0)
    loop_from_one(devices, lambda k: spread(k).wait())
    gain_rows = cols // 128
    for g in range(4):
        rows_of = small_out[g, pl.ds(0, gain_rows), :]
        for f in range(1, shards):
            rows_of = rows_of + small_out[f * 4 + g, pl.ds(0, gain_rows), :]
        gain_out[g] = rows_of
    total = small_out[0, pl.ds(gain_rows, 2), :]
    for d in range(1, devices):
        total = total + small_out[d, pl.ds(gain_rows, 2), :]
    head_out[...] = total
    for copy in swaps + keeps:
        copy.wait()
    for copy in stores(panels - 1):
        copy.wait()
    wq_out[...] = w_sum[:, :first]
    wk_out[...] = w_sum[:, first:second]
    wv_out[...] = w_sum[:, second:]
    columns.finish()
    for part in weights:
        part.finish()


def tail(gate_grad, up_grad, hidden, tokens, middle_grad, scale, gain, block_out, small, normed_low,
         pre_grad, wq_all, wk_all, wv_all, rows_in, pair_grad, nz, collective_id):
    rows, cols = tokens.shape
    pairs, features = rows_in.shape
    hidden_width = hidden.shape[1]
    panel = 256
    w_shape = (normed_low.shape[1] // (2 * nz), pre_grad.shape[1])
    query_width, kv_width = wq_all.shape[1], wk_all.shape[1]
    devices = 8 * nz
    any_space = pl.BlockSpec(memory_space=pl.ANY)
    vmem = pl.BlockSpec(memory_space=pltpu.VMEM)
    vm, shape, f32, low = pltpu.VMEM, jax.ShapeDtypeStruct, jnp.float32, jnp.bfloat16
    dma = pltpu.SemaphoreType.DMA
    return pl.pallas_call(
        functools.partial(tail_kernel, nz),
        in_specs=[vmem] * 5 + [any_space] * 11,
        out_specs=[vmem] * 3 + [any_space, any_space, vmem, vmem] + [any_space] * 3,
        out_shape=[
            shape((w_shape[0], query_width), f32), shape((w_shape[0], kv_width), f32),
            shape((w_shape[0], kv_width), f32), shape((rows, cols), low), shape((rows, cols), low),
            shape((4, cols // 128, 128), f32), shape((2, 128), f32),
            shape((features, hidden_width), low), shape((features, hidden_width), low),
            shape((hidden_width, features), low),
        ],
        scratch_shapes=[vm(normed_low.shape, low), vm(pre_grad.shape, low), vm((rows, cols), f32),
                        vm(wq_all.shape, low), vm(wk_all.shape, low), vm(wv_all.shape, low),
                        vm((rows, 4 * cols), low), dma((6,)), vm(w_shape, f32)] + [vm((pairs, hidden_width), low)] * 3 + [
            vm((pairs, panel), low), vm((pairs, panel), low),
            vm((panel, hidden_width), low), vm((panel, hidden_width), low),
            vm((hidden_width, panel), low), dma((5,)), dma((3,)),
            vm((devices, 8, 128), f32), vm((rows, cols), f32), vm((rows, cols), low),
            dma((2,)), dma((2,)), dma((2,)), dma((devices,)), dma((devices,)),
        ] + ReduceRows.scratch(nz, w_shape[0] // 2, w_shape[1], low) * 2 + ReduceCols.scratch(rows, cols, low)
        + RowSums.scratch(rows),
        compiler_params=pltpu.CompilerParams(
            collective_id=collective_id, has_side_effects=True, vmem_limit_bytes=62 << 20
        ),
        name="tail",
    )(tokens, scale, gain, block_out, small, normed_low, pre_grad, middle_grad, wq_all, wk_all, wv_all,
      gate_grad, up_grad, hidden, rows_in, pair_grad)


def join_kernel(nz, tok_ref, gain_ref, attn_part, middle_ref, scale_ref, low_ref, all_ref, *refs):
    z, x, y, c = place()
    rows, cols = tok_ref.shape
    f32 = jnp.float32
    n_c, n_s = len(ReduceCols.scratch(16, 128, jnp.bfloat16)), 3
    columns = ReduceCols(attn_part, middle_ref, refs[:n_c])
    sums = RowSums(refs[n_c : n_c + n_s])
    gather = GatherAll(nz, low_ref, all_ref, refs[n_c + n_s :], rows // 2)
    greet([(None, gather.xn), (z < nz - 1, gather.up), (z > 0, gather.down)]
          + [(None, peer) for peer in sums.peers])
    columns.start()
    eye = diagonal()
    columns.first()
    columns.second()

    def add(n, carry):
        here = pl.ds(pl.multiple_of(n * 128, 128), 128)
        total = middle_ref[here, :] + tok_ref[here, :].astype(f32)
        middle_ref[here, :] = total
        sums.got[0, pl.ds(n, 1), :] = to_row(jnp.sum(total * total, axis=1, keepdims=True), eye)
        return carry

    def norm(n, carry):
        here = pl.ds(pl.multiple_of(n * 128, 128), 128)
        scale = lax.rsqrt(to_column(sums.total(n), eye) / (4 * cols) + norm_eps)
        scale_ref[here, :] = scale
        low_ref[here, :] = (middle_ref[here, :] * scale * gain_ref[...]).astype(low_ref.dtype)
        return carry

    lax.fori_loop(0, rows // 128, add, 0)
    sums.start()
    sums.wait()
    lax.fori_loop(0, rows // 128, norm, 0)
    gather.own().start()
    gather.own().wait()

    def tick(k, carry):
        pl.when(k < nz)(lambda: gather.first(k))
        pl.when((k >= 1) & (k <= nz))(lambda: gather.second(k - 1))
        pl.when(k >= 2)(lambda: gather.third(k - 2))
        return carry

    lax.fori_loop(0, nz + 2, tick, 0)
    gather.finish()
    columns.finish()


def join(tokens, gain, attn_part, nz, collective_id):
    rows, cols = tokens.shape
    any_space = pl.BlockSpec(memory_space=pl.ANY)
    vmem = pl.BlockSpec(memory_space=pltpu.VMEM)
    shape, f32, low = jax.ShapeDtypeStruct, jnp.float32, jnp.bfloat16
    return pl.pallas_call(
        functools.partial(join_kernel, nz),
        in_specs=[vmem] * 2 + [any_space],
        out_specs=[vmem] * 3 + [any_space],
        out_shape=[shape((rows, cols), f32), shape((rows, 1), f32), shape((rows, cols), low),
                   shape((rows * 2 * nz, cols * 4), low)],
        scratch_shapes=ReduceCols.scratch(rows, cols, low) + RowSums.scratch(rows)
        + GatherAll.scratch(nz),
        compiler_params=pltpu.CompilerParams(
            collective_id=collective_id, has_side_effects=True, vmem_limit_bytes=62 << 20
        ),
        name="join",
    )(tokens, gain, attn_part)


def turn_kernel(middle_ref, scale_ref, inner_ref, grad_ref, out_ref, all_ref, low_ref, lsem,
                s_p, r_p, s_y, r_y, *refs):
    z, x, y, c = place()
    rows, cols = middle_ref.shape
    sums = RowSums(refs)
    partner, yn = device(z, x, y, 1 - c), device(z, x, 1 - y, c)
    greet([(None, peer) for peer in sums.peers])
    eye = diagonal()

    def block(yy):
        return all_ref.at[:, pl.ds(pl.multiple_of((yy * 2 + c) * cols, cols), cols)]

    def dots(n, carry):
        here = pl.ds(pl.multiple_of(n * 128, 128), 128)
        product = middle_ref[here, :] * inner_ref[here, :]
        sums.got[0, pl.ds(n, 1), :] = to_row(jnp.sum(product, axis=1, keepdims=True), eye)
        return carry

    def grads(n, carry):
        here = pl.ds(pl.multiple_of(n * 128, 128), 128)
        mean = to_column(sums.total(n), eye) / (4 * cols)
        scale = scale_ref[here, :]
        out = (grad_ref[here, :] + scale * inner_ref[here, :]
               - middle_ref[here, :] * (scale * scale * scale * mean))
        out_ref[here, :] = out
        low_ref[here, :] = out.astype(low_ref.dtype)
        return carry

    lax.fori_loop(0, rows // 128, dots, 0)
    sums.start()
    sums.wait()
    lax.fori_loop(0, rows // 128, grads, 0)
    to_y = remote(low_ref, block(y), s_y, r_y, yn)
    to_pair = remote(low_ref, block(y), s_p.at[0], r_p.at[0], partner)
    own = pltpu.make_async_copy(low_ref, block(y), lsem)
    on = remote(block(1 - y), block(1 - y), s_p.at[1], r_p.at[1], partner)
    for copy in (to_y, to_pair, own):
        copy.start()
    to_y.wait_recv()
    on.start()
    to_pair.wait()
    on.wait()
    to_y.wait_send()
    own.wait()


def turn(middle, scale, inner, grad, collective_id):
    rows, cols = middle.shape
    any_space = pl.BlockSpec(memory_space=pl.ANY)
    vmem = pl.BlockSpec(memory_space=pltpu.VMEM)
    shape, f32, low = jax.ShapeDtypeStruct, jnp.float32, jnp.bfloat16
    dma = pltpu.SemaphoreType.DMA
    return pl.pallas_call(
        turn_kernel,
        in_specs=[vmem] * 4,
        out_specs=[vmem, any_space],
        out_shape=[shape((rows, cols), f32), shape((rows, cols * 4), low)],
        scratch_shapes=[pltpu.VMEM((rows, cols), low), dma, dma((2,)), dma((2,)), dma, dma]
        + RowSums.scratch(rows),
        compiler_params=pltpu.CompilerParams(
            collective_id=collective_id, has_side_effects=True, vmem_limit_bytes=62 << 20
        ),
        name="turn",
    )(middle, scale, inner, grad)


def gathered_body(
    tokens,
    cotangent,
    routes,
    doc_ids,
    gain_attn,
    w_query,
    key_weight,
    value_weight,
    w_out,
    gain_query,
    key_norm_gain,
    gain_moe,
    router,
    w_gate,
    w_up,
    w_down,
):
    shard_count = lax.axis_size("fsdp")
    group_count = lax.axis_size("tp")
    shard_index = lax.axis_index("fsdp")
    group_index = lax.axis_index("tp")
    nz = shard_count // 2
    f32, low = jnp.float32, jnp.bfloat16
    row_count, slice_width = tokens.shape
    model_width = slice_width * group_count
    micro_count, micro_rows = doc_ids.shape
    head_width = gain_query.shape[0]
    query_width, kv_width = w_query.shape[1], key_weight.shape[1]
    query_local = query_width // head_width
    kv_local = kv_width // head_width
    group_width = query_local // kv_local
    expert_total = router.shape[1]
    capacity = max(2, 2 * micro_rows * TOPK // expert_total)
    block_keys = micro_rows * math.gcd(shard_count, max(1, 512 // micro_rows))
    my_columns = group_index * slice_width

    mirror_index = mirrored(nz, shard_index)
    owners = jnp.stack([shard_index, mirror_index])

    small = jnp.concatenate([routes.reshape(-1), doc_ids.reshape(-1)])
    small_rows = -(-small.shape[0] // 1024) * 8
    small = jnp.pad(small, (0, small_rows * 128 - small.shape[0])).reshape(small_rows, 128)
    small_all, wq_all, wk_all, wv_all, tokens, full_tokens = gather_rows(
        [small, w_query, key_weight, value_weight], nz, 2, [tokens], 2
    )
    small_all = small_all.reshape(shard_count, small_rows * 128)
    routes_all = small_all[:, : row_count * TOPK].reshape(shard_count * row_count, TOPK)
    ids_all = small_all[:, row_count * TOPK : row_count * (TOPK + 1)].reshape(
        shard_count, micro_count, micro_rows
    )
    doc_range = jnp.arange(DOCS)
    doc_totals = jnp.sum((ids_all[..., None] == doc_range).astype(jnp.int32), axis=(0, 2))
    doc_begin = jnp.cumsum(doc_totals, axis=1) - doc_totals
    query_index = owners[:, None] * micro_rows + jnp.arange(micro_rows)
    my_ids = jnp.stack(
        [lax.dynamic_index_in_dim(ids_all[:, m], owners[m], 0, False) for m in range(micro_count)]
    )
    query_start = jnp.sum(
        jnp.where(my_ids[:, :, None] == doc_range, doc_begin[:, None, :], 0), axis=2
    )
    positions = (query_index - query_start).reshape(row_count)
    cosine_lookup, sine_lookup = rope_tables(positions, head_width)

    turned_sine = jnp.where(jnp.arange(head_width) < head_width // 2, -sine_lookup, sine_lookup)
    query_gain, key_gain = gain_query.reshape(1, head_width), key_norm_gain.reshape(1, head_width)
    starts = query_start.reshape(micro_count, 1, micro_rows).astype(jnp.int32)
    (normed_low, token_scale, query_pre, key_pre, query_low, heads_low, log_total, keys_values,
     grads_all, wo_all) = attend(
        full_tokens, gain_attn.reshape(1, model_width), wq_all, wk_all, wv_all, query_gain, key_gain,
        cosine_lookup, turned_sine, starts, cotangent, w_out, nz, 3,
    )
    attn_part = dot_last(heads_low, wo_all).astype(low)
    gain_row = gain_moe.reshape(1, model_width)
    middle, scale, moe_low, _, out_part, back, gates_grad, gates, *kept = run_experts(
        tokens, gain_row, router, attn_part, grads_all, routes_all,
        w_gate[0], w_up[0], w_down[0], micro_rows, capacity, nz, 8,
    )
    rows_in, pair_grad, hidden_low, gate_pre_low, up_pre_low = (
        array.reshape(-1, array.shape[2]) for array in kept
    )
    middle_grad, pre_low, head_gains, out_sum, w_out_grad, summed = attend_back(
        query_low, query_pre, key_pre, key_gain, query_gain, cosine_lookup, turned_sine, keys_values,
        starts, log_total, gates, gates_grad, router, gain_row, moe_low, middle, scale,
        back, cotangent, grads_all, wo_all, heads_low, out_part, nz, 12,
    )
    block_out = (middle + out_sum).astype(low)
    gain_rows = slice_width // 128
    (w_query_grad, w_key_grad, w_value_grad, token_grad, block_out, attn_gains, head_gains,
     *expert_grads) = tail(
        gate_pre_low, up_pre_low, hidden_low, tokens, middle_grad, token_scale,
        gain_attn.reshape(1, model_width), block_out, head_gains, normed_low, pre_low, wq_all, wk_all, wv_all,
        rows_in, pair_grad, nz, 15,
    )
    per = expert_total // shard_count
    summed = summed.reshape(shard_count, group_count, -1, 128)
    router_grad = summed[:, :, : per * gain_rows].reshape(
        shard_count, group_count, per, slice_width
    ).transpose(1, 3, 0, 2).reshape(router.shape)
    return (
        block_out,
        token_grad,
        attn_gains.reshape(-1),
        w_query_grad,
        w_key_grad,
        w_value_grad,
        w_out_grad,
        head_gains[0],
        head_gains[1],
        summed[0, :, per * gain_rows : (per + 1) * gain_rows].reshape(-1),
        router_grad,
        expert_grads[0][None].astype(f32),
        expert_grads[1][None].astype(f32),
        expert_grads[2][None].astype(f32),
    )


def solution(mesh):
    small = mesh.shape["fsdp"] * mesh.shape["tp"] <= 32 and mesh.shape["tp"] == 4
    return jax.shard_map(
        gathered_body if small else body,
        mesh=mesh,
        in_specs=(
            P("fsdp", "tp"),
            P("fsdp", "tp"),
            P("fsdp", None),
            P(None, "fsdp"),
            P(),
            P("fsdp", "tp"),
            P("fsdp", "tp"),
            P("fsdp", "tp"),
            P("fsdp", "tp"),
            P(),
            P(),
            P(),
            P(),
            P(("fsdp", "tp"), None, None),
            P(("fsdp", "tp"), None, None),
            P(("fsdp", "tp"), None, None),
        ),
        out_specs=(
            P("fsdp", "tp"),
            P("fsdp", "tp"),
            P(),
            P("fsdp", "tp"),
            P("fsdp", "tp"),
            P("fsdp", "tp"),
            P("fsdp", "tp"),
            P(),
            P(),
            P(),
            P(),
            P(("fsdp", "tp"), None, None),
            P(("fsdp", "tp"), None, None),
            P(("fsdp", "tp"), None, None),
        ),
        check_vma=False,
    )
```
